32 devices in a mesh: section: 4 (over z), tm: 8 (over y, x, core).
Axes of the slice: x: 2, y: 2, z: 4, core: 2. Of those that a mesh axis runs over, the one named last changes fastest.
Arguments:
- acts: bfloat16 [4, 2, 512, 1024], P('section', None, 'tm'), may hold values from -600 to 600
- grad_top: bfloat16 [2, 512, 1024], P(None, 'tm'), may hold values from -6 to 6
- w_in: bfloat16 [4, 1024, 3072], P('section'), may hold values from -0.1875 to 0.1875
- w_out: bfloat16 [4, 1024, 1024], P('section'), may hold values from -0.1875 to 0.1875
- offsets: int32 [8, 3], P('tm'), may hold values from 0 to 4, as said below
Outputs:
- d_acts: bfloat16 [4, 2, 512, 1024], P('section', None, 'tm')
- d_w_in: float32 [4, 1024, 3072], P('section', 'tm')
- d_w_out: float32 [4, 1024, 1024], P('section', 'tm')
The draws below stay inside these ranges and needn't reach their ends.
Inputs may be any that keep to these rules, and one draw needn't show every extreme that they name: offsets[t, k] is 0 or 2**k, and 0 wherever t < 2**k; the last shard uses every level.
All inputs are finite; a program needn't handle non-finite values.
Results may differ from the reference program's by a relative error of at most 0.018.
The reference program's roundings to bfloat16 on the way count: a program that leaves them out, or rounds other values in their place, can miss the bound.
Values may be sent and summed in bfloat16 or wider, within the bound.
No kernel may reach another device: no remote copies, remote signals or barrier semaphores. Data moves between devices by JAX's collectives and lax.ppermute only.
A program may use at most 128 MiB of HBM per device.

```python
import math
import jax
import jax.numpy as jnp
from jax import lax

D = 1024
HEAD_DIM = 64
TOK_DEV = 64
MB = 2
LAYERS = 4
SHARDS = 8
LEVELS = 3
SEQ = 512


def draw_acts(key, part):
    shape = (LAYERS, MB, SEQ, D)
    first, second, third = jax.random.split(jax.random.fold_in(key, 11), 3)
    column_scale = jnp.exp(jax.random.uniform(second, (LAYERS, 1, 1, D), minval=0.0, maxval=math.log(10.0)))
    row_scale = jnp.exp(jax.random.uniform(third, (LAYERS, MB, SEQ, 1), minval=0.0, maxval=math.log(10.0)))
    values = jnp.clip(jax.random.normal(first, shape), -6.0, 6.0) * column_scale * row_scale
    return values.astype(jnp.bfloat16)


def draw_w_in(key, part):
    shape = (LAYERS, D, 3 * D)
    first = jax.random.fold_in(jax.random.fold_in(key, 23), 0)
    values = jnp.clip(jax.random.normal(first, shape), -6.0, 6.0) * D ** (-0.5)
    return values.astype(jnp.bfloat16)


def draw_offsets(key, part):
    chosen = jax.random.randint(jax.random.fold_in(key, 31), (SHARDS, LEVELS), 0, 4) < 3
    shard_row = jnp.arange(SHARDS, dtype=jnp.int32)[:, None]
    powers = (2 ** jnp.arange(LEVELS, dtype=jnp.int32))[None, :]
    chosen = chosen | (shard_row == SHARDS - 1)
    return jnp.where(chosen & (shard_row >= powers), powers, 0).astype(jnp.int32)


def levels(key, dims, cuts, smallest, top_value):
    def one(axis_at, parts):
        heights = jax.random.uniform(jax.random.fold_in(jax.random.fold_in(key, 6), axis_at), (parts,), jnp.float32, smallest / len(cuts), top_value / len(cuts))
        return jnp.repeat(jnp.exp(heights), dims[axis_at] // parts).reshape((-1,) + (1,) * (len(dims) - axis_at - 1))

    factor_of = one(*cuts[0])
    for cut in cuts[1:]:
        factor_of = factor_of * one(*cut)
    return factor_of


def gaussian(own_key, shape, width, reach, cuts=(), kind=jnp.bfloat16):
    result = jax.random.normal(own_key, shape, jnp.float32) * width
    if len(cuts) > 0:
        result = levels(own_key, shape, cuts, -0.22, 0.18) * result
    return jnp.clip(result, min=-reach, max=reach).astype(kind)


def setup_inputs(seed: int = 0) -> dict:
    arg_keys = jax.random.split(jax.random.key(seed), 6)
    return {
        "acts": draw_acts(jax.random.fold_in(arg_keys[5], 71), 0),
        "grad_top": gaussian(arg_keys[1], (MB, SEQ, D), 1.0, 6.0, ((1, 8),)),
        "w_in": draw_w_in(jax.random.fold_in(arg_keys[5], 71), 0),
        "w_out": gaussian(arg_keys[3], (LAYERS, D, D), D ** -0.5, 0.1875, ((0, 4),)),
        "offsets": draw_offsets(jax.random.fold_in(arg_keys[5], 71), 0),
    }


epsilon = 1e-06
negative_fill = -1e+30

def to_bf16(values):
    return lax.optimization_barrier(values.astype(jnp.bfloat16))

def normalize(inputs):
    values = inputs.astype(jnp.float32)
    inverse_rms = lax.rsqrt(lax.optimization_barrier(jnp.mean(values * values, axis=-1, keepdims=True)) + epsilon)
    return (values * inverse_rms, inverse_rms)

def shift_shards(stacked, offset):
    padding = jnp.zeros((abs(offset),) + stacked.shape[1:], stacked.dtype)
    if offset > 0:
        return jnp.concatenate([padding, stacked[:-offset]], 0)
    return jnp.concatenate([stacked[-offset:], padding], 0)

def key_bias(level_flags, shard_rows):
    position = jnp.arange(shard_rows)
    own_part = position[None, :] <= position[:, None]
    far_part = jnp.repeat(level_flags != 0, shard_rows)
    far_part = jnp.broadcast_to(far_part[None, :], (shard_rows, far_part.shape[0]))
    return jnp.concatenate([own_part, far_part], 1)

def softmax_keys(queries, key_heads, allowed):
    scores = jnp.einsum('ihd,jhd->hij', queries.astype(jnp.float32), key_heads.astype(jnp.float32)) * HEAD_DIM ** (-0.5)
    scores = jnp.where(allowed[None], scores, negative_fill)
    highest = lax.optimization_barrier(jnp.max(scores, axis=-1, keepdims=True))
    shifted_exp = jnp.where(allowed[None], jnp.exp(scores - highest), 0.0)
    return shifted_exp / lax.optimization_barrier(jnp.sum(shifted_exp, axis=-1, keepdims=True))

def attend_back(query_rows, key_rows, allowed, incoming, w_proj):
    shard_rows, model_width = query_rows.shape
    head_count = model_width // HEAD_DIM
    queries = query_rows.reshape(shard_rows, head_count, HEAD_DIM).astype(jnp.float32)
    key_heads = key_rows[:, :model_width].reshape(-1, head_count, HEAD_DIM).astype(jnp.float32)
    value_heads = key_rows[:, model_width:].reshape(-1, head_count, HEAD_DIM).astype(jnp.float32)
    probability = softmax_keys(queries, key_heads, allowed)
    rounded = to_bf16(probability).astype(jnp.float32)
    attended = jnp.einsum('hij,jhd->ihd', rounded, value_heads).reshape(shard_rows, model_width).astype(jnp.bfloat16)
    upstream = to_bf16(jnp.dot(incoming, w_proj.T, preferred_element_type=jnp.float32))
    up_heads = upstream.astype(jnp.float32).reshape(shard_rows, head_count, HEAD_DIM)
    att_heads = attended.astype(jnp.float32).reshape(shard_rows, head_count, HEAD_DIM)
    delta = jnp.einsum('ihd,ihd->hi', up_heads, att_heads)[..., None]
    prob_grad = jnp.einsum('ihd,jhd->hij', up_heads, value_heads)
    score_grad = to_bf16(probability * (prob_grad - delta)).astype(jnp.float32)
    scale_factor = HEAD_DIM ** (-0.5)
    query_grad = jnp.einsum('hij,jhd->ihd', score_grad, key_heads) * scale_factor
    key_grad = jnp.einsum('hij,ihd->jhd', score_grad, queries) * scale_factor
    value_grad = jnp.einsum('hij,ihd->jhd', rounded, up_heads)
    return (attended, query_grad.reshape(shard_rows, model_width), key_grad.reshape(-1, model_width), value_grad.reshape(-1, model_width))

def reference(acts, grad_top, w_in, w_out, offsets):
    model_width = acts.shape[-1]
    shard_rows = TOK_DEV
    shards = SHARDS
    grads_acts = [None] * LAYERS
    grads_in = [None] * LAYERS
    grads_out = [None] * LAYERS
    incoming = grad_top
    for layer in reversed(range(LAYERS)):
        w_qkv = w_in[layer]
        w_proj = w_out[layer]
        outgoing = []
        saved = []
        for micro in range(MB):
            normed, inverse_rms = normalize(acts[layer, micro])
            rounded_norm = normed.astype(jnp.bfloat16)
            qkv = jnp.dot(rounded_norm, w_qkv, preferred_element_type=jnp.float32).astype(jnp.bfloat16)
            shard_qkv = qkv.reshape(shards, shard_rows, 3 * model_width)
            queries = shard_qkv[..., :model_width]
            pairs = shard_qkv[..., model_width:]
            far_pairs = jnp.stack([shift_shards(pairs, 2 ** level) for level in range(LEVELS)], 1)
            gradient = incoming[micro].reshape(shards, shard_rows, model_width)

            def shard_pass(piece):
                query_rows, own_rows, far_rows, level_flags, grad_rows = piece
                key_rows = jnp.concatenate([own_rows, far_rows.reshape(-1, own_rows.shape[-1])], 0)
                return attend_back(query_rows, key_rows, key_bias(level_flags, shard_rows), grad_rows, w_proj)
            attended, query_grad, key_grad, value_grad = lax.map(shard_pass, (queries, pairs, far_pairs, offsets, gradient))
            owner_sum = jnp.concatenate([key_grad[:, :shard_rows], value_grad[:, :shard_rows]], -1)
            far_grad = jnp.concatenate([key_grad[:, shard_rows:], value_grad[:, shard_rows:]], -1)
            far_grad = far_grad.reshape(shards, LEVELS, shard_rows, 2 * model_width)
            for level in range(LEVELS):
                owner_sum = owner_sum + shift_shards(to_bf16(far_grad[:, level]).astype(jnp.float32), -2 ** level)
            qkv_grad = jnp.concatenate([query_grad, owner_sum], -1).astype(jnp.bfloat16).reshape(-1, 3 * model_width)
            norm_grad = jnp.dot(qkv_grad, w_qkv.T, preferred_element_type=jnp.float32)
            inner = lax.optimization_barrier(jnp.mean(norm_grad * normed, axis=-1, keepdims=True))
            grad_in = (incoming[micro].astype(jnp.float32) + inverse_rms * (norm_grad - normed * inner)).astype(jnp.bfloat16)
            outgoing.append(grad_in)
            saved.append((rounded_norm, qkv_grad, attended.reshape(-1, model_width), incoming[micro]))
        stacked = []
        for position in range(4):
            joined = jnp.stack([item[position] for item in saved], 0)
            joined = joined.reshape(MB, shards, shard_rows, joined.shape[-1])
            stacked.append(jnp.swapaxes(joined, 0, 1))

        def add_shard(carry, piece):
            normed_rows, qkv_rows, attended_rows, grad_rows = [item.reshape(-1, item.shape[-1]) for item in piece]
            first = jnp.dot(normed_rows.T, qkv_rows, preferred_element_type=jnp.float32)
            second = jnp.dot(attended_rows.T, grad_rows, preferred_element_type=jnp.float32)
            term = to_bf16(jnp.concatenate([first, second], 1)).astype(jnp.float32)
            return (carry + term, None)
        summed, _ = lax.scan(add_shard, jnp.zeros((model_width, 4 * model_width), jnp.float32), tuple(stacked))
        grads_in[layer] = summed[:, :3 * model_width]
        grads_out[layer] = summed[:, 3 * model_width:]
        incoming = jnp.stack(outgoing, 0)
        grads_acts[layer] = incoming
    return (jnp.stack(grads_acts, 0), jnp.stack(grads_in, 0), jnp.stack(grads_out, 0))
```

```python
import functools
import jax
import jax.numpy as jnp
from jax import lax
from jax.experimental import pallas as pl
from jax.experimental.pallas import tpu as pltpu
from jax.sharding import PartitionSpec as P

HEAD_DIM = 64


epsilon = 1e-06
negative_fill = -1e30


def shifted(value, axis, steps):
    count = lax.axis_size(axis)
    initial, last = (max(0, -steps), min(count, count - steps))
    return lax.ppermute(value, axis, [(source, source + steps) for source in range(initial, last)])


def normalize(inputs):
    values = inputs.astype(jnp.float32)
    inverse_rms = lax.rsqrt(jnp.mean(values * values, axis=-1, keepdims=True) + epsilon)
    return (values * inverse_rms, inverse_rms)


def key_bias(level_flags, shard_rows):
    position = jnp.arange(shard_rows)
    own_part = position[None, :] <= position[:, None]
    far_part = jnp.repeat(level_flags != 0, shard_rows)
    far_part = jnp.broadcast_to(far_part[None, :], (shard_rows, far_part.shape[0]))
    return jnp.concatenate([own_part, far_part], 1)


def split_heads(row_block):
    return row_block.reshape(row_block.shape[0], -1, HEAD_DIM)


def softmax_keys(queries, key_heads, allowed):
    scores = jnp.einsum(
        "ihd,jhd->hij", queries, key_heads, preferred_element_type=jnp.float32
    ) * HEAD_DIM ** (-0.5)
    scores = jnp.where(allowed[None], scores, negative_fill)
    highest = jnp.max(scores, axis=-1, keepdims=True)
    shifted_exp = jnp.where(allowed[None], jnp.exp(scores - highest), 0.0)
    return shifted_exp / jnp.sum(shifted_exp, axis=-1, keepdims=True)


def attend(query_rows, key_rows, allowed):
    model_width = query_rows.shape[1]
    probability = softmax_keys(
        split_heads(query_rows), split_heads(key_rows[:, :model_width]), allowed
    )
    attended = jnp.einsum(
        "hij,jhd->ihd",
        probability.astype(jnp.bfloat16),
        split_heads(key_rows[:, model_width:]),
        preferred_element_type=jnp.float32,
    )
    return attended.reshape(query_rows.shape).astype(jnp.bfloat16)


def attend_back(query_rows, key_rows, allowed, incoming, attended, w_proj):
    model_width = query_rows.shape[1]
    queries = split_heads(query_rows)
    key_heads = split_heads(key_rows[:, :model_width])
    value_heads = split_heads(key_rows[:, model_width:])
    probability = softmax_keys(queries, key_heads, allowed)
    rounded = probability.astype(jnp.bfloat16)
    upstream = lax.dot_general(
        incoming, w_proj, (((1,), (1,)), ((), ())), preferred_element_type=jnp.float32
    ).astype(jnp.bfloat16)
    up_heads = split_heads(upstream)
    delta = jnp.einsum(
        "ihd,ihd->hi", up_heads.astype(jnp.float32), split_heads(attended).astype(jnp.float32)
    )[..., None]
    prob_grad = jnp.einsum(
        "ihd,jhd->hij", up_heads, value_heads, preferred_element_type=jnp.float32
    )
    score_grad = (probability * (prob_grad - delta)).astype(jnp.bfloat16)
    scale_factor = HEAD_DIM ** (-0.5)
    query_grad = (
        jnp.einsum("hij,jhd->ihd", score_grad, key_heads, preferred_element_type=jnp.float32)
        * scale_factor
    )
    key_grad = (
        jnp.einsum("hij,ihd->jhd", score_grad, queries, preferred_element_type=jnp.float32)
        * scale_factor
    )
    value_grad = jnp.einsum("hij,ihd->jhd", rounded, up_heads, preferred_element_type=jnp.float32)
    return (
        query_grad.reshape(-1, model_width),
        key_grad.reshape(-1, model_width),
        value_grad.reshape(-1, model_width),
    )


def per_device(acts, grad_top, w_in, w_out, offsets):
    sections = lax.axis_size("section")
    shards = lax.axis_size("tm")
    levels = shards.bit_length() - 1
    section_index = lax.axis_index("section")
    micro_count = acts.shape[1]
    shard_rows = acts.shape[2]
    model_width = acts.shape[3]
    w_qkv = w_in[0]
    w_proj = w_out[0]
    level_flags = offsets[0]
    normed, inverse_rms = normalize(acts[0])
    rounded_norm = normed.astype(jnp.bfloat16)
    qkv = jnp.dot(rounded_norm.reshape(-1, model_width), w_qkv, preferred_element_type=jnp.float32)
    qkv = qkv.astype(jnp.bfloat16).reshape(micro_count, shard_rows, 3 * model_width)
    pairs = qkv[..., model_width:]
    far_list = [shifted(pairs, "tm", 2**level) for level in range(levels)]
    key_rows = jnp.concatenate([pairs] + far_list, 1)
    allowed = key_bias(level_flags, shard_rows)
    attended = jnp.stack(
        [
            attend(qkv[index, :, :model_width], key_rows[index], allowed)
            for index in range(micro_count)
        ],
        0,
    )

    def attention_part(incoming, slot):
        query_rows = lax.dynamic_index_in_dim(qkv, slot, 0, False)[:, :model_width]
        slot_keys = lax.dynamic_index_in_dim(key_rows, slot, 0, False)
        slot_attended = lax.dynamic_index_in_dim(attended, slot, 0, False)
        query_grad, key_grad, value_grad = attend_back(
            query_rows, slot_keys, allowed, incoming, slot_attended, w_proj
        )
        owner_sum = jnp.concatenate([key_grad[:shard_rows], value_grad[:shard_rows]], 1)
        far_part = jnp.concatenate([key_grad[shard_rows:], value_grad[shard_rows:]], 1)
        far_part = far_part.astype(jnp.bfloat16).reshape(levels, shard_rows, 2 * model_width)
        return (query_grad, owner_sum, far_part)

    def empty_attention(incoming, slot):
        return (
            jnp.zeros((shard_rows, model_width), jnp.float32),
            jnp.zeros((shard_rows, 2 * model_width), jnp.float32),
            jnp.zeros((levels, shard_rows, 2 * model_width), jnp.bfloat16),
        )

    def norm_part(qkv_grad, incoming, slot):
        norm_grad = lax.dot_general(
            qkv_grad, w_qkv, (((1,), (1,)), ((), ())), preferred_element_type=jnp.float32
        )
        slot_normed = lax.dynamic_index_in_dim(normed, slot, 0, False)
        slot_rms = lax.dynamic_index_in_dim(inverse_rms, slot, 0, False)
        inner = jnp.mean(norm_grad * slot_normed, axis=-1, keepdims=True)
        return (incoming.astype(jnp.float32) + slot_rms * (norm_grad - slot_normed * inner)).astype(
            jnp.bfloat16
        )

    def empty_norm(qkv_grad, incoming, slot):
        return jnp.zeros((shard_rows, model_width), jnp.bfloat16)

    def step(turn, carry):
        received, grad_store, qkv_store, incoming_store = carry
        slot_raw = turn - (sections - 1 - section_index)
        active = (slot_raw >= 0) & (slot_raw < micro_count)
        slot = jnp.clip(slot_raw, 0, micro_count - 1)
        incoming = jnp.where(
            section_index == sections - 1,
            lax.dynamic_index_in_dim(grad_top, slot, 0, False),
            received,
        )
        query_grad, owner_sum, far_part = lax.cond(
            active, attention_part, empty_attention, incoming, slot
        )
        for level in range(levels):
            owner_sum = owner_sum + shifted(far_part[level], "tm", -(2**level)).astype(jnp.float32)
        qkv_grad = jnp.concatenate([query_grad, owner_sum], 1).astype(jnp.bfloat16)
        grad_in = lax.cond(active, norm_part, empty_norm, qkv_grad, incoming, slot)
        sent_down = shifted(grad_in, "section", -1)
        grad_store = jnp.where(
            active, lax.dynamic_update_index_in_dim(grad_store, grad_in, slot, 0), grad_store
        )
        qkv_store = jnp.where(
            active, lax.dynamic_update_index_in_dim(qkv_store, qkv_grad, slot, 0), qkv_store
        )
        incoming_store = jnp.where(
            active,
            lax.dynamic_update_index_in_dim(incoming_store, incoming, slot, 0),
            incoming_store,
        )
        return (sent_down, grad_store, qkv_store, incoming_store)

    initial = (
        jnp.zeros((shard_rows, model_width), jnp.bfloat16),
        jnp.zeros((micro_count, shard_rows, model_width), jnp.bfloat16),
        jnp.zeros((micro_count, shard_rows, 3 * model_width), jnp.bfloat16),
        jnp.zeros((micro_count, shard_rows, model_width), jnp.bfloat16),
    )
    received, grad_store, qkv_store, incoming_store = lax.fori_loop(
        0, sections + micro_count - 1, step, initial
    )
    flat_norm = rounded_norm.reshape(-1, model_width)
    flat_attended = attended.reshape(-1, model_width)
    flat_qkv = qkv_store.reshape(-1, 3 * model_width)
    flat_incoming = incoming_store.reshape(-1, model_width)
    contract = (((0,), (0,)), ((), ()))
    first = lax.dot_general(flat_norm, flat_qkv, contract, preferred_element_type=jnp.float32)
    second = lax.dot_general(
        flat_attended, flat_incoming, contract, preferred_element_type=jnp.float32
    )
    summed = lax.psum_scatter(
        jnp.concatenate([first, second], 1).astype(jnp.bfloat16),
        "tm",
        scatter_dimension=0,
        tiled=True,
    ).astype(jnp.float32)
    return (
        grad_store[None],
        summed[None, :, : 3 * model_width],
        summed[None, :, 3 * model_width :],
    )


def normalize_kernel(acts_ref, rounded_ref):
    values = acts_ref[...].astype(jnp.float32)
    inverse_rms = lax.rsqrt(jnp.mean(values * values, axis=-1, keepdims=True) + epsilon)
    rounded_ref[...] = (values * inverse_rms).astype(jnp.bfloat16)


def round_norm(acts):
    return pl.pallas_call(
        normalize_kernel, out_shape=jax.ShapeDtypeStruct(acts.shape, jnp.bfloat16)
    )(acts)


def head_columns(shape, head):
    lane = lax.broadcasted_iota(jnp.int32, shape, 1)
    return (lane >= head * HEAD_DIM) & (lane < (head + 1) * HEAD_DIM)


def forward_kernel(
    shards, levels, norm_ref, wq_ref, wk_ref, wv_ref, flags_ref, prob_ref, q_ref, kt_ref, v_ref, at_ref
):
    seq = norm_ref.shape[0] * norm_ref.shape[2]
    columns = wq_ref.shape[1]
    rows = norm_ref[:, 0].reshape(seq, norm_ref.shape[3])
    queries = jnp.dot(rows, wq_ref[...], preferred_element_type=jnp.float32).astype(jnp.bfloat16)
    keys = jnp.dot(rows, wk_ref[...], preferred_element_type=jnp.float32).astype(jnp.bfloat16)
    values = jnp.dot(rows, wv_ref[...], preferred_element_type=jnp.float32).astype(jnp.bfloat16)
    keys_t = keys.T
    values_t = values.T
    q_ref[0] = queries
    v_ref[0] = values
    kt_ref[0] = keys_t
    shard_rows = seq // shards
    key_at = lax.broadcasted_iota(jnp.int32, (seq, seq), 0)
    query_at = lax.broadcasted_iota(jnp.int32, (seq, seq), 1)
    key_shard = lax.div(key_at, shard_rows)
    gap = lax.div(query_at, shard_rows) - key_shard
    allowed = (gap == 0) & (key_at <= query_at)
    for level in range(levels):
        allowed = allowed | ((gap == 2**level) & (flags_ref[level : level + 1, :] != 0))
    for head in range(columns // HEAD_DIM):
        at = slice(head * HEAD_DIM, (head + 1) * HEAD_DIM)
        own_keys = jnp.where(head_columns(keys.shape, head), keys, jnp.zeros_like(keys))
        scores = (
            lax.dot_general(
                own_keys, queries, (((1,), (1,)), ((), ())), preferred_element_type=jnp.float32
            )
            * HEAD_DIM ** (-0.5)
        )
        scores = jnp.where(allowed, scores, negative_fill)
        highest = jnp.max(scores, axis=0, keepdims=True)
        shifted_exp = jnp.where(allowed, jnp.exp(scores - highest), 0.0)
        probability = shifted_exp / jnp.sum(shifted_exp, axis=0, keepdims=True)
        prob_ref[0, head] = probability
        at_ref[0, at] = jnp.dot(
            values_t[at], probability.astype(jnp.bfloat16), preferred_element_type=jnp.float32
        ).astype(jnp.bfloat16)


def forward_heads(norm_all, w_qkv, flags):
    shards, micro_count, shard_rows, model_width = norm_all.shape
    columns = model_width // shards
    heads = columns // HEAD_DIM
    seq = shards * shard_rows
    index = lax.axis_index("tm")
    pieces = [
        lax.dynamic_slice_in_dim(w_qkv, block * model_width + index * columns, columns, 1)
        for block in range(3)
    ]
    whole = pl.BlockSpec((model_width, columns), lambda m: (0, 0))
    return pl.pallas_call(
        functools.partial(forward_kernel, shards, flags.shape[0]),
        grid=(micro_count,),
        in_specs=[
            pl.BlockSpec((shards, 1, shard_rows, model_width), lambda m: (0, m, 0, 0)),
            whole,
            whole,
            whole,
            pl.BlockSpec(flags.shape, lambda m: (0, 0)),
        ],
        out_specs=[
            pl.BlockSpec((1, heads, seq, seq), lambda m: (m, 0, 0, 0)),
            pl.BlockSpec((1, seq, columns), lambda m: (m, 0, 0)),
            pl.BlockSpec((1, columns, seq), lambda m: (m, 0, 0)),
            pl.BlockSpec((1, seq, columns), lambda m: (m, 0, 0)),
            pl.BlockSpec((1, columns, seq), lambda m: (m, 0, 0)),
        ],
        out_shape=[
            jax.ShapeDtypeStruct((micro_count, heads, seq, seq), jnp.float32),
            jax.ShapeDtypeStruct((micro_count, seq, columns), jnp.bfloat16),
            jax.ShapeDtypeStruct((micro_count, columns, seq), jnp.bfloat16),
            jax.ShapeDtypeStruct((micro_count, seq, columns), jnp.bfloat16),
            jax.ShapeDtypeStruct((micro_count, columns, seq), jnp.bfloat16),
        ],
        compiler_params=pltpu.CompilerParams(vmem_limit_bytes=40 * 2**20),
    )(norm_all, *pieces, flags)


def upstream_kernel(incoming_ref, w_ref, out_ref):
    micro_count, shard_rows, model_width = incoming_ref.shape
    rows = incoming_ref[...].reshape(micro_count * shard_rows, model_width)
    upstream = lax.dot_general(
        rows, w_ref[...], (((1,), (1,)), ((), ())), preferred_element_type=jnp.float32
    ).astype(jnp.bfloat16)
    shards = out_ref.shape[0]
    columns = model_width // shards
    for shard in range(shards):
        out_ref[shard] = upstream[:, shard * columns : (shard + 1) * columns].reshape(
            micro_count, shard_rows, columns
        )


def upstream_rows(incoming, w_proj, shards):
    micro_count, shard_rows, model_width = incoming.shape
    return pl.pallas_call(
        upstream_kernel,
        out_shape=jax.ShapeDtypeStruct(
            (shards, micro_count, shard_rows, model_width // shards), jnp.bfloat16
        ),
        compiler_params=pltpu.CompilerParams(vmem_limit_bytes=16 * 2**20),
    )(incoming, w_proj)


def backward_kernel(up_ref, prob_ref, q_ref, kt_ref, v_ref, at_ref, out_ref):
    shards, _, shard_rows, columns = up_ref.shape
    seq = shards * shard_rows
    upstream = up_ref[:, 0].reshape(seq, columns)
    upstream_t = upstream.T
    queries = q_ref[0]
    values = v_ref[0]
    product_t = upstream_t.astype(jnp.float32) * at_ref[0].astype(jnp.float32)
    key_grad = jnp.zeros((seq, columns), jnp.float32)
    value_grad = jnp.zeros((seq, columns), jnp.float32)
    query_parts = []
    for head in range(columns // HEAD_DIM):
        at = slice(head * HEAD_DIM, (head + 1) * HEAD_DIM)
        mine = head_columns((seq, columns), head)
        own_values = jnp.where(mine, values, jnp.zeros_like(values))
        own_queries = jnp.where(mine, queries, jnp.zeros_like(queries))
        own_upstream = jnp.where(mine, upstream, jnp.zeros_like(upstream))
        delta = jnp.sum(product_t[at], axis=0, keepdims=True)
        prob_grad = jnp.dot(own_values, upstream_t, preferred_element_type=jnp.float32)
        probability = prob_ref[0, head]
        score_grad = (probability * (prob_grad - delta)).astype(jnp.bfloat16)
        key_grad += jnp.dot(score_grad, own_queries, preferred_element_type=jnp.float32)
        value_grad += jnp.dot(
            probability.astype(jnp.bfloat16), own_upstream, preferred_element_type=jnp.float32
        )
        query_parts.append(
            jnp.dot(kt_ref[0, at], score_grad, preferred_element_type=jnp.float32)
        )
    scale_factor = HEAD_DIM ** (-0.5)
    query_grad = (jnp.concatenate(query_parts, 0) * scale_factor).T
    for block, part in enumerate((query_grad, key_grad * scale_factor, value_grad)):
        out_ref[:, 0, :, block * columns : (block + 1) * columns] = part.astype(
            jnp.bfloat16
        ).reshape(shards, shard_rows, columns)


def backward_heads(upstream, probability, queries, keys_t, values, attended_t):
    shards, micro_count, shard_rows, columns = upstream.shape
    seq = shards * shard_rows
    heads = columns // HEAD_DIM
    return pl.pallas_call(
        backward_kernel,
        grid=(micro_count,),
        in_specs=[
            pl.BlockSpec((shards, 1, shard_rows, columns), lambda m: (0, m, 0, 0)),
            pl.BlockSpec((1, heads, seq, seq), lambda m: (m, 0, 0, 0)),
            pl.BlockSpec((1, seq, columns), lambda m: (m, 0, 0)),
            pl.BlockSpec((1, columns, seq), lambda m: (m, 0, 0)),
            pl.BlockSpec((1, seq, columns), lambda m: (m, 0, 0)),
            pl.BlockSpec((1, columns, seq), lambda m: (m, 0, 0)),
        ],
        out_specs=pl.BlockSpec((shards, 1, shard_rows, 3 * columns), lambda m: (0, m, 0, 0)),
        out_shape=jax.ShapeDtypeStruct(
            (shards, micro_count, shard_rows, 3 * columns), jnp.bfloat16
        ),
        compiler_params=pltpu.CompilerParams(vmem_limit_bytes=40 * 2**20),
    )(upstream, probability, queries, keys_t, values, attended_t)


def norm_kernel(qkv_ref, acts_ref, incoming_ref, w_ref, out_ref, rows_ref):
    shards, micro_count, shard_rows, triple = qkv_ref.shape
    columns = triple // 3
    model_width = acts_ref.shape[2]
    rows = micro_count * shard_rows
    for shard in range(shards):
        piece = qkv_ref[shard].reshape(rows, triple)
        for block in range(3):
            first = block * model_width + shard * columns
            rows_ref[:, first : first + columns] = piece[:, block * columns : (block + 1) * columns]
    norm_grad = lax.dot_general(
        rows_ref[...], w_ref[...], (((1,), (1,)), ((), ())), preferred_element_type=jnp.float32
    )
    values = acts_ref[...].reshape(rows, model_width).astype(jnp.float32)
    inverse_rms = lax.rsqrt(jnp.mean(values * values, axis=-1, keepdims=True) + epsilon)
    normed = values * inverse_rms
    inner = jnp.mean(norm_grad * normed, axis=-1, keepdims=True)
    incoming = incoming_ref[...].reshape(rows, model_width).astype(jnp.float32)
    grad_in = incoming + inverse_rms * (norm_grad - normed * inner)
    out_ref[...] = grad_in.astype(jnp.bfloat16).reshape(out_ref.shape)


def norm_rows(qkv_rows, acts, incoming, w_qkv):
    rows = acts.shape[0] * acts.shape[1]
    return pl.pallas_call(
        norm_kernel,
        out_shape=jax.ShapeDtypeStruct(acts.shape, jnp.bfloat16),
        scratch_shapes=[pltpu.VMEM((rows, w_qkv.shape[1]), jnp.bfloat16)],
        compiler_params=pltpu.CompilerParams(vmem_limit_bytes=24 * 2**20),
    )(qkv_rows, acts, incoming, w_qkv)


def exchange(value):
    return lax.all_to_all(value, "tm", 0, 0, tiled=True)


def by_heads(acts, grad_top, w_in, w_out, offsets):
    sections = lax.axis_size("section")
    shards = lax.axis_size("tm")
    section_index = lax.axis_index("section")
    micro_count, shard_rows, model_width = acts.shape[1:]
    columns = model_width // shards
    w_qkv = w_in[0]
    w_proj = w_out[0]
    own_acts = acts[0]
    level_flags = lax.all_gather(offsets, "tm", axis=0, tiled=True)
    flags = jnp.repeat(level_flags.T, shard_rows, axis=1)
    norm_all = lax.all_gather(round_norm(own_acts), "tm", axis=0)
    probability, queries, keys_t, values, attended_t = forward_heads(norm_all, w_qkv, flags)
    incoming = grad_top
    for turn in range(sections):
        upstream = exchange(upstream_rows(incoming, w_proj, shards))
        qkv_grad = backward_heads(upstream, probability, queries, keys_t, values, attended_t)
        grad_in = norm_rows(exchange(qkv_grad), own_acts, incoming, w_qkv)
        if turn + 1 < sections:
            target = sections - 2 - turn
            received = lax.ppermute(grad_in, "section", [(target + 1, target)])
            incoming = jnp.where(section_index == target, received, incoming)
    incoming_all = lax.all_gather(incoming, "tm", axis=0)
    w_in_term = jnp.einsum(
        "tmrd,tmrc->dc", norm_all, qkv_grad, preferred_element_type=jnp.float32
    ).astype(jnp.bfloat16)
    w_in_rows = exchange(w_in_term.reshape(shards, model_width // shards, 3 * columns))
    w_in_rows = w_in_rows.reshape(shards, model_width // shards, 3, columns)
    d_w_in = jnp.transpose(w_in_rows, (1, 2, 0, 3)).reshape(-1, 3 * model_width)
    split_t = attended_t.reshape(micro_count, columns, shards, shard_rows)
    d_w_out = jnp.einsum(
        "mctr,tmrd->cd", split_t, incoming_all, preferred_element_type=jnp.float32
    )
    return (grad_in[None], d_w_in.astype(jnp.float32)[None], d_w_out[None])


def layer_gradients(acts, grad_top, w_in, w_out, offsets):
    columns = acts.shape[3] // lax.axis_size("tm")
    if columns % 128 == 0 and columns % HEAD_DIM == 0:
        return by_heads(acts, grad_top, w_in, w_out, offsets)
    return per_device(acts, grad_top, w_in, w_out, offsets)


def solution(mesh):
    placed = (
        P("section", None, "tm", None),
        P(None, "tm", None),
        P("section", None, None),
        P("section", None, None),
        P("tm", None),
    )
    return jax.shard_map(
        layer_gradients,
        mesh=mesh,
        in_specs=placed,
        out_specs=(
            P("section", None, "tm", None),
            P("section", "tm", None),
            P("section", "tm", None),
        ),
        check_vma=False,
    )
```

```python
import functools
import jax
import jax.numpy as jnp
from jax import lax
from jax.experimental import pallas as pl
from jax.experimental.pallas import tpu as pltpu
from jax.sharding import PartitionSpec as P

HEAD_DIM = 64


epsilon = 1e-06
negative_fill = -1e30


def shifted(value, axis, steps):
    count = lax.axis_size(axis)
    initial, last = (max(0, -steps), min(count, count - steps))
    return lax.ppermute(value, axis, [(source, source + steps) for source in range(initial, last)])


def normalize(inputs):
    values = inputs.astype(jnp.float32)
    inverse_rms = lax.rsqrt(jnp.mean(values * values, axis=-1, keepdims=True) + epsilon)
    return (values * inverse_rms, inverse_rms)


def key_bias(level_flags, shard_rows):
    position = jnp.arange(shard_rows)
    own_part = position[None, :] <= position[:, None]
    far_part = jnp.repeat(level_flags != 0, shard_rows)
    far_part = jnp.broadcast_to(far_part[None, :], (shard_rows, far_part.shape[0]))
    return jnp.concatenate([own_part, far_part], 1)


def split_heads(row_block):
    return row_block.reshape(row_block.shape[0], -1, HEAD_DIM)


def softmax_keys(queries, key_heads, allowed):
    scores = jnp.einsum(
        "ihd,jhd->hij", queries, key_heads, preferred_element_type=jnp.float32
    ) * HEAD_DIM ** (-0.5)
    scores = jnp.where(allowed[None], scores, negative_fill)
    highest = jnp.max(scores, axis=-1, keepdims=True)
    shifted_exp = jnp.where(allowed[None], jnp.exp(scores - highest), 0.0)
    return shifted_exp / jnp.sum(shifted_exp, axis=-1, keepdims=True)


def attend(query_rows, key_rows, allowed):
    model_width = query_rows.shape[1]
    probability = softmax_keys(
        split_heads(query_rows), split_heads(key_rows[:, :model_width]), allowed
    )
    attended = jnp.einsum(
        "hij,jhd->ihd",
        probability.astype(jnp.bfloat16),
        split_heads(key_rows[:, model_width:]),
        preferred_element_type=jnp.float32,
    )
    return attended.reshape(query_rows.shape).astype(jnp.bfloat16)


def attend_back(query_rows, key_rows, allowed, incoming, attended, w_proj):
    model_width = query_rows.shape[1]
    queries = split_heads(query_rows)
    key_heads = split_heads(key_rows[:, :model_width])
    value_heads = split_heads(key_rows[:, model_width:])
    probability = softmax_keys(queries, key_heads, allowed)
    rounded = probability.astype(jnp.bfloat16)
    upstream = lax.dot_general(
        incoming, w_proj, (((1,), (1,)), ((), ())), preferred_element_type=jnp.float32
    ).astype(jnp.bfloat16)
    up_heads = split_heads(upstream)
    delta = jnp.einsum(
        "ihd,ihd->hi", up_heads.astype(jnp.float32), split_heads(attended).astype(jnp.float32)
    )[..., None]
    prob_grad = jnp.einsum(
        "ihd,jhd->hij", up_heads, value_heads, preferred_element_type=jnp.float32
    )
    score_grad = (probability * (prob_grad - delta)).astype(jnp.bfloat16)
    scale_factor = HEAD_DIM ** (-0.5)
    query_grad = (
        jnp.einsum("hij,jhd->ihd", score_grad, key_heads, preferred_element_type=jnp.float32)
        * scale_factor
    )
    key_grad = (
        jnp.einsum("hij,ihd->jhd", score_grad, queries, preferred_element_type=jnp.float32)
        * scale_factor
    )
    value_grad = jnp.einsum("hij,ihd->jhd", rounded, up_heads, preferred_element_type=jnp.float32)
    return (
        query_grad.reshape(-1, model_width),
        key_grad.reshape(-1, model_width),
        value_grad.reshape(-1, model_width),
    )


def per_device(acts, grad_top, w_in, w_out, offsets):
    sections = lax.axis_size("section")
    shards = lax.axis_size("tm")
    levels = shards.bit_length() - 1
    section_index = lax.axis_index("section")
    micro_count = acts.shape[1]
    shard_rows = acts.shape[2]
    model_width = acts.shape[3]
    w_qkv = w_in[0]
    w_proj = w_out[0]
    level_flags = offsets[0]
    normed, inverse_rms = normalize(acts[0])
    rounded_norm = normed.astype(jnp.bfloat16)
    qkv = jnp.dot(rounded_norm.reshape(-1, model_width), w_qkv, preferred_element_type=jnp.float32)
    qkv = qkv.astype(jnp.bfloat16).reshape(micro_count, shard_rows, 3 * model_width)
    pairs = qkv[..., model_width:]
    far_list = [shifted(pairs, "tm", 2**level) for level in range(levels)]
    key_rows = jnp.concatenate([pairs] + far_list, 1)
    allowed = key_bias(level_flags, shard_rows)
    attended = jnp.stack(
        [
            attend(qkv[index, :, :model_width], key_rows[index], allowed)
            for index in range(micro_count)
        ],
        0,
    )

    def attention_part(incoming, slot):
        query_rows = lax.dynamic_index_in_dim(qkv, slot, 0, False)[:, :model_width]
        slot_keys = lax.dynamic_index_in_dim(key_rows, slot, 0, False)
        slot_attended = lax.dynamic_index_in_dim(attended, slot, 0, False)
        query_grad, key_grad, value_grad = attend_back(
            query_rows, slot_keys, allowed, incoming, slot_attended, w_proj
        )
        owner_sum = jnp.concatenate([key_grad[:shard_rows], value_grad[:shard_rows]], 1)
        far_part = jnp.concatenate([key_grad[shard_rows:], value_grad[shard_rows:]], 1)
        far_part = far_part.astype(jnp.bfloat16).reshape(levels, shard_rows, 2 * model_width)
        return (query_grad, owner_sum, far_part)

    def empty_attention(incoming, slot):
        return (
            jnp.zeros((shard_rows, model_width), jnp.float32),
            jnp.zeros((shard_rows, 2 * model_width), jnp.float32),
            jnp.zeros((levels, shard_rows, 2 * model_width), jnp.bfloat16),
        )

    def norm_part(qkv_grad, incoming, slot):
        norm_grad = lax.dot_general(
            qkv_grad, w_qkv, (((1,), (1,)), ((), ())), preferred_element_type=jnp.float32
        )
        slot_normed = lax.dynamic_index_in_dim(normed, slot, 0, False)
        slot_rms = lax.dynamic_index_in_dim(inverse_rms, slot, 0, False)
        inner = jnp.mean(norm_grad * slot_normed, axis=-1, keepdims=True)
        return (incoming.astype(jnp.float32) + slot_rms * (norm_grad - slot_normed * inner)).astype(
            jnp.bfloat16
        )

    def empty_norm(qkv_grad, incoming, slot):
        return jnp.zeros((shard_rows, model_width), jnp.bfloat16)

    def step(turn, carry):
        received, grad_store, qkv_store, incoming_store = carry
        slot_raw = turn - (sections - 1 - section_index)
        active = (slot_raw >= 0) & (slot_raw < micro_count)
        slot = jnp.clip(slot_raw, 0, micro_count - 1)
        incoming = jnp.where(
            section_index == sections - 1,
            lax.dynamic_index_in_dim(grad_top, slot, 0, False),
            received,
        )
        query_grad, owner_sum, far_part = lax.cond(
            active, attention_part, empty_attention, incoming, slot
        )
        for level in range(levels):
            owner_sum = owner_sum + shifted(far_part[level], "tm", -(2**level)).astype(jnp.float32)
        qkv_grad = jnp.concatenate([query_grad, owner_sum], 1).astype(jnp.bfloat16)
        grad_in = lax.cond(active, norm_part, empty_norm, qkv_grad, incoming, slot)
        sent_down = shifted(grad_in, "section", -1)
        grad_store = jnp.where(
            active, lax.dynamic_update_index_in_dim(grad_store, grad_in, slot, 0), grad_store
        )
        qkv_store = jnp.where(
            active, lax.dynamic_update_index_in_dim(qkv_store, qkv_grad, slot, 0), qkv_store
        )
        incoming_store = jnp.where(
            active,
            lax.dynamic_update_index_in_dim(incoming_store, incoming, slot, 0),
            incoming_store,
        )
        return (sent_down, grad_store, qkv_store, incoming_store)

    initial = (
        jnp.zeros((shard_rows, model_width), jnp.bfloat16),
        jnp.zeros((micro_count, shard_rows, model_width), jnp.bfloat16),
        jnp.zeros((micro_count, shard_rows, 3 * model_width), jnp.bfloat16),
        jnp.zeros((micro_count, shard_rows, model_width), jnp.bfloat16),
    )
    received, grad_store, qkv_store, incoming_store = lax.fori_loop(
        0, sections + micro_count - 1, step, initial
    )
    flat_norm = rounded_norm.reshape(-1, model_width)
    flat_attended = attended.reshape(-1, model_width)
    flat_qkv = qkv_store.reshape(-1, 3 * model_width)
    flat_incoming = incoming_store.reshape(-1, model_width)
    contract = (((0,), (0,)), ((), ()))
    first = lax.dot_general(flat_norm, flat_qkv, contract, preferred_element_type=jnp.float32)
    second = lax.dot_general(
        flat_attended, flat_incoming, contract, preferred_element_type=jnp.float32
    )
    summed = lax.psum_scatter(
        jnp.concatenate([first, second], 1).astype(jnp.bfloat16),
        "tm",
        scatter_dimension=0,
        tiled=True,
    ).astype(jnp.float32)
    return (
        grad_store[None],
        summed[None, :, : 3 * model_width],
        summed[None, :, 3 * model_width :],
    )


def pair_rows(transposed, head):
    width = 2 * HEAD_DIM
    pair = transposed[head // 2 * width : (head // 2 + 1) * width]
    empty = jnp.zeros((HEAD_DIM, pair.shape[1]), pair.dtype)
    if head % 2 == 0:
        return jnp.concatenate([pair[:HEAD_DIM], empty], 0)
    return jnp.concatenate([empty, pair[HEAD_DIM:]], 0)


def allowed_keys(flag_rows, levels, shard_rows, keys, first_query, count):
    key_at = lax.broadcasted_iota(jnp.int32, (keys, count), 0)
    query_at = lax.broadcasted_iota(jnp.int32, (keys, count), 1) + first_query
    gap = lax.div(query_at, shard_rows) - lax.div(key_at, shard_rows)
    allowed = (gap == 0) & (key_at <= query_at)
    for level in range(levels):
        allowed = allowed | ((gap == 2**level) & (flag_rows[level : level + 1] != 0))
    return allowed


def softmax_pass(queries, keys, values, allowed, prob_ref, at_ref):
    queries_t = queries.T
    values_t = values.T
    width = 2 * HEAD_DIM
    for head in range(queries.shape[1] // HEAD_DIM):
        at = slice(head * HEAD_DIM, (head + 1) * HEAD_DIM)
        pair = slice(head // 2 * width, (head // 2 + 1) * width)
        scores = (
            jnp.dot(keys[:, pair], pair_rows(queries_t, head), preferred_element_type=jnp.float32)
            * HEAD_DIM ** (-0.5)
        )
        scores = jnp.where(allowed, scores, negative_fill)
        highest = jnp.max(scores, axis=0, keepdims=True)
        shifted_exp = jnp.where(allowed, jnp.exp(scores - highest), 0.0)
        probability = shifted_exp / jnp.sum(shifted_exp, axis=0, keepdims=True)
        prob_ref[head] = probability
        at_ref[at] = jnp.dot(
            values_t[at], probability.astype(jnp.bfloat16), preferred_element_type=jnp.float32
        ).astype(jnp.bfloat16)


def upper_forward_kernel(
    levels,
    info_ref,
    acts_ref,
    wq_ref,
    wk_ref,
    wv_ref,
    norm_ref,
    flag_ref,
    q_ref,
    k_ref,
    v_ref,
    kt_ref,
    prob_ref,
    at_ref,
):
    shards, shard_rows = acts_ref.shape[:2]
    model_width = wq_ref.shape[0]
    seq = shards * shard_rows
    count = seq // 2
    normed, _ = normalize(acts_ref[:, :, :model_width].reshape(seq, model_width))
    rounded = normed.astype(jnp.bfloat16)
    norm_ref[...] = rounded
    flags = acts_ref[:, :, model_width:].reshape(seq, -1).astype(jnp.float32).T
    flag_ref[...] = flags
    for weight_ref, out_ref in ((wq_ref, q_ref), (wk_ref, k_ref), (wv_ref, v_ref)):
        out_ref[...] = jnp.dot(
            rounded, weight_ref[...], preferred_element_type=jnp.float32
        ).astype(jnp.bfloat16)
    kt_ref[...] = k_ref[...].T
    allowed = allowed_keys(flags[:, count:], levels, shard_rows, seq, count, count)
    softmax_pass(q_ref[count:], k_ref[...], v_ref[...], allowed, prob_ref, at_ref)


def lower_forward_kernel(
    levels, shard_rows, info_ref, norm_ref, flag_ref, q_ref, k_ref, v_ref, prob_ref, at_ref, gt_ref
):
    seq = norm_ref.shape[0]
    count = seq // 2
    allowed = allowed_keys(flag_ref[:, :count], levels, shard_rows, count, 0, count)
    softmax_pass(q_ref[:count], k_ref[:count], v_ref[:count], allowed, prob_ref, at_ref)
    rows = gt_ref.shape[1]
    half_width = norm_ref.shape[1] // 2
    for place in range(2):
        half = 1 - info_ref[2] if place == 0 else info_ref[2]
        first = pl.multiple_of(half * half_width + info_ref[1] * rows, 128)
        gt_ref[place] = norm_ref[:, pl.ds(first, rows)].T


def place_of(info_ref, step, replicas):
    return 2 * lax.rem(info_ref[1] - step + replicas, replicas)


def backward_kernel(upper, last, fresh_section, info_ref, *refs):
    refs = list(refs)
    got_ref, got_other_ref, kept_ref, kept_other_ref, w_ref, prob_ref, q_ref, v_ref, kt_ref, at_ref = (
        refs[:10]
    )
    refs = refs[10:]
    if not upper:
        key_sum_ref, value_sum_ref = refs[:2]
        refs = refs[2:]
    own_ref, other_ref, keep_ref, send_ref = refs[:4]
    refs = refs[4:]
    if upper:
        key_sum_ref, value_sum_ref = refs[:2]
        refs = refs[2:]
    if last:
        grads_ref, rows_ref = refs
    else:
        rows_ref, grads_ref = refs
    replicas, shard_rows, model_width = got_ref.shape
    count = rows_ref.shape[0] * shard_rows
    keys = prob_ref.shape[1]
    parity = info_ref[0]
    fresh = info_ref[3] == fresh_section

    @pl.when(fresh)
    def _():
        own_ref[...] = got_ref[...]
        other_ref[...] = got_other_ref[...]

    @pl.when(jnp.logical_not(fresh))
    def _():
        own_ref[...] = kept_ref[...]
        other_ref[...] = kept_other_ref[...]

    for step in range(replicas):
        place = place_of(info_ref, step, replicas)
        rows_ref[place + parity] = own_ref[step]
        rows_ref[place + 1 - parity] = other_ref[step]
    rows = rows_ref[...].reshape(count, model_width)
    upstream = lax.dot_general(
        rows, w_ref[...], (((1,), (1,)), ((), ())), preferred_element_type=jnp.float32
    ).astype(jnp.bfloat16)
    upstream_t = upstream.T
    product_t = upstream_t.astype(jnp.float32) * at_ref[...].astype(jnp.float32)
    first_query = keys - count
    columns = q_ref.shape[1]
    width = 2 * HEAD_DIM
    scale_factor = HEAD_DIM ** (-0.5)
    lane = lax.broadcasted_iota(jnp.int32, (count, width), 1)

    def put(block, pair, part):
        first = block * columns + pair * width
        grads_ref[:, :, first : first + width] = part.astype(jnp.bfloat16).reshape(
            -1, shard_rows, width
        )

    for pair in range(columns // width):
        at_pair = slice(pair * width, (pair + 1) * width)
        values = v_ref[:keys, at_pair]
        queries = q_ref[first_query : first_query + count, at_pair]
        up_pair = upstream[:, at_pair]
        key_grad = jnp.zeros((keys, width), jnp.float32)
        value_grad = jnp.zeros((keys, width), jnp.float32)
        query_parts = []
        for head in (2 * pair, 2 * pair + 1):
            at = slice(head * HEAD_DIM, (head + 1) * HEAD_DIM)
            mine = (lane < HEAD_DIM) if head % 2 == 0 else (lane >= HEAD_DIM)
            delta = jnp.sum(product_t[at], axis=0, keepdims=True)
            prob_grad = jnp.dot(
                values, pair_rows(upstream_t, head), preferred_element_type=jnp.float32
            )
            probability = prob_ref[head]
            score_grad = (probability * (prob_grad - delta)).astype(jnp.bfloat16)
            key_grad += jnp.dot(
                score_grad,
                jnp.where(mine, queries, jnp.zeros_like(queries)),
                preferred_element_type=jnp.float32,
            )
            value_grad += jnp.dot(
                probability.astype(jnp.bfloat16),
                jnp.where(mine, up_pair, jnp.zeros_like(up_pair)),
                preferred_element_type=jnp.float32,
            )
            query_parts.append(
                jnp.dot(kt_ref[at, :keys], score_grad, preferred_element_type=jnp.float32)
            )
        put(0, pair, (jnp.concatenate(query_parts, 0) * scale_factor).T)
        if upper:
            key_sum_ref[:, at_pair] = key_grad[:first_query]
            value_sum_ref[:, at_pair] = value_grad[:first_query]
            key_grad = key_grad[first_query:]
            value_grad = value_grad[first_query:]
        else:
            key_grad = key_grad + key_sum_ref[:, at_pair]
            value_grad = value_grad + value_sum_ref[:, at_pair]
        put(1, pair, key_grad * scale_factor)
        put(2, pair, value_grad)
    for step in range(replicas):
        place = place_of(info_ref, step, replicas)
        keep_ref[step] = grads_ref[place + parity]
        send_ref[step] = grads_ref[place + 1 - parity]


def norm_kernel(upper, info_ref, keep_ref, got_ref, acts_ref, incoming_ref, w_ref, out_ref, rows_ref):
    replicas, shard_rows, triple = keep_ref.shape
    columns = triple // 3
    model_width = w_ref.shape[0]
    rows = replicas * shard_rows
    parity = info_ref[0]
    for part_ref, half in ((keep_ref, parity), (got_ref, 1 - parity)):
        for block in range(3):
            first = pl.multiple_of(block * model_width + half * columns, 128)
            rows_ref[:, pl.ds(first, columns)] = part_ref[
                :, :, block * columns : (block + 1) * columns
            ].reshape(rows, columns)
    norm_grad = lax.dot_general(
        rows_ref[...], w_ref[...], (((1,), (1,)), ((), ())), preferred_element_type=jnp.float32
    )
    base = acts_ref.shape[0] // 2 if upper else 0
    values = jnp.concatenate(
        [
            acts_ref[base + place_of(info_ref, step, replicas) + parity][:, :model_width]
            for step in range(replicas)
        ],
        0,
    )
    normed, inverse_rms = normalize(values)
    inner = jnp.mean(norm_grad * normed, axis=-1, keepdims=True)
    incoming = incoming_ref[...].reshape(rows, model_width).astype(jnp.float32)
    grad_in = incoming + inverse_rms * (norm_grad - normed * inner)
    out_ref[...] = grad_in.astype(jnp.bfloat16).reshape(out_ref.shape)


def w_in_kernel(place, gt_ref, lower_ref, upper_ref, out_ref):
    count = lower_ref.shape[0] * lower_ref.shape[1]
    total = jnp.zeros(out_ref.shape, jnp.float32)
    for chunk, part_ref in enumerate((lower_ref, upper_ref)):
        total += jnp.dot(
            gt_ref[place, :, chunk * count : (chunk + 1) * count],
            part_ref[...].reshape(count, -1),
            preferred_element_type=jnp.float32,
        )
    out_ref[...] = total.astype(out_ref.dtype)


def w_out_kernel(info_ref, at_lower_ref, at_upper_ref, lower_ref, upper_ref, send_ref, own_ref):
    rows = own_ref.shape[0]
    first = pl.multiple_of(info_ref[1] * rows, 128)
    total = jnp.zeros(own_ref.shape, jnp.float32)
    for at_ref, part_ref in ((at_lower_ref, lower_ref), (at_upper_ref, upper_ref)):
        total += jnp.dot(
            at_ref[pl.ds(first, rows)],
            part_ref[...].reshape(-1, own_ref.shape[1]),
            preferred_element_type=jnp.float32,
        )
    own_ref[...] = total
    send_ref[...] = total.astype(jnp.bfloat16)


def sum_kernel(info_ref, own_ref, got_ref, keep_ref, send_ref):
    rows = keep_ref.shape[0]
    mine = pl.ds(pl.multiple_of(info_ref[0] * rows, rows), rows)
    others = pl.ds(pl.multiple_of((1 - info_ref[0]) * rows, rows), rows)
    keep_ref[...] = own_ref[mine] + got_ref[mine].astype(jnp.float32)
    send_ref[...] = (own_ref[others] + got_ref[others].astype(jnp.float32)).astype(jnp.bfloat16)


def place_in_kernel(info_ref, keep_ref, got_ref, out_ref):
    columns = keep_ref.shape[1] // 3
    for part_ref, half in ((keep_ref, info_ref[0]), (got_ref, 1 - info_ref[0])):
        for block in range(3):
            first = pl.multiple_of((2 * block + half) * columns, 128)
            out_ref[:, pl.ds(first, columns)] = part_ref[
                :, block * columns : (block + 1) * columns
            ].astype(jnp.float32)


def place_out_kernel(info_ref, keep_ref, got_ref, out_ref):
    owner = info_ref[0] == info_ref[2]

    @pl.when(owner)
    def _():
        out_ref[...] = keep_ref[...]

    @pl.when(jnp.logical_not(owner))
    def _():
        out_ref[...] = got_ref[...].astype(jnp.float32)


def call(kernel, outs, operands, scratch=(), flops=0, mebibytes=20):
    in_specs = [pl.BlockSpec(memory_space=pltpu.SMEM)] if operands[0].ndim == 1 else []
    in_specs += [pl.BlockSpec(memory_space=pltpu.VMEM)] * (len(operands) - len(in_specs))
    moved = sum(item.size * item.dtype.itemsize for item in [*operands, *outs])
    return pl.pallas_call(
        kernel,
        out_shape=list(outs),
        in_specs=in_specs,
        out_specs=[pl.BlockSpec(memory_space=pltpu.VMEM)] * len(outs),
        scratch_shapes=list(scratch),
        cost_estimate=pl.CostEstimate(flops=flops, bytes_accessed=moved, transcendentals=0),
        compiler_params=pltpu.CompilerParams(vmem_limit_bytes=mebibytes * 2**20),
    )(*operands)


def by_chips(acts, grad_top, w_in, w_out, offsets):
    half_type, full_type = jnp.bfloat16, jnp.float32
    shape = jax.ShapeDtypeStruct
    sections = lax.axis_size("section")
    shards = lax.axis_size("tm")
    levels = offsets.shape[1]
    half = shards // 2
    replicas = half // 2
    me = lax.axis_index("tm")
    parity = lax.rem(me, 2)
    side = lax.div(me, half)
    micro_count, shard_rows, model_width = acts.shape[1:]
    columns = model_width // 2
    heads = columns // HEAD_DIM
    seq = shards * shard_rows
    count = seq // 2
    w_qkv = w_in[0]
    info = jnp.stack(
        [parity, lax.div(lax.rem(me, half), 2), side, lax.axis_index("section")]
    ).astype(jnp.int32)
    across = [(source, (source + half) % shards) for source in range(shards)]
    cores = [(source, source + 1 - 2 * (source % 2)) for source in range(shards)]

    flags = jnp.zeros((1, 1, 128), half_type).at[0, 0, :levels].set(
        (offsets[0] != 0).astype(half_type)
    )
    flags = jnp.broadcast_to(flags, (micro_count, shard_rows, 128))
    payload = jnp.concatenate([acts[0], flags], 2)
    payload = jnp.repeat(payload, half, axis=0)
    acts_all = lax.all_to_all(payload, "tm", 0, 0, tiled=True)

    own_top = lax.dynamic_index_in_dim(grad_top, side, 0, False)
    other_top = lax.ppermute(
        lax.dynamic_index_in_dim(grad_top, 1 - side, 0, False), "tm", across
    )
    tops = jnp.where(side == 0, jnp.stack([own_top, other_top]), jnp.stack([other_top, own_top]))
    top_list = [tops]
    for step in range(1, replicas):
        around = [
            (source, source // half * half + (source % half + 2 * step) % half)
            for source in range(shards)
        ]
        top_list.append(lax.ppermute(tops, "tm", around))
    top_rows = jnp.stack(top_list, 1)

    pieces = [
        lax.dynamic_slice_in_dim(w_qkv, block * model_width + parity * columns, columns, 1)
        for block in range(3)
    ]
    w_rows = lax.dynamic_slice_in_dim(w_out[0], parity * columns, columns, 0)
    rows_shape = shape((seq, columns), half_type)
    norm, flag_rows, queries, keys, values, keys_t, upper_prob, upper_at = call(
        functools.partial(upper_forward_kernel, levels),
        [
            shape((seq, model_width), half_type),
            shape((128, seq), full_type),
            rows_shape,
            rows_shape,
            rows_shape,
            shape((columns, seq), half_type),
            shape((heads, seq, count), full_type),
            shape((columns, count), half_type),
        ],
        [info, acts_all, *pieces],
        flops=6 * seq * model_width * columns + 4 * columns * seq * count,
    )
    block_rows = 2 * model_width // shards
    lower_prob, lower_at, norm_t = call(
        functools.partial(lower_forward_kernel, levels, shard_rows),
        [
            shape((heads, count, count), full_type),
            shape((columns, count), half_type),
            shape((2, block_rows, seq), half_type),
        ],
        [info, norm, flag_rows, queries, keys, values],
        flops=4 * columns * count * count,
    )
    probs = {True: upper_prob, False: lower_prob}
    attended = {True: upper_at, False: lower_at}
    got = {True: top_rows[1], False: top_rows[0]}
    kept = {True: None, False: None}
    piece_shape = shape((replicas, shard_rows, model_width), half_type)
    grads_shape = shape((replicas, shard_rows, 3 * columns), half_type)
    sum_shape = shape((count, columns), full_type)
    full_grads = shape((half, shard_rows, 3 * columns), half_type)
    full_rows = shape((half, shard_rows, model_width), half_type)
    result, full, ordered = {}, {}, {}
    for turn in range(sections):
        last = turn + 1 == sections
        sums = []
        for upper in (True, False):
            got_other = lax.ppermute(got[upper], "tm", cores)
            own, other = kept[upper] if turn else (got[upper], got_other)
            outs = [piece_shape, piece_shape, grads_shape, grads_shape]
            outs += [sum_shape, sum_shape] if upper else []
            outs += [full_grads, full_rows] if last else []
            scratch = [
                pltpu.VMEM(full_rows.shape, half_type),
                pltpu.VMEM(full_grads.shape, half_type),
            ]
            part_keys = seq if upper else count
            answer = call(
                functools.partial(backward_kernel, upper, last, sections - 1 - turn),
                outs,
                [info, got[upper], got_other, own, other, w_rows, probs[upper], queries]
                + [values, keys_t, attended[upper], *sums],
                scratch=[] if last else scratch,
                flops=2 * count * columns * (model_width + 4 * part_keys),
            )
            kept[upper] = tuple(answer[:2])
            keep, send = answer[2:4]
            sums = answer[4:6] if upper else []
            if last:
                full[upper], ordered[upper] = answer[-2:]
            crossed = lax.ppermute(send, "tm", cores)
            (grad_in,) = call(
                functools.partial(norm_kernel, upper),
                [piece_shape],
                [info, keep, crossed, acts_all, kept[upper][0], w_qkv],
                scratch=[pltpu.VMEM((replicas * shard_rows, 3 * model_width), half_type)],
                flops=6 * replicas * shard_rows * model_width * model_width,
            )
            result[upper] = grad_in
            if not last:
                target = sections - 2 - turn
                got[upper] = lax.ppermute(grad_in, "section", [(target + 1, target)])

    out_send, out_own = call(
        w_out_kernel,
        [shape((block_rows, model_width), half_type), shape((block_rows, model_width), full_type)],
        [info, lower_at, upper_at, ordered[False], ordered[True]],
        flops=2 * block_rows * seq * model_width,
    )
    homeward = [pair for pair in across if pair[0] // half != pair[0] % 2]
    out_got = lax.ppermute(out_send, "tm", homeward)
    own_rows = block_rows // 2
    out_keep, out_pass = call(
        sum_kernel,
        [shape((own_rows, model_width), full_type), shape((own_rows, model_width), half_type)],
        [info, out_own, out_got],
    )
    to_sibling = [pair for pair in cores if pair[0] // half == pair[0] % 2]
    (d_w_out,) = call(
        place_out_kernel,
        [shape((own_rows, model_width), full_type)],
        [info, out_keep, lax.ppermute(out_pass, "tm", to_sibling)],
    )
    term_flops = 2 * block_rows * seq * 3 * columns
    (in_send,) = call(
        functools.partial(w_in_kernel, 0),
        [shape((block_rows, 3 * columns), half_type)],
        [norm_t, full[False], full[True]],
        flops=term_flops,
    )
    in_got = lax.ppermute(in_send, "tm", across)
    (in_own,) = call(
        functools.partial(w_in_kernel, 1),
        [shape((block_rows, 3 * columns), full_type)],
        [norm_t, full[False], full[True]],
        flops=term_flops,
    )
    in_keep, in_pass = call(
        sum_kernel,
        [shape((own_rows, 3 * columns), full_type), shape((own_rows, 3 * columns), half_type)],
        [info, in_own, in_got],
    )
    (d_w_in,) = call(
        place_in_kernel,
        [shape((own_rows, 3 * model_width), full_type)],
        [info, in_keep, lax.ppermute(in_pass, "tm", cores)],
    )

    upper_own, lower_own = result[True][0], result[False][0]
    mine = jnp.where(side == 1, upper_own, lower_own)
    partner = lax.ppermute(jnp.where(side == 1, lower_own, upper_own), "tm", across)
    d_acts = jnp.where(side == 0, jnp.stack([mine, partner]), jnp.stack([partner, mine]))
    return (d_acts[None], d_w_in[None], d_w_out[None])


def layer_gradients(acts, grad_top, w_in, w_out, offsets):
    shards = lax.axis_size("tm")
    micro_count, shard_rows, model_width = acts.shape[1:]
    heads = model_width // HEAD_DIM
    prob_bytes = 2 * heads * (shards * shard_rows) ** 2
    fits = prob_bytes <= 2**24 and model_width % (128 * shards) == 0 and shard_rows % 16 == 0
    if micro_count == 2 and shards % 4 == 0 and heads % 4 == 0 and fits:
        return by_chips(acts, grad_top, w_in, w_out, offsets)
    return per_device(acts, grad_top, w_in, w_out, offsets)


def solution(mesh):
    placed = (
        P("section", None, "tm", None),
        P(None, "tm", None),
        P("section", None, None),
        P("section", None, None),
        P("tm", None),
    )
    return jax.shard_map(
        layer_gradients,
        mesh=mesh,
        in_specs=placed,
        out_specs=(
            P("section", None, "tm", None),
            P("section", "tm", None),
            P("section", "tm", None),
        ),
        check_vma=False,
    )
```

```python
import functools
import jax
import jax.numpy as jnp
from jax import lax
from jax.experimental import pallas as pl
from jax.experimental.pallas import tpu as pltpu
from jax.sharding import PartitionSpec as P

HEAD_DIM = 64


epsilon = 1e-06
negative_fill = -1e30


def shifted(value, axis, steps):
    count = lax.axis_size(axis)
    initial, last = (max(0, -steps), min(count, count - steps))
    return lax.ppermute(value, axis, [(source, source + steps) for source in range(initial, last)])


def normalize(inputs):
    values = inputs.astype(jnp.float32)
    inverse_rms = lax.rsqrt(jnp.mean(values * values, axis=-1, keepdims=True) + epsilon)
    return (values * inverse_rms, inverse_rms)


def key_bias(level_flags, shard_rows):
    position = jnp.arange(shard_rows)
    own_part = position[None, :] <= position[:, None]
    far_part = jnp.repeat(level_flags != 0, shard_rows)
    far_part = jnp.broadcast_to(far_part[None, :], (shard_rows, far_part.shape[0]))
    return jnp.concatenate([own_part, far_part], 1)


def split_heads(row_block):
    return row_block.reshape(row_block.shape[0], -1, HEAD_DIM)


def softmax_keys(queries, key_heads, allowed):
    scores = jnp.einsum(
        "ihd,jhd->hij", queries, key_heads, preferred_element_type=jnp.float32
    ) * HEAD_DIM ** (-0.5)
    scores = jnp.where(allowed[None], scores, negative_fill)
    highest = jnp.max(scores, axis=-1, keepdims=True)
    shifted_exp = jnp.where(allowed[None], jnp.exp(scores - highest), 0.0)
    return shifted_exp / jnp.sum(shifted_exp, axis=-1, keepdims=True)


def attend(query_rows, key_rows, allowed):
    model_width = query_rows.shape[1]
    probability = softmax_keys(
        split_heads(query_rows), split_heads(key_rows[:, :model_width]), allowed
    )
    attended = jnp.einsum(
        "hij,jhd->ihd",
        probability.astype(jnp.bfloat16),
        split_heads(key_rows[:, model_width:]),
        preferred_element_type=jnp.float32,
    )
    return attended.reshape(query_rows.shape).astype(jnp.bfloat16)


def attend_back(query_rows, key_rows, allowed, incoming, attended, w_proj):
    model_width = query_rows.shape[1]
    queries = split_heads(query_rows)
    key_heads = split_heads(key_rows[:, :model_width])
    value_heads = split_heads(key_rows[:, model_width:])
    probability = softmax_keys(queries, key_heads, allowed)
    rounded = probability.astype(jnp.bfloat16)
    upstream = lax.dot_general(
        incoming, w_proj, (((1,), (1,)), ((), ())), preferred_element_type=jnp.float32
    ).astype(jnp.bfloat16)
    up_heads = split_heads(upstream)
    delta = jnp.einsum(
        "ihd,ihd->hi", up_heads.astype(jnp.float32), split_heads(attended).astype(jnp.float32)
    )[..., None]
    prob_grad = jnp.einsum(
        "ihd,jhd->hij", up_heads, value_heads, preferred_element_type=jnp.float32
    )
    score_grad = (probability * (prob_grad - delta)).astype(jnp.bfloat16)
    scale_factor = HEAD_DIM ** (-0.5)
    query_grad = (
        jnp.einsum("hij,jhd->ihd", score_grad, key_heads, preferred_element_type=jnp.float32)
        * scale_factor
    )
    key_grad = (
        jnp.einsum("hij,ihd->jhd", score_grad, queries, preferred_element_type=jnp.float32)
        * scale_factor
    )
    value_grad = jnp.einsum("hij,ihd->jhd", rounded, up_heads, preferred_element_type=jnp.float32)
    return (
        query_grad.reshape(-1, model_width),
        key_grad.reshape(-1, model_width),
        value_grad.reshape(-1, model_width),
    )


def per_device(acts, grad_top, w_in, w_out, offsets):
    sections = lax.axis_size("section")
    shards = lax.axis_size("tm")
    levels = shards.bit_length() - 1
    section_index = lax.axis_index("section")
    micro_count = acts.shape[1]
    shard_rows = acts.shape[2]
    model_width = acts.shape[3]
    w_qkv = w_in[0]
    w_proj = w_out[0]
    level_flags = offsets[0]
    normed, inverse_rms = normalize(acts[0])
    rounded_norm = normed.astype(jnp.bfloat16)
    qkv = jnp.dot(rounded_norm.reshape(-1, model_width), w_qkv, preferred_element_type=jnp.float32)
    qkv = qkv.astype(jnp.bfloat16).reshape(micro_count, shard_rows, 3 * model_width)
    pairs = qkv[..., model_width:]
    far_list = [shifted(pairs, "tm", 2**level) for level in range(levels)]
    key_rows = jnp.concatenate([pairs] + far_list, 1)
    allowed = key_bias(level_flags, shard_rows)
    attended = jnp.stack(
        [
            attend(qkv[index, :, :model_width], key_rows[index], allowed)
            for index in range(micro_count)
        ],
        0,
    )

    def attention_part(incoming, slot):
        query_rows = lax.dynamic_index_in_dim(qkv, slot, 0, False)[:, :model_width]
        slot_keys = lax.dynamic_index_in_dim(key_rows, slot, 0, False)
        slot_attended = lax.dynamic_index_in_dim(attended, slot, 0, False)
        query_grad, key_grad, value_grad = attend_back(
            query_rows, slot_keys, allowed, incoming, slot_attended, w_proj
        )
        owner_sum = jnp.concatenate([key_grad[:shard_rows], value_grad[:shard_rows]], 1)
        far_part = jnp.concatenate([key_grad[shard_rows:], value_grad[shard_rows:]], 1)
        far_part = far_part.astype(jnp.bfloat16).reshape(levels, shard_rows, 2 * model_width)
        return (query_grad, owner_sum, far_part)

    def empty_attention(incoming, slot):
        return (
            jnp.zeros((shard_rows, model_width), jnp.float32),
            jnp.zeros((shard_rows, 2 * model_width), jnp.float32),
            jnp.zeros((levels, shard_rows, 2 * model_width), jnp.bfloat16),
        )

    def norm_part(qkv_grad, incoming, slot):
        norm_grad = lax.dot_general(
            qkv_grad, w_qkv, (((1,), (1,)), ((), ())), preferred_element_type=jnp.float32
        )
        slot_normed = lax.dynamic_index_in_dim(normed, slot, 0, False)
        slot_rms = lax.dynamic_index_in_dim(inverse_rms, slot, 0, False)
        inner = jnp.mean(norm_grad * slot_normed, axis=-1, keepdims=True)
        return (incoming.astype(jnp.float32) + slot_rms * (norm_grad - slot_normed * inner)).astype(
            jnp.bfloat16
        )

    def empty_norm(qkv_grad, incoming, slot):
        return jnp.zeros((shard_rows, model_width), jnp.bfloat16)

    def step(turn, carry):
        received, grad_store, qkv_store, incoming_store = carry
        slot_raw = turn - (sections - 1 - section_index)
        active = (slot_raw >= 0) & (slot_raw < micro_count)
        slot = jnp.clip(slot_raw, 0, micro_count - 1)
        incoming = jnp.where(
            section_index == sections - 1,
            lax.dynamic_index_in_dim(grad_top, slot, 0, False),
            received,
        )
        query_grad, owner_sum, far_part = lax.cond(
            active, attention_part, empty_attention, incoming, slot
        )
        for level in range(levels):
            owner_sum = owner_sum + shifted(far_part[level], "tm", -(2**level)).astype(jnp.float32)
        qkv_grad = jnp.concatenate([query_grad, owner_sum], 1).astype(jnp.bfloat16)
        grad_in = lax.cond(active, norm_part, empty_norm, qkv_grad, incoming, slot)
        sent_down = shifted(grad_in, "section", -1)
        grad_store = jnp.where(
            active, lax.dynamic_update_index_in_dim(grad_store, grad_in, slot, 0), grad_store
        )
        qkv_store = jnp.where(
            active, lax.dynamic_update_index_in_dim(qkv_store, qkv_grad, slot, 0), qkv_store
        )
        incoming_store = jnp.where(
            active,
            lax.dynamic_update_index_in_dim(incoming_store, incoming, slot, 0),
            incoming_store,
        )
        return (sent_down, grad_store, qkv_store, incoming_store)

    initial = (
        jnp.zeros((shard_rows, model_width), jnp.bfloat16),
        jnp.zeros((micro_count, shard_rows, model_width), jnp.bfloat16),
        jnp.zeros((micro_count, shard_rows, 3 * model_width), jnp.bfloat16),
        jnp.zeros((micro_count, shard_rows, model_width), jnp.bfloat16),
    )
    received, grad_store, qkv_store, incoming_store = lax.fori_loop(
        0, sections + micro_count - 1, step, initial
    )
    flat_norm = rounded_norm.reshape(-1, model_width)
    flat_attended = attended.reshape(-1, model_width)
    flat_qkv = qkv_store.reshape(-1, 3 * model_width)
    flat_incoming = incoming_store.reshape(-1, model_width)
    contract = (((0,), (0,)), ((), ()))
    first = lax.dot_general(flat_norm, flat_qkv, contract, preferred_element_type=jnp.float32)
    second = lax.dot_general(
        flat_attended, flat_incoming, contract, preferred_element_type=jnp.float32
    )
    summed = lax.psum_scatter(
        jnp.concatenate([first, second], 1).astype(jnp.bfloat16),
        "tm",
        scatter_dimension=0,
        tiled=True,
    ).astype(jnp.float32)
    return (
        grad_store[None],
        summed[None, :, : 3 * model_width],
        summed[None, :, 3 * model_width :],
    )


def pair_rows(transposed, head):
    width = 2 * HEAD_DIM
    pair = transposed[head // 2 * width : (head // 2 + 1) * width]
    empty = jnp.zeros((HEAD_DIM, pair.shape[1]), pair.dtype)
    if head % 2 == 0:
        return jnp.concatenate([pair[:HEAD_DIM], empty], 0)
    return jnp.concatenate([empty, pair[HEAD_DIM:]], 0)


def allowed_keys(flag_rows, levels, shard_rows, keys, first_query, count):
    key_at = lax.broadcasted_iota(jnp.int32, (keys, count), 0)
    query_at = lax.broadcasted_iota(jnp.int32, (keys, count), 1) + first_query
    gap = lax.div(query_at, shard_rows) - lax.div(key_at, shard_rows)
    allowed = (gap == 0) & (key_at <= query_at)
    for level in range(levels):
        allowed = allowed | ((gap == 2**level) & (flag_rows[level : level + 1] != 0))
    return allowed


def softmax_pass(queries, keys, values, allowed, prob_ref, at_ref):
    queries_t = queries.T
    values_t = values.T
    width = 2 * HEAD_DIM
    for head in range(queries.shape[1] // HEAD_DIM):
        at = slice(head * HEAD_DIM, (head + 1) * HEAD_DIM)
        pair = slice(head // 2 * width, (head // 2 + 1) * width)
        scores = jnp.dot(
            keys[:, pair], pair_rows(queries_t, head), preferred_element_type=jnp.float32
        )
        scores = jnp.where(allowed, scores, negative_fill)
        shifted_exp = jnp.exp(scores - jnp.max(scores, axis=0, keepdims=True))
        probability = shifted_exp * (1.0 / jnp.sum(shifted_exp, axis=0, keepdims=True))
        prob_ref[head] = probability
        at_ref[at] = jnp.dot(
            values_t[at], probability.astype(jnp.bfloat16), preferred_element_type=jnp.float32
        ).astype(jnp.bfloat16)


def pack_kernel(
    levels, info_ref, offsets_ref, acts_ref, top_ref, own_ref, other_ref, own_top_ref, other_top_ref
):
    shard_rows, model_width = acts_ref.shape[1:]
    lane = lax.broadcasted_iota(jnp.int32, (shard_rows, own_ref.shape[1] - model_width), 1)
    flags = jnp.zeros(lane.shape, jnp.float32)
    for level in range(levels):
        seen = jnp.where(offsets_ref[0, level] != 0, 1.0, 0.0)
        flags = jnp.where(lane == level, seen, flags)
    for side, out_ref, out_top_ref in (
        (info_ref[2], own_ref, own_top_ref),
        (1 - info_ref[2], other_ref, other_top_ref),
    ):
        out_ref[:, :model_width] = acts_ref[side]
        out_ref[:, model_width:] = flags.astype(jnp.bfloat16)
        out_top_ref[...] = top_ref[side]


def project_kernel(replicas, info_ref, *refs):
    pieces = refs[: 4 * replicas]
    w_ref, acts_ref, norm_ref, flag_ref, q_ref, k_ref, v_ref, kt_ref, packed_ref = refs[
        4 * replicas :
    ]
    shards, shard_rows, model_width = acts_ref.shape
    seq = shards * shard_rows
    columns = q_ref.shape[1]
    at_piece = 0
    for core in (info_ref[0], 1 - info_ref[0]):
        for side in (info_ref[2], 1 - info_ref[2]):
            for step in range(replicas):
                shard = side * (shards // 2) + place_of(info_ref, step, replicas) + core
                packed_ref[shard] = pieces[at_piece][...]
                at_piece += 1
    acts_ref[...] = packed_ref[:, :, :model_width]
    normed, _ = normalize(acts_ref[...].reshape(seq, model_width))
    rounded = normed.astype(jnp.bfloat16)
    norm_ref[...] = rounded
    flag_ref[...] = packed_ref[:, :, model_width:].reshape(seq, -1).astype(jnp.float32).T
    scale_factor = HEAD_DIM ** (-0.5)
    for block, out_ref in enumerate((q_ref, k_ref, v_ref)):
        first = pl.multiple_of(block * model_width + info_ref[0] * columns, 128)
        product = jnp.dot(
            rounded, w_ref[:, pl.ds(first, columns)], preferred_element_type=jnp.float32
        ).astype(jnp.bfloat16)
        out_ref[...] = product * scale_factor if block == 0 else product
    kt_ref[...] = (k_ref[...] * scale_factor).T


def upper_forward_kernel(levels, shard_rows, flag_ref, q_ref, k_ref, v_ref, prob_ref, at_ref):
    seq = q_ref.shape[0]
    count = seq // 2
    allowed = allowed_keys(flag_ref[:, count:], levels, shard_rows, seq, count, count)
    softmax_pass(q_ref[count:], k_ref[...], v_ref[...], allowed, prob_ref, at_ref)


def lower_forward_kernel(
    levels, shard_rows, info_ref, norm_ref, flag_ref, q_ref, k_ref, v_ref, prob_ref, at_ref, gt_ref
):
    seq = norm_ref.shape[0]
    count = seq // 2
    allowed = allowed_keys(flag_ref[:, :count], levels, shard_rows, count, 0, count)
    softmax_pass(q_ref[:count], k_ref[:count], v_ref[:count], allowed, prob_ref, at_ref)
    rows = gt_ref.shape[1]
    half_width = norm_ref.shape[1] // 2
    for place in range(2):
        half = 1 - info_ref[2] if place == 0 else info_ref[2]
        first = pl.multiple_of(half * half_width + info_ref[1] * rows, 128)
        gt_ref[place] = norm_ref[:, pl.ds(first, rows)].T


def place_of(info_ref, step, replicas):
    return 2 * lax.rem(info_ref[1] - step + replicas, replicas)


def merge_rows(info_ref, fresh, got_refs, kept_refs, out_refs, rows_ref):
    @pl.when(fresh)
    def _():
        for out_ref, got_ref in zip(out_refs, got_refs):
            out_ref[...] = got_ref[...]

    @pl.when(jnp.logical_not(fresh))
    def _():
        for out_ref, kept_ref in zip(out_refs, kept_refs):
            out_ref[...] = kept_ref[...]

    place_rows(info_ref, out_refs, rows_ref)


def place_rows(info_ref, out_refs, rows_ref):
    replicas = out_refs[0].shape[0]
    for step in range(replicas):
        place = place_of(info_ref, step, replicas)
        rows_ref[place + info_ref[0]] = out_refs[0][step]
        rows_ref[place + 1 - info_ref[0]] = out_refs[1][step]


def merge_tops(info_ref, upper, piece_refs, out_refs, rows_ref):
    replicas = out_refs[0].shape[0]
    own_chunk = info_ref[2] == (1 if upper else 0)
    for core in range(2):
        refs = piece_refs[2 * replicas * core : 2 * replicas * (core + 1)]

        @pl.when(own_chunk)
        def _():
            for step in range(replicas):
                out_refs[core][step] = refs[step][...]

        @pl.when(jnp.logical_not(own_chunk))
        def _():
            for step in range(replicas):
                out_refs[core][step] = refs[replicas + step][...]

    place_rows(info_ref, out_refs, rows_ref)


def backward_kernel(upper, tops, fresh_section, info_ref, *refs):
    refs = list(refs)
    got = tops or 4
    got_refs = refs[:got]
    w_ref, prob_ref, q_ref, v_ref, kt_ref, at_ref = refs[got : got + 6]
    refs = refs[got + 6 :]
    if not upper:
        key_sum_ref, value_sum_ref, _ = refs[:3]
        refs = refs[3:]
    own_ref, other_ref, keep_ref, send_ref = refs[:4]
    refs = refs[4:]
    if upper:
        key_sum_ref, value_sum_ref = refs[:2]
        refs = refs[2:]
    grads_ref, rows_ref = refs
    replicas, shard_rows, model_width = own_ref.shape
    count = rows_ref.shape[0] * shard_rows
    keys = prob_ref.shape[1]
    parity = info_ref[0]
    columns = q_ref.shape[1]
    width = 2 * HEAD_DIM
    if tops:
        merge_tops(info_ref, upper, got_refs, (own_ref, other_ref), rows_ref)
    else:
        fresh = info_ref[3] == fresh_section
        merge_rows(info_ref, fresh, got_refs[:2], got_refs[2:], (own_ref, other_ref), rows_ref)
    rows = rows_ref[...].reshape(count, model_width)
    weights = w_ref[pl.ds(pl.multiple_of(parity * columns, 128), columns), :]
    over_width = (((1,), (1,)), ((), ()))
    upstream = lax.dot_general(
        rows, weights, over_width, preferred_element_type=jnp.float32
    ).astype(jnp.bfloat16)
    upstream_t = lax.dot_general(
        weights, rows, over_width, preferred_element_type=jnp.float32
    ).astype(jnp.bfloat16)
    product_t = upstream_t.astype(jnp.float32) * at_ref[...].astype(jnp.float32)
    first_query = keys - count
    lane = lax.broadcasted_iota(jnp.int32, (1, width), 1)
    head_masks = [
        jnp.where(lane < HEAD_DIM, 1.0, 0.0).astype(jnp.bfloat16),
        jnp.where(lane < HEAD_DIM, 0.0, 1.0).astype(jnp.bfloat16),
    ]

    def put(block, pair, part):
        first = block * columns + pair * width
        grads_ref[:, :, first : first + width] = part.astype(jnp.bfloat16).reshape(
            -1, shard_rows, width
        )

    for pair in range(columns // width):
        at_pair = slice(pair * width, (pair + 1) * width)
        values = v_ref[:keys, at_pair]
        queries = q_ref[first_query : first_query + count, at_pair]
        up_pair = upstream[:, at_pair]
        key_grad = jnp.zeros((keys, width), jnp.float32)
        value_grad = jnp.zeros((keys, width), jnp.float32)
        query_parts = []
        for head in (2 * pair, 2 * pair + 1):
            at = slice(head * HEAD_DIM, (head + 1) * HEAD_DIM)
            mask = head_masks[head % 2]
            delta = jnp.sum(product_t[at], axis=0, keepdims=True)
            prob_grad = jnp.dot(
                values, pair_rows(upstream_t, head), preferred_element_type=jnp.float32
            )
            probability = prob_ref[head]
            score_grad = (probability * (prob_grad - delta)).astype(jnp.bfloat16)
            key_grad += jnp.dot(score_grad, queries * mask, preferred_element_type=jnp.float32)
            value_grad += jnp.dot(
                probability.astype(jnp.bfloat16), up_pair * mask, preferred_element_type=jnp.float32
            )
            query_parts.append(
                jnp.dot(kt_ref[at, :keys], score_grad, preferred_element_type=jnp.float32)
            )
        put(0, pair, jnp.concatenate(query_parts, 0).astype(jnp.bfloat16).T)
        if upper:
            key_sum_ref[:, at_pair] = key_grad[:first_query]
            value_sum_ref[:, at_pair] = value_grad[:first_query]
            key_grad = key_grad[first_query:]
            value_grad = value_grad[first_query:]
        else:
            key_grad = key_grad + key_sum_ref[:, at_pair]
            value_grad = value_grad + value_sum_ref[:, at_pair]
        put(1, pair, key_grad)
        put(2, pair, value_grad)
    for step in range(replicas):
        place = place_of(info_ref, step, replicas)
        keep_ref[step] = grads_ref[place + parity]
        send_ref[step] = grads_ref[place + 1 - parity]


def norm_kernel(
    upper, info_ref, keep_ref, got_ref, acts_ref, incoming_ref, w_ref, after_ref, out_ref, rows_ref
):
    replicas, shard_rows, triple = keep_ref.shape
    columns = triple // 3
    model_width = w_ref.shape[0]
    rows = replicas * shard_rows
    parity = info_ref[0]
    for part_ref, half in ((keep_ref, parity), (got_ref, 1 - parity)):
        for block in range(3):
            first = pl.multiple_of(block * model_width + half * columns, 128)
            rows_ref[:, pl.ds(first, columns)] = part_ref[
                :, :, block * columns : (block + 1) * columns
            ].reshape(rows, columns)
    norm_grad = lax.dot_general(
        rows_ref[...], w_ref[...], (((1,), (1,)), ((), ())), preferred_element_type=jnp.float32
    )
    base = acts_ref.shape[0] // 2 if upper else 0
    values = jnp.concatenate(
        [
            acts_ref[base + place_of(info_ref, step, replicas) + parity]
            for step in range(replicas)
        ],
        0,
    )
    normed, inverse_rms = normalize(values)
    inner = jnp.mean(norm_grad * normed, axis=-1, keepdims=True)
    incoming = incoming_ref[...].reshape(rows, model_width).astype(jnp.float32)
    grad_in = incoming + inverse_rms * (norm_grad - normed * inner)
    out_ref[...] = grad_in.astype(jnp.bfloat16).reshape(out_ref.shape)


def w_in_kernel(place, gt_ref, lower_ref, upper_ref, out_ref):
    count = lower_ref.shape[0] * lower_ref.shape[1]
    total = jnp.zeros(out_ref.shape, jnp.float32)
    for chunk, part_ref in enumerate((lower_ref, upper_ref)):
        total += jnp.dot(
            gt_ref[place, :, chunk * count : (chunk + 1) * count],
            part_ref[...].reshape(count, -1),
            preferred_element_type=jnp.float32,
        )
    out_ref[...] = total.astype(out_ref.dtype)


def w_out_kernel(fresh_section, info_ref, *refs):
    got_refs, kept_refs = refs[:2], refs[2:4]
    at_lower_ref, at_upper_ref, upper_ref, send_ref, own_ref, part_ref, part_other_ref, rows_ref = (
        refs[4:]
    )
    merge_rows(
        info_ref,
        info_ref[3] == fresh_section,
        got_refs,
        kept_refs,
        (part_ref, part_other_ref),
        rows_ref,
    )
    rows = own_ref.shape[0]
    first = pl.multiple_of(info_ref[1] * rows, 128)
    total = jnp.zeros(own_ref.shape, jnp.float32)
    for at_ref, chunk_ref in ((at_lower_ref, rows_ref), (at_upper_ref, upper_ref)):
        total += jnp.dot(
            at_ref[pl.ds(first, rows)],
            chunk_ref[...].reshape(-1, own_ref.shape[1]),
            preferred_element_type=jnp.float32,
        )
    own_ref[...] = total
    send_ref[...] = total.astype(jnp.bfloat16)


def sum_kernel(info_ref, own_ref, got_ref, keep_ref, send_ref):
    rows = keep_ref.shape[0]
    mine = pl.ds(pl.multiple_of(info_ref[0] * rows, rows), rows)
    others = pl.ds(pl.multiple_of((1 - info_ref[0]) * rows, rows), rows)
    keep_ref[...] = own_ref[mine] + got_ref[mine].astype(jnp.float32)
    send_ref[...] = (own_ref[others] + got_ref[others].astype(jnp.float32)).astype(jnp.bfloat16)


def place_in_kernel(info_ref, keep_ref, got_ref, out_ref):
    columns = keep_ref.shape[1] // 3
    for part_ref, half in ((keep_ref, info_ref[0]), (got_ref, 1 - info_ref[0])):
        for block in range(3):
            first = pl.multiple_of((2 * block + half) * columns, 128)
            out_ref[:, pl.ds(first, columns)] = part_ref[
                :, block * columns : (block + 1) * columns
            ].astype(jnp.float32)


def place_out_kernel(info_ref, keep_ref, got_ref, out_ref):
    owner = info_ref[0] == info_ref[2]

    @pl.when(owner)
    def _():
        out_ref[...] = keep_ref[...]

    @pl.when(jnp.logical_not(owner))
    def _():
        out_ref[...] = got_ref[...].astype(jnp.float32)


def call(kernel, outs, operands, scratch=(), flops=0, scalars=1, after=None, mebibytes=16):
    in_specs = [pl.BlockSpec(memory_space=pltpu.SMEM)] * scalars
    in_specs += [pl.BlockSpec(memory_space=pltpu.VMEM)] * (len(operands) - scalars)
    moved = sum(item.size * item.dtype.itemsize for item in [*operands, *outs])
    if after is not None:
        operands = [*operands, after]
        in_specs.append(pl.BlockSpec(memory_space=pl.ANY))
    return pl.pallas_call(
        kernel,
        out_shape=list(outs),
        in_specs=in_specs,
        out_specs=[pl.BlockSpec(memory_space=pltpu.VMEM)] * len(outs),
        scratch_shapes=list(scratch),
        cost_estimate=pl.CostEstimate(flops=flops, bytes_accessed=moved, transcendentals=0),
        compiler_params=pltpu.CompilerParams(vmem_limit_bytes=mebibytes * 2**20),
    )(*operands)


def by_chips(acts, grad_top, w_in, w_out, offsets):
    half_type, full_type = jnp.bfloat16, jnp.float32
    shape = jax.ShapeDtypeStruct
    sections = lax.axis_size("section")
    shards = lax.axis_size("tm")
    levels = offsets.shape[1]
    half = shards // 2
    replicas = half // 2
    me = lax.axis_index("tm")
    parity = lax.rem(me, 2)
    side = lax.div(me, half)
    micro_count, shard_rows, model_width = acts.shape[1:]
    columns = model_width // 2
    heads = columns // HEAD_DIM
    seq = shards * shard_rows
    count = seq // 2
    w_qkv = w_in[0]
    w_rows = w_out[0]
    info = jnp.stack(
        [parity, lax.div(lax.rem(me, half), 2), side, lax.axis_index("section")]
    ).astype(jnp.int32)
    across = [(source, (source + half) % shards) for source in range(shards)]
    cores = [(source, source + 1 - 2 * (source % 2)) for source in range(shards)]
    homeward = [pair for pair in across if pair[0] // half != pair[0] % 2]
    around = [
        [
            (source, source // half * half + (source % half + 2 * step) % half)
            for source in range(shards)
        ]
        for step in range(replicas)
    ]

    packed = shape((shard_rows, model_width + 128), half_type)
    top_shape = shape((shard_rows, model_width), half_type)
    own_acts, other_acts, own_top, other_top = call(
        functools.partial(pack_kernel, levels),
        [packed, packed, top_shape, top_shape],
        [info, offsets, acts[0], grad_top],
        scalars=2,
    )
    swapped = lax.ppermute(other_acts, "tm", across)
    pieces = [own_acts]
    pieces += [lax.ppermute(own_acts, "tm", around[step]) for step in range(1, replicas)]
    pieces += [swapped]
    pieces += [lax.ppermute(swapped, "tm", around[step]) for step in range(1, replicas)]
    pieces += [lax.ppermute(piece, "tm", cores) for piece in pieces]
    other_top, _ = lax.optimization_barrier((other_top, own_acts))
    other_top = lax.ppermute(other_top, "tm", across)
    other_top, _ = lax.optimization_barrier((other_top, swapped))
    tops = [own_top]
    tops += [lax.ppermute(own_top, "tm", around[step]) for step in range(1, replicas)]
    tops += [other_top]
    tops += [lax.ppermute(other_top, "tm", around[step]) for step in range(1, replicas)]

    rows_shape = shape((seq, columns), half_type)
    acts_all, norm, flag_rows, queries, keys, values, keys_t = call(
        functools.partial(project_kernel, replicas),
        [
            shape((shards, shard_rows, model_width), half_type),
            shape((seq, model_width), half_type),
            shape((128, seq), full_type),
            rows_shape,
            rows_shape,
            rows_shape,
            shape((columns, seq), half_type),
        ],
        [info, *pieces, w_qkv],
        scratch=[pltpu.VMEM((shards, *packed.shape), half_type)],
        flops=6 * seq * model_width * columns,
    )
    tops, _ = lax.optimization_barrier((tuple(tops), keys_t))
    tops = [*tops, *[lax.ppermute(piece, "tm", cores) for piece in tops]]
    upper_prob, upper_at = call(
        functools.partial(upper_forward_kernel, levels, shard_rows),
        [shape((heads, seq, count), full_type), shape((columns, count), half_type)],
        [flag_rows, queries, keys, values],
        scalars=0,
        flops=4 * columns * seq * count,
    )
    block_rows = 2 * model_width // shards
    lower_prob, lower_at, norm_t = call(
        functools.partial(lower_forward_kernel, levels, shard_rows),
        [
            shape((heads, count, count), full_type),
            shape((columns, count), half_type),
            shape((2, block_rows, seq), half_type),
        ],
        [info, norm, flag_rows, queries, keys, values],
        flops=4 * columns * count * count,
    )
    probs = {True: upper_prob, False: lower_prob}
    attended = {True: upper_at, False: lower_at}
    got, kept = {}, {}
    piece_shape = shape((replicas, shard_rows, model_width), half_type)
    grads_shape = shape((replicas, shard_rows, 3 * columns), half_type)
    sum_shape = shape((count, columns), full_type)
    full_grads = shape((half, shard_rows, 3 * columns), half_type)
    full_rows = shape((half, shard_rows, model_width), half_type)
    rows_scratch = pltpu.VMEM(full_rows.shape, half_type)
    grads_scratch = pltpu.VMEM(full_grads.shape, half_type)
    result, full = {}, {}
    grad_in = keys_t
    for turn in range(sections):
        last = turn + 1 == sections
        fresh_section = sections - 1 - turn
        sums, parts, crossed = [], {}, {}
        for upper in (True, False):
            rows_in = tops
            if turn:
                before = result[False] if upper else keep
                got[upper], before = lax.optimization_barrier((got[upper], before))
                if upper:
                    result[False] = before
                else:
                    keep = parts[True] = before
                got_other = lax.ppermute(got[upper], "tm", cores)
                rows_in = [got[upper], got_other, *kept[upper]]
            after = None
            if last and not upper:
                out_send, out_own = call(
                    functools.partial(w_out_kernel, fresh_section),
                    [
                        shape((block_rows, model_width), half_type),
                        shape((block_rows, model_width), full_type),
                    ],
                    [info, *rows_in, lower_at, upper_at, ordered],
                    scratch=[
                        pltpu.VMEM(piece_shape.shape, half_type),
                        pltpu.VMEM(piece_shape.shape, half_type),
                        rows_scratch,
                    ],
                    flops=2 * block_rows * seq * model_width,
                )
                after = out_send
            elif not upper:
                after = keep
            outs = [piece_shape, piece_shape, grads_shape, grads_shape]
            outs += [sum_shape, sum_shape] if upper else []
            scratch = []
            if last:
                outs += [full_grads]
            else:
                scratch += [grads_scratch]
            if last and upper:
                outs += [full_rows]
            else:
                scratch += [rows_scratch]
            part_keys = seq if upper else count
            answer = call(
                functools.partial(backward_kernel, upper, 0 if turn else len(tops), fresh_section),
                outs,
                [info, *rows_in, w_rows, probs[upper], queries, values, keys_t]
                + [attended[upper], *sums],
                scratch=scratch,
                flops=2 * count * columns * (2 * model_width + 4 * part_keys),
                after=after,
            )
            kept[upper] = tuple(answer[:2])
            keep, send = answer[2:4]
            parts[upper] = keep
            if upper:
                sums = answer[4:6]
            if last:
                full[upper] = answer[6 if upper else 4]
            if last and upper:
                ordered = answer[7]
            crossed[upper] = lax.ppermute(send, "tm", cores)
        if last:
            out_got = lax.ppermute(out_send, "tm", homeward)
        for upper in (True, False):
            (grad_in,) = call(
                functools.partial(norm_kernel, upper),
                [piece_shape],
                [info, parts[upper], crossed[upper], acts_all, kept[upper][0], w_qkv],
                scratch=[pltpu.VMEM((replicas * shard_rows, 3 * model_width), half_type)],
                flops=6 * replicas * shard_rows * model_width * model_width,
                after=out_got if last else grad_in,
            )
            result[upper] = grad_in
            if not last:
                target = sections - 2 - turn
                got[upper] = lax.ppermute(grad_in, "section", [(target + 1, target)])

    own_rows = block_rows // 2
    term_flops = 2 * block_rows * seq * 3 * columns
    (in_send,) = call(
        functools.partial(w_in_kernel, 0),
        [shape((block_rows, 3 * columns), half_type)],
        [norm_t, full[False], full[True]],
        flops=term_flops,
        scalars=0,
    )
    in_got = lax.ppermute(in_send, "tm", across)
    (in_own,) = call(
        functools.partial(w_in_kernel, 1),
        [shape((block_rows, 3 * columns), full_type)],
        [norm_t, full[False], full[True]],
        flops=term_flops,
        scalars=0,
    )
    out_keep, out_pass = call(
        sum_kernel,
        [shape((own_rows, model_width), full_type), shape((own_rows, model_width), half_type)],
        [info, out_own, out_got],
    )
    to_sibling = [pair for pair in cores if pair[0] // half == pair[0] % 2]
    (d_w_out,) = call(
        place_out_kernel,
        [shape((own_rows, model_width), full_type)],
        [info, out_keep, lax.ppermute(out_pass, "tm", to_sibling)],
    )
    in_keep, in_pass = call(
        sum_kernel,
        [shape((own_rows, 3 * columns), full_type), shape((own_rows, 3 * columns), half_type)],
        [info, in_own, in_got],
    )
    (d_w_in,) = call(
        place_in_kernel,
        [shape((own_rows, 3 * model_width), full_type)],
        [info, in_keep, lax.ppermute(in_pass, "tm", cores)],
    )

    upper_own, lower_own = result[True][0], result[False][0]
    mine = jnp.where(side == 1, upper_own, lower_own)
    partner = lax.ppermute(jnp.where(side == 1, lower_own, upper_own), "tm", across)
    d_acts = jnp.where(side == 0, jnp.stack([mine, partner]), jnp.stack([partner, mine]))
    return (d_acts[None], d_w_in[None], d_w_out[None])


def layer_gradients(acts, grad_top, w_in, w_out, offsets):
    shards = lax.axis_size("tm")
    micro_count, shard_rows, model_width = acts.shape[1:]
    heads = model_width // HEAD_DIM
    prob_bytes = 2 * heads * (shards * shard_rows) ** 2
    fits = prob_bytes <= 2**24 and model_width % (128 * shards) == 0 and shard_rows % 16 == 0
    if micro_count == 2 and shards % 4 == 0 and heads % 4 == 0 and fits:
        return by_chips(acts, grad_top, w_in, w_out, offsets)
    return per_device(acts, grad_top, w_in, w_out, offsets)


def solution(mesh):
    placed = (
        P("section", None, "tm", None),
        P(None, "tm", None),
        P("section", None, None),
        P("section", None, None),
        P("tm", None),
    )
    return jax.shard_map(
        layer_gradients,
        mesh=mesh,
        in_specs=placed,
        out_specs=(
            P("section", None, "tm", None),
            P("section", "tm", None),
            P("section", "tm", None),
        ),
        check_vma=False,
    )
```

```python
import functools
import jax
import jax.numpy as jnp
from jax import lax
from jax.experimental import pallas as pl
from jax.experimental.pallas import tpu as pltpu
from jax.sharding import PartitionSpec as P

HEAD_DIM = 64


epsilon = 1e-06
negative_fill = -1e30


def shifted(value, axis, steps):
    count = lax.axis_size(axis)
    initial, last = (max(0, -steps), min(count, count - steps))
    return lax.ppermute(value, axis, [(source, source + steps) for source in range(initial, last)])


def normalize(inputs):
    values = inputs.astype(jnp.float32)
    inverse_rms = lax.rsqrt(jnp.mean(values * values, axis=-1, keepdims=True) + epsilon)
    return (values * inverse_rms, inverse_rms)


def key_bias(level_flags, shard_rows):
    position = jnp.arange(shard_rows)
    own_part = position[None, :] <= position[:, None]
    far_part = jnp.repeat(level_flags != 0, shard_rows)
    far_part = jnp.broadcast_to(far_part[None, :], (shard_rows, far_part.shape[0]))
    return jnp.concatenate([own_part, far_part], 1)


def split_heads(row_block):
    return row_block.reshape(row_block.shape[0], -1, HEAD_DIM)


def softmax_keys(queries, key_heads, allowed):
    scores = jnp.einsum(
        "ihd,jhd->hij", queries, key_heads, preferred_element_type=jnp.float32
    ) * HEAD_DIM ** (-0.5)
    scores = jnp.where(allowed[None], scores, negative_fill)
    highest = jnp.max(scores, axis=-1, keepdims=True)
    shifted_exp = jnp.where(allowed[None], jnp.exp(scores - highest), 0.0)
    return shifted_exp / jnp.sum(shifted_exp, axis=-1, keepdims=True)


def attend(query_rows, key_rows, allowed):
    model_width = query_rows.shape[1]
    probability = softmax_keys(
        split_heads(query_rows), split_heads(key_rows[:, :model_width]), allowed
    )
    attended = jnp.einsum(
        "hij,jhd->ihd",
        probability.astype(jnp.bfloat16),
        split_heads(key_rows[:, model_width:]),
        preferred_element_type=jnp.float32,
    )
    return attended.reshape(query_rows.shape).astype(jnp.bfloat16)


def attend_back(query_rows, key_rows, allowed, incoming, attended, w_proj):
    model_width = query_rows.shape[1]
    queries = split_heads(query_rows)
    key_heads = split_heads(key_rows[:, :model_width])
    value_heads = split_heads(key_rows[:, model_width:])
    probability = softmax_keys(queries, key_heads, allowed)
    rounded = probability.astype(jnp.bfloat16)
    upstream = lax.dot_general(
        incoming, w_proj, (((1,), (1,)), ((), ())), preferred_element_type=jnp.float32
    ).astype(jnp.bfloat16)
    up_heads = split_heads(upstream)
    delta = jnp.einsum(
        "ihd,ihd->hi", up_heads.astype(jnp.float32), split_heads(attended).astype(jnp.float32)
    )[..., None]
    prob_grad = jnp.einsum(
        "ihd,jhd->hij", up_heads, value_heads, preferred_element_type=jnp.float32
    )
    score_grad = (probability * (prob_grad - delta)).astype(jnp.bfloat16)
    scale_factor = HEAD_DIM ** (-0.5)
    query_grad = (
        jnp.einsum("hij,jhd->ihd", score_grad, key_heads, preferred_element_type=jnp.float32)
        * scale_factor
    )
    key_grad = (
        jnp.einsum("hij,ihd->jhd", score_grad, queries, preferred_element_type=jnp.float32)
        * scale_factor
    )
    value_grad = jnp.einsum("hij,ihd->jhd", rounded, up_heads, preferred_element_type=jnp.float32)
    return (
        query_grad.reshape(-1, model_width),
        key_grad.reshape(-1, model_width),
        value_grad.reshape(-1, model_width),
    )


def per_device(acts, grad_top, w_in, w_out, offsets):
    sections = lax.axis_size("section")
    shards = lax.axis_size("tm")
    levels = shards.bit_length() - 1
    section_index = lax.axis_index("section")
    micro_count = acts.shape[1]
    shard_rows = acts.shape[2]
    model_width = acts.shape[3]
    w_qkv = w_in[0]
    w_proj = w_out[0]
    level_flags = offsets[0]
    normed, inverse_rms = normalize(acts[0])
    rounded_norm = normed.astype(jnp.bfloat16)
    qkv = jnp.dot(rounded_norm.reshape(-1, model_width), w_qkv, preferred_element_type=jnp.float32)
    qkv = qkv.astype(jnp.bfloat16).reshape(micro_count, shard_rows, 3 * model_width)
    pairs = qkv[..., model_width:]
    far_list = [shifted(pairs, "tm", 2**level) for level in range(levels)]
    key_rows = jnp.concatenate([pairs] + far_list, 1)
    allowed = key_bias(level_flags, shard_rows)
    attended = jnp.stack(
        [
            attend(qkv[index, :, :model_width], key_rows[index], allowed)
            for index in range(micro_count)
        ],
        0,
    )

    def attention_part(incoming, slot):
        query_rows = lax.dynamic_index_in_dim(qkv, slot, 0, False)[:, :model_width]
        slot_keys = lax.dynamic_index_in_dim(key_rows, slot, 0, False)
        slot_attended = lax.dynamic_index_in_dim(attended, slot, 0, False)
        query_grad, key_grad, value_grad = attend_back(
            query_rows, slot_keys, allowed, incoming, slot_attended, w_proj
        )
        owner_sum = jnp.concatenate([key_grad[:shard_rows], value_grad[:shard_rows]], 1)
        far_part = jnp.concatenate([key_grad[shard_rows:], value_grad[shard_rows:]], 1)
        far_part = far_part.astype(jnp.bfloat16).reshape(levels, shard_rows, 2 * model_width)
        return (query_grad, owner_sum, far_part)

    def empty_attention(incoming, slot):
        return (
            jnp.zeros((shard_rows, model_width), jnp.float32),
            jnp.zeros((shard_rows, 2 * model_width), jnp.float32),
            jnp.zeros((levels, shard_rows, 2 * model_width), jnp.bfloat16),
        )

    def norm_part(qkv_grad, incoming, slot):
        norm_grad = lax.dot_general(
            qkv_grad, w_qkv, (((1,), (1,)), ((), ())), preferred_element_type=jnp.float32
        )
        slot_normed = lax.dynamic_index_in_dim(normed, slot, 0, False)
        slot_rms = lax.dynamic_index_in_dim(inverse_rms, slot, 0, False)
        inner = jnp.mean(norm_grad * slot_normed, axis=-1, keepdims=True)
        return (incoming.astype(jnp.float32) + slot_rms * (norm_grad - slot_normed * inner)).astype(
            jnp.bfloat16
        )

    def empty_norm(qkv_grad, incoming, slot):
        return jnp.zeros((shard_rows, model_width), jnp.bfloat16)

    def step(turn, carry):
        received, grad_store, qkv_store, incoming_store = carry
        slot_raw = turn - (sections - 1 - section_index)
        active = (slot_raw >= 0) & (slot_raw < micro_count)
        slot = jnp.clip(slot_raw, 0, micro_count - 1)
        incoming = jnp.where(
            section_index == sections - 1,
            lax.dynamic_index_in_dim(grad_top, slot, 0, False),
            received,
        )
        query_grad, owner_sum, far_part = lax.cond(
            active, attention_part, empty_attention, incoming, slot
        )
        for level in range(levels):
            owner_sum = owner_sum + shifted(far_part[level], "tm", -(2**level)).astype(jnp.float32)
        qkv_grad = jnp.concatenate([query_grad, owner_sum], 1).astype(jnp.bfloat16)
        grad_in = lax.cond(active, norm_part, empty_norm, qkv_grad, incoming, slot)
        sent_down = shifted(grad_in, "section", -1)
        grad_store = jnp.where(
            active, lax.dynamic_update_index_in_dim(grad_store, grad_in, slot, 0), grad_store
        )
        qkv_store = jnp.where(
            active, lax.dynamic_update_index_in_dim(qkv_store, qkv_grad, slot, 0), qkv_store
        )
        incoming_store = jnp.where(
            active,
            lax.dynamic_update_index_in_dim(incoming_store, incoming, slot, 0),
            incoming_store,
        )
        return (sent_down, grad_store, qkv_store, incoming_store)

    initial = (
        jnp.zeros((shard_rows, model_width), jnp.bfloat16),
        jnp.zeros((micro_count, shard_rows, model_width), jnp.bfloat16),
        jnp.zeros((micro_count, shard_rows, 3 * model_width), jnp.bfloat16),
        jnp.zeros((micro_count, shard_rows, model_width), jnp.bfloat16),
    )
    received, grad_store, qkv_store, incoming_store = lax.fori_loop(
        0, sections + micro_count - 1, step, initial
    )
    flat_norm = rounded_norm.reshape(-1, model_width)
    flat_attended = attended.reshape(-1, model_width)
    flat_qkv = qkv_store.reshape(-1, 3 * model_width)
    flat_incoming = incoming_store.reshape(-1, model_width)
    contract = (((0,), (0,)), ((), ()))
    first = lax.dot_general(flat_norm, flat_qkv, contract, preferred_element_type=jnp.float32)
    second = lax.dot_general(
        flat_attended, flat_incoming, contract, preferred_element_type=jnp.float32
    )
    summed = lax.psum_scatter(
        jnp.concatenate([first, second], 1).astype(jnp.bfloat16),
        "tm",
        scatter_dimension=0,
        tiled=True,
    ).astype(jnp.float32)
    return (
        grad_store[None],
        summed[None, :, : 3 * model_width],
        summed[None, :, 3 * model_width :],
    )


def pair_rows(transposed, head):
    width = 2 * HEAD_DIM
    pair = transposed[head // 2 * width : (head // 2 + 1) * width]
    empty = jnp.zeros((HEAD_DIM, pair.shape[1]), pair.dtype)
    if head % 2 == 0:
        return jnp.concatenate([pair[:HEAD_DIM], empty], 0)
    return jnp.concatenate([empty, pair[HEAD_DIM:]], 0)


def allowed_keys(flag_rows, levels, shard_rows, keys, first_query, count):
    key_at = lax.broadcasted_iota(jnp.int32, (keys, count), 0)
    query_at = lax.broadcasted_iota(jnp.int32, (keys, count), 1) + first_query
    gap = lax.div(query_at, shard_rows) - lax.div(key_at, shard_rows)
    allowed = (gap == 0) & (key_at <= query_at)
    for level in range(levels):
        allowed = allowed | ((gap == 2**level) & (flag_rows[level : level + 1] != 0))
    return allowed


def softmax_pass(queries, keys, values, allowed, prob_ref, at_ref):
    queries_t = queries.T
    values_t = values.T
    width = 2 * HEAD_DIM
    for head in range(queries.shape[1] // HEAD_DIM):
        at = slice(head * HEAD_DIM, (head + 1) * HEAD_DIM)
        pair = slice(head // 2 * width, (head // 2 + 1) * width)
        scores = jnp.dot(
            keys[:, pair], pair_rows(queries_t, head), preferred_element_type=jnp.float32
        )
        scores = jnp.where(allowed, scores, negative_fill)
        shifted_exp = jnp.exp(scores - jnp.max(scores, axis=0, keepdims=True))
        probability = shifted_exp * (1.0 / jnp.sum(shifted_exp, axis=0, keepdims=True))
        prob_ref[head] = probability
        at_ref[at] = jnp.dot(
            values_t[at], probability.astype(jnp.bfloat16), preferred_element_type=jnp.float32
        ).astype(jnp.bfloat16)


def pack_kernel(
    levels, info_ref, offsets_ref, acts_ref, top_ref, own_ref, other_ref, own_top_ref, other_top_ref
):
    shard_rows, model_width = acts_ref.shape[1:]
    lane = lax.broadcasted_iota(jnp.int32, (shard_rows, own_ref.shape[1] - model_width), 1)
    flags = jnp.zeros(lane.shape, jnp.float32)
    for level in range(levels):
        seen = jnp.where(offsets_ref[0, level] != 0, 1.0, 0.0)
        flags = jnp.where(lane == level, seen, flags)
    for side, out_ref, out_top_ref in (
        (info_ref[2], own_ref, own_top_ref),
        (1 - info_ref[2], other_ref, other_top_ref),
    ):
        out_ref[:, :model_width] = acts_ref[side]
        out_ref[:, model_width:] = flags.astype(jnp.bfloat16)
        out_top_ref[...] = top_ref[side]


def project_kernel(replicas, info_ref, *refs):
    pieces = refs[: 4 * replicas]
    w_ref, acts_ref, norm_ref, flag_ref, q_ref, k_ref, v_ref, kt_ref, packed_ref = refs[
        4 * replicas :
    ]
    shards, shard_rows, model_width = acts_ref.shape
    seq = shards * shard_rows
    columns = q_ref.shape[1]
    at_piece = 0
    for core in (info_ref[0], 1 - info_ref[0]):
        for side in (info_ref[2], 1 - info_ref[2]):
            for step in range(replicas):
                shard = side * (shards // 2) + place_of(info_ref, step, replicas) + core
                packed_ref[shard] = pieces[at_piece][...]
                at_piece += 1
    acts_ref[...] = packed_ref[:, :, :model_width]
    normed, _ = normalize(acts_ref[...].reshape(seq, model_width))
    rounded = normed.astype(jnp.bfloat16)
    norm_ref[...] = rounded
    flag_ref[...] = packed_ref[:, :, model_width:].reshape(seq, -1).astype(jnp.float32).T
    scale_factor = HEAD_DIM ** (-0.5)
    for block, out_ref in enumerate((q_ref, k_ref, v_ref)):
        first = pl.multiple_of(block * model_width + info_ref[0] * columns, 128)
        product = jnp.dot(
            rounded, w_ref[:, pl.ds(first, columns)], preferred_element_type=jnp.float32
        ).astype(jnp.bfloat16)
        out_ref[...] = product * scale_factor if block == 0 else product
    kt_ref[...] = (k_ref[...] * scale_factor).T


def upper_forward_kernel(levels, shard_rows, flag_ref, q_ref, k_ref, v_ref, prob_ref, at_ref):
    seq = q_ref.shape[0]
    count = seq // 2
    allowed = allowed_keys(flag_ref[:, count:], levels, shard_rows, seq, count, count)
    softmax_pass(q_ref[count:], k_ref[...], v_ref[...], allowed, prob_ref, at_ref)


def lower_forward_kernel(
    levels, shard_rows, info_ref, norm_ref, flag_ref, q_ref, k_ref, v_ref, prob_ref, at_ref, gt_ref
):
    seq = norm_ref.shape[0]
    count = seq // 2
    allowed = allowed_keys(flag_ref[:, :count], levels, shard_rows, count, 0, count)
    softmax_pass(q_ref[:count], k_ref[:count], v_ref[:count], allowed, prob_ref, at_ref)
    rows = gt_ref.shape[1]
    half_width = norm_ref.shape[1] // 2
    for place in range(2):
        half = 1 - info_ref[2] if place == 0 else info_ref[2]
        first = pl.multiple_of(half * half_width + info_ref[1] * rows, 128)
        gt_ref[place] = norm_ref[:, pl.ds(first, rows)].T


def place_of(info_ref, step, replicas):
    return 2 * lax.rem(info_ref[1] - step + replicas, replicas)


def merge_rows(info_ref, fresh, got_refs, kept_refs, out_refs, rows_ref):
    @pl.when(fresh)
    def _():
        for core, out_ref in enumerate(out_refs):
            refs = got_refs[core * len(got_refs) // 2 : (core + 1) * len(got_refs) // 2]
            if len(refs) == 1:
                out_ref[...] = refs[0][...]
            else:
                for step, got_ref in enumerate(refs):
                    out_ref[step] = got_ref[...]

    @pl.when(jnp.logical_not(fresh))
    def _():
        for out_ref, kept_ref in zip(out_refs, kept_refs):
            out_ref[...] = kept_ref[...]

    place_rows(info_ref, out_refs, rows_ref)


def place_rows(info_ref, out_refs, rows_ref):
    replicas = out_refs[0].shape[0]
    for step in range(replicas):
        place = place_of(info_ref, step, replicas)
        rows_ref[place + info_ref[0]] = out_refs[0][step]
        rows_ref[place + 1 - info_ref[0]] = out_refs[1][step]


def merge_tops(info_ref, upper, piece_refs, out_refs, rows_ref):
    replicas = out_refs[0].shape[0]
    own_chunk = info_ref[2] == (1 if upper else 0)
    for core in range(2):
        refs = piece_refs[2 * replicas * core : 2 * replicas * (core + 1)]

        @pl.when(own_chunk)
        def _():
            for step in range(replicas):
                out_refs[core][step] = refs[step][...]

        @pl.when(jnp.logical_not(own_chunk))
        def _():
            for step in range(replicas):
                out_refs[core][step] = refs[replicas + step][...]

    place_rows(info_ref, out_refs, rows_ref)


def backward_kernel(upper, tops, replicas, fresh_section, info_ref, *refs):
    refs = list(refs)
    got = tops or (2 * replicas + 2 if upper else 4)
    got_refs = refs[:got]
    w_ref, prob_ref, q_ref, v_ref, kt_ref, at_ref = refs[got : got + 6]
    refs = refs[got + 6 :]
    if not upper:
        key_sum_ref, value_sum_ref, _ = refs[:3]
        refs = refs[3:]
    own_ref, other_ref, keep_ref, send_ref = refs[:4]
    refs = refs[4:]
    if upper:
        key_sum_ref, value_sum_ref = refs[:2]
        refs = refs[2:]
    grads_ref, rows_ref = refs
    shard_rows, model_width = own_ref.shape[1:]
    count = rows_ref.shape[0] * shard_rows
    keys = prob_ref.shape[1]
    parity = info_ref[0]
    columns = q_ref.shape[1]
    width = 2 * HEAD_DIM
    if tops:
        merge_tops(info_ref, upper, got_refs, (own_ref, other_ref), rows_ref)
    else:
        fresh = info_ref[3] == fresh_section
        merge_rows(info_ref, fresh, got_refs[:-2], got_refs[-2:], (own_ref, other_ref), rows_ref)
    rows = rows_ref[...].reshape(count, model_width)
    weights = w_ref[pl.ds(pl.multiple_of(parity * columns, 128), columns), :]
    over_width = (((1,), (1,)), ((), ()))
    upstream = lax.dot_general(
        rows, weights, over_width, preferred_element_type=jnp.float32
    ).astype(jnp.bfloat16)
    upstream_t = lax.dot_general(
        weights, rows, over_width, preferred_element_type=jnp.float32
    ).astype(jnp.bfloat16)
    product_t = upstream_t.astype(jnp.float32) * at_ref[...].astype(jnp.float32)
    first_query = keys - count
    lane = lax.broadcasted_iota(jnp.int32, (1, width), 1)
    head_masks = [
        jnp.where(lane < HEAD_DIM, 1.0, 0.0).astype(jnp.bfloat16),
        jnp.where(lane < HEAD_DIM, 0.0, 1.0).astype(jnp.bfloat16),
    ]

    def put(block, pair, part):
        first = block * columns + pair * width
        grads_ref[:, :, first : first + width] = part.astype(jnp.bfloat16).reshape(
            -1, shard_rows, width
        )

    for pair in range(columns // width):
        at_pair = slice(pair * width, (pair + 1) * width)
        values = v_ref[:keys, at_pair]
        queries = q_ref[first_query : first_query + count, at_pair]
        up_pair = upstream[:, at_pair]
        key_grad = jnp.zeros((keys, width), jnp.float32)
        value_grad = jnp.zeros((keys, width), jnp.float32)
        query_parts = []
        for head in (2 * pair, 2 * pair + 1):
            at = slice(head * HEAD_DIM, (head + 1) * HEAD_DIM)
            mask = head_masks[head % 2]
            delta = jnp.sum(product_t[at], axis=0, keepdims=True)
            prob_grad = jnp.dot(
                values, pair_rows(upstream_t, head), preferred_element_type=jnp.float32
            )
            probability = prob_ref[head]
            score_grad = (probability * (prob_grad - delta)).astype(jnp.bfloat16)
            key_grad += jnp.dot(score_grad, queries * mask, preferred_element_type=jnp.float32)
            value_grad += jnp.dot(
                probability.astype(jnp.bfloat16), up_pair * mask, preferred_element_type=jnp.float32
            )
            query_parts.append(
                jnp.dot(kt_ref[at, :keys], score_grad, preferred_element_type=jnp.float32)
            )
        put(0, pair, jnp.concatenate(query_parts, 0).astype(jnp.bfloat16).T)
        if upper:
            key_sum_ref[:, at_pair] = key_grad[:first_query]
            value_sum_ref[:, at_pair] = value_grad[:first_query]
            key_grad = key_grad[first_query:]
            value_grad = value_grad[first_query:]
        else:
            key_grad = key_grad + key_sum_ref[:, at_pair]
            value_grad = value_grad + value_sum_ref[:, at_pair]
        put(1, pair, key_grad)
        put(2, pair, value_grad)
    for step in range(replicas):
        place = place_of(info_ref, step, replicas)
        keep_ref[step] = grads_ref[place + parity]
        send_ref[step] = grads_ref[place + 1 - parity]


def norm_kernel(
    upper, info_ref, keep_ref, got_ref, acts_ref, incoming_ref, w_ref, after_ref, *refs
):
    out_refs, rows_ref = refs[:-1], refs[-1]
    replicas, shard_rows, triple = keep_ref.shape
    columns = triple // 3
    model_width = w_ref.shape[0]
    rows = replicas * shard_rows
    parity = info_ref[0]
    for part_ref, half in ((keep_ref, parity), (got_ref, 1 - parity)):
        for block in range(3):
            first = pl.multiple_of(block * model_width + half * columns, 128)
            rows_ref[:, pl.ds(first, columns)] = part_ref[
                :, :, block * columns : (block + 1) * columns
            ].reshape(rows, columns)
    norm_grad = lax.dot_general(
        rows_ref[...], w_ref[...], (((1,), (1,)), ((), ())), preferred_element_type=jnp.float32
    )
    base = acts_ref.shape[0] // 2 if upper else 0
    values = jnp.concatenate(
        [
            acts_ref[base + place_of(info_ref, step, replicas) + parity]
            for step in range(replicas)
        ],
        0,
    )
    normed, inverse_rms = normalize(values)
    inner = jnp.mean(norm_grad * normed, axis=-1, keepdims=True)
    incoming = incoming_ref[...].reshape(rows, model_width).astype(jnp.float32)
    grad_in = incoming + inverse_rms * (norm_grad - normed * inner)
    grad_in = grad_in.astype(jnp.bfloat16)
    if upper:
        for step, out_ref in enumerate(out_refs):
            out_ref[...] = grad_in[step * shard_rows : (step + 1) * shard_rows]
    else:
        out_refs[0][...] = grad_in.reshape(out_refs[0].shape)


def w_in_kernel(place, gt_ref, lower_ref, upper_ref, after_ref, out_ref):
    count = lower_ref.shape[0] * lower_ref.shape[1]
    total = jnp.zeros(out_ref.shape, jnp.float32)
    for chunk, part_ref in enumerate((lower_ref, upper_ref)):
        total += jnp.dot(
            gt_ref[place, :, chunk * count : (chunk + 1) * count],
            part_ref[...].reshape(count, -1),
            preferred_element_type=jnp.float32,
        )
    out_ref[...] = total.astype(out_ref.dtype)


def w_out_kernel(fresh_section, info_ref, *refs):
    got_refs, kept_refs = refs[:2], refs[2:4]
    at_lower_ref, at_upper_ref, upper_ref, send_ref, own_ref, part_ref, part_other_ref, rows_ref = (
        refs[4:]
    )
    merge_rows(
        info_ref,
        info_ref[3] == fresh_section,
        got_refs,
        kept_refs,
        (part_ref, part_other_ref),
        rows_ref,
    )
    rows = own_ref.shape[0]
    first = pl.multiple_of(info_ref[1] * rows, 128)
    total = jnp.zeros(own_ref.shape, jnp.float32)
    for at_ref, chunk_ref in ((at_lower_ref, rows_ref), (at_upper_ref, upper_ref)):
        total += jnp.dot(
            at_ref[pl.ds(first, rows)],
            chunk_ref[...].reshape(-1, own_ref.shape[1]),
            preferred_element_type=jnp.float32,
        )
    own_ref[...] = total
    send_ref[...] = total.astype(jnp.bfloat16)


def sum_kernel(info_ref, own_ref, got_ref, keep_ref, send_ref):
    rows = keep_ref.shape[0]
    mine = pl.ds(pl.multiple_of(info_ref[0] * rows, rows), rows)
    others = pl.ds(pl.multiple_of((1 - info_ref[0]) * rows, rows), rows)
    keep_ref[...] = own_ref[mine] + got_ref[mine].astype(jnp.float32)
    send_ref[...] = (own_ref[others] + got_ref[others].astype(jnp.float32)).astype(jnp.bfloat16)


def place_in_kernel(info_ref, keep_ref, got_ref, out_ref):
    columns = keep_ref.shape[1] // 3
    for part_ref, half in ((keep_ref, info_ref[0]), (got_ref, 1 - info_ref[0])):
        for block in range(3):
            first = pl.multiple_of((2 * block + half) * columns, 128)
            out_ref[:, pl.ds(first, columns)] = part_ref[
                :, block * columns : (block + 1) * columns
            ].astype(jnp.float32)


def place_out_kernel(info_ref, keep_ref, got_ref, out_ref):
    owner = info_ref[0] == info_ref[2]

    @pl.when(owner)
    def _():
        out_ref[...] = keep_ref[...]

    @pl.when(jnp.logical_not(owner))
    def _():
        out_ref[...] = got_ref[...].astype(jnp.float32)


def call(kernel, outs, operands, scratch=(), flops=0, scalars=1, after=None, mebibytes=16):
    in_specs = [pl.BlockSpec(memory_space=pltpu.SMEM)] * scalars
    in_specs += [pl.BlockSpec(memory_space=pltpu.VMEM)] * (len(operands) - scalars)
    moved = sum(item.size * item.dtype.itemsize for item in [*operands, *outs])
    if after is not None:
        operands = [*operands, after]
        in_specs.append(pl.BlockSpec(memory_space=pl.ANY))
    return pl.pallas_call(
        kernel,
        out_shape=list(outs),
        in_specs=in_specs,
        out_specs=[pl.BlockSpec(memory_space=pltpu.VMEM)] * len(outs),
        scratch_shapes=list(scratch),
        cost_estimate=pl.CostEstimate(flops=flops, bytes_accessed=moved, transcendentals=0),
        compiler_params=pltpu.CompilerParams(vmem_limit_bytes=mebibytes * 2**20),
    )(*operands)


def by_chips(acts, grad_top, w_in, w_out, offsets):
    half_type, full_type = jnp.bfloat16, jnp.float32
    shape = jax.ShapeDtypeStruct
    sections = lax.axis_size("section")
    shards = lax.axis_size("tm")
    levels = offsets.shape[1]
    half = shards // 2
    replicas = half // 2
    me = lax.axis_index("tm")
    parity = lax.rem(me, 2)
    side = lax.div(me, half)
    micro_count, shard_rows, model_width = acts.shape[1:]
    columns = model_width // 2
    heads = columns // HEAD_DIM
    seq = shards * shard_rows
    count = seq // 2
    w_qkv = w_in[0]
    w_rows = w_out[0]
    info = jnp.stack(
        [parity, lax.div(lax.rem(me, half), 2), side, lax.axis_index("section")]
    ).astype(jnp.int32)
    across = [(source, (source + half) % shards) for source in range(shards)]
    cores = [(source, source + 1 - 2 * (source % 2)) for source in range(shards)]
    homeward = [pair for pair in across if pair[0] // half != pair[0] % 2]
    around = [
        [
            (source, source // half * half + (source % half + 2 * step) % half)
            for source in range(shards)
        ]
        for step in range(replicas)
    ]

    packed = shape((shard_rows, model_width + 128), half_type)
    top_shape = shape((shard_rows, model_width), half_type)
    own_acts, other_acts, own_top, other_top = call(
        functools.partial(pack_kernel, levels),
        [packed, packed, top_shape, top_shape],
        [info, offsets, acts[0], grad_top],
        scalars=2,
    )
    swapped = lax.ppermute(other_acts, "tm", across)
    pieces = [own_acts]
    pieces += [lax.ppermute(own_acts, "tm", around[step]) for step in range(1, replicas)]
    pieces += [swapped]
    pieces += [lax.ppermute(swapped, "tm", around[step]) for step in range(1, replicas)]
    pieces += [lax.ppermute(piece, "tm", cores) for piece in pieces]
    other_top, _ = lax.optimization_barrier((other_top, own_acts))
    other_top = lax.ppermute(other_top, "tm", across)
    other_top, _ = lax.optimization_barrier((other_top, swapped))
    tops = [own_top]
    tops += [lax.ppermute(own_top, "tm", around[step]) for step in range(1, replicas)]
    tops += [other_top]
    tops += [lax.ppermute(other_top, "tm", around[step]) for step in range(1, replicas)]

    rows_shape = shape((seq, columns), half_type)
    acts_all, norm, flag_rows, queries, keys, values, keys_t = call(
        functools.partial(project_kernel, replicas),
        [
            shape((shards, shard_rows, model_width), half_type),
            shape((seq, model_width), half_type),
            shape((128, seq), full_type),
            rows_shape,
            rows_shape,
            rows_shape,
            shape((columns, seq), half_type),
        ],
        [info, *pieces, w_qkv],
        scratch=[pltpu.VMEM((shards, *packed.shape), half_type)],
        flops=6 * seq * model_width * columns,
    )
    tops, _ = lax.optimization_barrier((tuple(tops), keys_t))
    tops = [*tops, *[lax.ppermute(piece, "tm", cores) for piece in tops]]
    upper_prob, upper_at = call(
        functools.partial(upper_forward_kernel, levels, shard_rows),
        [shape((heads, seq, count), full_type), shape((columns, count), half_type)],
        [flag_rows, queries, keys, values],
        scalars=0,
        flops=4 * columns * seq * count,
    )
    block_rows = 2 * model_width // shards
    lower_prob, lower_at, norm_t = call(
        functools.partial(lower_forward_kernel, levels, shard_rows),
        [
            shape((heads, count, count), full_type),
            shape((columns, count), half_type),
            shape((2, block_rows, seq), half_type),
        ],
        [info, norm, flag_rows, queries, keys, values],
        flops=4 * columns * count * count,
    )
    probs = {True: upper_prob, False: lower_prob}
    attended = {True: upper_at, False: lower_at}
    got, kept = {}, {}
    piece_shape = shape((replicas, shard_rows, model_width), half_type)
    grads_shape = shape((replicas, shard_rows, 3 * columns), half_type)
    sum_shape = shape((count, columns), full_type)
    full_grads = shape((half, shard_rows, 3 * columns), half_type)
    full_rows = shape((half, shard_rows, model_width), half_type)
    rows_scratch = pltpu.VMEM(full_rows.shape, half_type)
    grads_scratch = pltpu.VMEM(full_grads.shape, half_type)
    result, full = {}, {}
    grad_in = keys_t
    for turn in range(sections):
        last = turn + 1 == sections
        fresh_section = sections - 1 - turn
        sums, parts, crossed = [], {}, {}
        for upper in (True, False):
            rows_in = tops
            if turn:
                before = result[False] if upper else keep
                pieces = []
                for piece in got[upper]:
                    piece, before = lax.optimization_barrier((piece, before))
                    pieces.append(piece)
                got[upper] = pieces
                if upper:
                    result[False] = before
                else:
                    keep = parts[True] = before
                others = [lax.ppermute(piece, "tm", cores) for piece in got[upper]]
                rows_in = [*got[upper], *others, *kept[upper]]
            after = None
            if last and not upper:
                out_send, out_own = call(
                    functools.partial(w_out_kernel, fresh_section),
                    [
                        shape((block_rows, model_width), half_type),
                        shape((block_rows, model_width), full_type),
                    ],
                    [info, *rows_in, lower_at, upper_at, ordered],
                    scratch=[
                        pltpu.VMEM(piece_shape.shape, half_type),
                        pltpu.VMEM(piece_shape.shape, half_type),
                        rows_scratch,
                    ],
                    flops=2 * block_rows * seq * model_width,
                )
                after = out_send
            elif not upper:
                after = keep
            outs = [piece_shape, piece_shape, grads_shape, grads_shape]
            outs += [sum_shape, sum_shape] if upper else []
            scratch = []
            if last:
                outs += [full_grads]
            else:
                scratch += [grads_scratch]
            if last and upper:
                outs += [full_rows]
            else:
                scratch += [rows_scratch]
            part_keys = seq if upper else count
            answer = call(
                functools.partial(
                    backward_kernel, upper, 0 if turn else len(tops), replicas, fresh_section
                ),
                outs,
                [info, *rows_in, w_rows, probs[upper], queries, values, keys_t]
                + [attended[upper], *sums],
                scratch=scratch,
                flops=2 * count * columns * (2 * model_width + 4 * part_keys),
                after=after,
            )
            kept[upper] = tuple(answer[:2])
            keep, send = answer[2:4]
            parts[upper] = keep
            if upper:
                sums = answer[4:6]
            if last:
                full[upper] = answer[6 if upper else 4]
            if last and upper:
                ordered = answer[7]
            crossed[upper] = lax.ppermute(send, "tm", cores)
        if last:
            out_got = lax.ppermute(out_send, "tm", homeward)
        for upper in (True, False):
            grad_pieces = call(
                functools.partial(norm_kernel, upper),
                [top_shape] * replicas if upper else [piece_shape],
                [info, parts[upper], crossed[upper], acts_all, kept[upper][0], w_qkv],
                scratch=[pltpu.VMEM((replicas * shard_rows, 3 * model_width), half_type)],
                flops=6 * replicas * shard_rows * model_width * model_width,
                after=grad_in,
            )
            result[upper] = grad_pieces
            grad_in = grad_pieces[-1]
            if not last:
                hop = [(sections - 1 - turn, sections - 2 - turn)]
                got[upper] = [lax.ppermute(piece, "section", hop) for piece in grad_pieces]

    own_rows = block_rows // 2
    term_flops = 2 * block_rows * seq * 3 * columns
    (in_send,) = call(
        functools.partial(w_in_kernel, 0),
        [shape((block_rows, 3 * columns), half_type)],
        [norm_t, full[False], full[True]],
        flops=term_flops,
        scalars=0,
        after=out_got,
    )
    in_got = lax.ppermute(in_send, "tm", across)
    (in_own,) = call(
        functools.partial(w_in_kernel, 1),
        [shape((block_rows, 3 * columns), full_type)],
        [norm_t, full[False], full[True]],
        flops=term_flops,
        scalars=0,
        after=in_send,
    )
    out_keep, out_pass = call(
        sum_kernel,
        [shape((own_rows, model_width), full_type), shape((own_rows, model_width), half_type)],
        [info, out_own, out_got],
    )
    to_sibling = [pair for pair in cores if pair[0] // half == pair[0] % 2]
    (d_w_out,) = call(
        place_out_kernel,
        [shape((own_rows, model_width), full_type)],
        [info, out_keep, lax.ppermute(out_pass, "tm", to_sibling)],
    )
    in_keep, in_pass = call(
        sum_kernel,
        [shape((own_rows, 3 * columns), full_type), shape((own_rows, 3 * columns), half_type)],
        [info, in_own, in_got],
    )
    (d_w_in,) = call(
        place_in_kernel,
        [shape((own_rows, 3 * model_width), full_type)],
        [info, in_keep, lax.ppermute(in_pass, "tm", cores)],
    )

    upper_own, lower_own = result[True][0], result[False][0][0]
    mine = jnp.where(side == 1, upper_own, lower_own)
    partner = lax.ppermute(jnp.where(side == 1, lower_own, upper_own), "tm", across)
    d_acts = jnp.where(side == 0, jnp.stack([mine, partner]), jnp.stack([partner, mine]))
    return (d_acts[None], d_w_in[None], d_w_out[None])


def layer_gradients(acts, grad_top, w_in, w_out, offsets):
    shards = lax.axis_size("tm")
    micro_count, shard_rows, model_width = acts.shape[1:]
    heads = model_width // HEAD_DIM
    prob_bytes = 2 * heads * (shards * shard_rows) ** 2
    fits = prob_bytes <= 2**24 and model_width % (128 * shards) == 0 and shard_rows % 16 == 0
    if micro_count == 2 and shards % 4 == 0 and heads % 4 == 0 and fits:
        return by_chips(acts, grad_top, w_in, w_out, offsets)
    return per_device(acts, grad_top, w_in, w_out, offsets)


def solution(mesh):
    placed = (
        P("section", None, "tm", None),
        P(None, "tm", None),
        P("section", None, None),
        P("section", None, None),
        P("tm", None),
    )
    return jax.shard_map(
        layer_gradients,
        mesh=mesh,
        in_specs=placed,
        out_specs=(
            P("section", None, "tm", None),
            P("section", "tm", None),
            P("section", "tm", None),
        ),
        check_vma=False,
    )
```

```python
import functools
import jax
import jax.numpy as jnp
from jax import lax
from jax.experimental import pallas as pl
from jax.experimental.pallas import tpu as pltpu
from jax.sharding import PartitionSpec as P

HEAD_DIM = 64


epsilon = 1e-06
negative_fill = -1e30


def shifted(value, axis, steps):
    count = lax.axis_size(axis)
    initial, last = (max(0, -steps), min(count, count - steps))
    return lax.ppermute(value, axis, [(source, source + steps) for source in range(initial, last)])


def normalize(inputs):
    values = inputs.astype(jnp.float32)
    inverse_rms = lax.rsqrt(jnp.mean(values * values, axis=-1, keepdims=True) + epsilon)
    return (values * inverse_rms, inverse_rms)


def key_bias(level_flags, shard_rows):
    position = jnp.arange(shard_rows)
    own_part = position[None, :] <= position[:, None]
    far_part = jnp.repeat(level_flags != 0, shard_rows)
    far_part = jnp.broadcast_to(far_part[None, :], (shard_rows, far_part.shape[0]))
    return jnp.concatenate([own_part, far_part], 1)


def split_heads(row_block):
    return row_block.reshape(row_block.shape[0], -1, HEAD_DIM)


def softmax_keys(queries, key_heads, allowed):
    scores = jnp.einsum(
        "ihd,jhd->hij", queries, key_heads, preferred_element_type=jnp.float32
    ) * HEAD_DIM ** (-0.5)
    scores = jnp.where(allowed[None], scores, negative_fill)
    highest = jnp.max(scores, axis=-1, keepdims=True)
    shifted_exp = jnp.where(allowed[None], jnp.exp(scores - highest), 0.0)
    return shifted_exp / jnp.sum(shifted_exp, axis=-1, keepdims=True)


def attend(query_rows, key_rows, allowed):
    model_width = query_rows.shape[1]
    probability = softmax_keys(
        split_heads(query_rows), split_heads(key_rows[:, :model_width]), allowed
    )
    attended = jnp.einsum(
        "hij,jhd->ihd",
        probability.astype(jnp.bfloat16),
        split_heads(key_rows[:, model_width:]),
        preferred_element_type=jnp.float32,
    )
    return attended.reshape(query_rows.shape).astype(jnp.bfloat16)


def attend_back(query_rows, key_rows, allowed, incoming, attended, w_proj):
    model_width = query_rows.shape[1]
    queries = split_heads(query_rows)
    key_heads = split_heads(key_rows[:, :model_width])
    value_heads = split_heads(key_rows[:, model_width:])
    probability = softmax_keys(queries, key_heads, allowed)
    rounded = probability.astype(jnp.bfloat16)
    upstream = lax.dot_general(
        incoming, w_proj, (((1,), (1,)), ((), ())), preferred_element_type=jnp.float32
    ).astype(jnp.bfloat16)
    up_heads = split_heads(upstream)
    delta = jnp.einsum(
        "ihd,ihd->hi", up_heads.astype(jnp.float32), split_heads(attended).astype(jnp.float32)
    )[..., None]
    prob_grad = jnp.einsum(
        "ihd,jhd->hij", up_heads, value_heads, preferred_element_type=jnp.float32
    )
    score_grad = (probability * (prob_grad - delta)).astype(jnp.bfloat16)
    scale_factor = HEAD_DIM ** (-0.5)
    query_grad = (
        jnp.einsum("hij,jhd->ihd", score_grad, key_heads, preferred_element_type=jnp.float32)
        * scale_factor
    )
    key_grad = (
        jnp.einsum("hij,ihd->jhd", score_grad, queries, preferred_element_type=jnp.float32)
        * scale_factor
    )
    value_grad = jnp.einsum("hij,ihd->jhd", rounded, up_heads, preferred_element_type=jnp.float32)
    return (
        query_grad.reshape(-1, model_width),
        key_grad.reshape(-1, model_width),
        value_grad.reshape(-1, model_width),
    )


def per_device(acts, grad_top, w_in, w_out, offsets):
    sections = lax.axis_size("section")
    shards = lax.axis_size("tm")
    levels = shards.bit_length() - 1
    section_index = lax.axis_index("section")
    micro_count = acts.shape[1]
    shard_rows = acts.shape[2]
    model_width = acts.shape[3]
    w_qkv = w_in[0]
    w_proj = w_out[0]
    level_flags = offsets[0]
    normed, inverse_rms = normalize(acts[0])
    rounded_norm = normed.astype(jnp.bfloat16)
    qkv = jnp.dot(rounded_norm.reshape(-1, model_width), w_qkv, preferred_element_type=jnp.float32)
    qkv = qkv.astype(jnp.bfloat16).reshape(micro_count, shard_rows, 3 * model_width)
    pairs = qkv[..., model_width:]
    far_list = [shifted(pairs, "tm", 2**level) for level in range(levels)]
    key_rows = jnp.concatenate([pairs] + far_list, 1)
    allowed = key_bias(level_flags, shard_rows)
    attended = jnp.stack(
        [
            attend(qkv[index, :, :model_width], key_rows[index], allowed)
            for index in range(micro_count)
        ],
        0,
    )

    def attention_part(incoming, slot):
        query_rows = lax.dynamic_index_in_dim(qkv, slot, 0, False)[:, :model_width]
        slot_keys = lax.dynamic_index_in_dim(key_rows, slot, 0, False)
        slot_attended = lax.dynamic_index_in_dim(attended, slot, 0, False)
        query_grad, key_grad, value_grad = attend_back(
            query_rows, slot_keys, allowed, incoming, slot_attended, w_proj
        )
        owner_sum = jnp.concatenate([key_grad[:shard_rows], value_grad[:shard_rows]], 1)
        far_part = jnp.concatenate([key_grad[shard_rows:], value_grad[shard_rows:]], 1)
        far_part = far_part.astype(jnp.bfloat16).reshape(levels, shard_rows, 2 * model_width)
        return (query_grad, owner_sum, far_part)

    def empty_attention(incoming, slot):
        return (
            jnp.zeros((shard_rows, model_width), jnp.float32),
            jnp.zeros((shard_rows, 2 * model_width), jnp.float32),
            jnp.zeros((levels, shard_rows, 2 * model_width), jnp.bfloat16),
        )

    def norm_part(qkv_grad, incoming, slot):
        norm_grad = lax.dot_general(
            qkv_grad, w_qkv, (((1,), (1,)), ((), ())), preferred_element_type=jnp.float32
        )
        slot_normed = lax.dynamic_index_in_dim(normed, slot, 0, False)
        slot_rms = lax.dynamic_index_in_dim(inverse_rms, slot, 0, False)
        inner = jnp.mean(norm_grad * slot_normed, axis=-1, keepdims=True)
        return (incoming.astype(jnp.float32) + slot_rms * (norm_grad - slot_normed * inner)).astype(
            jnp.bfloat16
        )

    def empty_norm(qkv_grad, incoming, slot):
        return jnp.zeros((shard_rows, model_width), jnp.bfloat16)

    def step(turn, carry):
        received, grad_store, qkv_store, incoming_store = carry
        slot_raw = turn - (sections - 1 - section_index)
        active = (slot_raw >= 0) & (slot_raw < micro_count)
        slot = jnp.clip(slot_raw, 0, micro_count - 1)
        incoming = jnp.where(
            section_index == sections - 1,
            lax.dynamic_index_in_dim(grad_top, slot, 0, False),
            received,
        )
        query_grad, owner_sum, far_part = lax.cond(
            active, attention_part, empty_attention, incoming, slot
        )
        for level in range(levels):
            owner_sum = owner_sum + shifted(far_part[level], "tm", -(2**level)).astype(jnp.float32)
        qkv_grad = jnp.concatenate([query_grad, owner_sum], 1).astype(jnp.bfloat16)
        grad_in = lax.cond(active, norm_part, empty_norm, qkv_grad, incoming, slot)
        sent_down = shifted(grad_in, "section", -1)
        grad_store = jnp.where(
            active, lax.dynamic_update_index_in_dim(grad_store, grad_in, slot, 0), grad_store
        )
        qkv_store = jnp.where(
            active, lax.dynamic_update_index_in_dim(qkv_store, qkv_grad, slot, 0), qkv_store
        )
        incoming_store = jnp.where(
            active,
            lax.dynamic_update_index_in_dim(incoming_store, incoming, slot, 0),
            incoming_store,
        )
        return (sent_down, grad_store, qkv_store, incoming_store)

    initial = (
        jnp.zeros((shard_rows, model_width), jnp.bfloat16),
        jnp.zeros((micro_count, shard_rows, model_width), jnp.bfloat16),
        jnp.zeros((micro_count, shard_rows, 3 * model_width), jnp.bfloat16),
        jnp.zeros((micro_count, shard_rows, model_width), jnp.bfloat16),
    )
    received, grad_store, qkv_store, incoming_store = lax.fori_loop(
        0, sections + micro_count - 1, step, initial
    )
    flat_norm = rounded_norm.reshape(-1, model_width)
    flat_attended = attended.reshape(-1, model_width)
    flat_qkv = qkv_store.reshape(-1, 3 * model_width)
    flat_incoming = incoming_store.reshape(-1, model_width)
    contract = (((0,), (0,)), ((), ()))
    first = lax.dot_general(flat_norm, flat_qkv, contract, preferred_element_type=jnp.float32)
    second = lax.dot_general(
        flat_attended, flat_incoming, contract, preferred_element_type=jnp.float32
    )
    summed = lax.psum_scatter(
        jnp.concatenate([first, second], 1).astype(jnp.bfloat16),
        "tm",
        scatter_dimension=0,
        tiled=True,
    ).astype(jnp.float32)
    return (
        grad_store[None],
        summed[None, :, : 3 * model_width],
        summed[None, :, 3 * model_width :],
    )


def side_by_side(transposed, pair):
    width = 2 * HEAD_DIM
    rows = transposed[pair * width : (pair + 1) * width]
    empty = jnp.zeros((HEAD_DIM, rows.shape[1]), rows.dtype)
    return jnp.concatenate(
        [
            jnp.concatenate([rows[:HEAD_DIM], empty], 0),
            jnp.concatenate([empty, rows[HEAD_DIM:]], 0),
        ],
        1,
    )


def one_above_other(rows, masks):
    return jnp.concatenate([rows * masks[0], rows * masks[1]], 0)


def head_masks():
    lane = lax.broadcasted_iota(jnp.int32, (1, 2 * HEAD_DIM), 1)
    return [
        jnp.where(lane < HEAD_DIM, 1.0, 0.0).astype(jnp.bfloat16),
        jnp.where(lane < HEAD_DIM, 0.0, 1.0).astype(jnp.bfloat16),
    ]


def key_bias_rows(flag_rows, levels, shard_rows, keys, first_query, count):
    key_at = lax.broadcasted_iota(jnp.int32, (keys, count), 0)
    query_at = lax.broadcasted_iota(jnp.int32, (keys, count), 1) + first_query
    gap = lax.div(query_at, shard_rows) - lax.div(key_at, shard_rows)
    allowed = (gap == 0) & (key_at <= query_at)
    for level in range(levels):
        allowed = allowed | ((gap == 2**level) & (flag_rows[level : level + 1] != 0))
    return jnp.where(allowed, 0.0, negative_fill)


def softmax_pass(queries, keys, values, bias, prob_ref, rounded_ref, at_ref):
    queries_t = queries.T
    values_t = values.T
    width = 2 * HEAD_DIM
    count = queries.shape[0]
    for pair in range(queries.shape[1] // width):
        at_pair = slice(pair * width, (pair + 1) * width)
        scores = jnp.dot(
            keys[:, at_pair], side_by_side(queries_t, pair), preferred_element_type=jnp.float32
        )
        for half in range(2):
            at_half = slice(half * count, (half + 1) * count)
            biased = scores[:, at_half] + bias
            shifted_exp = jnp.exp(biased - jnp.max(biased, axis=0, keepdims=True))
            probability = shifted_exp * (1.0 / jnp.sum(shifted_exp, axis=0, keepdims=True))
            prob_ref[pair, :, at_half] = probability
            rounded_ref[pair, :, at_half] = probability.astype(jnp.bfloat16)
    for head in range(queries.shape[1] // HEAD_DIM):
        at = slice(head * HEAD_DIM, (head + 1) * HEAD_DIM)
        at_half = slice(head % 2 * count, (head % 2 + 1) * count)
        at_ref[at] = jnp.dot(
            values_t[at], rounded_ref[head // 2, :, at_half], preferred_element_type=jnp.float32
        ).astype(jnp.bfloat16)


def pack_kernel(
    levels, info_ref, acts_ref, top_ref, own_ref, other_ref, own_top_ref, other_top_ref, sems
):
    model_width = acts_ref.shape[2]
    shard_rows = own_ref.shape[0]
    side = info_ref[2]
    copies = [
        pltpu.make_async_copy(acts_ref.at[side], own_ref.at[:, :model_width], sems.at[0]),
        pltpu.make_async_copy(acts_ref.at[1 - side], other_ref.at[:, :model_width], sems.at[1]),
        pltpu.make_async_copy(top_ref.at[side], own_top_ref, sems.at[2]),
        pltpu.make_async_copy(top_ref.at[1 - side], other_top_ref, sems.at[3]),
    ]
    for copy in copies:
        copy.start()
    lane = lax.broadcasted_iota(jnp.int32, (shard_rows, own_ref.shape[1] - model_width), 1)
    flags = jnp.zeros(lane.shape, jnp.float32)
    for level in range(levels):
        seen = jnp.where(info_ref[4 + level] != 0, 1.0, 0.0)
        flags = jnp.where(lane == level, seen, flags)
    own_ref[:, model_width:] = flags.astype(jnp.bfloat16)
    other_ref[:, model_width:] = flags.astype(jnp.bfloat16)
    for copy in copies:
        copy.wait()


def touch_kernel(w_ref, after_ref, out_ref):
    out_ref[...] = w_ref[: out_ref.shape[0], : out_ref.shape[1]]


def project_kernel(replicas, info_ref, *refs):
    pieces = refs[: 4 * replicas]
    w_ref, _, acts_ref, norm_ref, flag_ref, q_ref, k_ref, v_ref, kt_ref, packed_ref = refs[
        4 * replicas :
    ]
    shards, shard_rows, model_width = acts_ref.shape
    seq = shards * shard_rows
    columns = q_ref.shape[1]
    at_piece = 0
    for core in (info_ref[0], 1 - info_ref[0]):
        for side in (info_ref[2], 1 - info_ref[2]):
            for step in range(replicas):
                shard = side * (shards // 2) + place_of(info_ref, step, replicas) + core
                packed_ref[shard] = pieces[at_piece][...]
                at_piece += 1
    acts_ref[...] = packed_ref[:, :, :model_width]
    normed, _ = normalize(acts_ref[...].reshape(seq, model_width))
    rounded = normed.astype(jnp.bfloat16)
    norm_ref[...] = rounded
    flag_ref[...] = packed_ref[:, :, model_width:].reshape(seq, -1).astype(jnp.float32).T
    scale_factor = HEAD_DIM ** (-0.5)
    for block, out_ref in enumerate((q_ref, k_ref, v_ref)):
        first = pl.multiple_of(block * model_width + info_ref[0] * columns, 128)
        product = jnp.dot(
            rounded, w_ref[:, pl.ds(first, columns)], preferred_element_type=jnp.float32
        ).astype(jnp.bfloat16)
        out_ref[...] = product * scale_factor if block == 0 else product
    kt_ref[...] = (k_ref[...] * scale_factor).T


def upper_forward_kernel(
    levels, shard_rows, flag_ref, q_ref, k_ref, v_ref, prob_ref, rounded_ref, at_ref
):
    seq = q_ref.shape[0]
    count = seq // 2
    bias = key_bias_rows(flag_ref[:, count:], levels, shard_rows, seq, count, count)
    softmax_pass(q_ref[count:], k_ref[...], v_ref[...], bias, prob_ref, rounded_ref, at_ref)


def lower_forward_kernel(
    levels,
    shard_rows,
    info_ref,
    norm_ref,
    flag_ref,
    q_ref,
    k_ref,
    v_ref,
    prob_ref,
    rounded_ref,
    at_ref,
    gt_ref,
):
    seq = norm_ref.shape[0]
    count = seq // 2
    bias = key_bias_rows(flag_ref[:, :count], levels, shard_rows, count, 0, count)
    softmax_pass(q_ref[:count], k_ref[:count], v_ref[:count], bias, prob_ref, rounded_ref, at_ref)
    rows = gt_ref.shape[1]
    half_width = norm_ref.shape[1] // 2
    for place in range(2):
        half = 1 - info_ref[2] if place == 0 else info_ref[2]
        first = pl.multiple_of(half * half_width + info_ref[1] * rows, 128)
        gt_ref[place] = norm_ref[:, pl.ds(first, rows)].T


def place_of(info_ref, step, replicas):
    return 2 * lax.rem(info_ref[1] - step + replicas, replicas)


def merge_rows(info_ref, fresh, got_refs, kept_refs, out_refs, rows_ref):
    @pl.when(fresh)
    def _():
        for core, out_ref in enumerate(out_refs):
            refs = got_refs[core * len(got_refs) // 2 : (core + 1) * len(got_refs) // 2]
            if len(refs) == 1:
                out_ref[...] = refs[0][...]
            else:
                for step, got_ref in enumerate(refs):
                    out_ref[step] = got_ref[...]

    @pl.when(jnp.logical_not(fresh))
    def _():
        for out_ref, kept_ref in zip(out_refs, kept_refs):
            out_ref[...] = kept_ref[...]

    place_rows(info_ref, out_refs, rows_ref)


def place_rows(info_ref, out_refs, rows_ref):
    replicas = out_refs[0].shape[0]
    for step in range(replicas):
        place = place_of(info_ref, step, replicas)
        rows_ref[place + info_ref[0]] = out_refs[0][step]
        rows_ref[place + 1 - info_ref[0]] = out_refs[1][step]


def merge_tops(info_ref, upper, piece_refs, out_refs, rows_ref):
    replicas = out_refs[0].shape[0]
    own_chunk = info_ref[2] == (1 if upper else 0)
    for core in range(2):
        refs = piece_refs[2 * replicas * core : 2 * replicas * (core + 1)]

        @pl.when(own_chunk)
        def _():
            for step in range(replicas):
                out_refs[core][step] = refs[step][...]

        @pl.when(jnp.logical_not(own_chunk))
        def _():
            for step in range(replicas):
                out_refs[core][step] = refs[replicas + step][...]

    place_rows(info_ref, out_refs, rows_ref)


def backward_kernel(upper, tops, replicas, fresh_section, info_ref, *refs):
    refs = list(refs)
    got = tops or (2 * replicas + 2 if upper else 4)
    got_refs = refs[:got]
    w_ref, prob_ref, rounded_ref, q_ref, v_ref, kt_ref, at_ref = refs[got : got + 7]
    refs = refs[got + 7 :]
    if not upper:
        key_sum_ref, value_sum_ref, _ = refs[:3]
        refs = refs[3:]
    own_ref, other_ref, keep_ref, send_ref = refs[:4]
    refs = refs[4:]
    if upper:
        key_sum_ref, value_sum_ref = refs[:2]
        refs = refs[2:]
    grads_ref, rows_ref, scores_ref = refs
    shard_rows, model_width = own_ref.shape[1:]
    count = rows_ref.shape[0] * shard_rows
    keys = prob_ref.shape[1]
    parity = info_ref[0]
    columns = q_ref.shape[1]
    width = 2 * HEAD_DIM
    if tops:
        merge_tops(info_ref, upper, got_refs, (own_ref, other_ref), rows_ref)
    else:
        fresh = info_ref[3] == fresh_section
        merge_rows(info_ref, fresh, got_refs[:-2], got_refs[-2:], (own_ref, other_ref), rows_ref)
    rows = rows_ref[...].reshape(count, model_width)
    weights = w_ref[pl.ds(pl.multiple_of(parity * columns, 128), columns), :]
    over_width = (((1,), (1,)), ((), ()))
    upstream = lax.dot_general(
        rows, weights, over_width, preferred_element_type=jnp.float32
    ).astype(jnp.bfloat16)
    upstream_t = upstream.T
    product_t = upstream_t.astype(jnp.float32) * at_ref[...].astype(jnp.float32)
    first_query = keys - count
    masks = head_masks()

    def put(block, pair, part):
        first = block * columns + pair * width
        grads_ref[:, :, first : first + width] = part.astype(jnp.bfloat16).reshape(
            -1, shard_rows, width
        )

    for pair in range(columns // width):
        at_pair = slice(pair * width, (pair + 1) * width)
        prob_grad = jnp.dot(
            v_ref[:keys, at_pair], side_by_side(upstream_t, pair), preferred_element_type=jnp.float32
        )
        for half in range(2):
            at_half = slice(half * count, (half + 1) * count)
            first = pair * width + half * HEAD_DIM
            delta = jnp.sum(product_t[first : first + HEAD_DIM], axis=0, keepdims=True)
            scores_ref[pair, :, at_half] = (
                prob_ref[pair, :, at_half] * (prob_grad[:, at_half] - delta)
            ).astype(jnp.bfloat16)
        value_grad = jnp.dot(
            rounded_ref[pair],
            one_above_other(upstream[:, at_pair], masks),
            preferred_element_type=jnp.float32,
        )
        if upper:
            value_sum_ref[:, at_pair] = value_grad[:first_query]
            value_grad = value_grad[first_query:]
        else:
            value_grad = value_grad + value_sum_ref[:, at_pair]
        put(2, pair, value_grad)
    for pair in range(columns // width):
        at_pair = slice(pair * width, (pair + 1) * width)
        queries = q_ref[first_query : first_query + count, at_pair]
        key_grad = jnp.dot(
            scores_ref[pair], one_above_other(queries, masks), preferred_element_type=jnp.float32
        )
        if upper:
            key_sum_ref[:, at_pair] = key_grad[:first_query]
            key_grad = key_grad[first_query:]
        else:
            key_grad = key_grad + key_sum_ref[:, at_pair]
        put(1, pair, key_grad)
        query_grad = [
            jnp.dot(
                kt_ref[pair * width + half * HEAD_DIM : pair * width + (half + 1) * HEAD_DIM, :keys],
                scores_ref[pair, :, half * count : (half + 1) * count],
                preferred_element_type=jnp.float32,
            )
            for half in range(2)
        ]
        put(0, pair, jnp.concatenate(query_grad, 0).astype(jnp.bfloat16).T)
    for step in range(replicas):
        place = place_of(info_ref, step, replicas)
        keep_ref[step] = grads_ref[place + parity]
        send_ref[step] = grads_ref[place + 1 - parity]


def norm_kernel(
    upper, info_ref, keep_ref, got_ref, acts_ref, incoming_ref, w_ref, after_ref, *refs
):
    out_refs, rows_ref = refs[:-1], refs[-1]
    replicas, shard_rows, triple = keep_ref.shape
    columns = triple // 3
    model_width = w_ref.shape[0]
    rows = replicas * shard_rows
    parity = info_ref[0]
    for part_ref, half in ((keep_ref, parity), (got_ref, 1 - parity)):
        for block in range(3):
            first = pl.multiple_of(block * model_width + half * columns, 128)
            rows_ref[:, pl.ds(first, columns)] = part_ref[
                :, :, block * columns : (block + 1) * columns
            ].reshape(rows, columns)
    norm_grad = lax.dot_general(
        rows_ref[...], w_ref[...], (((1,), (1,)), ((), ())), preferred_element_type=jnp.float32
    )
    base = acts_ref.shape[0] // 2 if upper else 0
    values = jnp.concatenate(
        [
            acts_ref[base + place_of(info_ref, step, replicas) + parity]
            for step in range(replicas)
        ],
        0,
    )
    normed, inverse_rms = normalize(values)
    inner = jnp.mean(norm_grad * normed, axis=-1, keepdims=True)
    incoming = incoming_ref[...].reshape(rows, model_width).astype(jnp.float32)
    grad_in = incoming + inverse_rms * (norm_grad - normed * inner)
    grad_in = grad_in.astype(jnp.bfloat16)
    if upper:
        for step, out_ref in enumerate(out_refs):
            out_ref[...] = grad_in[step * shard_rows : (step + 1) * shard_rows]
    else:
        out_refs[0][...] = grad_in.reshape(out_refs[0].shape)


def blocks_of(info_ref, ref, place=None):
    rows = ref.shape[-2] // 2
    picked = []
    for block in (1 - info_ref[0], info_ref[0]):
        at = pl.ds(pl.multiple_of(block * rows, rows), rows)
        picked.append(ref[at] if place is None else ref[place, at])
    return picked


def w_in_kernel(place, info_ref, gt_ref, lower_ref, upper_ref, after_ref, pass_ref, keep_ref):
    count = lower_ref.shape[0] * lower_ref.shape[1]
    for rows, out_ref in zip(blocks_of(info_ref, gt_ref, place), (pass_ref, keep_ref)):
        total = jnp.zeros(out_ref.shape, jnp.float32)
        for chunk, part_ref in enumerate((lower_ref, upper_ref)):
            total += jnp.dot(
                rows[:, chunk * count : (chunk + 1) * count],
                part_ref[...].reshape(count, -1),
                preferred_element_type=jnp.float32,
            )
        out_ref[...] = total.astype(out_ref.dtype)


def w_out_kernel(fresh_section, info_ref, *refs):
    got_refs, kept_refs = refs[:2], refs[2:4]
    at_lower_ref, at_upper_ref, upper_ref = refs[4:7]
    send_refs, own_refs = refs[7:9], refs[9:11]
    part_ref, part_other_ref, rows_ref = refs[11:]
    merge_rows(
        info_ref,
        info_ref[3] == fresh_section,
        got_refs,
        kept_refs,
        (part_ref, part_other_ref),
        rows_ref,
    )
    rows = own_refs[0].shape[0]
    for core, send_ref, own_ref in zip((1 - info_ref[0], info_ref[0]), send_refs, own_refs):
        first = pl.multiple_of((2 * info_ref[1] + core) * rows, 128)
        total = jnp.zeros(own_ref.shape, jnp.float32)
        for at_ref, chunk_ref in ((at_lower_ref, rows_ref), (at_upper_ref, upper_ref)):
            total += jnp.dot(
                at_ref[pl.ds(first, rows)],
                chunk_ref[...].reshape(-1, own_ref.shape[1]),
                preferred_element_type=jnp.float32,
            )
        own_ref[...] = total
        send_ref[...] = total.astype(jnp.bfloat16)


def sum_kernel(own_ref, got_ref, out_ref):
    out_ref[...] = (own_ref[...] + got_ref[...].astype(jnp.float32)).astype(jnp.bfloat16)


def place_in_kernel(info_ref, own_ref, got_ref, sibling_ref, out_ref):
    columns = own_ref.shape[1] // 3
    own = own_ref[...] + got_ref[...].astype(jnp.float32)
    sibling = sibling_ref[...].astype(jnp.float32)
    for part, half in ((own, info_ref[0]), (sibling, 1 - info_ref[0])):
        for block in range(3):
            first = pl.multiple_of((2 * block + half) * columns, 128)
            out_ref[:, pl.ds(first, columns)] = part[:, block * columns : (block + 1) * columns]


def place_out_kernel(info_ref, own_ref, got_ref, sibling_ref, out_ref):
    owner = info_ref[0] == info_ref[2]

    @pl.when(owner)
    def _():
        out_ref[...] = own_ref[...] + got_ref[...].astype(jnp.float32)

    @pl.when(jnp.logical_not(owner))
    def _():
        out_ref[...] = sibling_ref[...].astype(jnp.float32)


def call(kernel, outs, operands, scratch=(), flops=0, scalars=1, after=None, mebibytes=12, far=0):
    in_specs = [pl.BlockSpec(memory_space=pltpu.SMEM)] * scalars
    in_specs += [pl.BlockSpec(memory_space=pltpu.HBM)] * far
    in_specs += [pl.BlockSpec(memory_space=pltpu.VMEM)] * (len(operands) - scalars - far)
    moved = sum(item.size * item.dtype.itemsize for item in [*operands, *outs])
    if after is not None:
        operands = [*operands, after]
        in_specs.append(pl.BlockSpec(memory_space=pl.ANY))
    return pl.pallas_call(
        kernel,
        out_shape=list(outs),
        in_specs=in_specs,
        out_specs=[pl.BlockSpec(memory_space=pltpu.VMEM)] * len(outs),
        scratch_shapes=list(scratch),
        cost_estimate=pl.CostEstimate(flops=flops, bytes_accessed=moved, transcendentals=0),
        compiler_params=pltpu.CompilerParams(vmem_limit_bytes=mebibytes * 2**20),
    )(*operands)


def by_chips(acts, grad_top, w_in, w_out, offsets):
    half_type, full_type = jnp.bfloat16, jnp.float32
    shape = jax.ShapeDtypeStruct
    sections = lax.axis_size("section")
    shards = lax.axis_size("tm")
    levels = offsets.shape[1]
    half = shards // 2
    replicas = half // 2
    me = lax.axis_index("tm")
    parity = lax.rem(me, 2)
    side = lax.div(me, half)
    micro_count, shard_rows, model_width = acts.shape[1:]
    columns = model_width // 2
    heads = columns // HEAD_DIM
    seq = shards * shard_rows
    count = seq // 2
    w_qkv = w_in[0]
    w_rows = w_out[0]
    info = jnp.stack([parity, lax.div(lax.rem(me, half), 2), side, lax.axis_index("section")])
    info = jnp.concatenate([info.astype(jnp.int32), offsets[0]])
    across = [(source, (source + half) % shards) for source in range(shards)]
    cores = [(source, source + 1 - 2 * (source % 2)) for source in range(shards)]
    homeward = [pair for pair in across if pair[0] // half != pair[0] % 2]
    around = [
        [
            (source, source // half * half + (source % half + 2 * step) % half)
            for source in range(shards)
        ]
        for step in range(replicas)
    ]

    packed = shape((shard_rows, model_width + 128), half_type)
    top_shape = shape((shard_rows, model_width), half_type)
    own_acts, other_acts, own_top, other_top = call(
        functools.partial(pack_kernel, levels),
        [packed, packed, top_shape, top_shape],
        [info, acts[0], grad_top],
        scratch=[pltpu.SemaphoreType.DMA((4,))],
        far=2,
    )
    swapped = lax.ppermute(other_acts, "tm", across)
    pieces = [own_acts]
    pieces += [lax.ppermute(own_acts, "tm", around[step]) for step in range(1, replicas)]
    pieces += [swapped]
    pieces += [lax.ppermute(swapped, "tm", around[step]) for step in range(1, replicas)]
    other_top = lax.ppermute(other_top, "tm", across)
    pieces[-1], other_top = lax.optimization_barrier((pieces[-1], other_top))
    pieces += [lax.ppermute(piece, "tm", cores) for piece in pieces]
    (touched,) = call(
        touch_kernel, [shape((16, 128), half_type)], [w_qkv], scalars=0, after=swapped
    )
    tops = [own_top]
    tops += [lax.ppermute(own_top, "tm", around[step]) for step in range(1, replicas)]
    tops += [other_top]
    tops += [lax.ppermute(other_top, "tm", around[step]) for step in range(1, replicas)]

    rows_shape = shape((seq, columns), half_type)
    acts_all, norm, flag_rows, queries, keys, values, keys_t = call(
        functools.partial(project_kernel, replicas),
        [
            shape((shards, shard_rows, model_width), half_type),
            shape((seq, model_width), half_type),
            shape((128, seq), full_type),
            rows_shape,
            rows_shape,
            rows_shape,
            shape((columns, seq), half_type),
        ],
        [info, *pieces, w_qkv],
        scratch=[pltpu.VMEM((shards, *packed.shape), half_type)],
        flops=6 * seq * model_width * columns,
        after=touched,
    )
    tops, _ = lax.optimization_barrier((tuple(tops), keys_t))
    tops = [*tops, *[lax.ppermute(piece, "tm", cores) for piece in tops]]
    pairs = heads // 2
    upper_prob, upper_rounded, upper_at = call(
        functools.partial(upper_forward_kernel, levels, shard_rows),
        [
            shape((pairs, seq, 2 * count), full_type),
            shape((pairs, seq, 2 * count), half_type),
            shape((columns, count), half_type),
        ],
        [flag_rows, queries, keys, values],
        scalars=0,
        flops=4 * columns * seq * count,
    )
    own_rows = model_width // shards
    block_rows = 2 * own_rows
    lower_prob, lower_rounded, lower_at, norm_t = call(
        functools.partial(lower_forward_kernel, levels, shard_rows),
        [
            shape((pairs, count, 2 * count), full_type),
            shape((pairs, count, 2 * count), half_type),
            shape((columns, count), half_type),
            shape((2, block_rows, seq), half_type),
        ],
        [info, norm, flag_rows, queries, keys, values],
        flops=4 * columns * count * count,
    )
    probs = {True: (upper_prob, upper_rounded), False: (lower_prob, lower_rounded)}
    attended = {True: upper_at, False: lower_at}
    got, kept = {}, {}
    piece_shape = shape((replicas, shard_rows, model_width), half_type)
    grads_shape = shape((replicas, shard_rows, 3 * columns), half_type)
    sum_shape = shape((count, columns), full_type)
    full_grads = shape((half, shard_rows, 3 * columns), half_type)
    full_rows = shape((half, shard_rows, model_width), half_type)
    rows_scratch = pltpu.VMEM(full_rows.shape, half_type)
    grads_scratch = pltpu.VMEM(full_grads.shape, half_type)
    result, full = {}, {}
    grad_in = keys_t
    for turn in range(sections):
        last = turn + 1 == sections
        fresh_section = sections - 1 - turn
        sums, parts, crossed = [], {}, {}
        for upper in (True, False):
            rows_in = tops
            if turn:
                before = result[False] if upper else keep
                pieces = []
                for piece in got[upper]:
                    piece, before = lax.optimization_barrier((piece, before))
                    pieces.append(piece)
                got[upper] = pieces
                if upper:
                    result[False] = before
                else:
                    keep = parts[True] = before
                others = [lax.ppermute(piece, "tm", cores) for piece in got[upper]]
                rows_in = [*got[upper], *others, *kept[upper]]
            after = None
            if last and not upper:
                out_pass, out_keep, own_pass, own_keep = call(
                    functools.partial(w_out_kernel, fresh_section),
                    [shape((own_rows, model_width), half_type)] * 2
                    + [shape((own_rows, model_width), full_type)] * 2,
                    [info, *rows_in, lower_at, upper_at, ordered],
                    scratch=[
                        pltpu.VMEM(piece_shape.shape, half_type),
                        pltpu.VMEM(piece_shape.shape, half_type),
                        rows_scratch,
                    ],
                    flops=2 * block_rows * seq * model_width,
                )
                after = out_keep
            elif not upper:
                after = keep
            outs = [piece_shape, piece_shape, grads_shape, grads_shape]
            outs += [sum_shape, sum_shape] if upper else []
            scratch = []
            if last:
                outs += [full_grads]
            else:
                scratch += [grads_scratch]
            if last and upper:
                outs += [full_rows]
            else:
                scratch += [rows_scratch]
            part_keys = seq if upper else count
            scratch += [pltpu.VMEM((pairs, part_keys, 2 * count), half_type)]
            answer = call(
                functools.partial(
                    backward_kernel, upper, 0 if turn else len(tops), replicas, fresh_section
                ),
                outs,
                [info, *rows_in, w_rows, *probs[upper], queries, values, keys_t]
                + [attended[upper], *sums],
                scratch=scratch,
                flops=2 * count * columns * (2 * model_width + 4 * part_keys),
                after=after,
            )
            kept[upper] = tuple(answer[:2])
            keep, send = answer[2:4]
            parts[upper] = keep
            if upper:
                sums = answer[4:6]
            if last:
                full[upper] = answer[6 if upper else 4]
            if last and upper:
                ordered = answer[7]
            crossed[upper] = lax.ppermute(send, "tm", cores)
        if last:
            got_pass = lax.ppermute(out_pass, "tm", homeward)
            got_keep = lax.ppermute(out_keep, "tm", homeward)
            _, out_done = lax.optimization_barrier((got_keep, got_pass))
        for upper in (True, False):
            grad_pieces = call(
                functools.partial(norm_kernel, upper),
                [top_shape] * replicas if upper else [piece_shape],
                [info, parts[upper], crossed[upper], acts_all, kept[upper][0], w_qkv],
                scratch=[pltpu.VMEM((replicas * shard_rows, 3 * model_width), half_type)],
                flops=6 * replicas * shard_rows * model_width * model_width,
                after=grad_in,
            )
            result[upper] = grad_pieces
            grad_in = grad_pieces[-1]
            if not last:
                hop = [(sections - 1 - turn, sections - 2 - turn)]
                got[upper] = [lax.ppermute(piece, "section", hop) for piece in grad_pieces]

    term_flops = 2 * block_rows * seq * 3 * columns
    term_shape = (own_rows, 3 * columns)
    in_pass, in_keep = call(
        functools.partial(w_in_kernel, 0),
        [shape(term_shape, half_type)] * 2,
        [info, norm_t, full[False], full[True]],
        flops=term_flops,
        after=out_done,
    )
    in_got_pass = lax.ppermute(in_pass, "tm", across)
    in_got_keep = lax.ppermute(in_keep, "tm", across)

    upper_own, lower_own = result[True][0], result[False][0][0]
    mine = jnp.where(side == 1, upper_own, lower_own)
    partner = jnp.where(side == 1, lower_own, upper_own)
    in_own_pass, in_own_keep = call(
        functools.partial(w_in_kernel, 1),
        [shape(term_shape, full_type)] * 2,
        [info, norm_t, full[False], full[True]],
        flops=term_flops,
        after=partner,
    )
    partner = lax.ppermute(partner, "tm", across)

    (to_pass,) = call(
        sum_kernel, [shape((own_rows, model_width), half_type)], [own_pass, got_pass], scalars=0
    )
    to_sibling = [pair for pair in cores if pair[0] // half == pair[0] % 2]
    (d_w_out,) = call(
        place_out_kernel,
        [shape((own_rows, model_width), full_type)],
        [info, own_keep, got_keep, lax.ppermute(to_pass, "tm", to_sibling)],
    )
    (to_pass,) = call(
        sum_kernel, [shape(term_shape, half_type)], [in_own_pass, in_got_pass], scalars=0
    )
    (d_w_in,) = call(
        place_in_kernel,
        [shape((own_rows, 3 * model_width), full_type)],
        [info, in_own_keep, in_got_keep, lax.ppermute(to_pass, "tm", cores)],
    )
    d_acts = jnp.where(side == 0, jnp.stack([mine, partner]), jnp.stack([partner, mine]))
    return (d_acts[None], d_w_in[None], d_w_out[None])


def layer_gradients(acts, grad_top, w_in, w_out, offsets):
    shards = lax.axis_size("tm")
    micro_count, shard_rows, model_width = acts.shape[1:]
    heads = model_width // HEAD_DIM
    prob_bytes = 2 * heads * (shards * shard_rows) ** 2
    fits = prob_bytes <= 2**24 and model_width % (128 * shards) == 0 and shard_rows % 16 == 0
    if micro_count == 2 and shards % 4 == 0 and heads % 4 == 0 and fits:
        return by_chips(acts, grad_top, w_in, w_out, offsets)
    return per_device(acts, grad_top, w_in, w_out, offsets)


def solution(mesh):
    placed = (
        P("section", None, "tm", None),
        P(None, "tm", None),
        P("section", None, None),
        P("section", None, None),
        P("tm", None),
    )
    return jax.shard_map(
        layer_gradients,
        mesh=mesh,
        in_specs=placed,
        out_specs=(
            P("section", None, "tm", None),
            P("section", "tm", None),
            P("section", "tm", None),
        ),
        check_vma=False,
    )
```

```python
import functools
import jax
import jax.numpy as jnp
from jax import lax
from jax.experimental import pallas as pl
from jax.experimental.pallas import tpu as pltpu
from jax.sharding import PartitionSpec as P

HEAD_DIM = 64


epsilon = 1e-06
negative_fill = -1e30


def shifted(value, axis, steps):
    count = lax.axis_size(axis)
    initial, last = (max(0, -steps), min(count, count - steps))
    return lax.ppermute(value, axis, [(source, source + steps) for source in range(initial, last)])


def normalize(inputs):
    values = inputs.astype(jnp.float32)
    inverse_rms = lax.rsqrt(jnp.mean(values * values, axis=-1, keepdims=True) + epsilon)
    return (values * inverse_rms, inverse_rms)


def key_bias(level_flags, shard_rows):
    position = jnp.arange(shard_rows)
    own_part = position[None, :] <= position[:, None]
    far_part = jnp.repeat(level_flags != 0, shard_rows)
    far_part = jnp.broadcast_to(far_part[None, :], (shard_rows, far_part.shape[0]))
    return jnp.concatenate([own_part, far_part], 1)


def split_heads(row_block):
    return row_block.reshape(row_block.shape[0], -1, HEAD_DIM)


def softmax_keys(queries, key_heads, allowed):
    scores = jnp.einsum(
        "ihd,jhd->hij", queries, key_heads, preferred_element_type=jnp.float32
    ) * HEAD_DIM ** (-0.5)
    scores = jnp.where(allowed[None], scores, negative_fill)
    highest = jnp.max(scores, axis=-1, keepdims=True)
    shifted_exp = jnp.where(allowed[None], jnp.exp(scores - highest), 0.0)
    return shifted_exp / jnp.sum(shifted_exp, axis=-1, keepdims=True)


def attend(query_rows, key_rows, allowed):
    model_width = query_rows.shape[1]
    probability = softmax_keys(
        split_heads(query_rows), split_heads(key_rows[:, :model_width]), allowed
    )
    attended = jnp.einsum(
        "hij,jhd->ihd",
        probability.astype(jnp.bfloat16),
        split_heads(key_rows[:, model_width:]),
        preferred_element_type=jnp.float32,
    )
    return attended.reshape(query_rows.shape).astype(jnp.bfloat16)


def attend_back(query_rows, key_rows, allowed, incoming, attended, w_proj):
    model_width = query_rows.shape[1]
    queries = split_heads(query_rows)
    key_heads = split_heads(key_rows[:, :model_width])
    value_heads = split_heads(key_rows[:, model_width:])
    probability = softmax_keys(queries, key_heads, allowed)
    rounded = probability.astype(jnp.bfloat16)
    upstream = lax.dot_general(
        incoming, w_proj, (((1,), (1,)), ((), ())), preferred_element_type=jnp.float32
    ).astype(jnp.bfloat16)
    up_heads = split_heads(upstream)
    delta = jnp.einsum(
        "ihd,ihd->hi", up_heads.astype(jnp.float32), split_heads(attended).astype(jnp.float32)
    )[..., None]
    prob_grad = jnp.einsum(
        "ihd,jhd->hij", up_heads, value_heads, preferred_element_type=jnp.float32
    )
    score_grad = (probability * (prob_grad - delta)).astype(jnp.bfloat16)
    scale_factor = HEAD_DIM ** (-0.5)
    query_grad = (
        jnp.einsum("hij,jhd->ihd", score_grad, key_heads, preferred_element_type=jnp.float32)
        * scale_factor
    )
    key_grad = (
        jnp.einsum("hij,ihd->jhd", score_grad, queries, preferred_element_type=jnp.float32)
        * scale_factor
    )
    value_grad = jnp.einsum("hij,ihd->jhd", rounded, up_heads, preferred_element_type=jnp.float32)
    return (
        query_grad.reshape(-1, model_width),
        key_grad.reshape(-1, model_width),
        value_grad.reshape(-1, model_width),
    )


def per_device(acts, grad_top, w_in, w_out, offsets):
    sections = lax.axis_size("section")
    shards = lax.axis_size("tm")
    levels = shards.bit_length() - 1
    section_index = lax.axis_index("section")
    micro_count = acts.shape[1]
    shard_rows = acts.shape[2]
    model_width = acts.shape[3]
    w_qkv = w_in[0]
    w_proj = w_out[0]
    level_flags = offsets[0]
    normed, inverse_rms = normalize(acts[0])
    rounded_norm = normed.astype(jnp.bfloat16)
    qkv = jnp.dot(rounded_norm.reshape(-1, model_width), w_qkv, preferred_element_type=jnp.float32)
    qkv = qkv.astype(jnp.bfloat16).reshape(micro_count, shard_rows, 3 * model_width)
    pairs = qkv[..., model_width:]
    far_list = [shifted(pairs, "tm", 2**level) for level in range(levels)]
    key_rows = jnp.concatenate([pairs] + far_list, 1)
    allowed = key_bias(level_flags, shard_rows)
    attended = jnp.stack(
        [
            attend(qkv[index, :, :model_width], key_rows[index], allowed)
            for index in range(micro_count)
        ],
        0,
    )

    def attention_part(incoming, slot):
        query_rows = lax.dynamic_index_in_dim(qkv, slot, 0, False)[:, :model_width]
        slot_keys = lax.dynamic_index_in_dim(key_rows, slot, 0, False)
        slot_attended = lax.dynamic_index_in_dim(attended, slot, 0, False)
        query_grad, key_grad, value_grad = attend_back(
            query_rows, slot_keys, allowed, incoming, slot_attended, w_proj
        )
        owner_sum = jnp.concatenate([key_grad[:shard_rows], value_grad[:shard_rows]], 1)
        far_part = jnp.concatenate([key_grad[shard_rows:], value_grad[shard_rows:]], 1)
        far_part = far_part.astype(jnp.bfloat16).reshape(levels, shard_rows, 2 * model_width)
        return (query_grad, owner_sum, far_part)

    def empty_attention(incoming, slot):
        return (
            jnp.zeros((shard_rows, model_width), jnp.float32),
            jnp.zeros((shard_rows, 2 * model_width), jnp.float32),
            jnp.zeros((levels, shard_rows, 2 * model_width), jnp.bfloat16),
        )

    def norm_part(qkv_grad, incoming, slot):
        norm_grad = lax.dot_general(
            qkv_grad, w_qkv, (((1,), (1,)), ((), ())), preferred_element_type=jnp.float32
        )
        slot_normed = lax.dynamic_index_in_dim(normed, slot, 0, False)
        slot_rms = lax.dynamic_index_in_dim(inverse_rms, slot, 0, False)
        inner = jnp.mean(norm_grad * slot_normed, axis=-1, keepdims=True)
        return (incoming.astype(jnp.float32) + slot_rms * (norm_grad - slot_normed * inner)).astype(
            jnp.bfloat16
        )

    def empty_norm(qkv_grad, incoming, slot):
        return jnp.zeros((shard_rows, model_width), jnp.bfloat16)

    def step(turn, carry):
        received, grad_store, qkv_store, incoming_store = carry
        slot_raw = turn - (sections - 1 - section_index)
        active = (slot_raw >= 0) & (slot_raw < micro_count)
        slot = jnp.clip(slot_raw, 0, micro_count - 1)
        incoming = jnp.where(
            section_index == sections - 1,
            lax.dynamic_index_in_dim(grad_top, slot, 0, False),
            received,
        )
        query_grad, owner_sum, far_part = lax.cond(
            active, attention_part, empty_attention, incoming, slot
        )
        for level in range(levels):
            owner_sum = owner_sum + shifted(far_part[level], "tm", -(2**level)).astype(jnp.float32)
        qkv_grad = jnp.concatenate([query_grad, owner_sum], 1).astype(jnp.bfloat16)
        grad_in = lax.cond(active, norm_part, empty_norm, qkv_grad, incoming, slot)
        sent_down = shifted(grad_in, "section", -1)
        grad_store = jnp.where(
            active, lax.dynamic_update_index_in_dim(grad_store, grad_in, slot, 0), grad_store
        )
        qkv_store = jnp.where(
            active, lax.dynamic_update_index_in_dim(qkv_store, qkv_grad, slot, 0), qkv_store
        )
        incoming_store = jnp.where(
            active,
            lax.dynamic_update_index_in_dim(incoming_store, incoming, slot, 0),
            incoming_store,
        )
        return (sent_down, grad_store, qkv_store, incoming_store)

    initial = (
        jnp.zeros((shard_rows, model_width), jnp.bfloat16),
        jnp.zeros((micro_count, shard_rows, model_width), jnp.bfloat16),
        jnp.zeros((micro_count, shard_rows, 3 * model_width), jnp.bfloat16),
        jnp.zeros((micro_count, shard_rows, model_width), jnp.bfloat16),
    )
    received, grad_store, qkv_store, incoming_store = lax.fori_loop(
        0, sections + micro_count - 1, step, initial
    )
    flat_norm = rounded_norm.reshape(-1, model_width)
    flat_attended = attended.reshape(-1, model_width)
    flat_qkv = qkv_store.reshape(-1, 3 * model_width)
    flat_incoming = incoming_store.reshape(-1, model_width)
    contract = (((0,), (0,)), ((), ()))
    first = lax.dot_general(flat_norm, flat_qkv, contract, preferred_element_type=jnp.float32)
    second = lax.dot_general(
        flat_attended, flat_incoming, contract, preferred_element_type=jnp.float32
    )
    summed = lax.psum_scatter(
        jnp.concatenate([first, second], 1).astype(jnp.bfloat16),
        "tm",
        scatter_dimension=0,
        tiled=True,
    ).astype(jnp.float32)
    return (
        grad_store[None],
        summed[None, :, : 3 * model_width],
        summed[None, :, 3 * model_width :],
    )


def side_by_side(transposed, pair):
    width = 2 * HEAD_DIM
    rows = transposed[pair * width : (pair + 1) * width]
    empty = jnp.zeros((HEAD_DIM, rows.shape[1]), rows.dtype)
    return jnp.concatenate(
        [
            jnp.concatenate([rows[:HEAD_DIM], empty], 0),
            jnp.concatenate([empty, rows[HEAD_DIM:]], 0),
        ],
        1,
    )


def one_above_other(rows, masks):
    return jnp.concatenate([rows * masks[0], rows * masks[1]], 0)


def head_masks():
    lane = lax.broadcasted_iota(jnp.int32, (1, 2 * HEAD_DIM), 1)
    return [
        jnp.where(lane < HEAD_DIM, 1.0, 0.0).astype(jnp.bfloat16),
        jnp.where(lane < HEAD_DIM, 0.0, 1.0).astype(jnp.bfloat16),
    ]


def key_bias_rows(flag_rows, levels, shard_rows, keys, first_query, count):
    key_at = lax.broadcasted_iota(jnp.int32, (keys, count), 0)
    query_at = lax.broadcasted_iota(jnp.int32, (keys, count), 1) + first_query
    gap = lax.div(query_at, shard_rows) - lax.div(key_at, shard_rows)
    allowed = (gap == 0) & (key_at <= query_at)
    for level in range(levels):
        allowed = allowed | ((gap == 2**level) & (flag_rows[level : level + 1] != 0))
    return jnp.where(allowed, 0.0, negative_fill)


def softmax_pass(queries, keys, values, bias, prob_ref, at_ref):
    queries_t = queries.T
    values_t = values.T
    width = 2 * HEAD_DIM
    count = queries.shape[0]
    for pair in range(queries.shape[1] // width):
        at_pair = slice(pair * width, (pair + 1) * width)
        scores = jnp.dot(
            keys[:, at_pair], side_by_side(queries_t, pair), preferred_element_type=jnp.float32
        )
        for half in range(2):
            at_half = slice(half * count, (half + 1) * count)
            biased = scores[:, at_half] + bias
            shifted_exp = jnp.exp(biased - jnp.max(biased, axis=0, keepdims=True))
            probability = shifted_exp * (1.0 / jnp.sum(shifted_exp, axis=0, keepdims=True))
            prob_ref[pair, :, at_half] = probability.astype(jnp.bfloat16)
    for head in range(queries.shape[1] // HEAD_DIM):
        at = slice(head * HEAD_DIM, (head + 1) * HEAD_DIM)
        at_half = slice(head % 2 * count, (head % 2 + 1) * count)
        at_ref[at] = jnp.dot(
            values_t[at], prob_ref[head // 2, :, at_half], preferred_element_type=jnp.float32
        ).astype(jnp.bfloat16)


def pack_kernel(
    levels, info_ref, acts_ref, top_ref, own_ref, other_ref, own_top_ref, other_top_ref, sems
):
    model_width = acts_ref.shape[2]
    shard_rows = own_ref.shape[0]
    side = info_ref[2]
    copies = [
        pltpu.make_async_copy(acts_ref.at[side], own_ref.at[:, :model_width], sems.at[0]),
        pltpu.make_async_copy(acts_ref.at[1 - side], other_ref.at[:, :model_width], sems.at[1]),
        pltpu.make_async_copy(top_ref.at[side], own_top_ref, sems.at[2]),
        pltpu.make_async_copy(top_ref.at[1 - side], other_top_ref, sems.at[3]),
    ]
    for copy in copies:
        copy.start()
    lane = lax.broadcasted_iota(jnp.int32, (shard_rows, own_ref.shape[1] - model_width), 1)
    flags = jnp.zeros(lane.shape, jnp.float32)
    for level in range(levels):
        seen = jnp.where(info_ref[4 + level] != 0, 1.0, 0.0)
        flags = jnp.where(lane == level, seen, flags)
    own_ref[:, model_width:] = flags.astype(jnp.bfloat16)
    other_ref[:, model_width:] = flags.astype(jnp.bfloat16)
    for copy in copies:
        copy.wait()


def touch_kernel(w_ref, after_ref, out_ref):
    out_ref[...] = w_ref[: out_ref.shape[0], : out_ref.shape[1]]


def project_kernel(replicas, info_ref, *refs):
    pieces = refs[: 4 * replicas]
    w_ref, _, normed_ref, rms_ref, norm_ref, flag_ref, q_ref, k_ref, v_ref, kt_ref, packed_ref = refs[
        4 * replicas :
    ]
    shards, shard_rows = packed_ref.shape[:2]
    model_width = w_ref.shape[0]
    seq = shards * shard_rows
    columns = q_ref.shape[1]
    at_piece = 0
    for core in (info_ref[0], 1 - info_ref[0]):
        for side in (info_ref[2], 1 - info_ref[2]):
            for step in range(replicas):
                shard = side * (shards // 2) + place_of(info_ref, step, replicas) + core
                packed_ref[shard] = pieces[at_piece][...]
                at_piece += 1
    for chunk in range(2):
        for step in range(replicas):
            shard = chunk * (shards // 2) + place_of(info_ref, step, replicas) + info_ref[0]
            normed, inverse_rms = normalize(packed_ref[shard][:, :model_width])
            normed_ref[chunk, step] = normed
            rms_ref[chunk, step] = jnp.broadcast_to(inverse_rms, rms_ref.shape[2:])
    normed, _ = normalize(packed_ref[:, :, :model_width].reshape(seq, model_width))
    rounded = normed.astype(jnp.bfloat16)
    norm_ref[...] = rounded
    flag_ref[...] = packed_ref[:, :, model_width:].reshape(seq, -1).astype(jnp.float32).T
    scale_factor = HEAD_DIM ** (-0.5)
    for block, out_ref in enumerate((q_ref, k_ref, v_ref)):
        first = pl.multiple_of(block * model_width + info_ref[0] * columns, 128)
        product = jnp.dot(
            rounded, w_ref[:, pl.ds(first, columns)], preferred_element_type=jnp.float32
        ).astype(jnp.bfloat16)
        out_ref[...] = product * scale_factor if block == 0 else product
    kt_ref[...] = (k_ref[...] * scale_factor).T


def upper_forward_kernel(
    levels, shard_rows, flag_ref, q_ref, k_ref, v_ref, prob_ref, at_ref
):
    seq = q_ref.shape[0]
    count = seq // 2
    bias = key_bias_rows(flag_ref[:, count:], levels, shard_rows, seq, count, count)
    softmax_pass(q_ref[count:], k_ref[...], v_ref[...], bias, prob_ref, at_ref)


def lower_forward_kernel(
    levels,
    shard_rows,
    info_ref,
    norm_ref,
    flag_ref,
    q_ref,
    k_ref,
    v_ref,
    prob_ref,
    at_ref,
    gt_ref,
):
    seq = norm_ref.shape[0]
    count = seq // 2
    bias = key_bias_rows(flag_ref[:, :count], levels, shard_rows, count, 0, count)
    softmax_pass(q_ref[:count], k_ref[:count], v_ref[:count], bias, prob_ref, at_ref)
    rows = gt_ref.shape[1]
    half_width = norm_ref.shape[1] // 2
    for place in range(2):
        half = 1 - info_ref[2] if place == 0 else info_ref[2]
        first = pl.multiple_of(half * half_width + info_ref[1] * rows, 128)
        gt_ref[place] = norm_ref[:, pl.ds(first, rows)].T


def place_of(info_ref, step, replicas):
    return 2 * lax.rem(info_ref[1] - step + replicas, replicas)


def merge_rows(info_ref, fresh, got_refs, kept_refs, out_refs, rows_ref):
    @pl.when(fresh)
    def _():
        for core, out_ref in enumerate(out_refs):
            refs = got_refs[core * len(got_refs) // 2 : (core + 1) * len(got_refs) // 2]
            if len(refs) == 1:
                out_ref[...] = refs[0][...]
            else:
                for step, got_ref in enumerate(refs):
                    out_ref[step] = got_ref[...]

    @pl.when(jnp.logical_not(fresh))
    def _():
        for out_ref, kept_ref in zip(out_refs, kept_refs):
            out_ref[...] = kept_ref[...]

    place_rows(info_ref, out_refs, rows_ref)


def place_rows(info_ref, out_refs, rows_ref):
    replicas = out_refs[0].shape[0]
    for step in range(replicas):
        place = place_of(info_ref, step, replicas)
        rows_ref[place + info_ref[0]] = out_refs[0][step]
        rows_ref[place + 1 - info_ref[0]] = out_refs[1][step]


def merge_tops(info_ref, upper, piece_refs, out_refs, rows_ref):
    replicas = out_refs[0].shape[0]
    own_chunk = info_ref[2] == (1 if upper else 0)
    for core in range(2):
        refs = piece_refs[2 * replicas * core : 2 * replicas * (core + 1)]

        @pl.when(own_chunk)
        def _():
            for step in range(replicas):
                out_refs[core][step] = refs[step][...]

        @pl.when(jnp.logical_not(own_chunk))
        def _():
            for step in range(replicas):
                out_refs[core][step] = refs[replicas + step][...]

    place_rows(info_ref, out_refs, rows_ref)


def backward_kernel(upper, tops, replicas, fresh_section, info_ref, *refs):
    refs = list(refs)
    got = tops or (2 * replicas + 2 if upper else 4)
    got_refs = refs[:got]
    w_ref, prob_ref, q_ref, v_ref, kt_ref, at_ref = refs[got : got + 6]
    refs = refs[got + 6 :]
    if not upper:
        key_sum_ref, value_sum_ref, _ = refs[:3]
        refs = refs[3:]
    own_ref, other_ref, keep_ref, send_ref = refs[:4]
    refs = refs[4:]
    if upper:
        key_sum_ref, value_sum_ref = refs[:2]
        refs = refs[2:]
    grads_ref, rows_ref, scores_ref = refs
    shard_rows, model_width = own_ref.shape[1:]
    count = rows_ref.shape[0] * shard_rows
    keys = prob_ref.shape[1]
    parity = info_ref[0]
    columns = q_ref.shape[1]
    width = 2 * HEAD_DIM
    if tops:
        merge_tops(info_ref, upper, got_refs, (own_ref, other_ref), rows_ref)
    else:
        fresh = info_ref[3] == fresh_section
        merge_rows(info_ref, fresh, got_refs[:-2], got_refs[-2:], (own_ref, other_ref), rows_ref)
    rows = rows_ref[...].reshape(count, model_width)
    weights = w_ref[pl.ds(pl.multiple_of(parity * columns, 128), columns), :]
    over_width = (((1,), (1,)), ((), ()))
    upstream = lax.dot_general(
        rows, weights, over_width, preferred_element_type=jnp.float32
    ).astype(jnp.bfloat16)
    upstream_t = upstream.T
    product_t = upstream_t.astype(jnp.float32) * at_ref[...].astype(jnp.float32)
    first_query = keys - count
    masks = head_masks()

    def put(block, pair, part):
        first = block * columns + pair * width
        grads_ref[:, :, first : first + width] = part.astype(jnp.bfloat16).reshape(
            -1, shard_rows, width
        )

    for pair in range(columns // width):
        at_pair = slice(pair * width, (pair + 1) * width)
        prob_grad = jnp.dot(
            v_ref[:keys, at_pair], side_by_side(upstream_t, pair), preferred_element_type=jnp.float32
        )
        for half in range(2):
            at_half = slice(half * count, (half + 1) * count)
            first = pair * width + half * HEAD_DIM
            delta = jnp.sum(product_t[first : first + HEAD_DIM], axis=0, keepdims=True)
            scores_ref[pair, :, at_half] = (
                prob_ref[pair, :, at_half].astype(jnp.float32) * (prob_grad[:, at_half] - delta)
            ).astype(jnp.bfloat16)
        value_grad = jnp.dot(
            prob_ref[pair],
            one_above_other(upstream[:, at_pair], masks),
            preferred_element_type=jnp.float32,
        )
        if upper:
            value_sum_ref[:, at_pair] = value_grad[:first_query]
            value_grad = value_grad[first_query:]
        else:
            value_grad = value_grad + value_sum_ref[:, at_pair]
        put(2, pair, value_grad)
    for pair in range(columns // width):
        at_pair = slice(pair * width, (pair + 1) * width)
        queries = q_ref[first_query : first_query + count, at_pair]
        key_grad = jnp.dot(
            scores_ref[pair], one_above_other(queries, masks), preferred_element_type=jnp.float32
        )
        if upper:
            key_sum_ref[:, at_pair] = key_grad[:first_query]
            key_grad = key_grad[first_query:]
        else:
            key_grad = key_grad + key_sum_ref[:, at_pair]
        put(1, pair, key_grad)
        query_grad = [
            jnp.dot(
                kt_ref[pair * width + half * HEAD_DIM : pair * width + (half + 1) * HEAD_DIM, :keys],
                scores_ref[pair, :, half * count : (half + 1) * count],
                preferred_element_type=jnp.float32,
            )
            for half in range(2)
        ]
        put(0, pair, jnp.concatenate(query_grad, 0).astype(jnp.bfloat16).T)
    for step in range(replicas):
        place = place_of(info_ref, step, replicas)
        keep_ref[step] = grads_ref[place + parity]
        send_ref[step] = grads_ref[place + 1 - parity]


def norm_kernel(
    chunk, info_ref, keep_ref, got_ref, normed_ref, rms_ref, incoming_ref, w_ref, after_ref, *out_refs
):
    replicas, shard_rows, triple = keep_ref.shape
    columns = triple // 3
    model_width = w_ref.shape[0]
    rows = replicas * shard_rows
    norm_grad = jnp.zeros((rows, model_width), jnp.float32)
    for part_ref, half in ((keep_ref, info_ref[0]), (got_ref, 1 - info_ref[0])):
        for block in range(3):
            first = pl.multiple_of(block * model_width + half * columns, 128)
            norm_grad += lax.dot_general(
                part_ref[:, :, block * columns : (block + 1) * columns].reshape(rows, columns),
                w_ref[:, pl.ds(first, columns)],
                (((1,), (1,)), ((), ())),
                preferred_element_type=jnp.float32,
            )
    normed = normed_ref[chunk].reshape(rows, model_width)
    inverse_rms = rms_ref[chunk].reshape(rows, -1)[:, :1]
    inner = jnp.mean(norm_grad * normed, axis=-1, keepdims=True)
    incoming = incoming_ref[...].reshape(rows, model_width).astype(jnp.float32)
    grad_in = incoming + inverse_rms * (norm_grad - normed * inner)
    grad_in = grad_in.astype(jnp.bfloat16).reshape(replicas, shard_rows, model_width)
    if len(out_refs) == 1:
        out_refs[0][...] = grad_in
    else:
        for step, out_ref in enumerate(out_refs):
            out_ref[...] = grad_in[step]


def w_in_kernel(place, info_ref, gt_ref, lower_ref, upper_ref, after_ref, *refs):
    out_refs, sum_ref = refs[:2], refs[2]
    count = lower_ref.shape[0] * lower_ref.shape[1]
    rows = out_refs[0].shape[0]
    total = jnp.zeros(sum_ref.shape, jnp.float32)
    for chunk, part_ref in enumerate((lower_ref, upper_ref)):
        total += jnp.dot(
            gt_ref[place, :, chunk * count : (chunk + 1) * count],
            part_ref[...].reshape(count, -1),
            preferred_element_type=jnp.float32,
        )
    sum_ref[...] = total
    for core, out_ref in zip((1 - info_ref[0], info_ref[0]), out_refs):
        at = pl.ds(pl.multiple_of(core * rows, rows), rows)
        out_ref[...] = sum_ref[at].astype(out_ref.dtype)


def w_out_kernel(info_ref, at_lower_ref, at_upper_ref, lower_ref, upper_ref, after_ref, *refs):
    send_refs, own_refs = refs[:2], refs[2:]
    rows = own_refs[0].shape[0]
    for core, send_ref, own_ref in zip((1 - info_ref[0], info_ref[0]), send_refs, own_refs):
        first = pl.multiple_of((2 * info_ref[1] + core) * rows, 128)
        total = jnp.zeros(own_ref.shape, jnp.float32)
        for at_ref, chunk_ref in ((at_lower_ref, lower_ref), (at_upper_ref, upper_ref)):
            total += jnp.dot(
                at_ref[pl.ds(first, rows)],
                chunk_ref[...].reshape(-1, own_ref.shape[1]),
                preferred_element_type=jnp.float32,
            )
        own_ref[...] = total
        send_ref[...] = total.astype(jnp.bfloat16)


def sum_kernel(own_ref, got_ref, out_ref):
    out_ref[...] = (own_ref[...] + got_ref[...].astype(jnp.float32)).astype(jnp.bfloat16)


def place_in_kernel(info_ref, own_ref, got_ref, sibling_ref, out_ref):
    columns = own_ref.shape[1] // 3
    own = own_ref[...] + got_ref[...].astype(jnp.float32)
    sibling = sibling_ref[...].astype(jnp.float32)
    for part, half in ((own, info_ref[0]), (sibling, 1 - info_ref[0])):
        for block in range(3):
            first = pl.multiple_of((2 * block + half) * columns, 128)
            out_ref[:, pl.ds(first, columns)] = part[:, block * columns : (block + 1) * columns]


def place_out_kernel(info_ref, own_ref, got_ref, sibling_ref, out_ref):
    owner = info_ref[0] == info_ref[2]

    @pl.when(owner)
    def _():
        out_ref[...] = own_ref[...] + got_ref[...].astype(jnp.float32)

    @pl.when(jnp.logical_not(owner))
    def _():
        out_ref[...] = sibling_ref[...].astype(jnp.float32)


def call(kernel, outs, operands, scratch=(), flops=0, scalars=1, after=None, mebibytes=12, far=0):
    in_specs = [pl.BlockSpec(memory_space=pltpu.SMEM)] * scalars
    in_specs += [pl.BlockSpec(memory_space=pltpu.HBM)] * far
    in_specs += [pl.BlockSpec(memory_space=pltpu.VMEM)] * (len(operands) - scalars - far)
    moved = sum(item.size * item.dtype.itemsize for item in [*operands, *outs])
    if after is not None:
        operands = [*operands, after]
        in_specs.append(pl.BlockSpec(memory_space=pl.ANY))
    return pl.pallas_call(
        kernel,
        out_shape=list(outs),
        in_specs=in_specs,
        out_specs=[pl.BlockSpec(memory_space=pltpu.VMEM)] * len(outs),
        scratch_shapes=list(scratch),
        cost_estimate=pl.CostEstimate(flops=flops, bytes_accessed=moved, transcendentals=0),
        compiler_params=pltpu.CompilerParams(vmem_limit_bytes=mebibytes * 2**20),
    )(*operands)


def by_chips(acts, grad_top, w_in, w_out, offsets):
    half_type, full_type = jnp.bfloat16, jnp.float32
    shape = jax.ShapeDtypeStruct
    sections = lax.axis_size("section")
    shards = lax.axis_size("tm")
    levels = offsets.shape[1]
    half = shards // 2
    replicas = half // 2
    me = lax.axis_index("tm")
    parity = lax.rem(me, 2)
    side = lax.div(me, half)
    micro_count, shard_rows, model_width = acts.shape[1:]
    columns = model_width // 2
    heads = columns // HEAD_DIM
    seq = shards * shard_rows
    count = seq // 2
    w_qkv = w_in[0]
    w_rows = w_out[0]
    info = jnp.stack([parity, lax.div(lax.rem(me, half), 2), side, lax.axis_index("section")])
    info = jnp.concatenate([info.astype(jnp.int32), offsets[0]])
    across = [(source, (source + half) % shards) for source in range(shards)]
    cores = [(source, source + 1 - 2 * (source % 2)) for source in range(shards)]
    homeward = [pair for pair in across if pair[0] // half != pair[0] % 2]
    around = [
        [
            (source, source // half * half + (source % half + 2 * step) % half)
            for source in range(shards)
        ]
        for step in range(replicas)
    ]

    packed = shape((shard_rows, model_width + 128), half_type)
    top_shape = shape((shard_rows, model_width), half_type)
    own_acts, other_acts, own_top, other_top = call(
        functools.partial(pack_kernel, levels),
        [packed, packed, top_shape, top_shape],
        [info, acts[0], grad_top],
        scratch=[pltpu.SemaphoreType.DMA((4,))],
        far=2,
    )
    swapped = lax.ppermute(other_acts, "tm", across)
    (touched,) = call(
        touch_kernel, [shape((16, 128), half_type)], [w_qkv], scalars=0, after=own_acts
    )
    swapped, touched = lax.optimization_barrier((swapped, touched))
    pieces = [own_acts]
    pieces += [lax.ppermute(own_acts, "tm", around[step]) for step in range(1, replicas)]
    pieces += [swapped]
    pieces += [lax.ppermute(swapped, "tm", around[step]) for step in range(1, replicas)]
    other_top = lax.ppermute(other_top, "tm", across)
    pieces[-1], other_top = lax.optimization_barrier((pieces[-1], other_top))
    pieces += [lax.ppermute(piece, "tm", cores) for piece in pieces]
    tops = [own_top]
    tops += [lax.ppermute(own_top, "tm", around[step]) for step in range(1, replicas)]
    tops += [other_top]
    tops += [lax.ppermute(other_top, "tm", around[step]) for step in range(1, replicas)]

    rows_shape = shape((seq, columns), half_type)
    normed, rms, norm, flag_rows, queries, keys, values, keys_t = call(
        functools.partial(project_kernel, replicas),
        [
            shape((2, replicas, shard_rows, model_width), full_type),
            shape((2, replicas, shard_rows, 128), full_type),
            shape((seq, model_width), half_type),
            shape((128, seq), full_type),
            rows_shape,
            rows_shape,
            rows_shape,
            shape((columns, seq), half_type),
        ],
        [info, *pieces, w_qkv],
        scratch=[pltpu.VMEM((shards, *packed.shape), half_type)],
        flops=6 * seq * model_width * columns,
        after=touched,
    )
    tops, _ = lax.optimization_barrier((tuple(tops), keys_t))
    tops = [*tops, *[lax.ppermute(piece, "tm", cores) for piece in tops]]
    pairs = heads // 2
    upper_prob, upper_at = call(
        functools.partial(upper_forward_kernel, levels, shard_rows),
        [
            shape((pairs, seq, 2 * count), half_type),
            shape((columns, count), half_type),
        ],
        [flag_rows, queries, keys, values],
        scalars=0,
        flops=4 * columns * seq * count,
    )
    own_rows = model_width // shards
    block_rows = 2 * own_rows
    lower_prob, lower_at, norm_t = call(
        functools.partial(lower_forward_kernel, levels, shard_rows),
        [
            shape((pairs, count, 2 * count), half_type),
            shape((columns, count), half_type),
            shape((2, block_rows, seq), half_type),
        ],
        [info, norm, flag_rows, queries, keys, values],
        flops=4 * columns * count * count,
    )
    probs = {True: upper_prob, False: lower_prob}
    attended = {True: upper_at, False: lower_at}
    got, kept = {}, {}
    piece_shape = shape((replicas, shard_rows, model_width), half_type)
    grads_shape = shape((replicas, shard_rows, 3 * columns), half_type)
    sum_shape = shape((count, columns), full_type)
    full_grads = shape((half, shard_rows, 3 * columns), half_type)
    full_rows = shape((half, shard_rows, model_width), half_type)
    term_flops = 2 * block_rows * seq * 3 * columns
    term_shape = (own_rows, 3 * columns)
    term_scratch = pltpu.VMEM((block_rows, 3 * columns), full_type)
    rows_scratch = pltpu.VMEM(full_rows.shape, half_type)
    grads_scratch = pltpu.VMEM(full_grads.shape, half_type)
    result, full, ordered = {}, {}, {}
    grad_in = keys_t
    for turn in range(sections):
        last = turn + 1 == sections
        fresh_section = sections - 1 - turn
        sums, parts, crossed = [], {}, {}
        for upper in (True, False):
            rows_in = tops
            if turn:
                before = result[False] if upper else keep
                pieces = []
                for piece in got[upper]:
                    piece, before = lax.optimization_barrier((piece, before))
                    pieces.append(piece)
                got[upper] = pieces
                if upper:
                    result[False] = before
                else:
                    keep = parts[True] = before
                others = [lax.ppermute(piece, "tm", cores) for piece in got[upper]]
                rows_in = [*got[upper], *others, *kept[upper]]
            after = None if upper else keep
            outs = [piece_shape, piece_shape, grads_shape, grads_shape]
            outs += [sum_shape, sum_shape] if upper else []
            scratch = []
            if last:
                outs += [full_grads]
            else:
                scratch += [grads_scratch]
            if last:
                outs += [full_rows]
            else:
                scratch += [rows_scratch]
            part_keys = seq if upper else count
            scratch += [pltpu.VMEM((pairs, part_keys, 2 * count), half_type)]
            answer = call(
                functools.partial(
                    backward_kernel, upper, 0 if turn else len(tops), replicas, fresh_section
                ),
                outs,
                [info, *rows_in, w_rows, probs[upper], queries, values, keys_t]
                + [attended[upper], *sums],
                scratch=scratch,
                flops=2 * count * columns * (2 * model_width + 4 * part_keys),
                after=after,
            )
            kept[upper] = tuple(answer[:2])
            keep, send = answer[2:4]
            parts[upper] = keep
            if upper:
                sums = answer[4:6]
            if last:
                full[upper], ordered[upper] = answer[-2:]
            crossed[upper] = lax.ppermute(send, "tm", cores)
        if last:
            in_pass, in_keep = call(
                functools.partial(w_in_kernel, 0),
                [shape(term_shape, half_type)] * 2,
                [info, norm_t, full[False], full[True]],
                scratch=[term_scratch],
                flops=term_flops,
                after=keep,
            )
            grad_in = in_keep
        for upper in (True, False):
            grad_pieces = call(
                functools.partial(norm_kernel, 1 if upper else 0),
                [top_shape] * replicas if upper else [piece_shape],
                [info, parts[upper], crossed[upper], normed, rms, kept[upper][0], w_qkv],
                flops=6 * replicas * shard_rows * model_width * model_width,
                after=grad_in,
            )
            result[upper] = grad_pieces
            grad_in = grad_pieces[-1]
            if not last:
                hop = [(sections - 1 - turn, sections - 2 - turn)]
                got[upper] = [lax.ppermute(piece, "section", hop) for piece in grad_pieces]

    in_got_pass = lax.ppermute(in_pass, "tm", across)
    in_got_keep = lax.ppermute(in_keep, "tm", across)

    upper_own, lower_own = result[True][0], result[False][0][0]
    mine = jnp.where(side == 1, upper_own, lower_own)
    partner = jnp.where(side == 1, lower_own, upper_own)
    in_own_pass, in_own_keep = call(
        functools.partial(w_in_kernel, 1),
        [shape(term_shape, full_type)] * 2,
        [info, norm_t, full[False], full[True]],
        scratch=[term_scratch],
        flops=term_flops,
        after=partner,
    )
    out_pass, out_keep, own_pass, own_keep = call(
        w_out_kernel,
        [shape((own_rows, model_width), half_type)] * 2
        + [shape((own_rows, model_width), full_type)] * 2,
        [info, lower_at, upper_at, ordered[False], ordered[True]],
        flops=2 * block_rows * seq * model_width,
        after=in_keep,
    )
    got_pass = lax.ppermute(out_pass, "tm", homeward)
    got_keep = lax.ppermute(out_keep, "tm", homeward)
    partner = lax.ppermute(partner, "tm", across)

    (to_pass,) = call(
        sum_kernel, [shape((own_rows, model_width), half_type)], [own_pass, got_pass], scalars=0
    )
    to_sibling = [pair for pair in cores if pair[0] // half == pair[0] % 2]
    (d_w_out,) = call(
        place_out_kernel,
        [shape((own_rows, model_width), full_type)],
        [info, own_keep, got_keep, lax.ppermute(to_pass, "tm", to_sibling)],
    )
    (to_pass,) = call(
        sum_kernel, [shape(term_shape, half_type)], [in_own_pass, in_got_pass], scalars=0
    )
    (d_w_in,) = call(
        place_in_kernel,
        [shape((own_rows, 3 * model_width), full_type)],
        [info, in_own_keep, in_got_keep, lax.ppermute(to_pass, "tm", cores)],
    )
    d_acts = jnp.where(side == 0, jnp.stack([mine, partner]), jnp.stack([partner, mine]))
    return (d_acts[None], d_w_in[None], d_w_out[None])


def layer_gradients(acts, grad_top, w_in, w_out, offsets):
    shards = lax.axis_size("tm")
    micro_count, shard_rows, model_width = acts.shape[1:]
    heads = model_width // HEAD_DIM
    prob_bytes = 2 * heads * (shards * shard_rows) ** 2
    fits = prob_bytes <= 2**24 and model_width % (128 * shards) == 0 and shard_rows % 16 == 0
    if micro_count == 2 and shards % 4 == 0 and heads % 4 == 0 and fits:
        return by_chips(acts, grad_top, w_in, w_out, offsets)
    return per_device(acts, grad_top, w_in, w_out, offsets)


def solution(mesh):
    placed = (
        P("section", None, "tm", None),
        P(None, "tm", None),
        P("section", None, None),
        P("section", None, None),
        P("tm", None),
    )
    return jax.shard_map(
        layer_gradients,
        mesh=mesh,
        in_specs=placed,
        out_specs=(
            P("section", None, "tm", None),
            P("section", "tm", None),
            P("section", "tm", None),
        ),
        check_vma=False,
    )
```

```python
import functools
import jax
import jax.numpy as jnp
from jax import lax
from jax.experimental import pallas as pl
from jax.experimental.pallas import tpu as pltpu
from jax.sharding import PartitionSpec as P

HEAD_DIM = 64


epsilon = 1e-06
negative_fill = -1e30


def shifted(value, axis, steps):
    count = lax.axis_size(axis)
    initial, last = (max(0, -steps), min(count, count - steps))
    return lax.ppermute(value, axis, [(source, source + steps) for source in range(initial, last)])


def normalize(inputs):
    values = inputs.astype(jnp.float32)
    inverse_rms = lax.rsqrt(jnp.mean(values * values, axis=-1, keepdims=True) + epsilon)
    return (values * inverse_rms, inverse_rms)


def key_bias(level_flags, shard_rows):
    position = jnp.arange(shard_rows)
    own_part = position[None, :] <= position[:, None]
    far_part = jnp.repeat(level_flags != 0, shard_rows)
    far_part = jnp.broadcast_to(far_part[None, :], (shard_rows, far_part.shape[0]))
    return jnp.concatenate([own_part, far_part], 1)


def split_heads(row_block):
    return row_block.reshape(row_block.shape[0], -1, HEAD_DIM)


def softmax_keys(queries, key_heads, allowed):
    scores = jnp.einsum(
        "ihd,jhd->hij", queries, key_heads, preferred_element_type=jnp.float32
    ) * HEAD_DIM ** (-0.5)
    scores = jnp.where(allowed[None], scores, negative_fill)
    highest = jnp.max(scores, axis=-1, keepdims=True)
    shifted_exp = jnp.where(allowed[None], jnp.exp(scores - highest), 0.0)
    return shifted_exp / jnp.sum(shifted_exp, axis=-1, keepdims=True)


def attend(query_rows, key_rows, allowed):
    model_width = query_rows.shape[1]
    probability = softmax_keys(
        split_heads(query_rows), split_heads(key_rows[:, :model_width]), allowed
    )
    attended = jnp.einsum(
        "hij,jhd->ihd",
        probability.astype(jnp.bfloat16),
        split_heads(key_rows[:, model_width:]),
        preferred_element_type=jnp.float32,
    )
    return attended.reshape(query_rows.shape).astype(jnp.bfloat16)


def attend_back(query_rows, key_rows, allowed, incoming, attended, w_proj):
    model_width = query_rows.shape[1]
    queries = split_heads(query_rows)
    key_heads = split_heads(key_rows[:, :model_width])
    value_heads = split_heads(key_rows[:, model_width:])
    probability = softmax_keys(queries, key_heads, allowed)
    rounded = probability.astype(jnp.bfloat16)
    upstream = lax.dot_general(
        incoming, w_proj, (((1,), (1,)), ((), ())), preferred_element_type=jnp.float32
    ).astype(jnp.bfloat16)
    up_heads = split_heads(upstream)
    delta = jnp.einsum(
        "ihd,ihd->hi", up_heads.astype(jnp.float32), split_heads(attended).astype(jnp.float32)
    )[..., None]
    prob_grad = jnp.einsum(
        "ihd,jhd->hij", up_heads, value_heads, preferred_element_type=jnp.float32
    )
    score_grad = (probability * (prob_grad - delta)).astype(jnp.bfloat16)
    scale_factor = HEAD_DIM ** (-0.5)
    query_grad = (
        jnp.einsum("hij,jhd->ihd", score_grad, key_heads, preferred_element_type=jnp.float32)
        * scale_factor
    )
    key_grad = (
        jnp.einsum("hij,ihd->jhd", score_grad, queries, preferred_element_type=jnp.float32)
        * scale_factor
    )
    value_grad = jnp.einsum("hij,ihd->jhd", rounded, up_heads, preferred_element_type=jnp.float32)
    return (
        query_grad.reshape(-1, model_width),
        key_grad.reshape(-1, model_width),
        value_grad.reshape(-1, model_width),
    )


def per_device(acts, grad_top, w_in, w_out, offsets):
    sections = lax.axis_size("section")
    shards = lax.axis_size("tm")
    levels = shards.bit_length() - 1
    section_index = lax.axis_index("section")
    micro_count = acts.shape[1]
    shard_rows = acts.shape[2]
    model_width = acts.shape[3]
    w_qkv = w_in[0]
    w_proj = w_out[0]
    level_flags = offsets[0]
    normed, inverse_rms = normalize(acts[0])
    rounded_norm = normed.astype(jnp.bfloat16)
    qkv = jnp.dot(rounded_norm.reshape(-1, model_width), w_qkv, preferred_element_type=jnp.float32)
    qkv = qkv.astype(jnp.bfloat16).reshape(micro_count, shard_rows, 3 * model_width)
    pairs = qkv[..., model_width:]
    far_list = [shifted(pairs, "tm", 2**level) for level in range(levels)]
    key_rows = jnp.concatenate([pairs] + far_list, 1)
    allowed = key_bias(level_flags, shard_rows)
    attended = jnp.stack(
        [
            attend(qkv[index, :, :model_width], key_rows[index], allowed)
            for index in range(micro_count)
        ],
        0,
    )

    def attention_part(incoming, slot):
        query_rows = lax.dynamic_index_in_dim(qkv, slot, 0, False)[:, :model_width]
        slot_keys = lax.dynamic_index_in_dim(key_rows, slot, 0, False)
        slot_attended = lax.dynamic_index_in_dim(attended, slot, 0, False)
        query_grad, key_grad, value_grad = attend_back(
            query_rows, slot_keys, allowed, incoming, slot_attended, w_proj
        )
        owner_sum = jnp.concatenate([key_grad[:shard_rows], value_grad[:shard_rows]], 1)
        far_part = jnp.concatenate([key_grad[shard_rows:], value_grad[shard_rows:]], 1)
        far_part = far_part.astype(jnp.bfloat16).reshape(levels, shard_rows, 2 * model_width)
        return (query_grad, owner_sum, far_part)

    def empty_attention(incoming, slot):
        return (
            jnp.zeros((shard_rows, model_width), jnp.float32),
            jnp.zeros((shard_rows, 2 * model_width), jnp.float32),
            jnp.zeros((levels, shard_rows, 2 * model_width), jnp.bfloat16),
        )

    def norm_part(qkv_grad, incoming, slot):
        norm_grad = lax.dot_general(
            qkv_grad, w_qkv, (((1,), (1,)), ((), ())), preferred_element_type=jnp.float32
        )
        slot_normed = lax.dynamic_index_in_dim(normed, slot, 0, False)
        slot_rms = lax.dynamic_index_in_dim(inverse_rms, slot, 0, False)
        inner = jnp.mean(norm_grad * slot_normed, axis=-1, keepdims=True)
        return (incoming.astype(jnp.float32) + slot_rms * (norm_grad - slot_normed * inner)).astype(
            jnp.bfloat16
        )

    def empty_norm(qkv_grad, incoming, slot):
        return jnp.zeros((shard_rows, model_width), jnp.bfloat16)

    def step(turn, carry):
        received, grad_store, qkv_store, incoming_store = carry
        slot_raw = turn - (sections - 1 - section_index)
        active = (slot_raw >= 0) & (slot_raw < micro_count)
        slot = jnp.clip(slot_raw, 0, micro_count - 1)
        incoming = jnp.where(
            section_index == sections - 1,
            lax.dynamic_index_in_dim(grad_top, slot, 0, False),
            received,
        )
        query_grad, owner_sum, far_part = lax.cond(
            active, attention_part, empty_attention, incoming, slot
        )
        for level in range(levels):
            owner_sum = owner_sum + shifted(far_part[level], "tm", -(2**level)).astype(jnp.float32)
        qkv_grad = jnp.concatenate([query_grad, owner_sum], 1).astype(jnp.bfloat16)
        grad_in = lax.cond(active, norm_part, empty_norm, qkv_grad, incoming, slot)
        sent_down = shifted(grad_in, "section", -1)
        grad_store = jnp.where(
            active, lax.dynamic_update_index_in_dim(grad_store, grad_in, slot, 0), grad_store
        )
        qkv_store = jnp.where(
            active, lax.dynamic_update_index_in_dim(qkv_store, qkv_grad, slot, 0), qkv_store
        )
        incoming_store = jnp.where(
            active,
            lax.dynamic_update_index_in_dim(incoming_store, incoming, slot, 0),
            incoming_store,
        )
        return (sent_down, grad_store, qkv_store, incoming_store)

    initial = (
        jnp.zeros((shard_rows, model_width), jnp.bfloat16),
        jnp.zeros((micro_count, shard_rows, model_width), jnp.bfloat16),
        jnp.zeros((micro_count, shard_rows, 3 * model_width), jnp.bfloat16),
        jnp.zeros((micro_count, shard_rows, model_width), jnp.bfloat16),
    )
    received, grad_store, qkv_store, incoming_store = lax.fori_loop(
        0, sections + micro_count - 1, step, initial
    )
    flat_norm = rounded_norm.reshape(-1, model_width)
    flat_attended = attended.reshape(-1, model_width)
    flat_qkv = qkv_store.reshape(-1, 3 * model_width)
    flat_incoming = incoming_store.reshape(-1, model_width)
    contract = (((0,), (0,)), ((), ()))
    first = lax.dot_general(flat_norm, flat_qkv, contract, preferred_element_type=jnp.float32)
    second = lax.dot_general(
        flat_attended, flat_incoming, contract, preferred_element_type=jnp.float32
    )
    summed = lax.psum_scatter(
        jnp.concatenate([first, second], 1).astype(jnp.bfloat16),
        "tm",
        scatter_dimension=0,
        tiled=True,
    ).astype(jnp.float32)
    return (
        grad_store[None],
        summed[None, :, : 3 * model_width],
        summed[None, :, 3 * model_width :],
    )


def side_by_side(transposed, pair):
    width = 2 * HEAD_DIM
    rows = transposed[pair * width : (pair + 1) * width]
    empty = jnp.zeros((HEAD_DIM, rows.shape[1]), rows.dtype)
    return jnp.concatenate(
        [
            jnp.concatenate([rows[:HEAD_DIM], empty], 0),
            jnp.concatenate([empty, rows[HEAD_DIM:]], 0),
        ],
        1,
    )


def one_above_other(rows, masks):
    return jnp.concatenate([rows * masks[0], rows * masks[1]], 0)


def head_masks():
    lane = lax.broadcasted_iota(jnp.int32, (1, 2 * HEAD_DIM), 1)
    return [
        jnp.where(lane < HEAD_DIM, 1.0, 0.0).astype(jnp.bfloat16),
        jnp.where(lane < HEAD_DIM, 0.0, 1.0).astype(jnp.bfloat16),
    ]


def key_bias_rows(flag_rows, levels, shard_rows, keys, first_query, count):
    key_at = lax.broadcasted_iota(jnp.int32, (keys, count), 0)
    query_at = lax.broadcasted_iota(jnp.int32, (keys, count), 1) + first_query
    gap = lax.div(query_at, shard_rows) - lax.div(key_at, shard_rows)
    allowed = (gap == 0) & (key_at <= query_at)
    for level in range(levels):
        allowed = allowed | ((gap == 2**level) & (flag_rows[level : level + 1] != 0))
    return jnp.where(allowed, 0.0, negative_fill)


def softmax_pass(queries, keys, values, bias, prob_ref, at_ref):
    queries_t = queries.T
    values_t = values.T
    width = 2 * HEAD_DIM
    count = queries.shape[0]
    for pair in range(queries.shape[1] // width):
        at_pair = slice(pair * width, (pair + 1) * width)
        scores = jnp.dot(
            keys[:, at_pair], side_by_side(queries_t, pair), preferred_element_type=jnp.float32
        )
        for half in range(2):
            at_half = slice(half * count, (half + 1) * count)
            biased = scores[:, at_half] + bias
            shifted_exp = jnp.exp(biased - jnp.max(biased, axis=0, keepdims=True))
            probability = shifted_exp * (1.0 / jnp.sum(shifted_exp, axis=0, keepdims=True))
            prob_ref[pair, :, at_half] = probability.astype(jnp.bfloat16)
    for head in range(queries.shape[1] // HEAD_DIM):
        at = slice(head * HEAD_DIM, (head + 1) * HEAD_DIM)
        at_half = slice(head % 2 * count, (head % 2 + 1) * count)
        at_ref[at] = jnp.dot(
            values_t[at], prob_ref[head // 2, :, at_half], preferred_element_type=jnp.float32
        ).astype(jnp.bfloat16)


def pack_kernel(
    levels, info_ref, acts_ref, top_ref, own_ref, other_ref, own_top_ref, other_top_ref, sems
):
    model_width = acts_ref.shape[2]
    shard_rows = own_ref.shape[0]
    side = info_ref[2]
    copies = [
        pltpu.make_async_copy(acts_ref.at[side], own_ref.at[:, :model_width], sems.at[0]),
        pltpu.make_async_copy(acts_ref.at[1 - side], other_ref.at[:, :model_width], sems.at[1]),
        pltpu.make_async_copy(top_ref.at[side], own_top_ref, sems.at[2]),
        pltpu.make_async_copy(top_ref.at[1 - side], other_top_ref, sems.at[3]),
    ]
    for copy in copies:
        copy.start()
    lane = lax.broadcasted_iota(jnp.int32, (shard_rows, own_ref.shape[1] - model_width), 1)
    flags = jnp.zeros(lane.shape, jnp.float32)
    for level in range(levels):
        seen = jnp.where(info_ref[4 + level] != 0, 1.0, 0.0)
        flags = jnp.where(lane == level, seen, flags)
    own_ref[:, model_width:] = flags.astype(jnp.bfloat16)
    other_ref[:, model_width:] = flags.astype(jnp.bfloat16)
    for copy in copies:
        copy.wait()


def touch_kernel(w_ref, after_ref, out_ref):
    out_ref[...] = w_ref[: out_ref.shape[0], : out_ref.shape[1]]


def project_kernel(replicas, info_ref, *refs):
    pieces = refs[: 4 * replicas]
    w_ref, _, normed_ref, rms_ref, norm_ref, flag_ref, q_ref, k_ref, v_ref, kt_ref, packed_ref = refs[
        4 * replicas :
    ]
    shards, shard_rows = packed_ref.shape[:2]
    model_width = w_ref.shape[0]
    seq = shards * shard_rows
    columns = q_ref.shape[1]
    at_piece = 0
    for core in (info_ref[0], 1 - info_ref[0]):
        for side in (info_ref[2], 1 - info_ref[2]):
            for step in range(replicas):
                shard = side * (shards // 2) + place_of(info_ref, step, replicas) + core
                packed_ref[shard] = pieces[at_piece][...]
                at_piece += 1
    for chunk in range(2):
        for step in range(replicas):
            shard = chunk * (shards // 2) + place_of(info_ref, step, replicas) + info_ref[0]
            normed, inverse_rms = normalize(packed_ref[shard][:, :model_width])
            normed_ref[chunk, step] = normed
            rms_ref[chunk, step] = jnp.broadcast_to(inverse_rms, rms_ref.shape[2:])
    normed, _ = normalize(packed_ref[:, :, :model_width].reshape(seq, model_width))
    rounded = normed.astype(jnp.bfloat16)
    norm_ref[...] = rounded
    flag_ref[...] = packed_ref[:, :, model_width:].reshape(seq, -1).astype(jnp.float32).T
    scale_factor = HEAD_DIM ** (-0.5)
    for block, out_ref in enumerate((q_ref, k_ref, v_ref)):
        first = pl.multiple_of(block * model_width + info_ref[0] * columns, 128)
        product = jnp.dot(
            rounded, w_ref[:, pl.ds(first, columns)], preferred_element_type=jnp.float32
        ).astype(jnp.bfloat16)
        out_ref[...] = product * scale_factor if block == 0 else product
    kt_ref[...] = (k_ref[...] * scale_factor).T


def upper_forward_kernel(
    levels, shard_rows, flag_ref, q_ref, k_ref, v_ref, prob_ref, at_ref
):
    seq = q_ref.shape[0]
    count = seq // 2
    bias = key_bias_rows(flag_ref[:, count:], levels, shard_rows, seq, count, count)
    softmax_pass(q_ref[count:], k_ref[...], v_ref[...], bias, prob_ref, at_ref)


def lower_forward_kernel(
    levels,
    shard_rows,
    info_ref,
    norm_ref,
    flag_ref,
    q_ref,
    k_ref,
    v_ref,
    after_ref,
    prob_ref,
    at_ref,
    gt_ref,
):
    seq = norm_ref.shape[0]
    count = seq // 2
    bias = key_bias_rows(flag_ref[:, :count], levels, shard_rows, count, 0, count)
    softmax_pass(q_ref[:count], k_ref[:count], v_ref[:count], bias, prob_ref, at_ref)
    rows = gt_ref.shape[1]
    half_width = norm_ref.shape[1] // 2
    for place in range(2):
        half = 1 - info_ref[2] if place == 0 else info_ref[2]
        first = pl.multiple_of(half * half_width + info_ref[1] * rows, 128)
        gt_ref[place] = norm_ref[:, pl.ds(first, rows)].T


def place_of(info_ref, step, replicas):
    return 2 * lax.rem(info_ref[1] - step + replicas, replicas)


def merge_rows(info_ref, fresh, got_refs, kept_refs, out_refs, rows_ref):
    @pl.when(fresh)
    def _():
        for core, out_ref in enumerate(out_refs):
            refs = got_refs[core * len(got_refs) // 2 : (core + 1) * len(got_refs) // 2]
            if len(refs) == 1:
                out_ref[...] = refs[0][...]
            else:
                for step, got_ref in enumerate(refs):
                    out_ref[step] = got_ref[...]

    @pl.when(jnp.logical_not(fresh))
    def _():
        for out_ref, kept_ref in zip(out_refs, kept_refs):
            out_ref[...] = kept_ref[...]

    place_rows(info_ref, out_refs, rows_ref)


def place_rows(info_ref, out_refs, rows_ref):
    replicas = out_refs[0].shape[0]
    for step in range(replicas):
        place = place_of(info_ref, step, replicas)
        rows_ref[place + info_ref[0]] = out_refs[0][step]
        rows_ref[place + 1 - info_ref[0]] = out_refs[1][step]


def merge_tops(info_ref, upper, piece_refs, out_refs, rows_ref):
    replicas = out_refs[0].shape[0]
    own_chunk = info_ref[2] == (1 if upper else 0)
    for core in range(2):
        refs = piece_refs[2 * replicas * core : 2 * replicas * (core + 1)]

        @pl.when(own_chunk)
        def _():
            for step in range(replicas):
                out_refs[core][step] = refs[step][...]

        @pl.when(jnp.logical_not(own_chunk))
        def _():
            for step in range(replicas):
                out_refs[core][step] = refs[replicas + step][...]

    place_rows(info_ref, out_refs, rows_ref)


def backward_kernel(upper, tops, replicas, fresh_section, info_ref, *refs):
    refs = list(refs)
    got = tops or (2 * replicas + 2 if upper else 4)
    got_refs = refs[:got]
    w_ref, prob_ref, q_ref, v_ref, kt_ref, at_ref = refs[got : got + 6]
    refs = refs[got + 6 :]
    if not upper:
        key_sum_ref, value_sum_ref, _ = refs[:3]
        refs = refs[3:]
    own_ref, other_ref, keep_ref, send_ref = refs[:4]
    refs = refs[4:]
    if upper:
        key_sum_ref, value_sum_ref = refs[:2]
        refs = refs[2:]
    grads_ref, rows_ref, scores_ref = refs
    shard_rows, model_width = own_ref.shape[1:]
    count = rows_ref.shape[0] * shard_rows
    keys = prob_ref.shape[1]
    parity = info_ref[0]
    columns = q_ref.shape[1]
    width = 2 * HEAD_DIM
    if tops:
        merge_tops(info_ref, upper, got_refs, (own_ref, other_ref), rows_ref)
    else:
        fresh = info_ref[3] == fresh_section
        merge_rows(info_ref, fresh, got_refs[:-2], got_refs[-2:], (own_ref, other_ref), rows_ref)
    rows = rows_ref[...].reshape(count, model_width)
    weights = w_ref[pl.ds(pl.multiple_of(parity * columns, 128), columns), :]
    over_width = (((1,), (1,)), ((), ()))
    upstream = lax.dot_general(
        rows, weights, over_width, preferred_element_type=jnp.float32
    ).astype(jnp.bfloat16)
    upstream_t = upstream.T
    product_t = upstream_t.astype(jnp.float32) * at_ref[...].astype(jnp.float32)
    first_query = keys - count
    masks = head_masks()

    def put(block, pair, part):
        first = block * columns + pair * width
        grads_ref[:, :, first : first + width] = part.astype(jnp.bfloat16).reshape(
            -1, shard_rows, width
        )

    for pair in range(columns // width):
        at_pair = slice(pair * width, (pair + 1) * width)
        prob_grad = jnp.dot(
            v_ref[:keys, at_pair], side_by_side(upstream_t, pair), preferred_element_type=jnp.float32
        )
        for half in range(2):
            at_half = slice(half * count, (half + 1) * count)
            first = pair * width + half * HEAD_DIM
            delta = jnp.sum(product_t[first : first + HEAD_DIM], axis=0, keepdims=True)
            scores_ref[pair, :, at_half] = (
                prob_ref[pair, :, at_half].astype(jnp.float32) * (prob_grad[:, at_half] - delta)
            ).astype(jnp.bfloat16)
        value_grad = jnp.dot(
            prob_ref[pair],
            one_above_other(upstream[:, at_pair], masks),
            preferred_element_type=jnp.float32,
        )
        if upper:
            value_sum_ref[:, at_pair] = value_grad[:first_query]
            value_grad = value_grad[first_query:]
        else:
            value_grad = value_grad + value_sum_ref[:, at_pair]
        put(2, pair, value_grad)
    for pair in range(columns // width):
        at_pair = slice(pair * width, (pair + 1) * width)
        queries = q_ref[first_query : first_query + count, at_pair]
        key_grad = jnp.dot(
            scores_ref[pair], one_above_other(queries, masks), preferred_element_type=jnp.float32
        )
        if upper:
            key_sum_ref[:, at_pair] = key_grad[:first_query]
            key_grad = key_grad[first_query:]
        else:
            key_grad = key_grad + key_sum_ref[:, at_pair]
        put(1, pair, key_grad)
        query_grad = [
            jnp.dot(
                kt_ref[pair * width + half * HEAD_DIM : pair * width + (half + 1) * HEAD_DIM, :keys],
                scores_ref[pair, :, half * count : (half + 1) * count],
                preferred_element_type=jnp.float32,
            )
            for half in range(2)
        ]
        put(0, pair, jnp.concatenate(query_grad, 0).astype(jnp.bfloat16).T)
    for step in range(replicas):
        place = place_of(info_ref, step, replicas)
        keep_ref[step] = grads_ref[place + parity]
        send_ref[step] = grads_ref[place + 1 - parity]


def norm_product(part_ref, w_ref, half):
    replicas, shard_rows, triple = part_ref.shape
    columns = triple // 3
    model_width = w_ref.shape[0]
    total = jnp.zeros((replicas * shard_rows, model_width), jnp.float32)
    for block in range(3):
        first = pl.multiple_of(block * model_width + half * columns, 128)
        total += lax.dot_general(
            part_ref[:, :, block * columns : (block + 1) * columns].reshape(-1, columns),
            w_ref[:, pl.ds(first, columns)],
            (((1,), (1,)), ((), ())),
            preferred_element_type=jnp.float32,
        )
    return total


def norm_part_kernel(info_ref, keep_ref, w_ref, after_ref, out_ref):
    out_ref[...] = norm_product(keep_ref, w_ref, info_ref[0])


def norm_kernel(
    upper, info_ref, keep_ref, got_ref, normed_ref, rms_ref, incoming_ref, w_ref, after_ref, *out_refs
):
    replicas, shard_rows, triple = got_ref.shape
    model_width = w_ref.shape[0]
    rows = replicas * shard_rows
    norm_grad = norm_product(got_ref, w_ref, 1 - info_ref[0])
    norm_grad += keep_ref[...] if upper else norm_product(keep_ref, w_ref, info_ref[0])
    chunk = 1 if upper else 0
    normed = normed_ref[chunk].reshape(rows, model_width)
    inverse_rms = rms_ref[chunk].reshape(rows, -1)[:, :1]
    inner = jnp.mean(norm_grad * normed, axis=-1, keepdims=True)
    incoming = incoming_ref[...].reshape(rows, model_width).astype(jnp.float32)
    grad_in = incoming + inverse_rms * (norm_grad - normed * inner)
    grad_in = grad_in.astype(jnp.bfloat16).reshape(replicas, shard_rows, model_width)
    if len(out_refs) == 1:
        out_refs[0][...] = grad_in
    else:
        for step, out_ref in enumerate(out_refs):
            out_ref[...] = grad_in[step]


def w_in_kernel(place, passed, info_ref, gt_ref, lower_ref, upper_ref, after_ref, out_ref):
    count = lower_ref.shape[0] * lower_ref.shape[1]
    rows = out_ref.shape[0]
    core = 1 - info_ref[0] if passed else info_ref[0]
    own = gt_ref[place, pl.ds(pl.multiple_of(core * rows, rows), rows)]
    total = jnp.zeros(out_ref.shape, jnp.float32)
    for chunk, part_ref in enumerate((lower_ref, upper_ref)):
        total += jnp.dot(
            own[:, chunk * count : (chunk + 1) * count],
            part_ref[...].reshape(count, -1),
            preferred_element_type=jnp.float32,
        )
    out_ref[...] = total.astype(out_ref.dtype)


def w_out_kernel(info_ref, at_lower_ref, at_upper_ref, lower_ref, upper_ref, after_ref, *refs):
    send_refs, own_refs = refs[:2], refs[2:]
    rows = own_refs[0].shape[0]
    for core, send_ref, own_ref in zip((1 - info_ref[0], info_ref[0]), send_refs, own_refs):
        first = pl.multiple_of((2 * info_ref[1] + core) * rows, 128)
        total = jnp.zeros(own_ref.shape, jnp.float32)
        for at_ref, chunk_ref in ((at_lower_ref, lower_ref), (at_upper_ref, upper_ref)):
            total += jnp.dot(
                at_ref[pl.ds(first, rows)],
                chunk_ref[...].reshape(-1, own_ref.shape[1]),
                preferred_element_type=jnp.float32,
            )
        own_ref[...] = total
        send_ref[...] = total.astype(jnp.bfloat16)


def sum_kernel(own_ref, got_ref, out_ref):
    out_ref[...] = (own_ref[...] + got_ref[...].astype(jnp.float32)).astype(jnp.bfloat16)


def place_in_kernel(info_ref, own_ref, got_ref, sibling_ref, out_ref):
    columns = own_ref.shape[1] // 3
    own = own_ref[...] + got_ref[...].astype(jnp.float32)
    sibling = sibling_ref[...].astype(jnp.float32)
    for part, half in ((own, info_ref[0]), (sibling, 1 - info_ref[0])):
        for block in range(3):
            first = pl.multiple_of((2 * block + half) * columns, 128)
            out_ref[:, pl.ds(first, columns)] = part[:, block * columns : (block + 1) * columns]


def place_out_kernel(info_ref, own_ref, got_ref, sibling_ref, out_ref):
    owner = info_ref[0] == info_ref[2]

    @pl.when(owner)
    def _():
        out_ref[...] = own_ref[...] + got_ref[...].astype(jnp.float32)

    @pl.when(jnp.logical_not(owner))
    def _():
        out_ref[...] = sibling_ref[...].astype(jnp.float32)


def call(kernel, outs, operands, scratch=(), flops=0, scalars=1, after=None, mebibytes=5, far=0):
    in_specs = [pl.BlockSpec(memory_space=pltpu.SMEM)] * scalars
    in_specs += [pl.BlockSpec(memory_space=pltpu.HBM)] * far
    in_specs += [pl.BlockSpec(memory_space=pltpu.VMEM)] * (len(operands) - scalars - far)
    moved = sum(item.size * item.dtype.itemsize for item in [*operands, *outs])
    if after is not None:
        operands = [*operands, after]
        in_specs.append(pl.BlockSpec(memory_space=pl.ANY))
    return pl.pallas_call(
        kernel,
        out_shape=list(outs),
        in_specs=in_specs,
        out_specs=[pl.BlockSpec(memory_space=pltpu.VMEM)] * len(outs),
        scratch_shapes=list(scratch),
        cost_estimate=pl.CostEstimate(flops=flops, bytes_accessed=moved, transcendentals=0),
        compiler_params=pltpu.CompilerParams(vmem_limit_bytes=mebibytes * 2**20),
    )(*operands)


def by_chips(acts, grad_top, w_in, w_out, offsets):
    half_type, full_type = jnp.bfloat16, jnp.float32
    shape = jax.ShapeDtypeStruct
    sections = lax.axis_size("section")
    shards = lax.axis_size("tm")
    levels = offsets.shape[1]
    half = shards // 2
    replicas = half // 2
    me = lax.axis_index("tm")
    parity = lax.rem(me, 2)
    side = lax.div(me, half)
    micro_count, shard_rows, model_width = acts.shape[1:]
    columns = model_width // 2
    heads = columns // HEAD_DIM
    seq = shards * shard_rows
    count = seq // 2
    w_qkv = w_in[0]
    w_rows = w_out[0]
    info = jnp.stack([parity, lax.div(lax.rem(me, half), 2), side, lax.axis_index("section")])
    info = jnp.concatenate([info.astype(jnp.int32), offsets[0]])
    across = [(source, (source + half) % shards) for source in range(shards)]
    cores = [(source, source + 1 - 2 * (source % 2)) for source in range(shards)]
    homeward = [pair for pair in across if pair[0] // half != pair[0] % 2]
    around = [
        [
            (source, source // half * half + (source % half + 2 * step) % half)
            for source in range(shards)
        ]
        for step in range(replicas)
    ]

    packed = shape((shard_rows, model_width + 128), half_type)
    top_shape = shape((shard_rows, model_width), half_type)
    own_acts, other_acts, own_top, other_top = call(
        functools.partial(pack_kernel, levels),
        [packed, packed, top_shape, top_shape],
        [info, acts[0], grad_top],
        scratch=[pltpu.SemaphoreType.DMA((4,))],
        far=2,
    )
    swapped = lax.ppermute(other_acts, "tm", across)
    (touched,) = call(
        touch_kernel, [shape((16, 128), half_type)], [w_qkv], scalars=0, after=own_acts
    )
    swapped, touched = lax.optimization_barrier((swapped, touched))
    pieces = [own_acts]
    pieces += [lax.ppermute(own_acts, "tm", around[step]) for step in range(1, replicas)]
    pieces += [swapped]
    pieces += [lax.ppermute(swapped, "tm", around[step]) for step in range(1, replicas)]
    other_top = lax.ppermute(other_top, "tm", across)
    tops = [own_top]
    tops += [lax.ppermute(own_top, "tm", around[step]) for step in range(1, replicas)]
    pieces[-1], other_top, tops = lax.optimization_barrier((pieces[-1], other_top, tops))
    pieces += [lax.ppermute(piece, "tm", cores) for piece in pieces]
    tops += [other_top]
    tops += [lax.ppermute(other_top, "tm", around[step]) for step in range(1, replicas)]

    rows_shape = shape((seq, columns), half_type)
    normed, rms, norm, flag_rows, queries, keys, values, keys_t = call(
        functools.partial(project_kernel, replicas),
        [
            shape((2, replicas, shard_rows, model_width), full_type),
            shape((2, replicas, shard_rows, 128), full_type),
            shape((seq, model_width), half_type),
            shape((128, seq), full_type),
            rows_shape,
            rows_shape,
            rows_shape,
            shape((columns, seq), half_type),
        ],
        [info, *pieces, w_qkv],
        scratch=[pltpu.VMEM((shards, *packed.shape), half_type)],
        flops=6 * seq * model_width * columns,
        after=touched,
    )
    tops, _ = lax.optimization_barrier((tuple(tops), keys_t))
    tops = [*tops, *[lax.ppermute(piece, "tm", cores) for piece in tops]]
    pairs = heads // 2
    upper_prob, upper_at = call(
        functools.partial(upper_forward_kernel, levels, shard_rows),
        [
            shape((pairs, seq, 2 * count), half_type),
            shape((columns, count), half_type),
        ],
        [flag_rows, queries, keys, values],
        scalars=0,
        flops=4 * columns * seq * count,
    )
    own_rows = model_width // shards
    block_rows = 2 * own_rows
    probs, attended = {True: upper_prob}, {True: upper_at}
    got, kept = {}, {}
    piece_shape = shape((replicas, shard_rows, model_width), half_type)
    grads_shape = shape((replicas, shard_rows, 3 * columns), half_type)
    sum_shape = shape((count, columns), full_type)
    full_grads = shape((half, shard_rows, 3 * columns), half_type)
    full_rows = shape((half, shard_rows, model_width), half_type)
    term_flops = 2 * own_rows * seq * 3 * columns
    term_shape = (own_rows, 3 * columns)
    rows_scratch = pltpu.VMEM(full_rows.shape, half_type)
    grads_scratch = pltpu.VMEM(full_grads.shape, half_type)
    result, full, ordered = {}, {}, {}
    grad_in = keys_t
    for turn in range(sections):
        last = turn + 1 == sections
        fresh_section = sections - 1 - turn
        sums, parts, crossed = [], {}, {}
        for upper in (True, False):
            rows_in = tops
            if turn:
                before = result[False] if upper else keep
                pieces = []
                for piece in got[upper]:
                    piece, before = lax.optimization_barrier((piece, before))
                    pieces.append(piece)
                got[upper] = pieces
                if upper:
                    result[False] = before
                else:
                    keep = before
                others = [lax.ppermute(piece, "tm", cores) for piece in got[upper]]
                rows_in = [*got[upper], *others, *kept[upper]]
            after = None if upper else parts[True]
            outs = [piece_shape, piece_shape, grads_shape, grads_shape]
            outs += [sum_shape, sum_shape] if upper else []
            scratch = []
            if last:
                outs += [full_grads]
            else:
                scratch += [grads_scratch]
            if last:
                outs += [full_rows]
            else:
                scratch += [rows_scratch]
            part_keys = seq if upper else count
            scratch += [pltpu.VMEM((pairs, part_keys, 2 * count), half_type)]
            answer = call(
                functools.partial(
                    backward_kernel, upper, 0 if turn else len(tops), replicas, fresh_section
                ),
                outs,
                [info, *rows_in, w_rows, probs[upper], queries, values, keys_t]
                + [attended[upper], *sums],
                scratch=scratch,
                flops=2 * count * columns * (2 * model_width + 4 * part_keys),
                after=after,
            )
            kept[upper] = tuple(answer[:2])
            keep, send = answer[2:4]
            parts[upper] = keep
            if upper:
                sums = answer[4:6]
                (parts[True],) = call(
                    norm_part_kernel,
                    [shape((replicas * shard_rows, model_width), full_type)],
                    [info, keep, w_qkv],
                    flops=3 * replicas * shard_rows * model_width * model_width,
                    after=keep,
                )
                if turn == 0:
                    lower_prob, lower_at, norm_t = call(
                        functools.partial(lower_forward_kernel, levels, shard_rows),
                        [
                            shape((pairs, count, 2 * count), half_type),
                            shape((columns, count), half_type),
                            shape((2, block_rows, seq), half_type),
                        ],
                        [info, norm, flag_rows, queries, keys, values],
                        flops=4 * columns * count * count,
                        after=parts[True],
                    )
                    probs[False], attended[False] = lower_prob, lower_at
            if last:
                full[upper], ordered[upper] = answer[-2:]
            crossed[upper] = lax.ppermute(send, "tm", cores)
        if last:
            terms = [info, norm_t, full[False], full[True]]
            (in_pass,) = call(
                functools.partial(w_in_kernel, 0, True),
                [shape(term_shape, half_type)],
                terms,
                flops=term_flops,
                after=keep,
            )
            (in_keep,) = call(
                functools.partial(w_in_kernel, 0, False),
                [shape(term_shape, half_type)],
                terms,
                flops=term_flops,
                after=in_pass,
            )
            grad_in = in_keep
        for upper in (True, False):
            grad_pieces = call(
                functools.partial(norm_kernel, upper),
                [top_shape] * replicas if upper else [piece_shape],
                [info, parts[upper], crossed[upper], normed, rms, kept[upper][0], w_qkv],
                flops=6 * replicas * shard_rows * model_width * model_width,
                after=grad_in,
            )
            result[upper] = grad_pieces
            grad_in = grad_pieces[-1]
            if not last:
                hop = [(sections - 1 - turn, sections - 2 - turn)]
                got[upper] = [lax.ppermute(piece, "section", hop) for piece in grad_pieces]

    in_got_pass = lax.ppermute(in_pass, "tm", across)
    in_got_keep = lax.ppermute(in_keep, "tm", across)

    upper_own, lower_own = result[True][0], result[False][0][0]
    mine = jnp.where(side == 1, upper_own, lower_own)
    partner = jnp.where(side == 1, lower_own, upper_own)
    in_own_pass, in_own_keep = [
        call(
            functools.partial(w_in_kernel, 1, passed),
            [shape(term_shape, full_type)],
            terms,
            flops=term_flops,
            after=partner,
        )[0]
        for passed in (True, False)
    ]
    out_pass, out_keep, own_pass, own_keep = call(
        w_out_kernel,
        [shape((own_rows, model_width), half_type)] * 2
        + [shape((own_rows, model_width), full_type)] * 2,
        [info, lower_at, upper_at, ordered[False], ordered[True]],
        flops=2 * block_rows * seq * model_width,
        after=in_keep,
    )
    got_pass = lax.ppermute(out_pass, "tm", homeward)
    got_keep = lax.ppermute(out_keep, "tm", homeward)
    partner = lax.ppermute(partner, "tm", across)

    (to_pass,) = call(
        sum_kernel, [shape((own_rows, model_width), half_type)], [own_pass, got_pass], scalars=0
    )
    to_sibling = [pair for pair in cores if pair[0] // half == pair[0] % 2]
    (d_w_out,) = call(
        place_out_kernel,
        [shape((own_rows, model_width), full_type)],
        [info, own_keep, got_keep, lax.ppermute(to_pass, "tm", to_sibling)],
    )
    (to_pass,) = call(
        sum_kernel, [shape(term_shape, half_type)], [in_own_pass, in_got_pass], scalars=0
    )
    (d_w_in,) = call(
        place_in_kernel,
        [shape((own_rows, 3 * model_width), full_type)],
        [info, in_own_keep, in_got_keep, lax.ppermute(to_pass, "tm", cores)],
    )
    d_acts = jnp.where(side == 0, jnp.stack([mine, partner]), jnp.stack([partner, mine]))
    return (d_acts[None], d_w_in[None], d_w_out[None])


def layer_gradients(acts, grad_top, w_in, w_out, offsets):
    shards = lax.axis_size("tm")
    micro_count, shard_rows, model_width = acts.shape[1:]
    heads = model_width // HEAD_DIM
    prob_bytes = 2 * heads * (shards * shard_rows) ** 2
    fits = prob_bytes <= 2**24 and model_width % (128 * shards) == 0 and shard_rows % 16 == 0
    if micro_count == 2 and shards % 4 == 0 and heads % 4 == 0 and fits:
        return by_chips(acts, grad_top, w_in, w_out, offsets)
    return per_device(acts, grad_top, w_in, w_out, offsets)


def solution(mesh):
    placed = (
        P("section", None, "tm", None),
        P(None, "tm", None),
        P("section", None, None),
        P("section", None, None),
        P("tm", None),
    )
    return jax.shard_map(
        layer_gradients,
        mesh=mesh,
        in_specs=placed,
        out_specs=(
            P("section", None, "tm", None),
            P("section", "tm", None),
            P("section", "tm", None),
        ),
        check_vma=False,
    )
```

```python
import functools
import jax
import jax.numpy as jnp
from jax import lax
from jax.experimental import pallas as pl
from jax.experimental.pallas import tpu as pltpu
from jax.sharding import PartitionSpec as P

HEAD_DIM = 64


epsilon = 1e-06
negative_fill = -1e30


def shifted(value, axis, steps):
    count = lax.axis_size(axis)
    initial, last = (max(0, -steps), min(count, count - steps))
    return lax.ppermute(value, axis, [(source, source + steps) for source in range(initial, last)])


def normalize(inputs):
    values = inputs.astype(jnp.float32)
    inverse_rms = lax.rsqrt(jnp.mean(values * values, axis=-1, keepdims=True) + epsilon)
    return (values * inverse_rms, inverse_rms)


def key_bias(level_flags, shard_rows):
    position = jnp.arange(shard_rows)
    own_part = position[None, :] <= position[:, None]
    far_part = jnp.repeat(level_flags != 0, shard_rows)
    far_part = jnp.broadcast_to(far_part[None, :], (shard_rows, far_part.shape[0]))
    return jnp.concatenate([own_part, far_part], 1)


def split_heads(row_block):
    return row_block.reshape(row_block.shape[0], -1, HEAD_DIM)


def softmax_keys(queries, key_heads, allowed):
    scores = jnp.einsum(
        "ihd,jhd->hij", queries, key_heads, preferred_element_type=jnp.float32
    ) * HEAD_DIM ** (-0.5)
    scores = jnp.where(allowed[None], scores, negative_fill)
    highest = jnp.max(scores, axis=-1, keepdims=True)
    shifted_exp = jnp.where(allowed[None], jnp.exp(scores - highest), 0.0)
    return shifted_exp / jnp.sum(shifted_exp, axis=-1, keepdims=True)


def attend(query_rows, key_rows, allowed):
    model_width = query_rows.shape[1]
    probability = softmax_keys(
        split_heads(query_rows), split_heads(key_rows[:, :model_width]), allowed
    )
    attended = jnp.einsum(
        "hij,jhd->ihd",
        probability.astype(jnp.bfloat16),
        split_heads(key_rows[:, model_width:]),
        preferred_element_type=jnp.float32,
    )
    return attended.reshape(query_rows.shape).astype(jnp.bfloat16)


def attend_back(query_rows, key_rows, allowed, incoming, attended, w_proj):
    model_width = query_rows.shape[1]
    queries = split_heads(query_rows)
    key_heads = split_heads(key_rows[:, :model_width])
    value_heads = split_heads(key_rows[:, model_width:])
    probability = softmax_keys(queries, key_heads, allowed)
    rounded = probability.astype(jnp.bfloat16)
    upstream = lax.dot_general(
        incoming, w_proj, (((1,), (1,)), ((), ())), preferred_element_type=jnp.float32
    ).astype(jnp.bfloat16)
    up_heads = split_heads(upstream)
    delta = jnp.einsum(
        "ihd,ihd->hi", up_heads.astype(jnp.float32), split_heads(attended).astype(jnp.float32)
    )[..., None]
    prob_grad = jnp.einsum(
        "ihd,jhd->hij", up_heads, value_heads, preferred_element_type=jnp.float32
    )
    score_grad = (probability * (prob_grad - delta)).astype(jnp.bfloat16)
    scale_factor = HEAD_DIM ** (-0.5)
    query_grad = (
        jnp.einsum("hij,jhd->ihd", score_grad, key_heads, preferred_element_type=jnp.float32)
        * scale_factor
    )
    key_grad = (
        jnp.einsum("hij,ihd->jhd", score_grad, queries, preferred_element_type=jnp.float32)
        * scale_factor
    )
    value_grad = jnp.einsum("hij,ihd->jhd", rounded, up_heads, preferred_element_type=jnp.float32)
    return (
        query_grad.reshape(-1, model_width),
        key_grad.reshape(-1, model_width),
        value_grad.reshape(-1, model_width),
    )


def per_device(acts, grad_top, w_in, w_out, offsets):
    sections = lax.axis_size("section")
    shards = lax.axis_size("tm")
    levels = shards.bit_length() - 1
    section_index = lax.axis_index("section")
    micro_count = acts.shape[1]
    shard_rows = acts.shape[2]
    model_width = acts.shape[3]
    w_qkv = w_in[0]
    w_proj = w_out[0]
    level_flags = offsets[0]
    normed, inverse_rms = normalize(acts[0])
    rounded_norm = normed.astype(jnp.bfloat16)
    qkv = jnp.dot(rounded_norm.reshape(-1, model_width), w_qkv, preferred_element_type=jnp.float32)
    qkv = qkv.astype(jnp.bfloat16).reshape(micro_count, shard_rows, 3 * model_width)
    pairs = qkv[..., model_width:]
    far_list = [shifted(pairs, "tm", 2**level) for level in range(levels)]
    key_rows = jnp.concatenate([pairs] + far_list, 1)
    allowed = key_bias(level_flags, shard_rows)
    attended = jnp.stack(
        [
            attend(qkv[index, :, :model_width], key_rows[index], allowed)
            for index in range(micro_count)
        ],
        0,
    )

    def attention_part(incoming, slot):
        query_rows = lax.dynamic_index_in_dim(qkv, slot, 0, False)[:, :model_width]
        slot_keys = lax.dynamic_index_in_dim(key_rows, slot, 0, False)
        slot_attended = lax.dynamic_index_in_dim(attended, slot, 0, False)
        query_grad, key_grad, value_grad = attend_back(
            query_rows, slot_keys, allowed, incoming, slot_attended, w_proj
        )
        owner_sum = jnp.concatenate([key_grad[:shard_rows], value_grad[:shard_rows]], 1)
        far_part = jnp.concatenate([key_grad[shard_rows:], value_grad[shard_rows:]], 1)
        far_part = far_part.astype(jnp.bfloat16).reshape(levels, shard_rows, 2 * model_width)
        return (query_grad, owner_sum, far_part)

    def empty_attention(incoming, slot):
        return (
            jnp.zeros((shard_rows, model_width), jnp.float32),
            jnp.zeros((shard_rows, 2 * model_width), jnp.float32),
            jnp.zeros((levels, shard_rows, 2 * model_width), jnp.bfloat16),
        )

    def norm_part(qkv_grad, incoming, slot):
        norm_grad = lax.dot_general(
            qkv_grad, w_qkv, (((1,), (1,)), ((), ())), preferred_element_type=jnp.float32
        )
        slot_normed = lax.dynamic_index_in_dim(normed, slot, 0, False)
        slot_rms = lax.dynamic_index_in_dim(inverse_rms, slot, 0, False)
        inner = jnp.mean(norm_grad * slot_normed, axis=-1, keepdims=True)
        return (incoming.astype(jnp.float32) + slot_rms * (norm_grad - slot_normed * inner)).astype(
            jnp.bfloat16
        )

    def empty_norm(qkv_grad, incoming, slot):
        return jnp.zeros((shard_rows, model_width), jnp.bfloat16)

    def step(turn, carry):
        received, grad_store, qkv_store, incoming_store = carry
        slot_raw = turn - (sections - 1 - section_index)
        active = (slot_raw >= 0) & (slot_raw < micro_count)
        slot = jnp.clip(slot_raw, 0, micro_count - 1)
        incoming = jnp.where(
            section_index == sections - 1,
            lax.dynamic_index_in_dim(grad_top, slot, 0, False),
            received,
        )
        query_grad, owner_sum, far_part = lax.cond(
            active, attention_part, empty_attention, incoming, slot
        )
        for level in range(levels):
            owner_sum = owner_sum + shifted(far_part[level], "tm", -(2**level)).astype(jnp.float32)
        qkv_grad = jnp.concatenate([query_grad, owner_sum], 1).astype(jnp.bfloat16)
        grad_in = lax.cond(active, norm_part, empty_norm, qkv_grad, incoming, slot)
        sent_down = shifted(grad_in, "section", -1)
        grad_store = jnp.where(
            active, lax.dynamic_update_index_in_dim(grad_store, grad_in, slot, 0), grad_store
        )
        qkv_store = jnp.where(
            active, lax.dynamic_update_index_in_dim(qkv_store, qkv_grad, slot, 0), qkv_store
        )
        incoming_store = jnp.where(
            active,
            lax.dynamic_update_index_in_dim(incoming_store, incoming, slot, 0),
            incoming_store,
        )
        return (sent_down, grad_store, qkv_store, incoming_store)

    initial = (
        jnp.zeros((shard_rows, model_width), jnp.bfloat16),
        jnp.zeros((micro_count, shard_rows, model_width), jnp.bfloat16),
        jnp.zeros((micro_count, shard_rows, 3 * model_width), jnp.bfloat16),
        jnp.zeros((micro_count, shard_rows, model_width), jnp.bfloat16),
    )
    received, grad_store, qkv_store, incoming_store = lax.fori_loop(
        0, sections + micro_count - 1, step, initial
    )
    flat_norm = rounded_norm.reshape(-1, model_width)
    flat_attended = attended.reshape(-1, model_width)
    flat_qkv = qkv_store.reshape(-1, 3 * model_width)
    flat_incoming = incoming_store.reshape(-1, model_width)
    contract = (((0,), (0,)), ((), ()))
    first = lax.dot_general(flat_norm, flat_qkv, contract, preferred_element_type=jnp.float32)
    second = lax.dot_general(
        flat_attended, flat_incoming, contract, preferred_element_type=jnp.float32
    )
    summed = lax.psum_scatter(
        jnp.concatenate([first, second], 1).astype(jnp.bfloat16),
        "tm",
        scatter_dimension=0,
        tiled=True,
    ).astype(jnp.float32)
    return (
        grad_store[None],
        summed[None, :, : 3 * model_width],
        summed[None, :, 3 * model_width :],
    )


def side_by_side(transposed, pair):
    width = 2 * HEAD_DIM
    rows = transposed[pair * width : (pair + 1) * width]
    empty = jnp.zeros((HEAD_DIM, rows.shape[1]), rows.dtype)
    return jnp.concatenate(
        [
            jnp.concatenate([rows[:HEAD_DIM], empty], 0),
            jnp.concatenate([empty, rows[HEAD_DIM:]], 0),
        ],
        1,
    )


def one_above_other(rows, masks):
    return jnp.concatenate([rows * masks[0], rows * masks[1]], 0)


def head_masks():
    lane = lax.broadcasted_iota(jnp.int32, (1, 2 * HEAD_DIM), 1)
    return [
        jnp.where(lane < HEAD_DIM, 1.0, 0.0).astype(jnp.bfloat16),
        jnp.where(lane < HEAD_DIM, 0.0, 1.0).astype(jnp.bfloat16),
    ]


def key_bias_rows(flag_rows, levels, shard_rows, keys, first_query, count):
    key_at = lax.broadcasted_iota(jnp.int32, (keys, count), 0)
    query_at = lax.broadcasted_iota(jnp.int32, (keys, count), 1) + first_query
    gap = lax.div(query_at, shard_rows) - lax.div(key_at, shard_rows)
    allowed = (gap == 0) & (key_at <= query_at)
    for level in range(levels):
        allowed = allowed | ((gap == 2**level) & (flag_rows[level : level + 1] != 0))
    return jnp.where(allowed, 0.0, negative_fill)


def softmax_pass(queries, keys, values, bias, prob_ref, at_ref):
    queries_t = queries.T
    values_t = values.T
    width = 2 * HEAD_DIM
    count = queries.shape[0]
    for pair in range(queries.shape[1] // width):
        at_pair = slice(pair * width, (pair + 1) * width)
        scores = jnp.dot(
            keys[:, at_pair], side_by_side(queries_t, pair), preferred_element_type=jnp.float32
        )
        for half in range(2):
            at_half = slice(half * count, (half + 1) * count)
            biased = scores[:, at_half] + bias
            shifted_exp = jnp.exp(biased - jnp.max(biased, axis=0, keepdims=True))
            probability = shifted_exp * (1.0 / jnp.sum(shifted_exp, axis=0, keepdims=True))
            prob_ref[pair, :, at_half] = probability.astype(jnp.bfloat16)
    for head in range(queries.shape[1] // HEAD_DIM):
        at = slice(head * HEAD_DIM, (head + 1) * HEAD_DIM)
        at_half = slice(head % 2 * count, (head % 2 + 1) * count)
        at_ref[at] = jnp.dot(
            values_t[at], prob_ref[head // 2, :, at_half], preferred_element_type=jnp.float32
        ).astype(jnp.bfloat16)


def pack_kernel(
    levels, info_ref, acts_ref, top_ref, own_ref, other_ref, own_top_ref, other_top_ref, sems
):
    model_width = acts_ref.shape[2]
    shard_rows = own_ref.shape[0]
    side = info_ref[4]
    copies = [
        pltpu.make_async_copy(acts_ref.at[side], own_ref.at[:, :model_width], sems.at[0]),
        pltpu.make_async_copy(acts_ref.at[1 - side], other_ref.at[:, :model_width], sems.at[1]),
        pltpu.make_async_copy(top_ref.at[side], own_top_ref, sems.at[2]),
        pltpu.make_async_copy(top_ref.at[1 - side], other_top_ref, sems.at[3]),
    ]
    for copy in copies:
        copy.start()
    lane = lax.broadcasted_iota(jnp.int32, (shard_rows, own_ref.shape[1] - model_width), 1)
    flags = jnp.zeros(lane.shape, jnp.float32)
    for level in range(levels):
        seen = jnp.where(info_ref[5 + level] != 0, 1.0, 0.0)
        flags = jnp.where(lane == level, seen, flags)
    own_ref[:, model_width:] = flags.astype(jnp.bfloat16)
    other_ref[:, model_width:] = flags.astype(jnp.bfloat16)
    for copy in copies:
        copy.wait()


def touch_kernel(w_ref, after_ref, out_ref):
    out_ref[...] = w_ref[: out_ref.shape[0], : out_ref.shape[1]]


def project_kernel(replicas, info_ref, *refs):
    pieces = refs[: 4 * replicas]
    w_ref, _, normed_ref, rms_ref, norm_ref, flag_ref, q_ref, k_ref, v_ref, kt_ref, packed_ref = refs[
        4 * replicas :
    ]
    shards, shard_rows = packed_ref.shape[:2]
    model_width = w_ref.shape[0]
    seq = shards * shard_rows
    columns = q_ref.shape[1]
    at_piece = 0
    for core in (info_ref[0], 1 - info_ref[0]):
        for side in (info_ref[2], 1 - info_ref[2]):
            for step in range(replicas):
                shard = side * (shards // 2) + place_of(info_ref, step, replicas) + core
                packed_ref[shard] = pieces[at_piece][...]
                at_piece += 1
    for chunk in range(2):
        for step in range(replicas):
            shard = chunk * (shards // 2) + place_of(info_ref, step, replicas) + info_ref[0]
            normed, inverse_rms = normalize(packed_ref[shard][:, :model_width])
            normed_ref[chunk, step] = normed
            rms_ref[chunk, step] = jnp.broadcast_to(inverse_rms, rms_ref.shape[2:])
    normed, _ = normalize(packed_ref[:, :, :model_width].reshape(seq, model_width))
    rounded = normed.astype(jnp.bfloat16)
    norm_ref[...] = rounded
    flag_ref[...] = packed_ref[:, :, model_width:].reshape(seq, -1).astype(jnp.float32).T
    scale_factor = HEAD_DIM ** (-0.5)
    for block, out_ref in enumerate((q_ref, k_ref, v_ref)):
        first = pl.multiple_of(block * model_width + info_ref[0] * columns, 128)
        product = jnp.dot(
            rounded, w_ref[:, pl.ds(first, columns)], preferred_element_type=jnp.float32
        ).astype(jnp.bfloat16)
        out_ref[...] = product * scale_factor if block == 0 else product
    kt_ref[...] = (k_ref[...] * scale_factor).T


def upper_forward_kernel(
    levels, shard_rows, flag_ref, q_ref, k_ref, v_ref, prob_ref, at_ref
):
    seq = q_ref.shape[0]
    count = seq // 2
    bias = key_bias_rows(flag_ref[:, count:], levels, shard_rows, seq, count, count)
    softmax_pass(q_ref[count:], k_ref[...], v_ref[...], bias, prob_ref, at_ref)


def lower_forward_kernel(
    levels,
    shard_rows,
    info_ref,
    norm_ref,
    flag_ref,
    q_ref,
    k_ref,
    v_ref,
    after_ref,
    prob_ref,
    at_ref,
    gt_ref,
):
    seq = norm_ref.shape[0]
    count = seq // 2
    bias = key_bias_rows(flag_ref[:, :count], levels, shard_rows, count, 0, count)
    softmax_pass(q_ref[:count], k_ref[:count], v_ref[:count], bias, prob_ref, at_ref)
    rows = gt_ref.shape[0] // 4
    parity, x, y = info_ref[0], info_ref[1], info_ref[2]
    half = norm_ref.shape[1] // rows // 2
    for place, block in enumerate(
        (
            half * y + 2 * x + 1 - parity,
            half * y + 2 * x + parity,
            half * y + 2 * (1 - x) + 1 - parity,
            half * (1 - y) + 2 * x + parity,
        )
    ):
        first = pl.multiple_of(block * rows, 128)
        gt_ref[place * rows : (place + 1) * rows] = norm_ref[:, pl.ds(first, rows)].T


def place_of(info_ref, step, replicas):
    return 2 * lax.rem(info_ref[1] - step + replicas, replicas)


def merge_rows(info_ref, fresh, got_refs, kept_refs, out_refs, rows_ref):
    @pl.when(fresh)
    def _():
        for core, out_ref in enumerate(out_refs):
            refs = got_refs[core * len(got_refs) // 2 : (core + 1) * len(got_refs) // 2]
            if len(refs) == 1:
                out_ref[...] = refs[0][...]
            else:
                for step, got_ref in enumerate(refs):
                    out_ref[step] = got_ref[...]

    @pl.when(jnp.logical_not(fresh))
    def _():
        for out_ref, kept_ref in zip(out_refs, kept_refs):
            out_ref[...] = kept_ref[...]

    place_rows(info_ref, out_refs, rows_ref)


def place_rows(info_ref, out_refs, rows_ref):
    replicas = out_refs[0].shape[0]
    for step in range(replicas):
        place = place_of(info_ref, step, replicas)
        rows_ref[place + info_ref[0]] = out_refs[0][step]
        rows_ref[place + 1 - info_ref[0]] = out_refs[1][step]


def merge_tops(info_ref, upper, piece_refs, out_refs, rows_ref):
    replicas = out_refs[0].shape[0]
    own_chunk = info_ref[2] == (1 if upper else 0)
    for core in range(2):
        refs = piece_refs[2 * replicas * core : 2 * replicas * (core + 1)]

        @pl.when(own_chunk)
        def _():
            for step in range(replicas):
                out_refs[core][step] = refs[step][...]

        @pl.when(jnp.logical_not(own_chunk))
        def _():
            for step in range(replicas):
                out_refs[core][step] = refs[replicas + step][...]

    place_rows(info_ref, out_refs, rows_ref)


def backward_kernel(upper, tops, replicas, fresh_section, info_ref, *refs):
    refs = list(refs)
    got = tops or (2 * replicas + 2 if upper else 4)
    got_refs = refs[:got]
    w_ref, prob_ref, q_ref, v_ref, kt_ref, at_ref = refs[got : got + 6]
    refs = refs[got + 6 :]
    if not upper:
        key_sum_ref, value_sum_ref, _ = refs[:3]
        refs = refs[3:]
    own_ref, other_ref, keep_ref, send_ref = refs[:4]
    refs = refs[4:]
    if upper:
        key_sum_ref, value_sum_ref = refs[:2]
        refs = refs[2:]
    grads_ref, rows_ref, scores_ref = refs
    shard_rows, model_width = own_ref.shape[1:]
    count = rows_ref.shape[0] * shard_rows
    keys = prob_ref.shape[1]
    parity = info_ref[0]
    columns = q_ref.shape[1]
    width = 2 * HEAD_DIM
    if tops:
        merge_tops(info_ref, upper, got_refs, (own_ref, other_ref), rows_ref)
    else:
        fresh = info_ref[3] == fresh_section
        merge_rows(info_ref, fresh, got_refs[:-2], got_refs[-2:], (own_ref, other_ref), rows_ref)
    rows = rows_ref[...].reshape(count, model_width)
    weights = w_ref[pl.ds(pl.multiple_of(parity * columns, 128), columns), :]
    over_width = (((1,), (1,)), ((), ()))
    upstream = lax.dot_general(
        rows, weights, over_width, preferred_element_type=jnp.float32
    ).astype(jnp.bfloat16)
    upstream_t = upstream.T
    product_t = upstream_t.astype(jnp.float32) * at_ref[...].astype(jnp.float32)
    first_query = keys - count
    masks = head_masks()

    def put(block, pair, part):
        first = block * columns + pair * width
        grads_ref[:, :, first : first + width] = part.astype(jnp.bfloat16).reshape(
            -1, shard_rows, width
        )

    for pair in range(columns // width):
        at_pair = slice(pair * width, (pair + 1) * width)
        prob_grad = jnp.dot(
            v_ref[:keys, at_pair], side_by_side(upstream_t, pair), preferred_element_type=jnp.float32
        )
        for half in range(2):
            at_half = slice(half * count, (half + 1) * count)
            first = pair * width + half * HEAD_DIM
            delta = jnp.sum(product_t[first : first + HEAD_DIM], axis=0, keepdims=True)
            scores_ref[pair, :, at_half] = (
                prob_ref[pair, :, at_half].astype(jnp.float32) * (prob_grad[:, at_half] - delta)
            ).astype(jnp.bfloat16)
        value_grad = jnp.dot(
            prob_ref[pair],
            one_above_other(upstream[:, at_pair], masks),
            preferred_element_type=jnp.float32,
        )
        if upper:
            value_sum_ref[:, at_pair] = value_grad[:first_query]
            value_grad = value_grad[first_query:]
        else:
            value_grad = value_grad + value_sum_ref[:, at_pair]
        put(2, pair, value_grad)
    for pair in range(columns // width):
        at_pair = slice(pair * width, (pair + 1) * width)
        queries = q_ref[first_query : first_query + count, at_pair]
        key_grad = jnp.dot(
            scores_ref[pair], one_above_other(queries, masks), preferred_element_type=jnp.float32
        )
        if upper:
            key_sum_ref[:, at_pair] = key_grad[:first_query]
            key_grad = key_grad[first_query:]
        else:
            key_grad = key_grad + key_sum_ref[:, at_pair]
        put(1, pair, key_grad)
        query_grad = [
            jnp.dot(
                kt_ref[pair * width + half * HEAD_DIM : pair * width + (half + 1) * HEAD_DIM, :keys],
                scores_ref[pair, :, half * count : (half + 1) * count],
                preferred_element_type=jnp.float32,
            )
            for half in range(2)
        ]
        put(0, pair, jnp.concatenate(query_grad, 0).astype(jnp.bfloat16).T)
    for step in range(replicas):
        place = place_of(info_ref, step, replicas)
        keep_ref[step] = grads_ref[place + parity]
        send_ref[step] = grads_ref[place + 1 - parity]


def norm_product(part_ref, w_ref, half):
    replicas, shard_rows, triple = part_ref.shape
    columns = triple // 3
    model_width = w_ref.shape[0]
    total = jnp.zeros((replicas * shard_rows, model_width), jnp.float32)
    for block in range(3):
        first = pl.multiple_of(block * model_width + half * columns, 128)
        total += lax.dot_general(
            part_ref[:, :, block * columns : (block + 1) * columns].reshape(-1, columns),
            w_ref[:, pl.ds(first, columns)],
            (((1,), (1,)), ((), ())),
            preferred_element_type=jnp.float32,
        )
    return total


def norm_part_kernel(info_ref, keep_ref, w_ref, after_ref, out_ref):
    out_ref[...] = norm_product(keep_ref, w_ref, info_ref[0])


def norm_kernel(
    upper, info_ref, keep_ref, got_ref, normed_ref, rms_ref, incoming_ref, w_ref, after_ref, *out_refs
):
    replicas, shard_rows, triple = got_ref.shape
    model_width = w_ref.shape[0]
    rows = replicas * shard_rows
    norm_grad = norm_product(got_ref, w_ref, 1 - info_ref[0])
    norm_grad += keep_ref[...] if upper else norm_product(keep_ref, w_ref, info_ref[0])
    chunk = 1 if upper else 0
    normed = normed_ref[chunk].reshape(rows, model_width)
    inverse_rms = rms_ref[chunk].reshape(rows, -1)[:, :1]
    inner = jnp.mean(norm_grad * normed, axis=-1, keepdims=True)
    incoming = incoming_ref[...].reshape(rows, model_width).astype(jnp.float32)
    grad_in = incoming + inverse_rms * (norm_grad - normed * inner)
    grad_in = grad_in.astype(jnp.bfloat16).reshape(replicas, shard_rows, model_width)
    if len(out_refs) == 1:
        out_refs[0][...] = grad_in
    else:
        for step, out_ref in enumerate(out_refs):
            out_ref[...] = grad_in[step]


def term_kernel(info_ref, gt_ref, *refs):
    grad_refs, at_refs, row_refs = refs[:2], refs[2:4], refs[4:6]
    own_pass_ref, own_keep_ref, send_pass_ref, send_keep_ref = refs[6:10]
    out_pass_ref, out_keep_ref, out_send_ref = refs[10:]
    rows = own_pass_ref.shape[0]
    width = out_send_ref.shape[1]
    count = row_refs[0].shape[0] * row_refs[0].shape[1]
    parity, x, y = info_ref[0], info_ref[1], info_ref[2]
    for half, (pass_ref, keep_ref) in reversed(
        list(enumerate(((own_pass_ref, own_keep_ref), (send_pass_ref, send_keep_ref))))
    ):
        total = sum(
            jnp.dot(
                gt_ref[2 * half * rows : 2 * (half + 1) * rows, chunk * count : (chunk + 1) * count],
                part_ref[...].reshape(count, -1),
                preferred_element_type=jnp.float32,
            )
            for chunk, part_ref in enumerate(grad_refs)
        )
        pass_ref[...] = total[:rows].astype(pass_ref.dtype)
        keep_ref[...] = total[rows:].astype(keep_ref.dtype)
    sent = jnp.where(parity == y, 2 * (1 - x) + 1 - parity, 2 * x + parity)
    blocks = (sent, 2 * x + 1 - parity, 2 * x + parity)
    total = jnp.zeros((3 * rows, width), jnp.float32)
    for at_ref, part_ref in zip(at_refs, row_refs):
        picked = [at_ref[pl.ds(pl.multiple_of(block * rows, 128), rows)] for block in blocks]
        total += jnp.dot(
            jnp.concatenate(picked, 0),
            part_ref[...].reshape(count, width),
            preferred_element_type=jnp.float32,
        )
    out_send_ref[...] = total[:rows].astype(jnp.bfloat16)
    out_pass_ref[...] = total[rows : 2 * rows]
    out_keep_ref[...] = total[2 * rows :]


def sum_kernel(own_ref, got_ref, out_own_ref, out_got_ref, after_ref, sum_ref):
    columns = own_ref.shape[1]
    sum_ref[:, :columns] = (own_ref[...] + got_ref[...].astype(jnp.float32)).astype(jnp.bfloat16)
    sum_ref[:, columns:] = (out_own_ref[...] + out_got_ref[...].astype(jnp.float32)).astype(
        jnp.bfloat16
    )


def place_kernel(
    info_ref, own_ref, got_ref, out_own_ref, out_got_ref, sibling_ref, d_in_ref, d_out_ref
):
    columns = own_ref.shape[1] // 3
    own = own_ref[...] + got_ref[...].astype(jnp.float32)
    sibling = sibling_ref[:, : 3 * columns].astype(jnp.float32)
    for part, half in ((own, info_ref[0]), (sibling, 1 - info_ref[0])):
        for block in range(3):
            first = pl.multiple_of((2 * block + half) * columns, 128)
            d_in_ref[:, pl.ds(first, columns)] = part[:, block * columns : (block + 1) * columns]
    owner = info_ref[0] == info_ref[2]

    @pl.when(owner)
    def _():
        d_out_ref[...] = out_own_ref[...] + out_got_ref[...].astype(jnp.float32)

    @pl.when(jnp.logical_not(owner))
    def _():
        d_out_ref[...] = sibling_ref[:, 3 * columns :].astype(jnp.float32)


def call(kernel, outs, operands, scratch=(), flops=0, scalars=1, after=None, mebibytes=5, far=0):
    in_specs = [pl.BlockSpec(memory_space=pltpu.SMEM)] * scalars
    in_specs += [pl.BlockSpec(memory_space=pltpu.HBM)] * far
    in_specs += [pl.BlockSpec(memory_space=pltpu.VMEM)] * (len(operands) - scalars - far)
    moved = sum(item.size * item.dtype.itemsize for item in [*operands, *outs])
    if after is not None:
        operands = [*operands, after]
        in_specs.append(pl.BlockSpec(memory_space=pl.ANY))
    return pl.pallas_call(
        kernel,
        out_shape=list(outs),
        in_specs=in_specs,
        out_specs=[pl.BlockSpec(memory_space=pltpu.VMEM)] * len(outs),
        scratch_shapes=list(scratch),
        cost_estimate=pl.CostEstimate(flops=flops, bytes_accessed=moved, transcendentals=0),
        compiler_params=pltpu.CompilerParams(vmem_limit_bytes=mebibytes * 2**20),
    )(*operands)


def by_chips(acts, grad_top, w_in, w_out, offsets):
    half_type, full_type = jnp.bfloat16, jnp.float32
    shape = jax.ShapeDtypeStruct
    sections = lax.axis_size("section")
    shards = lax.axis_size("tm")
    levels = offsets.shape[1]
    half = shards // 2
    replicas = half // 2
    me = lax.axis_index("tm")
    parity = lax.rem(me, 2)
    side = lax.div(me, half)
    micro_count, shard_rows, model_width = acts.shape[1:]
    columns = model_width // 2
    heads = columns // HEAD_DIM
    seq = shards * shard_rows
    count = seq // 2
    w_qkv = w_in[0]
    w_rows = w_out[0]
    beside = lax.div(lax.rem(me, half), 2)
    micro = lax.rem(side + beside, 2)
    info = jnp.stack([parity, beside, side, lax.axis_index("section"), micro])
    info = jnp.concatenate([info.astype(jnp.int32), offsets[0]])

    def swapped(value, bits, chosen=None):
        pairs = [(device, device ^ bits) for device in range(shards)]
        pairs = [pair for pair in pairs if chosen is None or chosen(pair[0])]
        return lax.ppermute(value, "tm", pairs)

    core, near, far = 1, 2, half

    packed = shape((shard_rows, model_width + 128), half_type)
    top_shape = shape((shard_rows, model_width), half_type)
    own_acts, other_acts, own_top, other_top = call(
        functools.partial(pack_kernel, levels),
        [packed, packed, top_shape, top_shape],
        [info, acts[0], grad_top],
        scratch=[pltpu.SemaphoreType.DMA((4,))],
        far=2,
    )
    (touched,) = call(
        touch_kernel, [shape((16, 128), half_type)], [w_qkv], scalars=0, after=own_acts
    )
    pieces = [own_acts, swapped(other_acts, near), swapped(other_acts, far)]
    pieces += [swapped(own_acts, near + far)]
    tops = [own_top, swapped(other_top, near), swapped(other_top, far)]
    pieces[-1], tops, touched = lax.optimization_barrier((pieces[-1], tops, touched))
    tops += [swapped(own_top, near + far)]
    pieces += [swapped(piece, core) for piece in pieces]

    rows_shape = shape((seq, columns), half_type)
    normed, rms, norm, flag_rows, queries, keys, values, keys_t = call(
        functools.partial(project_kernel, replicas),
        [
            shape((2, replicas, shard_rows, model_width), full_type),
            shape((2, replicas, shard_rows, 128), full_type),
            shape((seq, model_width), half_type),
            shape((128, seq), full_type),
            rows_shape,
            rows_shape,
            rows_shape,
            shape((columns, seq), half_type),
        ],
        [info, *pieces, w_qkv],
        scratch=[pltpu.VMEM((shards, *packed.shape), half_type)],
        flops=6 * seq * model_width * columns,
        after=touched,
    )
    tops, _ = lax.optimization_barrier((tuple(tops), keys_t))
    tops = [*tops, *[swapped(piece, core) for piece in tops]]
    pairs = heads // 2
    upper_prob, upper_at = call(
        functools.partial(upper_forward_kernel, levels, shard_rows),
        [
            shape((pairs, seq, 2 * count), half_type),
            shape((columns, count), half_type),
        ],
        [flag_rows, queries, keys, values],
        scalars=0,
        flops=4 * columns * seq * count,
    )
    own_rows = model_width // shards
    probs, attended = {True: upper_prob}, {True: upper_at}
    got, kept = {}, {}
    piece_shape = shape((replicas, shard_rows, model_width), half_type)
    grads_shape = shape((replicas, shard_rows, 3 * columns), half_type)
    sum_shape = shape((count, columns), full_type)
    full_grads = shape((half, shard_rows, 3 * columns), half_type)
    full_rows = shape((half, shard_rows, model_width), half_type)
    term_shape = (own_rows, 3 * columns)
    rows_scratch = pltpu.VMEM(full_rows.shape, half_type)
    grads_scratch = pltpu.VMEM(full_grads.shape, half_type)
    result, full, ordered = {}, {}, {}
    grad_in = keys_t
    for turn in range(sections):
        last = turn + 1 == sections
        fresh_section = sections - 1 - turn
        sums, parts, crossed = [], {}, {}
        for upper in (True, False):
            rows_in = tops
            if turn:
                before = result[False] if upper else keep
                pieces = []
                for piece in got[upper]:
                    piece, before = lax.optimization_barrier((piece, before))
                    pieces.append(piece)
                got[upper] = pieces
                if upper:
                    result[False] = before
                else:
                    keep = before
                others = [swapped(piece, core) for piece in got[upper]]
                rows_in = [*got[upper], *others, *kept[upper]]
            after = None if upper else parts[True]
            outs = [piece_shape, piece_shape, grads_shape, grads_shape]
            outs += [sum_shape, sum_shape] if upper else []
            scratch = []
            if last:
                outs += [full_grads]
            else:
                scratch += [grads_scratch]
            if last:
                outs += [full_rows]
            else:
                scratch += [rows_scratch]
            part_keys = seq if upper else count
            scratch += [pltpu.VMEM((pairs, part_keys, 2 * count), half_type)]
            answer = call(
                functools.partial(
                    backward_kernel, upper, 0 if turn else len(tops), replicas, fresh_section
                ),
                outs,
                [info, *rows_in, w_rows, probs[upper], queries, values, keys_t]
                + [attended[upper], *sums],
                scratch=scratch,
                flops=2 * count * columns * (2 * model_width + 4 * part_keys),
                after=after,
            )
            kept[upper] = tuple(answer[:2])
            keep, send = answer[2:4]
            parts[upper] = keep
            if upper:
                sums = answer[4:6]
                (parts[True],) = call(
                    norm_part_kernel,
                    [shape((replicas * shard_rows, model_width), full_type)],
                    [info, keep, w_qkv],
                    flops=3 * replicas * shard_rows * model_width * model_width,
                    after=keep,
                )
                if turn == 0:
                    lower_prob, lower_at, norm_t = call(
                        functools.partial(lower_forward_kernel, levels, shard_rows),
                        [
                            shape((pairs, count, 2 * count), half_type),
                            shape((columns, count), half_type),
                            shape((4 * own_rows, seq), half_type),
                        ],
                        [info, norm, flag_rows, queries, keys, values],
                        flops=4 * columns * count * count,
                        after=parts[True],
                    )
                    probs[False], attended[False] = lower_prob, lower_at
            if last:
                full[upper], ordered[upper] = answer[-2:]
            crossed[upper] = swapped(send, core)
        if last:
            terms = call(
                term_kernel,
                [shape(term_shape, full_type)] * 2
                + [shape(term_shape, half_type)] * 2
                + [shape((own_rows, model_width), full_type)] * 2
                + [shape((own_rows, model_width), half_type)],
                [info, norm_t, full[False], full[True], attended[False], attended[True]]
                + [ordered[False], ordered[True]],
                flops=2 * own_rows * seq * (12 * columns + 3 * model_width),
                mebibytes=10,
            )
            grad_in = terms[3]
        for upper in (True, False):
            grad_pieces = call(
                functools.partial(norm_kernel, upper),
                [top_shape] * replicas if upper else [piece_shape],
                [info, parts[upper], crossed[upper], normed, rms, kept[upper][0], w_qkv],
                flops=6 * replicas * shard_rows * model_width * model_width,
                after=grad_in,
            )
            result[upper] = grad_pieces
            grad_in = grad_pieces[-1]
            if not last:
                hop = [(sections - 1 - turn, sections - 2 - turn)]
                got[upper] = [lax.ppermute(piece, "section", hop) for piece in grad_pieces]

    in_pass, in_keep, send_pass, send_keep, out_pass, out_keep, out_send = terms
    got_pass = swapped(send_pass, near)
    got_keep = swapped(send_keep, far)
    got_out_pass = swapped(out_send, near, lambda device: device // half == device % 2)
    got_out_keep = swapped(out_send, far, lambda device: device // half != device % 2)
    upper_own, lower_own = result[True][0], result[False][0][0]
    mine = jnp.where(side == 1, upper_own, lower_own)
    theirs = jnp.where(side == 1, lower_own, upper_own)
    partner = swapped(theirs, far)
    _, _, done = lax.optimization_barrier((got_keep, got_out_keep, partner))
    (summed,) = call(
        sum_kernel,
        [shape((own_rows, 3 * columns + model_width), half_type)],
        [in_pass, got_pass, out_pass, got_out_pass],
        scalars=0,
        after=done,
    )
    d_w_in, d_w_out = call(
        place_kernel,
        [
            shape((own_rows, 3 * model_width), full_type),
            shape((own_rows, model_width), full_type),
        ],
        [info, in_keep, got_keep, out_keep, got_out_keep, swapped(summed, core)],
    )
    d_acts = jnp.where(micro == 0, jnp.stack([mine, partner]), jnp.stack([partner, mine]))
    return (d_acts[None], d_w_in[None], d_w_out[None])


def layer_gradients(acts, grad_top, w_in, w_out, offsets):
    shards = lax.axis_size("tm")
    micro_count, shard_rows, model_width = acts.shape[1:]
    heads = model_width // HEAD_DIM
    prob_bytes = 2 * heads * (shards * shard_rows) ** 2
    fits = prob_bytes <= 2**24 and model_width % (128 * shards) == 0 and shard_rows % 16 == 0
    square = shards % 4 == 0 and shards // 4 == 2
    if micro_count == 2 and square and heads % 4 == 0 and fits:
        return by_chips(acts, grad_top, w_in, w_out, offsets)
    return per_device(acts, grad_top, w_in, w_out, offsets)


def solution(mesh):
    placed = (
        P("section", None, "tm", None),
        P(None, "tm", None),
        P("section", None, None),
        P("section", None, None),
        P("tm", None),
    )
    return jax.shard_map(
        layer_gradients,
        mesh=mesh,
        in_specs=placed,
        out_specs=(
            P("section", None, "tm", None),
            P("section", "tm", None),
            P("section", "tm", None),
        ),
        check_vma=False,
    )
```

```python
import functools
import jax
import jax.numpy as jnp
from jax import lax
from jax.experimental import pallas as pl
from jax.experimental.pallas import tpu as pltpu
from jax.sharding import PartitionSpec as P

HEAD_DIM = 64


epsilon = 1e-06
negative_fill = -1e30


def shifted(value, axis, steps):
    count = lax.axis_size(axis)
    initial, last = (max(0, -steps), min(count, count - steps))
    return lax.ppermute(value, axis, [(source, source + steps) for source in range(initial, last)])


def normalize(inputs):
    values = inputs.astype(jnp.float32)
    inverse_rms = lax.rsqrt(jnp.mean(values * values, axis=-1, keepdims=True) + epsilon)
    return (values * inverse_rms, inverse_rms)


def key_bias(level_flags, shard_rows):
    position = jnp.arange(shard_rows)
    own_part = position[None, :] <= position[:, None]
    far_part = jnp.repeat(level_flags != 0, shard_rows)
    far_part = jnp.broadcast_to(far_part[None, :], (shard_rows, far_part.shape[0]))
    return jnp.concatenate([own_part, far_part], 1)


def split_heads(row_block):
    return row_block.reshape(row_block.shape[0], -1, HEAD_DIM)


def softmax_keys(queries, key_heads, allowed):
    scores = jnp.einsum(
        "ihd,jhd->hij", queries, key_heads, preferred_element_type=jnp.float32
    ) * HEAD_DIM ** (-0.5)
    scores = jnp.where(allowed[None], scores, negative_fill)
    highest = jnp.max(scores, axis=-1, keepdims=True)
    shifted_exp = jnp.where(allowed[None], jnp.exp(scores - highest), 0.0)
    return shifted_exp / jnp.sum(shifted_exp, axis=-1, keepdims=True)


def attend(query_rows, key_rows, allowed):
    model_width = query_rows.shape[1]
    probability = softmax_keys(
        split_heads(query_rows), split_heads(key_rows[:, :model_width]), allowed
    )
    attended = jnp.einsum(
        "hij,jhd->ihd",
        probability.astype(jnp.bfloat16),
        split_heads(key_rows[:, model_width:]),
        preferred_element_type=jnp.float32,
    )
    return attended.reshape(query_rows.shape).astype(jnp.bfloat16)


def attend_back(query_rows, key_rows, allowed, incoming, attended, w_proj):
    model_width = query_rows.shape[1]
    queries = split_heads(query_rows)
    key_heads = split_heads(key_rows[:, :model_width])
    value_heads = split_heads(key_rows[:, model_width:])
    probability = softmax_keys(queries, key_heads, allowed)
    rounded = probability.astype(jnp.bfloat16)
    upstream = lax.dot_general(
        incoming, w_proj, (((1,), (1,)), ((), ())), preferred_element_type=jnp.float32
    ).astype(jnp.bfloat16)
    up_heads = split_heads(upstream)
    delta = jnp.einsum(
        "ihd,ihd->hi", up_heads.astype(jnp.float32), split_heads(attended).astype(jnp.float32)
    )[..., None]
    prob_grad = jnp.einsum(
        "ihd,jhd->hij", up_heads, value_heads, preferred_element_type=jnp.float32
    )
    score_grad = (probability * (prob_grad - delta)).astype(jnp.bfloat16)
    scale_factor = HEAD_DIM ** (-0.5)
    query_grad = (
        jnp.einsum("hij,jhd->ihd", score_grad, key_heads, preferred_element_type=jnp.float32)
        * scale_factor
    )
    key_grad = (
        jnp.einsum("hij,ihd->jhd", score_grad, queries, preferred_element_type=jnp.float32)
        * scale_factor
    )
    value_grad = jnp.einsum("hij,ihd->jhd", rounded, up_heads, preferred_element_type=jnp.float32)
    return (
        query_grad.reshape(-1, model_width),
        key_grad.reshape(-1, model_width),
        value_grad.reshape(-1, model_width),
    )


def per_device(acts, grad_top, w_in, w_out, offsets):
    sections = lax.axis_size("section")
    shards = lax.axis_size("tm")
    levels = shards.bit_length() - 1
    section_index = lax.axis_index("section")
    micro_count = acts.shape[1]
    shard_rows = acts.shape[2]
    model_width = acts.shape[3]
    w_qkv = w_in[0]
    w_proj = w_out[0]
    level_flags = offsets[0]
    normed, inverse_rms = normalize(acts[0])
    rounded_norm = normed.astype(jnp.bfloat16)
    qkv = jnp.dot(rounded_norm.reshape(-1, model_width), w_qkv, preferred_element_type=jnp.float32)
    qkv = qkv.astype(jnp.bfloat16).reshape(micro_count, shard_rows, 3 * model_width)
    pairs = qkv[..., model_width:]
    far_list = [shifted(pairs, "tm", 2**level) for level in range(levels)]
    key_rows = jnp.concatenate([pairs] + far_list, 1)
    allowed = key_bias(level_flags, shard_rows)
    attended = jnp.stack(
        [
            attend(qkv[index, :, :model_width], key_rows[index], allowed)
            for index in range(micro_count)
        ],
        0,
    )

    def attention_part(incoming, slot):
        query_rows = lax.dynamic_index_in_dim(qkv, slot, 0, False)[:, :model_width]
        slot_keys = lax.dynamic_index_in_dim(key_rows, slot, 0, False)
        slot_attended = lax.dynamic_index_in_dim(attended, slot, 0, False)
        query_grad, key_grad, value_grad = attend_back(
            query_rows, slot_keys, allowed, incoming, slot_attended, w_proj
        )
        owner_sum = jnp.concatenate([key_grad[:shard_rows], value_grad[:shard_rows]], 1)
        far_part = jnp.concatenate([key_grad[shard_rows:], value_grad[shard_rows:]], 1)
        far_part = far_part.astype(jnp.bfloat16).reshape(levels, shard_rows, 2 * model_width)
        return (query_grad, owner_sum, far_part)

    def empty_attention(incoming, slot):
        return (
            jnp.zeros((shard_rows, model_width), jnp.float32),
            jnp.zeros((shard_rows, 2 * model_width), jnp.float32),
            jnp.zeros((levels, shard_rows, 2 * model_width), jnp.bfloat16),
        )

    def norm_part(qkv_grad, incoming, slot):
        norm_grad = lax.dot_general(
            qkv_grad, w_qkv, (((1,), (1,)), ((), ())), preferred_element_type=jnp.float32
        )
        slot_normed = lax.dynamic_index_in_dim(normed, slot, 0, False)
        slot_rms = lax.dynamic_index_in_dim(inverse_rms, slot, 0, False)
        inner = jnp.mean(norm_grad * slot_normed, axis=-1, keepdims=True)
        return (incoming.astype(jnp.float32) + slot_rms * (norm_grad - slot_normed * inner)).astype(
            jnp.bfloat16
        )

    def empty_norm(qkv_grad, incoming, slot):
        return jnp.zeros((shard_rows, model_width), jnp.bfloat16)

    def step(turn, carry):
        received, grad_store, qkv_store, incoming_store = carry
        slot_raw = turn - (sections - 1 - section_index)
        active = (slot_raw >= 0) & (slot_raw < micro_count)
        slot = jnp.clip(slot_raw, 0, micro_count - 1)
        incoming = jnp.where(
            section_index == sections - 1,
            lax.dynamic_index_in_dim(grad_top, slot, 0, False),
            received,
        )
        query_grad, owner_sum, far_part = lax.cond(
            active, attention_part, empty_attention, incoming, slot
        )
        for level in range(levels):
            owner_sum = owner_sum + shifted(far_part[level], "tm", -(2**level)).astype(jnp.float32)
        qkv_grad = jnp.concatenate([query_grad, owner_sum], 1).astype(jnp.bfloat16)
        grad_in = lax.cond(active, norm_part, empty_norm, qkv_grad, incoming, slot)
        sent_down = shifted(grad_in, "section", -1)
        grad_store = jnp.where(
            active, lax.dynamic_update_index_in_dim(grad_store, grad_in, slot, 0), grad_store
        )
        qkv_store = jnp.where(
            active, lax.dynamic_update_index_in_dim(qkv_store, qkv_grad, slot, 0), qkv_store
        )
        incoming_store = jnp.where(
            active,
            lax.dynamic_update_index_in_dim(incoming_store, incoming, slot, 0),
            incoming_store,
        )
        return (sent_down, grad_store, qkv_store, incoming_store)

    initial = (
        jnp.zeros((shard_rows, model_width), jnp.bfloat16),
        jnp.zeros((micro_count, shard_rows, model_width), jnp.bfloat16),
        jnp.zeros((micro_count, shard_rows, 3 * model_width), jnp.bfloat16),
        jnp.zeros((micro_count, shard_rows, model_width), jnp.bfloat16),
    )
    received, grad_store, qkv_store, incoming_store = lax.fori_loop(
        0, sections + micro_count - 1, step, initial
    )
    flat_norm = rounded_norm.reshape(-1, model_width)
    flat_attended = attended.reshape(-1, model_width)
    flat_qkv = qkv_store.reshape(-1, 3 * model_width)
    flat_incoming = incoming_store.reshape(-1, model_width)
    contract = (((0,), (0,)), ((), ()))
    first = lax.dot_general(flat_norm, flat_qkv, contract, preferred_element_type=jnp.float32)
    second = lax.dot_general(
        flat_attended, flat_incoming, contract, preferred_element_type=jnp.float32
    )
    summed = lax.psum_scatter(
        jnp.concatenate([first, second], 1).astype(jnp.bfloat16),
        "tm",
        scatter_dimension=0,
        tiled=True,
    ).astype(jnp.float32)
    return (
        grad_store[None],
        summed[None, :, : 3 * model_width],
        summed[None, :, 3 * model_width :],
    )


def side_by_side(transposed, pair):
    width = 2 * HEAD_DIM
    rows = transposed[pair * width : (pair + 1) * width]
    empty = jnp.zeros((HEAD_DIM, rows.shape[1]), rows.dtype)
    return jnp.concatenate(
        [
            jnp.concatenate([rows[:HEAD_DIM], empty], 0),
            jnp.concatenate([empty, rows[HEAD_DIM:]], 0),
        ],
        1,
    )


def one_above_other(rows, masks):
    return jnp.concatenate([rows * masks[0], rows * masks[1]], 0)


def head_masks():
    lane = lax.broadcasted_iota(jnp.int32, (1, 2 * HEAD_DIM), 1)
    return [
        jnp.where(lane < HEAD_DIM, 1.0, 0.0).astype(jnp.bfloat16),
        jnp.where(lane < HEAD_DIM, 0.0, 1.0).astype(jnp.bfloat16),
    ]


def key_bias_rows(flag_rows, levels, shard_rows, keys, first_query, count):
    key_at = lax.broadcasted_iota(jnp.int32, (keys, count), 0)
    query_at = lax.broadcasted_iota(jnp.int32, (keys, count), 1) + first_query
    gap = lax.div(query_at, shard_rows) - lax.div(key_at, shard_rows)
    allowed = (gap == 0) & (key_at <= query_at)
    for level in range(levels):
        allowed = allowed | ((gap == 2**level) & (flag_rows[level : level + 1] != 0))
    return jnp.where(allowed, 0.0, negative_fill)


def softmax_pass(queries, keys, values, bias, prob_ref, at_ref):
    queries_t = queries.T
    values_t = values.T
    width = 2 * HEAD_DIM
    count = queries.shape[0]
    for pair in range(queries.shape[1] // width):
        at_pair = slice(pair * width, (pair + 1) * width)
        scores = jnp.dot(
            keys[:, at_pair], side_by_side(queries_t, pair), preferred_element_type=jnp.float32
        )
        for half in range(2):
            at_half = slice(half * count, (half + 1) * count)
            biased = scores[:, at_half] + bias
            shifted_exp = jnp.exp(biased - jnp.max(biased, axis=0, keepdims=True))
            probability = shifted_exp * (1.0 / jnp.sum(shifted_exp, axis=0, keepdims=True))
            prob_ref[pair, :, at_half] = probability.astype(jnp.bfloat16)
    for head in range(queries.shape[1] // HEAD_DIM):
        at = slice(head * HEAD_DIM, (head + 1) * HEAD_DIM)
        at_half = slice(head % 2 * count, (head % 2 + 1) * count)
        at_ref[at] = jnp.dot(
            values_t[at], prob_ref[head // 2, :, at_half], preferred_element_type=jnp.float32
        ).astype(jnp.bfloat16)


def pack_kernel(
    levels, info_ref, acts_ref, top_ref, own_ref, other_ref, own_top_ref, other_top_ref, sems
):
    model_width = acts_ref.shape[2]
    shard_rows = own_ref.shape[0]
    side = info_ref[4]
    copies = [
        pltpu.make_async_copy(acts_ref.at[side], own_ref.at[:, :model_width], sems.at[0]),
        pltpu.make_async_copy(acts_ref.at[1 - side], other_ref.at[:, :model_width], sems.at[1]),
        pltpu.make_async_copy(top_ref.at[side], own_top_ref, sems.at[2]),
        pltpu.make_async_copy(top_ref.at[1 - side], other_top_ref, sems.at[3]),
    ]
    for copy in copies:
        copy.start()
    lane = lax.broadcasted_iota(jnp.int32, (shard_rows, own_ref.shape[1] - model_width), 1)
    flags = jnp.zeros(lane.shape, jnp.float32)
    for level in range(levels):
        seen = jnp.where(info_ref[5 + level] != 0, 1.0, 0.0)
        flags = jnp.where(lane == level, seen, flags)
    own_ref[:, model_width:] = flags.astype(jnp.bfloat16)
    other_ref[:, model_width:] = flags.astype(jnp.bfloat16)
    for copy in copies:
        copy.wait()


def touch_kernel(w_ref, after_ref, out_ref):
    out_ref[...] = w_ref[: out_ref.shape[0], : out_ref.shape[1]]


def project_kernel(replicas, info_ref, *refs):
    pieces = refs[: 4 * replicas]
    w_ref, _, normed_ref, rms_ref, norm_ref, flag_ref, q_ref, k_ref, v_ref, kt_ref, packed_ref = refs[
        4 * replicas :
    ]
    shards, shard_rows = packed_ref.shape[:2]
    model_width = w_ref.shape[0]
    seq = shards * shard_rows
    columns = q_ref.shape[1]
    at_piece = 0
    for core in (info_ref[0], 1 - info_ref[0]):
        for side in (info_ref[2], 1 - info_ref[2]):
            for step in range(replicas):
                shard = side * (shards // 2) + place_of(info_ref, step, replicas) + core
                packed_ref[shard] = pieces[at_piece][...]
                at_piece += 1
    for chunk in range(2):
        for step in range(replicas):
            shard = chunk * (shards // 2) + place_of(info_ref, step, replicas) + info_ref[0]
            normed, inverse_rms = normalize(packed_ref[shard][:, :model_width])
            normed_ref[chunk, step] = normed
            rms_ref[chunk, step] = jnp.broadcast_to(inverse_rms, rms_ref.shape[2:])
    normed, _ = normalize(packed_ref[:, :, :model_width].reshape(seq, model_width))
    rounded = normed.astype(jnp.bfloat16)
    norm_ref[...] = rounded
    flag_ref[...] = packed_ref[:, :, model_width:].reshape(seq, -1).astype(jnp.float32).T
    scale_factor = HEAD_DIM ** (-0.5)
    for block, out_ref in enumerate((q_ref, k_ref, v_ref)):
        first = pl.multiple_of(block * model_width + info_ref[0] * columns, 128)
        product = jnp.dot(
            rounded, w_ref[:, pl.ds(first, columns)], preferred_element_type=jnp.float32
        ).astype(jnp.bfloat16)
        out_ref[...] = product * scale_factor if block == 0 else product
    kt_ref[...] = (k_ref[...] * scale_factor).T


def upper_forward_kernel(
    levels, shard_rows, flag_ref, q_ref, k_ref, v_ref, prob_ref, at_ref
):
    seq = q_ref.shape[0]
    count = seq // 2
    bias = key_bias_rows(flag_ref[:, count:], levels, shard_rows, seq, count, count)
    softmax_pass(q_ref[count:], k_ref[...], v_ref[...], bias, prob_ref, at_ref)


def lower_forward_kernel(
    levels,
    shard_rows,
    info_ref,
    norm_ref,
    flag_ref,
    q_ref,
    k_ref,
    v_ref,
    after_ref,
    prob_ref,
    at_ref,
    gt_ref,
):
    seq = norm_ref.shape[0]
    count = seq // 2
    bias = key_bias_rows(flag_ref[:, :count], levels, shard_rows, count, 0, count)
    softmax_pass(q_ref[:count], k_ref[:count], v_ref[:count], bias, prob_ref, at_ref)
    rows = gt_ref.shape[0] // 4
    parity, x, y = info_ref[0], info_ref[1], info_ref[2]
    half = norm_ref.shape[1] // rows // 2
    for place, block in enumerate(
        (
            half * y + 2 * x + 1 - parity,
            half * y + 2 * x + parity,
            half * y + 2 * (1 - x) + 1 - parity,
            half * (1 - y) + 2 * x + parity,
        )
    ):
        first = pl.multiple_of(block * rows, 128)
        gt_ref[place * rows : (place + 1) * rows] = norm_ref[:, pl.ds(first, rows)].T


def place_of(info_ref, step, replicas):
    return 2 * lax.rem(info_ref[1] - step + replicas, replicas)


def merge_rows(info_ref, fresh, got_refs, kept_refs, out_refs, rows_ref):
    @pl.when(fresh)
    def _():
        for core, out_ref in enumerate(out_refs):
            refs = got_refs[core * len(got_refs) // 2 : (core + 1) * len(got_refs) // 2]
            if len(refs) == 1:
                out_ref[...] = refs[0][...]
            else:
                for step, got_ref in enumerate(refs):
                    out_ref[step] = got_ref[...]

    @pl.when(jnp.logical_not(fresh))
    def _():
        for out_ref, kept_ref in zip(out_refs, kept_refs):
            out_ref[...] = kept_ref[...]

    place_rows(info_ref, out_refs, rows_ref)


def place_rows(info_ref, out_refs, rows_ref):
    replicas = out_refs[0].shape[0]
    for step in range(replicas):
        place = place_of(info_ref, step, replicas)
        rows_ref[place + info_ref[0]] = out_refs[0][step]
        rows_ref[place + 1 - info_ref[0]] = out_refs[1][step]


def merge_tops(info_ref, upper, piece_refs, out_refs, rows_ref):
    replicas = out_refs[0].shape[0]
    own_chunk = info_ref[2] == (1 if upper else 0)
    for core in range(2):
        refs = piece_refs[2 * replicas * core : 2 * replicas * (core + 1)]

        @pl.when(own_chunk)
        def _():
            for step in range(replicas):
                out_refs[core][step] = refs[step][...]

        @pl.when(jnp.logical_not(own_chunk))
        def _():
            for step in range(replicas):
                out_refs[core][step] = refs[replicas + step][...]

    place_rows(info_ref, out_refs, rows_ref)


def backward_kernel(upper, tops, replicas, fresh_section, info_ref, *refs):
    refs = list(refs)
    got = tops or (2 * replicas + 2 if upper else 4)
    got_refs = refs[:got]
    w_ref, prob_ref, q_ref, v_ref, kt_ref, at_ref = refs[got : got + 6]
    refs = refs[got + 6 :]
    if not upper:
        key_sum_ref, value_sum_ref, _ = refs[:3]
        refs = refs[3:]
    own_ref, other_ref, keep_ref, send_ref = refs[:4]
    refs = refs[4:]
    if upper:
        key_sum_ref, value_sum_ref = refs[:2]
        refs = refs[2:]
    grads_ref, rows_ref, scores_ref = refs
    shard_rows, model_width = own_ref.shape[1:]
    count = rows_ref.shape[0] * shard_rows
    keys = prob_ref.shape[1]
    parity = info_ref[0]
    columns = q_ref.shape[1]
    width = 2 * HEAD_DIM
    if tops:
        merge_tops(info_ref, upper, got_refs, (own_ref, other_ref), rows_ref)
    else:
        fresh = info_ref[3] == fresh_section
        merge_rows(info_ref, fresh, got_refs[:-2], got_refs[-2:], (own_ref, other_ref), rows_ref)
    rows = rows_ref[...].reshape(count, model_width)
    weights = w_ref[pl.ds(pl.multiple_of(parity * columns, 128), columns), :]
    over_width = (((1,), (1,)), ((), ()))
    upstream = lax.dot_general(
        rows, weights, over_width, preferred_element_type=jnp.float32
    ).astype(jnp.bfloat16)
    upstream_t = upstream.T
    product_t = upstream_t.astype(jnp.float32) * at_ref[...].astype(jnp.float32)
    first_query = keys - count
    masks = head_masks()

    def put(block, pair, part):
        first = block * columns + pair * width
        grads_ref[:, :, first : first + width] = part.astype(jnp.bfloat16).reshape(
            -1, shard_rows, width
        )

    for pair in range(columns // width):
        at_pair = slice(pair * width, (pair + 1) * width)
        prob_grad = jnp.dot(
            v_ref[:keys, at_pair], side_by_side(upstream_t, pair), preferred_element_type=jnp.float32
        )
        for half in range(2):
            at_half = slice(half * count, (half + 1) * count)
            first = pair * width + half * HEAD_DIM
            delta = jnp.sum(product_t[first : first + HEAD_DIM], axis=0, keepdims=True)
            scores_ref[pair, :, at_half] = (
                prob_ref[pair, :, at_half].astype(jnp.float32) * (prob_grad[:, at_half] - delta)
            ).astype(jnp.bfloat16)
        value_grad = jnp.dot(
            prob_ref[pair],
            one_above_other(upstream[:, at_pair], masks),
            preferred_element_type=jnp.float32,
        )
        if upper:
            value_sum_ref[:, at_pair] = value_grad[:first_query]
            value_grad = value_grad[first_query:]
        else:
            value_grad = value_grad + value_sum_ref[:, at_pair]
        put(2, pair, value_grad)
    for pair in range(columns // width):
        at_pair = slice(pair * width, (pair + 1) * width)
        queries = q_ref[first_query : first_query + count, at_pair]
        key_grad = jnp.dot(
            scores_ref[pair], one_above_other(queries, masks), preferred_element_type=jnp.float32
        )
        if upper:
            key_sum_ref[:, at_pair] = key_grad[:first_query]
            key_grad = key_grad[first_query:]
        else:
            key_grad = key_grad + key_sum_ref[:, at_pair]
        put(1, pair, key_grad)
        query_grad = [
            jnp.dot(
                kt_ref[pair * width + half * HEAD_DIM : pair * width + (half + 1) * HEAD_DIM, :keys],
                scores_ref[pair, :, half * count : (half + 1) * count],
                preferred_element_type=jnp.float32,
            )
            for half in range(2)
        ]
        put(0, pair, jnp.concatenate(query_grad, 0).astype(jnp.bfloat16).T)
    for step in range(replicas):
        place = place_of(info_ref, step, replicas)
        keep_ref[step] = grads_ref[place + parity]
        send_ref[step] = grads_ref[place + 1 - parity]


def norm_product(part_ref, w_ref, half):
    replicas, shard_rows, triple = part_ref.shape
    columns = triple // 3
    model_width = w_ref.shape[0]
    total = jnp.zeros((replicas * shard_rows, model_width), jnp.float32)
    for block in range(3):
        first = pl.multiple_of(block * model_width + half * columns, 128)
        total += lax.dot_general(
            part_ref[:, :, block * columns : (block + 1) * columns].reshape(-1, columns),
            w_ref[:, pl.ds(first, columns)],
            (((1,), (1,)), ((), ())),
            preferred_element_type=jnp.float32,
        )
    return total


def norm_part_kernel(info_ref, keep_ref, w_ref, after_ref, out_ref):
    out_ref[...] = norm_product(keep_ref, w_ref, info_ref[0])


def norm_kernel(
    upper, info_ref, keep_ref, got_ref, normed_ref, rms_ref, incoming_ref, w_ref, after_ref, *out_refs
):
    replicas, shard_rows, triple = got_ref.shape
    model_width = w_ref.shape[0]
    rows = replicas * shard_rows
    norm_grad = norm_product(got_ref, w_ref, 1 - info_ref[0])
    norm_grad += keep_ref[...] if upper else norm_product(keep_ref, w_ref, info_ref[0])
    chunk = 1 if upper else 0
    normed = normed_ref[chunk].reshape(rows, model_width)
    inverse_rms = rms_ref[chunk].reshape(rows, -1)[:, :1]
    inner = jnp.mean(norm_grad * normed, axis=-1, keepdims=True)
    incoming = incoming_ref[...].reshape(rows, model_width).astype(jnp.float32)
    grad_in = incoming + inverse_rms * (norm_grad - normed * inner)
    grad_in = grad_in.astype(jnp.bfloat16).reshape(replicas, shard_rows, model_width)
    if len(out_refs) == 1:
        out_refs[0][...] = grad_in
    else:
        for step, out_ref in enumerate(out_refs):
            out_ref[...] = grad_in[step]


def term_kernel(info_ref, gt_ref, *refs):
    grad_refs, at_refs, row_refs = refs[:2], refs[2:4], refs[4:6]
    own_pass_ref, own_keep_ref, send_pass_ref, send_keep_ref = refs[6:10]
    out_pass_ref, out_keep_ref, out_send_ref = refs[10:]
    rows = own_pass_ref.shape[0]
    width = out_send_ref.shape[1]
    count = row_refs[0].shape[0] * row_refs[0].shape[1]
    parity, x, y = info_ref[0], info_ref[1], info_ref[2]
    for half, (pass_ref, keep_ref) in reversed(
        list(enumerate(((own_pass_ref, own_keep_ref), (send_pass_ref, send_keep_ref))))
    ):
        total = sum(
            jnp.dot(
                gt_ref[2 * half * rows : 2 * (half + 1) * rows, chunk * count : (chunk + 1) * count],
                part_ref[...].reshape(count, -1),
                preferred_element_type=jnp.float32,
            )
            for chunk, part_ref in enumerate(grad_refs)
        )
        pass_ref[...] = total[:rows].astype(pass_ref.dtype)
        keep_ref[...] = total[rows:].astype(keep_ref.dtype)
    sent = jnp.where(parity == y, 2 * (1 - x) + 1 - parity, 2 * x + parity)
    blocks = (sent, 2 * x + 1 - parity, 2 * x + parity)
    total = jnp.zeros((3 * rows, width), jnp.float32)
    for at_ref, part_ref in zip(at_refs, row_refs):
        picked = [at_ref[pl.ds(pl.multiple_of(block * rows, 128), rows)] for block in blocks]
        total += jnp.dot(
            jnp.concatenate(picked, 0),
            part_ref[...].reshape(count, width),
            preferred_element_type=jnp.float32,
        )
    out_send_ref[...] = total[:rows].astype(jnp.bfloat16)
    out_pass_ref[...] = total[rows : 2 * rows]
    out_keep_ref[...] = total[2 * rows :]


def sum_kernel(own_ref, got_ref, out_own_ref, out_got_ref, after_ref, sum_ref):
    columns = own_ref.shape[1]
    sum_ref[:, :columns] = (own_ref[...] + got_ref[...].astype(jnp.float32)).astype(jnp.bfloat16)
    sum_ref[:, columns:] = (out_own_ref[...] + out_got_ref[...].astype(jnp.float32)).astype(
        jnp.bfloat16
    )


def pick_kernel(info_ref, upper_ref, lower_ref, out_ref):
    @pl.when(info_ref[2] == 1)
    def _():
        out_ref[...] = lower_ref[0]

    @pl.when(info_ref[2] != 1)
    def _():
        out_ref[...] = upper_ref[...]


def join_kernel(info_ref, upper_ref, lower_ref, got_ref, out_ref):
    micro = info_ref[4]
    out_ref[0, 1 - micro] = got_ref[...]

    @pl.when(info_ref[2] == 1)
    def _():
        out_ref[0, micro] = upper_ref[...]

    @pl.when(info_ref[2] != 1)
    def _():
        out_ref[0, micro] = lower_ref[0]


def place_kernel(
    info_ref, own_ref, got_ref, out_own_ref, out_got_ref, sibling_ref, d_in_ref, d_out_ref
):
    columns = own_ref.shape[1] // 3
    own = own_ref[...] + got_ref[...].astype(jnp.float32)
    sibling = sibling_ref[:, : 3 * columns].astype(jnp.float32)
    for part, half in ((own, info_ref[0]), (sibling, 1 - info_ref[0])):
        for block in range(3):
            first = pl.multiple_of((2 * block + half) * columns, 128)
            d_in_ref[:, pl.ds(first, columns)] = part[:, block * columns : (block + 1) * columns]
    owner = info_ref[0] == info_ref[2]

    @pl.when(owner)
    def _():
        d_out_ref[...] = out_own_ref[...] + out_got_ref[...].astype(jnp.float32)

    @pl.when(jnp.logical_not(owner))
    def _():
        d_out_ref[...] = sibling_ref[:, 3 * columns :].astype(jnp.float32)


def call(kernel, outs, operands, scratch=(), flops=0, scalars=1, after=None, mebibytes=5, far=0):
    in_specs = [pl.BlockSpec(memory_space=pltpu.SMEM)] * scalars
    in_specs += [pl.BlockSpec(memory_space=pltpu.HBM)] * far
    in_specs += [pl.BlockSpec(memory_space=pltpu.VMEM)] * (len(operands) - scalars - far)
    moved = sum(item.size * item.dtype.itemsize for item in [*operands, *outs])
    if after is not None:
        operands = [*operands, after]
        in_specs.append(pl.BlockSpec(memory_space=pl.ANY))
    return pl.pallas_call(
        kernel,
        out_shape=list(outs),
        in_specs=in_specs,
        out_specs=[pl.BlockSpec(memory_space=pltpu.VMEM)] * len(outs),
        scratch_shapes=list(scratch),
        cost_estimate=pl.CostEstimate(flops=flops, bytes_accessed=moved, transcendentals=0),
        compiler_params=pltpu.CompilerParams(vmem_limit_bytes=mebibytes * 2**20),
    )(*operands)


def by_chips(acts, grad_top, w_in, w_out, offsets):
    half_type, full_type = jnp.bfloat16, jnp.float32
    shape = jax.ShapeDtypeStruct
    sections = lax.axis_size("section")
    shards = lax.axis_size("tm")
    levels = offsets.shape[1]
    half = shards // 2
    replicas = half // 2
    me = lax.axis_index("tm")
    parity = lax.rem(me, 2)
    side = lax.div(me, half)
    micro_count, shard_rows, model_width = acts.shape[1:]
    columns = model_width // 2
    heads = columns // HEAD_DIM
    seq = shards * shard_rows
    count = seq // 2
    w_qkv = w_in[0]
    w_rows = w_out[0]
    beside = lax.div(lax.rem(me, half), 2)
    micro = lax.rem(side + beside, 2)
    info = jnp.stack([parity, beside, side, lax.axis_index("section"), micro])
    info = jnp.concatenate([info.astype(jnp.int32), offsets[0]])

    def swapped(value, bits, chosen=None):
        pairs = [(device, device ^ bits) for device in range(shards)]
        pairs = [pair for pair in pairs if chosen is None or chosen(pair[0])]
        return lax.ppermute(value, "tm", pairs)

    core, near, far = 1, 2, half

    packed = shape((shard_rows, model_width + 128), half_type)
    top_shape = shape((shard_rows, model_width), half_type)
    own_acts, other_acts, own_top, other_top = call(
        functools.partial(pack_kernel, levels),
        [packed, packed, top_shape, top_shape],
        [info, acts[0], grad_top],
        scratch=[pltpu.SemaphoreType.DMA((4,))],
        far=2,
    )
    (touched,) = call(
        touch_kernel, [shape((16, 128), half_type)], [w_qkv], scalars=0, after=own_acts
    )
    pieces = [own_acts, swapped(other_acts, near), swapped(other_acts, far)]
    pieces += [swapped(own_acts, near + far)]
    tops = [own_top, swapped(other_top, near), swapped(other_top, far)]
    pieces[-1], tops, touched = lax.optimization_barrier((pieces[-1], tops, touched))
    tops += [swapped(own_top, near + far)]
    pieces += [swapped(piece, core) for piece in pieces]

    rows_shape = shape((seq, columns), half_type)
    normed, rms, norm, flag_rows, queries, keys, values, keys_t = call(
        functools.partial(project_kernel, replicas),
        [
            shape((2, replicas, shard_rows, model_width), full_type),
            shape((2, replicas, shard_rows, 128), full_type),
            shape((seq, model_width), half_type),
            shape((128, seq), full_type),
            rows_shape,
            rows_shape,
            rows_shape,
            shape((columns, seq), half_type),
        ],
        [info, *pieces, w_qkv],
        scratch=[pltpu.VMEM((shards, *packed.shape), half_type)],
        flops=6 * seq * model_width * columns,
        after=touched,
    )
    tops, _ = lax.optimization_barrier((tuple(tops), keys_t))
    tops = [*tops, *[swapped(piece, core) for piece in tops]]
    pairs = heads // 2
    upper_prob, upper_at = call(
        functools.partial(upper_forward_kernel, levels, shard_rows),
        [
            shape((pairs, seq, 2 * count), half_type),
            shape((columns, count), half_type),
        ],
        [flag_rows, queries, keys, values],
        scalars=0,
        flops=4 * columns * seq * count,
    )
    own_rows = model_width // shards
    probs, attended = {True: upper_prob}, {True: upper_at}
    got, kept = {}, {}
    piece_shape = shape((replicas, shard_rows, model_width), half_type)
    grads_shape = shape((replicas, shard_rows, 3 * columns), half_type)
    sum_shape = shape((count, columns), full_type)
    full_grads = shape((half, shard_rows, 3 * columns), half_type)
    full_rows = shape((half, shard_rows, model_width), half_type)
    term_shape = (own_rows, 3 * columns)
    rows_scratch = pltpu.VMEM(full_rows.shape, half_type)
    grads_scratch = pltpu.VMEM(full_grads.shape, half_type)
    result, full, ordered = {}, {}, {}
    grad_in = keys_t
    for turn in range(sections):
        last = turn + 1 == sections
        fresh_section = sections - 1 - turn
        sums, parts, crossed = [], {}, {}
        for upper in (True, False):
            rows_in = tops
            if turn:
                before = result[False] if upper else keep
                pieces = []
                for piece in got[upper]:
                    piece, before = lax.optimization_barrier((piece, before))
                    pieces.append(piece)
                got[upper] = pieces
                if upper:
                    result[False] = before
                else:
                    keep = before
                others = [swapped(piece, core) for piece in got[upper]]
                rows_in = [*got[upper], *others, *kept[upper]]
            after = None if upper else parts[True]
            outs = [piece_shape, piece_shape, grads_shape, grads_shape]
            outs += [sum_shape, sum_shape] if upper else []
            scratch = []
            if last:
                outs += [full_grads]
            else:
                scratch += [grads_scratch]
            if last:
                outs += [full_rows]
            else:
                scratch += [rows_scratch]
            part_keys = seq if upper else count
            scratch += [pltpu.VMEM((pairs, part_keys, 2 * count), half_type)]
            answer = call(
                functools.partial(
                    backward_kernel, upper, 0 if turn else len(tops), replicas, fresh_section
                ),
                outs,
                [info, *rows_in, w_rows, probs[upper], queries, values, keys_t]
                + [attended[upper], *sums],
                scratch=scratch,
                flops=2 * count * columns * (2 * model_width + 4 * part_keys),
                after=after,
            )
            kept[upper] = tuple(answer[:2])
            keep, send = answer[2:4]
            parts[upper] = keep
            if upper:
                sums = answer[4:6]
                (parts[True],) = call(
                    norm_part_kernel,
                    [shape((replicas * shard_rows, model_width), full_type)],
                    [info, keep, w_qkv],
                    flops=3 * replicas * shard_rows * model_width * model_width,
                    after=keep,
                )
                if turn == 0:
                    lower_prob, lower_at, norm_t = call(
                        functools.partial(lower_forward_kernel, levels, shard_rows),
                        [
                            shape((pairs, count, 2 * count), half_type),
                            shape((columns, count), half_type),
                            shape((4 * own_rows, seq), half_type),
                        ],
                        [info, norm, flag_rows, queries, keys, values],
                        flops=4 * columns * count * count,
                        after=parts[True],
                    )
                    probs[False], attended[False] = lower_prob, lower_at
            if last:
                full[upper], ordered[upper] = answer[-2:]
            crossed[upper] = swapped(send, core)
        if last:
            terms = call(
                term_kernel,
                [shape(term_shape, full_type)] * 2
                + [shape(term_shape, half_type)] * 2
                + [shape((own_rows, model_width), full_type)] * 2
                + [shape((own_rows, model_width), half_type)],
                [info, norm_t, full[False], full[True], attended[False], attended[True]]
                + [ordered[False], ordered[True]],
                flops=2 * own_rows * seq * (12 * columns + 3 * model_width),
                mebibytes=10,
            )
            grad_in = terms[3]
        for upper in (True, False):
            grad_pieces = call(
                functools.partial(norm_kernel, upper),
                [top_shape] * replicas if upper else [piece_shape],
                [info, parts[upper], crossed[upper], normed, rms, kept[upper][0], w_qkv],
                flops=6 * replicas * shard_rows * model_width * model_width,
                after=grad_in,
            )
            result[upper] = grad_pieces
            grad_in = grad_pieces[-1]
            if not last:
                hop = [(sections - 1 - turn, sections - 2 - turn)]
                got[upper] = [lax.ppermute(piece, "section", hop) for piece in grad_pieces]

    in_pass, in_keep, send_pass, send_keep, out_pass, out_keep, out_send = terms
    got_pass = swapped(send_pass, near)
    got_keep = swapped(send_keep, far)
    got_out_pass = swapped(out_send, near, lambda device: device // half == device % 2)
    got_out_keep = swapped(out_send, far, lambda device: device // half != device % 2)
    own_rows_grad = [result[True][0], result[False][0]]
    (theirs,) = call(pick_kernel, [top_shape], [info, *own_rows_grad])
    partner = swapped(theirs, far)
    _, _, done = lax.optimization_barrier((got_keep, got_out_keep, partner))
    (summed,) = call(
        sum_kernel,
        [shape((own_rows, 3 * columns + model_width), half_type)],
        [in_pass, got_pass, out_pass, got_out_pass],
        scalars=0,
        after=done,
    )
    d_w_in, d_w_out = call(
        place_kernel,
        [
            shape((own_rows, 3 * model_width), full_type),
            shape((own_rows, model_width), full_type),
        ],
        [info, in_keep, got_keep, out_keep, got_out_keep, swapped(summed, core)],
    )
    (d_acts,) = call(
        join_kernel, [shape(acts.shape, half_type)], [info, *own_rows_grad, partner]
    )
    return (d_acts, d_w_in[None], d_w_out[None])


def layer_gradients(acts, grad_top, w_in, w_out, offsets):
    shards = lax.axis_size("tm")
    micro_count, shard_rows, model_width = acts.shape[1:]
    heads = model_width // HEAD_DIM
    prob_bytes = 2 * heads * (shards * shard_rows) ** 2
    fits = prob_bytes <= 2**24 and model_width % (128 * shards) == 0 and shard_rows % 16 == 0
    square = shards % 4 == 0 and shards // 4 == 2
    if micro_count == 2 and square and heads % 4 == 0 and fits:
        return by_chips(acts, grad_top, w_in, w_out, offsets)
    return per_device(acts, grad_top, w_in, w_out, offsets)


def solution(mesh):
    placed = (
        P("section", None, "tm", None),
        P(None, "tm", None),
        P("section", None, None),
        P("section", None, None),
        P("tm", None),
    )
    return jax.shard_map(
        layer_gradients,
        mesh=mesh,
        in_specs=placed,
        out_specs=(
            P("section", None, "tm", None),
            P("section", "tm", None),
            P("section", "tm", None),
        ),
        check_vma=False,
    )
```

```python
import functools
import jax
import jax.numpy as jnp
from jax import lax
from jax.experimental import pallas as pl
from jax.experimental.pallas import tpu as pltpu
from jax.sharding import PartitionSpec as P

HEAD_DIM = 64


epsilon = 1e-06
PIECES = {True: 2, False: 4}
negative_fill = -1e30


def shifted(value, axis, steps):
    count = lax.axis_size(axis)
    initial, last = (max(0, -steps), min(count, count - steps))
    return lax.ppermute(value, axis, [(source, source + steps) for source in range(initial, last)])


def normalize(inputs):
    values = inputs.astype(jnp.float32)
    inverse_rms = lax.rsqrt(jnp.mean(values * values, axis=-1, keepdims=True) + epsilon)
    return (values * inverse_rms, inverse_rms)


def key_bias(level_flags, shard_rows):
    position = jnp.arange(shard_rows)
    own_part = position[None, :] <= position[:, None]
    far_part = jnp.repeat(level_flags != 0, shard_rows)
    far_part = jnp.broadcast_to(far_part[None, :], (shard_rows, far_part.shape[0]))
    return jnp.concatenate([own_part, far_part], 1)


def split_heads(row_block):
    return row_block.reshape(row_block.shape[0], -1, HEAD_DIM)


def softmax_keys(queries, key_heads, allowed):
    scores = jnp.einsum(
        "ihd,jhd->hij", queries, key_heads, preferred_element_type=jnp.float32
    ) * HEAD_DIM ** (-0.5)
    scores = jnp.where(allowed[None], scores, negative_fill)
    highest = jnp.max(scores, axis=-1, keepdims=True)
    shifted_exp = jnp.where(allowed[None], jnp.exp(scores - highest), 0.0)
    return shifted_exp / jnp.sum(shifted_exp, axis=-1, keepdims=True)


def attend(query_rows, key_rows, allowed):
    model_width = query_rows.shape[1]
    probability = softmax_keys(
        split_heads(query_rows), split_heads(key_rows[:, :model_width]), allowed
    )
    attended = jnp.einsum(
        "hij,jhd->ihd",
        probability.astype(jnp.bfloat16),
        split_heads(key_rows[:, model_width:]),
        preferred_element_type=jnp.float32,
    )
    return attended.reshape(query_rows.shape).astype(jnp.bfloat16)


def attend_back(query_rows, key_rows, allowed, incoming, attended, w_proj):
    model_width = query_rows.shape[1]
    queries = split_heads(query_rows)
    key_heads = split_heads(key_rows[:, :model_width])
    value_heads = split_heads(key_rows[:, model_width:])
    probability = softmax_keys(queries, key_heads, allowed)
    rounded = probability.astype(jnp.bfloat16)
    upstream = lax.dot_general(
        incoming, w_proj, (((1,), (1,)), ((), ())), preferred_element_type=jnp.float32
    ).astype(jnp.bfloat16)
    up_heads = split_heads(upstream)
    delta = jnp.einsum(
        "ihd,ihd->hi", up_heads.astype(jnp.float32), split_heads(attended).astype(jnp.float32)
    )[..., None]
    prob_grad = jnp.einsum(
        "ihd,jhd->hij", up_heads, value_heads, preferred_element_type=jnp.float32
    )
    score_grad = (probability * (prob_grad - delta)).astype(jnp.bfloat16)
    scale_factor = HEAD_DIM ** (-0.5)
    query_grad = (
        jnp.einsum("hij,jhd->ihd", score_grad, key_heads, preferred_element_type=jnp.float32)
        * scale_factor
    )
    key_grad = (
        jnp.einsum("hij,ihd->jhd", score_grad, queries, preferred_element_type=jnp.float32)
        * scale_factor
    )
    value_grad = jnp.einsum("hij,ihd->jhd", rounded, up_heads, preferred_element_type=jnp.float32)
    return (
        query_grad.reshape(-1, model_width),
        key_grad.reshape(-1, model_width),
        value_grad.reshape(-1, model_width),
    )


def per_device(acts, grad_top, w_in, w_out, offsets):
    sections = lax.axis_size("section")
    shards = lax.axis_size("tm")
    levels = shards.bit_length() - 1
    section_index = lax.axis_index("section")
    micro_count = acts.shape[1]
    shard_rows = acts.shape[2]
    model_width = acts.shape[3]
    w_qkv = w_in[0]
    w_proj = w_out[0]
    level_flags = offsets[0]
    normed, inverse_rms = normalize(acts[0])
    rounded_norm = normed.astype(jnp.bfloat16)
    qkv = jnp.dot(rounded_norm.reshape(-1, model_width), w_qkv, preferred_element_type=jnp.float32)
    qkv = qkv.astype(jnp.bfloat16).reshape(micro_count, shard_rows, 3 * model_width)
    pairs = qkv[..., model_width:]
    far_list = [shifted(pairs, "tm", 2**level) for level in range(levels)]
    key_rows = jnp.concatenate([pairs] + far_list, 1)
    allowed = key_bias(level_flags, shard_rows)
    attended = jnp.stack(
        [
            attend(qkv[index, :, :model_width], key_rows[index], allowed)
            for index in range(micro_count)
        ],
        0,
    )

    def attention_part(incoming, slot):
        query_rows = lax.dynamic_index_in_dim(qkv, slot, 0, False)[:, :model_width]
        slot_keys = lax.dynamic_index_in_dim(key_rows, slot, 0, False)
        slot_attended = lax.dynamic_index_in_dim(attended, slot, 0, False)
        query_grad, key_grad, value_grad = attend_back(
            query_rows, slot_keys, allowed, incoming, slot_attended, w_proj
        )
        owner_sum = jnp.concatenate([key_grad[:shard_rows], value_grad[:shard_rows]], 1)
        far_part = jnp.concatenate([key_grad[shard_rows:], value_grad[shard_rows:]], 1)
        far_part = far_part.astype(jnp.bfloat16).reshape(levels, shard_rows, 2 * model_width)
        return (query_grad, owner_sum, far_part)

    def empty_attention(incoming, slot):
        return (
            jnp.zeros((shard_rows, model_width), jnp.float32),
            jnp.zeros((shard_rows, 2 * model_width), jnp.float32),
            jnp.zeros((levels, shard_rows, 2 * model_width), jnp.bfloat16),
        )

    def norm_part(qkv_grad, incoming, slot):
        norm_grad = lax.dot_general(
            qkv_grad, w_qkv, (((1,), (1,)), ((), ())), preferred_element_type=jnp.float32
        )
        slot_normed = lax.dynamic_index_in_dim(normed, slot, 0, False)
        slot_rms = lax.dynamic_index_in_dim(inverse_rms, slot, 0, False)
        inner = jnp.mean(norm_grad * slot_normed, axis=-1, keepdims=True)
        return (incoming.astype(jnp.float32) + slot_rms * (norm_grad - slot_normed * inner)).astype(
            jnp.bfloat16
        )

    def empty_norm(qkv_grad, incoming, slot):
        return jnp.zeros((shard_rows, model_width), jnp.bfloat16)

    def step(turn, carry):
        received, grad_store, qkv_store, incoming_store = carry
        slot_raw = turn - (sections - 1 - section_index)
        active = (slot_raw >= 0) & (slot_raw < micro_count)
        slot = jnp.clip(slot_raw, 0, micro_count - 1)
        incoming = jnp.where(
            section_index == sections - 1,
            lax.dynamic_index_in_dim(grad_top, slot, 0, False),
            received,
        )
        query_grad, owner_sum, far_part = lax.cond(
            active, attention_part, empty_attention, incoming, slot
        )
        for level in range(levels):
            owner_sum = owner_sum + shifted(far_part[level], "tm", -(2**level)).astype(jnp.float32)
        qkv_grad = jnp.concatenate([query_grad, owner_sum], 1).astype(jnp.bfloat16)
        grad_in = lax.cond(active, norm_part, empty_norm, qkv_grad, incoming, slot)
        sent_down = shifted(grad_in, "section", -1)
        grad_store = jnp.where(
            active, lax.dynamic_update_index_in_dim(grad_store, grad_in, slot, 0), grad_store
        )
        qkv_store = jnp.where(
            active, lax.dynamic_update_index_in_dim(qkv_store, qkv_grad, slot, 0), qkv_store
        )
        incoming_store = jnp.where(
            active,
            lax.dynamic_update_index_in_dim(incoming_store, incoming, slot, 0),
            incoming_store,
        )
        return (sent_down, grad_store, qkv_store, incoming_store)

    initial = (
        jnp.zeros((shard_rows, model_width), jnp.bfloat16),
        jnp.zeros((micro_count, shard_rows, model_width), jnp.bfloat16),
        jnp.zeros((micro_count, shard_rows, 3 * model_width), jnp.bfloat16),
        jnp.zeros((micro_count, shard_rows, model_width), jnp.bfloat16),
    )
    received, grad_store, qkv_store, incoming_store = lax.fori_loop(
        0, sections + micro_count - 1, step, initial
    )
    flat_norm = rounded_norm.reshape(-1, model_width)
    flat_attended = attended.reshape(-1, model_width)
    flat_qkv = qkv_store.reshape(-1, 3 * model_width)
    flat_incoming = incoming_store.reshape(-1, model_width)
    contract = (((0,), (0,)), ((), ()))
    first = lax.dot_general(flat_norm, flat_qkv, contract, preferred_element_type=jnp.float32)
    second = lax.dot_general(
        flat_attended, flat_incoming, contract, preferred_element_type=jnp.float32
    )
    summed = lax.psum_scatter(
        jnp.concatenate([first, second], 1).astype(jnp.bfloat16),
        "tm",
        scatter_dimension=0,
        tiled=True,
    ).astype(jnp.float32)
    return (
        grad_store[None],
        summed[None, :, : 3 * model_width],
        summed[None, :, 3 * model_width :],
    )


def side_by_side(transposed, pair):
    width = 2 * HEAD_DIM
    rows = transposed[pair * width : (pair + 1) * width]
    empty = jnp.zeros((HEAD_DIM, rows.shape[1]), rows.dtype)
    return jnp.concatenate(
        [
            jnp.concatenate([rows[:HEAD_DIM], empty], 0),
            jnp.concatenate([empty, rows[HEAD_DIM:]], 0),
        ],
        1,
    )


def one_above_other(rows, masks):
    return jnp.concatenate([rows * masks[0], rows * masks[1]], 0)


def head_masks():
    lane = lax.broadcasted_iota(jnp.int32, (1, 2 * HEAD_DIM), 1)
    return [
        jnp.where(lane < HEAD_DIM, 1.0, 0.0).astype(jnp.bfloat16),
        jnp.where(lane < HEAD_DIM, 0.0, 1.0).astype(jnp.bfloat16),
    ]


def key_bias_rows(flag_rows, levels, shard_rows, keys, first_query, count):
    key_at = lax.broadcasted_iota(jnp.int32, (keys, count), 0)
    query_at = lax.broadcasted_iota(jnp.int32, (keys, count), 1) + first_query
    gap = lax.div(query_at, shard_rows) - lax.div(key_at, shard_rows)
    allowed = (gap == 0) & (key_at <= query_at)
    for level in range(levels):
        allowed = allowed | ((gap == 2**level) & (flag_rows[level : level + 1] != 0))
    return jnp.where(allowed, 0.0, negative_fill)


def softmax_pass(queries, keys, values, bias, prob_ref, at_ref):
    queries_t = queries.T
    values_t = values.T
    width = 2 * HEAD_DIM
    count = queries.shape[0]
    for pair in range(queries.shape[1] // width):
        at_pair = slice(pair * width, (pair + 1) * width)
        scores = jnp.dot(
            keys[:, at_pair], side_by_side(queries_t, pair), preferred_element_type=jnp.float32
        )
        for half in range(2):
            at_half = slice(half * count, (half + 1) * count)
            biased = scores[:, at_half] + bias
            shifted_exp = jnp.exp(biased - jnp.max(biased, axis=0, keepdims=True))
            probability = shifted_exp * (1.0 / jnp.sum(shifted_exp, axis=0, keepdims=True))
            prob_ref[pair, :, at_half] = probability.astype(jnp.bfloat16)
    for head in range(queries.shape[1] // HEAD_DIM):
        at = slice(head * HEAD_DIM, (head + 1) * HEAD_DIM)
        at_half = slice(head % 2 * count, (head % 2 + 1) * count)
        at_ref[at] = jnp.dot(
            values_t[at], prob_ref[head // 2, :, at_half], preferred_element_type=jnp.float32
        ).astype(jnp.bfloat16)


def pack_kernel(
    levels, info_ref, acts_ref, top_ref, own_ref, other_ref, own_top_ref, other_top_ref, sems
):
    model_width = acts_ref.shape[2]
    shard_rows = own_ref.shape[0]
    side = info_ref[4]
    copies = [
        pltpu.make_async_copy(acts_ref.at[side], own_ref.at[:, :model_width], sems.at[0]),
        pltpu.make_async_copy(acts_ref.at[1 - side], other_ref.at[:, :model_width], sems.at[1]),
        pltpu.make_async_copy(top_ref.at[side], own_top_ref, sems.at[2]),
        pltpu.make_async_copy(top_ref.at[1 - side], other_top_ref, sems.at[3]),
    ]
    for copy in copies:
        copy.start()
    lane = lax.broadcasted_iota(jnp.int32, (shard_rows, own_ref.shape[1] - model_width), 1)
    flags = jnp.zeros(lane.shape, jnp.float32)
    for level in range(levels):
        seen = jnp.where(info_ref[5 + level] != 0, 1.0, 0.0)
        flags = jnp.where(lane == level, seen, flags)
    own_ref[:, model_width:] = flags.astype(jnp.bfloat16)
    other_ref[:, model_width:] = flags.astype(jnp.bfloat16)
    for copy in copies:
        copy.wait()


def touch_kernel(w_ref, after_ref, out_ref):
    out_ref[...] = w_ref[: out_ref.shape[0], : out_ref.shape[1]]


def project_kernel(replicas, info_ref, *refs):
    pieces = refs[: 4 * replicas]
    w_ref, _, normed_ref, rms_ref, norm_ref, flag_ref, q_ref, k_ref, v_ref, kt_ref, packed_ref = refs[
        4 * replicas :
    ]
    shards, shard_rows = packed_ref.shape[:2]
    model_width = w_ref.shape[0]
    seq = shards * shard_rows
    columns = q_ref.shape[1]
    at_piece = 0
    for core in (info_ref[0], 1 - info_ref[0]):
        for side in (info_ref[2], 1 - info_ref[2]):
            for step in range(replicas):
                shard = side * (shards // 2) + place_of(info_ref, step, replicas) + core
                packed_ref[shard] = pieces[at_piece][...]
                at_piece += 1
    for chunk in range(2):
        for step in range(replicas):
            shard = chunk * (shards // 2) + place_of(info_ref, step, replicas) + info_ref[0]
            normed, inverse_rms = normalize(packed_ref[shard][:, :model_width])
            normed_ref[chunk, step] = normed
            rms_ref[chunk, step] = jnp.broadcast_to(inverse_rms, rms_ref.shape[2:])
    normed, _ = normalize(packed_ref[:, :, :model_width].reshape(seq, model_width))
    rounded = normed.astype(jnp.bfloat16)
    norm_ref[...] = rounded
    flag_ref[...] = packed_ref[:, :, model_width:].reshape(seq, -1).astype(jnp.float32).T
    scale_factor = HEAD_DIM ** (-0.5)
    for block, out_ref in enumerate((q_ref, k_ref, v_ref)):
        first = pl.multiple_of(block * model_width + info_ref[0] * columns, 128)
        product = jnp.dot(
            rounded, w_ref[:, pl.ds(first, columns)], preferred_element_type=jnp.float32
        ).astype(jnp.bfloat16)
        out_ref[...] = product * scale_factor if block == 0 else product
    kt_ref[...] = (k_ref[...] * scale_factor).T


def upper_forward_kernel(
    levels, shard_rows, flag_ref, q_ref, k_ref, v_ref, prob_ref, at_ref
):
    seq = q_ref.shape[0]
    count = seq // 2
    bias = key_bias_rows(flag_ref[:, count:], levels, shard_rows, seq, count, count)
    softmax_pass(q_ref[count:], k_ref[...], v_ref[...], bias, prob_ref, at_ref)


def lower_forward_kernel(
    levels,
    shard_rows,
    info_ref,
    norm_ref,
    flag_ref,
    q_ref,
    k_ref,
    v_ref,
    after_ref,
    prob_ref,
    at_ref,
    gt_ref,
):
    seq = norm_ref.shape[0]
    count = seq // 2
    bias = key_bias_rows(flag_ref[:, :count], levels, shard_rows, count, 0, count)
    softmax_pass(q_ref[:count], k_ref[:count], v_ref[:count], bias, prob_ref, at_ref)
    rows = gt_ref.shape[0] // 4
    parity, x, y = info_ref[0], info_ref[1], info_ref[2]
    half = norm_ref.shape[1] // rows // 2
    for place, block in enumerate(
        (
            half * y + 2 * x + 1 - parity,
            half * y + 2 * x + parity,
            half * y + 2 * (1 - x) + 1 - parity,
            half * (1 - y) + 2 * x + parity,
        )
    ):
        first = pl.multiple_of(block * rows, 128)
        gt_ref[place * rows : (place + 1) * rows] = norm_ref[:, pl.ds(first, rows)].T


def place_of(info_ref, step, replicas):
    return 2 * lax.rem(info_ref[1] - step + replicas, replicas)


def merge_rows(info_ref, fresh, got_refs, kept_refs, out_refs, rows_ref):
    @pl.when(fresh)
    def _():
        for core, out_ref in enumerate(out_refs):
            refs = got_refs[core * len(got_refs) // 2 : (core + 1) * len(got_refs) // 2]
            if len(refs) == 1:
                out_ref[...] = refs[0][...]
            else:
                for step, got_ref in enumerate(refs):
                    out_ref[step] = got_ref[...]

    @pl.when(jnp.logical_not(fresh))
    def _():
        for out_ref, kept_ref in zip(out_refs, kept_refs):
            out_ref[...] = kept_ref[...]

    place_rows(info_ref, out_refs, rows_ref)


def place_rows(info_ref, out_refs, rows_ref):
    replicas = out_refs[0].shape[0]
    for step in range(replicas):
        place = place_of(info_ref, step, replicas)
        rows_ref[place + info_ref[0]] = out_refs[0][step]
        rows_ref[place + 1 - info_ref[0]] = out_refs[1][step]


def merge_tops(info_ref, upper, piece_refs, out_refs, rows_ref):
    replicas = out_refs[0].shape[0]
    own_chunk = info_ref[2] == (1 if upper else 0)
    for core in range(2):
        refs = piece_refs[2 * replicas * core : 2 * replicas * (core + 1)]

        @pl.when(own_chunk)
        def _():
            for step in range(replicas):
                out_refs[core][step] = refs[step][...]

        @pl.when(jnp.logical_not(own_chunk))
        def _():
            for step in range(replicas):
                out_refs[core][step] = refs[replicas + step][...]

    place_rows(info_ref, out_refs, rows_ref)


def backward_kernel(upper, tops, replicas, fresh_section, info_ref, *refs):
    refs = list(refs)
    got = tops or (2 * replicas + 2 if upper else 4)
    got_refs = refs[:got]
    w_ref, prob_ref, q_ref, v_ref, kt_ref, at_ref = refs[got : got + 6]
    refs = refs[got + 6 :]
    if not upper:
        key_sum_ref, value_sum_ref, _ = refs[:3]
        refs = refs[3:]
    own_ref, other_ref, keep_ref = refs[:3]
    send_refs = refs[3 : 3 + PIECES[upper]]
    refs = refs[3 + len(send_refs) :]
    if upper:
        key_sum_ref, value_sum_ref = refs[:2]
        refs = refs[2:]
    grads_ref, rows_ref, scores_ref = refs
    shard_rows, model_width = own_ref.shape[1:]
    count = rows_ref.shape[0] * shard_rows
    keys = prob_ref.shape[1]
    parity = info_ref[0]
    columns = q_ref.shape[1]
    width = 2 * HEAD_DIM
    if tops:
        merge_tops(info_ref, upper, got_refs, (own_ref, other_ref), rows_ref)
    else:
        fresh = info_ref[3] == fresh_section
        merge_rows(info_ref, fresh, got_refs[:-2], got_refs[-2:], (own_ref, other_ref), rows_ref)
    rows = rows_ref[...].reshape(count, model_width)
    weights = w_ref[pl.ds(pl.multiple_of(parity * columns, 128), columns), :]
    over_width = (((1,), (1,)), ((), ()))
    upstream = lax.dot_general(
        rows, weights, over_width, preferred_element_type=jnp.float32
    ).astype(jnp.bfloat16)
    upstream_t = upstream.T
    product_t = upstream_t.astype(jnp.float32) * at_ref[...].astype(jnp.float32)
    first_query = keys - count
    masks = head_masks()

    def put(block, pair, part):
        first = block * columns + pair * width
        grads_ref[:, :, first : first + width] = part.astype(jnp.bfloat16).reshape(
            -1, shard_rows, width
        )

    for pair in range(columns // width):
        at_pair = slice(pair * width, (pair + 1) * width)
        prob_grad = jnp.dot(
            v_ref[:keys, at_pair], side_by_side(upstream_t, pair), preferred_element_type=jnp.float32
        )
        for half in range(2):
            at_half = slice(half * count, (half + 1) * count)
            first = pair * width + half * HEAD_DIM
            delta = jnp.sum(product_t[first : first + HEAD_DIM], axis=0, keepdims=True)
            scores_ref[pair, :, at_half] = (
                prob_ref[pair, :, at_half].astype(jnp.float32) * (prob_grad[:, at_half] - delta)
            ).astype(jnp.bfloat16)
        value_grad = jnp.dot(
            prob_ref[pair],
            one_above_other(upstream[:, at_pair], masks),
            preferred_element_type=jnp.float32,
        )
        if upper:
            value_sum_ref[:, at_pair] = value_grad[:first_query]
            value_grad = value_grad[first_query:]
        else:
            value_grad = value_grad + value_sum_ref[:, at_pair]
        put(2, pair, value_grad)
    for pair in range(columns // width):
        at_pair = slice(pair * width, (pair + 1) * width)
        queries = q_ref[first_query : first_query + count, at_pair]
        key_grad = jnp.dot(
            scores_ref[pair], one_above_other(queries, masks), preferred_element_type=jnp.float32
        )
        if upper:
            key_sum_ref[:, at_pair] = key_grad[:first_query]
            key_grad = key_grad[first_query:]
        else:
            key_grad = key_grad + key_sum_ref[:, at_pair]
        put(1, pair, key_grad)
        query_grad = [
            jnp.dot(
                kt_ref[pair * width + half * HEAD_DIM : pair * width + (half + 1) * HEAD_DIM, :keys],
                scores_ref[pair, :, half * count : (half + 1) * count],
                preferred_element_type=jnp.float32,
            )
            for half in range(2)
        ]
        put(0, pair, jnp.concatenate(query_grad, 0).astype(jnp.bfloat16).T)
    for step in range(replicas):
        place = place_of(info_ref, step, replicas)
        keep_ref[step] = grads_ref[place + parity]
        crossing = grads_ref[place + 1 - parity]
        part = crossing.shape[1] // len(send_refs)
        for at, send_ref in enumerate(send_refs):
            send_ref[step] = crossing[:, at * part : (at + 1) * part]


def norm_product(part, w_ref, half):
    columns = part.shape[1] // 3
    model_width = w_ref.shape[0]
    total = jnp.zeros((part.shape[0], model_width), jnp.float32)
    for block in range(3):
        first = pl.multiple_of(block * model_width + half * columns, 128)
        total += lax.dot_general(
            part[:, block * columns : (block + 1) * columns],
            w_ref[:, pl.ds(first, columns)],
            (((1,), (1,)), ((), ())),
            preferred_element_type=jnp.float32,
        )
    return total


def norm_part_kernel(info_ref, keep_ref, w_ref, after_ref, out_ref):
    part = keep_ref[...].reshape(out_ref.shape[0], -1)
    out_ref[...] = norm_product(part, w_ref, info_ref[0])


def norm_kernel(upper, info_ref, keep_ref, normed_ref, rms_ref, incoming_ref, w_ref, *refs):
    got_refs = refs[: PIECES[upper]]
    out_refs = refs[len(got_refs) + 1 :]
    model_width = w_ref.shape[0]
    replicas, shard_rows = incoming_ref.shape[:2]
    rows = replicas * shard_rows
    got = [got_ref[...].reshape(rows, -1) for got_ref in got_refs]
    norm_grad = norm_product(jnp.concatenate(got, 1), w_ref, 1 - info_ref[0])
    norm_grad += (
        keep_ref[...]
        if upper
        else norm_product(keep_ref[...].reshape(rows, -1), w_ref, info_ref[0])
    )
    chunk = 1 if upper else 0
    normed = normed_ref[chunk].reshape(rows, model_width)
    inverse_rms = rms_ref[chunk].reshape(rows, -1)[:, :1]
    inner = jnp.mean(norm_grad * normed, axis=-1, keepdims=True)
    incoming = incoming_ref[...].reshape(rows, model_width).astype(jnp.float32)
    grad_in = incoming + inverse_rms * (norm_grad - normed * inner)
    grad_in = grad_in.astype(jnp.bfloat16).reshape(replicas, shard_rows, model_width)
    if len(out_refs) == 1:
        out_refs[0][...] = grad_in
    else:
        for step, out_ref in enumerate(out_refs):
            out_ref[...] = grad_in[step]


def term_kernel(info_ref, gt_ref, *refs):
    grad_refs, at_refs, row_refs = refs[:2], refs[2:4], refs[4:6]
    own_pass_ref, own_keep_ref, send_pass_ref, send_keep_ref = refs[6:10]
    out_pass_ref, out_keep_ref, out_send_ref = refs[10:]
    rows = own_pass_ref.shape[0]
    width = out_send_ref.shape[1]
    count = row_refs[0].shape[0] * row_refs[0].shape[1]
    parity, x, y = info_ref[0], info_ref[1], info_ref[2]
    for half, (pass_ref, keep_ref) in reversed(
        list(enumerate(((own_pass_ref, own_keep_ref), (send_pass_ref, send_keep_ref))))
    ):
        total = sum(
            jnp.dot(
                gt_ref[2 * half * rows : 2 * (half + 1) * rows, chunk * count : (chunk + 1) * count],
                part_ref[...].reshape(count, -1),
                preferred_element_type=jnp.float32,
            )
            for chunk, part_ref in enumerate(grad_refs)
        )
        pass_ref[...] = total[:rows].astype(pass_ref.dtype)
        keep_ref[...] = total[rows:].astype(keep_ref.dtype)
    sent = jnp.where(parity == y, 2 * (1 - x) + 1 - parity, 2 * x + parity)
    blocks = (sent, 2 * x + 1 - parity, 2 * x + parity)
    total = jnp.zeros((3 * rows, width), jnp.float32)
    for at_ref, part_ref in zip(at_refs, row_refs):
        picked = [at_ref[pl.ds(pl.multiple_of(block * rows, 128), rows)] for block in blocks]
        total += jnp.dot(
            jnp.concatenate(picked, 0),
            part_ref[...].reshape(count, width),
            preferred_element_type=jnp.float32,
        )
    out_send_ref[...] = total[:rows].astype(jnp.bfloat16)
    out_pass_ref[...] = total[rows : 2 * rows]
    out_keep_ref[...] = total[2 * rows :]


def sum_kernel(own_ref, got_ref, out_own_ref, out_got_ref, after_ref, sum_ref):
    columns = own_ref.shape[1]
    sum_ref[:, :columns] = (own_ref[...] + got_ref[...].astype(jnp.float32)).astype(jnp.bfloat16)
    sum_ref[:, columns:] = (out_own_ref[...] + out_got_ref[...].astype(jnp.float32)).astype(
        jnp.bfloat16
    )


def pick_kernel(info_ref, upper_ref, lower_ref, out_ref):
    @pl.when(info_ref[2] == 1)
    def _():
        out_ref[...] = lower_ref[0]

    @pl.when(info_ref[2] != 1)
    def _():
        out_ref[...] = upper_ref[...]


def join_kernel(info_ref, upper_ref, lower_ref, got_ref, out_ref):
    micro = info_ref[4]
    out_ref[0, 1 - micro] = got_ref[...]

    @pl.when(info_ref[2] == 1)
    def _():
        out_ref[0, micro] = upper_ref[...]

    @pl.when(info_ref[2] != 1)
    def _():
        out_ref[0, micro] = lower_ref[0]


def place_kernel(
    info_ref, own_ref, got_ref, out_own_ref, out_got_ref, sibling_ref, d_in_ref, d_out_ref
):
    columns = own_ref.shape[1] // 3
    own = own_ref[...] + got_ref[...].astype(jnp.float32)
    sibling = sibling_ref[:, : 3 * columns].astype(jnp.float32)
    for part, half in ((own, info_ref[0]), (sibling, 1 - info_ref[0])):
        for block in range(3):
            first = pl.multiple_of((2 * block + half) * columns, 128)
            d_in_ref[:, pl.ds(first, columns)] = part[:, block * columns : (block + 1) * columns]
    owner = info_ref[0] == info_ref[2]

    @pl.when(owner)
    def _():
        d_out_ref[...] = out_own_ref[...] + out_got_ref[...].astype(jnp.float32)

    @pl.when(jnp.logical_not(owner))
    def _():
        d_out_ref[...] = sibling_ref[:, 3 * columns :].astype(jnp.float32)


def call(kernel, outs, operands, scratch=(), flops=0, scalars=1, after=None, mebibytes=5, far=0):
    in_specs = [pl.BlockSpec(memory_space=pltpu.SMEM)] * scalars
    in_specs += [pl.BlockSpec(memory_space=pltpu.HBM)] * far
    in_specs += [pl.BlockSpec(memory_space=pltpu.VMEM)] * (len(operands) - scalars - far)
    if after is not None:
        operands = [*operands, after]
        in_specs.append(pl.BlockSpec(memory_space=pl.ANY))
    return pl.pallas_call(
        kernel,
        out_shape=list(outs),
        in_specs=in_specs,
        out_specs=[pl.BlockSpec(memory_space=pltpu.VMEM)] * len(outs),
        scratch_shapes=list(scratch),
        cost_estimate=pl.CostEstimate(flops=1, bytes_accessed=1, transcendentals=0),
        compiler_params=pltpu.CompilerParams(vmem_limit_bytes=mebibytes * 2**20),
    )(*operands)


def by_chips(acts, grad_top, w_in, w_out, offsets):
    half_type, full_type = jnp.bfloat16, jnp.float32
    shape = jax.ShapeDtypeStruct
    sections = lax.axis_size("section")
    shards = lax.axis_size("tm")
    levels = offsets.shape[1]
    half = shards // 2
    replicas = half // 2
    me = lax.axis_index("tm")
    parity = lax.rem(me, 2)
    side = lax.div(me, half)
    micro_count, shard_rows, model_width = acts.shape[1:]
    columns = model_width // 2
    heads = columns // HEAD_DIM
    seq = shards * shard_rows
    count = seq // 2
    w_qkv = w_in[0]
    w_rows = w_out[0]
    beside = lax.div(lax.rem(me, half), 2)
    micro = lax.rem(side + beside, 2)
    info = jnp.stack([parity, beside, side, lax.axis_index("section"), micro])
    info = jnp.concatenate([info.astype(jnp.int32), offsets[0]])

    def swapped(value, bits, chosen=None):
        pairs = [(device, device ^ bits) for device in range(shards)]
        pairs = [pair for pair in pairs if chosen is None or chosen(pair[0])]
        return lax.ppermute(value, "tm", pairs)

    core, near, far = 1, 2, half

    packed = shape((shard_rows, model_width + 128), half_type)
    top_shape = shape((shard_rows, model_width), half_type)
    own_acts, other_acts, own_top, other_top = call(
        functools.partial(pack_kernel, levels),
        [packed, packed, top_shape, top_shape],
        [info, acts[0], grad_top],
        scratch=[pltpu.SemaphoreType.DMA((4,))],
        far=2,
    )
    (touched,) = call(
        touch_kernel, [shape((16, 128), half_type)], [w_qkv], scalars=0, after=own_acts
    )
    pieces = [own_acts, swapped(other_acts, near), swapped(other_acts, far)]
    pieces += [swapped(own_acts, near + far)]
    tops = [own_top, swapped(other_top, near), swapped(other_top, far)]
    tops += [swapped(own_top, near + far)]
    pieces[-1], tops, touched = lax.optimization_barrier((pieces[-1], tops, touched))
    pieces += [swapped(piece, core) for piece in pieces]

    rows_shape = shape((seq, columns), half_type)
    normed, rms, norm, flag_rows, queries, keys, values, keys_t = call(
        functools.partial(project_kernel, replicas),
        [
            shape((2, replicas, shard_rows, model_width), full_type),
            shape((2, replicas, shard_rows, 128), full_type),
            shape((seq, model_width), half_type),
            shape((128, seq), full_type),
            rows_shape,
            rows_shape,
            rows_shape,
            shape((columns, seq), half_type),
        ],
        [info, *pieces, w_qkv],
        scratch=[pltpu.VMEM((shards, *packed.shape), half_type)],
        flops=6 * seq * model_width * columns,
        after=touched,
    )
    tops, _ = lax.optimization_barrier((tuple(tops), keys_t))
    tops = [*tops, *[swapped(piece, core) for piece in tops]]
    pairs = heads // 2
    upper_prob, upper_at = call(
        functools.partial(upper_forward_kernel, levels, shard_rows),
        [
            shape((pairs, seq, 2 * count), half_type),
            shape((columns, count), half_type),
        ],
        [flag_rows, queries, keys, values],
        scalars=0,
        flops=4 * columns * seq * count,
    )
    own_rows = model_width // shards
    probs, attended = {True: upper_prob}, {True: upper_at}
    got, kept = {}, {}
    piece_shape = shape((replicas, shard_rows, model_width), half_type)
    grads_shape = shape((replicas, shard_rows, 3 * columns), half_type)
    sum_shape = shape((count, columns), full_type)
    full_grads = shape((half, shard_rows, 3 * columns), half_type)
    full_rows = shape((half, shard_rows, model_width), half_type)
    term_shape = (own_rows, 3 * columns)
    rows_scratch = pltpu.VMEM(full_rows.shape, half_type)
    grads_scratch = pltpu.VMEM(full_grads.shape, half_type)
    result, full, ordered = {}, {}, {}
    for turn in range(sections):
        last = turn + 1 == sections
        fresh_section = sections - 1 - turn
        sums, parts, crossed = [], {}, {}

        def norm_step(upper, after):
            result[upper] = call(
                functools.partial(norm_kernel, upper),
                [top_shape] * replicas if upper else [piece_shape],
                [info, parts[upper], normed, rms, kept[upper][0], w_qkv, *crossed[upper]],
                after=after,
            )
            if not last:
                hop = [(sections - 1 - turn, sections - 2 - turn)]
                got[upper] = [lax.ppermute(piece, "section", hop) for piece in result[upper]]

        for upper in (True, False):
            rows_in = tops
            if turn:
                before = result[False] if upper else (keep if last else result[True])
                pieces = []
                for piece in got[upper]:
                    piece, before = lax.optimization_barrier((piece, before))
                    pieces.append(piece)
                got[upper] = pieces
                if upper:
                    result[False] = before
                elif last:
                    keep = before
                else:
                    result[True] = before
                others = [swapped(piece, core) for piece in got[upper]]
                rows_in = [*got[upper], *others, *kept[upper]]
            after = None if upper else (parts[True] if last else result[True][-1])
            part = 3 * columns // PIECES[upper]
            cross = [shape((replicas, shard_rows, part), half_type)] * PIECES[upper]
            outs = [piece_shape, piece_shape, grads_shape, *cross]
            outs += [sum_shape, sum_shape] if upper else []
            scratch = []
            if last:
                outs += [full_grads]
            else:
                scratch += [grads_scratch]
            if last:
                outs += [full_rows]
            else:
                scratch += [rows_scratch]
            part_keys = seq if upper else count
            scratch += [pltpu.VMEM((pairs, part_keys, 2 * count), half_type)]
            answer = call(
                functools.partial(
                    backward_kernel, upper, 0 if turn else len(tops), replicas, fresh_section
                ),
                outs,
                [info, *rows_in, w_rows, probs[upper], queries, values, keys_t]
                + [attended[upper], *sums],
                scratch=scratch,
                flops=2 * count * columns * (2 * model_width + 4 * part_keys),
                after=after,
            )
            kept[upper] = tuple(answer[:2])
            keep = answer[2]
            send = answer[3 : 3 + len(cross)]
            parts[upper] = keep
            if upper:
                sums = answer[3 + len(cross) : 5 + len(cross)]
                (parts[True],) = call(
                    norm_part_kernel,
                    [shape((replicas * shard_rows, model_width), full_type)],
                    [info, keep, w_qkv],
                    flops=3 * replicas * shard_rows * model_width * model_width,
                    after=keep,
                )
                if turn == 0:
                    lower_prob, lower_at, norm_t = call(
                        functools.partial(lower_forward_kernel, levels, shard_rows),
                        [
                            shape((pairs, count, 2 * count), half_type),
                            shape((columns, count), half_type),
                            shape((4 * own_rows, seq), half_type),
                        ],
                        [info, norm, flag_rows, queries, keys, values],
                        flops=4 * columns * count * count,
                        after=parts[True],
                    )
                    probs[False], attended[False] = lower_prob, lower_at
            if last:
                full[upper], ordered[upper] = answer[-2:]
            crossed[upper] = [swapped(piece, core) for piece in send]
            if upper and not last:
                norm_step(True, keep)
        if last:
            terms = call(
                term_kernel,
                [shape(term_shape, full_type)] * 2
                + [shape(term_shape, half_type)] * 2
                + [shape((own_rows, model_width), full_type)] * 2
                + [shape((own_rows, model_width), half_type)],
                [info, norm_t, full[False], full[True], attended[False], attended[True]]
                + [ordered[False], ordered[True]],
                flops=2 * own_rows * seq * (12 * columns + 3 * model_width),
                mebibytes=10,
            )
        if last:
            norm_step(True, terms[3])
        norm_step(False, result[True][-1] if not last else terms[3])

    in_pass, in_keep, send_pass, send_keep, out_pass, out_keep, out_send = terms
    got_pass = swapped(send_pass, near)
    got_keep = swapped(send_keep, far)
    own_rows_grad = [result[True][0], result[False][0]]
    (theirs,) = call(pick_kernel, [top_shape], [info, *own_rows_grad])
    partner = swapped(theirs, far)
    out_send, theirs = lax.optimization_barrier((out_send, theirs))
    got_out_pass = swapped(out_send, near, lambda device: device // half == device % 2)
    got_out_keep = swapped(out_send, far, lambda device: device // half != device % 2)
    _, _, done = lax.optimization_barrier((got_keep, got_out_keep, partner))
    (summed,) = call(
        sum_kernel,
        [shape((own_rows, 3 * columns + model_width), half_type)],
        [in_pass, got_pass, out_pass, got_out_pass],
        scalars=0,
        after=done,
    )
    d_w_in, d_w_out = call(
        place_kernel,
        [
            shape((own_rows, 3 * model_width), full_type),
            shape((own_rows, model_width), full_type),
        ],
        [info, in_keep, got_keep, out_keep, got_out_keep, swapped(summed, core)],
    )
    (d_acts,) = call(
        join_kernel, [shape(acts.shape, half_type)], [info, *own_rows_grad, partner]
    )
    return (d_acts, d_w_in[None], d_w_out[None])


def layer_gradients(acts, grad_top, w_in, w_out, offsets):
    shards = lax.axis_size("tm")
    micro_count, shard_rows, model_width = acts.shape[1:]
    heads = model_width // HEAD_DIM
    prob_bytes = 2 * heads * (shards * shard_rows) ** 2
    fits = prob_bytes <= 2**24 and model_width % (128 * shards) == 0 and shard_rows % 16 == 0
    square = shards % 4 == 0 and shards // 4 == 2
    if micro_count == 2 and square and heads % 4 == 0 and fits:
        return by_chips(acts, grad_top, w_in, w_out, offsets)
    return per_device(acts, grad_top, w_in, w_out, offsets)


def solution(mesh):
    placed = (
        P("section", None, "tm", None),
        P(None, "tm", None),
        P("section", None, None),
        P("section", None, None),
        P("tm", None),
    )
    return jax.shard_map(
        layer_gradients,
        mesh=mesh,
        in_specs=placed,
        out_specs=(
            P("section", None, "tm", None),
            P("section", "tm", None),
            P("section", "tm", None),
        ),
        check_vma=False,
    )
```

```python
import functools
import jax
import jax.numpy as jnp
from jax import lax
from jax.experimental import pallas as pl
from jax.experimental.pallas import tpu as pltpu
from jax.sharding import PartitionSpec as P

HEAD_DIM = 64


epsilon = 1e-06
PIECES = {True: 2, False: 4}
negative_fill = -1e30


def shifted(value, axis, steps):
    count = lax.axis_size(axis)
    initial, last = (max(0, -steps), min(count, count - steps))
    return lax.ppermute(value, axis, [(source, source + steps) for source in range(initial, last)])


def normalize(inputs):
    values = inputs.astype(jnp.float32)
    inverse_rms = lax.rsqrt(jnp.mean(values * values, axis=-1, keepdims=True) + epsilon)
    return (values * inverse_rms, inverse_rms)


def key_bias(level_flags, shard_rows):
    position = jnp.arange(shard_rows)
    own_part = position[None, :] <= position[:, None]
    far_part = jnp.repeat(level_flags != 0, shard_rows)
    far_part = jnp.broadcast_to(far_part[None, :], (shard_rows, far_part.shape[0]))
    return jnp.concatenate([own_part, far_part], 1)


def split_heads(row_block):
    return row_block.reshape(row_block.shape[0], -1, HEAD_DIM)


def softmax_keys(queries, key_heads, allowed):
    scores = jnp.einsum(
        "ihd,jhd->hij", queries, key_heads, preferred_element_type=jnp.float32
    ) * HEAD_DIM ** (-0.5)
    scores = jnp.where(allowed[None], scores, negative_fill)
    highest = jnp.max(scores, axis=-1, keepdims=True)
    shifted_exp = jnp.where(allowed[None], jnp.exp(scores - highest), 0.0)
    return shifted_exp / jnp.sum(shifted_exp, axis=-1, keepdims=True)


def attend(query_rows, key_rows, allowed):
    model_width = query_rows.shape[1]
    probability = softmax_keys(
        split_heads(query_rows), split_heads(key_rows[:, :model_width]), allowed
    )
    attended = jnp.einsum(
        "hij,jhd->ihd",
        probability.astype(jnp.bfloat16),
        split_heads(key_rows[:, model_width:]),
        preferred_element_type=jnp.float32,
    )
    return attended.reshape(query_rows.shape).astype(jnp.bfloat16)


def attend_back(query_rows, key_rows, allowed, incoming, attended, w_proj):
    model_width = query_rows.shape[1]
    queries = split_heads(query_rows)
    key_heads = split_heads(key_rows[:, :model_width])
    value_heads = split_heads(key_rows[:, model_width:])
    probability = softmax_keys(queries, key_heads, allowed)
    rounded = probability.astype(jnp.bfloat16)
    upstream = lax.dot_general(
        incoming, w_proj, (((1,), (1,)), ((), ())), preferred_element_type=jnp.float32
    ).astype(jnp.bfloat16)
    up_heads = split_heads(upstream)
    delta = jnp.einsum(
        "ihd,ihd->hi", up_heads.astype(jnp.float32), split_heads(attended).astype(jnp.float32)
    )[..., None]
    prob_grad = jnp.einsum(
        "ihd,jhd->hij", up_heads, value_heads, preferred_element_type=jnp.float32
    )
    score_grad = (probability * (prob_grad - delta)).astype(jnp.bfloat16)
    scale_factor = HEAD_DIM ** (-0.5)
    query_grad = (
        jnp.einsum("hij,jhd->ihd", score_grad, key_heads, preferred_element_type=jnp.float32)
        * scale_factor
    )
    key_grad = (
        jnp.einsum("hij,ihd->jhd", score_grad, queries, preferred_element_type=jnp.float32)
        * scale_factor
    )
    value_grad = jnp.einsum("hij,ihd->jhd", rounded, up_heads, preferred_element_type=jnp.float32)
    return (
        query_grad.reshape(-1, model_width),
        key_grad.reshape(-1, model_width),
        value_grad.reshape(-1, model_width),
    )


def per_device(acts, grad_top, w_in, w_out, offsets):
    sections = lax.axis_size("section")
    shards = lax.axis_size("tm")
    levels = shards.bit_length() - 1
    section_index = lax.axis_index("section")
    micro_count = acts.shape[1]
    shard_rows = acts.shape[2]
    model_width = acts.shape[3]
    w_qkv = w_in[0]
    w_proj = w_out[0]
    level_flags = offsets[0]
    normed, inverse_rms = normalize(acts[0])
    rounded_norm = normed.astype(jnp.bfloat16)
    qkv = jnp.dot(rounded_norm.reshape(-1, model_width), w_qkv, preferred_element_type=jnp.float32)
    qkv = qkv.astype(jnp.bfloat16).reshape(micro_count, shard_rows, 3 * model_width)
    pairs = qkv[..., model_width:]
    far_list = [shifted(pairs, "tm", 2**level) for level in range(levels)]
    key_rows = jnp.concatenate([pairs] + far_list, 1)
    allowed = key_bias(level_flags, shard_rows)
    attended = jnp.stack(
        [
            attend(qkv[index, :, :model_width], key_rows[index], allowed)
            for index in range(micro_count)
        ],
        0,
    )

    def attention_part(incoming, slot):
        query_rows = lax.dynamic_index_in_dim(qkv, slot, 0, False)[:, :model_width]
        slot_keys = lax.dynamic_index_in_dim(key_rows, slot, 0, False)
        slot_attended = lax.dynamic_index_in_dim(attended, slot, 0, False)
        query_grad, key_grad, value_grad = attend_back(
            query_rows, slot_keys, allowed, incoming, slot_attended, w_proj
        )
        owner_sum = jnp.concatenate([key_grad[:shard_rows], value_grad[:shard_rows]], 1)
        far_part = jnp.concatenate([key_grad[shard_rows:], value_grad[shard_rows:]], 1)
        far_part = far_part.astype(jnp.bfloat16).reshape(levels, shard_rows, 2 * model_width)
        return (query_grad, owner_sum, far_part)

    def empty_attention(incoming, slot):
        return (
            jnp.zeros((shard_rows, model_width), jnp.float32),
            jnp.zeros((shard_rows, 2 * model_width), jnp.float32),
            jnp.zeros((levels, shard_rows, 2 * model_width), jnp.bfloat16),
        )

    def norm_part(qkv_grad, incoming, slot):
        norm_grad = lax.dot_general(
            qkv_grad, w_qkv, (((1,), (1,)), ((), ())), preferred_element_type=jnp.float32
        )
        slot_normed = lax.dynamic_index_in_dim(normed, slot, 0, False)
        slot_rms = lax.dynamic_index_in_dim(inverse_rms, slot, 0, False)
        inner = jnp.mean(norm_grad * slot_normed, axis=-1, keepdims=True)
        return (incoming.astype(jnp.float32) + slot_rms * (norm_grad - slot_normed * inner)).astype(
            jnp.bfloat16
        )

    def empty_norm(qkv_grad, incoming, slot):
        return jnp.zeros((shard_rows, model_width), jnp.bfloat16)

    def step(turn, carry):
        received, grad_store, qkv_store, incoming_store = carry
        slot_raw = turn - (sections - 1 - section_index)
        active = (slot_raw >= 0) & (slot_raw < micro_count)
        slot = jnp.clip(slot_raw, 0, micro_count - 1)
        incoming = jnp.where(
            section_index == sections - 1,
            lax.dynamic_index_in_dim(grad_top, slot, 0, False),
            received,
        )
        query_grad, owner_sum, far_part = lax.cond(
            active, attention_part, empty_attention, incoming, slot
        )
        for level in range(levels):
            owner_sum = owner_sum + shifted(far_part[level], "tm", -(2**level)).astype(jnp.float32)
        qkv_grad = jnp.concatenate([query_grad, owner_sum], 1).astype(jnp.bfloat16)
        grad_in = lax.cond(active, norm_part, empty_norm, qkv_grad, incoming, slot)
        sent_down = shifted(grad_in, "section", -1)
        grad_store = jnp.where(
            active, lax.dynamic_update_index_in_dim(grad_store, grad_in, slot, 0), grad_store
        )
        qkv_store = jnp.where(
            active, lax.dynamic_update_index_in_dim(qkv_store, qkv_grad, slot, 0), qkv_store
        )
        incoming_store = jnp.where(
            active,
            lax.dynamic_update_index_in_dim(incoming_store, incoming, slot, 0),
            incoming_store,
        )
        return (sent_down, grad_store, qkv_store, incoming_store)

    initial = (
        jnp.zeros((shard_rows, model_width), jnp.bfloat16),
        jnp.zeros((micro_count, shard_rows, model_width), jnp.bfloat16),
        jnp.zeros((micro_count, shard_rows, 3 * model_width), jnp.bfloat16),
        jnp.zeros((micro_count, shard_rows, model_width), jnp.bfloat16),
    )
    received, grad_store, qkv_store, incoming_store = lax.fori_loop(
        0, sections + micro_count - 1, step, initial
    )
    flat_norm = rounded_norm.reshape(-1, model_width)
    flat_attended = attended.reshape(-1, model_width)
    flat_qkv = qkv_store.reshape(-1, 3 * model_width)
    flat_incoming = incoming_store.reshape(-1, model_width)
    contract = (((0,), (0,)), ((), ()))
    first = lax.dot_general(flat_norm, flat_qkv, contract, preferred_element_type=jnp.float32)
    second = lax.dot_general(
        flat_attended, flat_incoming, contract, preferred_element_type=jnp.float32
    )
    summed = lax.psum_scatter(
        jnp.concatenate([first, second], 1).astype(jnp.bfloat16),
        "tm",
        scatter_dimension=0,
        tiled=True,
    ).astype(jnp.float32)
    return (
        grad_store[None],
        summed[None, :, : 3 * model_width],
        summed[None, :, 3 * model_width :],
    )


def side_by_side(transposed, pair):
    width = 2 * HEAD_DIM
    rows = transposed[pair * width : (pair + 1) * width]
    empty = jnp.zeros((HEAD_DIM, rows.shape[1]), rows.dtype)
    return jnp.concatenate(
        [
            jnp.concatenate([rows[:HEAD_DIM], empty], 0),
            jnp.concatenate([empty, rows[HEAD_DIM:]], 0),
        ],
        1,
    )


def one_above_other(rows, masks):
    return jnp.concatenate([rows * masks[0], rows * masks[1]], 0)


def head_masks():
    lane = lax.broadcasted_iota(jnp.int32, (1, 2 * HEAD_DIM), 1)
    return [
        jnp.where(lane < HEAD_DIM, 1.0, 0.0).astype(jnp.bfloat16),
        jnp.where(lane < HEAD_DIM, 0.0, 1.0).astype(jnp.bfloat16),
    ]


def key_bias_rows(flag_rows, levels, shard_rows, keys, first_query, count):
    key_at = lax.broadcasted_iota(jnp.int32, (keys, count), 0)
    query_at = lax.broadcasted_iota(jnp.int32, (keys, count), 1) + first_query
    gap = lax.div(query_at, shard_rows) - lax.div(key_at, shard_rows)
    allowed = (gap == 0) & (key_at <= query_at)
    for level in range(levels):
        allowed = allowed | ((gap == 2**level) & (flag_rows[level : level + 1] != 0))
    return jnp.where(allowed, 0.0, negative_fill)


def softmax_pass(queries, keys, values, bias, prob_ref, at_ref):
    queries_t = queries.T
    values_t = values.T
    width = 2 * HEAD_DIM
    count = queries.shape[0]
    for pair in range(queries.shape[1] // width):
        at_pair = slice(pair * width, (pair + 1) * width)
        scores = jnp.dot(
            keys[:, at_pair], side_by_side(queries_t, pair), preferred_element_type=jnp.float32
        )
        for half in range(2):
            at_half = slice(half * count, (half + 1) * count)
            biased = scores[:, at_half] + bias
            shifted_exp = jnp.exp(biased - jnp.max(biased, axis=0, keepdims=True))
            probability = shifted_exp * (1.0 / jnp.sum(shifted_exp, axis=0, keepdims=True))
            prob_ref[pair, :, at_half] = probability.astype(jnp.bfloat16)
    for head in range(queries.shape[1] // HEAD_DIM):
        at = slice(head * HEAD_DIM, (head + 1) * HEAD_DIM)
        at_half = slice(head % 2 * count, (head % 2 + 1) * count)
        at_ref[at] = jnp.dot(
            values_t[at], prob_ref[head // 2, :, at_half], preferred_element_type=jnp.float32
        ).astype(jnp.bfloat16)


def pack_kernel(
    levels, info_ref, acts_ref, top_ref, own_ref, other_ref, own_top_ref, other_top_ref, sems
):
    model_width = acts_ref.shape[2]
    shard_rows = own_ref.shape[0]
    side = info_ref[4]
    copies = [
        pltpu.make_async_copy(acts_ref.at[side], own_ref.at[:, :model_width], sems.at[0]),
        pltpu.make_async_copy(acts_ref.at[1 - side], other_ref.at[:, :model_width], sems.at[1]),
        pltpu.make_async_copy(top_ref.at[side], own_top_ref, sems.at[2]),
        pltpu.make_async_copy(top_ref.at[1 - side], other_top_ref, sems.at[3]),
    ]
    for copy in copies:
        copy.start()
    lane = lax.broadcasted_iota(jnp.int32, (shard_rows, own_ref.shape[1] - model_width), 1)
    flags = jnp.zeros(lane.shape, jnp.float32)
    for level in range(levels):
        seen = jnp.where(info_ref[5 + level] != 0, 1.0, 0.0)
        flags = jnp.where(lane == level, seen, flags)
    own_ref[:, model_width:] = flags.astype(jnp.bfloat16)
    other_ref[:, model_width:] = flags.astype(jnp.bfloat16)
    for copy in copies:
        copy.wait()


def touch_kernel(w_ref, after_ref, out_ref):
    out_ref[...] = w_ref[: out_ref.shape[0], : out_ref.shape[1]]


def project_kernel(replicas, info_ref, *refs):
    pieces = refs[: 4 * replicas]
    w_ref, _, normed_ref, rms_ref, norm_ref, flag_ref, q_ref, k_ref, v_ref, kt_ref, packed_ref = refs[
        4 * replicas :
    ]
    shards, shard_rows = packed_ref.shape[:2]
    model_width = w_ref.shape[0]
    seq = shards * shard_rows
    columns = q_ref.shape[1]
    at_piece = 0
    for core in (info_ref[0], 1 - info_ref[0]):
        for side in (info_ref[2], 1 - info_ref[2]):
            for step in range(replicas):
                shard = side * (shards // 2) + place_of(info_ref, step, replicas) + core
                packed_ref[shard] = pieces[at_piece][...]
                at_piece += 1
    for chunk in range(2):
        for step in range(replicas):
            shard = chunk * (shards // 2) + place_of(info_ref, step, replicas) + info_ref[0]
            normed, inverse_rms = normalize(packed_ref[shard][:, :model_width])
            normed_ref[chunk, step] = normed
            rms_ref[chunk, step] = jnp.broadcast_to(inverse_rms, rms_ref.shape[2:])
    normed, _ = normalize(packed_ref[:, :, :model_width].reshape(seq, model_width))
    rounded = normed.astype(jnp.bfloat16)
    norm_ref[...] = rounded
    flag_ref[...] = packed_ref[:, :, model_width:].reshape(seq, -1).astype(jnp.float32).T
    scale_factor = HEAD_DIM ** (-0.5)
    for block, out_ref in enumerate((q_ref, k_ref, v_ref)):
        first = pl.multiple_of(block * model_width + info_ref[0] * columns, 128)
        product = jnp.dot(
            rounded, w_ref[:, pl.ds(first, columns)], preferred_element_type=jnp.float32
        ).astype(jnp.bfloat16)
        out_ref[...] = product * scale_factor if block == 0 else product
    kt_ref[...] = (k_ref[...] * scale_factor).T


def upper_forward_kernel(
    levels, shard_rows, flag_ref, q_ref, k_ref, v_ref, prob_ref, at_ref
):
    seq = q_ref.shape[0]
    count = seq // 2
    bias = key_bias_rows(flag_ref[:, count:], levels, shard_rows, seq, count, count)
    softmax_pass(q_ref[count:], k_ref[...], v_ref[...], bias, prob_ref, at_ref)


def lower_forward_kernel(
    levels,
    shard_rows,
    info_ref,
    norm_ref,
    flag_ref,
    q_ref,
    k_ref,
    v_ref,
    after_ref,
    prob_ref,
    at_ref,
    gt_ref,
):
    seq = norm_ref.shape[0]
    count = seq // 2
    bias = key_bias_rows(flag_ref[:, :count], levels, shard_rows, count, 0, count)
    softmax_pass(q_ref[:count], k_ref[:count], v_ref[:count], bias, prob_ref, at_ref)
    rows = gt_ref.shape[0] // 4
    parity, x, y = info_ref[0], info_ref[1], info_ref[2]
    half = norm_ref.shape[1] // rows // 2
    for place, block in enumerate(
        (
            half * y + 2 * x + 1 - parity,
            half * y + 2 * x + parity,
            half * y + 2 * (1 - x) + 1 - parity,
            half * (1 - y) + 2 * x + parity,
        )
    ):
        first = pl.multiple_of(block * rows, 128)
        gt_ref[place * rows : (place + 1) * rows] = norm_ref[:, pl.ds(first, rows)].T


def place_of(info_ref, step, replicas):
    return 2 * lax.rem(info_ref[1] - step + replicas, replicas)


def merge_rows(info_ref, fresh, got_refs, kept_refs, out_refs, rows_ref):
    @pl.when(fresh)
    def _():
        for core, out_ref in enumerate(out_refs):
            out_ref[...] = got_refs[core][...]

    @pl.when(jnp.logical_not(fresh))
    def _():
        for out_ref, kept_ref in zip(out_refs, kept_refs):
            out_ref[...] = kept_ref[...]

    place_rows(info_ref, out_refs, rows_ref)


def place_rows(info_ref, out_refs, rows_ref):
    replicas = out_refs[0].shape[0]
    for step in range(replicas):
        place = place_of(info_ref, step, replicas)
        rows_ref[place + info_ref[0]] = out_refs[0][step]
        rows_ref[place + 1 - info_ref[0]] = out_refs[1][step]


def merge_tops(info_ref, upper, piece_refs, out_refs, rows_ref):
    replicas = out_refs[0].shape[0]
    own_chunk = info_ref[2] == (1 if upper else 0)
    for core in range(2):
        refs = piece_refs[2 * replicas * core : 2 * replicas * (core + 1)]

        @pl.when(own_chunk)
        def _():
            for step in range(replicas):
                out_refs[core][step] = refs[step][...]

        @pl.when(jnp.logical_not(own_chunk))
        def _():
            for step in range(replicas):
                out_refs[core][step] = refs[replicas + step][...]

    place_rows(info_ref, out_refs, rows_ref)


def backward_kernel(upper, tops, fresh_section, info_ref, *refs):
    refs = list(refs)
    got = tops or 4
    got_refs = refs[:got]
    w_ref, prob_ref, q_ref, v_ref, kt_ref, at_ref = refs[got : got + 6]
    refs = refs[got + 6 :]
    if not upper:
        key_sum_ref, value_sum_ref = refs[:2]
        refs = refs[2:]
    refs = refs[1:]
    own_ref, other_ref, keep_ref = refs[:3]
    send_refs = refs[3 : 3 + PIECES[upper]]
    refs = refs[3 + len(send_refs) :]
    if upper:
        key_sum_ref, value_sum_ref = refs[:2]
        refs = refs[2:]
    grads_ref, rows_ref, scores_ref = refs
    replicas, shard_rows, model_width = own_ref.shape
    count = rows_ref.shape[0] * shard_rows
    keys = prob_ref.shape[1]
    parity = info_ref[0]
    columns = q_ref.shape[1]
    width = 2 * HEAD_DIM
    if tops:
        merge_tops(info_ref, upper, got_refs, (own_ref, other_ref), rows_ref)
    else:
        fresh = info_ref[3] == fresh_section
        merge_rows(info_ref, fresh, got_refs[:-2], got_refs[-2:], (own_ref, other_ref), rows_ref)
    rows = rows_ref[...].reshape(count, model_width)
    weights = w_ref[pl.ds(pl.multiple_of(parity * columns, 128), columns), :]
    over_width = (((1,), (1,)), ((), ()))
    upstream = lax.dot_general(
        rows, weights, over_width, preferred_element_type=jnp.float32
    ).astype(jnp.bfloat16)
    upstream_t = upstream.T
    product_t = upstream_t.astype(jnp.float32) * at_ref[...].astype(jnp.float32)
    first_query = keys - count
    masks = head_masks()

    def put(block, pair, part):
        first = block * columns + pair * width
        grads_ref[:, :, first : first + width] = part.astype(jnp.bfloat16).reshape(
            -1, shard_rows, width
        )

    for pair in range(columns // width):
        at_pair = slice(pair * width, (pair + 1) * width)
        prob_grad = jnp.dot(
            v_ref[:keys, at_pair], side_by_side(upstream_t, pair), preferred_element_type=jnp.float32
        )
        for half in range(2):
            at_half = slice(half * count, (half + 1) * count)
            first = pair * width + half * HEAD_DIM
            delta = jnp.sum(product_t[first : first + HEAD_DIM], axis=0, keepdims=True)
            scores_ref[pair, :, at_half] = (
                prob_ref[pair, :, at_half].astype(jnp.float32) * (prob_grad[:, at_half] - delta)
            ).astype(jnp.bfloat16)
        value_grad = jnp.dot(
            prob_ref[pair],
            one_above_other(upstream[:, at_pair], masks),
            preferred_element_type=jnp.float32,
        )
        if upper:
            value_sum_ref[:, at_pair] = value_grad[:first_query]
            value_grad = value_grad[first_query:]
        else:
            value_grad = value_grad + value_sum_ref[:, at_pair]
        put(2, pair, value_grad)
    for pair in range(columns // width):
        at_pair = slice(pair * width, (pair + 1) * width)
        queries = q_ref[first_query : first_query + count, at_pair]
        key_grad = jnp.dot(
            scores_ref[pair], one_above_other(queries, masks), preferred_element_type=jnp.float32
        )
        if upper:
            key_sum_ref[:, at_pair] = key_grad[:first_query]
            key_grad = key_grad[first_query:]
        else:
            key_grad = key_grad + key_sum_ref[:, at_pair]
        put(1, pair, key_grad)
        query_grad = [
            jnp.dot(
                kt_ref[pair * width + half * HEAD_DIM : pair * width + (half + 1) * HEAD_DIM, :keys],
                scores_ref[pair, :, half * count : (half + 1) * count],
                preferred_element_type=jnp.float32,
            )
            for half in range(2)
        ]
        put(0, pair, jnp.concatenate(query_grad, 0).astype(jnp.bfloat16).T)
    for step in range(replicas):
        place = place_of(info_ref, step, replicas)
        keep_ref[step] = grads_ref[place + parity]
        crossing = grads_ref[place + 1 - parity]
        part = crossing.shape[1] // len(send_refs)
        for at, send_ref in enumerate(send_refs):
            send_ref[step] = crossing[:, at * part : (at + 1) * part]


def norm_product(part, w_ref, half):
    columns = part.shape[1] // 3
    model_width = w_ref.shape[0]
    total = jnp.zeros((part.shape[0], model_width), jnp.float32)
    for block in range(3):
        first = pl.multiple_of(block * model_width + half * columns, 128)
        total += lax.dot_general(
            part[:, block * columns : (block + 1) * columns],
            w_ref[:, pl.ds(first, columns)],
            (((1,), (1,)), ((), ())),
            preferred_element_type=jnp.float32,
        )
    return total


def norm_part_kernel(info_ref, keep_ref, w_ref, after_ref, out_ref):
    part = keep_ref[...].reshape(out_ref.shape[0], -1)
    out_ref[...] = norm_product(part, w_ref, info_ref[0])


def norm_kernel(upper, info_ref, keep_ref, normed_ref, rms_ref, incoming_ref, w_ref, *refs):
    got_refs = refs[: PIECES[upper]]
    out_refs = refs[len(got_refs) :]
    model_width = w_ref.shape[0]
    replicas, shard_rows = incoming_ref.shape[:2]
    rows = replicas * shard_rows
    got = [got_ref[...].reshape(rows, -1) for got_ref in got_refs]
    norm_grad = norm_product(jnp.concatenate(got, 1), w_ref, 1 - info_ref[0])
    norm_grad += (
        keep_ref[...]
        if upper
        else norm_product(keep_ref[...].reshape(rows, -1), w_ref, info_ref[0])
    )
    chunk = 1 if upper else 0
    normed = normed_ref[chunk].reshape(rows, model_width)
    inverse_rms = rms_ref[chunk].reshape(rows, -1)[:, :1]
    inner = jnp.mean(norm_grad * normed, axis=-1, keepdims=True)
    incoming = incoming_ref[...].reshape(rows, model_width).astype(jnp.float32)
    grad_in = incoming + inverse_rms * (norm_grad - normed * inner)
    grad_in = grad_in.astype(jnp.bfloat16).reshape(replicas, shard_rows, model_width)
    out_refs[-1][...] = grad_in


def term_kernel(info_ref, gt_ref, *refs):
    grad_refs, at_refs, row_refs = refs[:2], refs[2:4], refs[4:6]
    own_pass_ref, own_keep_ref, send_pass_ref, send_keep_ref = refs[6:10]
    out_pass_ref, out_keep_ref, out_send_ref = refs[10:]
    rows = own_pass_ref.shape[0]
    width = out_send_ref.shape[1]
    count = row_refs[0].shape[0] * row_refs[0].shape[1]
    parity, x, y = info_ref[0], info_ref[1], info_ref[2]
    for half, (pass_ref, keep_ref) in reversed(
        list(enumerate(((own_pass_ref, own_keep_ref), (send_pass_ref, send_keep_ref))))
    ):
        total = sum(
            jnp.dot(
                gt_ref[2 * half * rows : 2 * (half + 1) * rows, chunk * count : (chunk + 1) * count],
                part_ref[...].reshape(count, -1),
                preferred_element_type=jnp.float32,
            )
            for chunk, part_ref in enumerate(grad_refs)
        )
        pass_ref[...] = total[:rows].astype(pass_ref.dtype)
        keep_ref[...] = total[rows:].astype(keep_ref.dtype)
    sent = jnp.where(parity == y, 2 * (1 - x) + 1 - parity, 2 * x + parity)
    blocks = (sent, 2 * x + 1 - parity, 2 * x + parity)
    total = jnp.zeros((3 * rows, width), jnp.float32)
    for at_ref, part_ref in zip(at_refs, row_refs):
        picked = [at_ref[pl.ds(pl.multiple_of(block * rows, 128), rows)] for block in blocks]
        total += jnp.dot(
            jnp.concatenate(picked, 0),
            part_ref[...].reshape(count, width),
            preferred_element_type=jnp.float32,
        )
    out_send_ref[...] = total[:rows].astype(jnp.bfloat16)
    out_pass_ref[...] = total[rows : 2 * rows]
    out_keep_ref[...] = total[2 * rows :]


def sum_kernel(own_ref, got_ref, out_own_ref, out_got_ref, after_ref, sum_ref):
    columns = own_ref.shape[1]
    sum_ref[:, :columns] = (own_ref[...] + got_ref[...].astype(jnp.float32)).astype(jnp.bfloat16)
    sum_ref[:, columns:] = (out_own_ref[...] + out_got_ref[...].astype(jnp.float32)).astype(
        jnp.bfloat16
    )


def pick_kernel(info_ref, upper_ref, lower_ref, out_ref):
    crossing = info_ref[0] == 0
    for step in range(2):
        for chunk, part_ref in enumerate((lower_ref, upper_ref)):
            wanted = info_ref[2] == (chunk if step == 1 else 1 - chunk)

            @pl.when(wanted & (crossing if step == 1 else jnp.logical_not(crossing)))
            def _():
                out_ref[...] = part_ref[step]


def join_kernel(info_ref, upper_ref, lower_ref, got_ref, out_ref):
    micro = info_ref[4]
    out_ref[0, 1 - micro] = got_ref[...]

    @pl.when(info_ref[2] == 1)
    def _():
        out_ref[0, micro] = upper_ref[0]

    @pl.when(info_ref[2] != 1)
    def _():
        out_ref[0, micro] = lower_ref[0]


def place_kernel(
    info_ref, own_ref, got_ref, out_own_ref, out_got_ref, sibling_ref, d_in_ref, d_out_ref
):
    columns = own_ref.shape[1] // 3
    own = own_ref[...] + got_ref[...].astype(jnp.float32)
    sibling = sibling_ref[:, : 3 * columns].astype(jnp.float32)
    for part, half in ((own, info_ref[0]), (sibling, 1 - info_ref[0])):
        for block in range(3):
            first = pl.multiple_of((2 * block + half) * columns, 128)
            d_in_ref[:, pl.ds(first, columns)] = part[:, block * columns : (block + 1) * columns]
    owner = info_ref[0] == info_ref[2]

    @pl.when(owner)
    def _():
        d_out_ref[...] = out_own_ref[...] + out_got_ref[...].astype(jnp.float32)

    @pl.when(jnp.logical_not(owner))
    def _():
        d_out_ref[...] = sibling_ref[:, 3 * columns :].astype(jnp.float32)


def call(kernel, outs, operands, scratch=(), flops=0, scalars=1, after=None, mebibytes=5, far=0):
    in_specs = [pl.BlockSpec(memory_space=pltpu.SMEM)] * scalars
    in_specs += [pl.BlockSpec(memory_space=pltpu.HBM)] * far
    in_specs += [pl.BlockSpec(memory_space=pltpu.VMEM)] * (len(operands) - scalars - far)
    if after is not None:
        operands = [*operands, after]
        in_specs.append(pl.BlockSpec(memory_space=pl.ANY))
    return pl.pallas_call(
        kernel,
        out_shape=list(outs),
        in_specs=in_specs,
        out_specs=[pl.BlockSpec(memory_space=pltpu.VMEM)] * len(outs),
        scratch_shapes=list(scratch),
        cost_estimate=pl.CostEstimate(flops=1, bytes_accessed=1, transcendentals=0),
        compiler_params=pltpu.CompilerParams(vmem_limit_bytes=mebibytes * 2**20),
    )(*operands)


def by_chips(acts, grad_top, w_in, w_out, offsets):
    half_type, full_type = jnp.bfloat16, jnp.float32
    shape = jax.ShapeDtypeStruct
    sections = lax.axis_size("section")
    shards = lax.axis_size("tm")
    levels = offsets.shape[1]
    half = shards // 2
    replicas = half // 2
    me = lax.axis_index("tm")
    parity = lax.rem(me, 2)
    side = lax.div(me, half)
    micro_count, shard_rows, model_width = acts.shape[1:]
    columns = model_width // 2
    heads = columns // HEAD_DIM
    seq = shards * shard_rows
    count = seq // 2
    w_qkv = w_in[0]
    w_rows = w_out[0]
    beside = lax.div(lax.rem(me, half), 2)
    micro = lax.rem(side + beside, 2)
    info = jnp.stack([parity, beside, side, lax.axis_index("section"), micro])
    info = jnp.concatenate([info.astype(jnp.int32), offsets[0]])

    def swapped(value, bits, chosen=None):
        pairs = [(device, device ^ bits) for device in range(shards)]
        pairs = [pair for pair in pairs if chosen is None or chosen(pair[0])]
        return lax.ppermute(value, "tm", pairs)

    core, near, far = 1, 2, half

    packed = shape((shard_rows, model_width + 128), half_type)
    top_shape = shape((shard_rows, model_width), half_type)
    own_acts, other_acts, own_top, other_top = call(
        functools.partial(pack_kernel, levels),
        [packed, packed, top_shape, top_shape],
        [info, acts[0], grad_top],
        scratch=[pltpu.SemaphoreType.DMA((4,))],
        far=2,
    )
    (touched,) = call(
        touch_kernel, [shape((16, 128), half_type)], [w_qkv], scalars=0, after=own_acts
    )
    pieces = [own_acts, swapped(other_acts, near), swapped(other_acts, far)]
    pieces += [swapped(own_acts, near + far)]
    tops = [own_top, swapped(other_top, near), swapped(other_top, far)]
    pieces[-1], tops, touched = lax.optimization_barrier((pieces[-1], tops, touched))
    tops += [swapped(own_top, near + far)]
    pieces += [swapped(piece, core) for piece in pieces]

    rows_shape = shape((seq, columns), half_type)
    normed, rms, norm, flag_rows, queries, keys, values, keys_t = call(
        functools.partial(project_kernel, replicas),
        [
            shape((2, replicas, shard_rows, model_width), full_type),
            shape((2, replicas, shard_rows, 128), full_type),
            shape((seq, model_width), half_type),
            shape((128, seq), full_type),
            rows_shape,
            rows_shape,
            rows_shape,
            shape((columns, seq), half_type),
        ],
        [info, *pieces, w_qkv],
        scratch=[pltpu.VMEM((shards, *packed.shape), half_type)],
        flops=6 * seq * model_width * columns,
        after=touched,
    )
    tops, _ = lax.optimization_barrier((tuple(tops), keys_t))
    tops = [*tops, *[swapped(piece, core) for piece in tops]]
    pairs = heads // 2
    upper_prob, upper_at = call(
        functools.partial(upper_forward_kernel, levels, shard_rows),
        [
            shape((pairs, seq, 2 * count), half_type),
            shape((columns, count), half_type),
        ],
        [flag_rows, queries, keys, values],
        scalars=0,
        flops=4 * columns * seq * count,
    )
    own_rows = model_width // shards
    probs, attended = {True: upper_prob}, {True: upper_at}
    got, kept = {}, {}
    piece_shape = shape((replicas, shard_rows, model_width), half_type)
    grads_shape = shape((replicas, shard_rows, 3 * columns), half_type)
    sum_shape = shape((count, columns), full_type)
    full_grads = shape((half, shard_rows, 3 * columns), half_type)
    full_rows = shape((half, shard_rows, model_width), half_type)
    term_shape = (own_rows, 3 * columns)
    rows_scratch = pltpu.VMEM(full_rows.shape, half_type)
    grads_scratch = pltpu.VMEM(full_grads.shape, half_type)
    result, full, ordered = {}, {}, {}
    for turn in range(sections):
        last = turn + 1 == sections
        fresh_section = sections - 1 - turn
        sums, parts, crossed = [], {}, {}

        def norm_step(upper, after):
            (result[upper],) = call(
                functools.partial(norm_kernel, upper),
                [piece_shape],
                [info, parts[upper], normed, rms, kept[upper][0], w_qkv, *crossed[upper]],
                after=after,
            )
            if not last:
                hop = [(sections - 1 - turn, sections - 2 - turn)]
                got[upper] = lax.ppermute(result[upper], "section", hop)

        for upper in (True, False):
            rows_in, after = tops, keys_t if upper else result.get(True)
            if turn:
                before = result[False] if upper else (parts[True] if last else result[True])
                got[upper], after = lax.optimization_barrier((got[upper], before))
                if not upper and last:
                    parts[True] = after
                elif not upper:
                    result[True] = after
                rows_in = [got[upper], swapped(got[upper], core), *kept[upper]]
            part = 3 * columns // PIECES[upper]
            cross = [shape((replicas, shard_rows, part), half_type)] * PIECES[upper]
            outs = [piece_shape, piece_shape, grads_shape, *cross]
            outs += [sum_shape, sum_shape] if upper else []
            scratch = []
            if last:
                outs += [full_grads]
            else:
                scratch += [grads_scratch]
            if last:
                outs += [full_rows]
            else:
                scratch += [rows_scratch]
            part_keys = seq if upper else count
            scratch += [pltpu.VMEM((pairs, part_keys, 2 * count), half_type)]
            answer = call(
                functools.partial(
                    backward_kernel, upper, 0 if turn else len(tops), fresh_section
                ),
                outs,
                [info, *rows_in, w_rows, probs[upper], queries, values, keys_t]
                + [attended[upper], *sums],
                scratch=scratch,
                flops=2 * count * columns * (2 * model_width + 4 * part_keys),
                after=after,
            )
            kept[upper] = tuple(answer[:2])
            keep = answer[2]
            send = answer[3 : 3 + len(cross)]
            parts[upper] = keep
            if upper:
                sums = answer[3 + len(cross) : 5 + len(cross)]
                (parts[True],) = call(
                    norm_part_kernel,
                    [shape((replicas * shard_rows, model_width), full_type)],
                    [info, keep, w_qkv],
                    flops=3 * replicas * shard_rows * model_width * model_width,
                    after=keep,
                )
                if turn == 0:
                    lower_prob, lower_at, norm_t = call(
                        functools.partial(lower_forward_kernel, levels, shard_rows),
                        [
                            shape((pairs, count, 2 * count), half_type),
                            shape((columns, count), half_type),
                            shape((4 * own_rows, seq), half_type),
                        ],
                        [info, norm, flag_rows, queries, keys, values],
                        flops=4 * columns * count * count,
                        after=parts[True],
                    )
                    probs[False], attended[False] = lower_prob, lower_at
            if last:
                full[upper], ordered[upper] = answer[-2:]
            crossed[upper] = [swapped(piece, core) for piece in send]
            if upper and not last:
                norm_step(True, keep)
        if last:
            terms = call(
                term_kernel,
                [shape(term_shape, full_type)] * 2
                + [shape(term_shape, half_type)] * 2
                + [shape((own_rows, model_width), full_type)] * 2
                + [shape((own_rows, model_width), half_type)],
                [info, norm_t, full[False], full[True], attended[False], attended[True]]
                + [ordered[False], ordered[True]],
                flops=2 * own_rows * seq * (12 * columns + 3 * model_width),
                mebibytes=10,
            )
        if last:
            norm_step(True, terms[3])
        norm_step(False, terms[3] if last else result[True])

    in_pass, in_keep, send_pass, send_keep, out_pass, out_keep, out_send = terms
    got_pass = swapped(send_pass, near)
    got_keep = swapped(send_keep, far)
    own_rows_grad = [result[True], result[False]]
    (theirs,) = call(pick_kernel, [top_shape], [info, *own_rows_grad])
    to_owner = [(device, device ^ (far if device % 2 else near)) for device in range(shards)]
    partner = lax.ppermute(theirs, "tm", to_owner)
    got_out_pass = swapped(out_send, near, lambda device: device // half == device % 2)
    got_out_keep = swapped(out_send, far, lambda device: device // half != device % 2)
    _, _, done = lax.optimization_barrier((got_keep, got_out_keep, partner))
    (summed,) = call(
        sum_kernel,
        [shape((own_rows, 3 * columns + model_width), half_type)],
        [in_pass, got_pass, out_pass, got_out_pass],
        scalars=0,
        after=done,
    )
    d_w_in, d_w_out = call(
        place_kernel,
        [
            shape((own_rows, 3 * model_width), full_type),
            shape((own_rows, model_width), full_type),
        ],
        [info, in_keep, got_keep, out_keep, got_out_keep, swapped(summed, core)],
    )
    (d_acts,) = call(
        join_kernel, [shape(acts.shape, half_type)], [info, *own_rows_grad, partner]
    )
    return (d_acts, d_w_in[None], d_w_out[None])


def layer_gradients(acts, grad_top, w_in, w_out, offsets):
    shards = lax.axis_size("tm")
    micro_count, shard_rows, model_width = acts.shape[1:]
    heads = model_width // HEAD_DIM
    prob_bytes = 2 * heads * (shards * shard_rows) ** 2
    fits = prob_bytes <= 2**24 and model_width % (128 * shards) == 0 and shard_rows % 16 == 0
    square = shards % 4 == 0 and shards // 4 == 2
    if micro_count == 2 and square and heads % 4 == 0 and fits:
        return by_chips(acts, grad_top, w_in, w_out, offsets)
    return per_device(acts, grad_top, w_in, w_out, offsets)


def solution(mesh):
    placed = (
        P("section", None, "tm", None),
        P(None, "tm", None),
        P("section", None, None),
        P("section", None, None),
        P("tm", None),
    )
    return jax.shard_map(
        layer_gradients,
        mesh=mesh,
        in_specs=placed,
        out_specs=(
            P("section", None, "tm", None),
            P("section", "tm", None),
            P("section", "tm", None),
        ),
        check_vma=False,
    )
```

```python
import functools
import jax
import jax.numpy as jnp
from jax import lax
from jax.experimental import pallas as pl
from jax.experimental.pallas import tpu as pltpu
from jax.sharding import PartitionSpec as P

HEAD_DIM = 64


epsilon = 1e-06
PIECES = {True: 2, False: 2}
negative_fill = -1e30


def shifted(value, axis, steps):
    count = lax.axis_size(axis)
    initial, last = (max(0, -steps), min(count, count - steps))
    return lax.ppermute(value, axis, [(source, source + steps) for source in range(initial, last)])


def normalize(inputs):
    values = inputs.astype(jnp.float32)
    inverse_rms = lax.rsqrt(jnp.mean(values * values, axis=-1, keepdims=True) + epsilon)
    return (values * inverse_rms, inverse_rms)


def key_bias(level_flags, shard_rows):
    position = jnp.arange(shard_rows)
    own_part = position[None, :] <= position[:, None]
    far_part = jnp.repeat(level_flags != 0, shard_rows)
    far_part = jnp.broadcast_to(far_part[None, :], (shard_rows, far_part.shape[0]))
    return jnp.concatenate([own_part, far_part], 1)


def split_heads(row_block):
    return row_block.reshape(row_block.shape[0], -1, HEAD_DIM)


def softmax_keys(queries, key_heads, allowed):
    scores = jnp.einsum(
        "ihd,jhd->hij", queries, key_heads, preferred_element_type=jnp.float32
    ) * HEAD_DIM ** (-0.5)
    scores = jnp.where(allowed[None], scores, negative_fill)
    highest = jnp.max(scores, axis=-1, keepdims=True)
    shifted_exp = jnp.where(allowed[None], jnp.exp(scores - highest), 0.0)
    return shifted_exp / jnp.sum(shifted_exp, axis=-1, keepdims=True)


def attend(query_rows, key_rows, allowed):
    model_width = query_rows.shape[1]
    probability = softmax_keys(
        split_heads(query_rows), split_heads(key_rows[:, :model_width]), allowed
    )
    attended = jnp.einsum(
        "hij,jhd->ihd",
        probability.astype(jnp.bfloat16),
        split_heads(key_rows[:, model_width:]),
        preferred_element_type=jnp.float32,
    )
    return attended.reshape(query_rows.shape).astype(jnp.bfloat16)


def attend_back(query_rows, key_rows, allowed, incoming, attended, w_proj):
    model_width = query_rows.shape[1]
    queries = split_heads(query_rows)
    key_heads = split_heads(key_rows[:, :model_width])
    value_heads = split_heads(key_rows[:, model_width:])
    probability = softmax_keys(queries, key_heads, allowed)
    rounded = probability.astype(jnp.bfloat16)
    upstream = lax.dot_general(
        incoming, w_proj, (((1,), (1,)), ((), ())), preferred_element_type=jnp.float32
    ).astype(jnp.bfloat16)
    up_heads = split_heads(upstream)
    delta = jnp.einsum(
        "ihd,ihd->hi", up_heads.astype(jnp.float32), split_heads(attended).astype(jnp.float32)
    )[..., None]
    prob_grad = jnp.einsum(
        "ihd,jhd->hij", up_heads, value_heads, preferred_element_type=jnp.float32
    )
    score_grad = (probability * (prob_grad - delta)).astype(jnp.bfloat16)
    scale_factor = HEAD_DIM ** (-0.5)
    query_grad = (
        jnp.einsum("hij,jhd->ihd", score_grad, key_heads, preferred_element_type=jnp.float32)
        * scale_factor
    )
    key_grad = (
        jnp.einsum("hij,ihd->jhd", score_grad, queries, preferred_element_type=jnp.float32)
        * scale_factor
    )
    value_grad = jnp.einsum("hij,ihd->jhd", rounded, up_heads, preferred_element_type=jnp.float32)
    return (
        query_grad.reshape(-1, model_width),
        key_grad.reshape(-1, model_width),
        value_grad.reshape(-1, model_width),
    )


def per_device(acts, grad_top, w_in, w_out, offsets):
    sections = lax.axis_size("section")
    shards = lax.axis_size("tm")
    levels = shards.bit_length() - 1
    section_index = lax.axis_index("section")
    micro_count = acts.shape[1]
    shard_rows = acts.shape[2]
    model_width = acts.shape[3]
    w_qkv = w_in[0]
    w_proj = w_out[0]
    level_flags = offsets[0]
    normed, inverse_rms = normalize(acts[0])
    rounded_norm = normed.astype(jnp.bfloat16)
    qkv = jnp.dot(rounded_norm.reshape(-1, model_width), w_qkv, preferred_element_type=jnp.float32)
    qkv = qkv.astype(jnp.bfloat16).reshape(micro_count, shard_rows, 3 * model_width)
    pairs = qkv[..., model_width:]
    far_list = [shifted(pairs, "tm", 2**level) for level in range(levels)]
    key_rows = jnp.concatenate([pairs] + far_list, 1)
    allowed = key_bias(level_flags, shard_rows)
    attended = jnp.stack(
        [
            attend(qkv[index, :, :model_width], key_rows[index], allowed)
            for index in range(micro_count)
        ],
        0,
    )

    def attention_part(incoming, slot):
        query_rows = lax.dynamic_index_in_dim(qkv, slot, 0, False)[:, :model_width]
        slot_keys = lax.dynamic_index_in_dim(key_rows, slot, 0, False)
        slot_attended = lax.dynamic_index_in_dim(attended, slot, 0, False)
        query_grad, key_grad, value_grad = attend_back(
            query_rows, slot_keys, allowed, incoming, slot_attended, w_proj
        )
        owner_sum = jnp.concatenate([key_grad[:shard_rows], value_grad[:shard_rows]], 1)
        far_part = jnp.concatenate([key_grad[shard_rows:], value_grad[shard_rows:]], 1)
        far_part = far_part.astype(jnp.bfloat16).reshape(levels, shard_rows, 2 * model_width)
        return (query_grad, owner_sum, far_part)

    def empty_attention(incoming, slot):
        return (
            jnp.zeros((shard_rows, model_width), jnp.float32),
            jnp.zeros((shard_rows, 2 * model_width), jnp.float32),
            jnp.zeros((levels, shard_rows, 2 * model_width), jnp.bfloat16),
        )

    def norm_part(qkv_grad, incoming, slot):
        norm_grad = lax.dot_general(
            qkv_grad, w_qkv, (((1,), (1,)), ((), ())), preferred_element_type=jnp.float32
        )
        slot_normed = lax.dynamic_index_in_dim(normed, slot, 0, False)
        slot_rms = lax.dynamic_index_in_dim(inverse_rms, slot, 0, False)
        inner = jnp.mean(norm_grad * slot_normed, axis=-1, keepdims=True)
        return (incoming.astype(jnp.float32) + slot_rms * (norm_grad - slot_normed * inner)).astype(
            jnp.bfloat16
        )

    def empty_norm(qkv_grad, incoming, slot):
        return jnp.zeros((shard_rows, model_width), jnp.bfloat16)

    def step(turn, carry):
        received, grad_store, qkv_store, incoming_store = carry
        slot_raw = turn - (sections - 1 - section_index)
        active = (slot_raw >= 0) & (slot_raw < micro_count)
        slot = jnp.clip(slot_raw, 0, micro_count - 1)
        incoming = jnp.where(
            section_index == sections - 1,
            lax.dynamic_index_in_dim(grad_top, slot, 0, False),
            received,
        )
        query_grad, owner_sum, far_part = lax.cond(
            active, attention_part, empty_attention, incoming, slot
        )
        for level in range(levels):
            owner_sum = owner_sum + shifted(far_part[level], "tm", -(2**level)).astype(jnp.float32)
        qkv_grad = jnp.concatenate([query_grad, owner_sum], 1).astype(jnp.bfloat16)
        grad_in = lax.cond(active, norm_part, empty_norm, qkv_grad, incoming, slot)
        sent_down = shifted(grad_in, "section", -1)
        grad_store = jnp.where(
            active, lax.dynamic_update_index_in_dim(grad_store, grad_in, slot, 0), grad_store
        )
        qkv_store = jnp.where(
            active, lax.dynamic_update_index_in_dim(qkv_store, qkv_grad, slot, 0), qkv_store
        )
        incoming_store = jnp.where(
            active,
            lax.dynamic_update_index_in_dim(incoming_store, incoming, slot, 0),
            incoming_store,
        )
        return (sent_down, grad_store, qkv_store, incoming_store)

    initial = (
        jnp.zeros((shard_rows, model_width), jnp.bfloat16),
        jnp.zeros((micro_count, shard_rows, model_width), jnp.bfloat16),
        jnp.zeros((micro_count, shard_rows, 3 * model_width), jnp.bfloat16),
        jnp.zeros((micro_count, shard_rows, model_width), jnp.bfloat16),
    )
    received, grad_store, qkv_store, incoming_store = lax.fori_loop(
        0, sections + micro_count - 1, step, initial
    )
    flat_norm = rounded_norm.reshape(-1, model_width)
    flat_attended = attended.reshape(-1, model_width)
    flat_qkv = qkv_store.reshape(-1, 3 * model_width)
    flat_incoming = incoming_store.reshape(-1, model_width)
    contract = (((0,), (0,)), ((), ()))
    first = lax.dot_general(flat_norm, flat_qkv, contract, preferred_element_type=jnp.float32)
    second = lax.dot_general(
        flat_attended, flat_incoming, contract, preferred_element_type=jnp.float32
    )
    summed = lax.psum_scatter(
        jnp.concatenate([first, second], 1).astype(jnp.bfloat16),
        "tm",
        scatter_dimension=0,
        tiled=True,
    ).astype(jnp.float32)
    return (
        grad_store[None],
        summed[None, :, : 3 * model_width],
        summed[None, :, 3 * model_width :],
    )


def side_by_side(transposed, pair):
    width = 2 * HEAD_DIM
    rows = transposed[pair * width : (pair + 1) * width]
    empty = jnp.zeros((HEAD_DIM, rows.shape[1]), rows.dtype)
    return jnp.concatenate(
        [
            jnp.concatenate([rows[:HEAD_DIM], empty], 0),
            jnp.concatenate([empty, rows[HEAD_DIM:]], 0),
        ],
        1,
    )


def one_above_other(rows, masks):
    return jnp.concatenate([rows * masks[0], rows * masks[1]], 0)


def head_masks():
    lane = lax.broadcasted_iota(jnp.int32, (1, 2 * HEAD_DIM), 1)
    return [
        jnp.where(lane < HEAD_DIM, 1.0, 0.0).astype(jnp.bfloat16),
        jnp.where(lane < HEAD_DIM, 0.0, 1.0).astype(jnp.bfloat16),
    ]


def key_bias_rows(flag_rows, levels, shard_rows, keys, first_query, count):
    key_at = lax.broadcasted_iota(jnp.int32, (keys, count), 0)
    query_at = lax.broadcasted_iota(jnp.int32, (keys, count), 1) + first_query
    gap = lax.div(query_at, shard_rows) - lax.div(key_at, shard_rows)
    allowed = (gap == 0) & (key_at <= query_at)
    for level in range(levels):
        allowed = allowed | ((gap == 2**level) & (flag_rows[level : level + 1] != 0))
    return jnp.where(allowed, 0.0, negative_fill)


def softmax_pass(queries, keys, values, bias, prob_ref, at_ref):
    queries_t = queries.T
    values_t = values.T
    width = 2 * HEAD_DIM
    count = queries.shape[0]
    for pair in range(queries.shape[1] // width):
        at_pair = slice(pair * width, (pair + 1) * width)
        scores = jnp.dot(
            keys[:, at_pair], side_by_side(queries_t, pair), preferred_element_type=jnp.float32
        )
        for half in range(2):
            at_half = slice(half * count, (half + 1) * count)
            biased = scores[:, at_half] + bias
            shifted_exp = jnp.exp(biased - jnp.max(biased, axis=0, keepdims=True))
            probability = shifted_exp * (1.0 / jnp.sum(shifted_exp, axis=0, keepdims=True))
            prob_ref[pair, :, at_half] = probability.astype(jnp.bfloat16)
    for head in range(queries.shape[1] // HEAD_DIM):
        at = slice(head * HEAD_DIM, (head + 1) * HEAD_DIM)
        at_half = slice(head % 2 * count, (head % 2 + 1) * count)
        at_ref[at] = jnp.dot(
            values_t[at], prob_ref[head // 2, :, at_half], preferred_element_type=jnp.float32
        ).astype(jnp.bfloat16)


def pack_kernel(
    levels, info_ref, acts_ref, top_ref, own_ref, other_ref, own_top_ref, other_top_ref, sems
):
    model_width = acts_ref.shape[2]
    shard_rows = own_ref.shape[0]
    side = info_ref[4]
    copies = [
        pltpu.make_async_copy(acts_ref.at[side], own_ref.at[:, :model_width], sems.at[0]),
        pltpu.make_async_copy(acts_ref.at[1 - side], other_ref.at[:, :model_width], sems.at[1]),
        pltpu.make_async_copy(top_ref.at[side], own_top_ref, sems.at[2]),
        pltpu.make_async_copy(top_ref.at[1 - side], other_top_ref, sems.at[3]),
    ]
    for copy in copies:
        copy.start()
    lane = lax.broadcasted_iota(jnp.int32, (shard_rows, own_ref.shape[1] - model_width), 1)
    flags = jnp.zeros(lane.shape, jnp.float32)
    for level in range(levels):
        seen = jnp.where(info_ref[5 + level] != 0, 1.0, 0.0)
        flags = jnp.where(lane == level, seen, flags)
    own_ref[:, model_width:] = flags.astype(jnp.bfloat16)
    other_ref[:, model_width:] = flags.astype(jnp.bfloat16)
    for copy in copies:
        copy.wait()


def touch_kernel(w_ref, after_ref, out_ref):
    out_ref[...] = w_ref[: out_ref.shape[0], : out_ref.shape[1]]


def project_kernel(replicas, info_ref, *refs):
    pieces = refs[: 4 * replicas]
    w_ref, _, normed_ref, rms_ref, norm_ref, flag_ref, q_ref, k_ref, v_ref, kt_ref, packed_ref = refs[
        4 * replicas :
    ]
    shards, shard_rows = packed_ref.shape[:2]
    model_width = w_ref.shape[0]
    seq = shards * shard_rows
    columns = q_ref.shape[1]
    at_piece = 0
    for core in (info_ref[0], 1 - info_ref[0]):
        for side in (info_ref[2], 1 - info_ref[2]):
            for step in range(replicas):
                shard = side * (shards // 2) + place_of(info_ref, step, replicas) + core
                packed_ref[shard] = pieces[at_piece][...]
                at_piece += 1
    for chunk in range(2):
        for step in range(replicas):
            shard = chunk * (shards // 2) + place_of(info_ref, step, replicas) + info_ref[0]
            normed, inverse_rms = normalize(packed_ref[shard][:, :model_width])
            normed_ref[chunk, step] = normed
            rms_ref[chunk, step] = jnp.broadcast_to(inverse_rms, rms_ref.shape[2:])
    normed, _ = normalize(packed_ref[:, :, :model_width].reshape(seq, model_width))
    rounded = normed.astype(jnp.bfloat16)
    norm_ref[...] = rounded
    flag_ref[...] = packed_ref[:, :, model_width:].reshape(seq, -1).astype(jnp.float32).T
    scale_factor = HEAD_DIM ** (-0.5)
    for block, out_ref in enumerate((q_ref, k_ref, v_ref)):
        first = pl.multiple_of(block * model_width + info_ref[0] * columns, 128)
        product = jnp.dot(
            rounded, w_ref[:, pl.ds(first, columns)], preferred_element_type=jnp.float32
        ).astype(jnp.bfloat16)
        out_ref[...] = product * scale_factor if block == 0 else product
    kt_ref[...] = (k_ref[...] * scale_factor).T


def upper_forward_kernel(
    levels, shard_rows, flag_ref, q_ref, k_ref, v_ref, prob_ref, at_ref
):
    seq = q_ref.shape[0]
    count = seq // 2
    bias = key_bias_rows(flag_ref[:, count:], levels, shard_rows, seq, count, count)
    softmax_pass(q_ref[count:], k_ref[...], v_ref[...], bias, prob_ref, at_ref)


def lower_forward_kernel(
    levels,
    shard_rows,
    info_ref,
    norm_ref,
    flag_ref,
    q_ref,
    k_ref,
    v_ref,
    after_ref,
    prob_ref,
    at_ref,
    gt_ref,
):
    seq = norm_ref.shape[0]
    count = seq // 2
    bias = key_bias_rows(flag_ref[:, :count], levels, shard_rows, count, 0, count)
    softmax_pass(q_ref[:count], k_ref[:count], v_ref[:count], bias, prob_ref, at_ref)
    rows = gt_ref.shape[0] // 4
    parity, x, y = info_ref[0], info_ref[1], info_ref[2]
    half = norm_ref.shape[1] // rows // 2
    for place, block in enumerate(
        (
            half * y + 2 * x + 1 - parity,
            half * y + 2 * x + parity,
            half * y + 2 * (1 - x) + 1 - parity,
            half * (1 - y) + 2 * x + parity,
        )
    ):
        first = pl.multiple_of(block * rows, 128)
        gt_ref[place * rows : (place + 1) * rows] = norm_ref[:, pl.ds(first, rows)].T


def place_of(info_ref, step, replicas):
    return 2 * lax.rem(info_ref[1] - step + replicas, replicas)


def merge_rows(info_ref, fresh, got_refs, kept_refs, out_refs, rows_ref):
    @pl.when(fresh)
    def _():
        for core, out_ref in enumerate(out_refs):
            out_ref[...] = got_refs[core][...]

    @pl.when(jnp.logical_not(fresh))
    def _():
        for out_ref, kept_ref in zip(out_refs, kept_refs):
            out_ref[...] = kept_ref[...]

    place_rows(info_ref, out_refs, rows_ref)


def place_rows(info_ref, out_refs, rows_ref):
    replicas = out_refs[0].shape[0]
    for step in range(replicas):
        place = place_of(info_ref, step, replicas)
        rows_ref[place + info_ref[0]] = out_refs[0][step]
        rows_ref[place + 1 - info_ref[0]] = out_refs[1][step]


def merge_tops(info_ref, upper, piece_refs, out_refs, rows_ref):
    replicas = out_refs[0].shape[0]
    own_chunk = info_ref[2] == (1 if upper else 0)
    for core in range(2):
        refs = piece_refs[2 * replicas * core : 2 * replicas * (core + 1)]

        @pl.when(own_chunk)
        def _():
            for step in range(replicas):
                out_refs[core][step] = refs[step][...]

        @pl.when(jnp.logical_not(own_chunk))
        def _():
            for step in range(replicas):
                out_refs[core][step] = refs[replicas + step][...]

    place_rows(info_ref, out_refs, rows_ref)


def backward_kernel(upper, tops, last, fresh_section, info_ref, *refs):
    refs = list(refs)
    got = tops or 4
    got_refs = refs[:got]
    w_ref, prob_ref, q_ref, v_ref, kt_ref, at_ref = refs[got : got + 6]
    refs = refs[got + 6 :]
    if not upper:
        key_sum_ref, value_sum_ref = refs[:2]
        refs = refs[2:]
    refs = refs[1:]
    if last:
        refs = [refs[0], refs[-1], *refs[1:-1]]
    own_ref, other_ref, keep_ref = refs[:3]
    send_refs = refs[3 : 3 + PIECES[upper]]
    refs = refs[3 + len(send_refs) :]
    if upper:
        key_sum_ref, value_sum_ref = refs[:2]
        refs = refs[2:]
    grads_ref, rows_ref, scores_ref = refs
    replicas, shard_rows, model_width = own_ref.shape
    count = rows_ref.shape[0] * shard_rows
    keys = prob_ref.shape[1]
    parity = info_ref[0]
    columns = q_ref.shape[1]
    width = 2 * HEAD_DIM
    if tops:
        merge_tops(info_ref, upper, got_refs, (own_ref, other_ref), rows_ref)
    else:
        fresh = info_ref[3] == fresh_section
        merge_rows(info_ref, fresh, got_refs[:-2], got_refs[-2:], (own_ref, other_ref), rows_ref)
    rows = rows_ref[...].reshape(count, model_width)
    weights = w_ref[pl.ds(pl.multiple_of(parity * columns, 128), columns), :]
    over_width = (((1,), (1,)), ((), ()))
    upstream = lax.dot_general(
        rows, weights, over_width, preferred_element_type=jnp.float32
    ).astype(jnp.bfloat16)
    upstream_t = upstream.T
    product_t = upstream_t.astype(jnp.float32) * at_ref[...].astype(jnp.float32)
    first_query = keys - count
    masks = head_masks()

    def put(block, pair, part):
        first = block * columns + pair * width
        grads_ref[:, :, first : first + width] = part.astype(jnp.bfloat16).reshape(
            -1, shard_rows, width
        )

    for pair in range(columns // width):
        at_pair = slice(pair * width, (pair + 1) * width)
        prob_grad = jnp.dot(
            v_ref[:keys, at_pair], side_by_side(upstream_t, pair), preferred_element_type=jnp.float32
        )
        for half in range(2):
            at_half = slice(half * count, (half + 1) * count)
            first = pair * width + half * HEAD_DIM
            delta = jnp.sum(product_t[first : first + HEAD_DIM], axis=0, keepdims=True)
            scores_ref[pair, :, at_half] = (
                prob_ref[pair, :, at_half].astype(jnp.float32) * (prob_grad[:, at_half] - delta)
            ).astype(jnp.bfloat16)
        value_grad = jnp.dot(
            prob_ref[pair],
            one_above_other(upstream[:, at_pair], masks),
            preferred_element_type=jnp.float32,
        )
        if upper:
            value_sum_ref[:, at_pair] = value_grad[:first_query]
            value_grad = value_grad[first_query:]
        else:
            value_grad = value_grad + value_sum_ref[:, at_pair]
        put(2, pair, value_grad)
    for pair in range(columns // width):
        at_pair = slice(pair * width, (pair + 1) * width)
        queries = q_ref[first_query : first_query + count, at_pair]
        key_grad = jnp.dot(
            scores_ref[pair], one_above_other(queries, masks), preferred_element_type=jnp.float32
        )
        if upper:
            key_sum_ref[:, at_pair] = key_grad[:first_query]
            key_grad = key_grad[first_query:]
        else:
            key_grad = key_grad + key_sum_ref[:, at_pair]
        put(1, pair, key_grad)
        query_grad = [
            jnp.dot(
                kt_ref[pair * width + half * HEAD_DIM : pair * width + (half + 1) * HEAD_DIM, :keys],
                scores_ref[pair, :, half * count : (half + 1) * count],
                preferred_element_type=jnp.float32,
            )
            for half in range(2)
        ]
        put(0, pair, jnp.concatenate(query_grad, 0).astype(jnp.bfloat16).T)
    for step in range(replicas):
        place = place_of(info_ref, step, replicas)
        keep_ref[step] = grads_ref[place + parity]
        crossing = grads_ref[place + 1 - parity]
        part = crossing.shape[1] // len(send_refs)
        for at, send_ref in enumerate(send_refs):
            send_ref[step] = crossing[:, at * part : (at + 1) * part]


def norm_product(part, w_ref, half):
    columns = part.shape[1] // 3
    model_width = w_ref.shape[0]
    total = jnp.zeros((part.shape[0], model_width), jnp.float32)
    for block in range(3):
        first = pl.multiple_of(block * model_width + half * columns, 128)
        total += lax.dot_general(
            part[:, block * columns : (block + 1) * columns],
            w_ref[:, pl.ds(first, columns)],
            (((1,), (1,)), ((), ())),
            preferred_element_type=jnp.float32,
        )
    return total


def norm_part_kernel(info_ref, keep_ref, w_ref, after_ref, out_ref):
    part = keep_ref[...].reshape(out_ref.shape[0], -1)
    out_ref[...] = norm_product(part, w_ref, info_ref[0])


def norm_kernel(upper, info_ref, keep_ref, normed_ref, rms_ref, incoming_ref, w_ref, *refs):
    got_refs = refs[: PIECES[upper]]
    out_refs = refs[len(got_refs) :]
    model_width = w_ref.shape[0]
    replicas, shard_rows = incoming_ref.shape[:2]
    rows = replicas * shard_rows
    got = [got_ref[...].reshape(rows, -1) for got_ref in got_refs]
    norm_grad = norm_product(jnp.concatenate(got, 1), w_ref, 1 - info_ref[0])
    norm_grad += (
        keep_ref[...]
        if upper
        else norm_product(keep_ref[...].reshape(rows, -1), w_ref, info_ref[0])
    )
    chunk = 1 if upper else 0
    normed = normed_ref[chunk].reshape(rows, model_width)
    inverse_rms = rms_ref[chunk].reshape(rows, -1)[:, :1]
    inner = jnp.mean(norm_grad * normed, axis=-1, keepdims=True)
    incoming = incoming_ref[...].reshape(rows, model_width).astype(jnp.float32)
    grad_in = incoming + inverse_rms * (norm_grad - normed * inner)
    grad_in = grad_in.astype(jnp.bfloat16).reshape(replicas, shard_rows, model_width)
    out_refs[-1][...] = grad_in


def term_kernel(info_ref, gt_ref, *refs):
    grad_refs, at_refs, row_refs = refs[:2], refs[2:4], refs[4:6]
    own_pass_ref, own_keep_ref, send_pass_ref, send_keep_ref = refs[6:10]
    out_pass_ref, out_keep_ref, out_send_ref = refs[10:]
    rows = own_pass_ref.shape[0]
    width = out_send_ref.shape[1]
    count = row_refs[0].shape[0] * row_refs[0].shape[1]
    parity, x, y = info_ref[0], info_ref[1], info_ref[2]
    for half, (pass_ref, keep_ref) in reversed(
        list(enumerate(((own_pass_ref, own_keep_ref), (send_pass_ref, send_keep_ref))))
    ):
        total = sum(
            jnp.dot(
                gt_ref[2 * half * rows : 2 * (half + 1) * rows, chunk * count : (chunk + 1) * count],
                part_ref[...].reshape(count, -1),
                preferred_element_type=jnp.float32,
            )
            for chunk, part_ref in enumerate(grad_refs)
        )
        pass_ref[...] = total[:rows].astype(pass_ref.dtype)
        keep_ref[...] = total[rows:].astype(keep_ref.dtype)
    sent = jnp.where(parity == y, 2 * (1 - x) + 1 - parity, 2 * x + parity)
    blocks = (sent, 2 * x + 1 - parity, 2 * x + parity)
    total = jnp.zeros((3 * rows, width), jnp.float32)
    for at_ref, part_ref in zip(at_refs, row_refs):
        picked = [at_ref[pl.ds(pl.multiple_of(block * rows, 128), rows)] for block in blocks]
        total += jnp.dot(
            jnp.concatenate(picked, 0),
            part_ref[...].reshape(count, width),
            preferred_element_type=jnp.float32,
        )
    out_send_ref[...] = total[:rows].astype(jnp.bfloat16)
    out_pass_ref[...] = total[rows : 2 * rows]
    out_keep_ref[...] = total[2 * rows :]


def sum_kernel(own_ref, got_ref, out_own_ref, out_got_ref, after_ref, sum_ref):
    columns = own_ref.shape[1]
    sum_ref[:, :columns] = (own_ref[...] + got_ref[...].astype(jnp.float32)).astype(jnp.bfloat16)
    sum_ref[:, columns:] = (out_own_ref[...] + out_got_ref[...].astype(jnp.float32)).astype(
        jnp.bfloat16
    )


def pick_kernel(info_ref, upper_ref, lower_ref, out_ref):
    crossing = info_ref[0] == 0
    for step in range(2):
        for chunk, part_ref in enumerate((lower_ref, upper_ref)):
            wanted = info_ref[2] == (chunk if step == 1 else 1 - chunk)

            @pl.when(wanted & (crossing if step == 1 else jnp.logical_not(crossing)))
            def _():
                out_ref[...] = part_ref[step]


def join_kernel(info_ref, upper_ref, lower_ref, got_ref, out_ref):
    micro = info_ref[4]
    out_ref[0, 1 - micro] = got_ref[...]

    @pl.when(info_ref[2] == 1)
    def _():
        out_ref[0, micro] = upper_ref[0]

    @pl.when(info_ref[2] != 1)
    def _():
        out_ref[0, micro] = lower_ref[0]


def place_kernel(
    info_ref, own_ref, got_ref, out_own_ref, out_got_ref, sibling_ref, d_in_ref, d_out_ref
):
    columns = own_ref.shape[1] // 3
    own = own_ref[...] + got_ref[...].astype(jnp.float32)
    sibling = sibling_ref[:, : 3 * columns].astype(jnp.float32)
    for part, half in ((own, info_ref[0]), (sibling, 1 - info_ref[0])):
        for block in range(3):
            first = pl.multiple_of((2 * block + half) * columns, 128)
            d_in_ref[:, pl.ds(first, columns)] = part[:, block * columns : (block + 1) * columns]
    owner = info_ref[0] == info_ref[2]

    @pl.when(owner)
    def _():
        d_out_ref[...] = out_own_ref[...] + out_got_ref[...].astype(jnp.float32)

    @pl.when(jnp.logical_not(owner))
    def _():
        d_out_ref[...] = sibling_ref[:, 3 * columns :].astype(jnp.float32)


def call(kernel, outs, operands, scratch=(), flops=0, scalars=1, after=None, mebibytes=5, far=0):
    in_specs = [pl.BlockSpec(memory_space=pltpu.SMEM)] * scalars
    in_specs += [pl.BlockSpec(memory_space=pltpu.HBM)] * far
    in_specs += [pl.BlockSpec(memory_space=pltpu.VMEM)] * (len(operands) - scalars - far)
    if after is not None:
        operands = [*operands, after]
        in_specs.append(pl.BlockSpec(memory_space=pl.ANY))
    return pl.pallas_call(
        kernel,
        out_shape=list(outs),
        in_specs=in_specs,
        out_specs=[pl.BlockSpec(memory_space=pltpu.VMEM)] * len(outs),
        scratch_shapes=list(scratch),
        cost_estimate=pl.CostEstimate(flops=1, bytes_accessed=1, transcendentals=0),
        compiler_params=pltpu.CompilerParams(vmem_limit_bytes=mebibytes * 2**20),
    )(*operands)


def by_chips(acts, grad_top, w_in, w_out, offsets):
    half_type, full_type = jnp.bfloat16, jnp.float32
    shape = jax.ShapeDtypeStruct
    sections = lax.axis_size("section")
    shards = lax.axis_size("tm")
    levels = offsets.shape[1]
    half = shards // 2
    replicas = half // 2
    me = lax.axis_index("tm")
    parity = lax.rem(me, 2)
    side = lax.div(me, half)
    micro_count, shard_rows, model_width = acts.shape[1:]
    columns = model_width // 2
    heads = columns // HEAD_DIM
    seq = shards * shard_rows
    count = seq // 2
    w_qkv = w_in[0]
    w_rows = w_out[0]
    beside = lax.div(lax.rem(me, half), 2)
    micro = lax.rem(side + beside, 2)
    info = jnp.stack([parity, beside, side, lax.axis_index("section"), micro])
    info = jnp.concatenate([info.astype(jnp.int32), offsets[0]])

    def swapped(value, bits, chosen=None):
        pairs = [(device, device ^ bits) for device in range(shards)]
        pairs = [pair for pair in pairs if chosen is None or chosen(pair[0])]
        return lax.ppermute(value, "tm", pairs)

    core, near, far = 1, 2, half

    packed = shape((shard_rows, model_width + 128), half_type)
    top_shape = shape((shard_rows, model_width), half_type)
    own_acts, other_acts, own_top, other_top = call(
        functools.partial(pack_kernel, levels),
        [packed, packed, top_shape, top_shape],
        [info, acts[0], grad_top],
        scratch=[pltpu.SemaphoreType.DMA((4,))],
        far=2,
    )
    (touched,) = call(
        touch_kernel, [shape((16, 128), half_type)], [w_qkv], scalars=0, after=own_acts
    )
    pieces = [own_acts, swapped(other_acts, near), swapped(other_acts, far)]
    pieces += [swapped(own_acts, near + far)]
    tops = [own_top, swapped(other_top, near), swapped(other_top, far)]
    pieces[-1], tops, touched = lax.optimization_barrier((pieces[-1], tops, touched))
    tops += [swapped(own_top, near + far)]
    pieces += [swapped(piece, core) for piece in pieces]

    rows_shape = shape((seq, columns), half_type)
    normed, rms, norm, flag_rows, queries, keys, values, keys_t = call(
        functools.partial(project_kernel, replicas),
        [
            shape((2, replicas, shard_rows, model_width), full_type),
            shape((2, replicas, shard_rows, 128), full_type),
            shape((seq, model_width), half_type),
            shape((128, seq), full_type),
            rows_shape,
            rows_shape,
            rows_shape,
            shape((columns, seq), half_type),
        ],
        [info, *pieces, w_qkv],
        scratch=[pltpu.VMEM((shards, *packed.shape), half_type)],
        flops=6 * seq * model_width * columns,
        after=touched,
    )
    tops, _ = lax.optimization_barrier((tuple(tops), keys_t))
    tops = [*tops, *[swapped(piece, core) for piece in tops]]
    pairs = heads // 2
    upper_prob, upper_at = call(
        functools.partial(upper_forward_kernel, levels, shard_rows),
        [
            shape((pairs, seq, 2 * count), half_type),
            shape((columns, count), half_type),
        ],
        [flag_rows, queries, keys, values],
        scalars=0,
        flops=4 * columns * seq * count,
    )
    own_rows = model_width // shards
    probs, attended = {True: upper_prob}, {True: upper_at}
    got, kept = {}, {}
    piece_shape = shape((replicas, shard_rows, model_width), half_type)
    grads_shape = shape((replicas, shard_rows, 3 * columns), half_type)
    sum_shape = shape((count, columns), full_type)
    full_grads = shape((half, shard_rows, 3 * columns), half_type)
    full_rows = shape((half, shard_rows, model_width), half_type)
    term_shape = (own_rows, 3 * columns)
    rows_scratch = pltpu.VMEM(full_rows.shape, half_type)
    grads_scratch = pltpu.VMEM(full_grads.shape, half_type)
    result, full, ordered = {}, {}, {}
    for turn in range(sections):
        last = turn + 1 == sections
        fresh_section = sections - 1 - turn
        sums, parts, crossed = [], {}, {}

        def norm_step(upper, after):
            (result[upper],) = call(
                functools.partial(norm_kernel, upper),
                [piece_shape],
                [info, parts[upper], normed, rms, kept[upper][0], w_qkv, *crossed[upper]],
                after=after,
            )
            if not last:
                hop = [(sections - 1 - turn, sections - 2 - turn)]
                got[upper] = lax.ppermute(result[upper], "section", hop)

        for upper in (True, False):
            rows_in, after = tops, keys_t if upper else result.get(True)
            if turn:
                before = result[False] if upper else result[True]
                got[upper], after = lax.optimization_barrier((got[upper], before))
                if not upper:
                    result[True] = after
                rows_in = [got[upper], swapped(got[upper], core), *kept[upper]]
            part = 3 * columns // PIECES[upper]
            cross = [shape((replicas, shard_rows, part), half_type)] * PIECES[upper]
            outs = [piece_shape] * (1 if last else 2) + [grads_shape, *cross]
            outs += [sum_shape, sum_shape] if upper else []
            scratch = []
            if last:
                outs += [full_grads]
            else:
                scratch += [grads_scratch]
            if last:
                outs += [full_rows]
            else:
                scratch += [rows_scratch]
            part_keys = seq if upper else count
            scratch += [pltpu.VMEM((pairs, part_keys, 2 * count), half_type)]
            if last:
                scratch += [pltpu.VMEM(piece_shape.shape, half_type)]
            answer = call(
                functools.partial(
                    backward_kernel, upper, 0 if turn else len(tops), last, fresh_section
                ),
                outs,
                [info, *rows_in, w_rows, probs[upper], queries, values, keys_t]
                + [attended[upper], *sums],
                scratch=scratch,
                flops=2 * count * columns * (2 * model_width + 4 * part_keys),
                after=after,
            )
            kept[upper] = tuple(answer[:2])
            answer = answer[1 if last else 2 :]
            keep = answer[0]
            send = answer[1 : 1 + len(cross)]
            parts[upper] = keep
            if upper:
                sums = answer[1 + len(cross) : 3 + len(cross)]
                (parts[True],) = call(
                    norm_part_kernel,
                    [shape((replicas * shard_rows, model_width), full_type)],
                    [info, keep, w_qkv],
                    flops=3 * replicas * shard_rows * model_width * model_width,
                    after=keep,
                )
                if turn == 0:
                    lower_prob, lower_at, norm_t = call(
                        functools.partial(lower_forward_kernel, levels, shard_rows),
                        [
                            shape((pairs, count, 2 * count), half_type),
                            shape((columns, count), half_type),
                            shape((4 * own_rows, seq), half_type),
                        ],
                        [info, norm, flag_rows, queries, keys, values],
                        flops=4 * columns * count * count,
                        after=parts[True],
                    )
                    probs[False], attended[False] = lower_prob, lower_at
            if last:
                full[upper], ordered[upper] = answer[-2:]
            crossed[upper] = [swapped(piece, core) for piece in send]
            if upper:
                norm_step(True, keep)
        if last:
            terms = call(
                term_kernel,
                [shape(term_shape, full_type)] * 2
                + [shape(term_shape, half_type)] * 2
                + [shape((own_rows, model_width), full_type)] * 2
                + [shape((own_rows, model_width), half_type)],
                [info, norm_t, full[False], full[True], attended[False], attended[True]]
                + [ordered[False], ordered[True]],
                flops=2 * own_rows * seq * (12 * columns + 3 * model_width),
                mebibytes=10,
            )
        norm_step(False, terms[3] if last else result[True])

    in_pass, in_keep, send_pass, send_keep, out_pass, out_keep, out_send = terms
    got_pass = swapped(send_pass, near)
    got_keep = swapped(send_keep, far)
    own_rows_grad = [result[True], result[False]]
    (theirs,) = call(pick_kernel, [top_shape], [info, *own_rows_grad])
    to_owner = [(device, device ^ (far if device % 2 else near)) for device in range(shards)]
    partner = lax.ppermute(theirs, "tm", to_owner)
    got_out_pass = swapped(out_send, near, lambda device: device // half == device % 2)
    got_out_keep = swapped(out_send, far, lambda device: device // half != device % 2)
    _, _, done = lax.optimization_barrier((got_keep, got_out_keep, partner))
    (summed,) = call(
        sum_kernel,
        [shape((own_rows, 3 * columns + model_width), half_type)],
        [in_pass, got_pass, out_pass, got_out_pass],
        scalars=0,
        after=done,
    )
    d_w_in, d_w_out = call(
        place_kernel,
        [
            shape((own_rows, 3 * model_width), full_type),
            shape((own_rows, model_width), full_type),
        ],
        [info, in_keep, got_keep, out_keep, got_out_keep, swapped(summed, core)],
    )
    (d_acts,) = call(
        join_kernel, [shape(acts.shape, half_type)], [info, *own_rows_grad, partner]
    )
    return (d_acts, d_w_in[None], d_w_out[None])


def layer_gradients(acts, grad_top, w_in, w_out, offsets):
    shards = lax.axis_size("tm")
    micro_count, shard_rows, model_width = acts.shape[1:]
    heads = model_width // HEAD_DIM
    prob_bytes = 2 * heads * (shards * shard_rows) ** 2
    fits = prob_bytes <= 2**24 and model_width % (128 * shards) == 0 and shard_rows % 16 == 0
    square = shards % 4 == 0 and shards // 4 == 2
    if micro_count == 2 and square and heads % 4 == 0 and fits:
        return by_chips(acts, grad_top, w_in, w_out, offsets)
    return per_device(acts, grad_top, w_in, w_out, offsets)


def solution(mesh):
    placed = (
        P("section", None, "tm", None),
        P(None, "tm", None),
        P("section", None, None),
        P("section", None, None),
        P("tm", None),
    )
    return jax.shard_map(
        layer_gradients,
        mesh=mesh,
        in_specs=placed,
        out_specs=(
            P("section", None, "tm", None),
            P("section", "tm", None),
            P("section", "tm", None),
        ),
        check_vma=False,
    )
```

```python
import functools
import jax
import jax.numpy as jnp
from jax import lax
from jax.experimental import pallas as pl
from jax.experimental.pallas import tpu as pltpu
from jax.sharding import PartitionSpec as P

HEAD_DIM = 64


epsilon = 1e-06
SPLITS = {True: (6, 6), False: (3, 3, 3, 3)}
negative_fill = -1e30


def shifted(value, axis, steps):
    count = lax.axis_size(axis)
    initial, last = (max(0, -steps), min(count, count - steps))
    return lax.ppermute(value, axis, [(source, source + steps) for source in range(initial, last)])


def normalize(inputs):
    values = inputs.astype(jnp.float32)
    inverse_rms = lax.rsqrt(jnp.mean(values * values, axis=-1, keepdims=True) + epsilon)
    return (values * inverse_rms, inverse_rms)


def key_bias(level_flags, shard_rows):
    position = jnp.arange(shard_rows)
    own_part = position[None, :] <= position[:, None]
    far_part = jnp.repeat(level_flags != 0, shard_rows)
    far_part = jnp.broadcast_to(far_part[None, :], (shard_rows, far_part.shape[0]))
    return jnp.concatenate([own_part, far_part], 1)


def split_heads(row_block):
    return row_block.reshape(row_block.shape[0], -1, HEAD_DIM)


def softmax_keys(queries, key_heads, allowed):
    scores = jnp.einsum(
        "ihd,jhd->hij", queries, key_heads, preferred_element_type=jnp.float32
    ) * HEAD_DIM ** (-0.5)
    scores = jnp.where(allowed[None], scores, negative_fill)
    highest = jnp.max(scores, axis=-1, keepdims=True)
    shifted_exp = jnp.where(allowed[None], jnp.exp(scores - highest), 0.0)
    return shifted_exp / jnp.sum(shifted_exp, axis=-1, keepdims=True)


def attend(query_rows, key_rows, allowed):
    model_width = query_rows.shape[1]
    probability = softmax_keys(
        split_heads(query_rows), split_heads(key_rows[:, :model_width]), allowed
    )
    attended = jnp.einsum(
        "hij,jhd->ihd",
        probability.astype(jnp.bfloat16),
        split_heads(key_rows[:, model_width:]),
        preferred_element_type=jnp.float32,
    )
    return attended.reshape(query_rows.shape).astype(jnp.bfloat16)


def attend_back(query_rows, key_rows, allowed, incoming, attended, w_proj):
    model_width = query_rows.shape[1]
    queries = split_heads(query_rows)
    key_heads = split_heads(key_rows[:, :model_width])
    value_heads = split_heads(key_rows[:, model_width:])
    probability = softmax_keys(queries, key_heads, allowed)
    rounded = probability.astype(jnp.bfloat16)
    upstream = lax.dot_general(
        incoming, w_proj, (((1,), (1,)), ((), ())), preferred_element_type=jnp.float32
    ).astype(jnp.bfloat16)
    up_heads = split_heads(upstream)
    delta = jnp.einsum(
        "ihd,ihd->hi", up_heads.astype(jnp.float32), split_heads(attended).astype(jnp.float32)
    )[..., None]
    prob_grad = jnp.einsum(
        "ihd,jhd->hij", up_heads, value_heads, preferred_element_type=jnp.float32
    )
    score_grad = (probability * (prob_grad - delta)).astype(jnp.bfloat16)
    scale_factor = HEAD_DIM ** (-0.5)
    query_grad = (
        jnp.einsum("hij,jhd->ihd", score_grad, key_heads, preferred_element_type=jnp.float32)
        * scale_factor
    )
    key_grad = (
        jnp.einsum("hij,ihd->jhd", score_grad, queries, preferred_element_type=jnp.float32)
        * scale_factor
    )
    value_grad = jnp.einsum("hij,ihd->jhd", rounded, up_heads, preferred_element_type=jnp.float32)
    return (
        query_grad.reshape(-1, model_width),
        key_grad.reshape(-1, model_width),
        value_grad.reshape(-1, model_width),
    )


def per_device(acts, grad_top, w_in, w_out, offsets):
    sections = lax.axis_size("section")
    shards = lax.axis_size("tm")
    levels = shards.bit_length() - 1
    section_index = lax.axis_index("section")
    micro_count = acts.shape[1]
    shard_rows = acts.shape[2]
    model_width = acts.shape[3]
    w_qkv = w_in[0]
    w_proj = w_out[0]
    level_flags = offsets[0]
    normed, inverse_rms = normalize(acts[0])
    rounded_norm = normed.astype(jnp.bfloat16)
    qkv = jnp.dot(rounded_norm.reshape(-1, model_width), w_qkv, preferred_element_type=jnp.float32)
    qkv = qkv.astype(jnp.bfloat16).reshape(micro_count, shard_rows, 3 * model_width)
    pairs = qkv[..., model_width:]
    far_list = [shifted(pairs, "tm", 2**level) for level in range(levels)]
    key_rows = jnp.concatenate([pairs] + far_list, 1)
    allowed = key_bias(level_flags, shard_rows)
    attended = jnp.stack(
        [
            attend(qkv[index, :, :model_width], key_rows[index], allowed)
            for index in range(micro_count)
        ],
        0,
    )

    def attention_part(incoming, slot):
        query_rows = lax.dynamic_index_in_dim(qkv, slot, 0, False)[:, :model_width]
        slot_keys = lax.dynamic_index_in_dim(key_rows, slot, 0, False)
        slot_attended = lax.dynamic_index_in_dim(attended, slot, 0, False)
        query_grad, key_grad, value_grad = attend_back(
            query_rows, slot_keys, allowed, incoming, slot_attended, w_proj
        )
        owner_sum = jnp.concatenate([key_grad[:shard_rows], value_grad[:shard_rows]], 1)
        far_part = jnp.concatenate([key_grad[shard_rows:], value_grad[shard_rows:]], 1)
        far_part = far_part.astype(jnp.bfloat16).reshape(levels, shard_rows, 2 * model_width)
        return (query_grad, owner_sum, far_part)

    def empty_attention(incoming, slot):
        return (
            jnp.zeros((shard_rows, model_width), jnp.float32),
            jnp.zeros((shard_rows, 2 * model_width), jnp.float32),
            jnp.zeros((levels, shard_rows, 2 * model_width), jnp.bfloat16),
        )

    def norm_part(qkv_grad, incoming, slot):
        norm_grad = lax.dot_general(
            qkv_grad, w_qkv, (((1,), (1,)), ((), ())), preferred_element_type=jnp.float32
        )
        slot_normed = lax.dynamic_index_in_dim(normed, slot, 0, False)
        slot_rms = lax.dynamic_index_in_dim(inverse_rms, slot, 0, False)
        inner = jnp.mean(norm_grad * slot_normed, axis=-1, keepdims=True)
        return (incoming.astype(jnp.float32) + slot_rms * (norm_grad - slot_normed * inner)).astype(
            jnp.bfloat16
        )

    def empty_norm(qkv_grad, incoming, slot):
        return jnp.zeros((shard_rows, model_width), jnp.bfloat16)

    def step(turn, carry):
        received, grad_store, qkv_store, incoming_store = carry
        slot_raw = turn - (sections - 1 - section_index)
        active = (slot_raw >= 0) & (slot_raw < micro_count)
        slot = jnp.clip(slot_raw, 0, micro_count - 1)
        incoming = jnp.where(
            section_index == sections - 1,
            lax.dynamic_index_in_dim(grad_top, slot, 0, False),
            received,
        )
        query_grad, owner_sum, far_part = lax.cond(
            active, attention_part, empty_attention, incoming, slot
        )
        for level in range(levels):
            owner_sum = owner_sum + shifted(far_part[level], "tm", -(2**level)).astype(jnp.float32)
        qkv_grad = jnp.concatenate([query_grad, owner_sum], 1).astype(jnp.bfloat16)
        grad_in = lax.cond(active, norm_part, empty_norm, qkv_grad, incoming, slot)
        sent_down = shifted(grad_in, "section", -1)
        grad_store = jnp.where(
            active, lax.dynamic_update_index_in_dim(grad_store, grad_in, slot, 0), grad_store
        )
        qkv_store = jnp.where(
            active, lax.dynamic_update_index_in_dim(qkv_store, qkv_grad, slot, 0), qkv_store
        )
        incoming_store = jnp.where(
            active,
            lax.dynamic_update_index_in_dim(incoming_store, incoming, slot, 0),
            incoming_store,
        )
        return (sent_down, grad_store, qkv_store, incoming_store)

    initial = (
        jnp.zeros((shard_rows, model_width), jnp.bfloat16),
        jnp.zeros((micro_count, shard_rows, model_width), jnp.bfloat16),
        jnp.zeros((micro_count, shard_rows, 3 * model_width), jnp.bfloat16),
        jnp.zeros((micro_count, shard_rows, model_width), jnp.bfloat16),
    )
    received, grad_store, qkv_store, incoming_store = lax.fori_loop(
        0, sections + micro_count - 1, step, initial
    )
    flat_norm = rounded_norm.reshape(-1, model_width)
    flat_attended = attended.reshape(-1, model_width)
    flat_qkv = qkv_store.reshape(-1, 3 * model_width)
    flat_incoming = incoming_store.reshape(-1, model_width)
    contract = (((0,), (0,)), ((), ()))
    first = lax.dot_general(flat_norm, flat_qkv, contract, preferred_element_type=jnp.float32)
    second = lax.dot_general(
        flat_attended, flat_incoming, contract, preferred_element_type=jnp.float32
    )
    summed = lax.psum_scatter(
        jnp.concatenate([first, second], 1).astype(jnp.bfloat16),
        "tm",
        scatter_dimension=0,
        tiled=True,
    ).astype(jnp.float32)
    return (
        grad_store[None],
        summed[None, :, : 3 * model_width],
        summed[None, :, 3 * model_width :],
    )


def side_by_side(transposed, pair):
    width = 2 * HEAD_DIM
    rows = transposed[pair * width : (pair + 1) * width]
    empty = jnp.zeros((HEAD_DIM, rows.shape[1]), rows.dtype)
    return jnp.concatenate(
        [
            jnp.concatenate([rows[:HEAD_DIM], empty], 0),
            jnp.concatenate([empty, rows[HEAD_DIM:]], 0),
        ],
        1,
    )


def one_above_other(rows, masks):
    return jnp.concatenate([rows * masks[0], rows * masks[1]], 0)


def head_masks():
    lane = lax.broadcasted_iota(jnp.int32, (1, 2 * HEAD_DIM), 1)
    return [
        jnp.where(lane < HEAD_DIM, 1.0, 0.0).astype(jnp.bfloat16),
        jnp.where(lane < HEAD_DIM, 0.0, 1.0).astype(jnp.bfloat16),
    ]


def key_bias_rows(flag_rows, levels, shard_rows, keys, first_query, count):
    key_at = lax.broadcasted_iota(jnp.int32, (keys, count), 0)
    query_at = lax.broadcasted_iota(jnp.int32, (keys, count), 1) + first_query
    gap = lax.div(query_at, shard_rows) - lax.div(key_at, shard_rows)
    allowed = (gap == 0) & (key_at <= query_at)
    for level in range(levels):
        allowed = allowed | ((gap == 2**level) & (flag_rows[level : level + 1] != 0))
    return jnp.where(allowed, 0.0, negative_fill)


def softmax_pass(queries, keys, values, bias, prob_ref, at_ref):
    queries_t = queries.T
    values_t = values.T
    width = 2 * HEAD_DIM
    count = queries.shape[0]
    for pair in range(queries.shape[1] // width):
        at_pair = slice(pair * width, (pair + 1) * width)
        scores = jnp.dot(
            keys[:, at_pair], side_by_side(queries_t, pair), preferred_element_type=jnp.float32
        )
        for half in range(2):
            at_half = slice(half * count, (half + 1) * count)
            biased = scores[:, at_half] + bias
            shifted_exp = jnp.exp(biased - jnp.max(biased, axis=0, keepdims=True))
            probability = shifted_exp * (1.0 / jnp.sum(shifted_exp, axis=0, keepdims=True))
            prob_ref[pair, :, at_half] = probability.astype(jnp.bfloat16)
    for head in range(queries.shape[1] // HEAD_DIM):
        at = slice(head * HEAD_DIM, (head + 1) * HEAD_DIM)
        at_half = slice(head % 2 * count, (head % 2 + 1) * count)
        at_ref[at] = jnp.dot(
            values_t[at], prob_ref[head // 2, :, at_half], preferred_element_type=jnp.float32
        ).astype(jnp.bfloat16)


def pack_kernel(
    levels, info_ref, acts_ref, top_ref, own_ref, other_ref, own_top_ref, other_top_ref, sems
):
    model_width = acts_ref.shape[2]
    shard_rows = own_ref.shape[0]
    side = info_ref[4]
    copies = [
        pltpu.make_async_copy(acts_ref.at[side], own_ref.at[:, :model_width], sems.at[0]),
        pltpu.make_async_copy(acts_ref.at[1 - side], other_ref.at[:, :model_width], sems.at[1]),
        pltpu.make_async_copy(top_ref.at[side], own_top_ref, sems.at[2]),
        pltpu.make_async_copy(top_ref.at[1 - side], other_top_ref, sems.at[3]),
    ]
    for copy in copies:
        copy.start()
    lane = lax.broadcasted_iota(jnp.int32, (shard_rows, own_ref.shape[1] - model_width), 1)
    flags = jnp.zeros(lane.shape, jnp.float32)
    for level in range(levels):
        seen = jnp.where(info_ref[5 + level] != 0, 1.0, 0.0)
        flags = jnp.where(lane == level, seen, flags)
    own_ref[:, model_width:] = flags.astype(jnp.bfloat16)
    other_ref[:, model_width:] = flags.astype(jnp.bfloat16)
    for copy in copies:
        copy.wait()


def touch_kernel(w_ref, after_ref, out_ref):
    out_ref[...] = w_ref[: out_ref.shape[0], : out_ref.shape[1]]


def project_kernel(replicas, info_ref, *refs):
    pieces = refs[: 4 * replicas]
    w_ref, _, normed_ref, rms_ref, norm_ref, flag_ref, q_ref, k_ref, v_ref, kt_ref, packed_ref = refs[
        4 * replicas :
    ]
    shards, shard_rows = packed_ref.shape[:2]
    model_width = w_ref.shape[0]
    seq = shards * shard_rows
    columns = q_ref.shape[1]
    at_piece = 0
    for core in (info_ref[0], 1 - info_ref[0]):
        for side in (info_ref[2], 1 - info_ref[2]):
            for step in range(replicas):
                shard = side * (shards // 2) + place_of(info_ref, step, replicas) + core
                packed_ref[shard] = pieces[at_piece][...]
                at_piece += 1
    for chunk in range(2):
        for step in range(replicas):
            shard = chunk * (shards // 2) + place_of(info_ref, step, replicas) + info_ref[0]
            normed, inverse_rms = normalize(packed_ref[shard][:, :model_width])
            normed_ref[chunk, step] = normed
            rms_ref[chunk, step] = jnp.broadcast_to(inverse_rms, rms_ref.shape[2:])
    normed, _ = normalize(packed_ref[:, :, :model_width].reshape(seq, model_width))
    rounded = normed.astype(jnp.bfloat16)
    norm_ref[...] = rounded
    flag_ref[...] = packed_ref[:, :, model_width:].reshape(seq, -1).astype(jnp.float32).T
    scale_factor = HEAD_DIM ** (-0.5)
    for block, out_ref in enumerate((q_ref, k_ref, v_ref)):
        first = pl.multiple_of(block * model_width + info_ref[0] * columns, 128)
        product = jnp.dot(
            rounded, w_ref[:, pl.ds(first, columns)], preferred_element_type=jnp.float32
        ).astype(jnp.bfloat16)
        out_ref[...] = product * scale_factor if block == 0 else product
    kt_ref[...] = (k_ref[...] * scale_factor).T


def upper_forward_kernel(
    levels, shard_rows, flag_ref, q_ref, k_ref, v_ref, prob_ref, at_ref
):
    seq = q_ref.shape[0]
    count = seq // 2
    bias = key_bias_rows(flag_ref[:, count:], levels, shard_rows, seq, count, count)
    softmax_pass(q_ref[count:], k_ref[...], v_ref[...], bias, prob_ref, at_ref)


def lower_forward_kernel(
    levels,
    shard_rows,
    info_ref,
    norm_ref,
    flag_ref,
    q_ref,
    k_ref,
    v_ref,
    after_ref,
    prob_ref,
    at_ref,
    gt_ref,
):
    seq = norm_ref.shape[0]
    count = seq // 2
    bias = key_bias_rows(flag_ref[:, :count], levels, shard_rows, count, 0, count)
    softmax_pass(q_ref[:count], k_ref[:count], v_ref[:count], bias, prob_ref, at_ref)
    rows = gt_ref.shape[0] // 4
    parity, x, y = info_ref[0], info_ref[1], info_ref[2]
    half = norm_ref.shape[1] // rows // 2
    for place, block in enumerate(
        (
            half * y + 2 * x + 1 - parity,
            half * y + 2 * x + parity,
            half * y + 2 * (1 - x) + 1 - parity,
            half * (1 - y) + 2 * x + parity,
        )
    ):
        first = pl.multiple_of(block * rows, 128)
        gt_ref[place * rows : (place + 1) * rows] = norm_ref[:, pl.ds(first, rows)].T


def place_of(info_ref, step, replicas):
    return 2 * lax.rem(info_ref[1] - step + replicas, replicas)


def merge_rows(info_ref, fresh, got_refs, kept_refs, out_refs, rows_ref):
    @pl.when(fresh)
    def _():
        for core, out_ref in enumerate(out_refs):
            out_ref[...] = got_refs[core][:, :, : out_ref.shape[2]]

    @pl.when(jnp.logical_not(fresh))
    def _():
        for out_ref, kept_ref in zip(out_refs, kept_refs):
            out_ref[...] = kept_ref[...]

    place_rows(info_ref, out_refs, rows_ref)


def place_rows(info_ref, out_refs, rows_ref):
    replicas = out_refs[0].shape[0]
    for step in range(replicas):
        place = place_of(info_ref, step, replicas)
        rows_ref[place + info_ref[0]] = out_refs[0][step]
        rows_ref[place + 1 - info_ref[0]] = out_refs[1][step]


def merge_tops(info_ref, upper, piece_refs, out_refs, rows_ref):
    replicas = out_refs[0].shape[0]
    own_chunk = info_ref[2] == (1 if upper else 0)
    for core in range(2):
        refs = piece_refs[2 * replicas * core : 2 * replicas * (core + 1)]

        @pl.when(own_chunk)
        def _():
            for step in range(replicas):
                out_refs[core][step] = refs[step][...]

        @pl.when(jnp.logical_not(own_chunk))
        def _():
            for step in range(replicas):
                out_refs[core][step] = refs[replicas + step][...]

    place_rows(info_ref, out_refs, rows_ref)


def backward_kernel(upper, tops, last, fresh_section, info_ref, *refs):
    refs = list(refs)
    got = tops or 4
    got_refs = refs[:got]
    w_ref, prob_ref, q_ref, v_ref, kt_ref, at_ref = refs[got : got + 6]
    refs = refs[got + 6 :]
    if not upper:
        key_sum_ref, value_sum_ref = refs[:2]
        refs = refs[2:]
    refs = refs[1:]
    if last:
        refs = [refs[0], refs[-1], *refs[1:-1]]
    own_ref, other_ref, keep_ref = refs[:3]
    send_refs = refs[3 : 3 + len(SPLITS[upper])]
    refs = refs[3 + len(send_refs) :]
    if upper:
        key_sum_ref, value_sum_ref = refs[:2]
        refs = refs[2:]
    grads_ref, rows_ref, scores_ref = refs
    replicas, shard_rows, model_width = own_ref.shape
    count = rows_ref.shape[0] * shard_rows
    keys = prob_ref.shape[1]
    parity = info_ref[0]
    columns = q_ref.shape[1]
    width = 2 * HEAD_DIM
    if tops:
        merge_tops(info_ref, upper, got_refs, (own_ref, other_ref), rows_ref)
    else:
        fresh = info_ref[3] == fresh_section
        merge_rows(info_ref, fresh, got_refs[:-2], got_refs[-2:], (own_ref, other_ref), rows_ref)
    rows = rows_ref[...].reshape(count, model_width)
    weights = w_ref[pl.ds(pl.multiple_of(parity * columns, 128), columns), :]
    over_width = (((1,), (1,)), ((), ()))
    upstream = lax.dot_general(
        rows, weights, over_width, preferred_element_type=jnp.float32
    ).astype(jnp.bfloat16)
    upstream_t = upstream.T
    product_t = upstream_t.astype(jnp.float32) * at_ref[...].astype(jnp.float32)
    first_query = keys - count
    masks = head_masks()

    def put(block, pair, part):
        first = block * columns + pair * width
        grads_ref[:, :, first : first + width] = part.astype(jnp.bfloat16).reshape(
            -1, shard_rows, width
        )

    for pair in range(columns // width):
        at_pair = slice(pair * width, (pair + 1) * width)
        prob_grad = jnp.dot(
            v_ref[:keys, at_pair], side_by_side(upstream_t, pair), preferred_element_type=jnp.float32
        )
        for half in range(2):
            at_half = slice(half * count, (half + 1) * count)
            first = pair * width + half * HEAD_DIM
            delta = jnp.sum(product_t[first : first + HEAD_DIM], axis=0, keepdims=True)
            scores_ref[pair, :, at_half] = (
                prob_ref[pair, :, at_half].astype(jnp.float32) * (prob_grad[:, at_half] - delta)
            ).astype(jnp.bfloat16)
        value_grad = jnp.dot(
            prob_ref[pair],
            one_above_other(upstream[:, at_pair], masks),
            preferred_element_type=jnp.float32,
        )
        if upper:
            value_sum_ref[:, at_pair] = value_grad[:first_query]
            value_grad = value_grad[first_query:]
        else:
            value_grad = value_grad + value_sum_ref[:, at_pair]
        put(2, pair, value_grad)
    for pair in range(columns // width):
        at_pair = slice(pair * width, (pair + 1) * width)
        queries = q_ref[first_query : first_query + count, at_pair]
        key_grad = jnp.dot(
            scores_ref[pair], one_above_other(queries, masks), preferred_element_type=jnp.float32
        )
        if upper:
            key_sum_ref[:, at_pair] = key_grad[:first_query]
            key_grad = key_grad[first_query:]
        else:
            key_grad = key_grad + key_sum_ref[:, at_pair]
        put(1, pair, key_grad)
        query_grad = [
            jnp.dot(
                kt_ref[pair * width + half * HEAD_DIM : pair * width + (half + 1) * HEAD_DIM, :keys],
                scores_ref[pair, :, half * count : (half + 1) * count],
                preferred_element_type=jnp.float32,
            )
            for half in range(2)
        ]
        put(0, pair, jnp.concatenate(query_grad, 0).astype(jnp.bfloat16).T)
    for step in range(replicas):
        place = place_of(info_ref, step, replicas)
        keep_ref[step] = grads_ref[place + parity]
        crossing = grads_ref[place + 1 - parity]
        first = 0
        for send_ref in send_refs:
            send_ref[step] = crossing[:, first : first + send_ref.shape[2]]
            first += send_ref.shape[2]


def norm_product(part, w_ref, half):
    columns = part.shape[1] // 3
    model_width = w_ref.shape[0]
    total = jnp.zeros((part.shape[0], model_width), jnp.float32)
    for block in range(3):
        first = pl.multiple_of(block * model_width + half * columns, 128)
        total += lax.dot_general(
            part[:, block * columns : (block + 1) * columns],
            w_ref[:, pl.ds(first, columns)],
            (((1,), (1,)), ((), ())),
            preferred_element_type=jnp.float32,
        )
    return total


def norm_part_kernel(info_ref, keep_ref, w_ref, after_ref, out_ref):
    part = keep_ref[...].reshape(out_ref.shape[0], -1)
    out_ref[...] = norm_product(part, w_ref, info_ref[0])


def norm_kernel(upper, info_ref, keep_ref, normed_ref, rms_ref, incoming_ref, w_ref, *refs):
    got_refs = refs[: len(SPLITS[upper])]
    out_refs = refs[len(got_refs) :]
    model_width = w_ref.shape[0]
    replicas, shard_rows = incoming_ref.shape[:2]
    rows = replicas * shard_rows
    got = [got_ref[...].reshape(rows, -1) for got_ref in got_refs]
    norm_grad = norm_product(jnp.concatenate(got, 1), w_ref, 1 - info_ref[0])
    norm_grad += (
        keep_ref[...]
        if upper
        else norm_product(keep_ref[...].reshape(rows, -1), w_ref, info_ref[0])
    )
    chunk = 1 if upper else 0
    normed = normed_ref[chunk].reshape(rows, model_width)
    inverse_rms = rms_ref[chunk].reshape(rows, -1)[:, :1]
    inner = jnp.mean(norm_grad * normed, axis=-1, keepdims=True)
    incoming = incoming_ref[...].reshape(rows, model_width).astype(jnp.float32)
    grad_in = incoming + inverse_rms * (norm_grad - normed * inner)
    grad_in = grad_in.astype(jnp.bfloat16).reshape(replicas, shard_rows, model_width)
    out_refs[-1][:, :, :model_width] = grad_in
    spare = out_refs[-1].shape[2] - model_width
    if spare:
        out_refs[-1][:, :, model_width:] = jnp.zeros((replicas, shard_rows, spare), jnp.bfloat16)


def in_terms(gt_ref, grad_refs, half, rows):
    count = grad_refs[0].shape[0] * grad_refs[0].shape[1]
    return sum(
        jnp.dot(
            gt_ref[2 * half * rows : 2 * (half + 1) * rows, chunk * count : (chunk + 1) * count],
            part_ref[...].reshape(count, -1),
            preferred_element_type=jnp.float32,
        )
        for chunk, part_ref in enumerate(grad_refs)
    )


def send_kernel(gt_ref, lower_ref, upper_ref, pass_ref, keep_ref):
    rows = pass_ref.shape[0]
    total = in_terms(gt_ref, (lower_ref, upper_ref), 1, rows)
    pass_ref[...] = total[:rows].astype(jnp.bfloat16)
    keep_ref[...] = total[rows:].astype(jnp.bfloat16)


def term_kernel(info_ref, gt_ref, *refs):
    grad_refs, at_refs, row_refs = refs[:2], refs[2:4], refs[4:6]
    pass_ref, keep_ref, out_pass_ref, out_keep_ref, out_send_ref = refs[7:]
    rows = pass_ref.shape[0]
    width = out_send_ref.shape[1]
    parity, x, y = info_ref[0], info_ref[1], info_ref[2]
    sent = jnp.where(parity == y, 2 * (1 - x) + 1 - parity, 2 * x + parity)
    blocks = (sent, 2 * x + 1 - parity, 2 * x + parity)
    total = jnp.zeros((3 * rows, width), jnp.float32)
    for at_ref, part_ref in zip(at_refs, row_refs):
        picked = [at_ref[pl.ds(pl.multiple_of(block * rows, 128), rows)] for block in blocks]
        total += jnp.dot(
            jnp.concatenate(picked, 0),
            part_ref[...].reshape(-1, width),
            preferred_element_type=jnp.float32,
        )
    out_send_ref[...] = total[:rows].astype(jnp.bfloat16)
    out_pass_ref[...] = total[rows : 2 * rows]
    out_keep_ref[...] = total[2 * rows :]
    total = in_terms(gt_ref, grad_refs, 0, rows)
    pass_ref[...] = total[:rows]
    keep_ref[...] = total[rows:]


def sum_kernel(own_ref, got_ref, out_own_ref, out_got_ref, after_ref, sum_ref):
    columns = own_ref.shape[1]
    sum_ref[:, :columns] = (own_ref[...] + got_ref[...].astype(jnp.float32)).astype(jnp.bfloat16)
    sum_ref[:, columns:] = (out_own_ref[...] + out_got_ref[...].astype(jnp.float32)).astype(
        jnp.bfloat16
    )


def pick_kernel(info_ref, upper_ref, lower_ref, out_ref):
    crossing = info_ref[0] == 0
    for step in range(2):
        for chunk, part_ref in enumerate((lower_ref, upper_ref)):
            wanted = info_ref[2] == (chunk if step == 1 else 1 - chunk)

            @pl.when(wanted & (crossing if step == 1 else jnp.logical_not(crossing)))
            def _():
                out_ref[...] = part_ref[step]


def join_kernel(info_ref, upper_ref, lower_ref, got_ref, out_ref):
    micro = info_ref[4]
    out_ref[0, 1 - micro] = got_ref[...]

    @pl.when(info_ref[2] == 1)
    def _():
        out_ref[0, micro] = upper_ref[0]

    @pl.when(info_ref[2] != 1)
    def _():
        out_ref[0, micro] = lower_ref[0]


def place_kernel(
    info_ref, own_ref, got_ref, out_own_ref, out_got_ref, sibling_ref, d_in_ref, d_out_ref
):
    columns = own_ref.shape[1] // 3
    own = own_ref[...] + got_ref[...].astype(jnp.float32)
    sibling = sibling_ref[:, : 3 * columns].astype(jnp.float32)
    for part, half in ((own, info_ref[0]), (sibling, 1 - info_ref[0])):
        for block in range(3):
            first = pl.multiple_of((2 * block + half) * columns, 128)
            d_in_ref[:, pl.ds(first, columns)] = part[:, block * columns : (block + 1) * columns]
    owner = info_ref[0] == info_ref[2]

    @pl.when(owner)
    def _():
        d_out_ref[...] = out_own_ref[...] + out_got_ref[...].astype(jnp.float32)

    @pl.when(jnp.logical_not(owner))
    def _():
        d_out_ref[...] = sibling_ref[:, 3 * columns :].astype(jnp.float32)


def call(kernel, outs, operands, scratch=(), flops=0, scalars=1, after=None, mebibytes=5, far=0):
    in_specs = [pl.BlockSpec(memory_space=pltpu.SMEM)] * scalars
    in_specs += [pl.BlockSpec(memory_space=pltpu.HBM)] * far
    in_specs += [pl.BlockSpec(memory_space=pltpu.VMEM)] * (len(operands) - scalars - far)
    if after is not None:
        operands = [*operands, after]
        in_specs.append(pl.BlockSpec(memory_space=pl.ANY))
    return pl.pallas_call(
        kernel,
        out_shape=list(outs),
        in_specs=in_specs,
        out_specs=[pl.BlockSpec(memory_space=pltpu.VMEM)] * len(outs),
        scratch_shapes=list(scratch),
        cost_estimate=pl.CostEstimate(flops=1, bytes_accessed=1, transcendentals=0),
        compiler_params=pltpu.CompilerParams(vmem_limit_bytes=mebibytes * 2**20),
    )(*operands)


def by_chips(acts, grad_top, w_in, w_out, offsets):
    half_type, full_type = jnp.bfloat16, jnp.float32
    shape = jax.ShapeDtypeStruct
    sections = lax.axis_size("section")
    shards = lax.axis_size("tm")
    levels = offsets.shape[1]
    half = shards // 2
    replicas = half // 2
    me = lax.axis_index("tm")
    parity = lax.rem(me, 2)
    side = lax.div(me, half)
    micro_count, shard_rows, model_width = acts.shape[1:]
    columns = model_width // 2
    heads = columns // HEAD_DIM
    seq = shards * shard_rows
    count = seq // 2
    w_qkv = w_in[0]
    w_rows = w_out[0]
    beside = lax.div(lax.rem(me, half), 2)
    micro = lax.rem(side + beside, 2)
    info = jnp.stack([parity, beside, side, lax.axis_index("section"), micro])
    info = jnp.concatenate([info.astype(jnp.int32), offsets[0]])

    def swapped(value, bits, chosen=None):
        pairs = [(device, device ^ bits) for device in range(shards)]
        pairs = [pair for pair in pairs if chosen is None or chosen(pair[0])]
        return lax.ppermute(value, "tm", pairs)

    core, near, far = 1, 2, half

    packed = shape((shard_rows, model_width + 128), half_type)
    top_shape = shape((shard_rows, model_width), half_type)
    own_acts, other_acts, own_top, other_top = call(
        functools.partial(pack_kernel, levels),
        [packed, packed, top_shape, top_shape],
        [info, acts[0], grad_top],
        scratch=[pltpu.SemaphoreType.DMA((4,))],
        far=2,
    )
    (touched,) = call(
        touch_kernel, [shape((16, 128), half_type)], [w_qkv], scalars=0, after=own_acts
    )
    pieces = [own_acts, swapped(other_acts, near), swapped(other_acts, far)]
    pieces += [swapped(own_acts, near + far)]
    tops = [own_top, swapped(other_top, near), swapped(other_top, far)]
    pieces[-1], tops, touched = lax.optimization_barrier((pieces[-1], tops, touched))
    tops += [swapped(own_top, near + far)]
    pieces += [swapped(piece, core) for piece in pieces]

    rows_shape = shape((seq, columns), half_type)
    normed, rms, norm, flag_rows, queries, keys, values, keys_t = call(
        functools.partial(project_kernel, replicas),
        [
            shape((2, replicas, shard_rows, model_width), full_type),
            shape((2, replicas, shard_rows, 128), full_type),
            shape((seq, model_width), half_type),
            shape((128, seq), full_type),
            rows_shape,
            rows_shape,
            rows_shape,
            shape((columns, seq), half_type),
        ],
        [info, *pieces, w_qkv],
        scratch=[pltpu.VMEM((shards, *packed.shape), half_type)],
        flops=6 * seq * model_width * columns,
        after=touched,
    )
    tops, _ = lax.optimization_barrier((tuple(tops), keys_t))
    tops = [*tops, *[swapped(piece, core) for piece in tops]]
    pairs = heads // 2
    upper_prob, upper_at = call(
        functools.partial(upper_forward_kernel, levels, shard_rows),
        [
            shape((pairs, seq, 2 * count), half_type),
            shape((columns, count), half_type),
        ],
        [flag_rows, queries, keys, values],
        scalars=0,
        flops=4 * columns * seq * count,
    )
    own_rows = model_width // shards
    probs, attended = {True: upper_prob}, {True: upper_at}
    got, kept = {}, {}
    piece_shape = shape((replicas, shard_rows, model_width), half_type)
    wide_shape = shape((replicas, shard_rows, model_width + 128), half_type)
    grads_shape = shape((replicas, shard_rows, 3 * columns), half_type)
    sum_shape = shape((count, columns), full_type)
    full_grads = shape((half, shard_rows, 3 * columns), half_type)
    full_rows = shape((half, shard_rows, model_width), half_type)
    term_shape = (own_rows, 3 * columns)
    rows_scratch = pltpu.VMEM(full_rows.shape, half_type)
    grads_scratch = pltpu.VMEM(full_grads.shape, half_type)
    result, full, ordered = {}, {}, {}
    for turn in range(sections):
        last = turn + 1 == sections
        fresh_section = sections - 1 - turn
        sums, parts, crossed = [], {}, {}

        def norm_step(upper, after):
            (result[upper],) = call(
                functools.partial(norm_kernel, upper),
                [piece_shape if upper or last else wide_shape],
                [info, parts[upper], normed, rms, kept[upper][0], w_qkv, *crossed[upper]],
                after=after,
            )
            if not last:
                hop = [(sections - 1 - turn, sections - 2 - turn)]
                got[upper] = lax.ppermute(result[upper], "section", hop)

        for upper in (True, False):
            rows_in, after = tops, keys_t if upper else result.get(True)
            if turn:
                before = result[False] if upper else parts[True]
                got[upper], after = lax.optimization_barrier((got[upper], before))
                if not upper:
                    parts[True] = after
                rows_in = [got[upper], swapped(got[upper], core), *kept[upper]]
            unit = 3 * columns // sum(SPLITS[upper])
            cross = [shape((replicas, shard_rows, part * unit), half_type) for part in SPLITS[upper]]
            outs = [piece_shape] * (1 if last else 2) + [grads_shape, *cross]
            outs += [sum_shape, sum_shape] if upper else []
            scratch = []
            if last:
                outs += [full_grads]
            else:
                scratch += [grads_scratch]
            if last:
                outs += [full_rows]
            else:
                scratch += [rows_scratch]
            part_keys = seq if upper else count
            scratch += [pltpu.VMEM((pairs, part_keys, 2 * count), half_type)]
            if last:
                scratch += [pltpu.VMEM(piece_shape.shape, half_type)]
            answer = call(
                functools.partial(
                    backward_kernel, upper, 0 if turn else len(tops), last, fresh_section
                ),
                outs,
                [info, *rows_in, w_rows, probs[upper], queries, values, keys_t]
                + [attended[upper], *sums],
                scratch=scratch,
                flops=2 * count * columns * (2 * model_width + 4 * part_keys),
                after=after,
            )
            kept[upper] = tuple(answer[:2])
            answer = answer[1 if last else 2 :]
            keep = answer[0]
            send = answer[1 : 1 + len(cross)]
            parts[upper] = keep
            if upper:
                sums = answer[1 + len(cross) : 3 + len(cross)]
                (parts[True],) = call(
                    norm_part_kernel,
                    [shape((replicas * shard_rows, model_width), full_type)],
                    [info, keep, w_qkv],
                    flops=3 * replicas * shard_rows * model_width * model_width,
                    after=keep,
                )
                if turn == 0:
                    lower_prob, lower_at, norm_t = call(
                        functools.partial(lower_forward_kernel, levels, shard_rows),
                        [
                            shape((pairs, count, 2 * count), half_type),
                            shape((columns, count), half_type),
                            shape((4 * own_rows, seq), half_type),
                        ],
                        [info, norm, flag_rows, queries, keys, values],
                        flops=4 * columns * count * count,
                        after=parts[True],
                    )
                    probs[False], attended[False] = lower_prob, lower_at
            if last:
                full[upper], ordered[upper] = answer[-2:]
            crossed[upper] = [swapped(piece, core) for piece in send]
            if upper:
                norm_step(True, keep)
        if last:
            send_pass, send_keep = call(
                send_kernel,
                [shape(term_shape, half_type)] * 2,
                [norm_t, full[False], full[True]],
                scalars=0,
            )
            terms = call(
                term_kernel,
                [shape(term_shape, full_type)] * 2
                + [shape((own_rows, model_width), full_type)] * 2
                + [shape((own_rows, model_width), half_type)],
                [info, norm_t, full[False], full[True], attended[False], attended[True]]
                + [ordered[False], ordered[True]],
                after=send_keep,
            )
        norm_step(False, terms[4] if last else result[True])

    in_pass, in_keep, out_pass, out_keep, out_send = terms
    got_pass = swapped(send_pass, near)
    got_keep = swapped(send_keep, far)
    own_rows_grad = [result[True], result[False]]
    (theirs,) = call(pick_kernel, [top_shape], [info, *own_rows_grad])
    to_owner = [(device, device ^ (far if device % 2 else near)) for device in range(shards)]
    partner = lax.ppermute(theirs, "tm", to_owner)
    got_out_pass = swapped(out_send, near, lambda device: device // half == device % 2)
    got_out_keep = swapped(out_send, far, lambda device: device // half != device % 2)
    _, _, done = lax.optimization_barrier((got_keep, got_out_keep, partner))
    (summed,) = call(
        sum_kernel,
        [shape((own_rows, 3 * columns + model_width), half_type)],
        [in_pass, got_pass, out_pass, got_out_pass],
        scalars=0,
        after=done,
    )
    d_w_in, d_w_out = call(
        place_kernel,
        [
            shape((own_rows, 3 * model_width), full_type),
            shape((own_rows, model_width), full_type),
        ],
        [info, in_keep, got_keep, out_keep, got_out_keep, swapped(summed, core)],
    )
    (d_acts,) = call(
        join_kernel, [shape(acts.shape, half_type)], [info, *own_rows_grad, partner]
    )
    return (d_acts, d_w_in[None], d_w_out[None])


def layer_gradients(acts, grad_top, w_in, w_out, offsets):
    shards = lax.axis_size("tm")
    micro_count, shard_rows, model_width = acts.shape[1:]
    heads = model_width // HEAD_DIM
    prob_bytes = 2 * heads * (shards * shard_rows) ** 2
    fits = prob_bytes <= 2**24 and model_width % (128 * shards) == 0 and shard_rows % 16 == 0
    square = shards % 4 == 0 and shards // 4 == 2
    if micro_count == 2 and square and heads % 4 == 0 and fits:
        return by_chips(acts, grad_top, w_in, w_out, offsets)
    return per_device(acts, grad_top, w_in, w_out, offsets)


def solution(mesh):
    placed = (
        P("section", None, "tm", None),
        P(None, "tm", None),
        P("section", None, None),
        P("section", None, None),
        P("tm", None),
    )
    return jax.shard_map(
        layer_gradients,
        mesh=mesh,
        in_specs=placed,
        out_specs=(
            P("section", None, "tm", None),
            P("section", "tm", None),
            P("section", "tm", None),
        ),
        check_vma=False,
    )
```

```python
import functools
import jax
import jax.numpy as jnp
from jax import lax
from jax.experimental import pallas as pl
from jax.experimental.pallas import tpu as pltpu
from jax.sharding import PartitionSpec as P

HEAD_DIM = 64


epsilon = 1e-06
PIECES = {True: 2, False: 2}
negative_fill = -1e30


def shifted(value, axis, steps):
    count = lax.axis_size(axis)
    initial, last = (max(0, -steps), min(count, count - steps))
    return lax.ppermute(value, axis, [(source, source + steps) for source in range(initial, last)])


def normalize(inputs):
    values = inputs.astype(jnp.float32)
    inverse_rms = lax.rsqrt(jnp.mean(values * values, axis=-1, keepdims=True) + epsilon)
    return (values * inverse_rms, inverse_rms)


def key_bias(level_flags, shard_rows):
    position = jnp.arange(shard_rows)
    own_part = position[None, :] <= position[:, None]
    far_part = jnp.repeat(level_flags != 0, shard_rows)
    far_part = jnp.broadcast_to(far_part[None, :], (shard_rows, far_part.shape[0]))
    return jnp.concatenate([own_part, far_part], 1)


def split_heads(row_block):
    return row_block.reshape(row_block.shape[0], -1, HEAD_DIM)


def softmax_keys(queries, key_heads, allowed):
    scores = jnp.einsum(
        "ihd,jhd->hij", queries, key_heads, preferred_element_type=jnp.float32
    ) * HEAD_DIM ** (-0.5)
    scores = jnp.where(allowed[None], scores, negative_fill)
    highest = jnp.max(scores, axis=-1, keepdims=True)
    shifted_exp = jnp.where(allowed[None], jnp.exp(scores - highest), 0.0)
    return shifted_exp / jnp.sum(shifted_exp, axis=-1, keepdims=True)


def attend(query_rows, key_rows, allowed):
    model_width = query_rows.shape[1]
    probability = softmax_keys(
        split_heads(query_rows), split_heads(key_rows[:, :model_width]), allowed
    )
    attended = jnp.einsum(
        "hij,jhd->ihd",
        probability.astype(jnp.bfloat16),
        split_heads(key_rows[:, model_width:]),
        preferred_element_type=jnp.float32,
    )
    return attended.reshape(query_rows.shape).astype(jnp.bfloat16)


def attend_back(query_rows, key_rows, allowed, incoming, attended, w_proj):
    model_width = query_rows.shape[1]
    queries = split_heads(query_rows)
    key_heads = split_heads(key_rows[:, :model_width])
    value_heads = split_heads(key_rows[:, model_width:])
    probability = softmax_keys(queries, key_heads, allowed)
    rounded = probability.astype(jnp.bfloat16)
    upstream = lax.dot_general(
        incoming, w_proj, (((1,), (1,)), ((), ())), preferred_element_type=jnp.float32
    ).astype(jnp.bfloat16)
    up_heads = split_heads(upstream)
    delta = jnp.einsum(
        "ihd,ihd->hi", up_heads.astype(jnp.float32), split_heads(attended).astype(jnp.float32)
    )[..., None]
    prob_grad = jnp.einsum(
        "ihd,jhd->hij", up_heads, value_heads, preferred_element_type=jnp.float32
    )
    score_grad = (probability * (prob_grad - delta)).astype(jnp.bfloat16)
    scale_factor = HEAD_DIM ** (-0.5)
    query_grad = (
        jnp.einsum("hij,jhd->ihd", score_grad, key_heads, preferred_element_type=jnp.float32)
        * scale_factor
    )
    key_grad = (
        jnp.einsum("hij,ihd->jhd", score_grad, queries, preferred_element_type=jnp.float32)
        * scale_factor
    )
    value_grad = jnp.einsum("hij,ihd->jhd", rounded, up_heads, preferred_element_type=jnp.float32)
    return (
        query_grad.reshape(-1, model_width),
        key_grad.reshape(-1, model_width),
        value_grad.reshape(-1, model_width),
    )


def per_device(acts, grad_top, w_in, w_out, offsets):
    sections = lax.axis_size("section")
    shards = lax.axis_size("tm")
    levels = shards.bit_length() - 1
    section_index = lax.axis_index("section")
    micro_count = acts.shape[1]
    shard_rows = acts.shape[2]
    model_width = acts.shape[3]
    w_qkv = w_in[0]
    w_proj = w_out[0]
    level_flags = offsets[0]
    normed, inverse_rms = normalize(acts[0])
    rounded_norm = normed.astype(jnp.bfloat16)
    qkv = jnp.dot(rounded_norm.reshape(-1, model_width), w_qkv, preferred_element_type=jnp.float32)
    qkv = qkv.astype(jnp.bfloat16).reshape(micro_count, shard_rows, 3 * model_width)
    pairs = qkv[..., model_width:]
    far_list = [shifted(pairs, "tm", 2**level) for level in range(levels)]
    key_rows = jnp.concatenate([pairs] + far_list, 1)
    allowed = key_bias(level_flags, shard_rows)
    attended = jnp.stack(
        [
            attend(qkv[index, :, :model_width], key_rows[index], allowed)
            for index in range(micro_count)
        ],
        0,
    )

    def attention_part(incoming, slot):
        query_rows = lax.dynamic_index_in_dim(qkv, slot, 0, False)[:, :model_width]
        slot_keys = lax.dynamic_index_in_dim(key_rows, slot, 0, False)
        slot_attended = lax.dynamic_index_in_dim(attended, slot, 0, False)
        query_grad, key_grad, value_grad = attend_back(
            query_rows, slot_keys, allowed, incoming, slot_attended, w_proj
        )
        owner_sum = jnp.concatenate([key_grad[:shard_rows], value_grad[:shard_rows]], 1)
        far_part = jnp.concatenate([key_grad[shard_rows:], value_grad[shard_rows:]], 1)
        far_part = far_part.astype(jnp.bfloat16).reshape(levels, shard_rows, 2 * model_width)
        return (query_grad, owner_sum, far_part)

    def empty_attention(incoming, slot):
        return (
            jnp.zeros((shard_rows, model_width), jnp.float32),
            jnp.zeros((shard_rows, 2 * model_width), jnp.float32),
            jnp.zeros((levels, shard_rows, 2 * model_width), jnp.bfloat16),
        )

    def norm_part(qkv_grad, incoming, slot):
        norm_grad = lax.dot_general(
            qkv_grad, w_qkv, (((1,), (1,)), ((), ())), preferred_element_type=jnp.float32
        )
        slot_normed = lax.dynamic_index_in_dim(normed, slot, 0, False)
        slot_rms = lax.dynamic_index_in_dim(inverse_rms, slot, 0, False)
        inner = jnp.mean(norm_grad * slot_normed, axis=-1, keepdims=True)
        return (incoming.astype(jnp.float32) + slot_rms * (norm_grad - slot_normed * inner)).astype(
            jnp.bfloat16
        )

    def empty_norm(qkv_grad, incoming, slot):
        return jnp.zeros((shard_rows, model_width), jnp.bfloat16)

    def step(turn, carry):
        received, grad_store, qkv_store, incoming_store = carry
        slot_raw = turn - (sections - 1 - section_index)
        active = (slot_raw >= 0) & (slot_raw < micro_count)
        slot = jnp.clip(slot_raw, 0, micro_count - 1)
        incoming = jnp.where(
            section_index == sections - 1,
            lax.dynamic_index_in_dim(grad_top, slot, 0, False),
            received,
        )
        query_grad, owner_sum, far_part = lax.cond(
            active, attention_part, empty_attention, incoming, slot
        )
        for level in range(levels):
            owner_sum = owner_sum + shifted(far_part[level], "tm", -(2**level)).astype(jnp.float32)
        qkv_grad = jnp.concatenate([query_grad, owner_sum], 1).astype(jnp.bfloat16)
        grad_in = lax.cond(active, norm_part, empty_norm, qkv_grad, incoming, slot)
        sent_down = shifted(grad_in, "section", -1)
        grad_store = jnp.where(
            active, lax.dynamic_update_index_in_dim(grad_store, grad_in, slot, 0), grad_store
        )
        qkv_store = jnp.where(
            active, lax.dynamic_update_index_in_dim(qkv_store, qkv_grad, slot, 0), qkv_store
        )
        incoming_store = jnp.where(
            active,
            lax.dynamic_update_index_in_dim(incoming_store, incoming, slot, 0),
            incoming_store,
        )
        return (sent_down, grad_store, qkv_store, incoming_store)

    initial = (
        jnp.zeros((shard_rows, model_width), jnp.bfloat16),
        jnp.zeros((micro_count, shard_rows, model_width), jnp.bfloat16),
        jnp.zeros((micro_count, shard_rows, 3 * model_width), jnp.bfloat16),
        jnp.zeros((micro_count, shard_rows, model_width), jnp.bfloat16),
    )
    received, grad_store, qkv_store, incoming_store = lax.fori_loop(
        0, sections + micro_count - 1, step, initial
    )
    flat_norm = rounded_norm.reshape(-1, model_width)
    flat_attended = attended.reshape(-1, model_width)
    flat_qkv = qkv_store.reshape(-1, 3 * model_width)
    flat_incoming = incoming_store.reshape(-1, model_width)
    contract = (((0,), (0,)), ((), ()))
    first = lax.dot_general(flat_norm, flat_qkv, contract, preferred_element_type=jnp.float32)
    second = lax.dot_general(
        flat_attended, flat_incoming, contract, preferred_element_type=jnp.float32
    )
    summed = lax.psum_scatter(
        jnp.concatenate([first, second], 1).astype(jnp.bfloat16),
        "tm",
        scatter_dimension=0,
        tiled=True,
    ).astype(jnp.float32)
    return (
        grad_store[None],
        summed[None, :, : 3 * model_width],
        summed[None, :, 3 * model_width :],
    )


def side_by_side(transposed, pair):
    width = 2 * HEAD_DIM
    rows = transposed[pair * width : (pair + 1) * width]
    empty = jnp.zeros((HEAD_DIM, rows.shape[1]), rows.dtype)
    return jnp.concatenate(
        [
            jnp.concatenate([rows[:HEAD_DIM], empty], 0),
            jnp.concatenate([empty, rows[HEAD_DIM:]], 0),
        ],
        1,
    )


def one_above_other(rows, masks):
    return jnp.concatenate([rows * masks[0], rows * masks[1]], 0)


def head_masks():
    lane = lax.broadcasted_iota(jnp.int32, (1, 2 * HEAD_DIM), 1)
    return [
        jnp.where(lane < HEAD_DIM, 1.0, 0.0).astype(jnp.bfloat16),
        jnp.where(lane < HEAD_DIM, 0.0, 1.0).astype(jnp.bfloat16),
    ]


def key_bias_rows(flag_rows, levels, shard_rows, keys, first_query, count):
    key_at = lax.broadcasted_iota(jnp.int32, (keys, count), 0)
    query_at = lax.broadcasted_iota(jnp.int32, (keys, count), 1) + first_query
    gap = lax.div(query_at, shard_rows) - lax.div(key_at, shard_rows)
    allowed = (gap == 0) & (key_at <= query_at)
    for level in range(levels):
        allowed = allowed | ((gap == 2**level) & (flag_rows[level : level + 1] != 0))
    return jnp.where(allowed, 0.0, negative_fill)


def softmax_pass(queries, keys, values, bias, prob_ref, at_ref):
    queries_t = queries.T
    values_t = values.T
    width = 2 * HEAD_DIM
    count = queries.shape[0]
    for pair in range(queries.shape[1] // width):
        at_pair = slice(pair * width, (pair + 1) * width)
        scores = jnp.dot(
            keys[:, at_pair], side_by_side(queries_t, pair), preferred_element_type=jnp.float32
        )
        for half in range(2):
            at_half = slice(half * count, (half + 1) * count)
            biased = scores[:, at_half] + bias
            shifted_exp = jnp.exp(biased - jnp.max(biased, axis=0, keepdims=True))
            probability = shifted_exp * (1.0 / jnp.sum(shifted_exp, axis=0, keepdims=True))
            prob_ref[pair, :, at_half] = probability.astype(jnp.bfloat16)
    for head in range(queries.shape[1] // HEAD_DIM):
        at = slice(head * HEAD_DIM, (head + 1) * HEAD_DIM)
        at_half = slice(head % 2 * count, (head % 2 + 1) * count)
        at_ref[at] = jnp.dot(
            values_t[at], prob_ref[head // 2, :, at_half], preferred_element_type=jnp.float32
        ).astype(jnp.bfloat16)


def pack_kernel(
    levels, info_ref, acts_ref, top_ref, own_ref, other_ref, own_top_ref, other_top_ref
):
    model_width = acts_ref.shape[2]
    shard_rows = own_ref.shape[0]
    micro = info_ref[4]
    lane = lax.broadcasted_iota(jnp.int32, (shard_rows, own_ref.shape[1] - model_width), 1)
    flags = jnp.zeros(lane.shape, jnp.float32)
    for level in range(levels):
        seen = jnp.where(info_ref[5 + level] != 0, 1.0, 0.0)
        flags = jnp.where(lane == level, seen, flags)
    for at, out_ref, out_top_ref in (
        (micro, own_ref, own_top_ref),
        (1 - micro, other_ref, other_top_ref),
    ):
        out_ref[:, :model_width] = acts_ref[at]
        out_ref[:, model_width:] = flags.astype(jnp.bfloat16)
        out_top_ref[...] = top_ref[at]


def touch_kernel(w_ref, after_ref, out_ref):
    out_ref[...] = w_ref[: out_ref.shape[0], : out_ref.shape[1]]


def project_kernel(replicas, info_ref, *refs):
    pieces = refs[: 4 * replicas]
    w_ref, _, normed_ref, rms_ref, norm_ref, flag_ref, q_ref, k_ref, v_ref, kt_ref, packed_ref = refs[
        4 * replicas :
    ]
    shards, shard_rows = packed_ref.shape[:2]
    model_width = w_ref.shape[0]
    seq = shards * shard_rows
    columns = q_ref.shape[1]
    at_piece = 0
    for core in (info_ref[0], 1 - info_ref[0]):
        for side in (info_ref[2], 1 - info_ref[2]):
            for step in range(replicas):
                shard = side * (shards // 2) + place_of(info_ref, step, replicas) + core
                packed_ref[shard] = pieces[at_piece][...]
                at_piece += 1
    for chunk in range(2):
        for step in range(replicas):
            shard = chunk * (shards // 2) + place_of(info_ref, step, replicas) + info_ref[0]
            normed, inverse_rms = normalize(packed_ref[shard][:, :model_width])
            normed_ref[chunk, step] = normed
            rms_ref[chunk, step] = jnp.broadcast_to(inverse_rms, rms_ref.shape[2:])
    normed, _ = normalize(packed_ref[:, :, :model_width].reshape(seq, model_width))
    rounded = normed.astype(jnp.bfloat16)
    norm_ref[...] = rounded
    flag_ref[...] = packed_ref[:, :, model_width:].reshape(seq, -1).astype(jnp.float32).T
    scale_factor = HEAD_DIM ** (-0.5)
    for block, out_ref in enumerate((q_ref, k_ref, v_ref)):
        first = pl.multiple_of(block * model_width + info_ref[0] * columns, 128)
        product = jnp.dot(
            rounded, w_ref[:, pl.ds(first, columns)], preferred_element_type=jnp.float32
        ).astype(jnp.bfloat16)
        out_ref[...] = product * scale_factor if block == 0 else product
    kt_ref[...] = (k_ref[...] * scale_factor).T


def upper_forward_kernel(
    levels, shard_rows, flag_ref, q_ref, k_ref, v_ref, prob_ref, at_ref
):
    seq = q_ref.shape[0]
    count = seq // 2
    bias = key_bias_rows(flag_ref[:, count:], levels, shard_rows, seq, count, count)
    softmax_pass(q_ref[count:], k_ref[...], v_ref[...], bias, prob_ref, at_ref)


def lower_forward_kernel(
    levels,
    shard_rows,
    info_ref,
    norm_ref,
    flag_ref,
    q_ref,
    k_ref,
    v_ref,
    after_ref,
    prob_ref,
    at_ref,
    gt_ref,
):
    seq = norm_ref.shape[0]
    count = seq // 2
    bias = key_bias_rows(flag_ref[:, :count], levels, shard_rows, count, 0, count)
    softmax_pass(q_ref[:count], k_ref[:count], v_ref[:count], bias, prob_ref, at_ref)
    rows = gt_ref.shape[0] // 4
    parity, x, y = info_ref[0], info_ref[1], info_ref[2]
    half = norm_ref.shape[1] // rows // 2
    for place, block in enumerate(
        (
            half * y + 2 * x + 1 - parity,
            half * y + 2 * x + parity,
            half * y + 2 * (1 - x) + 1 - parity,
            half * (1 - y) + 2 * x + parity,
        )
    ):
        first = pl.multiple_of(block * rows, 128)
        gt_ref[place * rows : (place + 1) * rows] = norm_ref[:, pl.ds(first, rows)].T


def place_of(info_ref, step, replicas):
    return 2 * lax.rem(info_ref[1] - step + replicas, replicas)


def merge_rows(info_ref, fresh, got_refs, kept_refs, out_refs, rows_ref):
    @pl.when(fresh)
    def _():
        for core, out_ref in enumerate(out_refs):
            out_ref[...] = got_refs[core][...]

    @pl.when(jnp.logical_not(fresh))
    def _():
        for out_ref, kept_ref in zip(out_refs, kept_refs):
            out_ref[...] = kept_ref[...]

    place_rows(info_ref, out_refs, rows_ref)


def place_rows(info_ref, out_refs, rows_ref):
    replicas = out_refs[0].shape[0]
    for step in range(replicas):
        place = place_of(info_ref, step, replicas)
        rows_ref[place + info_ref[0]] = out_refs[0][step]
        rows_ref[place + 1 - info_ref[0]] = out_refs[1][step]


def merge_tops(info_ref, upper, piece_refs, out_refs, rows_ref):
    replicas = out_refs[0].shape[0]
    own_chunk = info_ref[2] == (1 if upper else 0)
    for core in range(2):
        refs = piece_refs[2 * replicas * core : 2 * replicas * (core + 1)]

        @pl.when(own_chunk)
        def _():
            for step in range(replicas):
                out_refs[core][step] = refs[step][...]

        @pl.when(jnp.logical_not(own_chunk))
        def _():
            for step in range(replicas):
                out_refs[core][step] = refs[replicas + step][...]

    place_rows(info_ref, out_refs, rows_ref)


def backward_kernel(upper, tops, last, fresh_section, info_ref, *refs):
    refs = list(refs)
    got = tops or 4
    got_refs = refs[:got]
    w_ref, prob_ref, q_ref, v_ref, kt_ref, at_ref = refs[got : got + 6]
    refs = refs[got + 6 :]
    if not upper:
        key_sum_ref, value_sum_ref = refs[:2]
        refs = refs[2:]
    refs = refs[1:]
    if last:
        refs = [refs[0], refs[-1], *refs[1:-1]]
    own_ref, other_ref, keep_ref = refs[:3]
    send_refs = refs[3 : 3 + PIECES[upper]]
    refs = refs[3 + len(send_refs) :]
    if upper:
        key_sum_ref, value_sum_ref = refs[:2]
        refs = refs[2:]
    grads_ref, rows_ref, scores_ref = refs
    replicas, shard_rows, model_width = own_ref.shape
    count = rows_ref.shape[0] * shard_rows
    keys = prob_ref.shape[1]
    parity = info_ref[0]
    columns = q_ref.shape[1]
    width = 2 * HEAD_DIM
    if tops:
        merge_tops(info_ref, upper, got_refs, (own_ref, other_ref), rows_ref)
    else:
        fresh = info_ref[3] == fresh_section
        merge_rows(info_ref, fresh, got_refs[:-2], got_refs[-2:], (own_ref, other_ref), rows_ref)
    rows = rows_ref[...].reshape(count, model_width)
    weights = w_ref[pl.ds(pl.multiple_of(parity * columns, 128), columns), :]
    over_width = (((1,), (1,)), ((), ()))
    upstream = lax.dot_general(
        rows, weights, over_width, preferred_element_type=jnp.float32
    ).astype(jnp.bfloat16)
    upstream_t = upstream.T
    product_t = upstream_t.astype(jnp.float32) * at_ref[...].astype(jnp.float32)
    first_query = keys - count
    masks = head_masks()

    def put(block, pair, part):
        first = block * columns + pair * width
        grads_ref[:, :, first : first + width] = part.astype(jnp.bfloat16).reshape(
            -1, shard_rows, width
        )

    for pair in range(columns // width):
        at_pair = slice(pair * width, (pair + 1) * width)
        prob_grad = jnp.dot(
            v_ref[:keys, at_pair], side_by_side(upstream_t, pair), preferred_element_type=jnp.float32
        )
        for half in range(2):
            at_half = slice(half * count, (half + 1) * count)
            first = pair * width + half * HEAD_DIM
            delta = jnp.sum(product_t[first : first + HEAD_DIM], axis=0, keepdims=True)
            scores_ref[pair, :, at_half] = (
                prob_ref[pair, :, at_half].astype(jnp.float32) * (prob_grad[:, at_half] - delta)
            ).astype(jnp.bfloat16)
        value_grad = jnp.dot(
            prob_ref[pair],
            one_above_other(upstream[:, at_pair], masks),
            preferred_element_type=jnp.float32,
        )
        if upper:
            value_sum_ref[:, at_pair] = value_grad[:first_query]
            value_grad = value_grad[first_query:]
        else:
            value_grad = value_grad + value_sum_ref[:, at_pair]
        put(2, pair, value_grad)
    for pair in range(columns // width):
        at_pair = slice(pair * width, (pair + 1) * width)
        queries = q_ref[first_query : first_query + count, at_pair]
        key_grad = jnp.dot(
            scores_ref[pair], one_above_other(queries, masks), preferred_element_type=jnp.float32
        )
        if upper:
            key_sum_ref[:, at_pair] = key_grad[:first_query]
            key_grad = key_grad[first_query:]
        else:
            key_grad = key_grad + key_sum_ref[:, at_pair]
        put(1, pair, key_grad)
        query_grad = [
            jnp.dot(
                kt_ref[pair * width + half * HEAD_DIM : pair * width + (half + 1) * HEAD_DIM, :keys],
                scores_ref[pair, :, half * count : (half + 1) * count],
                preferred_element_type=jnp.float32,
            )
            for half in range(2)
        ]
        put(0, pair, jnp.concatenate(query_grad, 0).astype(jnp.bfloat16).T)
    for step in range(replicas):
        place = place_of(info_ref, step, replicas)
        keep_ref[step] = grads_ref[place + parity]
        crossing = grads_ref[place + 1 - parity]
        part = crossing.shape[1] // len(send_refs)
        for at, send_ref in enumerate(send_refs):
            send_ref[step] = crossing[:, at * part : (at + 1) * part]


def norm_product(part, w_ref, half):
    columns = part.shape[1] // 3
    model_width = w_ref.shape[0]
    total = jnp.zeros((part.shape[0], model_width), jnp.float32)
    for block in range(3):
        first = pl.multiple_of(block * model_width + half * columns, 128)
        total += lax.dot_general(
            part[:, block * columns : (block + 1) * columns],
            w_ref[:, pl.ds(first, columns)],
            (((1,), (1,)), ((), ())),
            preferred_element_type=jnp.float32,
        )
    return total


def norm_part_kernel(info_ref, keep_ref, w_ref, after_ref, out_ref):
    part = keep_ref[...].reshape(out_ref.shape[0], -1)
    out_ref[...] = norm_product(part, w_ref, info_ref[0])


def norm_kernel(upper, info_ref, keep_ref, normed_ref, rms_ref, incoming_ref, w_ref, *refs):
    got_refs = refs[: PIECES[upper]]
    out_refs = refs[len(got_refs) :]
    model_width = w_ref.shape[0]
    replicas, shard_rows = incoming_ref.shape[:2]
    rows = replicas * shard_rows
    got = [got_ref[...].reshape(rows, -1) for got_ref in got_refs]
    norm_grad = norm_product(jnp.concatenate(got, 1), w_ref, 1 - info_ref[0])
    norm_grad += (
        keep_ref[...]
        if upper
        else norm_product(keep_ref[...].reshape(rows, -1), w_ref, info_ref[0])
    )
    chunk = 1 if upper else 0
    normed = normed_ref[chunk].reshape(rows, model_width)
    inverse_rms = rms_ref[chunk].reshape(rows, -1)[:, :1]
    inner = jnp.mean(norm_grad * normed, axis=-1, keepdims=True)
    incoming = incoming_ref[...].reshape(rows, model_width).astype(jnp.float32)
    grad_in = incoming + inverse_rms * (norm_grad - normed * inner)
    grad_in = grad_in.astype(jnp.bfloat16).reshape(replicas, shard_rows, model_width)
    out_refs[-1][...] = grad_in


def in_terms(gt_ref, grad_refs, half, rows):
    count = grad_refs[0].shape[0] * grad_refs[0].shape[1]
    return sum(
        jnp.dot(
            gt_ref[2 * half * rows : 2 * (half + 1) * rows, chunk * count : (chunk + 1) * count],
            part_ref[...].reshape(count, -1),
            preferred_element_type=jnp.float32,
        )
        for chunk, part_ref in enumerate(grad_refs)
    )


def send_kernel(gt_ref, lower_ref, upper_ref, pass_ref, keep_ref):
    rows = pass_ref.shape[0]
    total = in_terms(gt_ref, (lower_ref, upper_ref), 1, rows)
    pass_ref[...] = total[:rows].astype(jnp.bfloat16)
    keep_ref[...] = total[rows:].astype(jnp.bfloat16)


def term_kernel(info_ref, gt_ref, *refs):
    grad_refs, at_refs, row_refs = refs[:2], refs[2:4], refs[4:6]
    pass_ref, keep_ref, out_pass_ref, out_keep_ref, out_send_ref = refs[7:]
    rows = pass_ref.shape[0]
    width = out_send_ref.shape[1]
    parity, x, y = info_ref[0], info_ref[1], info_ref[2]
    sent = jnp.where(parity == y, 2 * (1 - x) + 1 - parity, 2 * x + parity)
    blocks = (sent, 2 * x + 1 - parity, 2 * x + parity)
    total = jnp.zeros((3 * rows, width), jnp.float32)
    for at_ref, part_ref in zip(at_refs, row_refs):
        picked = [at_ref[pl.ds(pl.multiple_of(block * rows, 128), rows)] for block in blocks]
        total += jnp.dot(
            jnp.concatenate(picked, 0),
            part_ref[...].reshape(-1, width),
            preferred_element_type=jnp.float32,
        )
    out_send_ref[...] = total[:rows].astype(jnp.bfloat16)
    out_pass_ref[...] = total[rows : 2 * rows]
    out_keep_ref[...] = total[2 * rows :]
    total = in_terms(gt_ref, grad_refs, 0, rows)
    pass_ref[...] = total[:rows]
    keep_ref[...] = total[rows:]


def sum_kernel(own_ref, got_ref, out_own_ref, out_got_ref, after_ref, sum_ref):
    columns = own_ref.shape[1]
    sum_ref[:, :columns] = (own_ref[...] + got_ref[...].astype(jnp.float32)).astype(jnp.bfloat16)
    sum_ref[:, columns:] = (out_own_ref[...] + out_got_ref[...].astype(jnp.float32)).astype(
        jnp.bfloat16
    )


def pick_kernel(info_ref, upper_ref, lower_ref, out_ref):
    crossing = info_ref[0] == 0
    for step in range(2):
        for chunk, part_ref in enumerate((lower_ref, upper_ref)):
            wanted = info_ref[2] == (chunk if step == 1 else 1 - chunk)

            @pl.when(wanted & (crossing if step == 1 else jnp.logical_not(crossing)))
            def _():
                out_ref[...] = part_ref[step]


def join_kernel(info_ref, upper_ref, lower_ref, got_ref, out_ref):
    micro = info_ref[4]
    out_ref[0, 1 - micro] = got_ref[...]

    @pl.when(info_ref[2] == 1)
    def _():
        out_ref[0, micro] = upper_ref[0]

    @pl.when(info_ref[2] != 1)
    def _():
        out_ref[0, micro] = lower_ref[0]


def place_kernel(
    info_ref, own_ref, got_ref, out_own_ref, out_got_ref, sibling_ref, d_in_ref, d_out_ref
):
    columns = own_ref.shape[1] // 3
    own = own_ref[...] + got_ref[...].astype(jnp.float32)
    sibling = sibling_ref[:, : 3 * columns].astype(jnp.float32)
    for part, half in ((own, info_ref[0]), (sibling, 1 - info_ref[0])):
        for block in range(3):
            first = pl.multiple_of((2 * block + half) * columns, 128)
            d_in_ref[:, pl.ds(first, columns)] = part[:, block * columns : (block + 1) * columns]
    owner = info_ref[0] == info_ref[2]

    @pl.when(owner)
    def _():
        d_out_ref[...] = out_own_ref[...] + out_got_ref[...].astype(jnp.float32)

    @pl.when(jnp.logical_not(owner))
    def _():
        d_out_ref[...] = sibling_ref[:, 3 * columns :].astype(jnp.float32)


def call(kernel, outs, operands, scratch=(), flops=0, scalars=1, after=None, mebibytes=5, far=0):
    in_specs = [pl.BlockSpec(memory_space=pltpu.SMEM)] * scalars
    in_specs += [pl.BlockSpec(memory_space=pltpu.HBM)] * far
    in_specs += [pl.BlockSpec(memory_space=pltpu.VMEM)] * (len(operands) - scalars - far)
    if after is not None:
        operands = [*operands, after]
        in_specs.append(pl.BlockSpec(memory_space=pl.ANY))
    return pl.pallas_call(
        kernel,
        out_shape=list(outs),
        in_specs=in_specs,
        out_specs=[pl.BlockSpec(memory_space=pltpu.VMEM)] * len(outs),
        scratch_shapes=list(scratch),
        cost_estimate=pl.CostEstimate(flops=1, bytes_accessed=1, transcendentals=0),
        compiler_params=pltpu.CompilerParams(vmem_limit_bytes=mebibytes * 2**20),
    )(*operands)


def by_chips(acts, grad_top, w_in, w_out, offsets):
    half_type, full_type = jnp.bfloat16, jnp.float32
    shape = jax.ShapeDtypeStruct
    sections = lax.axis_size("section")
    shards = lax.axis_size("tm")
    levels = offsets.shape[1]
    half = shards // 2
    replicas = half // 2
    me = lax.axis_index("tm")
    parity = lax.rem(me, 2)
    side = lax.div(me, half)
    micro_count, shard_rows, model_width = acts.shape[1:]
    columns = model_width // 2
    heads = columns // HEAD_DIM
    seq = shards * shard_rows
    count = seq // 2
    w_qkv = w_in[0]
    w_rows = w_out[0]
    beside = lax.div(lax.rem(me, half), 2)
    micro = lax.rem(side + beside, 2)
    info = jnp.stack([parity, beside, side, lax.axis_index("section"), micro])
    info = jnp.concatenate([info.astype(jnp.int32), offsets[0]])

    def swapped(value, bits, chosen=None):
        pairs = [(device, device ^ bits) for device in range(shards)]
        pairs = [pair for pair in pairs if chosen is None or chosen(pair[0])]
        return lax.ppermute(value, "tm", pairs)

    core, near, far = 1, 2, half

    packed = shape((shard_rows, model_width + 128), half_type)
    top_shape = shape((shard_rows, model_width), half_type)
    own_acts, other_acts, own_top, other_top = call(
        functools.partial(pack_kernel, levels),
        [packed, packed, top_shape, top_shape],
        [info, acts[0], grad_top],
    )
    (touched,) = call(
        touch_kernel, [shape((16, 128), half_type)], [w_qkv], scalars=0, after=own_acts
    )
    pieces = [own_acts, swapped(other_acts, near), swapped(other_acts, far)]
    pieces += [swapped(own_acts, near + far)]
    tops = [own_top, swapped(other_top, near), swapped(other_top, far)]
    pieces[-1], tops, touched = lax.optimization_barrier((pieces[-1], tops, touched))
    tops += [swapped(own_top, near + far)]
    pieces += [swapped(piece, core) for piece in pieces]

    rows_shape = shape((seq, columns), half_type)
    normed, rms, norm, flag_rows, queries, keys, values, keys_t = call(
        functools.partial(project_kernel, replicas),
        [
            shape((2, replicas, shard_rows, model_width), full_type),
            shape((2, replicas, shard_rows, 128), full_type),
            shape((seq, model_width), half_type),
            shape((128, seq), full_type),
            rows_shape,
            rows_shape,
            rows_shape,
            shape((columns, seq), half_type),
        ],
        [info, *pieces, w_qkv],
        scratch=[pltpu.VMEM((shards, *packed.shape), half_type)],
        flops=6 * seq * model_width * columns,
        after=touched,
    )
    pairs = heads // 2
    upper_prob, upper_at = call(
        functools.partial(upper_forward_kernel, levels, shard_rows),
        [
            shape((pairs, seq, 2 * count), half_type),
            shape((columns, count), half_type),
        ],
        [flag_rows, queries, keys, values],
        scalars=0,
        flops=4 * columns * seq * count,
    )
    tops, upper_at = lax.optimization_barrier((tuple(tops), upper_at))
    tops = [*tops, *[swapped(piece, core) for piece in tops]]
    own_rows = model_width // shards
    probs, attended = {True: upper_prob}, {True: upper_at}
    got, kept = {}, {}
    piece_shape = shape((replicas, shard_rows, model_width), half_type)
    grads_shape = shape((replicas, shard_rows, 3 * columns), half_type)
    sum_shape = shape((count, columns), full_type)
    full_grads = shape((half, shard_rows, 3 * columns), half_type)
    full_rows = shape((half, shard_rows, model_width), half_type)
    term_shape = (own_rows, 3 * columns)
    rows_scratch = pltpu.VMEM(full_rows.shape, half_type)
    grads_scratch = pltpu.VMEM(full_grads.shape, half_type)
    result, full, ordered = {}, {}, {}
    for turn in range(sections):
        last = turn + 1 == sections
        fresh_section = sections - 1 - turn
        sums, parts, crossed = [], {}, {}

        def norm_step(upper, after):
            (result[upper],) = call(
                functools.partial(norm_kernel, upper),
                [piece_shape],
                [info, parts[upper], normed, rms, kept[upper][0], w_qkv, *crossed[upper]],
                after=after,
            )
            if not last:
                hop = [(sections - 1 - turn, sections - 2 - turn)]
                got[upper] = lax.ppermute(result[upper], "section", hop)

        for upper in (True, False):
            rows_in, after = tops, keys_t if upper else result.get(True)
            if turn:
                before = result[False] if upper else result[True]
                got[upper], after = lax.optimization_barrier((got[upper], before))
                if not upper:
                    result[True] = after
                rows_in = [got[upper], swapped(got[upper], core), *kept[upper]]
            part = 3 * columns // PIECES[upper]
            cross = [shape((replicas, shard_rows, part), half_type)] * PIECES[upper]
            outs = [piece_shape] * (1 if last else 2) + [grads_shape, *cross]
            outs += [sum_shape, sum_shape] if upper else []
            scratch = []
            if last:
                outs += [full_grads]
            else:
                scratch += [grads_scratch]
            if last:
                outs += [full_rows]
            else:
                scratch += [rows_scratch]
            part_keys = seq if upper else count
            scratch += [pltpu.VMEM((pairs, part_keys, 2 * count), half_type)]
            if last:
                scratch += [pltpu.VMEM(piece_shape.shape, half_type)]
            answer = call(
                functools.partial(
                    backward_kernel, upper, 0 if turn else len(tops), last, fresh_section
                ),
                outs,
                [info, *rows_in, w_rows, probs[upper], queries, values, keys_t]
                + [attended[upper], *sums],
                scratch=scratch,
                flops=2 * count * columns * (2 * model_width + 4 * part_keys),
                after=after,
            )
            kept[upper] = tuple(answer[:2])
            answer = answer[1 if last else 2 :]
            keep = answer[0]
            send = answer[1 : 1 + len(cross)]
            parts[upper] = keep
            if upper:
                sums = answer[1 + len(cross) : 3 + len(cross)]
                (parts[True],) = call(
                    norm_part_kernel,
                    [shape((replicas * shard_rows, model_width), full_type)],
                    [info, keep, w_qkv],
                    flops=3 * replicas * shard_rows * model_width * model_width,
                    after=keep,
                )
                if turn == 0:
                    lower_prob, lower_at, norm_t = call(
                        functools.partial(lower_forward_kernel, levels, shard_rows),
                        [
                            shape((pairs, count, 2 * count), half_type),
                            shape((columns, count), half_type),
                            shape((4 * own_rows, seq), half_type),
                        ],
                        [info, norm, flag_rows, queries, keys, values],
                        flops=4 * columns * count * count,
                        after=parts[True],
                    )
                    probs[False], attended[False] = lower_prob, lower_at
            if last:
                full[upper], ordered[upper] = answer[-2:]
            crossed[upper] = [swapped(piece, core) for piece in send]
            if upper:
                norm_step(True, keep)
        if last:
            send_pass, send_keep = call(
                send_kernel,
                [shape(term_shape, half_type)] * 2,
                [norm_t, full[False], full[True]],
                scalars=0,
            )
            terms = call(
                term_kernel,
                [shape(term_shape, full_type)] * 2
                + [shape((own_rows, model_width), full_type)] * 2
                + [shape((own_rows, model_width), half_type)],
                [info, norm_t, full[False], full[True], attended[False], attended[True]]
                + [ordered[False], ordered[True]],
                after=send_keep,
            )
        norm_step(False, terms[4] if last else result[True])

    in_pass, in_keep, out_pass, out_keep, out_send = terms
    got_pass = swapped(send_pass, near)
    got_keep = swapped(send_keep, far)
    own_rows_grad = [result[True], result[False]]
    (theirs,) = call(pick_kernel, [top_shape], [info, *own_rows_grad])
    to_owner = [(device, device ^ (far if device % 2 else near)) for device in range(shards)]
    partner = lax.ppermute(theirs, "tm", to_owner)
    got_out_pass = swapped(out_send, near, lambda device: device // half == device % 2)
    got_out_keep = swapped(out_send, far, lambda device: device // half != device % 2)
    _, _, done = lax.optimization_barrier((got_keep, got_out_keep, partner))
    (summed,) = call(
        sum_kernel,
        [shape((own_rows, 3 * columns + model_width), half_type)],
        [in_pass, got_pass, out_pass, got_out_pass],
        scalars=0,
        after=done,
    )
    d_w_in, d_w_out = call(
        place_kernel,
        [
            shape((own_rows, 3 * model_width), full_type),
            shape((own_rows, model_width), full_type),
        ],
        [info, in_keep, got_keep, out_keep, got_out_keep, swapped(summed, core)],
    )
    (d_acts,) = call(
        join_kernel, [shape(acts.shape, half_type)], [info, *own_rows_grad, partner]
    )
    return (d_acts, d_w_in[None], d_w_out[None])


def layer_gradients(acts, grad_top, w_in, w_out, offsets):
    shards = lax.axis_size("tm")
    micro_count, shard_rows, model_width = acts.shape[1:]
    heads = model_width // HEAD_DIM
    prob_bytes = 2 * heads * (shards * shard_rows) ** 2
    fits = prob_bytes <= 2**24 and model_width % (128 * shards) == 0 and shard_rows % 16 == 0
    square = shards % 4 == 0 and shards // 4 == 2
    if micro_count == 2 and square and heads % 4 == 0 and fits:
        return by_chips(acts, grad_top, w_in, w_out, offsets)
    return per_device(acts, grad_top, w_in, w_out, offsets)


def solution(mesh):
    placed = (
        P("section", None, "tm", None),
        P(None, "tm", None),
        P("section", None, None),
        P("section", None, None),
        P("tm", None),
    )
    return jax.shard_map(
        layer_gradients,
        mesh=mesh,
        in_specs=placed,
        out_specs=(
            P("section", None, "tm", None),
            P("section", "tm", None),
            P("section", "tm", None),
        ),
        check_vma=False,
    )
```

```python
import functools
import jax
import jax.numpy as jnp
from jax import lax
from jax.experimental import pallas as pl
from jax.experimental.pallas import tpu as pltpu
from jax.sharding import PartitionSpec as P

HEAD_DIM = 64


epsilon = 1e-06
PIECES = {True: 2, False: 2}
negative_fill = -1e30


def shifted(value, axis, steps):
    count = lax.axis_size(axis)
    initial, last = (max(0, -steps), min(count, count - steps))
    return lax.ppermute(value, axis, [(source, source + steps) for source in range(initial, last)])


def normalize(inputs):
    values = inputs.astype(jnp.float32)
    inverse_rms = lax.rsqrt(jnp.mean(values * values, axis=-1, keepdims=True) + epsilon)
    return (values * inverse_rms, inverse_rms)


def key_bias(level_flags, shard_rows):
    position = jnp.arange(shard_rows)
    own_part = position[None, :] <= position[:, None]
    far_part = jnp.repeat(level_flags != 0, shard_rows)
    far_part = jnp.broadcast_to(far_part[None, :], (shard_rows, far_part.shape[0]))
    return jnp.concatenate([own_part, far_part], 1)


def split_heads(row_block):
    return row_block.reshape(row_block.shape[0], -1, HEAD_DIM)


def softmax_keys(queries, key_heads, allowed):
    scores = jnp.einsum(
        "ihd,jhd->hij", queries, key_heads, preferred_element_type=jnp.float32
    ) * HEAD_DIM ** (-0.5)
    scores = jnp.where(allowed[None], scores, negative_fill)
    highest = jnp.max(scores, axis=-1, keepdims=True)
    shifted_exp = jnp.where(allowed[None], jnp.exp(scores - highest), 0.0)
    return shifted_exp / jnp.sum(shifted_exp, axis=-1, keepdims=True)


def attend(query_rows, key_rows, allowed):
    model_width = query_rows.shape[1]
    probability = softmax_keys(
        split_heads(query_rows), split_heads(key_rows[:, :model_width]), allowed
    )
    attended = jnp.einsum(
        "hij,jhd->ihd",
        probability.astype(jnp.bfloat16),
        split_heads(key_rows[:, model_width:]),
        preferred_element_type=jnp.float32,
    )
    return attended.reshape(query_rows.shape).astype(jnp.bfloat16)


def attend_back(query_rows, key_rows, allowed, incoming, attended, w_proj):
    model_width = query_rows.shape[1]
    queries = split_heads(query_rows)
    key_heads = split_heads(key_rows[:, :model_width])
    value_heads = split_heads(key_rows[:, model_width:])
    probability = softmax_keys(queries, key_heads, allowed)
    rounded = probability.astype(jnp.bfloat16)
    upstream = lax.dot_general(
        incoming, w_proj, (((1,), (1,)), ((), ())), preferred_element_type=jnp.float32
    ).astype(jnp.bfloat16)
    up_heads = split_heads(upstream)
    delta = jnp.einsum(
        "ihd,ihd->hi", up_heads.astype(jnp.float32), split_heads(attended).astype(jnp.float32)
    )[..., None]
    prob_grad = jnp.einsum(
        "ihd,jhd->hij", up_heads, value_heads, preferred_element_type=jnp.float32
    )
    score_grad = (probability * (prob_grad - delta)).astype(jnp.bfloat16)
    scale_factor = HEAD_DIM ** (-0.5)
    query_grad = (
        jnp.einsum("hij,jhd->ihd", score_grad, key_heads, preferred_element_type=jnp.float32)
        * scale_factor
    )
    key_grad = (
        jnp.einsum("hij,ihd->jhd", score_grad, queries, preferred_element_type=jnp.float32)
        * scale_factor
    )
    value_grad = jnp.einsum("hij,ihd->jhd", rounded, up_heads, preferred_element_type=jnp.float32)
    return (
        query_grad.reshape(-1, model_width),
        key_grad.reshape(-1, model_width),
        value_grad.reshape(-1, model_width),
    )


def per_device(acts, grad_top, w_in, w_out, offsets):
    sections = lax.axis_size("section")
    shards = lax.axis_size("tm")
    levels = shards.bit_length() - 1
    section_index = lax.axis_index("section")
    micro_count = acts.shape[1]
    shard_rows = acts.shape[2]
    model_width = acts.shape[3]
    w_qkv = w_in[0]
    w_proj = w_out[0]
    level_flags = offsets[0]
    normed, inverse_rms = normalize(acts[0])
    rounded_norm = normed.astype(jnp.bfloat16)
    qkv = jnp.dot(rounded_norm.reshape(-1, model_width), w_qkv, preferred_element_type=jnp.float32)
    qkv = qkv.astype(jnp.bfloat16).reshape(micro_count, shard_rows, 3 * model_width)
    pairs = qkv[..., model_width:]
    far_list = [shifted(pairs, "tm", 2**level) for level in range(levels)]
    key_rows = jnp.concatenate([pairs] + far_list, 1)
    allowed = key_bias(level_flags, shard_rows)
    attended = jnp.stack(
        [
            attend(qkv[index, :, :model_width], key_rows[index], allowed)
            for index in range(micro_count)
        ],
        0,
    )

    def attention_part(incoming, slot):
        query_rows = lax.dynamic_index_in_dim(qkv, slot, 0, False)[:, :model_width]
        slot_keys = lax.dynamic_index_in_dim(key_rows, slot, 0, False)
        slot_attended = lax.dynamic_index_in_dim(attended, slot, 0, False)
        query_grad, key_grad, value_grad = attend_back(
            query_rows, slot_keys, allowed, incoming, slot_attended, w_proj
        )
        owner_sum = jnp.concatenate([key_grad[:shard_rows], value_grad[:shard_rows]], 1)
        far_part = jnp.concatenate([key_grad[shard_rows:], value_grad[shard_rows:]], 1)
        far_part = far_part.astype(jnp.bfloat16).reshape(levels, shard_rows, 2 * model_width)
        return (query_grad, owner_sum, far_part)

    def empty_attention(incoming, slot):
        return (
            jnp.zeros((shard_rows, model_width), jnp.float32),
            jnp.zeros((shard_rows, 2 * model_width), jnp.float32),
            jnp.zeros((levels, shard_rows, 2 * model_width), jnp.bfloat16),
        )

    def norm_part(qkv_grad, incoming, slot):
        norm_grad = lax.dot_general(
            qkv_grad, w_qkv, (((1,), (1,)), ((), ())), preferred_element_type=jnp.float32
        )
        slot_normed = lax.dynamic_index_in_dim(normed, slot, 0, False)
        slot_rms = lax.dynamic_index_in_dim(inverse_rms, slot, 0, False)
        inner = jnp.mean(norm_grad * slot_normed, axis=-1, keepdims=True)
        return (incoming.astype(jnp.float32) + slot_rms * (norm_grad - slot_normed * inner)).astype(
            jnp.bfloat16
        )

    def empty_norm(qkv_grad, incoming, slot):
        return jnp.zeros((shard_rows, model_width), jnp.bfloat16)

    def step(turn, carry):
        received, grad_store, qkv_store, incoming_store = carry
        slot_raw = turn - (sections - 1 - section_index)
        active = (slot_raw >= 0) & (slot_raw < micro_count)
        slot = jnp.clip(slot_raw, 0, micro_count - 1)
        incoming = jnp.where(
            section_index == sections - 1,
            lax.dynamic_index_in_dim(grad_top, slot, 0, False),
            received,
        )
        query_grad, owner_sum, far_part = lax.cond(
            active, attention_part, empty_attention, incoming, slot
        )
        for level in range(levels):
            owner_sum = owner_sum + shifted(far_part[level], "tm", -(2**level)).astype(jnp.float32)
        qkv_grad = jnp.concatenate([query_grad, owner_sum], 1).astype(jnp.bfloat16)
        grad_in = lax.cond(active, norm_part, empty_norm, qkv_grad, incoming, slot)
        sent_down = shifted(grad_in, "section", -1)
        grad_store = jnp.where(
            active, lax.dynamic_update_index_in_dim(grad_store, grad_in, slot, 0), grad_store
        )
        qkv_store = jnp.where(
            active, lax.dynamic_update_index_in_dim(qkv_store, qkv_grad, slot, 0), qkv_store
        )
        incoming_store = jnp.where(
            active,
            lax.dynamic_update_index_in_dim(incoming_store, incoming, slot, 0),
            incoming_store,
        )
        return (sent_down, grad_store, qkv_store, incoming_store)

    initial = (
        jnp.zeros((shard_rows, model_width), jnp.bfloat16),
        jnp.zeros((micro_count, shard_rows, model_width), jnp.bfloat16),
        jnp.zeros((micro_count, shard_rows, 3 * model_width), jnp.bfloat16),
        jnp.zeros((micro_count, shard_rows, model_width), jnp.bfloat16),
    )
    received, grad_store, qkv_store, incoming_store = lax.fori_loop(
        0, sections + micro_count - 1, step, initial
    )
    flat_norm = rounded_norm.reshape(-1, model_width)
    flat_attended = attended.reshape(-1, model_width)
    flat_qkv = qkv_store.reshape(-1, 3 * model_width)
    flat_incoming = incoming_store.reshape(-1, model_width)
    contract = (((0,), (0,)), ((), ()))
    first = lax.dot_general(flat_norm, flat_qkv, contract, preferred_element_type=jnp.float32)
    second = lax.dot_general(
        flat_attended, flat_incoming, contract, preferred_element_type=jnp.float32
    )
    summed = lax.psum_scatter(
        jnp.concatenate([first, second], 1).astype(jnp.bfloat16),
        "tm",
        scatter_dimension=0,
        tiled=True,
    ).astype(jnp.float32)
    return (
        grad_store[None],
        summed[None, :, : 3 * model_width],
        summed[None, :, 3 * model_width :],
    )


def side_by_side(transposed, pair):
    width = 2 * HEAD_DIM
    rows = transposed[pair * width : (pair + 1) * width]
    empty = jnp.zeros((HEAD_DIM, rows.shape[1]), rows.dtype)
    return jnp.concatenate(
        [
            jnp.concatenate([rows[:HEAD_DIM], empty], 0),
            jnp.concatenate([empty, rows[HEAD_DIM:]], 0),
        ],
        1,
    )


def one_above_other(rows, masks):
    return jnp.concatenate([rows * masks[0], rows * masks[1]], 0)


def head_masks():
    lane = lax.broadcasted_iota(jnp.int32, (1, 2 * HEAD_DIM), 1)
    return [
        jnp.where(lane < HEAD_DIM, 1.0, 0.0).astype(jnp.bfloat16),
        jnp.where(lane < HEAD_DIM, 0.0, 1.0).astype(jnp.bfloat16),
    ]


def key_bias_rows(flag_rows, levels, shard_rows, keys, first_query, count):
    key_at = lax.broadcasted_iota(jnp.int32, (keys, count), 0)
    query_at = lax.broadcasted_iota(jnp.int32, (keys, count), 1) + first_query
    gap = lax.div(query_at, shard_rows) - lax.div(key_at, shard_rows)
    allowed = (gap == 0) & (key_at <= query_at)
    for level in range(levels):
        allowed = allowed | ((gap == 2**level) & (flag_rows[level : level + 1] != 0))
    return jnp.where(allowed, 0.0, negative_fill)


def softmax_pass(queries, keys, values, bias, prob_ref, at_ref):
    queries_t = queries.T
    values_t = values.T
    width = 2 * HEAD_DIM
    count = queries.shape[0]
    for pair in range(queries.shape[1] // width):
        at_pair = slice(pair * width, (pair + 1) * width)
        scores = jnp.dot(
            keys[:, at_pair], side_by_side(queries_t, pair), preferred_element_type=jnp.float32
        )
        for half in range(2):
            at_half = slice(half * count, (half + 1) * count)
            biased = scores[:, at_half] + bias
            shifted_exp = jnp.exp(biased - jnp.max(biased, axis=0, keepdims=True))
            probability = shifted_exp * (1.0 / jnp.sum(shifted_exp, axis=0, keepdims=True))
            prob_ref[pair, :, at_half] = probability.astype(jnp.bfloat16)
    for head in range(queries.shape[1] // HEAD_DIM):
        at = slice(head * HEAD_DIM, (head + 1) * HEAD_DIM)
        at_half = slice(head % 2 * count, (head % 2 + 1) * count)
        at_ref[at] = jnp.dot(
            values_t[at], prob_ref[head // 2, :, at_half], preferred_element_type=jnp.float32
        ).astype(jnp.bfloat16)


def pack_kernel(
    levels, info_ref, acts_ref, top_ref, own_ref, other_ref, own_top_ref, other_top_ref
):
    model_width = acts_ref.shape[2]
    shard_rows = own_ref.shape[0]
    micro = info_ref[4]
    lane = lax.broadcasted_iota(jnp.int32, (shard_rows, own_ref.shape[1] - model_width), 1)
    flags = jnp.zeros(lane.shape, jnp.float32)
    for level in range(levels):
        seen = jnp.where(info_ref[5 + level] != 0, 1.0, 0.0)
        flags = jnp.where(lane == level, seen, flags)
    for at, out_ref, out_top_ref in (
        (micro, own_ref, own_top_ref),
        (1 - micro, other_ref, other_top_ref),
    ):
        out_ref[:, :model_width] = acts_ref[at]
        out_ref[:, model_width:] = flags.astype(jnp.bfloat16)
        out_top_ref[...] = top_ref[at]


def touch_kernel(w_ref, after_ref, out_ref):
    out_ref[...] = w_ref[: out_ref.shape[0], : out_ref.shape[1]]


def turn_in_kernel(own, info_ref, w_ref, after_ref, out_ref):
    columns = out_ref.shape[0] // 3
    model_width = w_ref.shape[0]
    half = info_ref[0] if own else 1 - info_ref[0]
    for block in range(3):
        first = pl.multiple_of(block * model_width + half * columns, 128)
        out_ref[block * columns : (block + 1) * columns] = w_ref[:, pl.ds(first, columns)].T


def turn_out_kernel(info_ref, w_ref, after_ref, out_ref):
    columns = out_ref.shape[1]
    first = pl.multiple_of(info_ref[0] * columns, 128)
    out_ref[...] = w_ref[pl.ds(first, columns)].T


def project_kernel(replicas, info_ref, *refs):
    pieces = refs[: 4 * replicas]
    w_ref, _, normed_ref, rms_ref, norm_ref, flag_ref, q_ref, k_ref, v_ref, kt_ref, packed_ref = refs[
        4 * replicas :
    ]
    shards, shard_rows = packed_ref.shape[:2]
    model_width = w_ref.shape[0]
    seq = shards * shard_rows
    columns = q_ref.shape[1]
    at_piece = 0
    for core in (info_ref[0], 1 - info_ref[0]):
        for side in (info_ref[2], 1 - info_ref[2]):
            for step in range(replicas):
                shard = side * (shards // 2) + place_of(info_ref, step, replicas) + core
                packed_ref[shard] = pieces[at_piece][...]
                at_piece += 1
    for chunk in range(2):
        for step in range(replicas):
            shard = chunk * (shards // 2) + place_of(info_ref, step, replicas) + info_ref[0]
            normed, inverse_rms = normalize(packed_ref[shard][:, :model_width])
            normed_ref[chunk, step] = normed
            rms_ref[chunk, step] = jnp.broadcast_to(inverse_rms, rms_ref.shape[2:])
    normed, _ = normalize(packed_ref[:, :, :model_width].reshape(seq, model_width))
    rounded = normed.astype(jnp.bfloat16)
    norm_ref[...] = rounded
    flag_ref[...] = packed_ref[:, :, model_width:].reshape(seq, -1).astype(jnp.float32).T
    scale_factor = HEAD_DIM ** (-0.5)
    for block, out_ref in enumerate((q_ref, k_ref, v_ref)):
        first = pl.multiple_of(block * model_width + info_ref[0] * columns, 128)
        product = jnp.dot(
            rounded, w_ref[:, pl.ds(first, columns)], preferred_element_type=jnp.float32
        ).astype(jnp.bfloat16)
        out_ref[...] = product * scale_factor if block == 0 else product
    kt_ref[...] = (k_ref[...] * scale_factor).T


def upper_forward_kernel(
    levels, shard_rows, flag_ref, q_ref, k_ref, v_ref, prob_ref, at_ref
):
    seq = q_ref.shape[0]
    count = seq // 2
    bias = key_bias_rows(flag_ref[:, count:], levels, shard_rows, seq, count, count)
    softmax_pass(q_ref[count:], k_ref[...], v_ref[...], bias, prob_ref, at_ref)


def lower_forward_kernel(
    levels,
    shard_rows,
    info_ref,
    norm_ref,
    flag_ref,
    q_ref,
    k_ref,
    v_ref,
    after_ref,
    prob_ref,
    at_ref,
    gt_ref,
):
    seq = norm_ref.shape[0]
    count = seq // 2
    bias = key_bias_rows(flag_ref[:, :count], levels, shard_rows, count, 0, count)
    softmax_pass(q_ref[:count], k_ref[:count], v_ref[:count], bias, prob_ref, at_ref)
    rows = gt_ref.shape[0] // 4
    parity, x, y = info_ref[0], info_ref[1], info_ref[2]
    half = norm_ref.shape[1] // rows // 2
    for place, block in enumerate(
        (
            half * y + 2 * x + 1 - parity,
            half * y + 2 * x + parity,
            half * y + 2 * (1 - x) + 1 - parity,
            half * (1 - y) + 2 * x + parity,
        )
    ):
        first = pl.multiple_of(block * rows, 128)
        gt_ref[place * rows : (place + 1) * rows] = norm_ref[:, pl.ds(first, rows)].T


def place_of(info_ref, step, replicas):
    return 2 * lax.rem(info_ref[1] - step + replicas, replicas)


def merge_rows(info_ref, fresh, got_refs, kept_refs, out_refs, rows_ref):
    @pl.when(fresh)
    def _():
        for core, out_ref in enumerate(out_refs):
            out_ref[...] = got_refs[core][...]

    @pl.when(jnp.logical_not(fresh))
    def _():
        for out_ref, kept_ref in zip(out_refs, kept_refs):
            out_ref[...] = kept_ref[...]

    place_rows(info_ref, out_refs, rows_ref)


def place_rows(info_ref, out_refs, rows_ref):
    replicas = out_refs[0].shape[0]
    for step in range(replicas):
        place = place_of(info_ref, step, replicas)
        rows_ref[place + info_ref[0]] = out_refs[0][step]
        rows_ref[place + 1 - info_ref[0]] = out_refs[1][step]


def merge_tops(info_ref, upper, piece_refs, out_refs, rows_ref):
    replicas = out_refs[0].shape[0]
    own_chunk = info_ref[2] == (1 if upper else 0)
    for core in range(2):
        refs = piece_refs[2 * replicas * core : 2 * replicas * (core + 1)]

        @pl.when(own_chunk)
        def _():
            for step in range(replicas):
                out_refs[core][step] = refs[step][...]

        @pl.when(jnp.logical_not(own_chunk))
        def _():
            for step in range(replicas):
                out_refs[core][step] = refs[replicas + step][...]

    place_rows(info_ref, out_refs, rows_ref)


def backward_kernel(upper, tops, last, fresh_section, info_ref, *refs):
    refs = list(refs)
    got = tops or 4
    got_refs = refs[:got]
    w_ref, prob_ref, q_ref, v_ref, kt_ref, at_ref = refs[got : got + 6]
    refs = refs[got + 6 :]
    if not upper:
        key_sum_ref, value_sum_ref = refs[:2]
        refs = refs[2:]
    refs = refs[1:]
    if last:
        refs = [refs[0], refs[-1], *refs[1:-1]]
    own_ref, other_ref, keep_ref = refs[:3]
    send_refs = refs[3 : 3 + PIECES[upper]]
    refs = refs[3 + len(send_refs) :]
    if upper:
        key_sum_ref, value_sum_ref = refs[:2]
        refs = refs[2:]
    grads_ref, rows_ref, scores_ref = refs
    replicas, shard_rows, model_width = own_ref.shape
    count = rows_ref.shape[0] * shard_rows
    keys = prob_ref.shape[1]
    parity = info_ref[0]
    columns = q_ref.shape[1]
    width = 2 * HEAD_DIM
    if tops:
        merge_tops(info_ref, upper, got_refs, (own_ref, other_ref), rows_ref)
    else:
        fresh = info_ref[3] == fresh_section
        merge_rows(info_ref, fresh, got_refs[:-2], got_refs[-2:], (own_ref, other_ref), rows_ref)
    rows = rows_ref[...].reshape(count, model_width)
    upstream = jnp.dot(rows, w_ref[...], preferred_element_type=jnp.float32).astype(jnp.bfloat16)
    upstream_t = upstream.T
    product_t = upstream_t.astype(jnp.float32) * at_ref[...].astype(jnp.float32)
    first_query = keys - count
    masks = head_masks()

    def put(block, pair, part):
        first = block * columns + pair * width
        grads_ref[:, :, first : first + width] = part.astype(jnp.bfloat16).reshape(
            -1, shard_rows, width
        )

    for pair in range(columns // width):
        at_pair = slice(pair * width, (pair + 1) * width)
        prob_grad = jnp.dot(
            v_ref[:keys, at_pair], side_by_side(upstream_t, pair), preferred_element_type=jnp.float32
        )
        for half in range(2):
            at_half = slice(half * count, (half + 1) * count)
            first = pair * width + half * HEAD_DIM
            delta = jnp.sum(product_t[first : first + HEAD_DIM], axis=0, keepdims=True)
            scores_ref[pair, :, at_half] = (
                prob_ref[pair, :, at_half].astype(jnp.float32) * (prob_grad[:, at_half] - delta)
            ).astype(jnp.bfloat16)
        value_grad = jnp.dot(
            prob_ref[pair],
            one_above_other(upstream[:, at_pair], masks),
            preferred_element_type=jnp.float32,
        )
        if upper:
            value_sum_ref[:, at_pair] = value_grad[:first_query]
            value_grad = value_grad[first_query:]
        else:
            value_grad = value_grad + value_sum_ref[:, at_pair]
        put(2, pair, value_grad)
    for pair in range(columns // width):
        at_pair = slice(pair * width, (pair + 1) * width)
        queries = q_ref[first_query : first_query + count, at_pair]
        key_grad = jnp.dot(
            scores_ref[pair], one_above_other(queries, masks), preferred_element_type=jnp.float32
        )
        if upper:
            key_sum_ref[:, at_pair] = key_grad[:first_query]
            key_grad = key_grad[first_query:]
        else:
            key_grad = key_grad + key_sum_ref[:, at_pair]
        put(1, pair, key_grad)
        query_grad = [
            jnp.dot(
                kt_ref[pair * width + half * HEAD_DIM : pair * width + (half + 1) * HEAD_DIM, :keys],
                scores_ref[pair, :, half * count : (half + 1) * count],
                preferred_element_type=jnp.float32,
            )
            for half in range(2)
        ]
        put(0, pair, jnp.concatenate(query_grad, 0).astype(jnp.bfloat16).T)
    for step in range(replicas):
        place = place_of(info_ref, step, replicas)
        keep_ref[step] = grads_ref[place + parity]
        crossing = grads_ref[place + 1 - parity]
        part = crossing.shape[1] // len(send_refs)
        for at, send_ref in enumerate(send_refs):
            send_ref[step] = crossing[:, at * part : (at + 1) * part]


def norm_product(part, w_ref, half):
    columns = part.shape[1] // 3
    if w_ref.shape[0] == part.shape[1]:
        return jnp.dot(part, w_ref[...], preferred_element_type=jnp.float32)
    model_width = w_ref.shape[0]
    total = jnp.zeros((part.shape[0], model_width), jnp.float32)
    for block in range(3):
        first = pl.multiple_of(block * model_width + half * columns, 128)
        total += lax.dot_general(
            part[:, block * columns : (block + 1) * columns],
            w_ref[:, pl.ds(first, columns)],
            (((1,), (1,)), ((), ())),
            preferred_element_type=jnp.float32,
        )
    return total


def norm_part_kernel(info_ref, keep_ref, w_ref, after_ref, out_ref):
    part = keep_ref[...].reshape(out_ref.shape[0], -1)
    out_ref[...] = norm_product(part, w_ref, info_ref[0])


def norm_kernel(upper, info_ref, keep_ref, normed_ref, rms_ref, incoming_ref, *refs):
    w_own_ref, w_other_ref = refs[:2]
    refs = refs[2:]
    got_refs = refs[: PIECES[upper]]
    out_refs = refs[len(got_refs) :]
    replicas, shard_rows, model_width = incoming_ref.shape
    rows = replicas * shard_rows
    got = [got_ref[...].reshape(rows, -1) for got_ref in got_refs]
    norm_grad = norm_product(jnp.concatenate(got, 1), w_other_ref, 1 - info_ref[0])
    norm_grad += (
        keep_ref[...]
        if upper
        else norm_product(keep_ref[...].reshape(rows, -1), w_own_ref, info_ref[0])
    )
    chunk = 1 if upper else 0
    normed = normed_ref[chunk].reshape(rows, model_width)
    inverse_rms = rms_ref[chunk].reshape(rows, -1)[:, :1]
    inner = jnp.mean(norm_grad * normed, axis=-1, keepdims=True)
    incoming = incoming_ref[...].reshape(rows, model_width).astype(jnp.float32)
    grad_in = incoming + inverse_rms * (norm_grad - normed * inner)
    grad_in = grad_in.astype(jnp.bfloat16).reshape(replicas, shard_rows, model_width)
    out_refs[-1][...] = grad_in


def in_terms(gt_ref, grad_refs, half, rows):
    count = grad_refs[0].shape[0] * grad_refs[0].shape[1]
    return sum(
        jnp.dot(
            gt_ref[2 * half * rows : 2 * (half + 1) * rows, chunk * count : (chunk + 1) * count],
            part_ref[...].reshape(count, -1),
            preferred_element_type=jnp.float32,
        )
        for chunk, part_ref in enumerate(grad_refs)
    )


def send_kernel(gt_ref, lower_ref, upper_ref, pass_ref, keep_ref):
    rows = pass_ref.shape[0]
    total = in_terms(gt_ref, (lower_ref, upper_ref), 1, rows)
    pass_ref[...] = total[:rows].astype(jnp.bfloat16)
    keep_ref[...] = total[rows:].astype(jnp.bfloat16)


def term_kernel(info_ref, gt_ref, *refs):
    grad_refs, at_refs, row_refs = refs[:2], refs[2:4], refs[4:6]
    pass_ref, keep_ref, out_pass_ref, out_keep_ref, out_send_ref = refs[7:]
    rows = pass_ref.shape[0]
    width = out_send_ref.shape[1]
    parity, x, y = info_ref[0], info_ref[1], info_ref[2]
    sent = jnp.where(parity == y, 2 * (1 - x) + 1 - parity, 2 * x + parity)
    blocks = (sent, 2 * x + 1 - parity, 2 * x + parity)
    total = jnp.zeros((3 * rows, width), jnp.float32)
    for at_ref, part_ref in zip(at_refs, row_refs):
        picked = [at_ref[pl.ds(pl.multiple_of(block * rows, 128), rows)] for block in blocks]
        total += jnp.dot(
            jnp.concatenate(picked, 0),
            part_ref[...].reshape(-1, width),
            preferred_element_type=jnp.float32,
        )
    out_send_ref[...] = total[:rows].astype(jnp.bfloat16)
    out_pass_ref[...] = total[rows : 2 * rows]
    out_keep_ref[...] = total[2 * rows :]
    total = in_terms(gt_ref, grad_refs, 0, rows)
    pass_ref[...] = total[:rows]
    keep_ref[...] = total[rows:]


def sum_kernel(own_ref, got_ref, out_own_ref, out_got_ref, after_ref, sum_ref):
    columns = own_ref.shape[1]
    sum_ref[:, :columns] = (own_ref[...] + got_ref[...].astype(jnp.float32)).astype(jnp.bfloat16)
    sum_ref[:, columns:] = (out_own_ref[...] + out_got_ref[...].astype(jnp.float32)).astype(
        jnp.bfloat16
    )


def pick_kernel(info_ref, upper_ref, lower_ref, out_ref):
    crossing = info_ref[0] == 0
    for step in range(2):
        for chunk, part_ref in enumerate((lower_ref, upper_ref)):
            wanted = info_ref[2] == (chunk if step == 1 else 1 - chunk)

            @pl.when(wanted & (crossing if step == 1 else jnp.logical_not(crossing)))
            def _():
                out_ref[...] = part_ref[step]


def join_kernel(info_ref, upper_ref, lower_ref, got_ref, out_ref):
    micro = info_ref[4]
    out_ref[0, 1 - micro] = got_ref[...]

    @pl.when(info_ref[2] == 1)
    def _():
        out_ref[0, micro] = upper_ref[0]

    @pl.when(info_ref[2] != 1)
    def _():
        out_ref[0, micro] = lower_ref[0]


def place_kernel(
    info_ref, own_ref, got_ref, out_own_ref, out_got_ref, sibling_ref, d_in_ref, d_out_ref
):
    columns = own_ref.shape[1] // 3
    own = own_ref[...] + got_ref[...].astype(jnp.float32)
    sibling = sibling_ref[:, : 3 * columns].astype(jnp.float32)
    for part, half in ((own, info_ref[0]), (sibling, 1 - info_ref[0])):
        for block in range(3):
            first = pl.multiple_of((2 * block + half) * columns, 128)
            d_in_ref[:, pl.ds(first, columns)] = part[:, block * columns : (block + 1) * columns]
    owner = info_ref[0] == info_ref[2]

    @pl.when(owner)
    def _():
        d_out_ref[...] = out_own_ref[...] + out_got_ref[...].astype(jnp.float32)

    @pl.when(jnp.logical_not(owner))
    def _():
        d_out_ref[...] = sibling_ref[:, 3 * columns :].astype(jnp.float32)


def call(kernel, outs, operands, scratch=(), flops=0, scalars=1, after=None, mebibytes=5, far=0):
    in_specs = [pl.BlockSpec(memory_space=pltpu.SMEM)] * scalars
    in_specs += [pl.BlockSpec(memory_space=pltpu.HBM)] * far
    in_specs += [pl.BlockSpec(memory_space=pltpu.VMEM)] * (len(operands) - scalars - far)
    if after is not None:
        operands = [*operands, after]
        in_specs.append(pl.BlockSpec(memory_space=pl.ANY))
    return pl.pallas_call(
        kernel,
        out_shape=list(outs),
        in_specs=in_specs,
        out_specs=[pl.BlockSpec(memory_space=pltpu.VMEM)] * len(outs),
        scratch_shapes=list(scratch),
        cost_estimate=pl.CostEstimate(flops=1, bytes_accessed=1, transcendentals=0),
        compiler_params=pltpu.CompilerParams(vmem_limit_bytes=mebibytes * 2**20),
    )(*operands)


def by_chips(acts, grad_top, w_in, w_out, offsets):
    half_type, full_type = jnp.bfloat16, jnp.float32
    shape = jax.ShapeDtypeStruct
    sections = lax.axis_size("section")
    shards = lax.axis_size("tm")
    levels = offsets.shape[1]
    half = shards // 2
    replicas = half // 2
    me = lax.axis_index("tm")
    parity = lax.rem(me, 2)
    side = lax.div(me, half)
    micro_count, shard_rows, model_width = acts.shape[1:]
    columns = model_width // 2
    heads = columns // HEAD_DIM
    seq = shards * shard_rows
    count = seq // 2
    w_qkv = w_in[0]
    w_rows = w_out[0]
    beside = lax.div(lax.rem(me, half), 2)
    micro = lax.rem(side + beside, 2)
    info = jnp.stack([parity, beside, side, lax.axis_index("section"), micro])
    info = jnp.concatenate([info.astype(jnp.int32), offsets[0]])

    def swapped(value, bits, chosen=None):
        pairs = [(device, device ^ bits) for device in range(shards)]
        pairs = [pair for pair in pairs if chosen is None or chosen(pair[0])]
        return lax.ppermute(value, "tm", pairs)

    core, near, far = 1, 2, half

    packed = shape((shard_rows, model_width + 128), half_type)
    top_shape = shape((shard_rows, model_width), half_type)
    own_acts, other_acts, own_top, other_top = call(
        functools.partial(pack_kernel, levels),
        [packed, packed, top_shape, top_shape],
        [info, acts[0], grad_top],
    )
    (touched,) = call(
        touch_kernel, [shape((16, 128), half_type)], [w_qkv], scalars=0, after=own_acts
    )
    (w_rows,) = call(
        turn_out_kernel, [shape((model_width, columns), half_type)], [info, w_rows], after=touched
    )
    pieces = [own_acts, swapped(other_acts, near), swapped(other_acts, far)]
    pieces += [swapped(own_acts, near + far)]
    tops = [own_top, swapped(other_top, near), swapped(other_top, far)]
    pieces[-1], tops, touched, w_rows = lax.optimization_barrier(
        (pieces[-1], tops, touched, w_rows)
    )
    tops += [swapped(own_top, near + far)]
    pieces += [swapped(piece, core) for piece in pieces]

    rows_shape = shape((seq, columns), half_type)
    normed, rms, norm, flag_rows, queries, keys, values, keys_t = call(
        functools.partial(project_kernel, replicas),
        [
            shape((2, replicas, shard_rows, model_width), full_type),
            shape((2, replicas, shard_rows, 128), full_type),
            shape((seq, model_width), half_type),
            shape((128, seq), full_type),
            rows_shape,
            rows_shape,
            rows_shape,
            shape((columns, seq), half_type),
        ],
        [info, *pieces, w_qkv],
        scratch=[pltpu.VMEM((shards, *packed.shape), half_type)],
        flops=6 * seq * model_width * columns,
        after=touched,
    )
    pairs = heads // 2
    upper_prob, upper_at = call(
        functools.partial(upper_forward_kernel, levels, shard_rows),
        [
            shape((pairs, seq, 2 * count), half_type),
            shape((columns, count), half_type),
        ],
        [flag_rows, queries, keys, values],
        scalars=0,
        flops=4 * columns * seq * count,
    )
    tops, upper_at = lax.optimization_barrier((tuple(tops), upper_at))
    tops = [*tops, *[swapped(piece, core) for piece in tops]]
    own_rows = model_width // shards
    probs, attended = {True: upper_prob}, {True: upper_at}
    got, kept = {}, {}
    piece_shape = shape((replicas, shard_rows, model_width), half_type)
    grads_shape = shape((replicas, shard_rows, 3 * columns), half_type)
    sum_shape = shape((count, columns), full_type)
    full_grads = shape((half, shard_rows, 3 * columns), half_type)
    full_rows = shape((half, shard_rows, model_width), half_type)
    term_shape = (own_rows, 3 * columns)
    rows_scratch = pltpu.VMEM(full_rows.shape, half_type)
    grads_scratch = pltpu.VMEM(full_grads.shape, half_type)
    result, full, ordered = {}, {}, {}
    weights = [w_qkv, w_qkv]
    for turn in range(sections):
        last = turn + 1 == sections
        fresh_section = sections - 1 - turn
        sums, parts, crossed = [], {}, {}

        def norm_step(upper, after):
            (result[upper],) = call(
                functools.partial(norm_kernel, upper),
                [piece_shape],
                [info, parts[upper], normed, rms, kept[upper][0], *weights, *crossed[upper]],
                after=after,
            )
            if not last:
                hop = [(sections - 1 - turn, sections - 2 - turn)]
                got[upper] = lax.ppermute(result[upper], "section", hop)

        for upper in (True, False):
            rows_in, after = tops, keys_t if upper else result.get(True)
            if turn:
                before = result[False] if upper else result[True]
                if upper and turn <= 2:
                    (turned,) = call(
                        functools.partial(turn_in_kernel, turn == 1),
                        [shape((3 * columns, model_width), half_type)],
                        [info, w_qkv],
                        after=before,
                    )
                    got[upper], turned = lax.optimization_barrier((got[upper], turned))
                    weights[turn - 1] = turned
                got[upper], after = lax.optimization_barrier((got[upper], before))
                if not upper:
                    result[True] = after
                rows_in = [got[upper], swapped(got[upper], core), *kept[upper]]
            part = 3 * columns // PIECES[upper]
            cross = [shape((replicas, shard_rows, part), half_type)] * PIECES[upper]
            outs = [piece_shape] * (1 if last else 2) + [grads_shape, *cross]
            outs += [sum_shape, sum_shape] if upper else []
            scratch = []
            if last:
                outs += [full_grads]
            else:
                scratch += [grads_scratch]
            if last:
                outs += [full_rows]
            else:
                scratch += [rows_scratch]
            part_keys = seq if upper else count
            scratch += [pltpu.VMEM((pairs, part_keys, 2 * count), half_type)]
            if last:
                scratch += [pltpu.VMEM(piece_shape.shape, half_type)]
            answer = call(
                functools.partial(
                    backward_kernel, upper, 0 if turn else len(tops), last, fresh_section
                ),
                outs,
                [info, *rows_in, w_rows, probs[upper], queries, values, keys_t]
                + [attended[upper], *sums],
                scratch=scratch,
                flops=2 * count * columns * (2 * model_width + 4 * part_keys),
                after=after,
            )
            kept[upper] = tuple(answer[:2])
            answer = answer[1 if last else 2 :]
            keep = answer[0]
            send = answer[1 : 1 + len(cross)]
            parts[upper] = keep
            if upper:
                sums = answer[1 + len(cross) : 3 + len(cross)]
                (parts[True],) = call(
                    norm_part_kernel,
                    [shape((replicas * shard_rows, model_width), full_type)],
                    [info, keep, weights[0]],
                    flops=3 * replicas * shard_rows * model_width * model_width,
                    after=keep,
                )
                if turn == 0:
                    lower_prob, lower_at, norm_t = call(
                        functools.partial(lower_forward_kernel, levels, shard_rows),
                        [
                            shape((pairs, count, 2 * count), half_type),
                            shape((columns, count), half_type),
                            shape((4 * own_rows, seq), half_type),
                        ],
                        [info, norm, flag_rows, queries, keys, values],
                        flops=4 * columns * count * count,
                        after=parts[True],
                    )
                    probs[False], attended[False] = lower_prob, lower_at
            if last:
                full[upper], ordered[upper] = answer[-2:]
            crossed[upper] = [swapped(piece, core) for piece in send]
            if upper:
                norm_step(True, keep)
        if last:
            send_pass, send_keep = call(
                send_kernel,
                [shape(term_shape, half_type)] * 2,
                [norm_t, full[False], full[True]],
                scalars=0,
            )
            terms = call(
                term_kernel,
                [shape(term_shape, full_type)] * 2
                + [shape((own_rows, model_width), full_type)] * 2
                + [shape((own_rows, model_width), half_type)],
                [info, norm_t, full[False], full[True], attended[False], attended[True]]
                + [ordered[False], ordered[True]],
                after=send_keep,
            )
        norm_step(False, terms[4] if last else result[True])

    in_pass, in_keep, out_pass, out_keep, out_send = terms
    got_pass = swapped(send_pass, near)
    got_keep = swapped(send_keep, far)
    own_rows_grad = [result[True], result[False]]
    (theirs,) = call(pick_kernel, [top_shape], [info, *own_rows_grad])
    to_owner = [(device, device ^ (far if device % 2 else near)) for device in range(shards)]
    partner = lax.ppermute(theirs, "tm", to_owner)
    got_out_pass = swapped(out_send, near, lambda device: device // half == device % 2)
    got_out_keep = swapped(out_send, far, lambda device: device // half != device % 2)
    _, _, done = lax.optimization_barrier((got_keep, got_out_keep, partner))
    (summed,) = call(
        sum_kernel,
        [shape((own_rows, 3 * columns + model_width), half_type)],
        [in_pass, got_pass, out_pass, got_out_pass],
        scalars=0,
        after=done,
    )
    d_w_in, d_w_out = call(
        place_kernel,
        [
            shape((own_rows, 3 * model_width), full_type),
            shape((own_rows, model_width), full_type),
        ],
        [info, in_keep, got_keep, out_keep, got_out_keep, swapped(summed, core)],
    )
    (d_acts,) = call(
        join_kernel, [shape(acts.shape, half_type)], [info, *own_rows_grad, partner]
    )
    return (d_acts, d_w_in[None], d_w_out[None])


def layer_gradients(acts, grad_top, w_in, w_out, offsets):
    shards = lax.axis_size("tm")
    micro_count, shard_rows, model_width = acts.shape[1:]
    heads = model_width // HEAD_DIM
    prob_bytes = 2 * heads * (shards * shard_rows) ** 2
    fits = prob_bytes <= 2**24 and model_width % (128 * shards) == 0 and shard_rows % 16 == 0
    square = shards % 4 == 0 and shards // 4 == 2
    if micro_count == 2 and square and heads % 4 == 0 and fits:
        return by_chips(acts, grad_top, w_in, w_out, offsets)
    return per_device(acts, grad_top, w_in, w_out, offsets)


def solution(mesh):
    placed = (
        P("section", None, "tm", None),
        P(None, "tm", None),
        P("section", None, None),
        P("section", None, None),
        P("tm", None),
    )
    return jax.shard_map(
        layer_gradients,
        mesh=mesh,
        in_specs=placed,
        out_specs=(
            P("section", None, "tm", None),
            P("section", "tm", None),
            P("section", "tm", None),
        ),
        check_vma=False,
    )
```

```python
import functools
import jax
import jax.numpy as jnp
from jax import lax
from jax.experimental import pallas as pl
from jax.experimental.pallas import tpu as pltpu
from jax.sharding import PartitionSpec as P

HEAD_DIM = 64


epsilon = 1e-06
SPLITS = {True: (6,6), False: (4,4,4)}
negative_fill = -1e30


def shifted(value, axis, steps):
    count = lax.axis_size(axis)
    initial, last = (max(0, -steps), min(count, count - steps))
    return lax.ppermute(value, axis, [(source, source + steps) for source in range(initial, last)])


def normalize(inputs):
    values = inputs.astype(jnp.float32)
    inverse_rms = lax.rsqrt(jnp.mean(values * values, axis=-1, keepdims=True) + epsilon)
    return (values * inverse_rms, inverse_rms)


def key_bias(level_flags, shard_rows):
    position = jnp.arange(shard_rows)
    own_part = position[None, :] <= position[:, None]
    far_part = jnp.repeat(level_flags != 0, shard_rows)
    far_part = jnp.broadcast_to(far_part[None, :], (shard_rows, far_part.shape[0]))
    return jnp.concatenate([own_part, far_part], 1)


def split_heads(row_block):
    return row_block.reshape(row_block.shape[0], -1, HEAD_DIM)


def softmax_keys(queries, key_heads, allowed):
    scores = jnp.einsum(
        "ihd,jhd->hij", queries, key_heads, preferred_element_type=jnp.float32
    ) * HEAD_DIM ** (-0.5)
    scores = jnp.where(allowed[None], scores, negative_fill)
    highest = jnp.max(scores, axis=-1, keepdims=True)
    shifted_exp = jnp.where(allowed[None], jnp.exp(scores - highest), 0.0)
    return shifted_exp / jnp.sum(shifted_exp, axis=-1, keepdims=True)


def attend(query_rows, key_rows, allowed):
    model_width = query_rows.shape[1]
    probability = softmax_keys(
        split_heads(query_rows), split_heads(key_rows[:, :model_width]), allowed
    )
    attended = jnp.einsum(
        "hij,jhd->ihd",
        probability.astype(jnp.bfloat16),
        split_heads(key_rows[:, model_width:]),
        preferred_element_type=jnp.float32,
    )
    return attended.reshape(query_rows.shape).astype(jnp.bfloat16)


def attend_back(query_rows, key_rows, allowed, incoming, attended, w_proj):
    model_width = query_rows.shape[1]
    queries = split_heads(query_rows)
    key_heads = split_heads(key_rows[:, :model_width])
    value_heads = split_heads(key_rows[:, model_width:])
    probability = softmax_keys(queries, key_heads, allowed)
    rounded = probability.astype(jnp.bfloat16)
    upstream = lax.dot_general(
        incoming, w_proj, (((1,), (1,)), ((), ())), preferred_element_type=jnp.float32
    ).astype(jnp.bfloat16)
    up_heads = split_heads(upstream)
    delta = jnp.einsum(
        "ihd,ihd->hi", up_heads.astype(jnp.float32), split_heads(attended).astype(jnp.float32)
    )[..., None]
    prob_grad = jnp.einsum(
        "ihd,jhd->hij", up_heads, value_heads, preferred_element_type=jnp.float32
    )
    score_grad = (probability * (prob_grad - delta)).astype(jnp.bfloat16)
    scale_factor = HEAD_DIM ** (-0.5)
    query_grad = (
        jnp.einsum("hij,jhd->ihd", score_grad, key_heads, preferred_element_type=jnp.float32)
        * scale_factor
    )
    key_grad = (
        jnp.einsum("hij,ihd->jhd", score_grad, queries, preferred_element_type=jnp.float32)
        * scale_factor
    )
    value_grad = jnp.einsum("hij,ihd->jhd", rounded, up_heads, preferred_element_type=jnp.float32)
    return (
        query_grad.reshape(-1, model_width),
        key_grad.reshape(-1, model_width),
        value_grad.reshape(-1, model_width),
    )


def per_device(acts, grad_top, w_in, w_out, offsets):
    sections = lax.axis_size("section")
    shards = lax.axis_size("tm")
    levels = shards.bit_length() - 1
    section_index = lax.axis_index("section")
    micro_count = acts.shape[1]
    shard_rows = acts.shape[2]
    model_width = acts.shape[3]
    w_qkv = w_in[0]
    w_proj = w_out[0]
    level_flags = offsets[0]
    normed, inverse_rms = normalize(acts[0])
    rounded_norm = normed.astype(jnp.bfloat16)
    qkv = jnp.dot(rounded_norm.reshape(-1, model_width), w_qkv, preferred_element_type=jnp.float32)
    qkv = qkv.astype(jnp.bfloat16).reshape(micro_count, shard_rows, 3 * model_width)
    pairs = qkv[..., model_width:]
    far_list = [shifted(pairs, "tm", 2**level) for level in range(levels)]
    key_rows = jnp.concatenate([pairs] + far_list, 1)
    allowed = key_bias(level_flags, shard_rows)
    attended = jnp.stack(
        [
            attend(qkv[index, :, :model_width], key_rows[index], allowed)
            for index in range(micro_count)
        ],
        0,
    )

    def attention_part(incoming, slot):
        query_rows = lax.dynamic_index_in_dim(qkv, slot, 0, False)[:, :model_width]
        slot_keys = lax.dynamic_index_in_dim(key_rows, slot, 0, False)
        slot_attended = lax.dynamic_index_in_dim(attended, slot, 0, False)
        query_grad, key_grad, value_grad = attend_back(
            query_rows, slot_keys, allowed, incoming, slot_attended, w_proj
        )
        owner_sum = jnp.concatenate([key_grad[:shard_rows], value_grad[:shard_rows]], 1)
        far_part = jnp.concatenate([key_grad[shard_rows:], value_grad[shard_rows:]], 1)
        far_part = far_part.astype(jnp.bfloat16).reshape(levels, shard_rows, 2 * model_width)
        return (query_grad, owner_sum, far_part)

    def empty_attention(incoming, slot):
        return (
            jnp.zeros((shard_rows, model_width), jnp.float32),
            jnp.zeros((shard_rows, 2 * model_width), jnp.float32),
            jnp.zeros((levels, shard_rows, 2 * model_width), jnp.bfloat16),
        )

    def norm_part(qkv_grad, incoming, slot):
        norm_grad = lax.dot_general(
            qkv_grad, w_qkv, (((1,), (1,)), ((), ())), preferred_element_type=jnp.float32
        )
        slot_normed = lax.dynamic_index_in_dim(normed, slot, 0, False)
        slot_rms = lax.dynamic_index_in_dim(inverse_rms, slot, 0, False)
        inner = jnp.mean(norm_grad * slot_normed, axis=-1, keepdims=True)
        return (incoming.astype(jnp.float32) + slot_rms * (norm_grad - slot_normed * inner)).astype(
            jnp.bfloat16
        )

    def empty_norm(qkv_grad, incoming, slot):
        return jnp.zeros((shard_rows, model_width), jnp.bfloat16)

    def step(turn, carry):
        received, grad_store, qkv_store, incoming_store = carry
        slot_raw = turn - (sections - 1 - section_index)
        active = (slot_raw >= 0) & (slot_raw < micro_count)
        slot = jnp.clip(slot_raw, 0, micro_count - 1)
        incoming = jnp.where(
            section_index == sections - 1,
            lax.dynamic_index_in_dim(grad_top, slot, 0, False),
            received,
        )
        query_grad, owner_sum, far_part = lax.cond(
            active, attention_part, empty_attention, incoming, slot
        )
        for level in range(levels):
            owner_sum = owner_sum + shifted(far_part[level], "tm", -(2**level)).astype(jnp.float32)
        qkv_grad = jnp.concatenate([query_grad, owner_sum], 1).astype(jnp.bfloat16)
        grad_in = lax.cond(active, norm_part, empty_norm, qkv_grad, incoming, slot)
        sent_down = shifted(grad_in, "section", -1)
        grad_store = jnp.where(
            active, lax.dynamic_update_index_in_dim(grad_store, grad_in, slot, 0), grad_store
        )
        qkv_store = jnp.where(
            active, lax.dynamic_update_index_in_dim(qkv_store, qkv_grad, slot, 0), qkv_store
        )
        incoming_store = jnp.where(
            active,
            lax.dynamic_update_index_in_dim(incoming_store, incoming, slot, 0),
            incoming_store,
        )
        return (sent_down, grad_store, qkv_store, incoming_store)

    initial = (
        jnp.zeros((shard_rows, model_width), jnp.bfloat16),
        jnp.zeros((micro_count, shard_rows, model_width), jnp.bfloat16),
        jnp.zeros((micro_count, shard_rows, 3 * model_width), jnp.bfloat16),
        jnp.zeros((micro_count, shard_rows, model_width), jnp.bfloat16),
    )
    received, grad_store, qkv_store, incoming_store = lax.fori_loop(
        0, sections + micro_count - 1, step, initial
    )
    flat_norm = rounded_norm.reshape(-1, model_width)
    flat_attended = attended.reshape(-1, model_width)
    flat_qkv = qkv_store.reshape(-1, 3 * model_width)
    flat_incoming = incoming_store.reshape(-1, model_width)
    contract = (((0,), (0,)), ((), ()))
    first = lax.dot_general(flat_norm, flat_qkv, contract, preferred_element_type=jnp.float32)
    second = lax.dot_general(
        flat_attended, flat_incoming, contract, preferred_element_type=jnp.float32
    )
    summed = lax.psum_scatter(
        jnp.concatenate([first, second], 1).astype(jnp.bfloat16),
        "tm",
        scatter_dimension=0,
        tiled=True,
    ).astype(jnp.float32)
    return (
        grad_store[None],
        summed[None, :, : 3 * model_width],
        summed[None, :, 3 * model_width :],
    )


def side_by_side(transposed, pair):
    width = 2 * HEAD_DIM
    rows = transposed[pair * width : (pair + 1) * width]
    empty = jnp.zeros((HEAD_DIM, rows.shape[1]), rows.dtype)
    return jnp.concatenate(
        [
            jnp.concatenate([rows[:HEAD_DIM], empty], 0),
            jnp.concatenate([empty, rows[HEAD_DIM:]], 0),
        ],
        1,
    )


def one_above_other(rows, masks):
    return jnp.concatenate([rows * masks[0], rows * masks[1]], 0)


def head_masks():
    lane = lax.broadcasted_iota(jnp.int32, (1, 2 * HEAD_DIM), 1)
    return [
        jnp.where(lane < HEAD_DIM, 1.0, 0.0).astype(jnp.bfloat16),
        jnp.where(lane < HEAD_DIM, 0.0, 1.0).astype(jnp.bfloat16),
    ]


def key_bias_rows(flag_rows, levels, shard_rows, keys, first_query, count):
    key_at = lax.broadcasted_iota(jnp.int32, (keys, count), 0)
    query_at = lax.broadcasted_iota(jnp.int32, (keys, count), 1) + first_query
    gap = lax.div(query_at, shard_rows) - lax.div(key_at, shard_rows)
    allowed = (gap == 0) & (key_at <= query_at)
    for level in range(levels):
        allowed = allowed | ((gap == 2**level) & (flag_rows[level : level + 1] != 0))
    return jnp.where(allowed, 0.0, negative_fill)


def softmax_pass(queries, keys, values, bias, prob_ref, at_ref):
    queries_t = queries.T
    values_t = values.T
    width = 2 * HEAD_DIM
    count = queries.shape[0]
    for pair in range(queries.shape[1] // width):
        at_pair = slice(pair * width, (pair + 1) * width)
        scores = jnp.dot(
            keys[:, at_pair], side_by_side(queries_t, pair), preferred_element_type=jnp.float32
        )
        for half in range(2):
            at_half = slice(half * count, (half + 1) * count)
            biased = scores[:, at_half] + bias
            shifted_exp = jnp.exp(biased - jnp.max(biased, axis=0, keepdims=True))
            probability = shifted_exp * (1.0 / jnp.sum(shifted_exp, axis=0, keepdims=True))
            prob_ref[pair, :, at_half] = probability.astype(jnp.bfloat16)
    for head in range(queries.shape[1] // HEAD_DIM):
        at = slice(head * HEAD_DIM, (head + 1) * HEAD_DIM)
        at_half = slice(head % 2 * count, (head % 2 + 1) * count)
        at_ref[at] = jnp.dot(
            values_t[at], prob_ref[head // 2, :, at_half], preferred_element_type=jnp.float32
        ).astype(jnp.bfloat16)


def pack_kernel(
    levels, info_ref, acts_ref, top_ref, own_ref, other_ref, own_top_ref, other_top_ref
):
    model_width = acts_ref.shape[2]
    shard_rows = own_ref.shape[0]
    micro = info_ref[4]
    lane = lax.broadcasted_iota(jnp.int32, (shard_rows, own_ref.shape[1] - model_width), 1)
    flags = jnp.zeros(lane.shape, jnp.float32)
    for level in range(levels):
        seen = jnp.where(info_ref[5 + level] != 0, 1.0, 0.0)
        flags = jnp.where(lane == level, seen, flags)
    for at, out_ref, out_top_ref in (
        (micro, own_ref, own_top_ref),
        (1 - micro, other_ref, other_top_ref),
    ):
        out_ref[:, :model_width] = acts_ref[at]
        out_ref[:, model_width:] = flags.astype(jnp.bfloat16)
        out_top_ref[...] = top_ref[at]


def touch_kernel(w_ref, after_ref, out_ref):
    out_ref[...] = w_ref[: out_ref.shape[0], : out_ref.shape[1]]


def turn_in_kernel(own, info_ref, w_ref, after_ref, out_ref):
    columns = out_ref.shape[0] // 3
    model_width = w_ref.shape[0]
    half = info_ref[0] if own else 1 - info_ref[0]
    for block in range(3):
        first = pl.multiple_of(block * model_width + half * columns, 128)
        out_ref[block * columns : (block + 1) * columns] = w_ref[:, pl.ds(first, columns)].T


def turn_out_kernel(info_ref, w_ref, after_ref, out_ref):
    columns = out_ref.shape[1]
    first = pl.multiple_of(info_ref[0] * columns, 128)
    out_ref[...] = w_ref[pl.ds(first, columns)].T


def project_kernel(replicas, info_ref, *refs):
    pieces = refs[: 4 * replicas]
    w_ref, _, normed_ref, rms_ref, norm_ref, flag_ref, q_ref, k_ref, v_ref, kt_ref, packed_ref = refs[
        4 * replicas :
    ]
    shards, shard_rows = packed_ref.shape[:2]
    model_width = w_ref.shape[0]
    seq = shards * shard_rows
    columns = q_ref.shape[1]
    at_piece = 0
    for core in (info_ref[0], 1 - info_ref[0]):
        for side in (info_ref[2], 1 - info_ref[2]):
            for step in range(replicas):
                shard = side * (shards // 2) + place_of(info_ref, step, replicas) + core
                packed_ref[shard] = pieces[at_piece][...]
                at_piece += 1
    for chunk in range(2):
        for step in range(replicas):
            shard = chunk * (shards // 2) + place_of(info_ref, step, replicas) + info_ref[0]
            normed, inverse_rms = normalize(packed_ref[shard][:, :model_width])
            normed_ref[chunk, step] = normed
            rms_ref[chunk, step] = jnp.broadcast_to(inverse_rms, rms_ref.shape[2:])
    normed, _ = normalize(packed_ref[:, :, :model_width].reshape(seq, model_width))
    rounded = normed.astype(jnp.bfloat16)
    norm_ref[...] = rounded
    flag_ref[...] = packed_ref[:, :, model_width:].reshape(seq, -1).astype(jnp.float32).T
    scale_factor = HEAD_DIM ** (-0.5)
    for block, out_ref in enumerate((q_ref, k_ref, v_ref)):
        first = pl.multiple_of(block * model_width + info_ref[0] * columns, 128)
        product = jnp.dot(
            rounded, w_ref[:, pl.ds(first, columns)], preferred_element_type=jnp.float32
        ).astype(jnp.bfloat16)
        out_ref[...] = product * scale_factor if block == 0 else product
    kt_ref[...] = (k_ref[...] * scale_factor).T


def upper_forward_kernel(
    levels, shard_rows, flag_ref, q_ref, k_ref, v_ref, prob_ref, at_ref
):
    seq = q_ref.shape[0]
    count = seq // 2
    bias = key_bias_rows(flag_ref[:, count:], levels, shard_rows, seq, count, count)
    softmax_pass(q_ref[count:], k_ref[...], v_ref[...], bias, prob_ref, at_ref)


def lower_forward_kernel(
    levels,
    shard_rows,
    info_ref,
    norm_ref,
    flag_ref,
    q_ref,
    k_ref,
    v_ref,
    after_ref,
    prob_ref,
    at_ref,
    gt_ref,
):
    seq = norm_ref.shape[0]
    count = seq // 2
    bias = key_bias_rows(flag_ref[:, :count], levels, shard_rows, count, 0, count)
    softmax_pass(q_ref[:count], k_ref[:count], v_ref[:count], bias, prob_ref, at_ref)
    rows = gt_ref.shape[0] // 4
    parity, x, y = info_ref[0], info_ref[1], info_ref[2]
    half = norm_ref.shape[1] // rows // 2
    for place, block in enumerate(
        (
            half * y + 2 * x + 1 - parity,
            half * y + 2 * x + parity,
            half * y + 2 * (1 - x) + 1 - parity,
            half * (1 - y) + 2 * x + parity,
        )
    ):
        first = pl.multiple_of(block * rows, 128)
        gt_ref[place * rows : (place + 1) * rows] = norm_ref[:, pl.ds(first, rows)].T


def place_of(info_ref, step, replicas):
    return 2 * lax.rem(info_ref[1] - step + replicas, replicas)


def merge_rows(info_ref, fresh, got_refs, kept_refs, out_refs, rows_ref):
    @pl.when(fresh)
    def _():
        for core, out_ref in enumerate(out_refs):
            out_ref[...] = got_refs[core][:, :, : out_ref.shape[2]]

    @pl.when(jnp.logical_not(fresh))
    def _():
        for out_ref, kept_ref in zip(out_refs, kept_refs):
            out_ref[...] = kept_ref[...]

    place_rows(info_ref, out_refs, rows_ref)


def place_rows(info_ref, out_refs, rows_ref):
    replicas = out_refs[0].shape[0]
    for step in range(replicas):
        place = place_of(info_ref, step, replicas)
        rows_ref[place + info_ref[0]] = out_refs[0][step]
        rows_ref[place + 1 - info_ref[0]] = out_refs[1][step]


def merge_tops(info_ref, upper, piece_refs, out_refs, rows_ref):
    replicas = out_refs[0].shape[0]
    own_chunk = info_ref[2] == (1 if upper else 0)
    for core in range(2):
        refs = piece_refs[2 * replicas * core : 2 * replicas * (core + 1)]

        @pl.when(own_chunk)
        def _():
            for step in range(replicas):
                out_refs[core][step] = refs[step][...]

        @pl.when(jnp.logical_not(own_chunk))
        def _():
            for step in range(replicas):
                out_refs[core][step] = refs[replicas + step][...]

    place_rows(info_ref, out_refs, rows_ref)


def backward_kernel(upper, tops, last, fresh_section, info_ref, *refs):
    refs = list(refs)
    got = tops or 4
    got_refs = refs[:got]
    w_ref, prob_ref, q_ref, v_ref, kt_ref, at_ref = refs[got : got + 6]
    refs = refs[got + 6 :]
    if not upper:
        key_sum_ref, value_sum_ref = refs[:2]
        refs = refs[2:]
    refs = refs[1:]
    if last:
        refs = [refs[0], refs[-1], *refs[1:-1]]
    own_ref, other_ref, keep_ref = refs[:3]
    send_refs = refs[3 : 3 + len(SPLITS[upper])]
    refs = refs[3 + len(send_refs) :]
    if upper:
        key_sum_ref, value_sum_ref = refs[:2]
        refs = refs[2:]
    grads_ref, rows_ref, scores_ref = refs
    replicas, shard_rows, model_width = own_ref.shape
    count = rows_ref.shape[0] * shard_rows
    keys = prob_ref.shape[1]
    parity = info_ref[0]
    columns = q_ref.shape[1]
    width = 2 * HEAD_DIM
    if tops:
        merge_tops(info_ref, upper, got_refs, (own_ref, other_ref), rows_ref)
    else:
        fresh = info_ref[3] == fresh_section
        merge_rows(info_ref, fresh, got_refs[:-2], got_refs[-2:], (own_ref, other_ref), rows_ref)
    rows = rows_ref[...].reshape(count, model_width)
    upstream = jnp.dot(rows, w_ref[...], preferred_element_type=jnp.float32).astype(jnp.bfloat16)
    upstream_t = upstream.T
    product_t = upstream_t.astype(jnp.float32) * at_ref[...].astype(jnp.float32)
    first_query = keys - count
    masks = head_masks()

    def put(block, pair, part):
        first = block * columns + pair * width
        grads_ref[:, :, first : first + width] = part.astype(jnp.bfloat16).reshape(
            -1, shard_rows, width
        )

    for pair in range(columns // width):
        at_pair = slice(pair * width, (pair + 1) * width)
        prob_grad = jnp.dot(
            v_ref[:keys, at_pair], side_by_side(upstream_t, pair), preferred_element_type=jnp.float32
        )
        for half in range(2):
            at_half = slice(half * count, (half + 1) * count)
            first = pair * width + half * HEAD_DIM
            delta = jnp.sum(product_t[first : first + HEAD_DIM], axis=0, keepdims=True)
            scores_ref[pair, :, at_half] = (
                prob_ref[pair, :, at_half].astype(jnp.float32) * (prob_grad[:, at_half] - delta)
            ).astype(jnp.bfloat16)
        value_grad = jnp.dot(
            prob_ref[pair],
            one_above_other(upstream[:, at_pair], masks),
            preferred_element_type=jnp.float32,
        )
        if upper:
            value_sum_ref[:, at_pair] = value_grad[:first_query]
            value_grad = value_grad[first_query:]
        else:
            value_grad = value_grad + value_sum_ref[:, at_pair]
        put(2, pair, value_grad)
    for pair in range(columns // width):
        at_pair = slice(pair * width, (pair + 1) * width)
        queries = q_ref[first_query : first_query + count, at_pair]
        key_grad = jnp.dot(
            scores_ref[pair], one_above_other(queries, masks), preferred_element_type=jnp.float32
        )
        if upper:
            key_sum_ref[:, at_pair] = key_grad[:first_query]
            key_grad = key_grad[first_query:]
        else:
            key_grad = key_grad + key_sum_ref[:, at_pair]
        put(1, pair, key_grad)
        query_grad = [
            jnp.dot(
                kt_ref[pair * width + half * HEAD_DIM : pair * width + (half + 1) * HEAD_DIM, :keys],
                scores_ref[pair, :, half * count : (half + 1) * count],
                preferred_element_type=jnp.float32,
            )
            for half in range(2)
        ]
        put(0, pair, jnp.concatenate(query_grad, 0).astype(jnp.bfloat16).T)
    for step in range(replicas):
        place = place_of(info_ref, step, replicas)
        keep_ref[step] = grads_ref[place + parity]
        crossing = grads_ref[place + 1 - parity]
        first = 0
        for send_ref in send_refs:
            send_ref[step] = crossing[:, first : first + send_ref.shape[2]]
            first += send_ref.shape[2]


def norm_product(part, w_ref, half):
    columns = part.shape[1] // 3
    if w_ref.shape[0] == part.shape[1]:
        return jnp.dot(part, w_ref[...], preferred_element_type=jnp.float32)
    model_width = w_ref.shape[0]
    total = jnp.zeros((part.shape[0], model_width), jnp.float32)
    for block in range(3):
        first = pl.multiple_of(block * model_width + half * columns, 128)
        total += lax.dot_general(
            part[:, block * columns : (block + 1) * columns],
            w_ref[:, pl.ds(first, columns)],
            (((1,), (1,)), ((), ())),
            preferred_element_type=jnp.float32,
        )
    return total


def norm_part_kernel(info_ref, keep_ref, w_ref, after_ref, out_ref):
    part = keep_ref[...].reshape(out_ref.shape[0], -1)
    out_ref[...] = norm_product(part, w_ref, info_ref[0])


def norm_kernel(upper, info_ref, keep_ref, normed_ref, rms_ref, incoming_ref, *refs):
    w_own_ref, w_other_ref = refs[:2]
    refs = refs[2:]
    got_refs = refs[: len(SPLITS[upper])]
    out_refs = refs[len(got_refs) :]
    replicas, shard_rows, model_width = incoming_ref.shape
    rows = replicas * shard_rows
    got = [got_ref[...].reshape(rows, -1) for got_ref in got_refs]
    norm_grad = norm_product(jnp.concatenate(got, 1), w_other_ref, 1 - info_ref[0])
    norm_grad += (
        keep_ref[...]
        if upper
        else norm_product(keep_ref[...].reshape(rows, -1), w_own_ref, info_ref[0])
    )
    chunk = 1 if upper else 0
    normed = normed_ref[chunk].reshape(rows, model_width)
    inverse_rms = rms_ref[chunk].reshape(rows, -1)[:, :1]
    inner = jnp.mean(norm_grad * normed, axis=-1, keepdims=True)
    incoming = incoming_ref[...].reshape(rows, model_width).astype(jnp.float32)
    grad_in = incoming + inverse_rms * (norm_grad - normed * inner)
    grad_in = grad_in.astype(jnp.bfloat16).reshape(replicas, shard_rows, model_width)
    out_refs[-1][:, :, :model_width] = grad_in
    spare = out_refs[-1].shape[2] - model_width
    if spare:
        out_refs[-1][:, :, model_width:] = jnp.zeros((replicas, shard_rows, spare), jnp.bfloat16)


def in_terms(gt_ref, grad_refs, half, rows):
    count = grad_refs[0].shape[0] * grad_refs[0].shape[1]
    return sum(
        jnp.dot(
            gt_ref[2 * half * rows : 2 * (half + 1) * rows, chunk * count : (chunk + 1) * count],
            part_ref[...].reshape(count, -1),
            preferred_element_type=jnp.float32,
        )
        for chunk, part_ref in enumerate(grad_refs)
    )


def send_kernel(gt_ref, lower_ref, upper_ref, pass_ref, keep_ref):
    rows = pass_ref.shape[0]
    total = in_terms(gt_ref, (lower_ref, upper_ref), 1, rows)
    pass_ref[...] = total[:rows].astype(jnp.bfloat16)
    keep_ref[...] = total[rows:].astype(jnp.bfloat16)


def term_kernel(info_ref, gt_ref, *refs):
    grad_refs, at_refs, row_refs = refs[:2], refs[2:4], refs[4:6]
    pass_ref, keep_ref, out_pass_ref, out_keep_ref, out_send_ref = refs[7:]
    rows = pass_ref.shape[0]
    width = out_send_ref.shape[1]
    parity, x, y = info_ref[0], info_ref[1], info_ref[2]
    sent = jnp.where(parity == y, 2 * (1 - x) + 1 - parity, 2 * x + parity)
    blocks = (sent, 2 * x + 1 - parity, 2 * x + parity)
    total = jnp.zeros((3 * rows, width), jnp.float32)
    for at_ref, part_ref in zip(at_refs, row_refs):
        picked = [at_ref[pl.ds(pl.multiple_of(block * rows, 128), rows)] for block in blocks]
        total += jnp.dot(
            jnp.concatenate(picked, 0),
            part_ref[...].reshape(-1, width),
            preferred_element_type=jnp.float32,
        )
    out_send_ref[...] = total[:rows].astype(jnp.bfloat16)
    out_pass_ref[...] = total[rows : 2 * rows]
    out_keep_ref[...] = total[2 * rows :]
    total = in_terms(gt_ref, grad_refs, 0, rows)
    pass_ref[...] = total[:rows]
    keep_ref[...] = total[rows:]


def sum_kernel(own_ref, got_ref, out_own_ref, out_got_ref, after_ref, sum_ref):
    columns = own_ref.shape[1]
    sum_ref[:, :columns] = (own_ref[...] + got_ref[...].astype(jnp.float32)).astype(jnp.bfloat16)
    sum_ref[:, columns:] = (out_own_ref[...] + out_got_ref[...].astype(jnp.float32)).astype(
        jnp.bfloat16
    )


def pick_kernel(info_ref, upper_ref, lower_ref, out_ref):
    crossing = info_ref[0] == 0
    for step in range(2):
        for chunk, part_ref in enumerate((lower_ref, upper_ref)):
            wanted = info_ref[2] == (chunk if step == 1 else 1 - chunk)

            @pl.when(wanted & (crossing if step == 1 else jnp.logical_not(crossing)))
            def _():
                out_ref[...] = part_ref[step]


def join_kernel(info_ref, upper_ref, lower_ref, got_ref, out_ref):
    micro = info_ref[4]
    out_ref[0, 1 - micro] = got_ref[...]

    @pl.when(info_ref[2] == 1)
    def _():
        out_ref[0, micro] = upper_ref[0]

    @pl.when(info_ref[2] != 1)
    def _():
        out_ref[0, micro] = lower_ref[0]


def place_kernel(
    info_ref, own_ref, got_ref, out_own_ref, out_got_ref, sibling_ref, d_in_ref, d_out_ref
):
    columns = own_ref.shape[1] // 3
    own = own_ref[...] + got_ref[...].astype(jnp.float32)
    sibling = sibling_ref[:, : 3 * columns].astype(jnp.float32)
    for part, half in ((own, info_ref[0]), (sibling, 1 - info_ref[0])):
        for block in range(3):
            first = pl.multiple_of((2 * block + half) * columns, 128)
            d_in_ref[:, pl.ds(first, columns)] = part[:, block * columns : (block + 1) * columns]
    owner = info_ref[0] == info_ref[2]

    @pl.when(owner)
    def _():
        d_out_ref[...] = out_own_ref[...] + out_got_ref[...].astype(jnp.float32)

    @pl.when(jnp.logical_not(owner))
    def _():
        d_out_ref[...] = sibling_ref[:, 3 * columns :].astype(jnp.float32)


def call(kernel, outs, operands, scratch=(), flops=0, scalars=1, after=None, mebibytes=5, far=0):
    in_specs = [pl.BlockSpec(memory_space=pltpu.SMEM)] * scalars
    in_specs += [pl.BlockSpec(memory_space=pltpu.HBM)] * far
    in_specs += [pl.BlockSpec(memory_space=pltpu.VMEM)] * (len(operands) - scalars - far)
    if after is not None:
        operands = [*operands, after]
        in_specs.append(pl.BlockSpec(memory_space=pl.ANY))
    return pl.pallas_call(
        kernel,
        out_shape=list(outs),
        in_specs=in_specs,
        out_specs=[pl.BlockSpec(memory_space=pltpu.VMEM)] * len(outs),
        scratch_shapes=list(scratch),
        cost_estimate=pl.CostEstimate(flops=1, bytes_accessed=1, transcendentals=0),
        compiler_params=pltpu.CompilerParams(vmem_limit_bytes=mebibytes * 2**20),
    )(*operands)


def by_chips(acts, grad_top, w_in, w_out, offsets):
    half_type, full_type = jnp.bfloat16, jnp.float32
    shape = jax.ShapeDtypeStruct
    sections = lax.axis_size("section")
    shards = lax.axis_size("tm")
    levels = offsets.shape[1]
    half = shards // 2
    replicas = half // 2
    me = lax.axis_index("tm")
    parity = lax.rem(me, 2)
    side = lax.div(me, half)
    micro_count, shard_rows, model_width = acts.shape[1:]
    columns = model_width // 2
    heads = columns // HEAD_DIM
    seq = shards * shard_rows
    count = seq // 2
    w_qkv = w_in[0]
    w_rows = w_out[0]
    beside = lax.div(lax.rem(me, half), 2)
    micro = lax.rem(side + beside, 2)
    info = jnp.stack([parity, beside, side, lax.axis_index("section"), micro])
    info = jnp.concatenate([info.astype(jnp.int32), offsets[0]])

    def swapped(value, bits, chosen=None):
        pairs = [(device, device ^ bits) for device in range(shards)]
        pairs = [pair for pair in pairs if chosen is None or chosen(pair[0])]
        return lax.ppermute(value, "tm", pairs)

    core, near, far = 1, 2, half

    packed = shape((shard_rows, model_width + 128), half_type)
    top_shape = shape((shard_rows, model_width), half_type)
    own_acts, other_acts, own_top, other_top = call(
        functools.partial(pack_kernel, levels),
        [packed, packed, top_shape, top_shape],
        [info, acts[0], grad_top],
    )
    (touched,) = call(
        touch_kernel, [shape((16, 128), half_type)], [w_qkv], scalars=0, after=own_acts
    )
    (w_rows,) = call(
        turn_out_kernel, [shape((model_width, columns), half_type)], [info, w_rows], after=touched
    )
    pieces = [own_acts, swapped(other_acts, near), swapped(other_acts, far)]
    pieces += [swapped(own_acts, near + far)]
    tops = [own_top, swapped(other_top, near), swapped(other_top, far)]
    pieces[-1], tops, touched, w_rows = lax.optimization_barrier(
        (pieces[-1], tops, touched, w_rows)
    )
    tops += [swapped(own_top, near + far)]
    pieces += [swapped(piece, core) for piece in pieces]

    rows_shape = shape((seq, columns), half_type)
    normed, rms, norm, flag_rows, queries, keys, values, keys_t = call(
        functools.partial(project_kernel, replicas),
        [
            shape((2, replicas, shard_rows, model_width), full_type),
            shape((2, replicas, shard_rows, 128), full_type),
            shape((seq, model_width), half_type),
            shape((128, seq), full_type),
            rows_shape,
            rows_shape,
            rows_shape,
            shape((columns, seq), half_type),
        ],
        [info, *pieces, w_qkv],
        scratch=[pltpu.VMEM((shards, *packed.shape), half_type)],
        flops=6 * seq * model_width * columns,
        after=touched,
    )
    pairs = heads // 2
    upper_prob, upper_at = call(
        functools.partial(upper_forward_kernel, levels, shard_rows),
        [
            shape((pairs, seq, 2 * count), half_type),
            shape((columns, count), half_type),
        ],
        [flag_rows, queries, keys, values],
        scalars=0,
        flops=4 * columns * seq * count,
    )
    tops, upper_at = lax.optimization_barrier((tuple(tops), upper_at))
    tops = [*tops, *[swapped(piece, core) for piece in tops]]
    own_rows = model_width // shards
    probs, attended = {True: upper_prob}, {True: upper_at}
    got, kept = {}, {}
    piece_shape = shape((replicas, shard_rows, model_width), half_type)
    wide_shape = shape((replicas, shard_rows, model_width + 128), half_type)
    grads_shape = shape((replicas, shard_rows, 3 * columns), half_type)
    sum_shape = shape((count, columns), full_type)
    full_grads = shape((half, shard_rows, 3 * columns), half_type)
    full_rows = shape((half, shard_rows, model_width), half_type)
    term_shape = (own_rows, 3 * columns)
    rows_scratch = pltpu.VMEM(full_rows.shape, half_type)
    grads_scratch = pltpu.VMEM(full_grads.shape, half_type)
    result, full, ordered = {}, {}, {}
    weights = [w_qkv, w_qkv]
    for turn in range(sections):
        last = turn + 1 == sections
        fresh_section = sections - 1 - turn
        sums, parts, crossed = [], {}, {}

        def norm_step(upper, after):
            (result[upper],) = call(
                functools.partial(norm_kernel, upper),
                [piece_shape if upper or last else wide_shape],
                [info, parts[upper], normed, rms, kept[upper][0], *weights, *crossed[upper]],
                after=after,
            )
            if not last:
                hop = [(sections - 1 - turn, sections - 2 - turn)]
                got[upper] = lax.ppermute(result[upper], "section", hop)

        for upper in (True, False):
            rows_in, after = tops, keys_t if upper else result.get(True)
            if turn:
                tied = result if last else parts
                before = result[False] if upper else tied[True]
                if upper and turn <= 2:
                    (turned,) = call(
                        functools.partial(turn_in_kernel, turn == 1),
                        [shape((3 * columns, model_width), half_type)],
                        [info, w_qkv],
                        after=before,
                    )
                    got[upper], turned = lax.optimization_barrier((got[upper], turned))
                    weights[turn - 1] = turned
                got[upper], after = lax.optimization_barrier((got[upper], before))
                if not upper:
                    tied[True] = after
                rows_in = [got[upper], swapped(got[upper], core), *kept[upper]]
            unit = 3 * columns // sum(SPLITS[upper])
            cross = [shape((replicas, shard_rows, part * unit), half_type) for part in SPLITS[upper]]
            outs = [piece_shape] * (1 if last else 2) + [grads_shape, *cross]
            outs += [sum_shape, sum_shape] if upper else []
            scratch = []
            if last:
                outs += [full_grads]
            else:
                scratch += [grads_scratch]
            if last:
                outs += [full_rows]
            else:
                scratch += [rows_scratch]
            part_keys = seq if upper else count
            scratch += [pltpu.VMEM((pairs, part_keys, 2 * count), half_type)]
            if last:
                scratch += [pltpu.VMEM(piece_shape.shape, half_type)]
            answer = call(
                functools.partial(
                    backward_kernel, upper, 0 if turn else len(tops), last, fresh_section
                ),
                outs,
                [info, *rows_in, w_rows, probs[upper], queries, values, keys_t]
                + [attended[upper], *sums],
                scratch=scratch,
                flops=2 * count * columns * (2 * model_width + 4 * part_keys),
                after=after,
            )
            kept[upper] = tuple(answer[:2])
            answer = answer[1 if last else 2 :]
            keep = answer[0]
            send = answer[1 : 1 + len(cross)]
            parts[upper] = keep
            if upper:
                sums = answer[1 + len(cross) : 3 + len(cross)]
                (parts[True],) = call(
                    norm_part_kernel,
                    [shape((replicas * shard_rows, model_width), full_type)],
                    [info, keep, weights[0]],
                    flops=3 * replicas * shard_rows * model_width * model_width,
                    after=keep,
                )
                if turn == 0:
                    lower_prob, lower_at, norm_t = call(
                        functools.partial(lower_forward_kernel, levels, shard_rows),
                        [
                            shape((pairs, count, 2 * count), half_type),
                            shape((columns, count), half_type),
                            shape((4 * own_rows, seq), half_type),
                        ],
                        [info, norm, flag_rows, queries, keys, values],
                        flops=4 * columns * count * count,
                        after=parts[True],
                    )
                    probs[False], attended[False] = lower_prob, lower_at
            if last:
                full[upper], ordered[upper] = answer[-2:]
            crossed[upper] = [swapped(piece, core) for piece in send]
            if upper:
                norm_step(True, keep)
        if last:
            send_pass, send_keep = call(
                send_kernel,
                [shape(term_shape, half_type)] * 2,
                [norm_t, full[False], full[True]],
                scalars=0,
            )
            terms = call(
                term_kernel,
                [shape(term_shape, full_type)] * 2
                + [shape((own_rows, model_width), full_type)] * 2
                + [shape((own_rows, model_width), half_type)],
                [info, norm_t, full[False], full[True], attended[False], attended[True]]
                + [ordered[False], ordered[True]],
                after=send_keep,
            )
        norm_step(False, terms[4] if last else result[True])

    in_pass, in_keep, out_pass, out_keep, out_send = terms
    got_pass = swapped(send_pass, near)
    got_keep = swapped(send_keep, far)
    own_rows_grad = [result[True], result[False]]
    (theirs,) = call(pick_kernel, [top_shape], [info, *own_rows_grad])
    to_owner = [(device, device ^ (far if device % 2 else near)) for device in range(shards)]
    partner = lax.ppermute(theirs, "tm", to_owner)
    got_out_pass = swapped(out_send, near, lambda device: device // half == device % 2)
    got_out_keep = swapped(out_send, far, lambda device: device // half != device % 2)
    _, _, done = lax.optimization_barrier((got_keep, got_out_keep, partner))
    (summed,) = call(
        sum_kernel,
        [shape((own_rows, 3 * columns + model_width), half_type)],
        [in_pass, got_pass, out_pass, got_out_pass],
        scalars=0,
        after=done,
    )
    d_w_in, d_w_out = call(
        place_kernel,
        [
            shape((own_rows, 3 * model_width), full_type),
            shape((own_rows, model_width), full_type),
        ],
        [info, in_keep, got_keep, out_keep, got_out_keep, swapped(summed, core)],
    )
    (d_acts,) = call(
        join_kernel, [shape(acts.shape, half_type)], [info, *own_rows_grad, partner]
    )
    return (d_acts, d_w_in[None], d_w_out[None])


def layer_gradients(acts, grad_top, w_in, w_out, offsets):
    shards = lax.axis_size("tm")
    micro_count, shard_rows, model_width = acts.shape[1:]
    heads = model_width // HEAD_DIM
    prob_bytes = 2 * heads * (shards * shard_rows) ** 2
    fits = prob_bytes <= 2**24 and model_width % (128 * shards) == 0 and shard_rows % 16 == 0
    square = shards % 4 == 0 and shards // 4 == 2
    if micro_count == 2 and square and heads % 4 == 0 and fits:
        return by_chips(acts, grad_top, w_in, w_out, offsets)
    return per_device(acts, grad_top, w_in, w_out, offsets)


def solution(mesh):
    placed = (
        P("section", None, "tm", None),
        P(None, "tm", None),
        P("section", None, None),
        P("section", None, None),
        P("tm", None),
    )
    return jax.shard_map(
        layer_gradients,
        mesh=mesh,
        in_specs=placed,
        out_specs=(
            P("section", None, "tm", None),
            P("section", "tm", None),
            P("section", "tm", None),
        ),
        check_vma=False,
    )
```

```python
import functools
import jax
import jax.numpy as jnp
from jax import lax
from jax.experimental import pallas as pl
from jax.experimental.pallas import tpu as pltpu
from jax.sharding import PartitionSpec as P

HEAD_DIM = 64


epsilon = 1e-06
PIECES = {True: 2, False: 2}
negative_fill = -1e30


def shifted(value, axis, steps):
    count = lax.axis_size(axis)
    initial, last = (max(0, -steps), min(count, count - steps))
    return lax.ppermute(value, axis, [(source, source + steps) for source in range(initial, last)])


def normalize(inputs):
    values = inputs.astype(jnp.float32)
    inverse_rms = lax.rsqrt(jnp.mean(values * values, axis=-1, keepdims=True) + epsilon)
    return (values * inverse_rms, inverse_rms)


def key_bias(level_flags, shard_rows):
    position = jnp.arange(shard_rows)
    own_part = position[None, :] <= position[:, None]
    far_part = jnp.repeat(level_flags != 0, shard_rows)
    far_part = jnp.broadcast_to(far_part[None, :], (shard_rows, far_part.shape[0]))
    return jnp.concatenate([own_part, far_part], 1)


def split_heads(row_block):
    return row_block.reshape(row_block.shape[0], -1, HEAD_DIM)


def softmax_keys(queries, key_heads, allowed):
    scores = jnp.einsum(
        "ihd,jhd->hij", queries, key_heads, preferred_element_type=jnp.float32
    ) * HEAD_DIM ** (-0.5)
    scores = jnp.where(allowed[None], scores, negative_fill)
    highest = jnp.max(scores, axis=-1, keepdims=True)
    shifted_exp = jnp.where(allowed[None], jnp.exp(scores - highest), 0.0)
    return shifted_exp / jnp.sum(shifted_exp, axis=-1, keepdims=True)


def attend(query_rows, key_rows, allowed):
    model_width = query_rows.shape[1]
    probability = softmax_keys(
        split_heads(query_rows), split_heads(key_rows[:, :model_width]), allowed
    )
    attended = jnp.einsum(
        "hij,jhd->ihd",
        probability.astype(jnp.bfloat16),
        split_heads(key_rows[:, model_width:]),
        preferred_element_type=jnp.float32,
    )
    return attended.reshape(query_rows.shape).astype(jnp.bfloat16)


def attend_back(query_rows, key_rows, allowed, incoming, attended, w_proj):
    model_width = query_rows.shape[1]
    queries = split_heads(query_rows)
    key_heads = split_heads(key_rows[:, :model_width])
    value_heads = split_heads(key_rows[:, model_width:])
    probability = softmax_keys(queries, key_heads, allowed)
    rounded = probability.astype(jnp.bfloat16)
    upstream = lax.dot_general(
        incoming, w_proj, (((1,), (1,)), ((), ())), preferred_element_type=jnp.float32
    ).astype(jnp.bfloat16)
    up_heads = split_heads(upstream)
    delta = jnp.einsum(
        "ihd,ihd->hi", up_heads.astype(jnp.float32), split_heads(attended).astype(jnp.float32)
    )[..., None]
    prob_grad = jnp.einsum(
        "ihd,jhd->hij", up_heads, value_heads, preferred_element_type=jnp.float32
    )
    score_grad = (probability * (prob_grad - delta)).astype(jnp.bfloat16)
    scale_factor = HEAD_DIM ** (-0.5)
    query_grad = (
        jnp.einsum("hij,jhd->ihd", score_grad, key_heads, preferred_element_type=jnp.float32)
        * scale_factor
    )
    key_grad = (
        jnp.einsum("hij,ihd->jhd", score_grad, queries, preferred_element_type=jnp.float32)
        * scale_factor
    )
    value_grad = jnp.einsum("hij,ihd->jhd", rounded, up_heads, preferred_element_type=jnp.float32)
    return (
        query_grad.reshape(-1, model_width),
        key_grad.reshape(-1, model_width),
        value_grad.reshape(-1, model_width),
    )


def per_device(acts, grad_top, w_in, w_out, offsets):
    sections = lax.axis_size("section")
    shards = lax.axis_size("tm")
    levels = shards.bit_length() - 1
    section_index = lax.axis_index("section")
    micro_count = acts.shape[1]
    shard_rows = acts.shape[2]
    model_width = acts.shape[3]
    w_qkv = w_in[0]
    w_proj = w_out[0]
    level_flags = offsets[0]
    normed, inverse_rms = normalize(acts[0])
    rounded_norm = normed.astype(jnp.bfloat16)
    qkv = jnp.dot(rounded_norm.reshape(-1, model_width), w_qkv, preferred_element_type=jnp.float32)
    qkv = qkv.astype(jnp.bfloat16).reshape(micro_count, shard_rows, 3 * model_width)
    pairs = qkv[..., model_width:]
    far_list = [shifted(pairs, "tm", 2**level) for level in range(levels)]
    key_rows = jnp.concatenate([pairs] + far_list, 1)
    allowed = key_bias(level_flags, shard_rows)
    attended = jnp.stack(
        [
            attend(qkv[index, :, :model_width], key_rows[index], allowed)
            for index in range(micro_count)
        ],
        0,
    )

    def attention_part(incoming, slot):
        query_rows = lax.dynamic_index_in_dim(qkv, slot, 0, False)[:, :model_width]
        slot_keys = lax.dynamic_index_in_dim(key_rows, slot, 0, False)
        slot_attended = lax.dynamic_index_in_dim(attended, slot, 0, False)
        query_grad, key_grad, value_grad = attend_back(
            query_rows, slot_keys, allowed, incoming, slot_attended, w_proj
        )
        owner_sum = jnp.concatenate([key_grad[:shard_rows], value_grad[:shard_rows]], 1)
        far_part = jnp.concatenate([key_grad[shard_rows:], value_grad[shard_rows:]], 1)
        far_part = far_part.astype(jnp.bfloat16).reshape(levels, shard_rows, 2 * model_width)
        return (query_grad, owner_sum, far_part)

    def empty_attention(incoming, slot):
        return (
            jnp.zeros((shard_rows, model_width), jnp.float32),
            jnp.zeros((shard_rows, 2 * model_width), jnp.float32),
            jnp.zeros((levels, shard_rows, 2 * model_width), jnp.bfloat16),
        )

    def norm_part(qkv_grad, incoming, slot):
        norm_grad = lax.dot_general(
            qkv_grad, w_qkv, (((1,), (1,)), ((), ())), preferred_element_type=jnp.float32
        )
        slot_normed = lax.dynamic_index_in_dim(normed, slot, 0, False)
        slot_rms = lax.dynamic_index_in_dim(inverse_rms, slot, 0, False)
        inner = jnp.mean(norm_grad * slot_normed, axis=-1, keepdims=True)
        return (incoming.astype(jnp.float32) + slot_rms * (norm_grad - slot_normed * inner)).astype(
            jnp.bfloat16
        )

    def empty_norm(qkv_grad, incoming, slot):
        return jnp.zeros((shard_rows, model_width), jnp.bfloat16)

    def step(turn, carry):
        received, grad_store, qkv_store, incoming_store = carry
        slot_raw = turn - (sections - 1 - section_index)
        active = (slot_raw >= 0) & (slot_raw < micro_count)
        slot = jnp.clip(slot_raw, 0, micro_count - 1)
        incoming = jnp.where(
            section_index == sections - 1,
            lax.dynamic_index_in_dim(grad_top, slot, 0, False),
            received,
        )
        query_grad, owner_sum, far_part = lax.cond(
            active, attention_part, empty_attention, incoming, slot
        )
        for level in range(levels):
            owner_sum = owner_sum + shifted(far_part[level], "tm", -(2**level)).astype(jnp.float32)
        qkv_grad = jnp.concatenate([query_grad, owner_sum], 1).astype(jnp.bfloat16)
        grad_in = lax.cond(active, norm_part, empty_norm, qkv_grad, incoming, slot)
        sent_down = shifted(grad_in, "section", -1)
        grad_store = jnp.where(
            active, lax.dynamic_update_index_in_dim(grad_store, grad_in, slot, 0), grad_store
        )
        qkv_store = jnp.where(
            active, lax.dynamic_update_index_in_dim(qkv_store, qkv_grad, slot, 0), qkv_store
        )
        incoming_store = jnp.where(
            active,
            lax.dynamic_update_index_in_dim(incoming_store, incoming, slot, 0),
            incoming_store,
        )
        return (sent_down, grad_store, qkv_store, incoming_store)

    initial = (
        jnp.zeros((shard_rows, model_width), jnp.bfloat16),
        jnp.zeros((micro_count, shard_rows, model_width), jnp.bfloat16),
        jnp.zeros((micro_count, shard_rows, 3 * model_width), jnp.bfloat16),
        jnp.zeros((micro_count, shard_rows, model_width), jnp.bfloat16),
    )
    received, grad_store, qkv_store, incoming_store = lax.fori_loop(
        0, sections + micro_count - 1, step, initial
    )
    flat_norm = rounded_norm.reshape(-1, model_width)
    flat_attended = attended.reshape(-1, model_width)
    flat_qkv = qkv_store.reshape(-1, 3 * model_width)
    flat_incoming = incoming_store.reshape(-1, model_width)
    contract = (((0,), (0,)), ((), ()))
    first = lax.dot_general(flat_norm, flat_qkv, contract, preferred_element_type=jnp.float32)
    second = lax.dot_general(
        flat_attended, flat_incoming, contract, preferred_element_type=jnp.float32
    )
    summed = lax.psum_scatter(
        jnp.concatenate([first, second], 1).astype(jnp.bfloat16),
        "tm",
        scatter_dimension=0,
        tiled=True,
    ).astype(jnp.float32)
    return (
        grad_store[None],
        summed[None, :, : 3 * model_width],
        summed[None, :, 3 * model_width :],
    )


def side_by_side(transposed, pair):
    width = 2 * HEAD_DIM
    rows = transposed[pair * width : (pair + 1) * width]
    empty = jnp.zeros((HEAD_DIM, rows.shape[1]), rows.dtype)
    return jnp.concatenate(
        [
            jnp.concatenate([rows[:HEAD_DIM], empty], 0),
            jnp.concatenate([empty, rows[HEAD_DIM:]], 0),
        ],
        1,
    )


def one_above_other(rows, masks):
    return jnp.concatenate([rows * masks[0], rows * masks[1]], 0)


def head_masks():
    lane = lax.broadcasted_iota(jnp.int32, (1, 2 * HEAD_DIM), 1)
    return [
        jnp.where(lane < HEAD_DIM, 1.0, 0.0).astype(jnp.bfloat16),
        jnp.where(lane < HEAD_DIM, 0.0, 1.0).astype(jnp.bfloat16),
    ]


def key_bias_rows(flag_rows, levels, shard_rows, keys, first_query, count):
    key_at = lax.broadcasted_iota(jnp.int32, (keys, count), 0)
    query_at = lax.broadcasted_iota(jnp.int32, (keys, count), 1) + first_query
    gap = lax.div(query_at, shard_rows) - lax.div(key_at, shard_rows)
    allowed = (gap == 0) & (key_at <= query_at)
    for level in range(levels):
        allowed = allowed | ((gap == 2**level) & (flag_rows[level : level + 1] != 0))
    return jnp.where(allowed, 0.0, negative_fill)


def softmax_pass(queries, keys, values, bias, prob_ref, at_ref):
    queries_t = queries.T
    values_t = values.T
    width = 2 * HEAD_DIM
    count = queries.shape[0]
    for pair in range(queries.shape[1] // width):
        at_pair = slice(pair * width, (pair + 1) * width)
        scores = jnp.dot(
            keys[:, at_pair], side_by_side(queries_t, pair), preferred_element_type=jnp.float32
        )
        for half in range(2):
            at_half = slice(half * count, (half + 1) * count)
            biased = scores[:, at_half] + bias
            shifted_exp = jnp.exp(biased - jnp.max(biased, axis=0, keepdims=True))
            probability = shifted_exp * (1.0 / jnp.sum(shifted_exp, axis=0, keepdims=True))
            prob_ref[pair, :, at_half] = probability.astype(jnp.bfloat16)
    for head in range(queries.shape[1] // HEAD_DIM):
        at = slice(head * HEAD_DIM, (head + 1) * HEAD_DIM)
        at_half = slice(head % 2 * count, (head % 2 + 1) * count)
        at_ref[at] = jnp.dot(
            values_t[at], prob_ref[head // 2, :, at_half], preferred_element_type=jnp.float32
        ).astype(jnp.bfloat16)


def pack_kernel(
    levels, info_ref, acts_ref, top_ref, own_ref, other_ref, own_top_ref, other_top_ref
):
    model_width = acts_ref.shape[2]
    shard_rows = own_ref.shape[0]
    micro = info_ref[4]
    lane = lax.broadcasted_iota(jnp.int32, (shard_rows, own_ref.shape[1] - model_width), 1)
    flags = jnp.zeros(lane.shape, jnp.float32)
    for level in range(levels):
        seen = jnp.where(info_ref[5 + level] != 0, 1.0, 0.0)
        flags = jnp.where(lane == level, seen, flags)
    for at, out_ref, out_top_ref in (
        (micro, own_ref, own_top_ref),
        (1 - micro, other_ref, other_top_ref),
    ):
        out_ref[:, :model_width] = acts_ref[at]
        out_ref[:, model_width:] = flags.astype(jnp.bfloat16)
        out_top_ref[...] = top_ref[at]


def turn_kernel(own, info_ref, w_ref, after_ref, out_ref):
    columns = out_ref.shape[0] // 3
    model_width = w_ref.shape[0]
    half = info_ref[0] if own else 1 - info_ref[0]
    for block in range(3):
        first = pl.multiple_of(block * model_width + half * columns, 128)
        out_ref[block * columns : (block + 1) * columns] = w_ref[:, pl.ds(first, columns)].T


def project_kernel(replicas, info_ref, *refs):
    pieces = refs[: 4 * replicas]
    w_ref, _, normed_ref, rms_ref, norm_ref, flag_ref, q_ref, k_ref, v_ref, kt_ref, packed_ref = refs[
        4 * replicas :
    ]
    shards, shard_rows = packed_ref.shape[:2]
    model_width = w_ref.shape[0]
    seq = shards * shard_rows
    columns = q_ref.shape[1]
    at_piece = 0
    for core in (info_ref[0], 1 - info_ref[0]):
        for side in (info_ref[2], 1 - info_ref[2]):
            for step in range(replicas):
                shard = side * (shards // 2) + place_of(info_ref, step, replicas) + core
                packed_ref[shard] = pieces[at_piece][...]
                at_piece += 1
    for chunk in range(2):
        for step in range(replicas):
            shard = chunk * (shards // 2) + place_of(info_ref, step, replicas) + info_ref[0]
            normed, inverse_rms = normalize(packed_ref[shard][:, :model_width])
            normed_ref[chunk, step] = normed
            rms_ref[chunk, step] = jnp.broadcast_to(inverse_rms, rms_ref.shape[2:])
    normed, _ = normalize(packed_ref[:, :, :model_width].reshape(seq, model_width))
    rounded = normed.astype(jnp.bfloat16)
    norm_ref[...] = rounded
    flag_ref[...] = packed_ref[:, :, model_width:].reshape(seq, -1).astype(jnp.float32).T
    scale_factor = HEAD_DIM ** (-0.5)
    for block, out_ref in enumerate((q_ref, k_ref, v_ref)):
        first = pl.multiple_of(block * model_width + info_ref[0] * columns, 128)
        product = jnp.dot(
            rounded, w_ref[:, pl.ds(first, columns)], preferred_element_type=jnp.float32
        ).astype(jnp.bfloat16)
        out_ref[...] = product * scale_factor if block == 0 else product
    kt_ref[...] = (k_ref[...] * scale_factor).T


def upper_forward_kernel(
    levels, shard_rows, flag_ref, q_ref, k_ref, v_ref, prob_ref, at_ref
):
    seq = q_ref.shape[0]
    count = seq // 2
    bias = key_bias_rows(flag_ref[:, count:], levels, shard_rows, seq, count, count)
    softmax_pass(q_ref[count:], k_ref[...], v_ref[...], bias, prob_ref, at_ref)


def lower_forward_kernel(
    levels,
    shard_rows,
    info_ref,
    norm_ref,
    flag_ref,
    q_ref,
    k_ref,
    v_ref,
    after_ref,
    prob_ref,
    at_ref,
    gt_ref,
):
    seq = norm_ref.shape[0]
    count = seq // 2
    bias = key_bias_rows(flag_ref[:, :count], levels, shard_rows, count, 0, count)
    softmax_pass(q_ref[:count], k_ref[:count], v_ref[:count], bias, prob_ref, at_ref)
    rows = gt_ref.shape[0] // 4
    parity, x, y = info_ref[0], info_ref[1], info_ref[2]
    half = norm_ref.shape[1] // rows // 2
    for place, block in enumerate(
        (
            half * y + 2 * x + 1 - parity,
            half * y + 2 * x + parity,
            half * y + 2 * (1 - x) + 1 - parity,
            half * (1 - y) + 2 * x + parity,
        )
    ):
        first = pl.multiple_of(block * rows, 128)
        gt_ref[place * rows : (place + 1) * rows] = norm_ref[:, pl.ds(first, rows)].T


def place_of(info_ref, step, replicas):
    return 2 * lax.rem(info_ref[1] - step + replicas, replicas)


def merge_rows(info_ref, fresh, got_refs, kept_refs, out_refs, rows_ref):
    @pl.when(fresh)
    def _():
        for core, out_ref in enumerate(out_refs):
            out_ref[...] = got_refs[core][...]

    @pl.when(jnp.logical_not(fresh))
    def _():
        for out_ref, kept_ref in zip(out_refs, kept_refs):
            out_ref[...] = kept_ref[...]

    place_rows(info_ref, out_refs, rows_ref)


def place_rows(info_ref, out_refs, rows_ref):
    replicas = out_refs[0].shape[0]
    for step in range(replicas):
        place = place_of(info_ref, step, replicas)
        rows_ref[place + info_ref[0]] = out_refs[0][step]
        rows_ref[place + 1 - info_ref[0]] = out_refs[1][step]


def merge_tops(info_ref, upper, piece_refs, out_refs, rows_ref):
    replicas = out_refs[0].shape[0]
    own_chunk = info_ref[2] == (1 if upper else 0)
    for core in range(2):
        refs = piece_refs[2 * replicas * core : 2 * replicas * (core + 1)]

        @pl.when(own_chunk)
        def _():
            for step in range(replicas):
                out_refs[core][step] = refs[step][...]

        @pl.when(jnp.logical_not(own_chunk))
        def _():
            for step in range(replicas):
                out_refs[core][step] = refs[replicas + step][...]

    place_rows(info_ref, out_refs, rows_ref)


def backward_kernel(upper, tops, last, fresh_section, info_ref, *refs):
    refs = list(refs)
    got = tops or 4
    got_refs = refs[:got]
    w_ref, prob_ref, q_ref, v_ref, kt_ref, at_ref = refs[got : got + 6]
    refs = refs[got + 6 :]
    if not upper:
        key_sum_ref, value_sum_ref = refs[:2]
        refs = refs[2:]
    refs = refs[1:]
    if last:
        refs = [refs[0], refs[-1], *refs[1:-1]]
    own_ref, other_ref, keep_ref = refs[:3]
    send_refs = refs[3 : 3 + PIECES[upper]]
    refs = refs[3 + len(send_refs) :]
    if upper:
        key_sum_ref, value_sum_ref = refs[:2]
        refs = refs[2:]
    grads_ref, rows_ref, scores_ref = refs
    replicas, shard_rows, model_width = own_ref.shape
    count = rows_ref.shape[0] * shard_rows
    keys = prob_ref.shape[1]
    parity = info_ref[0]
    columns = q_ref.shape[1]
    width = 2 * HEAD_DIM
    if tops:
        merge_tops(info_ref, upper, got_refs, (own_ref, other_ref), rows_ref)
    else:
        fresh = info_ref[3] == fresh_section
        merge_rows(info_ref, fresh, got_refs[:-2], got_refs[-2:], (own_ref, other_ref), rows_ref)
    rows = rows_ref[...].reshape(count, model_width)
    weights = w_ref[pl.ds(pl.multiple_of(parity * columns, 128), columns), :]
    over_width = (((1,), (1,)), ((), ()))
    upstream = lax.dot_general(
        rows, weights, over_width, preferred_element_type=jnp.float32
    ).astype(jnp.bfloat16)
    upstream_t = upstream.T
    product_t = upstream_t.astype(jnp.float32) * at_ref[...].astype(jnp.float32)
    first_query = keys - count
    masks = head_masks()

    def put(block, pair, part):
        first = block * columns + pair * width
        grads_ref[:, :, first : first + width] = part.astype(jnp.bfloat16).reshape(
            -1, shard_rows, width
        )

    for pair in range(columns // width):
        at_pair = slice(pair * width, (pair + 1) * width)
        prob_grad = jnp.dot(
            v_ref[:keys, at_pair], side_by_side(upstream_t, pair), preferred_element_type=jnp.float32
        )
        for half in range(2):
            at_half = slice(half * count, (half + 1) * count)
            first = pair * width + half * HEAD_DIM
            delta = jnp.sum(product_t[first : first + HEAD_DIM], axis=0, keepdims=True)
            scores_ref[pair, :, at_half] = (
                prob_ref[pair, :, at_half].astype(jnp.float32) * (prob_grad[:, at_half] - delta)
            ).astype(jnp.bfloat16)
        value_grad = jnp.dot(
            prob_ref[pair],
            one_above_other(upstream[:, at_pair], masks),
            preferred_element_type=jnp.float32,
        )
        if upper:
            value_sum_ref[:, at_pair] = value_grad[:first_query]
            value_grad = value_grad[first_query:]
        else:
            value_grad = value_grad + value_sum_ref[:, at_pair]
        put(2, pair, value_grad)
    for pair in range(columns // width):
        at_pair = slice(pair * width, (pair + 1) * width)
        queries = q_ref[first_query : first_query + count, at_pair]
        key_grad = jnp.dot(
            scores_ref[pair], one_above_other(queries, masks), preferred_element_type=jnp.float32
        )
        if upper:
            key_sum_ref[:, at_pair] = key_grad[:first_query]
            key_grad = key_grad[first_query:]
        else:
            key_grad = key_grad + key_sum_ref[:, at_pair]
        put(1, pair, key_grad)
        query_grad = [
            jnp.dot(
                kt_ref[pair * width + half * HEAD_DIM : pair * width + (half + 1) * HEAD_DIM, :keys],
                scores_ref[pair, :, half * count : (half + 1) * count],
                preferred_element_type=jnp.float32,
            )
            for half in range(2)
        ]
        put(0, pair, jnp.concatenate(query_grad, 0).astype(jnp.bfloat16).T)
    for step in range(replicas):
        place = place_of(info_ref, step, replicas)
        keep_ref[step] = grads_ref[place + parity]
        crossing = grads_ref[place + 1 - parity]
        part = crossing.shape[1] // len(send_refs)
        for at, send_ref in enumerate(send_refs):
            send_ref[step] = crossing[:, at * part : (at + 1) * part]


def norm_part_kernel(info_ref, keep_ref, w_ref, after_ref, out_ref):
    part = keep_ref[...].reshape(out_ref.shape[0], -1)
    out_ref[...] = jnp.dot(part, w_ref[...], preferred_element_type=jnp.float32)


def norm_kernel(upper, info_ref, keep_ref, normed_ref, rms_ref, incoming_ref, *refs):
    w_own_ref, w_other_ref = refs[:2]
    refs = refs[2:]
    got_refs = refs[: PIECES[upper]]
    out_refs = refs[len(got_refs) :]
    replicas, shard_rows, model_width = incoming_ref.shape
    rows = replicas * shard_rows
    got = [got_ref[...].reshape(rows, -1) for got_ref in got_refs]
    norm_grad = jnp.dot(
        jnp.concatenate(got, 1), w_other_ref[...], preferred_element_type=jnp.float32
    )
    if upper:
        norm_grad += keep_ref[...]
    else:
        norm_grad += jnp.dot(
            keep_ref[...].reshape(rows, -1), w_own_ref[...], preferred_element_type=jnp.float32
        )
    chunk = 1 if upper else 0
    normed = normed_ref[chunk].reshape(rows, model_width)
    inverse_rms = rms_ref[chunk].reshape(rows, -1)[:, :1]
    inner = jnp.mean(norm_grad * normed, axis=-1, keepdims=True)
    incoming = incoming_ref[...].reshape(rows, model_width).astype(jnp.float32)
    grad_in = incoming + inverse_rms * (norm_grad - normed * inner)
    grad_in = grad_in.astype(jnp.bfloat16).reshape(replicas, shard_rows, model_width)
    out_refs[-1][...] = grad_in


def in_terms(gt_ref, grad_refs, half, rows):
    count = grad_refs[0].shape[0] * grad_refs[0].shape[1]
    return sum(
        jnp.dot(
            gt_ref[2 * half * rows : 2 * (half + 1) * rows, chunk * count : (chunk + 1) * count],
            part_ref[...].reshape(count, -1),
            preferred_element_type=jnp.float32,
        )
        for chunk, part_ref in enumerate(grad_refs)
    )


def send_kernel(gt_ref, lower_ref, upper_ref, pass_ref, keep_ref):
    rows = pass_ref.shape[0]
    total = in_terms(gt_ref, (lower_ref, upper_ref), 1, rows)
    pass_ref[...] = total[:rows].astype(jnp.bfloat16)
    keep_ref[...] = total[rows:].astype(jnp.bfloat16)


def term_kernel(info_ref, gt_ref, *refs):
    grad_refs, at_refs, row_refs = refs[:2], refs[2:4], refs[4:6]
    pass_ref, keep_ref, out_pass_ref, out_keep_ref, out_send_ref = refs[7:]
    rows = pass_ref.shape[0]
    width = out_send_ref.shape[1]
    parity, x, y = info_ref[0], info_ref[1], info_ref[2]
    sent = jnp.where(parity == y, 2 * (1 - x) + 1 - parity, 2 * x + parity)
    blocks = (sent, 2 * x + 1 - parity, 2 * x + parity)
    total = jnp.zeros((3 * rows, width), jnp.float32)
    for at_ref, part_ref in zip(at_refs, row_refs):
        picked = [at_ref[pl.ds(pl.multiple_of(block * rows, 128), rows)] for block in blocks]
        total += jnp.dot(
            jnp.concatenate(picked, 0),
            part_ref[...].reshape(-1, width),
            preferred_element_type=jnp.float32,
        )
    out_send_ref[...] = total[:rows].astype(jnp.bfloat16)
    out_pass_ref[...] = total[rows : 2 * rows]
    out_keep_ref[...] = total[2 * rows :]
    total = in_terms(gt_ref, grad_refs, 0, rows)
    pass_ref[...] = total[:rows]
    keep_ref[...] = total[rows:]


def sum_kernel(own_ref, got_ref, out_own_ref, out_got_ref, after_ref, sum_ref):
    columns = own_ref.shape[1]
    sum_ref[:, :columns] = (own_ref[...] + got_ref[...].astype(jnp.float32)).astype(jnp.bfloat16)
    sum_ref[:, columns:] = (out_own_ref[...] + out_got_ref[...].astype(jnp.float32)).astype(
        jnp.bfloat16
    )


def pick_kernel(info_ref, upper_ref, lower_ref, out_ref):
    crossing = info_ref[0] == 0
    for step in range(2):
        for chunk, part_ref in enumerate((lower_ref, upper_ref)):
            wanted = info_ref[2] == (chunk if step == 1 else 1 - chunk)

            @pl.when(wanted & (crossing if step == 1 else jnp.logical_not(crossing)))
            def _():
                out_ref[...] = part_ref[step]


def join_kernel(info_ref, upper_ref, lower_ref, got_ref, out_ref):
    micro = info_ref[4]
    out_ref[0, 1 - micro] = got_ref[...]

    @pl.when(info_ref[2] == 1)
    def _():
        out_ref[0, micro] = upper_ref[0]

    @pl.when(info_ref[2] != 1)
    def _():
        out_ref[0, micro] = lower_ref[0]


def place_kernel(
    info_ref, own_ref, got_ref, out_own_ref, out_got_ref, sibling_ref, d_in_ref, d_out_ref
):
    columns = own_ref.shape[1] // 3
    own = own_ref[...] + got_ref[...].astype(jnp.float32)
    sibling = sibling_ref[:, : 3 * columns].astype(jnp.float32)
    for part, half in ((own, info_ref[0]), (sibling, 1 - info_ref[0])):
        for block in range(3):
            first = pl.multiple_of((2 * block + half) * columns, 128)
            d_in_ref[:, pl.ds(first, columns)] = part[:, block * columns : (block + 1) * columns]
    owner = info_ref[0] == info_ref[2]

    @pl.when(owner)
    def _():
        d_out_ref[...] = out_own_ref[...] + out_got_ref[...].astype(jnp.float32)

    @pl.when(jnp.logical_not(owner))
    def _():
        d_out_ref[...] = sibling_ref[:, 3 * columns :].astype(jnp.float32)


def call(kernel, outs, operands, scratch=(), flops=0, scalars=1, after=None, mebibytes=5, far=0):
    in_specs = [pl.BlockSpec(memory_space=pltpu.SMEM)] * scalars
    in_specs += [pl.BlockSpec(memory_space=pltpu.HBM)] * far
    in_specs += [pl.BlockSpec(memory_space=pltpu.VMEM)] * (len(operands) - scalars - far)
    if after is not None:
        operands = [*operands, after]
        in_specs.append(pl.BlockSpec(memory_space=pl.ANY))
    return pl.pallas_call(
        kernel,
        out_shape=list(outs),
        in_specs=in_specs,
        out_specs=[pl.BlockSpec(memory_space=pltpu.VMEM)] * len(outs),
        scratch_shapes=list(scratch),
        cost_estimate=pl.CostEstimate(flops=1, bytes_accessed=1, transcendentals=0),
        compiler_params=pltpu.CompilerParams(vmem_limit_bytes=mebibytes * 2**20),
    )(*operands)


def by_chips(acts, grad_top, w_in, w_out, offsets):
    half_type, full_type = jnp.bfloat16, jnp.float32
    shape = jax.ShapeDtypeStruct
    sections = lax.axis_size("section")
    shards = lax.axis_size("tm")
    levels = offsets.shape[1]
    half = shards // 2
    replicas = half // 2
    me = lax.axis_index("tm")
    parity = lax.rem(me, 2)
    side = lax.div(me, half)
    micro_count, shard_rows, model_width = acts.shape[1:]
    columns = model_width // 2
    heads = columns // HEAD_DIM
    seq = shards * shard_rows
    count = seq // 2
    w_qkv = w_in[0]
    w_rows = w_out[0]
    beside = lax.div(lax.rem(me, half), 2)
    micro = lax.rem(side + beside, 2)
    info = jnp.stack([parity, beside, side, lax.axis_index("section"), micro])
    info = jnp.concatenate([info.astype(jnp.int32), offsets[0]])

    def swapped(value, bits, chosen=None):
        pairs = [(device, device ^ bits) for device in range(shards)]
        pairs = [pair for pair in pairs if chosen is None or chosen(pair[0])]
        return lax.ppermute(value, "tm", pairs)

    core, near, far = 1, 2, half

    packed = shape((shard_rows, model_width + 128), half_type)
    top_shape = shape((shard_rows, model_width), half_type)
    own_acts, other_acts, own_top, other_top = call(
        functools.partial(pack_kernel, levels),
        [packed, packed, top_shape, top_shape],
        [info, acts[0], grad_top],
    )
    weights = [
        call(
            functools.partial(turn_kernel, own),
            [shape((3 * columns, model_width), half_type)],
            [info, w_qkv],
            after=own_acts,
        )[0]
        for own in (True, False)
    ]
    pieces = [own_acts, swapped(other_acts, near), swapped(other_acts, far)]
    pieces += [swapped(own_acts, near + far)]
    tops = [own_top, swapped(other_top, near), swapped(other_top, far)]
    pieces[-1], tops, weights = lax.optimization_barrier((pieces[-1], tops, weights))
    tops += [swapped(own_top, near + far)]
    pieces += [swapped(piece, core) for piece in pieces]

    rows_shape = shape((seq, columns), half_type)
    normed, rms, norm, flag_rows, queries, keys, values, keys_t = call(
        functools.partial(project_kernel, replicas),
        [
            shape((2, replicas, shard_rows, model_width), full_type),
            shape((2, replicas, shard_rows, 128), full_type),
            shape((seq, model_width), half_type),
            shape((128, seq), full_type),
            rows_shape,
            rows_shape,
            rows_shape,
            shape((columns, seq), half_type),
        ],
        [info, *pieces, w_qkv],
        scratch=[pltpu.VMEM((shards, *packed.shape), half_type)],
        flops=6 * seq * model_width * columns,
        after=weights[1],
    )
    pairs = heads // 2
    upper_prob, upper_at = call(
        functools.partial(upper_forward_kernel, levels, shard_rows),
        [
            shape((pairs, seq, 2 * count), half_type),
            shape((columns, count), half_type),
        ],
        [flag_rows, queries, keys, values],
        scalars=0,
        flops=4 * columns * seq * count,
    )
    tops, upper_at = lax.optimization_barrier((tuple(tops), upper_at))
    tops = [*tops, *[swapped(piece, core) for piece in tops]]
    own_rows = model_width // shards
    probs, attended = {True: upper_prob}, {True: upper_at}
    got, kept = {}, {}
    piece_shape = shape((replicas, shard_rows, model_width), half_type)
    grads_shape = shape((replicas, shard_rows, 3 * columns), half_type)
    sum_shape = shape((count, columns), full_type)
    full_grads = shape((half, shard_rows, 3 * columns), half_type)
    full_rows = shape((half, shard_rows, model_width), half_type)
    term_shape = (own_rows, 3 * columns)
    rows_scratch = pltpu.VMEM(full_rows.shape, half_type)
    grads_scratch = pltpu.VMEM(full_grads.shape, half_type)
    result, full, ordered = {}, {}, {}
    for turn in range(sections):
        last = turn + 1 == sections
        fresh_section = sections - 1 - turn
        sums, parts, crossed = [], {}, {}

        def norm_step(upper, after):
            (result[upper],) = call(
                functools.partial(norm_kernel, upper),
                [piece_shape],
                [info, parts[upper], normed, rms, kept[upper][0], *weights, *crossed[upper]],
                after=after,
            )
            if not last:
                hop = [(sections - 1 - turn, sections - 2 - turn)]
                got[upper] = lax.ppermute(result[upper], "section", hop)

        for upper in (True, False):
            rows_in, after = tops, keys_t if upper else result.get(True)
            if turn:
                before = result[False] if upper else result[True]
                got[upper], after = lax.optimization_barrier((got[upper], before))
                if not upper:
                    result[True] = after
                rows_in = [got[upper], swapped(got[upper], core), *kept[upper]]
            part = 3 * columns // PIECES[upper]
            cross = [shape((replicas, shard_rows, part), half_type)] * PIECES[upper]
            outs = [piece_shape] * (1 if last else 2) + [grads_shape, *cross]
            outs += [sum_shape, sum_shape] if upper else []
            scratch = []
            if last:
                outs += [full_grads]
            else:
                scratch += [grads_scratch]
            if last:
                outs += [full_rows]
            else:
                scratch += [rows_scratch]
            part_keys = seq if upper else count
            scratch += [pltpu.VMEM((pairs, part_keys, 2 * count), half_type)]
            if last:
                scratch += [pltpu.VMEM(piece_shape.shape, half_type)]
            answer = call(
                functools.partial(
                    backward_kernel, upper, 0 if turn else len(tops), last, fresh_section
                ),
                outs,
                [info, *rows_in, w_rows, probs[upper], queries, values, keys_t]
                + [attended[upper], *sums],
                scratch=scratch,
                flops=2 * count * columns * (2 * model_width + 4 * part_keys),
                after=after,
            )
            kept[upper] = tuple(answer[:2])
            answer = answer[1 if last else 2 :]
            keep = answer[0]
            send = answer[1 : 1 + len(cross)]
            parts[upper] = keep
            if upper:
                sums = answer[1 + len(cross) : 3 + len(cross)]
                (parts[True],) = call(
                    norm_part_kernel,
                    [shape((replicas * shard_rows, model_width), full_type)],
                    [info, keep, weights[0]],
                    flops=3 * replicas * shard_rows * model_width * model_width,
                    after=keep,
                )
                if turn == 0:
                    lower_prob, lower_at, norm_t = call(
                        functools.partial(lower_forward_kernel, levels, shard_rows),
                        [
                            shape((pairs, count, 2 * count), half_type),
                            shape((columns, count), half_type),
                            shape((4 * own_rows, seq), half_type),
                        ],
                        [info, norm, flag_rows, queries, keys, values],
                        flops=4 * columns * count * count,
                        after=parts[True],
                    )
                    probs[False], attended[False] = lower_prob, lower_at
            if last:
                full[upper], ordered[upper] = answer[-2:]
            crossed[upper] = [swapped(piece, core) for piece in send]
            if upper:
                norm_step(True, keep)
        if last:
            send_pass, send_keep = call(
                send_kernel,
                [shape(term_shape, half_type)] * 2,
                [norm_t, full[False], full[True]],
                scalars=0,
            )
            terms = call(
                term_kernel,
                [shape(term_shape, full_type)] * 2
                + [shape((own_rows, model_width), full_type)] * 2
                + [shape((own_rows, model_width), half_type)],
                [info, norm_t, full[False], full[True], attended[False], attended[True]]
                + [ordered[False], ordered[True]],
                after=send_keep,
            )
        norm_step(False, terms[4] if last else result[True])

    in_pass, in_keep, out_pass, out_keep, out_send = terms
    got_pass = swapped(send_pass, near)
    got_keep = swapped(send_keep, far)
    own_rows_grad = [result[True], result[False]]
    (theirs,) = call(pick_kernel, [top_shape], [info, *own_rows_grad])
    to_owner = [(device, device ^ (far if device % 2 else near)) for device in range(shards)]
    partner = lax.ppermute(theirs, "tm", to_owner)
    got_out_pass = swapped(out_send, near, lambda device: device // half == device % 2)
    got_out_keep = swapped(out_send, far, lambda device: device // half != device % 2)
    _, _, done = lax.optimization_barrier((got_keep, got_out_keep, partner))
    (summed,) = call(
        sum_kernel,
        [shape((own_rows, 3 * columns + model_width), half_type)],
        [in_pass, got_pass, out_pass, got_out_pass],
        scalars=0,
        after=done,
    )
    d_w_in, d_w_out = call(
        place_kernel,
        [
            shape((own_rows, 3 * model_width), full_type),
            shape((own_rows, model_width), full_type),
        ],
        [info, in_keep, got_keep, out_keep, got_out_keep, swapped(summed, core)],
    )
    (d_acts,) = call(
        join_kernel, [shape(acts.shape, half_type)], [info, *own_rows_grad, partner]
    )
    return (d_acts, d_w_in[None], d_w_out[None])


def layer_gradients(acts, grad_top, w_in, w_out, offsets):
    shards = lax.axis_size("tm")
    micro_count, shard_rows, model_width = acts.shape[1:]
    heads = model_width // HEAD_DIM
    prob_bytes = 2 * heads * (shards * shard_rows) ** 2
    fits = prob_bytes <= 2**24 and model_width % (128 * shards) == 0 and shard_rows % 16 == 0
    square = shards % 4 == 0 and shards // 4 == 2
    if micro_count == 2 and square and heads % 4 == 0 and fits:
        return by_chips(acts, grad_top, w_in, w_out, offsets)
    return per_device(acts, grad_top, w_in, w_out, offsets)


def solution(mesh):
    placed = (
        P("section", None, "tm", None),
        P(None, "tm", None),
        P("section", None, None),
        P("section", None, None),
        P("tm", None),
    )
    return jax.shard_map(
        layer_gradients,
        mesh=mesh,
        in_specs=placed,
        out_specs=(
            P("section", None, "tm", None),
            P("section", "tm", None),
            P("section", "tm", None),
        ),
        check_vma=False,
    )
```

```python
import functools
import jax
import jax.numpy as jnp
from jax import lax
from jax.experimental import pallas as pl
from jax.experimental.pallas import tpu as pltpu
from jax.sharding import PartitionSpec as P

HEAD_DIM = 64


epsilon = 1e-06
SPLITS = {True: (6,6), False: (4,4,4)}
negative_fill = -1e30


def shifted(value, axis, steps):
    count = lax.axis_size(axis)
    initial, last = (max(0, -steps), min(count, count - steps))
    return lax.ppermute(value, axis, [(source, source + steps) for source in range(initial, last)])


def normalize(inputs):
    values = inputs.astype(jnp.float32)
    inverse_rms = lax.rsqrt(jnp.mean(values * values, axis=-1, keepdims=True) + epsilon)
    return (values * inverse_rms, inverse_rms)


def key_bias(level_flags, shard_rows):
    position = jnp.arange(shard_rows)
    own_part = position[None, :] <= position[:, None]
    far_part = jnp.repeat(level_flags != 0, shard_rows)
    far_part = jnp.broadcast_to(far_part[None, :], (shard_rows, far_part.shape[0]))
    return jnp.concatenate([own_part, far_part], 1)


def split_heads(row_block):
    return row_block.reshape(row_block.shape[0], -1, HEAD_DIM)


def softmax_keys(queries, key_heads, allowed):
    scores = jnp.einsum(
        "ihd,jhd->hij", queries, key_heads, preferred_element_type=jnp.float32
    ) * HEAD_DIM ** (-0.5)
    scores = jnp.where(allowed[None], scores, negative_fill)
    highest = jnp.max(scores, axis=-1, keepdims=True)
    shifted_exp = jnp.where(allowed[None], jnp.exp(scores - highest), 0.0)
    return shifted_exp / jnp.sum(shifted_exp, axis=-1, keepdims=True)


def attend(query_rows, key_rows, allowed):
    model_width = query_rows.shape[1]
    probability = softmax_keys(
        split_heads(query_rows), split_heads(key_rows[:, :model_width]), allowed
    )
    attended = jnp.einsum(
        "hij,jhd->ihd",
        probability.astype(jnp.bfloat16),
        split_heads(key_rows[:, model_width:]),
        preferred_element_type=jnp.float32,
    )
    return attended.reshape(query_rows.shape).astype(jnp.bfloat16)


def attend_back(query_rows, key_rows, allowed, incoming, attended, w_proj):
    model_width = query_rows.shape[1]
    queries = split_heads(query_rows)
    key_heads = split_heads(key_rows[:, :model_width])
    value_heads = split_heads(key_rows[:, model_width:])
    probability = softmax_keys(queries, key_heads, allowed)
    rounded = probability.astype(jnp.bfloat16)
    upstream = lax.dot_general(
        incoming, w_proj, (((1,), (1,)), ((), ())), preferred_element_type=jnp.float32
    ).astype(jnp.bfloat16)
    up_heads = split_heads(upstream)
    delta = jnp.einsum(
        "ihd,ihd->hi", up_heads.astype(jnp.float32), split_heads(attended).astype(jnp.float32)
    )[..., None]
    prob_grad = jnp.einsum(
        "ihd,jhd->hij", up_heads, value_heads, preferred_element_type=jnp.float32
    )
    score_grad = (probability * (prob_grad - delta)).astype(jnp.bfloat16)
    scale_factor = HEAD_DIM ** (-0.5)
    query_grad = (
        jnp.einsum("hij,jhd->ihd", score_grad, key_heads, preferred_element_type=jnp.float32)
        * scale_factor
    )
    key_grad = (
        jnp.einsum("hij,ihd->jhd", score_grad, queries, preferred_element_type=jnp.float32)
        * scale_factor
    )
    value_grad = jnp.einsum("hij,ihd->jhd", rounded, up_heads, preferred_element_type=jnp.float32)
    return (
        query_grad.reshape(-1, model_width),
        key_grad.reshape(-1, model_width),
        value_grad.reshape(-1, model_width),
    )


def per_device(acts, grad_top, w_in, w_out, offsets):
    sections = lax.axis_size("section")
    shards = lax.axis_size("tm")
    levels = shards.bit_length() - 1
    section_index = lax.axis_index("section")
    micro_count = acts.shape[1]
    shard_rows = acts.shape[2]
    model_width = acts.shape[3]
    w_qkv = w_in[0]
    w_proj = w_out[0]
    level_flags = offsets[0]
    normed, inverse_rms = normalize(acts[0])
    rounded_norm = normed.astype(jnp.bfloat16)
    qkv = jnp.dot(rounded_norm.reshape(-1, model_width), w_qkv, preferred_element_type=jnp.float32)
    qkv = qkv.astype(jnp.bfloat16).reshape(micro_count, shard_rows, 3 * model_width)
    pairs = qkv[..., model_width:]
    far_list = [shifted(pairs, "tm", 2**level) for level in range(levels)]
    key_rows = jnp.concatenate([pairs] + far_list, 1)
    allowed = key_bias(level_flags, shard_rows)
    attended = jnp.stack(
        [
            attend(qkv[index, :, :model_width], key_rows[index], allowed)
            for index in range(micro_count)
        ],
        0,
    )

    def attention_part(incoming, slot):
        query_rows = lax.dynamic_index_in_dim(qkv, slot, 0, False)[:, :model_width]
        slot_keys = lax.dynamic_index_in_dim(key_rows, slot, 0, False)
        slot_attended = lax.dynamic_index_in_dim(attended, slot, 0, False)
        query_grad, key_grad, value_grad = attend_back(
            query_rows, slot_keys, allowed, incoming, slot_attended, w_proj
        )
        owner_sum = jnp.concatenate([key_grad[:shard_rows], value_grad[:shard_rows]], 1)
        far_part = jnp.concatenate([key_grad[shard_rows:], value_grad[shard_rows:]], 1)
        far_part = far_part.astype(jnp.bfloat16).reshape(levels, shard_rows, 2 * model_width)
        return (query_grad, owner_sum, far_part)

    def empty_attention(incoming, slot):
        return (
            jnp.zeros((shard_rows, model_width), jnp.float32),
            jnp.zeros((shard_rows, 2 * model_width), jnp.float32),
            jnp.zeros((levels, shard_rows, 2 * model_width), jnp.bfloat16),
        )

    def norm_part(qkv_grad, incoming, slot):
        norm_grad = lax.dot_general(
            qkv_grad, w_qkv, (((1,), (1,)), ((), ())), preferred_element_type=jnp.float32
        )
        slot_normed = lax.dynamic_index_in_dim(normed, slot, 0, False)
        slot_rms = lax.dynamic_index_in_dim(inverse_rms, slot, 0, False)
        inner = jnp.mean(norm_grad * slot_normed, axis=-1, keepdims=True)
        return (incoming.astype(jnp.float32) + slot_rms * (norm_grad - slot_normed * inner)).astype(
            jnp.bfloat16
        )

    def empty_norm(qkv_grad, incoming, slot):
        return jnp.zeros((shard_rows, model_width), jnp.bfloat16)

    def step(turn, carry):
        received, grad_store, qkv_store, incoming_store = carry
        slot_raw = turn - (sections - 1 - section_index)
        active = (slot_raw >= 0) & (slot_raw < micro_count)
        slot = jnp.clip(slot_raw, 0, micro_count - 1)
        incoming = jnp.where(
            section_index == sections - 1,
            lax.dynamic_index_in_dim(grad_top, slot, 0, False),
            received,
        )
        query_grad, owner_sum, far_part = lax.cond(
            active, attention_part, empty_attention, incoming, slot
        )
        for level in range(levels):
            owner_sum = owner_sum + shifted(far_part[level], "tm", -(2**level)).astype(jnp.float32)
        qkv_grad = jnp.concatenate([query_grad, owner_sum], 1).astype(jnp.bfloat16)
        grad_in = lax.cond(active, norm_part, empty_norm, qkv_grad, incoming, slot)
        sent_down = shifted(grad_in, "section", -1)
        grad_store = jnp.where(
            active, lax.dynamic_update_index_in_dim(grad_store, grad_in, slot, 0), grad_store
        )
        qkv_store = jnp.where(
            active, lax.dynamic_update_index_in_dim(qkv_store, qkv_grad, slot, 0), qkv_store
        )
        incoming_store = jnp.where(
            active,
            lax.dynamic_update_index_in_dim(incoming_store, incoming, slot, 0),
            incoming_store,
        )
        return (sent_down, grad_store, qkv_store, incoming_store)

    initial = (
        jnp.zeros((shard_rows, model_width), jnp.bfloat16),
        jnp.zeros((micro_count, shard_rows, model_width), jnp.bfloat16),
        jnp.zeros((micro_count, shard_rows, 3 * model_width), jnp.bfloat16),
        jnp.zeros((micro_count, shard_rows, model_width), jnp.bfloat16),
    )
    received, grad_store, qkv_store, incoming_store = lax.fori_loop(
        0, sections + micro_count - 1, step, initial
    )
    flat_norm = rounded_norm.reshape(-1, model_width)
    flat_attended = attended.reshape(-1, model_width)
    flat_qkv = qkv_store.reshape(-1, 3 * model_width)
    flat_incoming = incoming_store.reshape(-1, model_width)
    contract = (((0,), (0,)), ((), ()))
    first = lax.dot_general(flat_norm, flat_qkv, contract, preferred_element_type=jnp.float32)
    second = lax.dot_general(
        flat_attended, flat_incoming, contract, preferred_element_type=jnp.float32
    )
    summed = lax.psum_scatter(
        jnp.concatenate([first, second], 1).astype(jnp.bfloat16),
        "tm",
        scatter_dimension=0,
        tiled=True,
    ).astype(jnp.float32)
    return (
        grad_store[None],
        summed[None, :, : 3 * model_width],
        summed[None, :, 3 * model_width :],
    )


def side_by_side(transposed, pair):
    width = 2 * HEAD_DIM
    rows = transposed[pair * width : (pair + 1) * width]
    empty = jnp.zeros((HEAD_DIM, rows.shape[1]), rows.dtype)
    return jnp.concatenate(
        [
            jnp.concatenate([rows[:HEAD_DIM], empty], 0),
            jnp.concatenate([empty, rows[HEAD_DIM:]], 0),
        ],
        1,
    )


def one_above_other(rows, masks):
    return jnp.concatenate([rows * masks[0], rows * masks[1]], 0)


def head_masks():
    lane = lax.broadcasted_iota(jnp.int32, (1, 2 * HEAD_DIM), 1)
    return [
        jnp.where(lane < HEAD_DIM, 1.0, 0.0).astype(jnp.bfloat16),
        jnp.where(lane < HEAD_DIM, 0.0, 1.0).astype(jnp.bfloat16),
    ]


def key_bias_rows(flag_rows, levels, shard_rows, keys, first_query, count):
    key_at = lax.broadcasted_iota(jnp.int32, (keys, count), 0)
    query_at = lax.broadcasted_iota(jnp.int32, (keys, count), 1) + first_query
    gap = lax.div(query_at, shard_rows) - lax.div(key_at, shard_rows)
    allowed = (gap == 0) & (key_at <= query_at)
    for level in range(levels):
        allowed = allowed | ((gap == 2**level) & (flag_rows[level : level + 1] != 0))
    return jnp.where(allowed, 0.0, negative_fill)


def softmax_pass(queries, keys, values, bias, prob_ref, at_ref):
    queries_t = queries.T
    values_t = values.T
    width = 2 * HEAD_DIM
    count = queries.shape[0]
    for pair in range(queries.shape[1] // width):
        at_pair = slice(pair * width, (pair + 1) * width)
        scores = jnp.dot(
            keys[:, at_pair], side_by_side(queries_t, pair), preferred_element_type=jnp.float32
        )
        for half in range(2):
            at_half = slice(half * count, (half + 1) * count)
            biased = scores[:, at_half] + bias
            shifted_exp = jnp.exp(biased - jnp.max(biased, axis=0, keepdims=True))
            probability = shifted_exp * (1.0 / jnp.sum(shifted_exp, axis=0, keepdims=True))
            prob_ref[pair, :, at_half] = probability.astype(jnp.bfloat16)
    for head in range(queries.shape[1] // HEAD_DIM):
        at = slice(head * HEAD_DIM, (head + 1) * HEAD_DIM)
        at_half = slice(head % 2 * count, (head % 2 + 1) * count)
        at_ref[at] = jnp.dot(
            values_t[at], prob_ref[head // 2, :, at_half], preferred_element_type=jnp.float32
        ).astype(jnp.bfloat16)


def pack_kernel(
    levels, info_ref, acts_ref, top_ref, own_ref, other_ref, own_top_ref, other_top_ref
):
    model_width = acts_ref.shape[2]
    shard_rows = own_ref.shape[0]
    micro = info_ref[4]
    lane = lax.broadcasted_iota(jnp.int32, (shard_rows, own_ref.shape[1] - model_width), 1)
    flags = jnp.zeros(lane.shape, jnp.float32)
    for level in range(levels):
        seen = jnp.where(info_ref[5 + level] != 0, 1.0, 0.0)
        flags = jnp.where(lane == level, seen, flags)
    for at, out_ref, out_top_ref in (
        (micro, own_ref, own_top_ref),
        (1 - micro, other_ref, other_top_ref),
    ):
        out_ref[:, :model_width] = acts_ref[at]
        out_ref[:, model_width:] = flags.astype(jnp.bfloat16)
        out_top_ref[...] = top_ref[at]


def turn_kernel(own, info_ref, w_ref, after_ref, out_ref):
    columns = out_ref.shape[0] // 3
    model_width = w_ref.shape[0]
    half = info_ref[0] if own else 1 - info_ref[0]
    for block in range(3):
        first = pl.multiple_of(block * model_width + half * columns, 128)
        out_ref[block * columns : (block + 1) * columns] = w_ref[:, pl.ds(first, columns)].T


def project_kernel(replicas, info_ref, *refs):
    pieces = refs[: 4 * replicas]
    w_ref, _, normed_ref, rms_ref, norm_ref, flag_ref, q_ref, k_ref, v_ref, kt_ref, packed_ref = refs[
        4 * replicas :
    ]
    shards, shard_rows = packed_ref.shape[:2]
    model_width = w_ref.shape[0]
    seq = shards * shard_rows
    columns = q_ref.shape[1]
    at_piece = 0
    for core in (info_ref[0], 1 - info_ref[0]):
        for side in (info_ref[2], 1 - info_ref[2]):
            for step in range(replicas):
                shard = side * (shards // 2) + place_of(info_ref, step, replicas) + core
                packed_ref[shard] = pieces[at_piece][...]
                at_piece += 1
    for chunk in range(2):
        for step in range(replicas):
            shard = chunk * (shards // 2) + place_of(info_ref, step, replicas) + info_ref[0]
            normed, inverse_rms = normalize(packed_ref[shard][:, :model_width])
            normed_ref[chunk, step] = normed
            rms_ref[chunk, step] = jnp.broadcast_to(inverse_rms, rms_ref.shape[2:])
    normed, _ = normalize(packed_ref[:, :, :model_width].reshape(seq, model_width))
    rounded = normed.astype(jnp.bfloat16)
    norm_ref[...] = rounded
    flag_ref[...] = packed_ref[:, :, model_width:].reshape(seq, -1).astype(jnp.float32).T
    scale_factor = HEAD_DIM ** (-0.5)
    for block, out_ref in enumerate((q_ref, k_ref, v_ref)):
        first = pl.multiple_of(block * model_width + info_ref[0] * columns, 128)
        product = jnp.dot(
            rounded, w_ref[:, pl.ds(first, columns)], preferred_element_type=jnp.float32
        ).astype(jnp.bfloat16)
        out_ref[...] = product * scale_factor if block == 0 else product
    kt_ref[...] = (k_ref[...] * scale_factor).T


def upper_forward_kernel(
    levels, shard_rows, flag_ref, q_ref, k_ref, v_ref, prob_ref, at_ref
):
    seq = q_ref.shape[0]
    count = seq // 2
    bias = key_bias_rows(flag_ref[:, count:], levels, shard_rows, seq, count, count)
    softmax_pass(q_ref[count:], k_ref[...], v_ref[...], bias, prob_ref, at_ref)


def lower_forward_kernel(
    levels,
    shard_rows,
    info_ref,
    norm_ref,
    flag_ref,
    q_ref,
    k_ref,
    v_ref,
    after_ref,
    prob_ref,
    at_ref,
    gt_ref,
):
    seq = norm_ref.shape[0]
    count = seq // 2
    bias = key_bias_rows(flag_ref[:, :count], levels, shard_rows, count, 0, count)
    softmax_pass(q_ref[:count], k_ref[:count], v_ref[:count], bias, prob_ref, at_ref)
    rows = gt_ref.shape[0] // 4
    parity, x, y = info_ref[0], info_ref[1], info_ref[2]
    half = norm_ref.shape[1] // rows // 2
    for place, block in enumerate(
        (
            half * y + 2 * x + 1 - parity,
            half * y + 2 * x + parity,
            half * y + 2 * (1 - x) + 1 - parity,
            half * (1 - y) + 2 * x + parity,
        )
    ):
        first = pl.multiple_of(block * rows, 128)
        gt_ref[place * rows : (place + 1) * rows] = norm_ref[:, pl.ds(first, rows)].T


def place_of(info_ref, step, replicas):
    return 2 * lax.rem(info_ref[1] - step + replicas, replicas)


def merge_rows(info_ref, fresh, got_refs, kept_refs, out_refs, rows_ref):
    @pl.when(fresh)
    def _():
        for core, out_ref in enumerate(out_refs):
            out_ref[...] = got_refs[core][:, :, : out_ref.shape[2]]

    @pl.when(jnp.logical_not(fresh))
    def _():
        for out_ref, kept_ref in zip(out_refs, kept_refs):
            out_ref[...] = kept_ref[...]

    place_rows(info_ref, out_refs, rows_ref)


def place_rows(info_ref, out_refs, rows_ref):
    replicas = out_refs[0].shape[0]
    for step in range(replicas):
        place = place_of(info_ref, step, replicas)
        rows_ref[place + info_ref[0]] = out_refs[0][step]
        rows_ref[place + 1 - info_ref[0]] = out_refs[1][step]


def merge_tops(info_ref, upper, piece_refs, out_refs, rows_ref):
    replicas = out_refs[0].shape[0]
    own_chunk = info_ref[2] == (1 if upper else 0)
    for core in range(2):
        refs = piece_refs[2 * replicas * core : 2 * replicas * (core + 1)]

        @pl.when(own_chunk)
        def _():
            for step in range(replicas):
                out_refs[core][step] = refs[step][...]

        @pl.when(jnp.logical_not(own_chunk))
        def _():
            for step in range(replicas):
                out_refs[core][step] = refs[replicas + step][...]

    place_rows(info_ref, out_refs, rows_ref)


def backward_kernel(upper, tops, last, fresh_section, info_ref, *refs):
    refs = list(refs)
    got = tops or 4
    got_refs = refs[:got]
    w_ref, prob_ref, q_ref, v_ref, kt_ref, at_ref = refs[got : got + 6]
    refs = refs[got + 6 :]
    if not upper:
        key_sum_ref, value_sum_ref = refs[:2]
        refs = refs[2:]
    refs = refs[1:]
    if last:
        refs = [refs[0], refs[-1], *refs[1:-1]]
    own_ref, other_ref, keep_ref = refs[:3]
    send_refs = refs[3 : 3 + len(SPLITS[upper])]
    refs = refs[3 + len(send_refs) :]
    if upper:
        key_sum_ref, value_sum_ref = refs[:2]
        refs = refs[2:]
    grads_ref, rows_ref, scores_ref = refs
    replicas, shard_rows, model_width = own_ref.shape
    count = rows_ref.shape[0] * shard_rows
    keys = prob_ref.shape[1]
    parity = info_ref[0]
    columns = q_ref.shape[1]
    width = 2 * HEAD_DIM
    if tops:
        merge_tops(info_ref, upper, got_refs, (own_ref, other_ref), rows_ref)
    else:
        fresh = info_ref[3] == fresh_section
        merge_rows(info_ref, fresh, got_refs[:-2], got_refs[-2:], (own_ref, other_ref), rows_ref)
    rows = rows_ref[...].reshape(count, model_width)
    weights = w_ref[pl.ds(pl.multiple_of(parity * columns, 128), columns), :]
    over_width = (((1,), (1,)), ((), ()))
    upstream = lax.dot_general(
        rows, weights, over_width, preferred_element_type=jnp.float32
    ).astype(jnp.bfloat16)
    upstream_t = upstream.T
    product_t = upstream_t.astype(jnp.float32) * at_ref[...].astype(jnp.float32)
    first_query = keys - count
    masks = head_masks()

    def put(block, pair, part):
        first = block * columns + pair * width
        grads_ref[:, :, first : first + width] = part.astype(jnp.bfloat16).reshape(
            -1, shard_rows, width
        )

    for pair in range(columns // width):
        at_pair = slice(pair * width, (pair + 1) * width)
        prob_grad = jnp.dot(
            v_ref[:keys, at_pair], side_by_side(upstream_t, pair), preferred_element_type=jnp.float32
        )
        for half in range(2):
            at_half = slice(half * count, (half + 1) * count)
            first = pair * width + half * HEAD_DIM
            delta = jnp.sum(product_t[first : first + HEAD_DIM], axis=0, keepdims=True)
            scores_ref[pair, :, at_half] = (
                prob_ref[pair, :, at_half].astype(jnp.float32) * (prob_grad[:, at_half] - delta)
            ).astype(jnp.bfloat16)
        value_grad = jnp.dot(
            prob_ref[pair],
            one_above_other(upstream[:, at_pair], masks),
            preferred_element_type=jnp.float32,
        )
        if upper:
            value_sum_ref[:, at_pair] = value_grad[:first_query]
            value_grad = value_grad[first_query:]
        else:
            value_grad = value_grad + value_sum_ref[:, at_pair]
        put(2, pair, value_grad)
    for pair in range(columns // width):
        at_pair = slice(pair * width, (pair + 1) * width)
        queries = q_ref[first_query : first_query + count, at_pair]
        key_grad = jnp.dot(
            scores_ref[pair], one_above_other(queries, masks), preferred_element_type=jnp.float32
        )
        if upper:
            key_sum_ref[:, at_pair] = key_grad[:first_query]
            key_grad = key_grad[first_query:]
        else:
            key_grad = key_grad + key_sum_ref[:, at_pair]
        put(1, pair, key_grad)
        query_grad = [
            jnp.dot(
                kt_ref[pair * width + half * HEAD_DIM : pair * width + (half + 1) * HEAD_DIM, :keys],
                scores_ref[pair, :, half * count : (half + 1) * count],
                preferred_element_type=jnp.float32,
            )
            for half in range(2)
        ]
        put(0, pair, jnp.concatenate(query_grad, 0).astype(jnp.bfloat16).T)
    for step in range(replicas):
        place = place_of(info_ref, step, replicas)
        keep_ref[step] = grads_ref[place + parity]
        crossing = grads_ref[place + 1 - parity]
        first = 0
        for send_ref in send_refs:
            send_ref[step] = crossing[:, first : first + send_ref.shape[2]]
            first += send_ref.shape[2]


def norm_part_kernel(info_ref, keep_ref, w_ref, after_ref, out_ref):
    part = keep_ref[...].reshape(out_ref.shape[0], -1)
    out_ref[...] = jnp.dot(part, w_ref[...], preferred_element_type=jnp.float32)


def norm_kernel(upper, info_ref, keep_ref, normed_ref, rms_ref, incoming_ref, *refs):
    w_own_ref, w_other_ref = refs[:2]
    refs = refs[2:]
    got_refs = refs[: len(SPLITS[upper])]
    out_refs = refs[len(got_refs) :]
    replicas, shard_rows, model_width = incoming_ref.shape
    rows = replicas * shard_rows
    got = [got_ref[...].reshape(rows, -1) for got_ref in got_refs]
    norm_grad = jnp.dot(
        jnp.concatenate(got, 1), w_other_ref[...], preferred_element_type=jnp.float32
    )
    if upper:
        norm_grad += keep_ref[...]
    else:
        norm_grad += jnp.dot(
            keep_ref[...].reshape(rows, -1), w_own_ref[...], preferred_element_type=jnp.float32
        )
    chunk = 1 if upper else 0
    normed = normed_ref[chunk].reshape(rows, model_width)
    inverse_rms = rms_ref[chunk].reshape(rows, -1)[:, :1]
    inner = jnp.mean(norm_grad * normed, axis=-1, keepdims=True)
    incoming = incoming_ref[...].reshape(rows, model_width).astype(jnp.float32)
    grad_in = incoming + inverse_rms * (norm_grad - normed * inner)
    grad_in = grad_in.astype(jnp.bfloat16).reshape(replicas, shard_rows, model_width)
    out_refs[-1][:, :, :model_width] = grad_in
    spare = out_refs[-1].shape[2] - model_width
    if spare:
        out_refs[-1][:, :, model_width:] = jnp.zeros((replicas, shard_rows, spare), jnp.bfloat16)


def in_terms(gt_ref, grad_refs, half, rows):
    count = grad_refs[0].shape[0] * grad_refs[0].shape[1]
    return sum(
        jnp.dot(
            gt_ref[2 * half * rows : 2 * (half + 1) * rows, chunk * count : (chunk + 1) * count],
            part_ref[...].reshape(count, -1),
            preferred_element_type=jnp.float32,
        )
        for chunk, part_ref in enumerate(grad_refs)
    )


def send_kernel(gt_ref, lower_ref, upper_ref, pass_ref, keep_ref):
    rows = pass_ref.shape[0]
    total = in_terms(gt_ref, (lower_ref, upper_ref), 1, rows)
    pass_ref[...] = total[:rows].astype(jnp.bfloat16)
    keep_ref[...] = total[rows:].astype(jnp.bfloat16)


def term_kernel(info_ref, gt_ref, *refs):
    grad_refs, at_refs, row_refs = refs[:2], refs[2:4], refs[4:6]
    pass_ref, keep_ref, out_pass_ref, out_keep_ref, out_send_ref = refs[7:]
    rows = pass_ref.shape[0]
    width = out_send_ref.shape[1]
    parity, x, y = info_ref[0], info_ref[1], info_ref[2]
    sent = jnp.where(parity == y, 2 * (1 - x) + 1 - parity, 2 * x + parity)
    blocks = (sent, 2 * x + 1 - parity, 2 * x + parity)
    total = jnp.zeros((3 * rows, width), jnp.float32)
    for at_ref, part_ref in zip(at_refs, row_refs):
        picked = [at_ref[pl.ds(pl.multiple_of(block * rows, 128), rows)] for block in blocks]
        total += jnp.dot(
            jnp.concatenate(picked, 0),
            part_ref[...].reshape(-1, width),
            preferred_element_type=jnp.float32,
        )
    out_send_ref[...] = total[:rows].astype(jnp.bfloat16)
    out_pass_ref[...] = total[rows : 2 * rows]
    out_keep_ref[...] = total[2 * rows :]
    total = in_terms(gt_ref, grad_refs, 0, rows)
    pass_ref[...] = total[:rows]
    keep_ref[...] = total[rows:]


def sum_kernel(own_ref, got_ref, out_own_ref, out_got_ref, after_ref, sum_ref):
    columns = own_ref.shape[1]
    sum_ref[:, :columns] = (own_ref[...] + got_ref[...].astype(jnp.float32)).astype(jnp.bfloat16)
    sum_ref[:, columns:] = (out_own_ref[...] + out_got_ref[...].astype(jnp.float32)).astype(
        jnp.bfloat16
    )


def pick_kernel(info_ref, upper_ref, lower_ref, out_ref):
    crossing = info_ref[0] == 0
    for step in range(2):
        for chunk, part_ref in enumerate((lower_ref, upper_ref)):
            wanted = info_ref[2] == (chunk if step == 1 else 1 - chunk)

            @pl.when(wanted & (crossing if step == 1 else jnp.logical_not(crossing)))
            def _():
                out_ref[...] = part_ref[step]


def join_kernel(info_ref, upper_ref, lower_ref, got_ref, out_ref):
    micro = info_ref[4]
    out_ref[0, 1 - micro] = got_ref[...]

    @pl.when(info_ref[2] == 1)
    def _():
        out_ref[0, micro] = upper_ref[0]

    @pl.when(info_ref[2] != 1)
    def _():
        out_ref[0, micro] = lower_ref[0]


def place_kernel(
    info_ref, own_ref, got_ref, out_own_ref, out_got_ref, sibling_ref, d_in_ref, d_out_ref
):
    columns = own_ref.shape[1] // 3
    own = own_ref[...] + got_ref[...].astype(jnp.float32)
    sibling = sibling_ref[:, : 3 * columns].astype(jnp.float32)
    for part, half in ((own, info_ref[0]), (sibling, 1 - info_ref[0])):
        for block in range(3):
            first = pl.multiple_of((2 * block + half) * columns, 128)
            d_in_ref[:, pl.ds(first, columns)] = part[:, block * columns : (block + 1) * columns]
    owner = info_ref[0] == info_ref[2]

    @pl.when(owner)
    def _():
        d_out_ref[...] = out_own_ref[...] + out_got_ref[...].astype(jnp.float32)

    @pl.when(jnp.logical_not(owner))
    def _():
        d_out_ref[...] = sibling_ref[:, 3 * columns :].astype(jnp.float32)


def call(kernel, outs, operands, scratch=(), flops=0, scalars=1, after=None, mebibytes=5, far=0):
    in_specs = [pl.BlockSpec(memory_space=pltpu.SMEM)] * scalars
    in_specs += [pl.BlockSpec(memory_space=pltpu.HBM)] * far
    in_specs += [pl.BlockSpec(memory_space=pltpu.VMEM)] * (len(operands) - scalars - far)
    if after is not None:
        operands = [*operands, after]
        in_specs.append(pl.BlockSpec(memory_space=pl.ANY))
    return pl.pallas_call(
        kernel,
        out_shape=list(outs),
        in_specs=in_specs,
        out_specs=[pl.BlockSpec(memory_space=pltpu.VMEM)] * len(outs),
        scratch_shapes=list(scratch),
        cost_estimate=pl.CostEstimate(flops=1, bytes_accessed=1, transcendentals=0),
        compiler_params=pltpu.CompilerParams(vmem_limit_bytes=mebibytes * 2**20),
    )(*operands)


def by_chips(acts, grad_top, w_in, w_out, offsets):
    half_type, full_type = jnp.bfloat16, jnp.float32
    shape = jax.ShapeDtypeStruct
    sections = lax.axis_size("section")
    shards = lax.axis_size("tm")
    levels = offsets.shape[1]
    half = shards // 2
    replicas = half // 2
    me = lax.axis_index("tm")
    parity = lax.rem(me, 2)
    side = lax.div(me, half)
    micro_count, shard_rows, model_width = acts.shape[1:]
    columns = model_width // 2
    heads = columns // HEAD_DIM
    seq = shards * shard_rows
    count = seq // 2
    w_qkv = w_in[0]
    w_rows = w_out[0]
    beside = lax.div(lax.rem(me, half), 2)
    micro = lax.rem(side + beside, 2)
    info = jnp.stack([parity, beside, side, lax.axis_index("section"), micro])
    info = jnp.concatenate([info.astype(jnp.int32), offsets[0]])

    def swapped(value, bits, chosen=None):
        pairs = [(device, device ^ bits) for device in range(shards)]
        pairs = [pair for pair in pairs if chosen is None or chosen(pair[0])]
        return lax.ppermute(value, "tm", pairs)

    core, near, far = 1, 2, half

    packed = shape((shard_rows, model_width + 128), half_type)
    top_shape = shape((shard_rows, model_width), half_type)
    own_acts, other_acts, own_top, other_top = call(
        functools.partial(pack_kernel, levels),
        [packed, packed, top_shape, top_shape],
        [info, acts[0], grad_top],
    )
    weights = [
        call(
            functools.partial(turn_kernel, own),
            [shape((3 * columns, model_width), half_type)],
            [info, w_qkv],
            after=own_acts,
        )[0]
        for own in (True, False)
    ]
    pieces = [own_acts, swapped(other_acts, near), swapped(other_acts, far)]
    pieces += [swapped(own_acts, near + far)]
    tops = [own_top, swapped(other_top, near), swapped(other_top, far)]
    pieces[-1], tops, weights = lax.optimization_barrier((pieces[-1], tops, weights))
    tops += [swapped(own_top, near + far)]
    pieces += [swapped(piece, core) for piece in pieces]

    rows_shape = shape((seq, columns), half_type)
    normed, rms, norm, flag_rows, queries, keys, values, keys_t = call(
        functools.partial(project_kernel, replicas),
        [
            shape((2, replicas, shard_rows, model_width), full_type),
            shape((2, replicas, shard_rows, 128), full_type),
            shape((seq, model_width), half_type),
            shape((128, seq), full_type),
            rows_shape,
            rows_shape,
            rows_shape,
            shape((columns, seq), half_type),
        ],
        [info, *pieces, w_qkv],
        scratch=[pltpu.VMEM((shards, *packed.shape), half_type)],
        flops=6 * seq * model_width * columns,
        after=weights[1],
    )
    pairs = heads // 2
    upper_prob, upper_at = call(
        functools.partial(upper_forward_kernel, levels, shard_rows),
        [
            shape((pairs, seq, 2 * count), half_type),
            shape((columns, count), half_type),
        ],
        [flag_rows, queries, keys, values],
        scalars=0,
        flops=4 * columns * seq * count,
    )
    tops, upper_at = lax.optimization_barrier((tuple(tops), upper_at))
    tops = [*tops, *[swapped(piece, core) for piece in tops]]
    own_rows = model_width // shards
    probs, attended = {True: upper_prob}, {True: upper_at}
    got, kept = {}, {}
    piece_shape = shape((replicas, shard_rows, model_width), half_type)
    wide_shape = shape((replicas, shard_rows, model_width + 128), half_type)
    grads_shape = shape((replicas, shard_rows, 3 * columns), half_type)
    sum_shape = shape((count, columns), full_type)
    full_grads = shape((half, shard_rows, 3 * columns), half_type)
    full_rows = shape((half, shard_rows, model_width), half_type)
    term_shape = (own_rows, 3 * columns)
    rows_scratch = pltpu.VMEM(full_rows.shape, half_type)
    grads_scratch = pltpu.VMEM(full_grads.shape, half_type)
    result, full, ordered = {}, {}, {}
    for turn in range(sections):
        last = turn + 1 == sections
        fresh_section = sections - 1 - turn
        sums, parts, crossed = [], {}, {}

        def norm_step(upper, after):
            (result[upper],) = call(
                functools.partial(norm_kernel, upper),
                [piece_shape if upper or last else wide_shape],
                [info, parts[upper], normed, rms, kept[upper][0], *weights, *crossed[upper]],
                after=after,
            )
            if not last:
                hop = [(sections - 1 - turn, sections - 2 - turn)]
                got[upper] = lax.ppermute(result[upper], "section", hop)

        for upper in (True, False):
            rows_in, after = tops, keys_t if upper else result.get(True)
            if turn:
                tied = result if last else parts
                before = result[False] if upper else tied[True]
                got[upper], after = lax.optimization_barrier((got[upper], before))
                if not upper:
                    tied[True] = after
                rows_in = [got[upper], swapped(got[upper], core), *kept[upper]]
            unit = 3 * columns // sum(SPLITS[upper])
            cross = [shape((replicas, shard_rows, part * unit), half_type) for part in SPLITS[upper]]
            outs = [piece_shape] * (1 if last else 2) + [grads_shape, *cross]
            outs += [sum_shape, sum_shape] if upper else []
            scratch = []
            if last:
                outs += [full_grads]
            else:
                scratch += [grads_scratch]
            if last:
                outs += [full_rows]
            else:
                scratch += [rows_scratch]
            part_keys = seq if upper else count
            scratch += [pltpu.VMEM((pairs, part_keys, 2 * count), half_type)]
            if last:
                scratch += [pltpu.VMEM(piece_shape.shape, half_type)]
            answer = call(
                functools.partial(
                    backward_kernel, upper, 0 if turn else len(tops), last, fresh_section
                ),
                outs,
                [info, *rows_in, w_rows, probs[upper], queries, values, keys_t]
                + [attended[upper], *sums],
                scratch=scratch,
                flops=2 * count * columns * (2 * model_width + 4 * part_keys),
                after=after,
            )
            kept[upper] = tuple(answer[:2])
            answer = answer[1 if last else 2 :]
            keep = answer[0]
            send = answer[1 : 1 + len(cross)]
            parts[upper] = keep
            if upper:
                sums = answer[1 + len(cross) : 3 + len(cross)]
                (parts[True],) = call(
                    norm_part_kernel,
                    [shape((replicas * shard_rows, model_width), full_type)],
                    [info, keep, weights[0]],
                    flops=3 * replicas * shard_rows * model_width * model_width,
                    after=keep,
                )
                if turn == 0:
                    lower_prob, lower_at, norm_t = call(
                        functools.partial(lower_forward_kernel, levels, shard_rows),
                        [
                            shape((pairs, count, 2 * count), half_type),
                            shape((columns, count), half_type),
                            shape((4 * own_rows, seq), half_type),
                        ],
                        [info, norm, flag_rows, queries, keys, values],
                        flops=4 * columns * count * count,
                        after=parts[True],
                    )
                    probs[False], attended[False] = lower_prob, lower_at
            if last:
                full[upper], ordered[upper] = answer[-2:]
            crossed[upper] = [swapped(piece, core) for piece in send]
            if upper:
                norm_step(True, keep)
        if last:
            send_pass, send_keep = call(
                send_kernel,
                [shape(term_shape, half_type)] * 2,
                [norm_t, full[False], full[True]],
                scalars=0,
            )
            terms = call(
                term_kernel,
                [shape(term_shape, full_type)] * 2
                + [shape((own_rows, model_width), full_type)] * 2
                + [shape((own_rows, model_width), half_type)],
                [info, norm_t, full[False], full[True], attended[False], attended[True]]
                + [ordered[False], ordered[True]],
                after=send_keep,
            )
        norm_step(False, terms[4] if last else result[True])

    in_pass, in_keep, out_pass, out_keep, out_send = terms
    got_pass = swapped(send_pass, near)
    got_keep = swapped(send_keep, far)
    own_rows_grad = [result[True], result[False]]
    (theirs,) = call(pick_kernel, [top_shape], [info, *own_rows_grad])
    to_owner = [(device, device ^ (far if device % 2 else near)) for device in range(shards)]
    partner = lax.ppermute(theirs, "tm", to_owner)
    got_out_pass = swapped(out_send, near, lambda device: device // half == device % 2)
    got_out_keep = swapped(out_send, far, lambda device: device // half != device % 2)
    _, _, done = lax.optimization_barrier((got_keep, got_out_keep, partner))
    (summed,) = call(
        sum_kernel,
        [shape((own_rows, 3 * columns + model_width), half_type)],
        [in_pass, got_pass, out_pass, got_out_pass],
        scalars=0,
        after=done,
    )
    d_w_in, d_w_out = call(
        place_kernel,
        [
            shape((own_rows, 3 * model_width), full_type),
            shape((own_rows, model_width), full_type),
        ],
        [info, in_keep, got_keep, out_keep, got_out_keep, swapped(summed, core)],
    )
    (d_acts,) = call(
        join_kernel, [shape(acts.shape, half_type)], [info, *own_rows_grad, partner]
    )
    return (d_acts, d_w_in[None], d_w_out[None])


def layer_gradients(acts, grad_top, w_in, w_out, offsets):
    shards = lax.axis_size("tm")
    micro_count, shard_rows, model_width = acts.shape[1:]
    heads = model_width // HEAD_DIM
    prob_bytes = 2 * heads * (shards * shard_rows) ** 2
    fits = prob_bytes <= 2**24 and model_width % (128 * shards) == 0 and shard_rows % 16 == 0
    square = shards % 4 == 0 and shards // 4 == 2
    if micro_count == 2 and square and heads % 4 == 0 and fits:
        return by_chips(acts, grad_top, w_in, w_out, offsets)
    return per_device(acts, grad_top, w_in, w_out, offsets)


def solution(mesh):
    placed = (
        P("section", None, "tm", None),
        P(None, "tm", None),
        P("section", None, None),
        P("section", None, None),
        P("tm", None),
    )
    return jax.shard_map(
        layer_gradients,
        mesh=mesh,
        in_specs=placed,
        out_specs=(
            P("section", None, "tm", None),
            P("section", "tm", None),
            P("section", "tm", None),
        ),
        check_vma=False,
    )
```

```python
import functools
import jax
import jax.numpy as jnp
from jax import lax
from jax.experimental import pallas as pl
from jax.experimental.pallas import tpu as pltpu
from jax.sharding import PartitionSpec as P

HEAD_DIM = 64


epsilon = 1e-06
PIECES = {True: 2, False: 2}
negative_fill = -1e30


def shifted(value, axis, steps):
    count = lax.axis_size(axis)
    initial, last = (max(0, -steps), min(count, count - steps))
    return lax.ppermute(value, axis, [(source, source + steps) for source in range(initial, last)])


def normalize(inputs):
    values = inputs.astype(jnp.float32)
    inverse_rms = lax.rsqrt(jnp.mean(values * values, axis=-1, keepdims=True) + epsilon)
    return (values * inverse_rms, inverse_rms)


def key_bias(level_flags, shard_rows):
    position = jnp.arange(shard_rows)
    own_part = position[None, :] <= position[:, None]
    far_part = jnp.repeat(level_flags != 0, shard_rows)
    far_part = jnp.broadcast_to(far_part[None, :], (shard_rows, far_part.shape[0]))
    return jnp.concatenate([own_part, far_part], 1)


def split_heads(row_block):
    return row_block.reshape(row_block.shape[0], -1, HEAD_DIM)


def softmax_keys(queries, key_heads, allowed):
    scores = jnp.einsum(
        "ihd,jhd->hij", queries, key_heads, preferred_element_type=jnp.float32
    ) * HEAD_DIM ** (-0.5)
    scores = jnp.where(allowed[None], scores, negative_fill)
    highest = jnp.max(scores, axis=-1, keepdims=True)
    shifted_exp = jnp.where(allowed[None], jnp.exp(scores - highest), 0.0)
    return shifted_exp / jnp.sum(shifted_exp, axis=-1, keepdims=True)


def attend(query_rows, key_rows, allowed):
    model_width = query_rows.shape[1]
    probability = softmax_keys(
        split_heads(query_rows), split_heads(key_rows[:, :model_width]), allowed
    )
    attended = jnp.einsum(
        "hij,jhd->ihd",
        probability.astype(jnp.bfloat16),
        split_heads(key_rows[:, model_width:]),
        preferred_element_type=jnp.float32,
    )
    return attended.reshape(query_rows.shape).astype(jnp.bfloat16)


def attend_back(query_rows, key_rows, allowed, incoming, attended, w_proj):
    model_width = query_rows.shape[1]
    queries = split_heads(query_rows)
    key_heads = split_heads(key_rows[:, :model_width])
    value_heads = split_heads(key_rows[:, model_width:])
    probability = softmax_keys(queries, key_heads, allowed)
    rounded = probability.astype(jnp.bfloat16)
    upstream = lax.dot_general(
        incoming, w_proj, (((1,), (1,)), ((), ())), preferred_element_type=jnp.float32
    ).astype(jnp.bfloat16)
    up_heads = split_heads(upstream)
    delta = jnp.einsum(
        "ihd,ihd->hi", up_heads.astype(jnp.float32), split_heads(attended).astype(jnp.float32)
    )[..., None]
    prob_grad = jnp.einsum(
        "ihd,jhd->hij", up_heads, value_heads, preferred_element_type=jnp.float32
    )
    score_grad = (probability * (prob_grad - delta)).astype(jnp.bfloat16)
    scale_factor = HEAD_DIM ** (-0.5)
    query_grad = (
        jnp.einsum("hij,jhd->ihd", score_grad, key_heads, preferred_element_type=jnp.float32)
        * scale_factor
    )
    key_grad = (
        jnp.einsum("hij,ihd->jhd", score_grad, queries, preferred_element_type=jnp.float32)
        * scale_factor
    )
    value_grad = jnp.einsum("hij,ihd->jhd", rounded, up_heads, preferred_element_type=jnp.float32)
    return (
        query_grad.reshape(-1, model_width),
        key_grad.reshape(-1, model_width),
        value_grad.reshape(-1, model_width),
    )


def per_device(acts, grad_top, w_in, w_out, offsets):
    sections = lax.axis_size("section")
    shards = lax.axis_size("tm")
    levels = shards.bit_length() - 1
    section_index = lax.axis_index("section")
    micro_count = acts.shape[1]
    shard_rows = acts.shape[2]
    model_width = acts.shape[3]
    w_qkv = w_in[0]
    w_proj = w_out[0]
    level_flags = offsets[0]
    normed, inverse_rms = normalize(acts[0])
    rounded_norm = normed.astype(jnp.bfloat16)
    qkv = jnp.dot(rounded_norm.reshape(-1, model_width), w_qkv, preferred_element_type=jnp.float32)
    qkv = qkv.astype(jnp.bfloat16).reshape(micro_count, shard_rows, 3 * model_width)
    pairs = qkv[..., model_width:]
    far_list = [shifted(pairs, "tm", 2**level) for level in range(levels)]
    key_rows = jnp.concatenate([pairs] + far_list, 1)
    allowed = key_bias(level_flags, shard_rows)
    attended = jnp.stack(
        [
            attend(qkv[index, :, :model_width], key_rows[index], allowed)
            for index in range(micro_count)
        ],
        0,
    )

    def attention_part(incoming, slot):
        query_rows = lax.dynamic_index_in_dim(qkv, slot, 0, False)[:, :model_width]
        slot_keys = lax.dynamic_index_in_dim(key_rows, slot, 0, False)
        slot_attended = lax.dynamic_index_in_dim(attended, slot, 0, False)
        query_grad, key_grad, value_grad = attend_back(
            query_rows, slot_keys, allowed, incoming, slot_attended, w_proj
        )
        owner_sum = jnp.concatenate([key_grad[:shard_rows], value_grad[:shard_rows]], 1)
        far_part = jnp.concatenate([key_grad[shard_rows:], value_grad[shard_rows:]], 1)
        far_part = far_part.astype(jnp.bfloat16).reshape(levels, shard_rows, 2 * model_width)
        return (query_grad, owner_sum, far_part)

    def empty_attention(incoming, slot):
        return (
            jnp.zeros((shard_rows, model_width), jnp.float32),
            jnp.zeros((shard_rows, 2 * model_width), jnp.float32),
            jnp.zeros((levels, shard_rows, 2 * model_width), jnp.bfloat16),
        )

    def norm_part(qkv_grad, incoming, slot):
        norm_grad = lax.dot_general(
            qkv_grad, w_qkv, (((1,), (1,)), ((), ())), preferred_element_type=jnp.float32
        )
        slot_normed = lax.dynamic_index_in_dim(normed, slot, 0, False)
        slot_rms = lax.dynamic_index_in_dim(inverse_rms, slot, 0, False)
        inner = jnp.mean(norm_grad * slot_normed, axis=-1, keepdims=True)
        return (incoming.astype(jnp.float32) + slot_rms * (norm_grad - slot_normed * inner)).astype(
            jnp.bfloat16
        )

    def empty_norm(qkv_grad, incoming, slot):
        return jnp.zeros((shard_rows, model_width), jnp.bfloat16)

    def step(turn, carry):
        received, grad_store, qkv_store, incoming_store = carry
        slot_raw = turn - (sections - 1 - section_index)
        active = (slot_raw >= 0) & (slot_raw < micro_count)
        slot = jnp.clip(slot_raw, 0, micro_count - 1)
        incoming = jnp.where(
            section_index == sections - 1,
            lax.dynamic_index_in_dim(grad_top, slot, 0, False),
            received,
        )
        query_grad, owner_sum, far_part = lax.cond(
            active, attention_part, empty_attention, incoming, slot
        )
        for level in range(levels):
            owner_sum = owner_sum + shifted(far_part[level], "tm", -(2**level)).astype(jnp.float32)
        qkv_grad = jnp.concatenate([query_grad, owner_sum], 1).astype(jnp.bfloat16)
        grad_in = lax.cond(active, norm_part, empty_norm, qkv_grad, incoming, slot)
        sent_down = shifted(grad_in, "section", -1)
        grad_store = jnp.where(
            active, lax.dynamic_update_index_in_dim(grad_store, grad_in, slot, 0), grad_store
        )
        qkv_store = jnp.where(
            active, lax.dynamic_update_index_in_dim(qkv_store, qkv_grad, slot, 0), qkv_store
        )
        incoming_store = jnp.where(
            active,
            lax.dynamic_update_index_in_dim(incoming_store, incoming, slot, 0),
            incoming_store,
        )
        return (sent_down, grad_store, qkv_store, incoming_store)

    initial = (
        jnp.zeros((shard_rows, model_width), jnp.bfloat16),
        jnp.zeros((micro_count, shard_rows, model_width), jnp.bfloat16),
        jnp.zeros((micro_count, shard_rows, 3 * model_width), jnp.bfloat16),
        jnp.zeros((micro_count, shard_rows, model_width), jnp.bfloat16),
    )
    received, grad_store, qkv_store, incoming_store = lax.fori_loop(
        0, sections + micro_count - 1, step, initial
    )
    flat_norm = rounded_norm.reshape(-1, model_width)
    flat_attended = attended.reshape(-1, model_width)
    flat_qkv = qkv_store.reshape(-1, 3 * model_width)
    flat_incoming = incoming_store.reshape(-1, model_width)
    contract = (((0,), (0,)), ((), ()))
    first = lax.dot_general(flat_norm, flat_qkv, contract, preferred_element_type=jnp.float32)
    second = lax.dot_general(
        flat_attended, flat_incoming, contract, preferred_element_type=jnp.float32
    )
    summed = lax.psum_scatter(
        jnp.concatenate([first, second], 1).astype(jnp.bfloat16),
        "tm",
        scatter_dimension=0,
        tiled=True,
    ).astype(jnp.float32)
    return (
        grad_store[None],
        summed[None, :, : 3 * model_width],
        summed[None, :, 3 * model_width :],
    )


def side_by_side(transposed, pair):
    width = 2 * HEAD_DIM
    rows = transposed[pair * width : (pair + 1) * width]
    empty = jnp.zeros((HEAD_DIM, rows.shape[1]), rows.dtype)
    return jnp.concatenate(
        [
            jnp.concatenate([rows[:HEAD_DIM], empty], 0),
            jnp.concatenate([empty, rows[HEAD_DIM:]], 0),
        ],
        1,
    )


def one_above_other(rows, masks):
    return jnp.concatenate([rows * masks[0], rows * masks[1]], 0)


def head_masks():
    lane = lax.broadcasted_iota(jnp.int32, (1, 2 * HEAD_DIM), 1)
    return [
        jnp.where(lane < HEAD_DIM, 1.0, 0.0).astype(jnp.bfloat16),
        jnp.where(lane < HEAD_DIM, 0.0, 1.0).astype(jnp.bfloat16),
    ]


def key_bias_rows(flag_rows, levels, shard_rows, keys, first_query, count):
    key_at = lax.broadcasted_iota(jnp.int32, (keys, count), 0)
    query_at = lax.broadcasted_iota(jnp.int32, (keys, count), 1) + first_query
    gap = lax.div(query_at, shard_rows) - lax.div(key_at, shard_rows)
    allowed = (gap == 0) & (key_at <= query_at)
    for level in range(levels):
        allowed = allowed | ((gap == 2**level) & (flag_rows[level : level + 1] != 0))
    return jnp.where(allowed, 0.0, negative_fill)


def softmax_pass(queries, keys, values, bias, prob_ref, at_ref):
    queries_t = queries.T
    values_t = values.T
    width = 2 * HEAD_DIM
    count = queries.shape[0]
    for pair in range(queries.shape[1] // width):
        at_pair = slice(pair * width, (pair + 1) * width)
        scores = jnp.dot(
            keys[:, at_pair], side_by_side(queries_t, pair), preferred_element_type=jnp.float32
        )
        for half in range(2):
            at_half = slice(half * count, (half + 1) * count)
            biased = scores[:, at_half] + bias
            shifted_exp = jnp.exp(biased - jnp.max(biased, axis=0, keepdims=True))
            probability = shifted_exp * (1.0 / jnp.sum(shifted_exp, axis=0, keepdims=True))
            prob_ref[pair, :, at_half] = probability.astype(jnp.bfloat16)
    for head in range(queries.shape[1] // HEAD_DIM):
        at = slice(head * HEAD_DIM, (head + 1) * HEAD_DIM)
        at_half = slice(head % 2 * count, (head % 2 + 1) * count)
        at_ref[at] = jnp.dot(
            values_t[at], prob_ref[head // 2, :, at_half], preferred_element_type=jnp.float32
        ).astype(jnp.bfloat16)


def pack_kernel(
    levels, info_ref, acts_ref, top_ref, own_ref, other_ref, own_top_ref, other_top_ref
):
    model_width = acts_ref.shape[2]
    shard_rows = own_ref.shape[0]
    micro = info_ref[4]
    lane = lax.broadcasted_iota(jnp.int32, (shard_rows, own_ref.shape[1] - model_width), 1)
    flags = jnp.zeros(lane.shape, jnp.float32)
    for level in range(levels):
        seen = jnp.where(info_ref[5 + level] != 0, 1.0, 0.0)
        flags = jnp.where(lane == level, seen, flags)
    for at, out_ref, out_top_ref in (
        (micro, own_ref, own_top_ref),
        (1 - micro, other_ref, other_top_ref),
    ):
        out_ref[:, :model_width] = acts_ref[at]
        out_ref[:, model_width:] = flags.astype(jnp.bfloat16)
        out_top_ref[...] = top_ref[at]


def turn_kernel(own, info_ref, w_ref, after_ref, out_ref):
    columns = out_ref.shape[0] // 3
    model_width = w_ref.shape[0]
    half = info_ref[0] if own else 1 - info_ref[0]
    for block in range(3):
        first = pl.multiple_of(block * model_width + half * columns, 128)
        out_ref[block * columns : (block + 1) * columns] = w_ref[:, pl.ds(first, columns)].T


def project_kernel(replicas, info_ref, *refs):
    pieces = refs[: 4 * replicas]
    w_ref, _, normed_ref, rms_ref, norm_ref, flag_ref, q_ref, k_ref, v_ref, kt_ref, packed_ref = refs[
        4 * replicas :
    ]
    shards, shard_rows = packed_ref.shape[:2]
    model_width = w_ref.shape[0]
    seq = shards * shard_rows
    columns = q_ref.shape[1]
    at_piece = 0
    for core in (info_ref[0], 1 - info_ref[0]):
        for side in (info_ref[2], 1 - info_ref[2]):
            for step in range(replicas):
                shard = side * (shards // 2) + place_of(info_ref, step, replicas) + core
                packed_ref[shard] = pieces[at_piece][...]
                at_piece += 1
    for chunk in range(2):
        for step in range(replicas):
            shard = chunk * (shards // 2) + place_of(info_ref, step, replicas) + info_ref[0]
            normed, inverse_rms = normalize(packed_ref[shard][:, :model_width])
            normed_ref[chunk, step] = normed
            rms_ref[chunk, step] = jnp.broadcast_to(inverse_rms, rms_ref.shape[2:])
    normed, _ = normalize(packed_ref[:, :, :model_width].reshape(seq, model_width))
    rounded = normed.astype(jnp.bfloat16)
    norm_ref[...] = rounded
    flag_ref[...] = packed_ref[:, :, model_width:].reshape(seq, -1).astype(jnp.float32).T
    scale_factor = HEAD_DIM ** (-0.5)
    for block, out_ref in enumerate((q_ref, k_ref, v_ref)):
        first = pl.multiple_of(block * model_width + info_ref[0] * columns, 128)
        product = jnp.dot(
            rounded, w_ref[:, pl.ds(first, columns)], preferred_element_type=jnp.float32
        ).astype(jnp.bfloat16)
        out_ref[...] = product * scale_factor if block == 0 else product
    kt_ref[...] = (k_ref[...] * scale_factor).T


def upper_forward_kernel(
    levels, shard_rows, flag_ref, q_ref, k_ref, v_ref, prob_ref, at_ref
):
    seq = q_ref.shape[0]
    count = seq // 2
    bias = key_bias_rows(flag_ref[:, count:], levels, shard_rows, seq, count, count)
    softmax_pass(q_ref[count:], k_ref[...], v_ref[...], bias, prob_ref, at_ref)


def lower_forward_kernel(
    levels,
    shard_rows,
    info_ref,
    norm_ref,
    flag_ref,
    q_ref,
    k_ref,
    v_ref,
    after_ref,
    prob_ref,
    at_ref,
    gt_ref,
):
    seq = norm_ref.shape[0]
    count = seq // 2
    bias = key_bias_rows(flag_ref[:, :count], levels, shard_rows, count, 0, count)
    softmax_pass(q_ref[:count], k_ref[:count], v_ref[:count], bias, prob_ref, at_ref)
    rows = gt_ref.shape[0] // 4
    parity, x, y = info_ref[0], info_ref[1], info_ref[2]
    half = norm_ref.shape[1] // rows // 2
    for place, block in enumerate(
        (
            half * y + 2 * x + 1 - parity,
            half * y + 2 * x + parity,
            half * y + 2 * (1 - x) + 1 - parity,
            half * (1 - y) + 2 * x + parity,
        )
    ):
        first = pl.multiple_of(block * rows, 128)
        gt_ref[place * rows : (place + 1) * rows] = norm_ref[:, pl.ds(first, rows)].T


def place_of(info_ref, step, replicas):
    return 2 * lax.rem(info_ref[1] - step + replicas, replicas)


def merge_rows(info_ref, fresh, got_refs, kept_refs, out_refs, rows_ref):
    @pl.when(fresh)
    def _():
        for core, out_ref in enumerate(out_refs):
            out_ref[...] = got_refs[core][:, :, : out_ref.shape[2]]

    @pl.when(jnp.logical_not(fresh))
    def _():
        for out_ref, kept_ref in zip(out_refs, kept_refs):
            out_ref[...] = kept_ref[...]

    place_rows(info_ref, out_refs, rows_ref)


def place_rows(info_ref, out_refs, rows_ref):
    replicas = out_refs[0].shape[0]
    for step in range(replicas):
        place = place_of(info_ref, step, replicas)
        rows_ref[place + info_ref[0]] = out_refs[0][step]
        rows_ref[place + 1 - info_ref[0]] = out_refs[1][step]


def merge_tops(info_ref, upper, piece_refs, out_refs, rows_ref):
    replicas = out_refs[0].shape[0]
    own_chunk = info_ref[2] == (1 if upper else 0)
    for core in range(2):
        refs = piece_refs[2 * replicas * core : 2 * replicas * (core + 1)]

        @pl.when(own_chunk)
        def _():
            for step in range(replicas):
                out_refs[core][step] = refs[step][...]

        @pl.when(jnp.logical_not(own_chunk))
        def _():
            for step in range(replicas):
                out_refs[core][step] = refs[replicas + step][...]

    place_rows(info_ref, out_refs, rows_ref)


def backward_kernel(upper, tops, last, fresh_section, info_ref, *refs):
    refs = list(refs)
    got = tops or 4
    got_refs = refs[:got]
    w_ref, prob_ref, q_ref, v_ref, kt_ref, at_ref = refs[got : got + 6]
    refs = refs[got + 6 :]
    if not upper:
        key_sum_ref, value_sum_ref = refs[:2]
        refs = refs[2:]
    refs = refs[1:]
    if last:
        refs = [refs[0], refs[-1], *refs[1:-1]]
    own_ref, other_ref, keep_ref = refs[:3]
    send_refs = refs[3 : 3 + PIECES[upper]]
    refs = refs[3 + len(send_refs) :]
    if upper:
        key_sum_ref, value_sum_ref = refs[:2]
        refs = refs[2:]
    grads_ref, rows_ref, scores_ref = refs
    replicas, shard_rows, model_width = own_ref.shape
    count = rows_ref.shape[0] * shard_rows
    keys = prob_ref.shape[1]
    parity = info_ref[0]
    columns = q_ref.shape[1]
    width = 2 * HEAD_DIM
    if tops:
        merge_tops(info_ref, upper, got_refs, (own_ref, other_ref), rows_ref)
    else:
        fresh = info_ref[3] == fresh_section
        merge_rows(info_ref, fresh, got_refs[:-2], got_refs[-2:], (own_ref, other_ref), rows_ref)
    rows = rows_ref[...].reshape(count, model_width)
    weights = w_ref[pl.ds(pl.multiple_of(parity * columns, 128), columns), :]
    over_width = (((1,), (1,)), ((), ()))
    upstream = lax.dot_general(
        rows, weights, over_width, preferred_element_type=jnp.float32
    ).astype(jnp.bfloat16)
    upstream_t = upstream.T
    product_t = upstream_t.astype(jnp.float32) * at_ref[...].astype(jnp.float32)
    first_query = keys - count
    masks = head_masks()

    def put(block, pair, part):
        first = block * columns + pair * width
        grads_ref[:, :, first : first + width] = part.astype(jnp.bfloat16).reshape(
            -1, shard_rows, width
        )

    for pair in range(columns // width):
        at_pair = slice(pair * width, (pair + 1) * width)
        prob_grad = jnp.dot(
            v_ref[:keys, at_pair], side_by_side(upstream_t, pair), preferred_element_type=jnp.float32
        )
        for half in range(2):
            at_half = slice(half * count, (half + 1) * count)
            first = pair * width + half * HEAD_DIM
            delta = jnp.sum(product_t[first : first + HEAD_DIM], axis=0, keepdims=True)
            scores_ref[pair, :, at_half] = (
                prob_ref[pair, :, at_half].astype(jnp.float32) * (prob_grad[:, at_half] - delta)
            ).astype(jnp.bfloat16)
        value_grad = jnp.dot(
            prob_ref[pair],
            one_above_other(upstream[:, at_pair], masks),
            preferred_element_type=jnp.float32,
        )
        if upper:
            value_sum_ref[:, at_pair] = value_grad[:first_query]
            value_grad = value_grad[first_query:]
        else:
            value_grad = value_grad + value_sum_ref[:, at_pair]
        put(2, pair, value_grad)
    for pair in range(columns // width):
        at_pair = slice(pair * width, (pair + 1) * width)
        queries = q_ref[first_query : first_query + count, at_pair]
        key_grad = jnp.dot(
            scores_ref[pair], one_above_other(queries, masks), preferred_element_type=jnp.float32
        )
        if upper:
            key_sum_ref[:, at_pair] = key_grad[:first_query]
            key_grad = key_grad[first_query:]
        else:
            key_grad = key_grad + key_sum_ref[:, at_pair]
        put(1, pair, key_grad)
        query_grad = [
            jnp.dot(
                kt_ref[pair * width + half * HEAD_DIM : pair * width + (half + 1) * HEAD_DIM, :keys],
                scores_ref[pair, :, half * count : (half + 1) * count],
                preferred_element_type=jnp.float32,
            )
            for half in range(2)
        ]
        put(0, pair, jnp.concatenate(query_grad, 0).astype(jnp.bfloat16).T)
    for step in range(replicas):
        place = place_of(info_ref, step, replicas)
        keep_ref[step] = grads_ref[place + parity]
        crossing = grads_ref[place + 1 - parity]
        part = crossing.shape[1] // len(send_refs)
        for at, send_ref in enumerate(send_refs):
            send_ref[step] = crossing[:, at * part : (at + 1) * part]


def norm_part_kernel(info_ref, keep_ref, w_ref, after_ref, out_ref):
    part = keep_ref[...].reshape(out_ref.shape[0], -1)
    out_ref[...] = jnp.dot(part, w_ref[...], preferred_element_type=jnp.float32)


def norm_kernel(upper, info_ref, keep_ref, normed_ref, rms_ref, incoming_ref, *refs):
    w_own_ref, w_other_ref = refs[:2]
    refs = refs[2:]
    got_refs = refs[: PIECES[upper]]
    out_refs = refs[len(got_refs) :]
    replicas, shard_rows, model_width = incoming_ref.shape
    rows = replicas * shard_rows
    got = [got_ref[...].reshape(rows, -1) for got_ref in got_refs]
    norm_grad = jnp.dot(
        jnp.concatenate(got, 1), w_other_ref[...], preferred_element_type=jnp.float32
    )
    if upper:
        norm_grad += keep_ref[...]
    else:
        norm_grad += jnp.dot(
            keep_ref[...].reshape(rows, -1), w_own_ref[...], preferred_element_type=jnp.float32
        )
    chunk = 1 if upper else 0
    normed = normed_ref[chunk].reshape(rows, model_width)
    inverse_rms = rms_ref[chunk].reshape(rows, -1)[:, :1]
    inner = jnp.mean(norm_grad * normed, axis=-1, keepdims=True)
    incoming = incoming_ref[...].reshape(rows, model_width).astype(jnp.float32)
    grad_in = incoming + inverse_rms * (norm_grad - normed * inner)
    grad_in = grad_in.astype(jnp.bfloat16).reshape(replicas, shard_rows, model_width)
    out_refs[-1][:, :, :model_width] = grad_in
    spare = out_refs[-1].shape[2] - model_width
    if spare:
        out_refs[-1][:, :, model_width:] = jnp.zeros((replicas, shard_rows, spare), jnp.bfloat16)


def in_terms(gt_ref, grad_refs, half, rows):
    count = grad_refs[0].shape[0] * grad_refs[0].shape[1]
    return sum(
        jnp.dot(
            gt_ref[2 * half * rows : 2 * (half + 1) * rows, chunk * count : (chunk + 1) * count],
            part_ref[...].reshape(count, -1),
            preferred_element_type=jnp.float32,
        )
        for chunk, part_ref in enumerate(grad_refs)
    )


def send_kernel(gt_ref, lower_ref, upper_ref, pass_ref, keep_ref):
    rows = pass_ref.shape[0]
    total = in_terms(gt_ref, (lower_ref, upper_ref), 1, rows)
    pass_ref[...] = total[:rows].astype(jnp.bfloat16)
    keep_ref[...] = total[rows:].astype(jnp.bfloat16)


def term_kernel(info_ref, gt_ref, *refs):
    grad_refs, at_refs, row_refs = refs[:2], refs[2:4], refs[4:6]
    pass_ref, keep_ref, out_pass_ref, out_keep_ref, out_send_ref = refs[7:]
    rows = pass_ref.shape[0]
    width = out_send_ref.shape[1]
    parity, x, y = info_ref[0], info_ref[1], info_ref[2]
    sent = jnp.where(parity == y, 2 * (1 - x) + 1 - parity, 2 * x + parity)
    blocks = (sent, 2 * x + 1 - parity, 2 * x + parity)
    total = jnp.zeros((3 * rows, width), jnp.float32)
    for at_ref, part_ref in zip(at_refs, row_refs):
        picked = [at_ref[pl.ds(pl.multiple_of(block * rows, 128), rows)] for block in blocks]
        total += jnp.dot(
            jnp.concatenate(picked, 0),
            part_ref[...].reshape(-1, width),
            preferred_element_type=jnp.float32,
        )
    out_send_ref[...] = total[:rows].astype(jnp.bfloat16)
    out_pass_ref[...] = total[rows : 2 * rows]
    out_keep_ref[...] = total[2 * rows :]
    total = in_terms(gt_ref, grad_refs, 0, rows)
    pass_ref[...] = total[:rows]
    keep_ref[...] = total[rows:]


def sum_kernel(own_ref, got_ref, out_own_ref, out_got_ref, after_ref, sum_ref):
    columns = own_ref.shape[1]
    sum_ref[:, :columns] = (own_ref[...] + got_ref[...].astype(jnp.float32)).astype(jnp.bfloat16)
    sum_ref[:, columns:] = (out_own_ref[...] + out_got_ref[...].astype(jnp.float32)).astype(
        jnp.bfloat16
    )


def pick_kernel(info_ref, upper_ref, lower_ref, out_ref):
    crossing = info_ref[0] == 0
    for step in range(2):
        for chunk, part_ref in enumerate((lower_ref, upper_ref)):
            wanted = info_ref[2] == (chunk if step == 1 else 1 - chunk)

            @pl.when(wanted & (crossing if step == 1 else jnp.logical_not(crossing)))
            def _():
                out_ref[...] = part_ref[step]


def join_kernel(info_ref, upper_ref, lower_ref, got_ref, out_ref):
    micro = info_ref[4]
    out_ref[0, 1 - micro] = got_ref[...]

    @pl.when(info_ref[2] == 1)
    def _():
        out_ref[0, micro] = upper_ref[0]

    @pl.when(info_ref[2] != 1)
    def _():
        out_ref[0, micro] = lower_ref[0]


def place_kernel(
    info_ref, own_ref, got_ref, out_own_ref, out_got_ref, sibling_ref, d_in_ref, d_out_ref
):
    columns = own_ref.shape[1] // 3
    own = own_ref[...] + got_ref[...].astype(jnp.float32)
    sibling = sibling_ref[:, : 3 * columns].astype(jnp.float32)
    for part, half in ((own, info_ref[0]), (sibling, 1 - info_ref[0])):
        for block in range(3):
            first = pl.multiple_of((2 * block + half) * columns, 128)
            d_in_ref[:, pl.ds(first, columns)] = part[:, block * columns : (block + 1) * columns]
    owner = info_ref[0] == info_ref[2]

    @pl.when(owner)
    def _():
        d_out_ref[...] = out_own_ref[...] + out_got_ref[...].astype(jnp.float32)

    @pl.when(jnp.logical_not(owner))
    def _():
        d_out_ref[...] = sibling_ref[:, 3 * columns :].astype(jnp.float32)


def call(kernel, outs, operands, scratch=(), flops=0, scalars=1, after=None, mebibytes=5, far=0):
    in_specs = [pl.BlockSpec(memory_space=pltpu.SMEM)] * scalars
    in_specs += [pl.BlockSpec(memory_space=pltpu.HBM)] * far
    in_specs += [pl.BlockSpec(memory_space=pltpu.VMEM)] * (len(operands) - scalars - far)
    if after is not None:
        operands = [*operands, after]
        in_specs.append(pl.BlockSpec(memory_space=pl.ANY))
    return pl.pallas_call(
        kernel,
        out_shape=list(outs),
        in_specs=in_specs,
        out_specs=[pl.BlockSpec(memory_space=pltpu.VMEM)] * len(outs),
        scratch_shapes=list(scratch),
        cost_estimate=pl.CostEstimate(flops=1, bytes_accessed=1, transcendentals=0),
        compiler_params=pltpu.CompilerParams(vmem_limit_bytes=mebibytes * 2**20),
    )(*operands)


def by_chips(acts, grad_top, w_in, w_out, offsets):
    half_type, full_type = jnp.bfloat16, jnp.float32
    shape = jax.ShapeDtypeStruct
    sections = lax.axis_size("section")
    shards = lax.axis_size("tm")
    levels = offsets.shape[1]
    half = shards // 2
    replicas = half // 2
    me = lax.axis_index("tm")
    parity = lax.rem(me, 2)
    side = lax.div(me, half)
    micro_count, shard_rows, model_width = acts.shape[1:]
    columns = model_width // 2
    heads = columns // HEAD_DIM
    seq = shards * shard_rows
    count = seq // 2
    w_qkv = w_in[0]
    w_rows = w_out[0]
    beside = lax.div(lax.rem(me, half), 2)
    micro = lax.rem(side + beside, 2)
    info = jnp.stack([parity, beside, side, lax.axis_index("section"), micro])
    info = jnp.concatenate([info.astype(jnp.int32), offsets[0]])

    def swapped(value, bits, chosen=None):
        pairs = [(device, device ^ bits) for device in range(shards)]
        pairs = [pair for pair in pairs if chosen is None or chosen(pair[0])]
        return lax.ppermute(value, "tm", pairs)

    core, near, far = 1, 2, half

    packed = shape((shard_rows, model_width + 128), half_type)
    top_shape = shape((shard_rows, model_width), half_type)
    own_acts, other_acts, own_top, other_top = call(
        functools.partial(pack_kernel, levels),
        [packed, packed, top_shape, top_shape],
        [info, acts[0], grad_top],
    )
    weights = [
        call(
            functools.partial(turn_kernel, own),
            [shape((3 * columns, model_width), half_type)],
            [info, w_qkv],
            after=own_acts,
        )[0]
        for own in (True, False)
    ]
    pieces = [own_acts, swapped(other_acts, near), swapped(other_acts, far)]
    pieces += [swapped(own_acts, near + far)]
    tops = [own_top, swapped(other_top, near), swapped(other_top, far)]
    pieces[-1], tops, weights = lax.optimization_barrier((pieces[-1], tops, weights))
    tops += [swapped(own_top, near + far)]
    pieces += [swapped(piece, core) for piece in pieces]

    rows_shape = shape((seq, columns), half_type)
    normed, rms, norm, flag_rows, queries, keys, values, keys_t = call(
        functools.partial(project_kernel, replicas),
        [
            shape((2, replicas, shard_rows, model_width), full_type),
            shape((2, replicas, shard_rows, 128), full_type),
            shape((seq, model_width), half_type),
            shape((128, seq), full_type),
            rows_shape,
            rows_shape,
            rows_shape,
            shape((columns, seq), half_type),
        ],
        [info, *pieces, w_qkv],
        scratch=[pltpu.VMEM((shards, *packed.shape), half_type)],
        flops=6 * seq * model_width * columns,
        after=weights[1],
    )
    pairs = heads // 2
    upper_prob, upper_at = call(
        functools.partial(upper_forward_kernel, levels, shard_rows),
        [
            shape((pairs, seq, 2 * count), half_type),
            shape((columns, count), half_type),
        ],
        [flag_rows, queries, keys, values],
        scalars=0,
        flops=4 * columns * seq * count,
    )
    tops, upper_at = lax.optimization_barrier((tuple(tops), upper_at))
    tops = [*tops, *[swapped(piece, core) for piece in tops]]
    own_rows = model_width // shards
    probs, attended = {True: upper_prob}, {True: upper_at}
    got, kept = {}, {}
    piece_shape = shape((replicas, shard_rows, model_width), half_type)
    wide_shape = shape((replicas, shard_rows, model_width + 128), half_type)
    grads_shape = shape((replicas, shard_rows, 3 * columns), half_type)
    sum_shape = shape((count, columns), full_type)
    full_grads = shape((half, shard_rows, 3 * columns), half_type)
    full_rows = shape((half, shard_rows, model_width), half_type)
    term_shape = (own_rows, 3 * columns)
    rows_scratch = pltpu.VMEM(full_rows.shape, half_type)
    grads_scratch = pltpu.VMEM(full_grads.shape, half_type)
    result, full, ordered = {}, {}, {}
    for turn in range(sections):
        last = turn + 1 == sections
        fresh_section = sections - 1 - turn
        sums, parts, crossed = [], {}, {}

        def norm_step(upper, after):
            (result[upper],) = call(
                functools.partial(norm_kernel, upper),
                [wide_shape if turn + 2 == sections and not upper else piece_shape],
                [info, parts[upper], normed, rms, kept[upper][0], *weights, *crossed[upper]],
                after=after,
            )
            if not last:
                hop = [(sections - 1 - turn, sections - 2 - turn)]
                got[upper] = lax.ppermute(result[upper], "section", hop)

        for upper in (True, False):
            rows_in, after = tops, keys_t if upper else result.get(True)
            if turn:
                tied = parts if last else result
                before = result[False] if upper else tied[True]
                got[upper], after = lax.optimization_barrier((got[upper], before))
                if not upper:
                    tied[True] = after
                if last and not upper:
                    after, result[True] = lax.optimization_barrier((after, result[True]))
                rows_in = [got[upper], swapped(got[upper], core), *kept[upper]]
            part = 3 * columns // PIECES[upper]
            cross = [shape((replicas, shard_rows, part), half_type)] * PIECES[upper]
            outs = [piece_shape] * (1 if last else 2) + [grads_shape, *cross]
            outs += [sum_shape, sum_shape] if upper else []
            scratch = []
            if last:
                outs += [full_grads]
            else:
                scratch += [grads_scratch]
            if last:
                outs += [full_rows]
            else:
                scratch += [rows_scratch]
            part_keys = seq if upper else count
            scratch += [pltpu.VMEM((pairs, part_keys, 2 * count), half_type)]
            if last:
                scratch += [pltpu.VMEM(piece_shape.shape, half_type)]
            answer = call(
                functools.partial(
                    backward_kernel, upper, 0 if turn else len(tops), last, fresh_section
                ),
                outs,
                [info, *rows_in, w_rows, probs[upper], queries, values, keys_t]
                + [attended[upper], *sums],
                scratch=scratch,
                flops=2 * count * columns * (2 * model_width + 4 * part_keys),
                after=after,
            )
            kept[upper] = tuple(answer[:2])
            answer = answer[1 if last else 2 :]
            keep = answer[0]
            send = answer[1 : 1 + len(cross)]
            parts[upper] = keep
            if upper:
                sums = answer[1 + len(cross) : 3 + len(cross)]
                (parts[True],) = call(
                    norm_part_kernel,
                    [shape((replicas * shard_rows, model_width), full_type)],
                    [info, keep, weights[0]],
                    flops=3 * replicas * shard_rows * model_width * model_width,
                    after=keep,
                )
                if turn == 0:
                    lower_prob, lower_at, norm_t = call(
                        functools.partial(lower_forward_kernel, levels, shard_rows),
                        [
                            shape((pairs, count, 2 * count), half_type),
                            shape((columns, count), half_type),
                            shape((4 * own_rows, seq), half_type),
                        ],
                        [info, norm, flag_rows, queries, keys, values],
                        flops=4 * columns * count * count,
                        after=parts[True],
                    )
                    probs[False], attended[False] = lower_prob, lower_at
            if last:
                full[upper], ordered[upper] = answer[-2:]
            crossed[upper] = [swapped(piece, core) for piece in send]
            if upper:
                norm_step(True, keep)
        if last:
            send_pass, send_keep = call(
                send_kernel,
                [shape(term_shape, half_type)] * 2,
                [norm_t, full[False], full[True]],
                scalars=0,
            )
            terms = call(
                term_kernel,
                [shape(term_shape, full_type)] * 2
                + [shape((own_rows, model_width), full_type)] * 2
                + [shape((own_rows, model_width), half_type)],
                [info, norm_t, full[False], full[True], attended[False], attended[True]]
                + [ordered[False], ordered[True]],
                after=send_keep,
            )
        norm_step(False, terms[4] if last else result[True])

    in_pass, in_keep, out_pass, out_keep, out_send = terms
    got_pass = swapped(send_pass, near)
    got_keep = swapped(send_keep, far)
    own_rows_grad = [result[True], result[False]]
    (theirs,) = call(pick_kernel, [top_shape], [info, *own_rows_grad])
    to_owner = [(device, device ^ (far if device % 2 else near)) for device in range(shards)]
    partner = lax.ppermute(theirs, "tm", to_owner)
    got_out_pass = swapped(out_send, near, lambda device: device // half == device % 2)
    got_out_keep = swapped(out_send, far, lambda device: device // half != device % 2)
    _, _, done = lax.optimization_barrier((got_keep, got_out_keep, partner))
    (summed,) = call(
        sum_kernel,
        [shape((own_rows, 3 * columns + model_width), half_type)],
        [in_pass, got_pass, out_pass, got_out_pass],
        scalars=0,
        after=done,
    )
    d_w_in, d_w_out = call(
        place_kernel,
        [
            shape((own_rows, 3 * model_width), full_type),
            shape((own_rows, model_width), full_type),
        ],
        [info, in_keep, got_keep, out_keep, got_out_keep, swapped(summed, core)],
    )
    (d_acts,) = call(
        join_kernel, [shape(acts.shape, half_type)], [info, *own_rows_grad, partner]
    )
    return (d_acts, d_w_in[None], d_w_out[None])


def layer_gradients(acts, grad_top, w_in, w_out, offsets):
    shards = lax.axis_size("tm")
    micro_count, shard_rows, model_width = acts.shape[1:]
    heads = model_width // HEAD_DIM
    prob_bytes = 2 * heads * (shards * shard_rows) ** 2
    fits = prob_bytes <= 2**24 and model_width % (128 * shards) == 0 and shard_rows % 16 == 0
    square = shards % 4 == 0 and shards // 4 == 2
    if micro_count == 2 and square and heads % 4 == 0 and fits:
        return by_chips(acts, grad_top, w_in, w_out, offsets)
    return per_device(acts, grad_top, w_in, w_out, offsets)


def solution(mesh):
    placed = (
        P("section", None, "tm", None),
        P(None, "tm", None),
        P("section", None, None),
        P("section", None, None),
        P("tm", None),
    )
    return jax.shard_map(
        layer_gradients,
        mesh=mesh,
        in_specs=placed,
        out_specs=(
            P("section", None, "tm", None),
            P("section", "tm", None),
            P("section", "tm", None),
        ),
        check_vma=False,
    )
```

```python
import functools
import jax
import jax.numpy as jnp
from jax import lax
from jax.experimental import pallas as pl
from jax.experimental.pallas import tpu as pltpu
from jax.sharding import PartitionSpec as P

HEAD_DIM = 64


epsilon = 1e-06
PIECES = {True: 2, False: 2}
negative_fill = -1e30


def shifted(value, axis, steps):
    count = lax.axis_size(axis)
    initial, last = (max(0, -steps), min(count, count - steps))
    return lax.ppermute(value, axis, [(source, source + steps) for source in range(initial, last)])


def normalize(inputs):
    values = inputs.astype(jnp.float32)
    inverse_rms = lax.rsqrt(jnp.mean(values * values, axis=-1, keepdims=True) + epsilon)
    return (values * inverse_rms, inverse_rms)


def key_bias(level_flags, shard_rows):
    position = jnp.arange(shard_rows)
    own_part = position[None, :] <= position[:, None]
    far_part = jnp.repeat(level_flags != 0, shard_rows)
    far_part = jnp.broadcast_to(far_part[None, :], (shard_rows, far_part.shape[0]))
    return jnp.concatenate([own_part, far_part], 1)


def split_heads(row_block):
    return row_block.reshape(row_block.shape[0], -1, HEAD_DIM)


def softmax_keys(queries, key_heads, allowed):
    scores = jnp.einsum(
        "ihd,jhd->hij", queries, key_heads, preferred_element_type=jnp.float32
    ) * HEAD_DIM ** (-0.5)
    scores = jnp.where(allowed[None], scores, negative_fill)
    highest = jnp.max(scores, axis=-1, keepdims=True)
    shifted_exp = jnp.where(allowed[None], jnp.exp(scores - highest), 0.0)
    return shifted_exp / jnp.sum(shifted_exp, axis=-1, keepdims=True)


def attend(query_rows, key_rows, allowed):
    model_width = query_rows.shape[1]
    probability = softmax_keys(
        split_heads(query_rows), split_heads(key_rows[:, :model_width]), allowed
    )
    attended = jnp.einsum(
        "hij,jhd->ihd",
        probability.astype(jnp.bfloat16),
        split_heads(key_rows[:, model_width:]),
        preferred_element_type=jnp.float32,
    )
    return attended.reshape(query_rows.shape).astype(jnp.bfloat16)


def attend_back(query_rows, key_rows, allowed, incoming, attended, w_proj):
    model_width = query_rows.shape[1]
    queries = split_heads(query_rows)
    key_heads = split_heads(key_rows[:, :model_width])
    value_heads = split_heads(key_rows[:, model_width:])
    probability = softmax_keys(queries, key_heads, allowed)
    rounded = probability.astype(jnp.bfloat16)
    upstream = lax.dot_general(
        incoming, w_proj, (((1,), (1,)), ((), ())), preferred_element_type=jnp.float32
    ).astype(jnp.bfloat16)
    up_heads = split_heads(upstream)
    delta = jnp.einsum(
        "ihd,ihd->hi", up_heads.astype(jnp.float32), split_heads(attended).astype(jnp.float32)
    )[..., None]
    prob_grad = jnp.einsum(
        "ihd,jhd->hij", up_heads, value_heads, preferred_element_type=jnp.float32
    )
    score_grad = (probability * (prob_grad - delta)).astype(jnp.bfloat16)
    scale_factor = HEAD_DIM ** (-0.5)
    query_grad = (
        jnp.einsum("hij,jhd->ihd", score_grad, key_heads, preferred_element_type=jnp.float32)
        * scale_factor
    )
    key_grad = (
        jnp.einsum("hij,ihd->jhd", score_grad, queries, preferred_element_type=jnp.float32)
        * scale_factor
    )
    value_grad = jnp.einsum("hij,ihd->jhd", rounded, up_heads, preferred_element_type=jnp.float32)
    return (
        query_grad.reshape(-1, model_width),
        key_grad.reshape(-1, model_width),
        value_grad.reshape(-1, model_width),
    )


def per_device(acts, grad_top, w_in, w_out, offsets):
    sections = lax.axis_size("section")
    shards = lax.axis_size("tm")
    levels = shards.bit_length() - 1
    section_index = lax.axis_index("section")
    micro_count = acts.shape[1]
    shard_rows = acts.shape[2]
    model_width = acts.shape[3]
    w_qkv = w_in[0]
    w_proj = w_out[0]
    level_flags = offsets[0]
    normed, inverse_rms = normalize(acts[0])
    rounded_norm = normed.astype(jnp.bfloat16)
    qkv = jnp.dot(rounded_norm.reshape(-1, model_width), w_qkv, preferred_element_type=jnp.float32)
    qkv = qkv.astype(jnp.bfloat16).reshape(micro_count, shard_rows, 3 * model_width)
    pairs = qkv[..., model_width:]
    far_list = [shifted(pairs, "tm", 2**level) for level in range(levels)]
    key_rows = jnp.concatenate([pairs] + far_list, 1)
    allowed = key_bias(level_flags, shard_rows)
    attended = jnp.stack(
        [
            attend(qkv[index, :, :model_width], key_rows[index], allowed)
            for index in range(micro_count)
        ],
        0,
    )

    def attention_part(incoming, slot):
        query_rows = lax.dynamic_index_in_dim(qkv, slot, 0, False)[:, :model_width]
        slot_keys = lax.dynamic_index_in_dim(key_rows, slot, 0, False)
        slot_attended = lax.dynamic_index_in_dim(attended, slot, 0, False)
        query_grad, key_grad, value_grad = attend_back(
            query_rows, slot_keys, allowed, incoming, slot_attended, w_proj
        )
        owner_sum = jnp.concatenate([key_grad[:shard_rows], value_grad[:shard_rows]], 1)
        far_part = jnp.concatenate([key_grad[shard_rows:], value_grad[shard_rows:]], 1)
        far_part = far_part.astype(jnp.bfloat16).reshape(levels, shard_rows, 2 * model_width)
        return (query_grad, owner_sum, far_part)

    def empty_attention(incoming, slot):
        return (
            jnp.zeros((shard_rows, model_width), jnp.float32),
            jnp.zeros((shard_rows, 2 * model_width), jnp.float32),
            jnp.zeros((levels, shard_rows, 2 * model_width), jnp.bfloat16),
        )

    def norm_part(qkv_grad, incoming, slot):
        norm_grad = lax.dot_general(
            qkv_grad, w_qkv, (((1,), (1,)), ((), ())), preferred_element_type=jnp.float32
        )
        slot_normed = lax.dynamic_index_in_dim(normed, slot, 0, False)
        slot_rms = lax.dynamic_index_in_dim(inverse_rms, slot, 0, False)
        inner = jnp.mean(norm_grad * slot_normed, axis=-1, keepdims=True)
        return (incoming.astype(jnp.float32) + slot_rms * (norm_grad - slot_normed * inner)).astype(
            jnp.bfloat16
        )

    def empty_norm(qkv_grad, incoming, slot):
        return jnp.zeros((shard_rows, model_width), jnp.bfloat16)

    def step(turn, carry):
        received, grad_store, qkv_store, incoming_store = carry
        slot_raw = turn - (sections - 1 - section_index)
        active = (slot_raw >= 0) & (slot_raw < micro_count)
        slot = jnp.clip(slot_raw, 0, micro_count - 1)
        incoming = jnp.where(
            section_index == sections - 1,
            lax.dynamic_index_in_dim(grad_top, slot, 0, False),
            received,
        )
        query_grad, owner_sum, far_part = lax.cond(
            active, attention_part, empty_attention, incoming, slot
        )
        for level in range(levels):
            owner_sum = owner_sum + shifted(far_part[level], "tm", -(2**level)).astype(jnp.float32)
        qkv_grad = jnp.concatenate([query_grad, owner_sum], 1).astype(jnp.bfloat16)
        grad_in = lax.cond(active, norm_part, empty_norm, qkv_grad, incoming, slot)
        sent_down = shifted(grad_in, "section", -1)
        grad_store = jnp.where(
            active, lax.dynamic_update_index_in_dim(grad_store, grad_in, slot, 0), grad_store
        )
        qkv_store = jnp.where(
            active, lax.dynamic_update_index_in_dim(qkv_store, qkv_grad, slot, 0), qkv_store
        )
        incoming_store = jnp.where(
            active,
            lax.dynamic_update_index_in_dim(incoming_store, incoming, slot, 0),
            incoming_store,
        )
        return (sent_down, grad_store, qkv_store, incoming_store)

    initial = (
        jnp.zeros((shard_rows, model_width), jnp.bfloat16),
        jnp.zeros((micro_count, shard_rows, model_width), jnp.bfloat16),
        jnp.zeros((micro_count, shard_rows, 3 * model_width), jnp.bfloat16),
        jnp.zeros((micro_count, shard_rows, model_width), jnp.bfloat16),
    )
    received, grad_store, qkv_store, incoming_store = lax.fori_loop(
        0, sections + micro_count - 1, step, initial
    )
    flat_norm = rounded_norm.reshape(-1, model_width)
    flat_attended = attended.reshape(-1, model_width)
    flat_qkv = qkv_store.reshape(-1, 3 * model_width)
    flat_incoming = incoming_store.reshape(-1, model_width)
    contract = (((0,), (0,)), ((), ()))
    first = lax.dot_general(flat_norm, flat_qkv, contract, preferred_element_type=jnp.float32)
    second = lax.dot_general(
        flat_attended, flat_incoming, contract, preferred_element_type=jnp.float32
    )
    summed = lax.psum_scatter(
        jnp.concatenate([first, second], 1).astype(jnp.bfloat16),
        "tm",
        scatter_dimension=0,
        tiled=True,
    ).astype(jnp.float32)
    return (
        grad_store[None],
        summed[None, :, : 3 * model_width],
        summed[None, :, 3 * model_width :],
    )


def side_by_side(transposed, pair):
    width = 2 * HEAD_DIM
    rows = transposed[pair * width : (pair + 1) * width]
    empty = jnp.zeros((HEAD_DIM, rows.shape[1]), rows.dtype)
    return jnp.concatenate(
        [
            jnp.concatenate([rows[:HEAD_DIM], empty], 0),
            jnp.concatenate([empty, rows[HEAD_DIM:]], 0),
        ],
        1,
    )


def one_above_other(rows, masks):
    return jnp.concatenate([rows * masks[0], rows * masks[1]], 0)


def head_masks():
    lane = lax.broadcasted_iota(jnp.int32, (1, 2 * HEAD_DIM), 1)
    return [
        jnp.where(lane < HEAD_DIM, 1.0, 0.0).astype(jnp.bfloat16),
        jnp.where(lane < HEAD_DIM, 0.0, 1.0).astype(jnp.bfloat16),
    ]


def key_bias_rows(flag_rows, levels, shard_rows, keys, first_query, count):
    key_at = lax.broadcasted_iota(jnp.int32, (keys, count), 0)
    query_at = lax.broadcasted_iota(jnp.int32, (keys, count), 1) + first_query
    gap = lax.div(query_at, shard_rows) - lax.div(key_at, shard_rows)
    allowed = (gap == 0) & (key_at <= query_at)
    for level in range(levels):
        allowed = allowed | ((gap == 2**level) & (flag_rows[level : level + 1] != 0))
    return jnp.where(allowed, 0.0, negative_fill)


def softmax_pass(queries, keys, values, bias, prob_ref, at_ref):
    queries_t = queries.T
    values_t = values.T
    width = 2 * HEAD_DIM
    count = queries.shape[0]
    for pair in range(queries.shape[1] // width):
        at_pair = slice(pair * width, (pair + 1) * width)
        scores = jnp.dot(
            keys[:, at_pair], side_by_side(queries_t, pair), preferred_element_type=jnp.float32
        )
        for half in range(2):
            at_half = slice(half * count, (half + 1) * count)
            biased = scores[:, at_half] + bias
            shifted_exp = jnp.exp(biased - jnp.max(biased, axis=0, keepdims=True))
            probability = shifted_exp * (1.0 / jnp.sum(shifted_exp, axis=0, keepdims=True))
            prob_ref[pair, :, at_half] = probability.astype(jnp.bfloat16)
    for head in range(queries.shape[1] // HEAD_DIM):
        at = slice(head * HEAD_DIM, (head + 1) * HEAD_DIM)
        at_half = slice(head % 2 * count, (head % 2 + 1) * count)
        at_ref[at] = jnp.dot(
            values_t[at], prob_ref[head // 2, :, at_half], preferred_element_type=jnp.float32
        ).astype(jnp.bfloat16)


def pack_kernel(
    levels, info_ref, acts_ref, top_ref, own_ref, other_ref, own_top_ref, other_top_ref
):
    model_width = acts_ref.shape[2]
    shard_rows = own_ref.shape[0]
    micro = info_ref[4]
    lane = lax.broadcasted_iota(jnp.int32, (shard_rows, own_ref.shape[1] - model_width), 1)
    flags = jnp.zeros(lane.shape, jnp.float32)
    for level in range(levels):
        seen = jnp.where(info_ref[5 + level] != 0, 1.0, 0.0)
        flags = jnp.where(lane == level, seen, flags)
    for at, out_ref, out_top_ref in (
        (micro, own_ref, own_top_ref),
        (1 - micro, other_ref, other_top_ref),
    ):
        out_ref[:, :model_width] = acts_ref[at]
        out_ref[:, model_width:] = flags.astype(jnp.bfloat16)
        out_top_ref[...] = top_ref[at]


def turn_kernel(own, info_ref, w_ref, after_ref, out_ref):
    columns = out_ref.shape[0] // 3
    model_width = w_ref.shape[0]
    half = info_ref[0] if own else 1 - info_ref[0]
    for block in range(3):
        first = pl.multiple_of(block * model_width + half * columns, 128)
        out_ref[block * columns : (block + 1) * columns] = w_ref[:, pl.ds(first, columns)].T


def project_kernel(replicas, info_ref, *refs):
    pieces = refs[: 4 * replicas]
    w_ref, _, normed_ref, rms_ref, norm_ref, flag_ref, q_ref, k_ref, v_ref, kt_ref, packed_ref = refs[
        4 * replicas :
    ]
    shards, shard_rows = packed_ref.shape[:2]
    model_width = w_ref.shape[0]
    seq = shards * shard_rows
    columns = q_ref.shape[1]
    at_piece = 0
    for core in (info_ref[0], 1 - info_ref[0]):
        for side in (info_ref[2], 1 - info_ref[2]):
            for step in range(replicas):
                shard = side * (shards // 2) + place_of(info_ref, step, replicas) + core
                packed_ref[shard] = pieces[at_piece][...]
                at_piece += 1
    for chunk in range(2):
        for step in range(replicas):
            shard = chunk * (shards // 2) + place_of(info_ref, step, replicas) + info_ref[0]
            normed, inverse_rms = normalize(packed_ref[shard][:, :model_width])
            normed_ref[chunk, step] = normed
            rms_ref[chunk, step] = jnp.broadcast_to(inverse_rms, rms_ref.shape[2:])
    normed, _ = normalize(packed_ref[:, :, :model_width].reshape(seq, model_width))
    rounded = normed.astype(jnp.bfloat16)
    norm_ref[...] = rounded
    flag_ref[...] = packed_ref[:, :, model_width:].reshape(seq, -1).astype(jnp.float32).T
    scale_factor = HEAD_DIM ** (-0.5)
    for block, out_ref in enumerate((q_ref, k_ref, v_ref)):
        first = pl.multiple_of(block * model_width + info_ref[0] * columns, 128)
        product = jnp.dot(
            rounded, w_ref[:, pl.ds(first, columns)], preferred_element_type=jnp.float32
        ).astype(jnp.bfloat16)
        out_ref[...] = product * scale_factor if block == 0 else product
    kt_ref[...] = (k_ref[...] * scale_factor).T


def upper_forward_kernel(
    levels, shard_rows, flag_ref, q_ref, k_ref, v_ref, prob_ref, at_ref
):
    seq = q_ref.shape[0]
    count = seq // 2
    bias = key_bias_rows(flag_ref[:, count:], levels, shard_rows, seq, count, count)
    softmax_pass(q_ref[count:], k_ref[...], v_ref[...], bias, prob_ref, at_ref)


def lower_forward_kernel(
    levels,
    shard_rows,
    info_ref,
    norm_ref,
    flag_ref,
    q_ref,
    k_ref,
    v_ref,
    after_ref,
    prob_ref,
    at_ref,
    gt_ref,
):
    seq = norm_ref.shape[0]
    count = seq // 2
    bias = key_bias_rows(flag_ref[:, :count], levels, shard_rows, count, 0, count)
    softmax_pass(q_ref[:count], k_ref[:count], v_ref[:count], bias, prob_ref, at_ref)
    rows = gt_ref.shape[0] // 4
    parity, x, y = info_ref[0], info_ref[1], info_ref[2]
    half = norm_ref.shape[1] // rows // 2
    for place, block in enumerate(
        (
            half * y + 2 * x + 1 - parity,
            half * y + 2 * x + parity,
            half * y + 2 * (1 - x) + 1 - parity,
            half * (1 - y) + 2 * x + parity,
        )
    ):
        first = pl.multiple_of(block * rows, 128)
        gt_ref[place * rows : (place + 1) * rows] = norm_ref[:, pl.ds(first, rows)].T


def place_of(info_ref, step, replicas):
    return 2 * lax.rem(info_ref[1] - step + replicas, replicas)


def merge_rows(info_ref, fresh, got_refs, kept_refs, out_refs, rows_ref):
    @pl.when(fresh)
    def _():
        for core, out_ref in enumerate(out_refs):
            out_ref[...] = got_refs[core][:, :, : out_ref.shape[2]]

    @pl.when(jnp.logical_not(fresh))
    def _():
        for out_ref, kept_ref in zip(out_refs, kept_refs):
            out_ref[...] = kept_ref[...]

    place_rows(info_ref, out_refs, rows_ref)


def place_rows(info_ref, out_refs, rows_ref):
    replicas = out_refs[0].shape[0]
    for step in range(replicas):
        place = place_of(info_ref, step, replicas)
        rows_ref[place + info_ref[0]] = out_refs[0][step]
        rows_ref[place + 1 - info_ref[0]] = out_refs[1][step]


def merge_tops(info_ref, upper, piece_refs, out_refs, rows_ref):
    replicas = out_refs[0].shape[0]
    own_chunk = info_ref[2] == (1 if upper else 0)
    for core in range(2):
        refs = piece_refs[2 * replicas * core : 2 * replicas * (core + 1)]

        @pl.when(own_chunk)
        def _():
            for step in range(replicas):
                out_refs[core][step] = refs[step][...]

        @pl.when(jnp.logical_not(own_chunk))
        def _():
            for step in range(replicas):
                out_refs[core][step] = refs[replicas + step][...]

    place_rows(info_ref, out_refs, rows_ref)


def backward_kernel(upper, tops, last, fresh_section, info_ref, *refs):
    refs = list(refs)
    got = tops or 4
    got_refs = refs[:got]
    w_ref, prob_ref, q_ref, v_ref, kt_ref, at_ref = refs[got : got + 6]
    refs = refs[got + 6 :]
    if not upper:
        key_sum_ref, value_sum_ref = refs[:2]
        refs = refs[2:]
    refs = refs[1:]
    if last:
        refs = [refs[0], refs[-1], *refs[1:-1]]
    own_ref, other_ref, keep_ref = refs[:3]
    send_refs = refs[3 : 3 + PIECES[upper]]
    refs = refs[3 + len(send_refs) :]
    if upper:
        key_sum_ref, value_sum_ref = refs[:2]
        refs = refs[2:]
    grads_ref, rows_ref, scores_ref = refs
    replicas, shard_rows, model_width = own_ref.shape
    count = rows_ref.shape[0] * shard_rows
    keys = prob_ref.shape[1]
    parity = info_ref[0]
    columns = q_ref.shape[1]
    width = 2 * HEAD_DIM
    if tops:
        merge_tops(info_ref, upper, got_refs, (own_ref, other_ref), rows_ref)
    else:
        fresh = info_ref[3] == fresh_section
        merge_rows(info_ref, fresh, got_refs[:-2], got_refs[-2:], (own_ref, other_ref), rows_ref)
    rows = rows_ref[...].reshape(count, model_width)
    weights = w_ref[pl.ds(pl.multiple_of(parity * columns, 128), columns), :]
    over_width = (((1,), (1,)), ((), ()))
    upstream = lax.dot_general(
        rows, weights, over_width, preferred_element_type=jnp.float32
    ).astype(jnp.bfloat16)
    upstream_t = upstream.T
    product_t = upstream_t.astype(jnp.float32) * at_ref[...].astype(jnp.float32)
    first_query = keys - count
    masks = head_masks()

    def put(block, pair, part):
        first = block * columns + pair * width
        grads_ref[:, :, first : first + width] = part.astype(jnp.bfloat16).reshape(
            -1, shard_rows, width
        )

    for pair in range(columns // width):
        at_pair = slice(pair * width, (pair + 1) * width)
        prob_grad = jnp.dot(
            v_ref[:keys, at_pair], side_by_side(upstream_t, pair), preferred_element_type=jnp.float32
        )
        for half in range(2):
            at_half = slice(half * count, (half + 1) * count)
            first = pair * width + half * HEAD_DIM
            delta = jnp.sum(product_t[first : first + HEAD_DIM], axis=0, keepdims=True)
            scores_ref[pair, :, at_half] = (
                prob_ref[pair, :, at_half].astype(jnp.float32) * (prob_grad[:, at_half] - delta)
            ).astype(jnp.bfloat16)
        value_grad = jnp.dot(
            prob_ref[pair],
            one_above_other(upstream[:, at_pair], masks),
            preferred_element_type=jnp.float32,
        )
        if upper:
            value_sum_ref[:, at_pair] = value_grad[:first_query]
            value_grad = value_grad[first_query:]
        else:
            value_grad = value_grad + value_sum_ref[:, at_pair]
        put(2, pair, value_grad)
    for pair in range(columns // width):
        at_pair = slice(pair * width, (pair + 1) * width)
        queries = q_ref[first_query : first_query + count, at_pair]
        key_grad = jnp.dot(
            scores_ref[pair], one_above_other(queries, masks), preferred_element_type=jnp.float32
        )
        if upper:
            key_sum_ref[:, at_pair] = key_grad[:first_query]
            key_grad = key_grad[first_query:]
        else:
            key_grad = key_grad + key_sum_ref[:, at_pair]
        put(1, pair, key_grad)
        query_grad = [
            jnp.dot(
                kt_ref[pair * width + half * HEAD_DIM : pair * width + (half + 1) * HEAD_DIM, :keys],
                scores_ref[pair, :, half * count : (half + 1) * count],
                preferred_element_type=jnp.float32,
            )
            for half in range(2)
        ]
        put(0, pair, jnp.concatenate(query_grad, 0).astype(jnp.bfloat16).T)
    for step in range(replicas):
        place = place_of(info_ref, step, replicas)
        keep_ref[step] = grads_ref[place + parity]
        crossing = grads_ref[place + 1 - parity]
        part = crossing.shape[1] // len(send_refs)
        for at, send_ref in enumerate(send_refs):
            send_ref[step] = crossing[:, at * part : (at + 1) * part]


def norm_part_kernel(info_ref, keep_ref, w_ref, after_ref, out_ref):
    part = keep_ref[...].reshape(out_ref.shape[0], -1)
    out_ref[...] = jnp.dot(part, w_ref[...], preferred_element_type=jnp.float32)


def norm_kernel(upper, info_ref, keep_ref, normed_ref, rms_ref, incoming_ref, *refs):
    w_own_ref, w_other_ref = refs[:2]
    refs = refs[2:]
    got_refs = refs[: PIECES[upper]]
    out_refs = refs[len(got_refs) :]
    replicas, shard_rows, model_width = incoming_ref.shape
    rows = replicas * shard_rows
    got = [got_ref[...].reshape(rows, -1) for got_ref in got_refs]
    norm_grad = jnp.dot(
        jnp.concatenate(got, 1), w_other_ref[...], preferred_element_type=jnp.float32
    )
    if upper:
        norm_grad += keep_ref[...]
    else:
        norm_grad += jnp.dot(
            keep_ref[...].reshape(rows, -1), w_own_ref[...], preferred_element_type=jnp.float32
        )
    chunk = 1 if upper else 0
    normed = normed_ref[chunk].reshape(rows, model_width)
    inverse_rms = rms_ref[chunk].reshape(rows, -1)[:, :1]
    inner = jnp.mean(norm_grad * normed, axis=-1, keepdims=True)
    incoming = incoming_ref[...].reshape(rows, model_width).astype(jnp.float32)
    grad_in = incoming + inverse_rms * (norm_grad - normed * inner)
    grad_in = grad_in.astype(jnp.bfloat16).reshape(replicas, shard_rows, model_width)
    out_refs[-1][:, :, :model_width] = grad_in
    spare = out_refs[-1].shape[2] - model_width
    if spare:
        out_refs[-1][:, :, model_width:] = jnp.zeros((replicas, shard_rows, spare), jnp.bfloat16)


def in_terms(gt_ref, grad_refs, half, rows):
    count = grad_refs[0].shape[0] * grad_refs[0].shape[1]
    return sum(
        jnp.dot(
            gt_ref[2 * half * rows : 2 * (half + 1) * rows, chunk * count : (chunk + 1) * count],
            part_ref[...].reshape(count, -1),
            preferred_element_type=jnp.float32,
        )
        for chunk, part_ref in enumerate(grad_refs)
    )


def send_kernel(gt_ref, lower_ref, upper_ref, pass_ref, keep_ref):
    rows = pass_ref.shape[0]
    total = in_terms(gt_ref, (lower_ref, upper_ref), 1, rows)
    pass_ref[...] = total[:rows].astype(jnp.bfloat16)
    keep_ref[...] = total[rows:].astype(jnp.bfloat16)


def term_kernel(info_ref, gt_ref, *refs):
    grad_refs, at_refs, row_refs = refs[:2], refs[2:4], refs[4:6]
    pass_ref, keep_ref, out_pass_ref, out_keep_ref, out_send_ref = refs[7:]
    rows = pass_ref.shape[0]
    width = out_send_ref.shape[1]
    parity, x, y = info_ref[0], info_ref[1], info_ref[2]
    sent = jnp.where(parity == y, 2 * (1 - x) + 1 - parity, 2 * x + parity)
    blocks = (sent, 2 * x + 1 - parity, 2 * x + parity)
    total = jnp.zeros((3 * rows, width), jnp.float32)
    for at_ref, part_ref in zip(at_refs, row_refs):
        picked = [at_ref[pl.ds(pl.multiple_of(block * rows, 128), rows)] for block in blocks]
        total += jnp.dot(
            jnp.concatenate(picked, 0),
            part_ref[...].reshape(-1, width),
            preferred_element_type=jnp.float32,
        )
    out_send_ref[...] = total[:rows].astype(jnp.bfloat16)
    out_pass_ref[...] = total[rows : 2 * rows]
    out_keep_ref[...] = total[2 * rows :]
    total = in_terms(gt_ref, grad_refs, 0, rows)
    pass_ref[...] = total[:rows]
    keep_ref[...] = total[rows:]


def sum_kernel(own_ref, got_ref, out_own_ref, out_got_ref, after_ref, sum_ref):
    columns = own_ref.shape[1]
    sum_ref[:, :columns] = (own_ref[...] + got_ref[...].astype(jnp.float32)).astype(jnp.bfloat16)
    sum_ref[:, columns:] = (out_own_ref[...] + out_got_ref[...].astype(jnp.float32)).astype(
        jnp.bfloat16
    )


def pick_kernel(info_ref, upper_ref, lower_ref, out_ref):
    crossing = info_ref[0] == 0
    for step in range(2):
        for chunk, part_ref in enumerate((lower_ref, upper_ref)):
            wanted = info_ref[2] == (chunk if step == 1 else 1 - chunk)

            @pl.when(wanted & (crossing if step == 1 else jnp.logical_not(crossing)))
            def _():
                out_ref[...] = part_ref[step]


def join_kernel(info_ref, upper_ref, lower_ref, got_ref, out_ref):
    micro = info_ref[4]
    out_ref[0, 1 - micro] = got_ref[...]

    @pl.when(info_ref[2] == 1)
    def _():
        out_ref[0, micro] = upper_ref[0]

    @pl.when(info_ref[2] != 1)
    def _():
        out_ref[0, micro] = lower_ref[0]


def place_kernel(
    info_ref,
    own_ref,
    got_ref,
    out_own_ref,
    out_got_ref,
    sibling_ref,
    d_in_ref,
    d_out_ref,
    in_rows_ref,
    out_rows_ref,
    sems,
):
    columns = own_ref.shape[1] // 3
    owner = info_ref[0] == info_ref[2]
    copies = []
    for place in range(6):
        half = info_ref[0] if place < 3 else 1 - info_ref[0]
        block = place % 3
        at = slice(block * columns, (block + 1) * columns)
        if place < 3:
            in_rows_ref[place] = own_ref[:, at] + got_ref[:, at].astype(jnp.float32)
        else:
            in_rows_ref[place] = sibling_ref[:, at].astype(jnp.float32)
        first = pl.multiple_of((2 * block + half) * columns, 128)
        copy = pltpu.make_async_copy(
            in_rows_ref.at[place], d_in_ref.at[:, pl.ds(first, columns)], sems.at[place]
        )
        copy.start()
        copies.append(copy)

    @pl.when(owner)
    def _():
        out_rows_ref[...] = out_own_ref[...] + out_got_ref[...].astype(jnp.float32)

    @pl.when(jnp.logical_not(owner))
    def _():
        out_rows_ref[...] = sibling_ref[:, 3 * columns :].astype(jnp.float32)

    copy = pltpu.make_async_copy(out_rows_ref, d_out_ref, sems.at[6])
    copy.start()
    for started in [*copies, copy]:
        started.wait()


def call(kernel, outs, operands, scratch=(), flops=0, scalars=1, after=None, mebibytes=5, far=0, space=pltpu.VMEM):
    in_specs = [pl.BlockSpec(memory_space=pltpu.SMEM)] * scalars
    in_specs += [pl.BlockSpec(memory_space=pltpu.HBM)] * far
    in_specs += [pl.BlockSpec(memory_space=pltpu.VMEM)] * (len(operands) - scalars - far)
    if after is not None:
        operands = [*operands, after]
        in_specs.append(pl.BlockSpec(memory_space=pl.ANY))
    return pl.pallas_call(
        kernel,
        out_shape=list(outs),
        in_specs=in_specs,
        out_specs=[pl.BlockSpec(memory_space=space)] * len(outs),
        scratch_shapes=list(scratch),
        cost_estimate=pl.CostEstimate(flops=1, bytes_accessed=1, transcendentals=0),
        compiler_params=pltpu.CompilerParams(vmem_limit_bytes=mebibytes * 2**20),
    )(*operands)


def by_chips(acts, grad_top, w_in, w_out, offsets):
    half_type, full_type = jnp.bfloat16, jnp.float32
    shape = jax.ShapeDtypeStruct
    sections = lax.axis_size("section")
    shards = lax.axis_size("tm")
    levels = offsets.shape[1]
    half = shards // 2
    replicas = half // 2
    me = lax.axis_index("tm")
    parity = lax.rem(me, 2)
    side = lax.div(me, half)
    micro_count, shard_rows, model_width = acts.shape[1:]
    columns = model_width // 2
    heads = columns // HEAD_DIM
    seq = shards * shard_rows
    count = seq // 2
    w_qkv = w_in[0]
    w_rows = w_out[0]
    beside = lax.div(lax.rem(me, half), 2)
    micro = lax.rem(side + beside, 2)
    info = jnp.stack([parity, beside, side, lax.axis_index("section"), micro])
    info = jnp.concatenate([info.astype(jnp.int32), offsets[0]])

    def swapped(value, bits, chosen=None):
        pairs = [(device, device ^ bits) for device in range(shards)]
        pairs = [pair for pair in pairs if chosen is None or chosen(pair[0])]
        return lax.ppermute(value, "tm", pairs)

    core, near, far = 1, 2, half

    packed = shape((shard_rows, model_width + 128), half_type)
    top_shape = shape((shard_rows, model_width), half_type)
    own_acts, other_acts, own_top, other_top = call(
        functools.partial(pack_kernel, levels),
        [packed, packed, top_shape, top_shape],
        [info, acts[0], grad_top],
    )
    weights = [
        call(
            functools.partial(turn_kernel, own),
            [shape((3 * columns, model_width), half_type)],
            [info, w_qkv],
            after=own_acts,
        )[0]
        for own in (True, False)
    ]
    pieces = [own_acts, swapped(other_acts, near), swapped(other_acts, far)]
    pieces += [swapped(own_acts, near + far)]
    tops = [own_top, swapped(other_top, near), swapped(other_top, far)]
    pieces[-1], tops, weights = lax.optimization_barrier((pieces[-1], tops, weights))
    tops += [swapped(own_top, near + far)]
    pieces += [swapped(piece, core) for piece in pieces]

    rows_shape = shape((seq, columns), half_type)
    normed, rms, norm, flag_rows, queries, keys, values, keys_t = call(
        functools.partial(project_kernel, replicas),
        [
            shape((2, replicas, shard_rows, model_width), full_type),
            shape((2, replicas, shard_rows, 128), full_type),
            shape((seq, model_width), half_type),
            shape((128, seq), full_type),
            rows_shape,
            rows_shape,
            rows_shape,
            shape((columns, seq), half_type),
        ],
        [info, *pieces, w_qkv],
        scratch=[pltpu.VMEM((shards, *packed.shape), half_type)],
        flops=6 * seq * model_width * columns,
        after=weights[1],
    )
    pairs = heads // 2
    upper_prob, upper_at = call(
        functools.partial(upper_forward_kernel, levels, shard_rows),
        [
            shape((pairs, seq, 2 * count), half_type),
            shape((columns, count), half_type),
        ],
        [flag_rows, queries, keys, values],
        scalars=0,
        flops=4 * columns * seq * count,
    )
    tops, upper_at = lax.optimization_barrier((tuple(tops), upper_at))
    tops = [*tops, *[swapped(piece, core) for piece in tops]]
    own_rows = model_width // shards
    probs, attended = {True: upper_prob}, {True: upper_at}
    got, kept = {}, {}
    piece_shape = shape((replicas, shard_rows, model_width), half_type)
    wide_shape = shape((replicas, shard_rows, model_width + 128), half_type)
    grads_shape = shape((replicas, shard_rows, 3 * columns), half_type)
    sum_shape = shape((count, columns), full_type)
    full_grads = shape((half, shard_rows, 3 * columns), half_type)
    full_rows = shape((half, shard_rows, model_width), half_type)
    term_shape = (own_rows, 3 * columns)
    rows_scratch = pltpu.VMEM(full_rows.shape, half_type)
    grads_scratch = pltpu.VMEM(full_grads.shape, half_type)
    result, full, ordered = {}, {}, {}
    for turn in range(sections):
        last = turn + 1 == sections
        fresh_section = sections - 1 - turn
        sums, parts, crossed = [], {}, {}

        def norm_step(upper, after):
            (result[upper],) = call(
                functools.partial(norm_kernel, upper),
                [wide_shape if turn + 2 == sections and not upper else piece_shape],
                [info, parts[upper], normed, rms, kept[upper][0], *weights, *crossed[upper]],
                after=after,
            )
            if not last:
                hop = [(sections - 1 - turn, sections - 2 - turn)]
                got[upper] = lax.ppermute(result[upper], "section", hop)

        for upper in (True, False):
            rows_in, after = tops, keys_t if upper else result.get(True)
            if turn:
                tied = parts if last else result
                before = result[False] if upper else tied[True]
                got[upper], after = lax.optimization_barrier((got[upper], before))
                if not upper:
                    tied[True] = after
                if last and not upper:
                    after, result[True] = lax.optimization_barrier((after, result[True]))
                rows_in = [got[upper], swapped(got[upper], core), *kept[upper]]
            part = 3 * columns // PIECES[upper]
            cross = [shape((replicas, shard_rows, part), half_type)] * PIECES[upper]
            outs = [piece_shape] * (1 if last else 2) + [grads_shape, *cross]
            outs += [sum_shape, sum_shape] if upper else []
            scratch = []
            if last:
                outs += [full_grads]
            else:
                scratch += [grads_scratch]
            if last:
                outs += [full_rows]
            else:
                scratch += [rows_scratch]
            part_keys = seq if upper else count
            scratch += [pltpu.VMEM((pairs, part_keys, 2 * count), half_type)]
            if last:
                scratch += [pltpu.VMEM(piece_shape.shape, half_type)]
            answer = call(
                functools.partial(
                    backward_kernel, upper, 0 if turn else len(tops), last, fresh_section
                ),
                outs,
                [info, *rows_in, w_rows, probs[upper], queries, values, keys_t]
                + [attended[upper], *sums],
                scratch=scratch,
                flops=2 * count * columns * (2 * model_width + 4 * part_keys),
                after=after,
            )
            kept[upper] = tuple(answer[:2])
            answer = answer[1 if last else 2 :]
            keep = answer[0]
            send = answer[1 : 1 + len(cross)]
            parts[upper] = keep
            if upper:
                sums = answer[1 + len(cross) : 3 + len(cross)]
                (parts[True],) = call(
                    norm_part_kernel,
                    [shape((replicas * shard_rows, model_width), full_type)],
                    [info, keep, weights[0]],
                    flops=3 * replicas * shard_rows * model_width * model_width,
                    after=keep,
                )
                if turn == 0:
                    lower_prob, lower_at, norm_t = call(
                        functools.partial(lower_forward_kernel, levels, shard_rows),
                        [
                            shape((pairs, count, 2 * count), half_type),
                            shape((columns, count), half_type),
                            shape((4 * own_rows, seq), half_type),
                        ],
                        [info, norm, flag_rows, queries, keys, values],
                        flops=4 * columns * count * count,
                        after=parts[True],
                    )
                    probs[False], attended[False] = lower_prob, lower_at
            if last:
                full[upper], ordered[upper] = answer[-2:]
            crossed[upper] = [swapped(piece, core) for piece in send]
            if upper:
                norm_step(True, keep)
        if last:
            send_pass, send_keep = call(
                send_kernel,
                [shape(term_shape, half_type)] * 2,
                [norm_t, full[False], full[True]],
                scalars=0,
            )
            terms = call(
                term_kernel,
                [shape(term_shape, full_type)] * 2
                + [shape((own_rows, model_width), full_type)] * 2
                + [shape((own_rows, model_width), half_type)],
                [info, norm_t, full[False], full[True], attended[False], attended[True]]
                + [ordered[False], ordered[True]],
                after=send_keep,
            )
        norm_step(False, terms[4] if last else result[True])

    in_pass, in_keep, out_pass, out_keep, out_send = terms
    got_pass = swapped(send_pass, near)
    got_keep = swapped(send_keep, far)
    own_rows_grad = [result[True], result[False]]
    (theirs,) = call(pick_kernel, [top_shape], [info, *own_rows_grad])
    to_owner = [(device, device ^ (far if device % 2 else near)) for device in range(shards)]
    partner = lax.ppermute(theirs, "tm", to_owner)
    got_out_pass = swapped(out_send, near, lambda device: device // half == device % 2)
    got_out_keep = swapped(out_send, far, lambda device: device // half != device % 2)
    _, _, done = lax.optimization_barrier((got_keep, got_out_keep, partner))
    (summed,) = call(
        sum_kernel,
        [shape((own_rows, 3 * columns + model_width), half_type)],
        [in_pass, got_pass, out_pass, got_out_pass],
        scalars=0,
        after=done,
    )
    d_w_in, d_w_out = call(
        place_kernel,
        [
            shape((own_rows, 3 * model_width), full_type),
            shape((own_rows, model_width), full_type),
        ],
        [info, in_keep, got_keep, out_keep, got_out_keep, swapped(summed, core)],
        scratch=[
            pltpu.VMEM((6, own_rows, columns), full_type),
            pltpu.VMEM((own_rows, model_width), full_type),
            pltpu.SemaphoreType.DMA((7,)),
        ],
        space=pltpu.HBM,
    )
    (d_acts,) = call(
        join_kernel, [shape(acts.shape, half_type)], [info, *own_rows_grad, partner]
    )
    return (d_acts, d_w_in[None], d_w_out[None])


def layer_gradients(acts, grad_top, w_in, w_out, offsets):
    shards = lax.axis_size("tm")
    micro_count, shard_rows, model_width = acts.shape[1:]
    heads = model_width // HEAD_DIM
    prob_bytes = 2 * heads * (shards * shard_rows) ** 2
    fits = prob_bytes <= 2**24 and model_width % (128 * shards) == 0 and shard_rows % 16 == 0
    square = shards % 4 == 0 and shards // 4 == 2
    if micro_count == 2 and square and heads % 4 == 0 and fits:
        return by_chips(acts, grad_top, w_in, w_out, offsets)
    return per_device(acts, grad_top, w_in, w_out, offsets)


def solution(mesh):
    placed = (
        P("section", None, "tm", None),
        P(None, "tm", None),
        P("section", None, None),
        P("section", None, None),
        P("tm", None),
    )
    return jax.shard_map(
        layer_gradients,
        mesh=mesh,
        in_specs=placed,
        out_specs=(
            P("section", None, "tm", None),
            P("section", "tm", None),
            P("section", "tm", None),
        ),
        check_vma=False,
    )
```

```python
import functools
import jax
import jax.numpy as jnp
from jax import lax
from jax.experimental import pallas as pl
from jax.experimental.pallas import tpu as pltpu
from jax.sharding import PartitionSpec as P

HEAD_DIM = 64


epsilon = 1e-06
PIECES = {True: 2, False: 2}
negative_fill = -1e30


def shifted(value, axis, steps):
    count = lax.axis_size(axis)
    initial, last = (max(0, -steps), min(count, count - steps))
    return lax.ppermute(value, axis, [(source, source + steps) for source in range(initial, last)])


def normalize(inputs):
    values = inputs.astype(jnp.float32)
    inverse_rms = lax.rsqrt(jnp.mean(values * values, axis=-1, keepdims=True) + epsilon)
    return (values * inverse_rms, inverse_rms)


def key_bias(level_flags, shard_rows):
    position = jnp.arange(shard_rows)
    own_part = position[None, :] <= position[:, None]
    far_part = jnp.repeat(level_flags != 0, shard_rows)
    far_part = jnp.broadcast_to(far_part[None, :], (shard_rows, far_part.shape[0]))
    return jnp.concatenate([own_part, far_part], 1)


def split_heads(row_block):
    return row_block.reshape(row_block.shape[0], -1, HEAD_DIM)


def softmax_keys(queries, key_heads, allowed):
    scores = jnp.einsum(
        "ihd,jhd->hij", queries, key_heads, preferred_element_type=jnp.float32
    ) * HEAD_DIM ** (-0.5)
    scores = jnp.where(allowed[None], scores, negative_fill)
    highest = jnp.max(scores, axis=-1, keepdims=True)
    shifted_exp = jnp.where(allowed[None], jnp.exp(scores - highest), 0.0)
    return shifted_exp / jnp.sum(shifted_exp, axis=-1, keepdims=True)


def attend(query_rows, key_rows, allowed):
    model_width = query_rows.shape[1]
    probability = softmax_keys(
        split_heads(query_rows), split_heads(key_rows[:, :model_width]), allowed
    )
    attended = jnp.einsum(
        "hij,jhd->ihd",
        probability.astype(jnp.bfloat16),
        split_heads(key_rows[:, model_width:]),
        preferred_element_type=jnp.float32,
    )
    return attended.reshape(query_rows.shape).astype(jnp.bfloat16)


def attend_back(query_rows, key_rows, allowed, incoming, attended, w_proj):
    model_width = query_rows.shape[1]
    queries = split_heads(query_rows)
    key_heads = split_heads(key_rows[:, :model_width])
    value_heads = split_heads(key_rows[:, model_width:])
    probability = softmax_keys(queries, key_heads, allowed)
    rounded = probability.astype(jnp.bfloat16)
    upstream = lax.dot_general(
        incoming, w_proj, (((1,), (1,)), ((), ())), preferred_element_type=jnp.float32
    ).astype(jnp.bfloat16)
    up_heads = split_heads(upstream)
    delta = jnp.einsum(
        "ihd,ihd->hi", up_heads.astype(jnp.float32), split_heads(attended).astype(jnp.float32)
    )[..., None]
    prob_grad = jnp.einsum(
        "ihd,jhd->hij", up_heads, value_heads, preferred_element_type=jnp.float32
    )
    score_grad = (probability * (prob_grad - delta)).astype(jnp.bfloat16)
    scale_factor = HEAD_DIM ** (-0.5)
    query_grad = (
        jnp.einsum("hij,jhd->ihd", score_grad, key_heads, preferred_element_type=jnp.float32)
        * scale_factor
    )
    key_grad = (
        jnp.einsum("hij,ihd->jhd", score_grad, queries, preferred_element_type=jnp.float32)
        * scale_factor
    )
    value_grad = jnp.einsum("hij,ihd->jhd", rounded, up_heads, preferred_element_type=jnp.float32)
    return (
        query_grad.reshape(-1, model_width),
        key_grad.reshape(-1, model_width),
        value_grad.reshape(-1, model_width),
    )


def per_device(acts, grad_top, w_in, w_out, offsets):
    sections = lax.axis_size("section")
    shards = lax.axis_size("tm")
    levels = shards.bit_length() - 1
    section_index = lax.axis_index("section")
    micro_count = acts.shape[1]
    shard_rows = acts.shape[2]
    model_width = acts.shape[3]
    w_qkv = w_in[0]
    w_proj = w_out[0]
    level_flags = offsets[0]
    normed, inverse_rms = normalize(acts[0])
    rounded_norm = normed.astype(jnp.bfloat16)
    qkv = jnp.dot(rounded_norm.reshape(-1, model_width), w_qkv, preferred_element_type=jnp.float32)
    qkv = qkv.astype(jnp.bfloat16).reshape(micro_count, shard_rows, 3 * model_width)
    pairs = qkv[..., model_width:]
    far_list = [shifted(pairs, "tm", 2**level) for level in range(levels)]
    key_rows = jnp.concatenate([pairs] + far_list, 1)
    allowed = key_bias(level_flags, shard_rows)
    attended = jnp.stack(
        [
            attend(qkv[index, :, :model_width], key_rows[index], allowed)
            for index in range(micro_count)
        ],
        0,
    )

    def attention_part(incoming, slot):
        query_rows = lax.dynamic_index_in_dim(qkv, slot, 0, False)[:, :model_width]
        slot_keys = lax.dynamic_index_in_dim(key_rows, slot, 0, False)
        slot_attended = lax.dynamic_index_in_dim(attended, slot, 0, False)
        query_grad, key_grad, value_grad = attend_back(
            query_rows, slot_keys, allowed, incoming, slot_attended, w_proj
        )
        owner_sum = jnp.concatenate([key_grad[:shard_rows], value_grad[:shard_rows]], 1)
        far_part = jnp.concatenate([key_grad[shard_rows:], value_grad[shard_rows:]], 1)
        far_part = far_part.astype(jnp.bfloat16).reshape(levels, shard_rows, 2 * model_width)
        return (query_grad, owner_sum, far_part)

    def empty_attention(incoming, slot):
        return (
            jnp.zeros((shard_rows, model_width), jnp.float32),
            jnp.zeros((shard_rows, 2 * model_width), jnp.float32),
            jnp.zeros((levels, shard_rows, 2 * model_width), jnp.bfloat16),
        )

    def norm_part(qkv_grad, incoming, slot):
        norm_grad = lax.dot_general(
            qkv_grad, w_qkv, (((1,), (1,)), ((), ())), preferred_element_type=jnp.float32
        )
        slot_normed = lax.dynamic_index_in_dim(normed, slot, 0, False)
        slot_rms = lax.dynamic_index_in_dim(inverse_rms, slot, 0, False)
        inner = jnp.mean(norm_grad * slot_normed, axis=-1, keepdims=True)
        return (incoming.astype(jnp.float32) + slot_rms * (norm_grad - slot_normed * inner)).astype(
            jnp.bfloat16
        )

    def empty_norm(qkv_grad, incoming, slot):
        return jnp.zeros((shard_rows, model_width), jnp.bfloat16)

    def step(turn, carry):
        received, grad_store, qkv_store, incoming_store = carry
        slot_raw = turn - (sections - 1 - section_index)
        active = (slot_raw >= 0) & (slot_raw < micro_count)
        slot = jnp.clip(slot_raw, 0, micro_count - 1)
        incoming = jnp.where(
            section_index == sections - 1,
            lax.dynamic_index_in_dim(grad_top, slot, 0, False),
            received,
        )
        query_grad, owner_sum, far_part = lax.cond(
            active, attention_part, empty_attention, incoming, slot
        )
        for level in range(levels):
            owner_sum = owner_sum + shifted(far_part[level], "tm", -(2**level)).astype(jnp.float32)
        qkv_grad = jnp.concatenate([query_grad, owner_sum], 1).astype(jnp.bfloat16)
        grad_in = lax.cond(active, norm_part, empty_norm, qkv_grad, incoming, slot)
        sent_down = shifted(grad_in, "section", -1)
        grad_store = jnp.where(
            active, lax.dynamic_update_index_in_dim(grad_store, grad_in, slot, 0), grad_store
        )
        qkv_store = jnp.where(
            active, lax.dynamic_update_index_in_dim(qkv_store, qkv_grad, slot, 0), qkv_store
        )
        incoming_store = jnp.where(
            active,
            lax.dynamic_update_index_in_dim(incoming_store, incoming, slot, 0),
            incoming_store,
        )
        return (sent_down, grad_store, qkv_store, incoming_store)

    initial = (
        jnp.zeros((shard_rows, model_width), jnp.bfloat16),
        jnp.zeros((micro_count, shard_rows, model_width), jnp.bfloat16),
        jnp.zeros((micro_count, shard_rows, 3 * model_width), jnp.bfloat16),
        jnp.zeros((micro_count, shard_rows, model_width), jnp.bfloat16),
    )
    received, grad_store, qkv_store, incoming_store = lax.fori_loop(
        0, sections + micro_count - 1, step, initial
    )
    flat_norm = rounded_norm.reshape(-1, model_width)
    flat_attended = attended.reshape(-1, model_width)
    flat_qkv = qkv_store.reshape(-1, 3 * model_width)
    flat_incoming = incoming_store.reshape(-1, model_width)
    contract = (((0,), (0,)), ((), ()))
    first = lax.dot_general(flat_norm, flat_qkv, contract, preferred_element_type=jnp.float32)
    second = lax.dot_general(
        flat_attended, flat_incoming, contract, preferred_element_type=jnp.float32
    )
    summed = lax.psum_scatter(
        jnp.concatenate([first, second], 1).astype(jnp.bfloat16),
        "tm",
        scatter_dimension=0,
        tiled=True,
    ).astype(jnp.float32)
    return (
        grad_store[None],
        summed[None, :, : 3 * model_width],
        summed[None, :, 3 * model_width :],
    )


def side_by_side(transposed, pair):
    width = 2 * HEAD_DIM
    rows = transposed[pair * width : (pair + 1) * width]
    empty = jnp.zeros((HEAD_DIM, rows.shape[1]), rows.dtype)
    return jnp.concatenate(
        [
            jnp.concatenate([rows[:HEAD_DIM], empty], 0),
            jnp.concatenate([empty, rows[HEAD_DIM:]], 0),
        ],
        1,
    )


def one_above_other(rows, masks):
    return jnp.concatenate([rows * masks[0], rows * masks[1]], 0)


def head_masks():
    lane = lax.broadcasted_iota(jnp.int32, (1, 2 * HEAD_DIM), 1)
    return [
        jnp.where(lane < HEAD_DIM, 1.0, 0.0).astype(jnp.bfloat16),
        jnp.where(lane < HEAD_DIM, 0.0, 1.0).astype(jnp.bfloat16),
    ]


def key_bias_rows(flag_rows, levels, shard_rows, keys, first_query, count):
    key_at = lax.broadcasted_iota(jnp.int32, (keys, count), 0)
    query_at = lax.broadcasted_iota(jnp.int32, (keys, count), 1) + first_query
    gap = lax.div(query_at, shard_rows) - lax.div(key_at, shard_rows)
    allowed = (gap == 0) & (key_at <= query_at)
    for level in range(levels):
        allowed = allowed | ((gap == 2**level) & (flag_rows[level : level + 1] != 0))
    return jnp.where(allowed, 0.0, negative_fill)


def softmax_pass(queries, keys, values, bias, prob_ref, at_ref):
    queries_t = queries.T
    values_t = values.T
    width = 2 * HEAD_DIM
    count = queries.shape[0]
    for pair in range(queries.shape[1] // width):
        at_pair = slice(pair * width, (pair + 1) * width)
        scores = jnp.dot(
            keys[:, at_pair], side_by_side(queries_t, pair), preferred_element_type=jnp.float32
        )
        for half in range(2):
            at_half = slice(half * count, (half + 1) * count)
            biased = scores[:, at_half] + bias
            shifted_exp = jnp.exp(biased - jnp.max(biased, axis=0, keepdims=True))
            probability = shifted_exp * (1.0 / jnp.sum(shifted_exp, axis=0, keepdims=True))
            prob_ref[pair, :, at_half] = probability.astype(jnp.bfloat16)
    for head in range(queries.shape[1] // HEAD_DIM):
        at = slice(head * HEAD_DIM, (head + 1) * HEAD_DIM)
        at_half = slice(head % 2 * count, (head % 2 + 1) * count)
        at_ref[at] = jnp.dot(
            values_t[at], prob_ref[head // 2, :, at_half], preferred_element_type=jnp.float32
        ).astype(jnp.bfloat16)


def pack_kernel(
    levels, info_ref, acts_ref, top_ref, own_ref, other_ref, own_top_ref, other_top_ref
):
    model_width = acts_ref.shape[2]
    shard_rows = own_ref.shape[0]
    micro = info_ref[4]
    lane = lax.broadcasted_iota(jnp.int32, (shard_rows, own_ref.shape[1] - model_width), 1)
    flags = jnp.zeros(lane.shape, jnp.float32)
    for level in range(levels):
        seen = jnp.where(info_ref[5 + level] != 0, 1.0, 0.0)
        flags = jnp.where(lane == level, seen, flags)
    for at, out_ref, out_top_ref in (
        (micro, own_ref, own_top_ref),
        (1 - micro, other_ref, other_top_ref),
    ):
        out_ref[:, :model_width] = acts_ref[at]
        out_ref[:, model_width:] = flags.astype(jnp.bfloat16)
        out_top_ref[...] = top_ref[at]


def turn_kernel(own, info_ref, w_ref, after_ref, out_ref):
    columns = out_ref.shape[0] // 3
    model_width = w_ref.shape[0]
    half = info_ref[0] if own else 1 - info_ref[0]
    for block in range(3):
        first = pl.multiple_of(block * model_width + half * columns, 128)
        out_ref[block * columns : (block + 1) * columns] = w_ref[:, pl.ds(first, columns)].T


def project_kernel(replicas, info_ref, *refs):
    pieces = refs[: 4 * replicas]
    w_ref, _, normed_ref, rms_ref, norm_ref, flag_ref, q_ref, k_ref, v_ref, kt_ref, packed_ref = refs[
        4 * replicas :
    ]
    shards, shard_rows = packed_ref.shape[:2]
    model_width = w_ref.shape[0]
    seq = shards * shard_rows
    columns = q_ref.shape[1]
    at_piece = 0
    for core in (info_ref[0], 1 - info_ref[0]):
        for side in (info_ref[2], 1 - info_ref[2]):
            for step in range(replicas):
                shard = side * (shards // 2) + place_of(info_ref, step, replicas) + core
                packed_ref[shard] = pieces[at_piece][...]
                at_piece += 1
    for chunk in range(2):
        for step in range(replicas):
            shard = chunk * (shards // 2) + place_of(info_ref, step, replicas) + info_ref[0]
            normed, inverse_rms = normalize(packed_ref[shard][:, :model_width])
            normed_ref[chunk, step] = normed
            rms_ref[chunk, step] = jnp.broadcast_to(inverse_rms, rms_ref.shape[2:])
    normed, _ = normalize(packed_ref[:, :, :model_width].reshape(seq, model_width))
    rounded = normed.astype(jnp.bfloat16)
    norm_ref[...] = rounded
    flag_ref[...] = packed_ref[:, :, model_width:].reshape(seq, -1).astype(jnp.float32).T
    scale_factor = HEAD_DIM ** (-0.5)
    for block, out_ref in enumerate((q_ref, k_ref, v_ref)):
        first = pl.multiple_of(block * model_width + info_ref[0] * columns, 128)
        product = jnp.dot(
            rounded, w_ref[:, pl.ds(first, columns)], preferred_element_type=jnp.float32
        ).astype(jnp.bfloat16)
        out_ref[...] = product * scale_factor if block == 0 else product
    kt_ref[...] = (k_ref[...] * scale_factor).T


def upper_forward_kernel(
    levels, shard_rows, flag_ref, q_ref, k_ref, v_ref, prob_ref, at_ref
):
    seq = q_ref.shape[0]
    count = seq // 2
    bias = key_bias_rows(flag_ref[:, count:], levels, shard_rows, seq, count, count)
    softmax_pass(q_ref[count:], k_ref[...], v_ref[...], bias, prob_ref, at_ref)


def lower_forward_kernel(
    levels,
    shard_rows,
    info_ref,
    norm_ref,
    flag_ref,
    q_ref,
    k_ref,
    v_ref,
    after_ref,
    prob_ref,
    at_ref,
    gt_ref,
):
    seq = norm_ref.shape[0]
    count = seq // 2
    bias = key_bias_rows(flag_ref[:, :count], levels, shard_rows, count, 0, count)
    softmax_pass(q_ref[:count], k_ref[:count], v_ref[:count], bias, prob_ref, at_ref)
    rows = gt_ref.shape[0] // 4
    parity, x, y = info_ref[0], info_ref[1], info_ref[2]
    half = norm_ref.shape[1] // rows // 2
    for place, block in enumerate(
        (
            half * y + 2 * x + 1 - parity,
            half * y + 2 * x + parity,
            half * y + 2 * (1 - x) + 1 - parity,
            half * (1 - y) + 2 * x + parity,
        )
    ):
        first = pl.multiple_of(block * rows, 128)
        gt_ref[place * rows : (place + 1) * rows] = norm_ref[:, pl.ds(first, rows)].T


def place_of(info_ref, step, replicas):
    return 2 * lax.rem(info_ref[1] - step + replicas, replicas)


def merge_rows(info_ref, fresh, got_refs, kept_refs, out_refs, rows_ref):
    @pl.when(fresh)
    def _():
        for core, out_ref in enumerate(out_refs):
            out_ref[...] = got_refs[core][:, :, : out_ref.shape[2]]

    @pl.when(jnp.logical_not(fresh))
    def _():
        for out_ref, kept_ref in zip(out_refs, kept_refs):
            out_ref[...] = kept_ref[...]

    place_rows(info_ref, out_refs, rows_ref)


def place_rows(info_ref, out_refs, rows_ref):
    replicas = out_refs[0].shape[0]
    for step in range(replicas):
        place = place_of(info_ref, step, replicas)
        rows_ref[place + info_ref[0]] = out_refs[0][step]
        rows_ref[place + 1 - info_ref[0]] = out_refs[1][step]


def merge_tops(info_ref, upper, piece_refs, out_refs, rows_ref):
    replicas = out_refs[0].shape[0]
    own_chunk = info_ref[2] == (1 if upper else 0)
    for core in range(2):
        refs = piece_refs[2 * replicas * core : 2 * replicas * (core + 1)]

        @pl.when(own_chunk)
        def _():
            for step in range(replicas):
                out_refs[core][step] = refs[step][...]

        @pl.when(jnp.logical_not(own_chunk))
        def _():
            for step in range(replicas):
                out_refs[core][step] = refs[replicas + step][...]

    place_rows(info_ref, out_refs, rows_ref)


def backward_kernel(upper, tops, last, fresh_section, info_ref, *refs):
    refs = list(refs)
    got = tops or 4
    got_refs = refs[:got]
    w_ref, prob_ref, q_ref, v_ref, kt_ref, at_ref = refs[got : got + 6]
    refs = refs[got + 6 :]
    if not upper:
        key_sum_ref, value_sum_ref = refs[:2]
        refs = refs[2:]
    refs = refs[1:]
    if last:
        refs = [refs[0], refs[-1], *refs[1:-1]]
    own_ref, other_ref, keep_ref = refs[:3]
    send_refs = refs[3 : 3 + PIECES[upper]]
    refs = refs[3 + len(send_refs) :]
    if upper:
        key_sum_ref, value_sum_ref = refs[:2]
        refs = refs[2:]
    grads_ref, rows_ref, scores_ref = refs
    replicas, shard_rows, model_width = own_ref.shape
    count = rows_ref.shape[0] * shard_rows
    keys = prob_ref.shape[1]
    parity = info_ref[0]
    columns = q_ref.shape[1]
    width = 2 * HEAD_DIM
    if tops:
        merge_tops(info_ref, upper, got_refs, (own_ref, other_ref), rows_ref)
    else:
        fresh = info_ref[3] == fresh_section
        merge_rows(info_ref, fresh, got_refs[:-2], got_refs[-2:], (own_ref, other_ref), rows_ref)
    rows = rows_ref[...].reshape(count, model_width)
    weights = w_ref[pl.ds(pl.multiple_of(parity * columns, 128), columns), :]
    over_width = (((1,), (1,)), ((), ()))
    upstream = lax.dot_general(
        rows, weights, over_width, preferred_element_type=jnp.float32
    ).astype(jnp.bfloat16)
    upstream_t = upstream.T
    product_t = upstream_t.astype(jnp.float32) * at_ref[...].astype(jnp.float32)
    first_query = keys - count
    masks = head_masks()

    def put(block, pair, part):
        first = block * columns + pair * width
        grads_ref[:, :, first : first + width] = part.astype(jnp.bfloat16).reshape(
            -1, shard_rows, width
        )

    for pair in range(columns // width):
        at_pair = slice(pair * width, (pair + 1) * width)
        prob_grad = jnp.dot(
            v_ref[:keys, at_pair], side_by_side(upstream_t, pair), preferred_element_type=jnp.float32
        )
        for half in range(2):
            at_half = slice(half * count, (half + 1) * count)
            first = pair * width + half * HEAD_DIM
            delta = jnp.sum(product_t[first : first + HEAD_DIM], axis=0, keepdims=True)
            scores_ref[pair, :, at_half] = (
                prob_ref[pair, :, at_half].astype(jnp.float32) * (prob_grad[:, at_half] - delta)
            ).astype(jnp.bfloat16)
        value_grad = jnp.dot(
            prob_ref[pair],
            one_above_other(upstream[:, at_pair], masks),
            preferred_element_type=jnp.float32,
        )
        if upper:
            value_sum_ref[:, at_pair] = value_grad[:first_query]
            value_grad = value_grad[first_query:]
        else:
            value_grad = value_grad + value_sum_ref[:, at_pair]
        put(2, pair, value_grad)
    for pair in range(columns // width):
        at_pair = slice(pair * width, (pair + 1) * width)
        queries = q_ref[first_query : first_query + count, at_pair]
        key_grad = jnp.dot(
            scores_ref[pair], one_above_other(queries, masks), preferred_element_type=jnp.float32
        )
        if upper:
            key_sum_ref[:, at_pair] = key_grad[:first_query]
            key_grad = key_grad[first_query:]
        else:
            key_grad = key_grad + key_sum_ref[:, at_pair]
        put(1, pair, key_grad)
        query_grad = [
            jnp.dot(
                kt_ref[pair * width + half * HEAD_DIM : pair * width + (half + 1) * HEAD_DIM, :keys],
                scores_ref[pair, :, half * count : (half + 1) * count],
                preferred_element_type=jnp.float32,
            )
            for half in range(2)
        ]
        put(0, pair, jnp.concatenate(query_grad, 0).astype(jnp.bfloat16).T)
    for step in range(replicas):
        place = place_of(info_ref, step, replicas)
        keep_ref[step] = grads_ref[place + parity]
        crossing = grads_ref[place + 1 - parity]
        part = crossing.shape[1] // len(send_refs)
        for at, send_ref in enumerate(send_refs):
            send_ref[step] = crossing[:, at * part : (at + 1) * part]


def norm_part_kernel(info_ref, keep_ref, w_ref, after_ref, out_ref):
    part = keep_ref[...].reshape(out_ref.shape[0], -1)
    out_ref[...] = jnp.dot(part, w_ref[...], preferred_element_type=jnp.float32)


def norm_kernel(upper, info_ref, keep_ref, normed_ref, rms_ref, incoming_ref, *refs):
    w_own_ref, w_other_ref = refs[:2]
    refs = refs[2:]
    got_refs = refs[: PIECES[upper]]
    out_refs = refs[len(got_refs) :]
    replicas, shard_rows, model_width = incoming_ref.shape
    rows = replicas * shard_rows
    got = [got_ref[...].reshape(rows, -1) for got_ref in got_refs]
    norm_grad = jnp.dot(
        jnp.concatenate(got, 1), w_other_ref[...], preferred_element_type=jnp.float32
    )
    if upper:
        norm_grad += keep_ref[...]
    else:
        norm_grad += jnp.dot(
            keep_ref[...].reshape(rows, -1), w_own_ref[...], preferred_element_type=jnp.float32
        )
    chunk = 1 if upper else 0
    normed = normed_ref[chunk].reshape(rows, model_width)
    inverse_rms = rms_ref[chunk].reshape(rows, -1)[:, :1]
    inner = jnp.mean(norm_grad * normed, axis=-1, keepdims=True)
    incoming = incoming_ref[...].reshape(rows, model_width).astype(jnp.float32)
    grad_in = incoming + inverse_rms * (norm_grad - normed * inner)
    grad_in = grad_in.astype(jnp.bfloat16).reshape(replicas, shard_rows, model_width)
    out_refs[-1][:, :, :model_width] = grad_in
    spare = out_refs[-1].shape[2] - model_width
    if spare:
        out_refs[-1][:, :, model_width:] = jnp.zeros((replicas, shard_rows, spare), jnp.bfloat16)


def in_terms(gt_ref, grad_refs, half, rows):
    count = grad_refs[0].shape[0] * grad_refs[0].shape[1]
    return sum(
        jnp.dot(
            gt_ref[2 * half * rows : 2 * (half + 1) * rows, chunk * count : (chunk + 1) * count],
            part_ref[...].reshape(count, -1),
            preferred_element_type=jnp.float32,
        )
        for chunk, part_ref in enumerate(grad_refs)
    )


def send_kernel(gt_ref, lower_ref, upper_ref, pass_ref, keep_ref):
    rows = pass_ref.shape[0]
    total = in_terms(gt_ref, (lower_ref, upper_ref), 1, rows)
    pass_ref[...] = total[:rows].astype(jnp.bfloat16)
    keep_ref[...] = total[rows:].astype(jnp.bfloat16)


def term_kernel(info_ref, gt_ref, *refs):
    grad_refs, at_refs, row_refs = refs[:2], refs[2:4], refs[4:6]
    pass_ref, keep_ref, out_pass_ref, out_keep_ref, out_send_ref = refs[7:]
    rows = pass_ref.shape[0]
    width = out_send_ref.shape[1]
    parity, x, y = info_ref[0], info_ref[1], info_ref[2]
    sent = jnp.where(parity == y, 2 * (1 - x) + 1 - parity, 2 * x + parity)
    blocks = (sent, 2 * x + 1 - parity, 2 * x + parity)
    total = jnp.zeros((3 * rows, width), jnp.float32)
    for at_ref, part_ref in zip(at_refs, row_refs):
        picked = [at_ref[pl.ds(pl.multiple_of(block * rows, 128), rows)] for block in blocks]
        total += jnp.dot(
            jnp.concatenate(picked, 0),
            part_ref[...].reshape(-1, width),
            preferred_element_type=jnp.float32,
        )
    out_send_ref[...] = total[:rows].astype(jnp.bfloat16)
    out_pass_ref[...] = total[rows : 2 * rows]
    out_keep_ref[...] = total[2 * rows :]
    total = in_terms(gt_ref, grad_refs, 0, rows)
    pass_ref[...] = total[:rows]
    keep_ref[...] = total[rows:]


def sum_kernel(own_ref, got_ref, out_own_ref, out_got_ref, after_ref, sum_ref):
    columns = own_ref.shape[1]
    sum_ref[:, :columns] = (own_ref[...] + got_ref[...].astype(jnp.float32)).astype(jnp.bfloat16)
    sum_ref[:, columns:] = (out_own_ref[...] + out_got_ref[...].astype(jnp.float32)).astype(
        jnp.bfloat16
    )


def pick_kernel(info_ref, upper_ref, lower_ref, out_ref):
    crossing = info_ref[0] == 0
    for step in range(2):
        for chunk, part_ref in enumerate((lower_ref, upper_ref)):
            wanted = info_ref[2] == (chunk if step == 1 else 1 - chunk)

            @pl.when(wanted & (crossing if step == 1 else jnp.logical_not(crossing)))
            def _():
                out_ref[...] = part_ref[step]


def join_kernel(info_ref, upper_ref, lower_ref, got_ref, out_ref):
    micro = info_ref[4]
    out_ref[0, 1 - micro] = got_ref[...]

    @pl.when(info_ref[2] == 1)
    def _():
        out_ref[0, micro] = upper_ref[0]

    @pl.when(info_ref[2] != 1)
    def _():
        out_ref[0, micro] = lower_ref[0]


def place_kernel(
    info_ref, own_ref, got_ref, out_own_ref, out_got_ref, sibling_ref, d_in_ref, d_out_ref
):
    columns = own_ref.shape[1] // 3
    own = own_ref[...] + got_ref[...].astype(jnp.float32)
    sibling = sibling_ref[:, : 3 * columns].astype(jnp.float32)
    for part, half in ((own, info_ref[0]), (sibling, 1 - info_ref[0])):
        for block in range(3):
            first = pl.multiple_of((2 * block + half) * columns, 128)
            d_in_ref[:, pl.ds(first, columns)] = part[:, block * columns : (block + 1) * columns]
    owner = info_ref[0] == info_ref[2]

    @pl.when(owner)
    def _():
        d_out_ref[...] = out_own_ref[...] + out_got_ref[...].astype(jnp.float32)

    @pl.when(jnp.logical_not(owner))
    def _():
        d_out_ref[...] = sibling_ref[:, 3 * columns :].astype(jnp.float32)


def call(kernel, outs, operands, scratch=(), flops=0, scalars=1, after=None, mebibytes=5, far=0):
    in_specs = [pl.BlockSpec(memory_space=pltpu.SMEM)] * scalars
    in_specs += [pl.BlockSpec(memory_space=pltpu.HBM)] * far
    in_specs += [pl.BlockSpec(memory_space=pltpu.VMEM)] * (len(operands) - scalars - far)
    if after is not None:
        operands = [*operands, after]
        in_specs.append(pl.BlockSpec(memory_space=pl.ANY))
    return pl.pallas_call(
        kernel,
        out_shape=list(outs),
        in_specs=in_specs,
        out_specs=[pl.BlockSpec(memory_space=pltpu.VMEM)] * len(outs),
        scratch_shapes=list(scratch),
        cost_estimate=pl.CostEstimate(flops=1, bytes_accessed=1, transcendentals=0),
        compiler_params=pltpu.CompilerParams(vmem_limit_bytes=mebibytes * 2**20),
    )(*operands)


def by_chips(acts, grad_top, w_in, w_out, offsets):
    half_type, full_type = jnp.bfloat16, jnp.float32
    shape = jax.ShapeDtypeStruct
    sections = lax.axis_size("section")
    shards = lax.axis_size("tm")
    levels = offsets.shape[1]
    half = shards // 2
    replicas = half // 2
    me = lax.axis_index("tm")
    parity = lax.rem(me, 2)
    side = lax.div(me, half)
    micro_count, shard_rows, model_width = acts.shape[1:]
    columns = model_width // 2
    heads = columns // HEAD_DIM
    seq = shards * shard_rows
    count = seq // 2
    w_qkv = w_in[0]
    w_rows = w_out[0]
    beside = lax.div(lax.rem(me, half), 2)
    micro = lax.rem(side + beside, 2)
    info = jnp.stack([parity, beside, side, lax.axis_index("section"), micro])
    info = jnp.concatenate([info.astype(jnp.int32), offsets[0]])

    def swapped(value, bits, chosen=None):
        pairs = [(device, device ^ bits) for device in range(shards)]
        pairs = [pair for pair in pairs if chosen is None or chosen(pair[0])]
        return lax.ppermute(value, "tm", pairs)

    core, near, far = 1, 2, half

    packed = shape((shard_rows, model_width + 128), half_type)
    top_shape = shape((shard_rows, model_width), half_type)
    own_acts, other_acts, own_top, other_top = call(
        functools.partial(pack_kernel, levels),
        [packed, packed, top_shape, top_shape],
        [info, acts[0], grad_top],
    )
    weights = [
        call(
            functools.partial(turn_kernel, own),
            [shape((3 * columns, model_width), half_type)],
            [info, w_qkv],
            after=own_acts,
        )[0]
        for own in (True, False)
    ]
    pieces = [own_acts, swapped(other_acts, near), swapped(other_acts, far)]
    pieces += [swapped(own_acts, near + far)]
    tops = [own_top, swapped(other_top, near), swapped(other_top, far)]
    pieces[-1], tops, weights = lax.optimization_barrier((pieces[-1], tops, weights))
    tops += [swapped(own_top, near + far)]
    pieces += [swapped(piece, core) for piece in pieces]

    rows_shape = shape((seq, columns), half_type)
    normed, rms, norm, flag_rows, queries, keys, values, keys_t = call(
        functools.partial(project_kernel, replicas),
        [
            shape((2, replicas, shard_rows, model_width), full_type),
            shape((2, replicas, shard_rows, 128), full_type),
            shape((seq, model_width), half_type),
            shape((128, seq), full_type),
            rows_shape,
            rows_shape,
            rows_shape,
            shape((columns, seq), half_type),
        ],
        [info, *pieces, w_qkv],
        scratch=[pltpu.VMEM((shards, *packed.shape), half_type)],
        flops=6 * seq * model_width * columns,
        after=weights[1],
    )
    pairs = heads // 2
    upper_prob, upper_at = call(
        functools.partial(upper_forward_kernel, levels, shard_rows),
        [
            shape((pairs, seq, 2 * count), half_type),
            shape((columns, count), half_type),
        ],
        [flag_rows, queries, keys, values],
        scalars=0,
        flops=4 * columns * seq * count,
    )
    tops, upper_at = lax.optimization_barrier((tuple(tops), upper_at))
    tops = [*tops, *[swapped(piece, core) for piece in tops]]
    own_rows = model_width // shards
    probs, attended = {True: upper_prob}, {True: upper_at}
    got, kept = {}, {}
    piece_shape = shape((replicas, shard_rows, model_width), half_type)
    wide_shape = shape((replicas, shard_rows, model_width + 128), half_type)
    grads_shape = shape((replicas, shard_rows, 3 * columns), half_type)
    sum_shape = shape((count, columns), full_type)
    full_grads = shape((half, shard_rows, 3 * columns), half_type)
    full_rows = shape((half, shard_rows, model_width), half_type)
    term_shape = (own_rows, 3 * columns)
    rows_scratch = pltpu.VMEM(full_rows.shape, half_type)
    grads_scratch = pltpu.VMEM(full_grads.shape, half_type)
    result, full, ordered = {}, {}, {}
    for turn in range(sections):
        last = turn + 1 == sections
        fresh_section = sections - 1 - turn
        sums, parts, crossed = [], {}, {}

        def norm_step(upper, after):
            (result[upper],) = call(
                functools.partial(norm_kernel, upper),
                [wide_shape if turn + 2 == sections and not upper else piece_shape],
                [info, parts[upper], normed, rms, kept[upper][0], *weights, *crossed[upper]],
                after=after,
            )
            if not last:
                hop = [(sections - 1 - turn, sections - 2 - turn)]
                got[upper] = lax.ppermute(result[upper], "section", hop)

        for upper in (True, False):
            rows_in, after = tops, keys_t if upper else result.get(True)
            if turn:
                tied = parts if last else result
                before = result[False] if upper else tied[True]
                got[upper], after = lax.optimization_barrier((got[upper], before))
                if not upper:
                    tied[True] = after
                if last and not upper:
                    after, result[True] = lax.optimization_barrier((after, result[True]))
                rows_in = [got[upper], swapped(got[upper], core), *kept[upper]]
            part = 3 * columns // PIECES[upper]
            cross = [shape((replicas, shard_rows, part), half_type)] * PIECES[upper]
            outs = [piece_shape] * (1 if last else 2) + [grads_shape, *cross]
            outs += [sum_shape, sum_shape] if upper else []
            scratch = []
            if last:
                outs += [full_grads]
            else:
                scratch += [grads_scratch]
            if last:
                outs += [full_rows]
            else:
                scratch += [rows_scratch]
            part_keys = seq if upper else count
            scratch += [pltpu.VMEM((pairs, part_keys, 2 * count), half_type)]
            if last:
                scratch += [pltpu.VMEM(piece_shape.shape, half_type)]
            answer = call(
                functools.partial(
                    backward_kernel, upper, 0 if turn else len(tops), last, fresh_section
                ),
                outs,
                [info, *rows_in, w_rows, probs[upper], queries, values, keys_t]
                + [attended[upper], *sums],
                scratch=scratch,
                flops=2 * count * columns * (2 * model_width + 4 * part_keys),
                after=after,
            )
            kept[upper] = tuple(answer[:2])
            answer = answer[1 if last else 2 :]
            keep = answer[0]
            send = answer[1 : 1 + len(cross)]
            parts[upper] = keep
            if upper:
                sums = answer[1 + len(cross) : 3 + len(cross)]
                (parts[True],) = call(
                    norm_part_kernel,
                    [shape((replicas * shard_rows, model_width), full_type)],
                    [info, keep, weights[0]],
                    flops=3 * replicas * shard_rows * model_width * model_width,
                    after=keep,
                )
                if turn == 0:
                    lower_prob, lower_at, norm_t = call(
                        functools.partial(lower_forward_kernel, levels, shard_rows),
                        [
                            shape((pairs, count, 2 * count), half_type),
                            shape((columns, count), half_type),
                            shape((4 * own_rows, seq), half_type),
                        ],
                        [info, norm, flag_rows, queries, keys, values],
                        flops=4 * columns * count * count,
                        after=parts[True],
                    )
                    probs[False], attended[False] = lower_prob, lower_at
            if last:
                full[upper], ordered[upper] = answer[-2:]
            crossed[upper] = [swapped(piece, core) for piece in send]
            if upper:
                norm_step(True, keep)
        if last:
            send_pass, send_keep = call(
                send_kernel,
                [shape(term_shape, half_type)] * 2,
                [norm_t, full[False], full[True]],
                scalars=0,
            )
        norm_step(False, send_keep if last else result[True])

    got_pass = swapped(send_pass, near)
    got_keep = swapped(send_keep, far)
    own_rows_grad = [result[True], result[False]]
    (theirs,) = call(pick_kernel, [top_shape], [info, *own_rows_grad])
    to_owner = [(device, device ^ (far if device % 2 else near)) for device in range(shards)]
    partner = lax.ppermute(theirs, "tm", to_owner)
    terms = call(
        term_kernel,
        [shape(term_shape, full_type)] * 2
        + [shape((own_rows, model_width), full_type)] * 2
        + [shape((own_rows, model_width), half_type)],
        [info, norm_t, full[False], full[True], attended[False], attended[True]]
        + [ordered[False], ordered[True]],
        after=theirs,
    )
    in_pass, in_keep, out_pass, out_keep, out_send = terms
    got_out_pass = swapped(out_send, near, lambda device: device // half == device % 2)
    got_out_keep = swapped(out_send, far, lambda device: device // half != device % 2)
    _, _, done = lax.optimization_barrier((got_keep, got_out_keep, partner))
    (summed,) = call(
        sum_kernel,
        [shape((own_rows, 3 * columns + model_width), half_type)],
        [in_pass, got_pass, out_pass, got_out_pass],
        scalars=0,
        after=done,
    )
    d_w_in, d_w_out = call(
        place_kernel,
        [
            shape((own_rows, 3 * model_width), full_type),
            shape((own_rows, model_width), full_type),
        ],
        [info, in_keep, got_keep, out_keep, got_out_keep, swapped(summed, core)],
    )
    (d_acts,) = call(
        join_kernel, [shape(acts.shape, half_type)], [info, *own_rows_grad, partner]
    )
    return (d_acts, d_w_in[None], d_w_out[None])


def layer_gradients(acts, grad_top, w_in, w_out, offsets):
    shards = lax.axis_size("tm")
    micro_count, shard_rows, model_width = acts.shape[1:]
    heads = model_width // HEAD_DIM
    prob_bytes = 2 * heads * (shards * shard_rows) ** 2
    fits = prob_bytes <= 2**24 and model_width % (128 * shards) == 0 and shard_rows % 16 == 0
    square = shards % 4 == 0 and shards // 4 == 2
    if micro_count == 2 and square and heads % 4 == 0 and fits:
        return by_chips(acts, grad_top, w_in, w_out, offsets)
    return per_device(acts, grad_top, w_in, w_out, offsets)


def solution(mesh):
    placed = (
        P("section", None, "tm", None),
        P(None, "tm", None),
        P("section", None, None),
        P("section", None, None),
        P("tm", None),
    )
    return jax.shard_map(
        layer_gradients,
        mesh=mesh,
        in_specs=placed,
        out_specs=(
            P("section", None, "tm", None),
            P("section", "tm", None),
            P("section", "tm", None),
        ),
        check_vma=False,
    )
```
